32 devices in a mesh: groups: 2 (over y), epoch: 4 (over z), space: 2 (over x), sub: 2 (over core).
Axes of the slice: x: 2, y: 2, z: 4, core: 2. Of those that a mesh axis runs over, the one named last changes fastest.
Arguments:
- slc: bfloat16 [2, 64, 128, 1024], P(None, ('groups', 'epoch'), 'space', 'sub'), parts along dimension 1, may hold values from -8 to 8
- offsets: int32 [64, 4], P(('groups', 'epoch')), parts along dimension 0, may hold values from 1 to 8, as said below
- weights: float32 [64, 4], P(('groups', 'epoch')), parts along dimension 0, may hold values from 0.3 to 3
- estimate: float32 [64, 32, 1024], P(('groups', 'epoch'), 'space', 'sub'), parts along dimension 0, may hold values from -2 to 2
- direction: float32 [64, 32, 1024], P(('groups', 'epoch'), 'space', 'sub'), parts along dimension 0, may hold values from -2 to 2
- prev_mean: float32 [1], replicated, may hold values from 0.05 to 0.5
Outputs:
- new_estimate: float32 [64, 32, 1024], P(('groups', 'epoch'), 'space', 'sub'), parts along dimension 0
- new_direction: float32 [64, 32, 1024], P(('groups', 'epoch'), 'space', 'sub'), parts along dimension 0
The draws below stay inside these ranges and needn't reach their ends.
There are 2 independent parts, one for each index of `groups`. The reference program is written for one: setup_inputs(seed, part) draws one part's arguments, and reference() takes and returns one part's arrays. A program takes and returns all parts, laid end to end along the dimension named above; an argument that names none is the same for every part. Nothing has to cross between parts.
Inputs may be any that keep to these rules, and one draw needn't show every extreme that they name: `offsets`: each row holds 4 different distances; partners wrap past the last epoch to the first.
All inputs are finite; a program needn't handle non-finite values.
Results may differ from the reference program's by a relative error of at most 0.0003.
Values may be sent and summed in bfloat16 or wider, within the bound.
No kernel may reach another device: no remote copies, remote signals or barrier semaphores. Data moves between devices by JAX's collectives and lax.ppermute only.
A program may use at most 64 MiB of HBM per device.

```python
import math
import jax
import jax.numpy as jnp
from jax import lax

SLOTS = 4
OFFS = 8
LOOK = 4
RADIUS = 3
EPOCHS = 32
ROWS = 128
COLS = 1024


def draw_slc(key, part):
    keys = jax.random.split(jax.random.fold_in(key, 7), 6)
    scene_real = jax.random.normal(keys[0], (ROWS, COLS), jnp.float32) * math.sqrt(0.5)
    scene_imag = jax.random.normal(keys[1], (ROWS, COLS), jnp.float32) * math.sqrt(0.5)
    offset_phase = jax.random.uniform(keys[2], (EPOCHS, 1, 1), jnp.float32, -math.pi, math.pi)
    jitter = 0.4 * jax.random.normal(keys[3], (EPOCHS, ROWS, COLS), jnp.float32)
    noise_level = jnp.exp(jax.random.uniform(keys[4], (EPOCHS, 1, 1), jnp.float32, math.log(0.2), math.log(3.0)))
    noise = jax.random.normal(keys[5], (2, EPOCHS, ROWS, COLS), jnp.float32) * math.sqrt(0.5) * noise_level
    phase = offset_phase + jitter
    cosine = jnp.cos(phase)
    sine = jnp.sin(phase)
    real_part = scene_real * cosine - scene_imag * sine + noise[0]
    imag_part = scene_real * sine + scene_imag * cosine + noise[1]
    stacked = jnp.stack([real_part, imag_part])
    return jnp.clip(stacked, -8.0, 8.0).astype(jnp.bfloat16)


def leading(row_values, wanted):
    position = jnp.argmax(row_values == wanted)
    return jnp.roll(row_values, -position)


def draw_offsets(key, part):
    keys = jax.random.split(jax.random.fold_in(key, 11), EPOCHS)
    ordered = jax.vmap(lambda single: jax.random.permutation(single, OFFS))(keys) + 1
    ordered = ordered.astype(jnp.int32)
    ordered = ordered.at[0].set(leading(ordered[0], OFFS))
    ordered = ordered.at[1].set(leading(ordered[1], 1))
    return ordered[:, :SLOTS].astype(jnp.int32)


def shard_levels(own_key, dims, cuts, smallest, largest):
    def one(dim, shards_of):
        draws = jax.random.uniform(jax.random.fold_in(jax.random.fold_in(own_key, 6), dim), (shards_of,), jnp.float32, smallest / len(cuts), largest / len(cuts))
        return jnp.repeat(jnp.exp(draws), dims[dim] // shards_of).reshape((-1,) + (1,) * (len(dims) - dim - 1))

    loudness = one(*cuts[0])
    for cut in cuts[1:]:
        loudness = loudness * one(*cut)
    return loudness


def normal_values(own_key, shape, scale, most, shards=(), kind=jnp.bfloat16):
    drawn = jax.random.normal(own_key, shape, jnp.float32) * scale
    if len(shards) > 0:
        drawn = shard_levels(own_key, shape, shards, -0.22, 0.18) * drawn
    return jnp.clip(drawn, min=-most, max=most).astype(kind)


def setup_inputs(seed: int = 0, part: int = 0) -> dict:
    key_list = jax.random.split(jax.random.key(seed), 7)
    part_splits = jax.random.split(jax.random.fold_in(key_list[6], part), 7)
    slc = draw_slc(jax.random.fold_in(jax.random.fold_in(key_list[6], part), 71), part)
    offsets = draw_offsets(jax.random.fold_in(jax.random.fold_in(key_list[6], part), 71), part)
    weights = jnp.clip(jnp.exp(math.log(3.0) - 2.3025851 * jax.random.uniform(part_splits[2], (EPOCHS, SLOTS), jnp.float32) ** shard_levels(part_splits[2], (EPOCHS, SLOTS), ((0, 4),), -0.2, 0.2)), 0.3, 3.0)
    estimate = normal_values(part_splits[3], (EPOCHS, ROWS // LOOK, COLS), 0.3, 2.0, ((0, 4), (1, 2), (2, 2)), jnp.float32)
    direction = normal_values(part_splits[4], (EPOCHS, ROWS // LOOK, COLS), 0.3, 2.0, ((0, 4), (1, 2), (2, 2)), jnp.float32)
    prev_mean = jnp.clip(jnp.exp(jax.random.uniform(key_list[5], (1,), jnp.float32, math.log(0.05), math.log(0.5))), 0.05, 0.5)
    return dict(slc=slc, offsets=offsets, weights=weights, estimate=estimate, direction=direction, prev_mean=prev_mean)


EPSILON = 1e-06

def looked_sum(field):
    shape = field.shape
    return lax.optimization_barrier(jnp.sum(field.reshape(shape[:-2] + (shape[-2] // LOOK, LOOK, shape[-1])), axis=-2))

def window_sum(padded, axis):
    length = padded.shape[axis] - 2 * RADIUS
    total = lax.slice_in_dim(padded, 0, length, axis=axis)
    for shift_at in range(1, 2 * RADIUS + 1):
        total = total + lax.slice_in_dim(padded, shift_at, shift_at + length, axis=axis)
    return total

def box_sum(field):
    widths = [(0, 0)] * (field.ndim - 2) + [(RADIUS, RADIUS), (RADIUS, RADIUS)]
    padded = jnp.pad(field, widths)
    return window_sum(window_sum(padded, field.ndim - 2), field.ndim - 1)

def reference(slc, offsets, weights, estimate, direction, prev_mean):
    numbers = jnp.arange(EPOCHS, dtype=jnp.int32)
    partner = ((numbers[:, None] + offsets) % EPOCHS).astype(jnp.int32)

    def one_epoch(epoch_index):
        own_real = slc[0, epoch_index].astype(jnp.float32)
        own_imag = slc[1, epoch_index].astype(jnp.float32)
        powers = looked_sum(own_real * own_real + own_imag * own_imag)
        pieces = []
        for slot_index in range(SLOTS):
            mate_index = partner[epoch_index, slot_index]
            mate_real = slc[0, mate_index].astype(jnp.float32)
            mate_imag = slc[1, mate_index].astype(jnp.float32)
            pieces.append(looked_sum(own_real * mate_real + own_imag * mate_imag))
            pieces.append(looked_sum(own_imag * mate_real - own_real * mate_imag))
        return (jnp.stack(pieces), powers)
    looked, powers = lax.map(one_epoch, numbers)
    boxed = box_sum(looked)
    power_box = box_sum(powers)
    coh_real = boxed[:, 0::2]
    coh_imag = boxed[:, 1::2]
    denominator = power_box[:, None] * power_box[partner] + EPSILON
    coherence = (coh_real * coh_real + coh_imag * coh_imag) / denominator
    observed = coh_imag / jnp.sqrt(denominator)
    fitted = estimate[:, None] - estimate[partner]
    factor = weights[:, :, None, None] * coherence
    weighted = factor * (observed - fitted)
    gradient = lax.optimization_barrier(jnp.sum(weighted, axis=1)) - jax.ops.segment_sum(weighted.reshape((-1,) + weighted.shape[2:]), partner.reshape(-1), num_segments=EPOCHS)
    cell_count = float(EPOCHS * (ROWS // LOOK) * COLS)
    grad_norm = jnp.sum(gradient * gradient)
    crossed = jnp.sum(gradient * direction)
    momentum = grad_norm / cell_count / prev_mean[0]
    new_direction = gradient + momentum * direction
    along_sum = grad_norm + momentum * crossed
    spread = new_direction[:, None] - new_direction[partner]
    curvature = jnp.sum(factor * spread * spread)
    step_size = along_sum / curvature
    return (estimate + step_size * new_direction, new_direction)
```

```python
import functools

import jax
import jax.numpy as jnp
from jax import lax
from jax.experimental import pallas as pl
from jax.experimental.pallas import tpu as pltpu
from jax.sharding import PartitionSpec as P

SLOTS = 4
OFFS = 8
LOOK = 4
RADIUS = 3


EPSILON = 1e-06


def passed_along(x, axis, by):
    size = lax.axis_size(axis)
    return lax.ppermute(x, axis, [(i, (i + by) % size) for i in range(size)])


def extended_2(block, sides, width):
    for axis, dim in sides:
        count = lax.axis_size(axis)
        forward = [(i, i + 1) for i in range(count - 1)]
        backward = [(target, source) for source, target in forward]
        low = lax.ppermute(
            lax.slice_in_dim(block, block.shape[dim] - width, None, axis=dim), axis, forward
        )
        high = lax.ppermute(lax.slice_in_dim(block, 0, width, axis=dim), axis, backward)
        block = jnp.concatenate([low, block, high], axis=dim)
    return block


def looked_sum(field):
    shape = field.shape
    return jnp.sum(field.reshape(shape[:-2] + (shape[-2] // LOOK, LOOK, shape[-1])), axis=-2)


def window_sum(padded, axis):
    length = padded.shape[axis] - 2 * RADIUS
    total = lax.slice_in_dim(padded, 0, length, axis=axis)
    for shift_at in range(1, 2 * RADIUS + 1):
        total = total + lax.slice_in_dim(padded, shift_at, shift_at + length, axis=axis)
    return total


def ring_plan(slc, offsets, weights, estimate, direction, prev_mean):
    epochs_here = slc.shape[1]
    look_rows = slc.shape[2] // LOOK
    col_count = slc.shape[3]
    ahead = passed_along(slc, "epoch", -1)
    extended = jnp.concatenate([slc, ahead], axis=1)
    numbers = jnp.arange(epochs_here, dtype=jnp.int32)
    partner = numbers[:, None] + offsets
    own_real = slc[0].astype(jnp.float32)
    own_imag = slc[1].astype(jnp.float32)
    ext_real = extended[0].astype(jnp.float32)
    ext_imag = extended[1].astype(jnp.float32)
    powers = looked_sum(ext_real * ext_real + ext_imag * ext_imag)
    pieces = []
    for slot_index in range(SLOTS):
        mate_real = jnp.take(ext_real, partner[:, slot_index], axis=0)
        mate_imag = jnp.take(ext_imag, partner[:, slot_index], axis=0)
        pieces.append(looked_sum(own_real * mate_real + own_imag * mate_imag))
        pieces.append(looked_sum(own_imag * mate_real - own_real * mate_imag))
    pair_count = epochs_here * 2 * SLOTS
    stacked = jnp.concatenate(
        [jnp.stack(pieces, axis=1).reshape(pair_count, look_rows, col_count), powers], axis=0
    )
    padded = extended_2(stacked, (("space", 1), ("sub", 2)), RADIUS)
    boxed = window_sum(window_sum(padded, 1), 2)
    pair_boxed = boxed[:pair_count].reshape(epochs_here, 2 * SLOTS, look_rows, col_count)
    power_box = boxed[pair_count:]
    coh_real = pair_boxed[:, 0::2]
    coh_imag = pair_boxed[:, 1::2]
    denominator = power_box[:epochs_here, None] * jnp.take(power_box, partner, axis=0) + EPSILON
    coherence = (coh_real * coh_real + coh_imag * coh_imag) / denominator
    observed = coh_imag / jnp.sqrt(denominator)
    est_ahead = passed_along(estimate, "epoch", -1)
    est_extended = jnp.concatenate([estimate, est_ahead], axis=0)
    fitted = estimate[:, None] - jnp.take(est_extended, partner, axis=0)
    factor = weights[:, :, None, None] * coherence
    weighted = factor * (observed - fitted)
    flattened = weighted.reshape(epochs_here * SLOTS, look_rows * col_count)
    selector = (
        jnp.arange(epochs_here + OFFS, dtype=jnp.int32)[:, None] == partner.reshape(1, -1)
    ).astype(jnp.float32)
    gathered = jnp.dot(
        selector, flattened, precision=lax.Precision.HIGHEST, preferred_element_type=jnp.float32
    ).reshape(epochs_here + OFFS, look_rows, col_count)
    own_part = jnp.sum(weighted, axis=1) - gathered[:epochs_here]
    returned = passed_along(-gathered[epochs_here:], "epoch", 1)
    gradient = jnp.concatenate([own_part + returned, own_part[OFFS:]], axis=0)
    cell_count = float(
        epochs_here
        * lax.axis_size("epoch")
        * look_rows
        * lax.axis_size("space")
        * col_count
        * lax.axis_size("sub")
    )
    local_norm = jnp.sum(gradient * gradient)
    local_crossed = jnp.sum(gradient * direction)
    mean_before = prev_mean[0]
    fields_ahead = passed_along(
        jnp.stack([gradient, direction]).astype(jnp.bfloat16), "epoch", -1
    ).astype(jnp.float32)
    grad_extended = jnp.concatenate([gradient, fields_ahead[0]], axis=0)
    old_extended = jnp.concatenate([direction, fields_ahead[1]], axis=0)
    grad_spread = gradient[:, None] - jnp.take(grad_extended, partner, axis=0)
    old_spread = direction[:, None] - jnp.take(old_extended, partner, axis=0)
    totals = lax.psum(
        (
            local_norm,
            local_crossed,
            jnp.sum(factor * grad_spread * grad_spread),
            jnp.sum(factor * grad_spread * old_spread),
            jnp.sum(factor * old_spread * old_spread),
        ),
        ("epoch", "space", "sub"),
    )
    grad_norm, crossed, grad_term, mixed_term, old_term = totals
    momentum = grad_norm / cell_count / mean_before
    new_direction = gradient + momentum * direction
    curvature = grad_term + 2.0 * momentum * mixed_term + momentum * momentum * old_term
    along_sum = grad_norm + momentum * crossed
    step_size = along_sum / curvature
    return (estimate + step_size * new_direction, new_direction)


LANES = 128
SIDES = 2 * RADIUS
HALO = 16
PARAM_LANE = 96
VMEM = pl.BlockSpec(memory_space=pltpu.VMEM)
SMEM = pl.BlockSpec(memory_space=pltpu.SMEM)
VMEM_BYTES = 48 * 1024 * 1024


def split_two(value):
    high = value.astype(jnp.bfloat16)
    low = (value - high.astype(jnp.float32)).astype(jnp.bfloat16)
    return high, low


def pack_kernel(slc, estimate, direction, params, strips, edge, fields):
    tiles = strips.shape[0]
    epochs = slc.shape[1]
    rows = slc.shape[2]
    look_rows = estimate.shape[1]
    lane = lax.broadcasted_iota(jnp.int32, (rows, LANES), 1)
    value = params[...]
    high = value.astype(jnp.bfloat16).astype(jnp.float32)
    middle = (value - high).astype(jnp.bfloat16).astype(jnp.float32)
    low = value - high - middle
    third = PARAM_LANE + 2 * SLOTS
    split = jnp.where(lane < third, high, jnp.where(lane < third + SLOTS, middle, low))
    split = jnp.where(lane >= PARAM_LANE, split, 0.0)

    def tile_of(part, epoch, tile):
        return slc[part, epoch, :, tile * LANES : (tile + 1) * LANES].astype(jnp.float32)

    def placed(total, source, start, target):
        moved = pltpu.roll(source, (target - start) % LANES, axis=1)
        inside = (lane >= target) & (lane < target + RADIUS)
        return jnp.where(inside, moved, total)

    for tile in range(tiles):
        total = split
        for part in range(2):
            for epoch in range(epochs):
                at = (part * epochs + epoch) * SIDES
                if tile > 0:
                    total = placed(total, tile_of(part, epoch, tile - 1), LANES - RADIUS, at)
                if tile < tiles - 1:
                    total = placed(total, tile_of(part, epoch, tile + 1), 0, at + RADIUS)
        strips[tile] = total.astype(jnp.bfloat16)
    total = jnp.zeros((rows, LANES), jnp.float32)
    for part in range(2):
        for epoch in range(epochs):
            at = (part * epochs + epoch) * SIDES
            total = placed(total, tile_of(part, epoch, tiles - 1), LANES - RADIUS, at)
            total = placed(total, tile_of(part, epoch, 0), 0, at + RADIUS)
    edge[...] = total.astype(jnp.bfloat16)
    for tile in range(tiles):
        columns = slice(tile * LANES, (tile + 1) * LANES)
        for epoch in range(epochs):
            here = slice(epoch * look_rows, (epoch + 1) * look_rows)
            first, second = split_two(estimate[epoch, :, columns])
            fields[tile, 0, here, :] = first
            fields[tile, 1, here, :] = second
            fields[tile, 2, here, :] = direction[epoch, :, columns].astype(jnp.bfloat16)


def main_kernel(sizes, partner, weight, present, *refs):
    tiles, epochs, rows = sizes
    blocks = refs[:tiles]
    strips = refs[tiles : 2 * tiles]
    fields = refs[2 * tiles : 3 * tiles]
    top, bottom, gradient, sums = refs[3 * tiles : 3 * tiles + 4]
    full, rim_full, main, rim, looked, power, boxed, power_box, factors, est, old = refs[3 * tiles + 4 :]
    look_rows = rows // LOOK
    tall = (rows + 2 * HALO) // LOOK
    halo_looks = HALO // LOOK
    total = tiles * epochs
    group = 2 * SLOTS
    has_top = present[0]
    has_bottom = present[1]
    f32 = jnp.float32

    band_from = lax.broadcasted_iota(jnp.int32, (2 * LANES, LANES), 0)
    band_to = lax.broadcasted_iota(jnp.int32, (2 * LANES, LANES), 1)
    rim_lane = band_from - LANES
    side = rim_lane % SIDES
    rim_column = jnp.where(side < RADIUS, side - RADIUS, LANES + side - RADIUS)
    rim_column = jnp.where(rim_lane < LOOK * SIDES, rim_column, 4 * LANES)
    column = jnp.where(band_from < LANES, band_from, rim_column)
    band = (jnp.abs(column - band_to) <= RADIUS).astype(f32).astype(jnp.bfloat16)
    out_at = lax.broadcasted_iota(jnp.int32, (group * look_rows, group * tall), 0)
    in_at = lax.broadcasted_iota(jnp.int32, (group * look_rows, group * tall), 1)
    near = jnp.abs(in_at % tall - halo_looks - out_at % look_rows) <= RADIUS
    near = near & (in_at // tall == out_at // look_rows)
    sum_rows = near.astype(f32).astype(jnp.bfloat16)

    lane = lax.broadcasted_iota(jnp.int32, (tall, LANES), 1)
    for block in range(tiles):
        for part in range(2):

            @pl.loop(0, epochs)
            def _(epoch):
                at = part * total + block * epochs + epoch
                row = pl.multiple_of((part * epochs + epoch) * HALO, HALO)
                full[at, :HALO] = top[block, pl.ds(row, HALO), :].astype(f32) * has_top
                full[at, HALO : HALO + rows] = blocks[block][part, epoch].astype(f32)
                full[at, HALO + rows :] = bottom[block, pl.ds(row, HALO), :].astype(f32) * has_bottom

        last = slice(2 * epochs * HALO, 2 * epochs * HALO + HALO)
        rim_full[block, :HALO] = top[block, last, :].astype(f32) * has_top
        rim_full[block, HALO : HALO + rows] = strips[block][...].astype(f32)
        rim_full[block, HALO + rows :] = bottom[block, last, :].astype(f32) * has_bottom

        @pl.loop(0, epochs)
        def _(epoch):
            here = pl.ds(pl.multiple_of(epoch * look_rows, look_rows), look_rows)
            est[block * epochs + epoch] = fields[block][0, here, :].astype(f32) + fields[block][1, here, :].astype(f32)
            old[block * epochs + epoch] = fields[block][2, here, :].astype(f32)

    @pl.loop(0, 2 * total)
    def _(at):
        for look in range(LOOK):
            main[at, look] = full[at, pl.ds(look, tall, stride=LOOK), :]

    for block in range(tiles):
        by_look = [rim_full[block, pl.ds(look, tall, stride=LOOK), :] for look in range(LOOK)]
        for part in range(2):
            for epoch in range(epochs):
                start = (part * epochs + epoch) * SIDES
                value = jnp.zeros((tall, LANES), f32)
                for look in range(LOOK):
                    target = look * SIDES
                    moved = pltpu.roll(by_look[look], (target - start) % LANES, axis=1)
                    value = jnp.where((lane >= target) & (lane < target + SIDES), moved, value)
                rim[part * total + block * epochs + epoch] = value

    @pl.loop(0, total)
    def _(epoch):
        for piece in range(0, tall, 8):
            rows_at = slice(piece, piece + 8)
            own_re = [main[epoch, look, rows_at] for look in range(LOOK)]
            own_im = [main[total + epoch, look, rows_at] for look in range(LOOK)]
            rim_re = rim[epoch, rows_at]
            rim_im = rim[total + epoch, rows_at]
            value = own_re[0] * own_re[0] + own_im[0] * own_im[0]
            for look in range(1, LOOK):
                value = value + (own_re[look] * own_re[look] + own_im[look] * own_im[look])
            at = pl.multiple_of(epoch * tall + piece, 8)
            power[pl.ds(at, 8), :LANES] = value
            power[pl.ds(at, 8), LANES:] = rim_re * rim_re + rim_im * rim_im
            for slot in range(SLOTS):
                mate = partner[epoch * SLOTS + slot]
                real = None
                for look in range(LOOK):
                    mate_re = main[mate, look, rows_at]
                    mate_im = main[total + mate, look, rows_at]
                    one = own_re[look] * mate_re + own_im[look] * mate_im
                    two = own_im[look] * mate_re - own_re[look] * mate_im
                    real = one if real is None else real + one
                    imag = two if look == 0 else imag + two
                mate_re = rim[mate, rows_at]
                mate_im = rim[total + mate, rows_at]
                at = pl.multiple_of(epoch * (group * tall) + 2 * slot * tall + piece, 8)
                looked[pl.ds(at, 8), :LANES] = real
                looked[pl.ds(at, 8), LANES:] = rim_re * mate_re + rim_im * mate_im
                at = pl.multiple_of(epoch * (group * tall) + (2 * slot + 1) * tall + piece, 8)
                looked[pl.ds(at, 8), :LANES] = imag
                looked[pl.ds(at, 8), LANES:] = rim_im * mate_re - rim_re * mate_im

    def box(value):
        high, low = split_two(value)
        wide = jnp.dot(high, band, preferred_element_type=f32) + jnp.dot(low, band, preferred_element_type=f32)
        high, low = split_two(wide)
        return jnp.dot(sum_rows, high, preferred_element_type=f32) + jnp.dot(sum_rows, low, preferred_element_type=f32)

    for block in range(total // group):
        value = box(power[block * group * tall : (block + 1) * group * tall, :])
        for at in range(group):
            power_box[block * group + at] = value[at * look_rows : (at + 1) * look_rows]

    @pl.loop(0, total // 4)
    def _(quad):
        for extra in range(4):
            epoch = quad * 4 + extra
            at = pl.multiple_of(epoch * (group * tall), group * tall)
            boxed[epoch] = box(looked[pl.ds(at, group * tall), :])

    grad = gradient
    for block in range(tiles):
        grad[block] = jnp.zeros(grad.shape[1:], f32)

    def rows_of(epoch):
        return epoch // epochs, pl.ds(pl.multiple_of((epoch % epochs) * look_rows, look_rows), look_rows)

    @pl.loop(0, total)
    def _(epoch):
        own_power = power_box[epoch]
        own_est = est[epoch]
        own = jnp.zeros((look_rows, LANES), f32)
        for slot in range(SLOTS):
            mate = partner[epoch * SLOTS + slot]
            coh_re = boxed[epoch, 2 * slot * look_rows : (2 * slot + 1) * look_rows, :]
            coh_im = boxed[epoch, (2 * slot + 1) * look_rows : (2 * slot + 2) * look_rows, :]
            inverse = lax.rsqrt(own_power * power_box[mate] + EPSILON)
            unit_re = coh_re * inverse
            unit_im = coh_im * inverse
            factor = weight[epoch * SLOTS + slot] * (unit_re * unit_re + unit_im * unit_im)
            factors[epoch * SLOTS + slot] = factor
            weighted = factor * (unit_im - (own_est - est[mate]))
            own = own + weighted
            at, here = rows_of(mate)
            grad[at, here, :] = grad[at, here, :] - weighted
        at, here = rows_of(epoch)
        grad[at, here, :] = grad[at, here, :] + own

    def totals(epoch, carry):
        norm, crossed, grad_term, mixed, old_term = carry
        at, here = rows_of(epoch)
        own_grad = grad[at, here, :]
        own_old = old[epoch]
        norm = norm + own_grad * own_grad
        crossed = crossed + own_grad * own_old
        for slot in range(SLOTS):
            mate = partner[epoch * SLOTS + slot]
            factor = factors[epoch * SLOTS + slot]
            at, here = rows_of(mate)
            grad_spread = own_grad - grad[at, here, :]
            old_spread = own_old - old[mate]
            pulled = factor * grad_spread
            grad_term = grad_term + pulled * grad_spread
            mixed = mixed + pulled * old_spread
            old_term = old_term + factor * old_spread * old_spread
        return norm, crossed, grad_term, mixed, old_term

    zero = jnp.zeros((look_rows, LANES), f32)
    results = lax.fori_loop(0, total, totals, (zero,) * 5)
    sums[...] = jnp.zeros(sums.shape, f32)
    for at, value in enumerate(results):
        sums[at : at + 1, :] = jnp.sum(value, axis=0, keepdims=True)


def update_kernel(cell_count, me, prev_mean, estimate, direction, *refs):
    new_estimate, new_direction = refs[-2:]
    tiles = estimate.shape[2] // LANES
    pieces = refs[:tiles]
    scalars = refs[tiles:-2]
    epochs = estimate.shape[0]
    look_rows = estimate.shape[1]
    total = scalars[0][...]
    for other in scalars[1:]:
        total = total + other[...]
    total = jnp.sum(total, axis=1, keepdims=True)
    grad_norm, crossed, grad_term, mixed, old_term = (total[at : at + 1, :] for at in range(5))
    momentum = grad_norm / cell_count / prev_mean[0]
    curvature = grad_term + 2.0 * momentum * mixed + momentum * momentum * old_term
    step = (grad_norm + momentum * crossed) / curvature
    momentum = jnp.broadcast_to(momentum, (look_rows, LANES))
    step = jnp.broadcast_to(step, (look_rows, LANES))
    for shift, piece in enumerate(pieces):
        tile = lax.rem(me[0] - shift + tiles, tiles)
        columns = pl.ds(pl.multiple_of(tile * LANES, LANES), LANES)
        for epoch in range(epochs):
            gradient = piece[epoch * look_rows : (epoch + 1) * look_rows, :]
            moved = gradient + momentum * direction[epoch, :, columns]
            new_direction[epoch, :, columns] = moved
            new_estimate[epoch, :, columns] = estimate[epoch, :, columns] + step * moved


def swapped(up, down, axis):
    size = lax.axis_size(axis)
    if size == 1:
        return jnp.zeros_like(up), jnp.zeros_like(down)
    if size == 2:
        first = lax.axis_index(axis) == 0
        got = lax.ppermute(jnp.where(first, up, down), axis, [(0, 1), (1, 0)])
        return got, got
    forward = [(i, i + 1) for i in range(size - 1)]
    backward = [(target, source) for source, target in forward]
    return lax.ppermute(up, axis, forward), lax.ppermute(down, axis, backward)


def to_ahead(x, axis, by):
    size = lax.axis_size(axis)
    return lax.ppermute(x, axis, [(i, (i + by) % size) for i in range(size)])


def transposed_plan(slc, offsets, weights, estimate, direction, prev_mean):
    f32 = jnp.float32
    bf16 = jnp.bfloat16
    tiles = lax.axis_size("epoch")
    me = lax.axis_index("epoch")
    epochs, rows, columns = slc.shape[1:]
    look_rows = rows // LOOK
    total = tiles * epochs
    tall = (rows + 2 * HALO) // LOOK

    def for_device(shift):
        return lax.rem(me + shift, tiles)

    def piece_for(shift):
        return lax.dynamic_slice_in_dim(slc, for_device(shift) * LANES, LANES, axis=3)

    blocks = [piece_for(0)]
    order = sorted(range(1, tiles), key=lambda shift: min(shift, tiles - shift))
    arrived = {}
    for shift in order:
        arrived[shift] = to_ahead(piece_for(tiles - shift), "epoch", tiles - shift)
    blocks += [arrived[shift] for shift in range(1, tiles)]

    params = jnp.zeros((rows, LANES), f32)
    listed = jnp.concatenate([offsets.astype(f32), weights, weights, weights], axis=1)
    params = lax.dynamic_update_slice(params, listed, (0, PARAM_LANE))
    strips, edge, fields = pl.pallas_call(
        pack_kernel,
        out_shape=(
            jax.ShapeDtypeStruct((tiles, rows, LANES), bf16),
            jax.ShapeDtypeStruct((rows, LANES), bf16),
            jax.ShapeDtypeStruct((tiles, 3, epochs * look_rows, LANES), bf16),
        ),
        in_specs=[VMEM] * 4,
        out_specs=(VMEM,) * 3,
        compiler_params=pltpu.CompilerParams(vmem_limit_bytes=VMEM_BYTES),
        cost_estimate=pl.CostEstimate(flops=4_000_000, bytes_accessed=3_000_000, transcendentals=0),
    )(slc, estimate, direction, params)

    before, after = swapped(edge, edge, "sub")
    sub = lax.axis_index("sub")
    lane = lax.broadcasted_iota(jnp.int32, (rows, LANES), 1)
    left_side = (lane < 2 * epochs * SIDES) & (lane % SIDES < RADIUS)
    right_side = (lane < 2 * epochs * SIDES) & (lane % SIDES >= RADIUS)
    nothing = jnp.zeros_like(edge)
    left_edge = jnp.where(left_side & (sub > 0), before, nothing)
    right_edge = jnp.where(right_side & (sub < lax.axis_size("sub") - 1), after, nothing)

    def strip_for(shift):
        target = for_device(shift)
        value = lax.dynamic_index_in_dim(strips, target, axis=0, keepdims=False)
        value = jnp.where(left_side & (target == 0), left_edge, value)
        return jnp.where(right_side & (target == tiles - 1), right_edge, value)

    def field_for(shift):
        return lax.dynamic_index_in_dim(fields, for_device(shift), axis=0, keepdims=False)

    strip_blocks = [strip_for(0)]
    strip_blocks += [to_ahead(strip_for(tiles - shift), "epoch", tiles - shift) for shift in range(1, tiles)]
    field_blocks = [field_for(0)]
    field_blocks += [to_ahead(field_for(tiles - shift), "epoch", tiles - shift) for shift in range(1, tiles)]

    def border(from_row):
        parts = []
        for block, strip in zip(blocks, strip_blocks):
            main = lax.dynamic_slice_in_dim(block, from_row, HALO, axis=2).reshape(2 * epochs * HALO, LANES)
            parts.append(jnp.concatenate([main, lax.dynamic_slice_in_dim(strip, from_row, HALO, axis=0)], axis=0))
        return jnp.stack(parts)

    space = lax.axis_index("space")
    spaces = lax.axis_size("space")
    if spaces == 2:
        mine = border(jnp.where(space == 0, rows - HALO, 0))
        top = bottom = lax.ppermute(mine, "space", [(0, 1), (1, 0)])
    else:
        top, bottom = swapped(border(rows - HALO), border(0), "space")
    present = jnp.stack([space > 0, space < spaces - 1]).astype(f32)

    listed = jnp.concatenate([strip[:epochs, PARAM_LANE : PARAM_LANE + 4 * SLOTS] for strip in strip_blocks], axis=0)
    listed = listed.astype(f32)
    partner = jnp.arange(total, dtype=jnp.int32)[:, None] + listed[:, :SLOTS].astype(jnp.int32)
    partner = lax.rem(partner, total).reshape(-1)
    weight = listed[:, SLOTS : 2 * SLOTS] + listed[:, 2 * SLOTS : 3 * SLOTS] + listed[:, 3 * SLOTS :]
    group = 2 * SLOTS
    gradient, sums = pl.pallas_call(
        functools.partial(main_kernel, (tiles, epochs, rows)),
        out_shape=(
            jax.ShapeDtypeStruct((tiles, epochs * look_rows, LANES), f32),
            jax.ShapeDtypeStruct((8, LANES), f32),
        ),
        in_specs=[SMEM] * 3 + [VMEM] * (3 * tiles + 2),
        out_specs=(VMEM, VMEM),
        scratch_shapes=[
            pltpu.VMEM((2 * total, rows + 2 * HALO, LANES), f32),
            pltpu.VMEM((tiles, rows + 2 * HALO, LANES), f32),
            pltpu.VMEM((2 * total, LOOK, tall, LANES), f32),
            pltpu.VMEM((2 * total, tall, LANES), f32),
            pltpu.VMEM((total * group * tall, 2 * LANES), f32),
            pltpu.VMEM((total * tall, 2 * LANES), f32),
            pltpu.VMEM((total, group * look_rows, LANES), f32),
            pltpu.VMEM((total, look_rows, LANES), f32),
            pltpu.VMEM((total * SLOTS, look_rows, LANES), f32),
            pltpu.VMEM((total, look_rows, LANES), f32),
            pltpu.VMEM((total, look_rows, LANES), f32),
        ],
        compiler_params=pltpu.CompilerParams(vmem_limit_bytes=VMEM_BYTES),
        cost_estimate=pl.CostEstimate(flops=40_000_000, bytes_accessed=4_000_000, transcendentals=0),
    )(partner, weight.reshape(-1), present, *blocks, *strip_blocks, *field_blocks, top, bottom)

    returned = [gradient[0]]
    returned += [to_ahead(gradient[shift], "epoch", shift) for shift in range(1, tiles)]
    place = ("space", "sub")
    count = spaces * lax.axis_size("sub")
    shared = [sums] + [lax.ppermute(sums, place, [(i, (i + by) % count) for i in range(count)]) for by in range(1, count)]
    here = sum(shared[1:], shared[0])
    scalars = [here] + [to_ahead(here, "epoch", by) for by in range(1, tiles)]
    cell_count = float(total * look_rows * spaces * columns * lax.axis_size("sub"))
    return pl.pallas_call(
        functools.partial(update_kernel, cell_count),
        out_shape=(jax.ShapeDtypeStruct(estimate.shape, f32),) * 2,
        in_specs=[SMEM] * 2 + [VMEM] * (2 + 2 * tiles),
        out_specs=(VMEM, VMEM),
        compiler_params=pltpu.CompilerParams(vmem_limit_bytes=VMEM_BYTES),
        cost_estimate=pl.CostEstimate(flops=1_000_000, bytes_accessed=2_000_000, transcendentals=0),
    )(me.reshape(1), prev_mean, estimate, direction, *returned, *scalars)


def on_device(slc, offsets, weights, estimate, direction, prev_mean):
    epochs, rows, columns = slc.shape[1:]
    fits = columns == LANES * lax.axis_size("epoch") and lax.axis_size("epoch") > 1
    fits = fits and 2 * epochs * SIDES <= PARAM_LANE and rows % HALO == 0 and epochs * lax.axis_size("epoch") % (2 * SLOTS) == 0
    plan = transposed_plan if fits else ring_plan
    return plan(slc, offsets, weights, estimate, direction, prev_mean)


def solution(mesh):
    return jax.shard_map(
        on_device,
        mesh=mesh,
        in_specs=(
            P(None, ("groups", "epoch"), "space", "sub"),
            P(("groups", "epoch"), None),
            P(("groups", "epoch"), None),
            P(("groups", "epoch"), "space", "sub"),
            P(("groups", "epoch"), "space", "sub"),
            P(),
        ),
        out_specs=(P(("groups", "epoch"), "space", "sub"), P(("groups", "epoch"), "space", "sub")),
        check_vma=False,
    )
```

```python
import functools

import jax
import jax.numpy as jnp
from jax import lax
from jax.experimental import pallas as pl
from jax.experimental.pallas import tpu as pltpu
from jax.sharding import PartitionSpec as P

SLOTS = 4
OFFS = 8
LOOK = 4
RADIUS = 3


EPSILON = 1e-06


def passed_along(x, axis, by):
    size = lax.axis_size(axis)
    return lax.ppermute(x, axis, [(i, (i + by) % size) for i in range(size)])


def extended_2(block, sides, width):
    for axis, dim in sides:
        count = lax.axis_size(axis)
        forward = [(i, i + 1) for i in range(count - 1)]
        backward = [(target, source) for source, target in forward]
        low = lax.ppermute(
            lax.slice_in_dim(block, block.shape[dim] - width, None, axis=dim), axis, forward
        )
        high = lax.ppermute(lax.slice_in_dim(block, 0, width, axis=dim), axis, backward)
        block = jnp.concatenate([low, block, high], axis=dim)
    return block


def looked_sum(field):
    shape = field.shape
    return jnp.sum(field.reshape(shape[:-2] + (shape[-2] // LOOK, LOOK, shape[-1])), axis=-2)


def window_sum(padded, axis):
    length = padded.shape[axis] - 2 * RADIUS
    total = lax.slice_in_dim(padded, 0, length, axis=axis)
    for shift_at in range(1, 2 * RADIUS + 1):
        total = total + lax.slice_in_dim(padded, shift_at, shift_at + length, axis=axis)
    return total


def ring_plan(slc, offsets, weights, estimate, direction, prev_mean):
    epochs_here = slc.shape[1]
    look_rows = slc.shape[2] // LOOK
    col_count = slc.shape[3]
    ahead = passed_along(slc, "epoch", -1)
    extended = jnp.concatenate([slc, ahead], axis=1)
    numbers = jnp.arange(epochs_here, dtype=jnp.int32)
    partner = numbers[:, None] + offsets
    own_real = slc[0].astype(jnp.float32)
    own_imag = slc[1].astype(jnp.float32)
    ext_real = extended[0].astype(jnp.float32)
    ext_imag = extended[1].astype(jnp.float32)
    powers = looked_sum(ext_real * ext_real + ext_imag * ext_imag)
    pieces = []
    for slot_index in range(SLOTS):
        mate_real = jnp.take(ext_real, partner[:, slot_index], axis=0)
        mate_imag = jnp.take(ext_imag, partner[:, slot_index], axis=0)
        pieces.append(looked_sum(own_real * mate_real + own_imag * mate_imag))
        pieces.append(looked_sum(own_imag * mate_real - own_real * mate_imag))
    pair_count = epochs_here * 2 * SLOTS
    stacked = jnp.concatenate(
        [jnp.stack(pieces, axis=1).reshape(pair_count, look_rows, col_count), powers], axis=0
    )
    padded = extended_2(stacked, (("space", 1), ("sub", 2)), RADIUS)
    boxed = window_sum(window_sum(padded, 1), 2)
    pair_boxed = boxed[:pair_count].reshape(epochs_here, 2 * SLOTS, look_rows, col_count)
    power_box = boxed[pair_count:]
    coh_real = pair_boxed[:, 0::2]
    coh_imag = pair_boxed[:, 1::2]
    denominator = power_box[:epochs_here, None] * jnp.take(power_box, partner, axis=0) + EPSILON
    coherence = (coh_real * coh_real + coh_imag * coh_imag) / denominator
    observed = coh_imag / jnp.sqrt(denominator)
    est_ahead = passed_along(estimate, "epoch", -1)
    est_extended = jnp.concatenate([estimate, est_ahead], axis=0)
    fitted = estimate[:, None] - jnp.take(est_extended, partner, axis=0)
    factor = weights[:, :, None, None] * coherence
    weighted = factor * (observed - fitted)
    flattened = weighted.reshape(epochs_here * SLOTS, look_rows * col_count)
    selector = (
        jnp.arange(epochs_here + OFFS, dtype=jnp.int32)[:, None] == partner.reshape(1, -1)
    ).astype(jnp.float32)
    gathered = jnp.dot(
        selector, flattened, precision=lax.Precision.HIGHEST, preferred_element_type=jnp.float32
    ).reshape(epochs_here + OFFS, look_rows, col_count)
    own_part = jnp.sum(weighted, axis=1) - gathered[:epochs_here]
    returned = passed_along(-gathered[epochs_here:], "epoch", 1)
    gradient = jnp.concatenate([own_part + returned, own_part[OFFS:]], axis=0)
    cell_count = float(
        epochs_here
        * lax.axis_size("epoch")
        * look_rows
        * lax.axis_size("space")
        * col_count
        * lax.axis_size("sub")
    )
    local_norm = jnp.sum(gradient * gradient)
    local_crossed = jnp.sum(gradient * direction)
    mean_before = prev_mean[0]
    fields_ahead = passed_along(
        jnp.stack([gradient, direction]).astype(jnp.bfloat16), "epoch", -1
    ).astype(jnp.float32)
    grad_extended = jnp.concatenate([gradient, fields_ahead[0]], axis=0)
    old_extended = jnp.concatenate([direction, fields_ahead[1]], axis=0)
    grad_spread = gradient[:, None] - jnp.take(grad_extended, partner, axis=0)
    old_spread = direction[:, None] - jnp.take(old_extended, partner, axis=0)
    totals = lax.psum(
        (
            local_norm,
            local_crossed,
            jnp.sum(factor * grad_spread * grad_spread),
            jnp.sum(factor * grad_spread * old_spread),
            jnp.sum(factor * old_spread * old_spread),
        ),
        ("epoch", "space", "sub"),
    )
    grad_norm, crossed, grad_term, mixed_term, old_term = totals
    momentum = grad_norm / cell_count / mean_before
    new_direction = gradient + momentum * direction
    curvature = grad_term + 2.0 * momentum * mixed_term + momentum * momentum * old_term
    along_sum = grad_norm + momentum * crossed
    step_size = along_sum / curvature
    return (estimate + step_size * new_direction, new_direction)


LANES = 128
SIDES = 2 * RADIUS
HALO = 16
PARAM_LANE = 96
VMEM = pl.BlockSpec(memory_space=pltpu.VMEM)
SMEM = pl.BlockSpec(memory_space=pltpu.SMEM)
VMEM_BYTES = 48 * 1024 * 1024


def split_two(value):
    high = value.astype(jnp.bfloat16)
    low = (value - high.astype(jnp.float32)).astype(jnp.bfloat16)
    return high, low


def edge_kernel(slc, estimate, direction, edge, fields):
    tiles = fields.shape[0]
    epochs = slc.shape[1]
    rows = slc.shape[2]
    look_rows = estimate.shape[1]
    lane = lax.broadcasted_iota(jnp.int32, (rows, LANES), 1)
    total = jnp.zeros((rows, LANES), jnp.float32)
    for part in range(2):
        for epoch in range(epochs):
            at = (part * epochs + epoch) * SIDES
            total = placed(lane, total, tile_of(slc, part, epoch, tiles - 1), LANES - RADIUS, at)
            total = placed(lane, total, tile_of(slc, part, epoch, 0), 0, at + RADIUS)
    edge[...] = total.astype(jnp.bfloat16)
    for tile in range(tiles):
        columns = slice(tile * LANES, (tile + 1) * LANES)
        for epoch in range(epochs):
            here = slice(epoch * look_rows, (epoch + 1) * look_rows)
            first, second = split_two(estimate[epoch, :, columns])
            fields[tile, 0, here, :] = first
            fields[tile, 1, here, :] = second
            fields[tile, 2, here, :] = direction[epoch, :, columns].astype(jnp.bfloat16)


def tile_of(slc, part, epoch, tile):
    return slc[part, epoch, :, tile * LANES : (tile + 1) * LANES].astype(jnp.float32)


def placed(lane, total, source, start, target):
    moved = pltpu.roll(source, (target - start) % LANES, axis=1)
    return jnp.where((lane >= target) & (lane < target + RADIUS), moved, total)


def pack_kernel(slc, params, left, right, message):
    tiles = message.shape[0]
    epochs = slc.shape[1]
    rows = slc.shape[2]
    lane = lax.broadcasted_iota(jnp.int32, (rows, LANES), 1)
    value = params[...]
    high = value.astype(jnp.bfloat16).astype(jnp.float32)
    middle = (value - high).astype(jnp.bfloat16).astype(jnp.float32)
    low = value - high - middle
    third = PARAM_LANE + 2 * SLOTS
    split = jnp.where(lane < third, high, jnp.where(lane < third + SLOTS, middle, low))
    split = jnp.where(lane >= PARAM_LANE, split, 0.0)
    for tile in range(tiles):
        total = split
        if tile == 0:
            total = total + left[...].astype(jnp.float32)
        if tile == tiles - 1:
            total = total + right[...].astype(jnp.float32)
        for part in range(2):
            for epoch in range(epochs):
                block = part * epochs + epoch
                at = block * SIDES
                if tile > 0:
                    total = placed(lane, total, tile_of(slc, part, epoch, tile - 1), LANES - RADIUS, at)
                if tile < tiles - 1:
                    total = placed(lane, total, tile_of(slc, part, epoch, tile + 1), 0, at + RADIUS)
                own = slc[part, epoch, :, tile * LANES : (tile + 1) * LANES]
                message[tile, block * rows : (block + 1) * rows, :] = own
        message[tile, 2 * epochs * rows :, :] = total.astype(jnp.bfloat16)


def main_kernel(sizes, partner, weight, present, *refs):
    tiles, epochs, rows = sizes
    message, fields, top, bottom, gradient, sums = refs[:6]
    full, rim_full, main, rim, looked, power, boxed, power_box, factors, est, old = refs[6:]
    look_rows = rows // LOOK
    tall = (rows + 2 * HALO) // LOOK
    halo_looks = HALO // LOOK
    total = tiles * epochs
    group = 2 * SLOTS
    has_top = present[0]
    has_bottom = present[1]
    f32 = jnp.float32

    band_from = lax.broadcasted_iota(jnp.int32, (2 * LANES, LANES), 0)
    band_to = lax.broadcasted_iota(jnp.int32, (2 * LANES, LANES), 1)
    rim_lane = band_from - LANES
    side = rim_lane % SIDES
    rim_column = jnp.where(side < RADIUS, side - RADIUS, LANES + side - RADIUS)
    rim_column = jnp.where(rim_lane < LOOK * SIDES, rim_column, 4 * LANES)
    column = jnp.where(band_from < LANES, band_from, rim_column)
    band = (jnp.abs(column - band_to) <= RADIUS).astype(f32).astype(jnp.bfloat16)
    out_at = lax.broadcasted_iota(jnp.int32, (group * look_rows, group * tall), 0)
    in_at = lax.broadcasted_iota(jnp.int32, (group * look_rows, group * tall), 1)
    near = jnp.abs(in_at % tall - halo_looks - out_at % look_rows) <= RADIUS
    near = near & (in_at // tall == out_at // look_rows)
    sum_rows = near.astype(f32).astype(jnp.bfloat16)

    lane = lax.broadcasted_iota(jnp.int32, (tall, LANES), 1)
    for block in range(tiles):
        for part in range(2):

            @pl.loop(0, epochs)
            def _(epoch):
                at = part * total + block * epochs + epoch
                row = pl.multiple_of((part * epochs + epoch) * HALO, HALO)
                full[at, :HALO] = top[block, pl.ds(row, HALO), :].astype(f32) * has_top
                own = pl.ds(pl.multiple_of((part * epochs + epoch) * rows, rows), rows)
                full[at, HALO : HALO + rows] = message[block, own, :].astype(f32)
                full[at, HALO + rows :] = bottom[block, pl.ds(row, HALO), :].astype(f32) * has_bottom

        last = slice(2 * epochs * HALO, 2 * epochs * HALO + HALO)
        rim_full[block, :HALO] = top[block, last, :].astype(f32) * has_top
        rim_full[block, HALO : HALO + rows] = message[block, 2 * epochs * rows :, :].astype(f32)
        rim_full[block, HALO + rows :] = bottom[block, last, :].astype(f32) * has_bottom

        @pl.loop(0, epochs)
        def _(epoch):
            here = pl.ds(pl.multiple_of(epoch * look_rows, look_rows), look_rows)
            est[block * epochs + epoch] = fields[block, 0, here, :].astype(f32) + fields[block, 1, here, :].astype(f32)
            old[block * epochs + epoch] = fields[block, 2, here, :].astype(f32)

    @pl.loop(0, 2 * total)
    def _(at):
        for look in range(LOOK):
            main[at, look] = full[at, pl.ds(look, tall, stride=LOOK), :]

    for block in range(tiles):
        by_look = [rim_full[block, pl.ds(look, tall, stride=LOOK), :] for look in range(LOOK)]
        for part in range(2):
            for epoch in range(epochs):
                start = (part * epochs + epoch) * SIDES
                value = jnp.zeros((tall, LANES), f32)
                for look in range(LOOK):
                    target = look * SIDES
                    moved = pltpu.roll(by_look[look], (target - start) % LANES, axis=1)
                    value = jnp.where((lane >= target) & (lane < target + SIDES), moved, value)
                rim[part * total + block * epochs + epoch] = value

    @pl.loop(0, total)
    def _(epoch):
        for piece in range(0, tall, 8):
            rows_at = slice(piece, piece + 8)
            own_re = [main[epoch, look, rows_at] for look in range(LOOK)]
            own_im = [main[total + epoch, look, rows_at] for look in range(LOOK)]
            rim_re = rim[epoch, rows_at]
            rim_im = rim[total + epoch, rows_at]
            value = own_re[0] * own_re[0] + own_im[0] * own_im[0]
            for look in range(1, LOOK):
                value = value + (own_re[look] * own_re[look] + own_im[look] * own_im[look])
            at = pl.multiple_of(epoch * tall + piece, 8)
            power[pl.ds(at, 8), :LANES] = value
            power[pl.ds(at, 8), LANES:] = rim_re * rim_re + rim_im * rim_im
            for slot in range(SLOTS):
                mate = partner[epoch * SLOTS + slot]
                real = None
                for look in range(LOOK):
                    mate_re = main[mate, look, rows_at]
                    mate_im = main[total + mate, look, rows_at]
                    one = own_re[look] * mate_re + own_im[look] * mate_im
                    two = own_im[look] * mate_re - own_re[look] * mate_im
                    real = one if real is None else real + one
                    imag = two if look == 0 else imag + two
                mate_re = rim[mate, rows_at]
                mate_im = rim[total + mate, rows_at]
                at = pl.multiple_of(epoch * (group * tall) + 2 * slot * tall + piece, 8)
                looked[pl.ds(at, 8), :LANES] = real
                looked[pl.ds(at, 8), LANES:] = rim_re * mate_re + rim_im * mate_im
                at = pl.multiple_of(epoch * (group * tall) + (2 * slot + 1) * tall + piece, 8)
                looked[pl.ds(at, 8), :LANES] = imag
                looked[pl.ds(at, 8), LANES:] = rim_im * mate_re - rim_re * mate_im

    def box(value):
        high, low = split_two(value)
        wide = jnp.dot(high, band, preferred_element_type=f32) + jnp.dot(low, band, preferred_element_type=f32)
        high, low = split_two(wide)
        return jnp.dot(sum_rows, high, preferred_element_type=f32) + jnp.dot(sum_rows, low, preferred_element_type=f32)

    for block in range(total // group):
        value = box(power[block * group * tall : (block + 1) * group * tall, :])
        for at in range(group):
            power_box[block * group + at] = value[at * look_rows : (at + 1) * look_rows]

    @pl.loop(0, total // 4)
    def _(quad):
        for extra in range(4):
            epoch = quad * 4 + extra
            at = pl.multiple_of(epoch * (group * tall), group * tall)
            boxed[epoch] = box(looked[pl.ds(at, group * tall), :])

    grad = gradient
    for block in range(tiles):
        grad[block] = jnp.zeros(grad.shape[1:], f32)

    def rows_of(epoch):
        return epoch // epochs, pl.ds(pl.multiple_of((epoch % epochs) * look_rows, look_rows), look_rows)

    @pl.loop(0, total)
    def _(epoch):
        own_power = power_box[epoch]
        own_est = est[epoch]
        own = jnp.zeros((look_rows, LANES), f32)
        for slot in range(SLOTS):
            mate = partner[epoch * SLOTS + slot]
            coh_re = boxed[epoch, 2 * slot * look_rows : (2 * slot + 1) * look_rows, :]
            coh_im = boxed[epoch, (2 * slot + 1) * look_rows : (2 * slot + 2) * look_rows, :]
            inverse = lax.rsqrt(own_power * power_box[mate] + EPSILON)
            unit_re = coh_re * inverse
            unit_im = coh_im * inverse
            factor = weight[epoch * SLOTS + slot] * (unit_re * unit_re + unit_im * unit_im)
            factors[epoch * SLOTS + slot] = factor
            weighted = factor * (unit_im - (own_est - est[mate]))
            own = own + weighted
            at, here = rows_of(mate)
            grad[at, here, :] = grad[at, here, :] - weighted
        at, here = rows_of(epoch)
        grad[at, here, :] = grad[at, here, :] + own

    def totals(epoch, carry):
        norm, crossed, grad_term, mixed, old_term = carry
        at, here = rows_of(epoch)
        own_grad = grad[at, here, :]
        own_old = old[epoch]
        norm = norm + own_grad * own_grad
        crossed = crossed + own_grad * own_old
        for slot in range(SLOTS):
            mate = partner[epoch * SLOTS + slot]
            factor = factors[epoch * SLOTS + slot]
            at, here = rows_of(mate)
            grad_spread = own_grad - grad[at, here, :]
            old_spread = own_old - old[mate]
            pulled = factor * grad_spread
            grad_term = grad_term + pulled * grad_spread
            mixed = mixed + pulled * old_spread
            old_term = old_term + factor * old_spread * old_spread
        return norm, crossed, grad_term, mixed, old_term

    zero = jnp.zeros((look_rows, LANES), f32)
    results = lax.fori_loop(0, total, totals, (zero,) * 5)
    sums[...] = jnp.zeros(sums.shape, f32)
    for at, value in enumerate(results):
        sums[at : at + 1, :] = jnp.sum(value, axis=0, keepdims=True)


def update_kernel(cell_count, prev_mean, estimate, direction, pieces, *refs):
    new_estimate, new_direction = refs[-2:]
    tiles = estimate.shape[2] // LANES
    scalars = refs[:-2]
    epochs = estimate.shape[0]
    look_rows = estimate.shape[1]
    total = scalars[0][...]
    for other in scalars[1:]:
        total = total + other[...]
    total = jnp.sum(total, axis=1, keepdims=True)
    grad_norm, crossed, grad_term, mixed, old_term = (total[at : at + 1, :] for at in range(5))
    momentum = grad_norm / cell_count / prev_mean[0]
    curvature = grad_term + 2.0 * momentum * mixed + momentum * momentum * old_term
    step = (grad_norm + momentum * crossed) / curvature
    momentum = jnp.broadcast_to(momentum, (look_rows, LANES))
    step = jnp.broadcast_to(step, (look_rows, LANES))
    for tile in range(tiles):
        columns = slice(tile * LANES, (tile + 1) * LANES)
        for epoch in range(epochs):
            gradient = pieces[tile, epoch * look_rows : (epoch + 1) * look_rows, :]
            moved = gradient + momentum * direction[epoch, :, columns]
            new_direction[epoch, :, columns] = moved
            new_estimate[epoch, :, columns] = estimate[epoch, :, columns] + step * moved


def swapped(up, down, axis):
    size = lax.axis_size(axis)
    if size == 1:
        return jnp.zeros_like(up), jnp.zeros_like(down)
    if size == 2:
        first = lax.axis_index(axis) == 0
        got = lax.ppermute(jnp.where(first, up, down), axis, [(0, 1), (1, 0)])
        return got, got
    forward = [(i, i + 1) for i in range(size - 1)]
    backward = [(target, source) for source, target in forward]
    return lax.ppermute(up, axis, forward), lax.ppermute(down, axis, backward)


def to_ahead(x, axis, by):
    size = lax.axis_size(axis)
    return lax.ppermute(x, axis, [(i, (i + by) % size) for i in range(size)])


def transposed_plan(slc, offsets, weights, estimate, direction, prev_mean):
    f32 = jnp.float32
    bf16 = jnp.bfloat16
    tiles = lax.axis_size("epoch")
    epochs, rows, columns = slc.shape[1:]
    look_rows = rows // LOOK
    total = tiles * epochs
    tall = (rows + 2 * HALO) // LOOK

    params = jnp.zeros((rows, LANES), f32)
    listed = jnp.concatenate([offsets.astype(f32), weights, weights, weights], axis=1)
    params = lax.dynamic_update_slice(params, listed, (0, PARAM_LANE))
    params_of = pltpu.CompilerParams(vmem_limit_bytes=VMEM_BYTES)
    edge, fields = pl.pallas_call(
        edge_kernel,
        out_shape=(
            jax.ShapeDtypeStruct((rows, LANES), bf16),
            jax.ShapeDtypeStruct((tiles, 3, epochs * look_rows, LANES), bf16),
        ),
        in_specs=[VMEM] * 3,
        out_specs=(VMEM,) * 2,
        compiler_params=params_of,
        cost_estimate=pl.CostEstimate(flops=1_000_000, bytes_accessed=2_000_000, transcendentals=0),
    )(slc, estimate, direction)

    before, after = swapped(edge, edge, "sub")
    sub = lax.axis_index("sub")
    lane = lax.broadcasted_iota(jnp.int32, (rows, LANES), 1)
    inside = lane < 2 * epochs * SIDES
    left = jnp.where(inside & (lane % SIDES < RADIUS) & (sub > 0), before, jnp.zeros_like(edge))
    right = inside & (lane % SIDES >= RADIUS) & (sub < lax.axis_size("sub") - 1)
    right = jnp.where(right, after, jnp.zeros_like(edge))
    message_rows = 2 * epochs * rows + rows
    message = pl.pallas_call(
        pack_kernel,
        out_shape=jax.ShapeDtypeStruct((tiles, message_rows, LANES), bf16),
        in_specs=[VMEM] * 4,
        out_specs=VMEM,
        compiler_params=params_of,
        cost_estimate=pl.CostEstimate(flops=3_000_000, bytes_accessed=2_000_000, transcendentals=0),
    )(slc, params, left, right)
    message = lax.all_to_all(message, "epoch", 0, 0)
    fields = lax.all_to_all(fields, "epoch", 0, 0)

    def border(from_row):
        blocks = message.reshape(tiles, 2 * epochs + 1, rows, LANES)
        return lax.dynamic_slice_in_dim(blocks, from_row, HALO, axis=2).reshape(tiles, (2 * epochs + 1) * HALO, LANES)

    space = lax.axis_index("space")
    spaces = lax.axis_size("space")
    if spaces == 2:
        mine = border(jnp.where(space == 0, rows - HALO, 0))
        top = bottom = lax.ppermute(mine, "space", [(0, 1), (1, 0)])
    else:
        top, bottom = swapped(border(rows - HALO), border(0), "space")
    present = jnp.stack([space > 0, space < spaces - 1]).astype(f32)

    listed = message[:, 2 * epochs * rows : 2 * epochs * rows + epochs, PARAM_LANE : PARAM_LANE + 4 * SLOTS]
    listed = listed.reshape(total, 4 * SLOTS).astype(f32)
    partner = jnp.arange(total, dtype=jnp.int32)[:, None] + listed[:, :SLOTS].astype(jnp.int32)
    partner = lax.rem(partner, total).reshape(-1)
    weight = listed[:, SLOTS : 2 * SLOTS] + listed[:, 2 * SLOTS : 3 * SLOTS] + listed[:, 3 * SLOTS :]
    group = 2 * SLOTS
    gradient, sums = pl.pallas_call(
        functools.partial(main_kernel, (tiles, epochs, rows)),
        out_shape=(
            jax.ShapeDtypeStruct((tiles, epochs * look_rows, LANES), f32),
            jax.ShapeDtypeStruct((8, LANES), f32),
        ),
        in_specs=[SMEM] * 3 + [VMEM] * 4,
        out_specs=(VMEM, VMEM),
        scratch_shapes=[
            pltpu.VMEM((2 * total, rows + 2 * HALO, LANES), f32),
            pltpu.VMEM((tiles, rows + 2 * HALO, LANES), f32),
            pltpu.VMEM((2 * total, LOOK, tall, LANES), f32),
            pltpu.VMEM((2 * total, tall, LANES), f32),
            pltpu.VMEM((total * group * tall, 2 * LANES), f32),
            pltpu.VMEM((total * tall, 2 * LANES), f32),
            pltpu.VMEM((total, group * look_rows, LANES), f32),
            pltpu.VMEM((total, look_rows, LANES), f32),
            pltpu.VMEM((total * SLOTS, look_rows, LANES), f32),
            pltpu.VMEM((total, look_rows, LANES), f32),
            pltpu.VMEM((total, look_rows, LANES), f32),
        ],
        compiler_params=params_of,
        cost_estimate=pl.CostEstimate(flops=40_000_000, bytes_accessed=4_000_000, transcendentals=0),
    )(partner, weight.reshape(-1), present, message, fields, top, bottom)

    returned = lax.all_to_all(gradient, "epoch", 0, 0)
    place = ("space", "sub")
    count = spaces * lax.axis_size("sub")
    shared = [sums] + [lax.ppermute(sums, place, [(i, (i + by) % count) for i in range(count)]) for by in range(1, count)]
    here = sum(shared[1:], shared[0])
    scalars = [here] + [to_ahead(here, "epoch", by) for by in range(1, tiles)]
    cell_count = float(total * look_rows * spaces * columns * lax.axis_size("sub"))
    return pl.pallas_call(
        functools.partial(update_kernel, cell_count),
        out_shape=(jax.ShapeDtypeStruct(estimate.shape, f32),) * 2,
        in_specs=[SMEM] + [VMEM] * (3 + tiles),
        out_specs=(VMEM, VMEM),
        compiler_params=params_of,
        cost_estimate=pl.CostEstimate(flops=1_000_000, bytes_accessed=2_000_000, transcendentals=0),
    )(prev_mean, estimate, direction, returned, *scalars)


def on_device(slc, offsets, weights, estimate, direction, prev_mean):
    epochs, rows, columns = slc.shape[1:]
    fits = columns == LANES * lax.axis_size("epoch") and lax.axis_size("epoch") > 1
    fits = fits and 2 * epochs * SIDES <= PARAM_LANE and rows % HALO == 0 and epochs * lax.axis_size("epoch") % (2 * SLOTS) == 0
    plan = transposed_plan if fits else ring_plan
    return plan(slc, offsets, weights, estimate, direction, prev_mean)


def solution(mesh):
    return jax.shard_map(
        on_device,
        mesh=mesh,
        in_specs=(
            P(None, ("groups", "epoch"), "space", "sub"),
            P(("groups", "epoch"), None),
            P(("groups", "epoch"), None),
            P(("groups", "epoch"), "space", "sub"),
            P(("groups", "epoch"), "space", "sub"),
            P(),
        ),
        out_specs=(P(("groups", "epoch"), "space", "sub"), P(("groups", "epoch"), "space", "sub")),
        check_vma=False,
    )
```

```python
import functools

import jax
import jax.numpy as jnp
from jax import lax
from jax.experimental import pallas as pl
from jax.experimental.pallas import tpu as pltpu
from jax.sharding import PartitionSpec as P

SLOTS = 4
OFFS = 8
LOOK = 4
RADIUS = 3


EPSILON = 1e-06


def passed_along(x, axis, by):
    size = lax.axis_size(axis)
    return lax.ppermute(x, axis, [(i, (i + by) % size) for i in range(size)])


def extended_2(block, sides, width):
    for axis, dim in sides:
        count = lax.axis_size(axis)
        forward = [(i, i + 1) for i in range(count - 1)]
        backward = [(target, source) for source, target in forward]
        low = lax.ppermute(
            lax.slice_in_dim(block, block.shape[dim] - width, None, axis=dim), axis, forward
        )
        high = lax.ppermute(lax.slice_in_dim(block, 0, width, axis=dim), axis, backward)
        block = jnp.concatenate([low, block, high], axis=dim)
    return block


def looked_sum(field):
    shape = field.shape
    return jnp.sum(field.reshape(shape[:-2] + (shape[-2] // LOOK, LOOK, shape[-1])), axis=-2)


def window_sum(padded, axis):
    length = padded.shape[axis] - 2 * RADIUS
    total = lax.slice_in_dim(padded, 0, length, axis=axis)
    for shift_at in range(1, 2 * RADIUS + 1):
        total = total + lax.slice_in_dim(padded, shift_at, shift_at + length, axis=axis)
    return total


def ring_plan(slc, offsets, weights, estimate, direction, prev_mean):
    epochs_here = slc.shape[1]
    look_rows = slc.shape[2] // LOOK
    col_count = slc.shape[3]
    ahead = passed_along(slc, "epoch", -1)
    extended = jnp.concatenate([slc, ahead], axis=1)
    numbers = jnp.arange(epochs_here, dtype=jnp.int32)
    partner = numbers[:, None] + offsets
    own_real = slc[0].astype(jnp.float32)
    own_imag = slc[1].astype(jnp.float32)
    ext_real = extended[0].astype(jnp.float32)
    ext_imag = extended[1].astype(jnp.float32)
    powers = looked_sum(ext_real * ext_real + ext_imag * ext_imag)
    pieces = []
    for slot_index in range(SLOTS):
        mate_real = jnp.take(ext_real, partner[:, slot_index], axis=0)
        mate_imag = jnp.take(ext_imag, partner[:, slot_index], axis=0)
        pieces.append(looked_sum(own_real * mate_real + own_imag * mate_imag))
        pieces.append(looked_sum(own_imag * mate_real - own_real * mate_imag))
    pair_count = epochs_here * 2 * SLOTS
    stacked = jnp.concatenate(
        [jnp.stack(pieces, axis=1).reshape(pair_count, look_rows, col_count), powers], axis=0
    )
    padded = extended_2(stacked, (("space", 1), ("sub", 2)), RADIUS)
    boxed = window_sum(window_sum(padded, 1), 2)
    pair_boxed = boxed[:pair_count].reshape(epochs_here, 2 * SLOTS, look_rows, col_count)
    power_box = boxed[pair_count:]
    coh_real = pair_boxed[:, 0::2]
    coh_imag = pair_boxed[:, 1::2]
    denominator = power_box[:epochs_here, None] * jnp.take(power_box, partner, axis=0) + EPSILON
    coherence = (coh_real * coh_real + coh_imag * coh_imag) / denominator
    observed = coh_imag / jnp.sqrt(denominator)
    est_ahead = passed_along(estimate, "epoch", -1)
    est_extended = jnp.concatenate([estimate, est_ahead], axis=0)
    fitted = estimate[:, None] - jnp.take(est_extended, partner, axis=0)
    factor = weights[:, :, None, None] * coherence
    weighted = factor * (observed - fitted)
    flattened = weighted.reshape(epochs_here * SLOTS, look_rows * col_count)
    selector = (
        jnp.arange(epochs_here + OFFS, dtype=jnp.int32)[:, None] == partner.reshape(1, -1)
    ).astype(jnp.float32)
    gathered = jnp.dot(
        selector, flattened, precision=lax.Precision.HIGHEST, preferred_element_type=jnp.float32
    ).reshape(epochs_here + OFFS, look_rows, col_count)
    own_part = jnp.sum(weighted, axis=1) - gathered[:epochs_here]
    returned = passed_along(-gathered[epochs_here:], "epoch", 1)
    gradient = jnp.concatenate([own_part + returned, own_part[OFFS:]], axis=0)
    cell_count = float(
        epochs_here
        * lax.axis_size("epoch")
        * look_rows
        * lax.axis_size("space")
        * col_count
        * lax.axis_size("sub")
    )
    local_norm = jnp.sum(gradient * gradient)
    local_crossed = jnp.sum(gradient * direction)
    mean_before = prev_mean[0]
    fields_ahead = passed_along(
        jnp.stack([gradient, direction]).astype(jnp.bfloat16), "epoch", -1
    ).astype(jnp.float32)
    grad_extended = jnp.concatenate([gradient, fields_ahead[0]], axis=0)
    old_extended = jnp.concatenate([direction, fields_ahead[1]], axis=0)
    grad_spread = gradient[:, None] - jnp.take(grad_extended, partner, axis=0)
    old_spread = direction[:, None] - jnp.take(old_extended, partner, axis=0)
    totals = lax.psum(
        (
            local_norm,
            local_crossed,
            jnp.sum(factor * grad_spread * grad_spread),
            jnp.sum(factor * grad_spread * old_spread),
            jnp.sum(factor * old_spread * old_spread),
        ),
        ("epoch", "space", "sub"),
    )
    grad_norm, crossed, grad_term, mixed_term, old_term = totals
    momentum = grad_norm / cell_count / mean_before
    new_direction = gradient + momentum * direction
    curvature = grad_term + 2.0 * momentum * mixed_term + momentum * momentum * old_term
    along_sum = grad_norm + momentum * crossed
    step_size = along_sum / curvature
    return (estimate + step_size * new_direction, new_direction)


LANES = 128
SIDES = 2 * RADIUS
HALO = 16
PARAM_LANE = 96
VMEM = pl.BlockSpec(memory_space=pltpu.VMEM)
SMEM = pl.BlockSpec(memory_space=pltpu.SMEM)
VMEM_BYTES = 48 * 1024 * 1024


def split_two(value):
    high = value.astype(jnp.bfloat16)
    low = (value - high.astype(jnp.float32)).astype(jnp.bfloat16)
    return high, low


def edge_kernel(slc, estimate, direction, edge, fields):
    tiles = fields.shape[0]
    epochs = slc.shape[1]
    rows = slc.shape[2]
    look_rows = estimate.shape[1]
    lane = lax.broadcasted_iota(jnp.int32, (rows, LANES), 1)
    total = jnp.zeros((rows, LANES), jnp.float32)
    for part in range(2):
        for epoch in range(epochs):
            at = (part * epochs + epoch) * SIDES
            total = placed(lane, total, tile_of(slc, part, epoch, tiles - 1), LANES - RADIUS, at)
            total = placed(lane, total, tile_of(slc, part, epoch, 0), 0, at + RADIUS)
    edge[...] = total.astype(jnp.bfloat16)
    for tile in range(tiles):
        columns = slice(tile * LANES, (tile + 1) * LANES)
        for epoch in range(epochs):
            here = slice(epoch * look_rows, (epoch + 1) * look_rows)
            first, second = split_two(estimate[epoch, :, columns])
            fields[tile, 0, here, :] = first
            fields[tile, 1, here, :] = second
            fields[tile, 2, here, :] = direction[epoch, :, columns].astype(jnp.bfloat16)


def tile_of(slc, part, epoch, tile):
    return slc[part, epoch, :, tile * LANES : (tile + 1) * LANES].astype(jnp.float32)


def placed(lane, total, source, start, target):
    moved = pltpu.roll(source, (target - start) % LANES, axis=1)
    return jnp.where((lane >= target) & (lane < target + RADIUS), moved, total)


def pack_kernel(slc, params, left, right, strips):
    tiles = strips.shape[0]
    epochs = slc.shape[1]
    rows = slc.shape[2]
    lane = lax.broadcasted_iota(jnp.int32, (rows, LANES), 1)
    value = params[...]
    high = value.astype(jnp.bfloat16).astype(jnp.float32)
    middle = (value - high).astype(jnp.bfloat16).astype(jnp.float32)
    low = value - high - middle
    third = PARAM_LANE + 2 * SLOTS
    split = jnp.where(lane < third, high, jnp.where(lane < third + SLOTS, middle, low))
    split = jnp.where(lane >= PARAM_LANE, split, 0.0)
    for tile in range(tiles):
        total = split
        if tile == 0:
            total = total + left[...].astype(jnp.float32)
        if tile == tiles - 1:
            total = total + right[...].astype(jnp.float32)
        for part in range(2):
            for epoch in range(epochs):
                at = (part * epochs + epoch) * SIDES
                if tile > 0:
                    total = placed(lane, total, tile_of(slc, part, epoch, tile - 1), LANES - RADIUS, at)
                if tile < tiles - 1:
                    total = placed(lane, total, tile_of(slc, part, epoch, tile + 1), 0, at + RADIUS)
        strips[tile] = total.astype(jnp.bfloat16)


def pair_kernel(sizes, places, partner, weight, present, *refs):
    epochs, rows, operands = sizes
    inputs = refs[:operands]
    factors, pulls = refs[operands : operands + 2]
    full, rim_full, main, rim, looked, rim_looked, power, rim_power, power_box = refs[operands + 2 :]
    count = len(places)
    look_rows = rows // LOOK
    tall = (rows + 2 * HALO) // LOOK
    halo_looks = HALO // LOOK
    total = count * epochs
    own_total = total - epochs
    group = 2 * SLOTS
    share = LANES // SLOTS
    has_top = present[0]
    has_bottom = present[1]
    f32 = jnp.float32

    def band_of(shape, from_of, to_of):
        at = lax.broadcasted_iota(jnp.int32, shape, 0)
        to = lax.broadcasted_iota(jnp.int32, shape, 1)
        return (jnp.abs(from_of(at, to) - to_of(to)) <= RADIUS).astype(f32).astype(jnp.bfloat16)

    def rim_column(at, to):
        at = at % LANES
        side = at % share % SIDES
        column = jnp.where(side < RADIUS, side - RADIUS, LANES + side - RADIUS)
        inside = (at // share == to // LANES) & (at % share < LOOK * SIDES)
        return jnp.where(inside, column, -4 * LANES)

    band = band_of((2 * LANES, LANES), lambda at, to: at % LANES, lambda to: to)
    rim_band = band_of((2 * LANES, SLOTS * LANES), rim_column, lambda to: to % LANES)
    out_at = lax.broadcasted_iota(jnp.int32, (group * look_rows, group * tall), 0)
    in_at = lax.broadcasted_iota(jnp.int32, (group * look_rows, group * tall), 1)
    near = jnp.abs(in_at % tall - halo_looks - out_at % look_rows) <= RADIUS
    near = near & (in_at // tall == out_at // look_rows)
    sum_rows = near.astype(f32).astype(jnp.bfloat16)

    lane = lax.broadcasted_iota(jnp.int32, (tall, LANES), 1)
    for block, (tile_at, strip_at, strip_row, top_at, bottom_at, halo_slot) in enumerate(places):
        tile, strip, top, bottom = inputs[tile_at], inputs[strip_at], inputs[top_at], inputs[bottom_at]
        for part in range(2):

            @pl.loop(0, epochs)
            def _(epoch):
                at = part * total + block * epochs + epoch
                row = pl.multiple_of((part * epochs + epoch) * HALO, HALO)
                own = pl.multiple_of((part * epochs + epoch) * rows, rows)
                full[at, :HALO] = top[halo_slot, pl.ds(row, HALO), :].astype(f32) * has_top
                full[at, HALO : HALO + rows] = tile[pl.ds(own, rows), :].astype(f32)
                full[at, HALO + rows :] = bottom[halo_slot, pl.ds(row, HALO), :].astype(f32) * has_bottom

        last = slice(2 * epochs * HALO, 2 * epochs * HALO + HALO)
        rim_full[block, :HALO] = top[halo_slot, last, :].astype(f32) * has_top
        rim_full[block, HALO : HALO + rows] = strip[strip_row : strip_row + rows, :].astype(f32)
        rim_full[block, HALO + rows :] = bottom[halo_slot, last, :].astype(f32) * has_bottom

    @pl.loop(0, 2 * total)
    def _(at):
        for look in range(LOOK):
            main[at, look] = full[at, pl.ds(look, tall, stride=LOOK), :]

    for block in range(count):
        by_look = [rim_full[block, pl.ds(look, tall, stride=LOOK), :] for look in range(LOOK)]
        for part in range(2):
            for epoch in range(epochs):
                start = (part * epochs + epoch) * SIDES
                value = jnp.zeros((tall, LANES), f32)
                for look in range(LOOK):
                    target = look * SIDES
                    moved = pltpu.roll(by_look[look], (target - start) % LANES, axis=1)
                    value = jnp.where((lane >= target) & (lane < target + SIDES), moved, value)
                spread = share
                while spread < LANES:
                    value = value + pltpu.roll(value, spread, axis=1)
                    spread = 2 * spread
                rim[part * total + block * epochs + epoch] = value

    piece_lane = lax.broadcasted_iota(jnp.int32, (8, LANES), 1)
    slot_lane = [piece_lane // share == slot for slot in range(SLOTS)]

    def mixed(values):
        result = values[-1]
        for slot in range(SLOTS - 1):
            result = jnp.where(slot_lane[slot], values[slot], result)
        return result

    @pl.loop(0, total // SLOTS)
    def _(quad):
        for piece in range(0, tall, 8):
            rows_at = slice(piece, piece + 8)
            squares = []
            for extra in range(SLOTS):
                epoch = quad * SLOTS + extra
                value = None
                for look in range(LOOK):
                    real = main[epoch, look, rows_at]
                    imag = main[total + epoch, look, rows_at]
                    one = real * real + imag * imag
                    value = one if value is None else value + one
                power[pl.ds(pl.multiple_of(epoch * tall + piece, 8), 8), :] = value
                real = rim[epoch, rows_at]
                imag = rim[total + epoch, rows_at]
                squares.append(real * real + imag * imag)
            rim_power[pl.ds(pl.multiple_of(quad * tall + piece, 8), 8), :] = mixed(squares)

    @pl.loop(0, own_total)
    def _(epoch):
        mates = [partner[epoch * SLOTS + slot] for slot in range(SLOTS)]
        for piece in range(0, tall, 8):
            rows_at = slice(piece, piece + 8)
            own_re = [main[epoch, look, rows_at] for look in range(LOOK)]
            own_im = [main[total + epoch, look, rows_at] for look in range(LOOK)]
            for slot, mate in enumerate(mates):
                real = None
                for look in range(LOOK):
                    mate_re = main[mate, look, rows_at]
                    mate_im = main[total + mate, look, rows_at]
                    one = own_re[look] * mate_re + own_im[look] * mate_im
                    two = own_im[look] * mate_re - own_re[look] * mate_im
                    real = one if real is None else real + one
                    imag = two if look == 0 else imag + two
                at = pl.multiple_of(epoch * (group * tall) + 2 * slot * tall + piece, 8)
                looked[pl.ds(at, 8), :] = real
                at = pl.multiple_of(epoch * (group * tall) + (2 * slot + 1) * tall + piece, 8)
                looked[pl.ds(at, 8), :] = imag
            rim_re = rim[epoch, rows_at]
            rim_im = rim[total + epoch, rows_at]
            mate_re = mixed([rim[mate, rows_at] for mate in mates])
            mate_im = mixed([rim[total + mate, rows_at] for mate in mates])
            at = pl.multiple_of(epoch * (2 * tall) + piece, 8)
            rim_looked[pl.ds(at, 8), :] = rim_re * mate_re + rim_im * mate_im
            at = pl.multiple_of(epoch * (2 * tall) + tall + piece, 8)
            rim_looked[pl.ds(at, 8), :] = rim_im * mate_re - rim_re * mate_im

    def box(value, rim_value, by_slot):
        wide = jnp.dot(jnp.concatenate(split_two(value), axis=1), band, preferred_element_type=f32)
        outer = jnp.dot(jnp.concatenate(split_two(rim_value), axis=1), rim_band, preferred_element_type=f32)
        order = []
        for at in range(group):
            half, slot = (at % 2, at // 2) if by_slot else (at // SLOTS, at % SLOTS)
            order.append(outer[half * tall : (half + 1) * tall, slot * LANES : (slot + 1) * LANES])
        high, low = split_two(wide + jnp.concatenate(order, axis=0))
        return jnp.dot(sum_rows, high, preferred_element_type=f32) + jnp.dot(sum_rows, low, preferred_element_type=f32)

    for block in range(total // group):
        here = slice(block * group * tall, (block + 1) * group * tall)
        value = box(power[here, :], rim_power[2 * block * tall : 2 * (block + 1) * tall, :], False)
        for at in range(group):
            power_box[block * group + at] = value[at * look_rows : (at + 1) * look_rows]

    @pl.loop(0, own_total // 4)
    def _(quad):
        for extra in range(4):
            epoch = quad * 4 + extra
            at = pl.multiple_of(epoch * (group * tall), group * tall)
            rim_at = pl.multiple_of(epoch * (2 * tall), 2 * tall)
            boxed = box(looked[pl.ds(at, group * tall), :], rim_looked[pl.ds(rim_at, 2 * tall), :], True)
            own_power = power_box[epoch]
            for slot in range(SLOTS):
                pair = epoch * SLOTS + slot
                coh_re = boxed[2 * slot * look_rows : (2 * slot + 1) * look_rows, :]
                coh_im = boxed[(2 * slot + 1) * look_rows : (2 * slot + 2) * look_rows, :]
                inverse = lax.rsqrt(own_power * power_box[partner[pair]] + EPSILON)
                unit_re = coh_re * inverse
                unit_im = coh_im * inverse
                factor = weight[pair] * (unit_re * unit_re + unit_im * unit_im)
                factors[pair] = factor
                pulls[pair] = factor * unit_im


def gradient_kernel(sizes, partner, *refs):
    tiles, epochs, stages = sizes
    fields = refs[:tiles]
    factors = refs[tiles : tiles + len(stages)]
    pulls = refs[tiles + len(stages) : tiles + 2 * len(stages)]
    gradient, sums, est, old = refs[tiles + 2 * len(stages) :]
    look_rows = est.shape[1]
    total = tiles * epochs
    f32 = jnp.float32
    for block in range(tiles):

        @pl.loop(0, epochs)
        def _(epoch):
            here = pl.ds(pl.multiple_of(epoch * look_rows, look_rows), look_rows)
            est[block * epochs + epoch] = fields[block][0, here, :].astype(f32) + fields[block][1, here, :].astype(f32)
            old[block * epochs + epoch] = fields[block][2, here, :].astype(f32)

    @pl.loop(0, total)
    def _(epoch):
        gradient[epoch] = jnp.zeros((look_rows, LANES), f32)

    for stage, own_blocks in enumerate(stages):
        for number, block in enumerate(own_blocks):

            @pl.loop(0, epochs)
            def _(here):
                epoch = block * epochs + here
                own_est = est[epoch]
                own = jnp.zeros((look_rows, LANES), f32)
                for slot in range(SLOTS):
                    mate = partner[epoch * SLOTS + slot]
                    pair = (number * epochs + here) * SLOTS + slot
                    weighted = pulls[stage][pair] - factors[stage][pair] * (own_est - est[mate])
                    own = own + weighted
                    gradient[mate] = gradient[mate] - weighted
                gradient[epoch] = gradient[epoch] + own

    zero = jnp.zeros((look_rows, LANES), f32)
    results = (zero,) * 5
    for stage, own_blocks in enumerate(stages):
        for number, block in enumerate(own_blocks):

            def totals(here, carry):
                norm, crossed, grad_term, mixed, old_term = carry
                epoch = block * epochs + here
                own_grad = gradient[epoch]
                own_old = old[epoch]
                norm = norm + own_grad * own_grad
                crossed = crossed + own_grad * own_old
                for slot in range(SLOTS):
                    mate = partner[epoch * SLOTS + slot]
                    factor = factors[stage][(number * epochs + here) * SLOTS + slot]
                    grad_spread = own_grad - gradient[mate]
                    old_spread = own_old - old[mate]
                    pulled = factor * grad_spread
                    grad_term = grad_term + pulled * grad_spread
                    mixed = mixed + pulled * old_spread
                    old_term = old_term + factor * old_spread * old_spread
                return norm, crossed, grad_term, mixed, old_term

            results = lax.fori_loop(0, epochs, totals, results)
    sums[...] = jnp.zeros(sums.shape, f32)
    for at, value in enumerate(results):
        sums[at : at + 1, :] = jnp.sum(value, axis=0, keepdims=True)


def update_kernel(cell_count, me, prev_mean, estimate, direction, *refs):
    new_estimate, new_direction = refs[-2:]
    tiles = estimate.shape[2] // LANES
    pieces = refs[:tiles]
    scalars = refs[tiles:-2]
    epochs = estimate.shape[0]
    look_rows = estimate.shape[1]
    total = scalars[0][...]
    for other in scalars[1:]:
        total = total + other[...]
    total = jnp.sum(total, axis=1, keepdims=True)
    grad_norm, crossed, grad_term, mixed, old_term = (total[at : at + 1, :] for at in range(5))
    momentum = grad_norm / cell_count / prev_mean[0]
    curvature = grad_term + 2.0 * momentum * mixed + momentum * momentum * old_term
    step = (grad_norm + momentum * crossed) / curvature
    momentum = jnp.broadcast_to(momentum, (look_rows, LANES))
    step = jnp.broadcast_to(step, (look_rows, LANES))
    for shift, piece in enumerate(pieces):
        tile = lax.rem(me[0] - shift + tiles, tiles)
        columns = pl.ds(pl.multiple_of(tile * LANES, LANES), LANES)
        for epoch in range(epochs):
            gradient = piece[epoch]
            moved = gradient + momentum * direction[epoch, :, columns]
            new_direction[epoch, :, columns] = moved
            new_estimate[epoch, :, columns] = estimate[epoch, :, columns] + step * moved


def swapped(up, down, axis):
    size = lax.axis_size(axis)
    if size == 1:
        return jnp.zeros_like(up), jnp.zeros_like(down)
    if size == 2:
        first = lax.axis_index(axis) == 0
        got = lax.ppermute(jnp.where(first, up, down), axis, [(0, 1), (1, 0)])
        return got, got
    forward = [(i, i + 1) for i in range(size - 1)]
    backward = [(target, source) for source, target in forward]
    return lax.ppermute(up, axis, forward), lax.ppermute(down, axis, backward)


def to_ahead(x, axis, by):
    size = lax.axis_size(axis)
    return lax.ppermute(x, axis, [(i, (i + by) % size) for i in range(size)])


def transposed_plan(slc, offsets, weights, estimate, direction, prev_mean):
    f32 = jnp.float32
    bf16 = jnp.bfloat16
    tiles = lax.axis_size("epoch")
    me = lax.axis_index("epoch")
    epochs, rows, columns = slc.shape[1:]
    look_rows = rows // LOOK
    total = tiles * epochs
    tall = (rows + 2 * HALO) // LOOK
    tile_rows = 2 * epochs * rows
    params_of = pltpu.CompilerParams(vmem_limit_bytes=VMEM_BYTES)

    def for_device(shift):
        return lax.rem(me + shift, tiles)

    def tile_for(shift):
        return lax.dynamic_slice_in_dim(slc, for_device(shift) * LANES, LANES, axis=3).reshape(tile_rows, LANES)

    def fetched(send, shift):
        return to_ahead(send(tiles - shift), "epoch", tiles - shift)

    beside = [tiles - 1, 0, 1]
    far = list(range(2, tiles - 1))
    tile = {0: tile_for(0), 1: fetched(tile_for, 1), tiles - 1: fetched(tile_for, tiles - 1)}

    params = jnp.zeros((rows, LANES), f32)
    listed = jnp.concatenate([offsets.astype(f32), weights, weights, weights], axis=1)
    params = lax.dynamic_update_slice(params, listed, (0, PARAM_LANE))
    edge, fields = pl.pallas_call(
        edge_kernel,
        out_shape=(
            jax.ShapeDtypeStruct((rows, LANES), bf16),
            jax.ShapeDtypeStruct((tiles, 3, epochs * look_rows, LANES), bf16),
        ),
        in_specs=[VMEM] * 3,
        out_specs=(VMEM,) * 2,
        compiler_params=params_of,
        cost_estimate=pl.CostEstimate(flops=1_000_000, bytes_accessed=2_000_000, transcendentals=0),
    )(slc, estimate, direction)
    before, after = swapped(edge, edge, "sub")
    sub = lax.axis_index("sub")
    lane = lax.broadcasted_iota(jnp.int32, (rows, LANES), 1)
    inside = lane < 2 * epochs * SIDES
    left = jnp.where(inside & (lane % SIDES < RADIUS) & (sub > 0), before, jnp.zeros_like(edge))
    right = inside & (lane % SIDES >= RADIUS) & (sub < lax.axis_size("sub") - 1)
    right = jnp.where(right, after, jnp.zeros_like(edge))
    strips = pl.pallas_call(
        pack_kernel,
        out_shape=jax.ShapeDtypeStruct((tiles, rows, LANES), bf16),
        in_specs=[VMEM] * 4,
        out_specs=VMEM,
        compiler_params=params_of,
        cost_estimate=pl.CostEstimate(flops=3_000_000, bytes_accessed=2_000_000, transcendentals=0),
    )(slc, params, left, right)

    def strip_for(shift):
        return lax.dynamic_index_in_dim(strips, for_device(shift), axis=0, keepdims=False)

    def field_for(shift):
        return lax.dynamic_index_in_dim(fields, for_device(shift), axis=0, keepdims=False)

    def both_for(shift):
        return jnp.concatenate([tile_for(shift), strip_for(shift)], axis=0)

    strip = {0: strip_for(0), 1: fetched(strip_for, 1), tiles - 1: fetched(strip_for, tiles - 1)}
    both = {block: fetched(both_for, block) for block in far}
    field = {0: field_for(0)}
    fields = lax.optimization_barrier((fields, tile[1], tile[tiles - 1]))[0]
    for block in [1, tiles - 1] + far:
        field[block] = fetched(field_for, block)

    space = lax.axis_index("space")
    spaces = lax.axis_size("space")
    present = jnp.stack([space > 0, space < spaces - 1]).astype(f32)

    def halo(blocks):
        def border(from_row):
            parts = []
            for block in blocks:
                if block in tile:
                    own = tile[block].reshape(2 * epochs, rows, LANES)
                    rim = strip[block].reshape(1, rows, LANES)
                    pieces = [own, rim]
                else:
                    pieces = [both[block].reshape(2 * epochs + 1, rows, LANES)]
                for piece in pieces:
                    cut = lax.dynamic_slice_in_dim(piece, from_row, HALO, axis=1)
                    parts.append(cut.reshape(-1, LANES))
            return jnp.concatenate(parts, axis=0).reshape(len(blocks), (2 * epochs + 1) * HALO, LANES)

        if spaces == 2:
            mine = border(jnp.where(space == 0, rows - HALO, 0))
            got = lax.ppermute(mine, "space", [(0, 1), (1, 0)])
            return got, got
        return swapped(border(rows - HALO), border(0), "space")

    def params_in(block):
        source = strip[block] if block in strip else both[block][tile_rows:]
        return source[:epochs, PARAM_LANE : PARAM_LANE + 4 * SLOTS].astype(f32)

    def pairs_of(blocks, loaded):
        listed = jnp.concatenate([params_in(block) for block in blocks], axis=0)
        mate = jnp.arange(len(blocks) * epochs, dtype=jnp.int32)[:, None] + listed[:, :SLOTS].astype(jnp.int32)
        weight = listed[:, SLOTS : 2 * SLOTS] + listed[:, 2 * SLOTS : 3 * SLOTS] + listed[:, 3 * SLOTS :]
        return mate.reshape(-1), weight.reshape(-1)

    near_halo = halo(beside)
    def pair_stage(loaded):
        own = loaded[:-1]
        mate, weight = pairs_of(own, loaded)
        operands = []

        def index_of(array):
            for at, other in enumerate(operands):
                if other is array:
                    return at
            operands.append(array)
            return len(operands) - 1

        places = []
        for block in loaded:
            if block in tile:
                at = index_of(tile[block]), index_of(strip[block]), 0
            else:
                at = index_of(both[block]), index_of(both[block]), tile_rows
            source, slots = (near_halo, beside) if block in beside else (far_halo, far)
            places.append(at + (index_of(source[0]), index_of(source[1]), slots.index(block)))
        here = len(loaded) * epochs
        owned = len(own) * epochs
        group = 2 * SLOTS
        shape = jax.ShapeDtypeStruct((owned * SLOTS, look_rows, LANES), f32)
        return pl.pallas_call(
            functools.partial(pair_kernel, (epochs, rows, len(operands)), tuple(places)),
            out_shape=(shape, shape),
            in_specs=[SMEM] * 3 + [VMEM] * len(operands),
            out_specs=(VMEM, VMEM),
            scratch_shapes=[
                pltpu.VMEM((2 * here, rows + 2 * HALO, LANES), f32),
                pltpu.VMEM((len(loaded), rows + 2 * HALO, LANES), f32),
                pltpu.VMEM((2 * here, LOOK, tall, LANES), f32),
                pltpu.VMEM((2 * here, tall, LANES), f32),
                pltpu.VMEM((owned * group * tall, LANES), f32),
                pltpu.VMEM((owned * 2 * tall, LANES), f32),
                pltpu.VMEM((here * tall, LANES), f32),
                pltpu.VMEM((here // SLOTS * tall, LANES), f32),
                pltpu.VMEM((here, look_rows, LANES), f32),
            ],
            compiler_params=params_of,
            cost_estimate=pl.CostEstimate(flops=20_000_000, bytes_accessed=30_000_000, transcendentals=0),
        )(mate, weight, present, *operands)

    near_stage = beside
    far_stage = list(range(1, tiles))
    near_pairs = pair_stage(near_stage)
    both, near_pairs = lax.optimization_barrier((both, near_pairs))
    far_halo = halo(far)
    far_pairs = pair_stage(far_stage)

    listed = jnp.concatenate([params_in(block) for block in range(tiles)], axis=0)
    partner = jnp.arange(total, dtype=jnp.int32)[:, None] + listed[:, :SLOTS].astype(jnp.int32)
    partner = lax.rem(partner, total).reshape(-1)
    stages = (tuple(near_stage[:-1]), tuple(far_stage[:-1]))
    gradient, sums = pl.pallas_call(
        functools.partial(gradient_kernel, (tiles, epochs, stages)),
        out_shape=(
            jax.ShapeDtypeStruct((total, look_rows, LANES), f32),
            jax.ShapeDtypeStruct((8, LANES), f32),
        ),
        in_specs=[SMEM] + [VMEM] * (tiles + 4),
        out_specs=(VMEM, VMEM),
        scratch_shapes=[pltpu.VMEM((total, look_rows, LANES), f32)] * 2,
        compiler_params=params_of,
        cost_estimate=pl.CostEstimate(flops=10_000_000, bytes_accessed=8_000_000, transcendentals=0),
    )(partner, *[field[block] for block in range(tiles)], near_pairs[0], far_pairs[0], near_pairs[1], far_pairs[1])

    place = ("space", "sub")
    count = spaces * lax.axis_size("sub")
    shared = [sums] + [lax.ppermute(sums, place, [(i, (i + by) % count) for i in range(count)]) for by in range(1, count)]
    here = sum(shared[1:], shared[0])
    scalars = [here] + [to_ahead(here, "epoch", by) for by in range(1, tiles)]
    returned = [gradient[:epochs]]
    returned += [to_ahead(gradient[by * epochs : (by + 1) * epochs], "epoch", by) for by in range(1, tiles)]
    cell_count = float(total * look_rows * spaces * columns * lax.axis_size("sub"))
    return pl.pallas_call(
        functools.partial(update_kernel, cell_count),
        out_shape=(jax.ShapeDtypeStruct(estimate.shape, f32),) * 2,
        in_specs=[SMEM] * 2 + [VMEM] * (2 + 2 * tiles),
        out_specs=(VMEM, VMEM),
        compiler_params=params_of,
        cost_estimate=pl.CostEstimate(flops=1_000_000, bytes_accessed=2_000_000, transcendentals=0),
    )(me.reshape(1), prev_mean, estimate, direction, *returned, *scalars)


def on_device(slc, offsets, weights, estimate, direction, prev_mean):
    epochs, rows, columns = slc.shape[1:]
    fits = columns == LANES * lax.axis_size("epoch") and lax.axis_size("epoch") > 3
    fits = fits and 2 * epochs * SIDES <= PARAM_LANE and rows % HALO == 0 and epochs % (2 * SLOTS) == 0
    plan = transposed_plan if fits else ring_plan
    return plan(slc, offsets, weights, estimate, direction, prev_mean)


def solution(mesh):
    return jax.shard_map(
        on_device,
        mesh=mesh,
        in_specs=(
            P(None, ("groups", "epoch"), "space", "sub"),
            P(("groups", "epoch"), None),
            P(("groups", "epoch"), None),
            P(("groups", "epoch"), "space", "sub"),
            P(("groups", "epoch"), "space", "sub"),
            P(),
        ),
        out_specs=(P(("groups", "epoch"), "space", "sub"), P(("groups", "epoch"), "space", "sub")),
        check_vma=False,
    )
```

```python
import functools

import jax
import jax.numpy as jnp
from jax import lax
from jax.experimental import pallas as pl
from jax.experimental.pallas import tpu as pltpu
from jax.sharding import PartitionSpec as P

SLOTS = 4
OFFS = 8
LOOK = 4
RADIUS = 3


EPSILON = 1e-06


def passed_along(x, axis, by):
    size = lax.axis_size(axis)
    return lax.ppermute(x, axis, [(i, (i + by) % size) for i in range(size)])


def extended_2(block, sides, width):
    for axis, dim in sides:
        count = lax.axis_size(axis)
        forward = [(i, i + 1) for i in range(count - 1)]
        backward = [(target, source) for source, target in forward]
        low = lax.ppermute(
            lax.slice_in_dim(block, block.shape[dim] - width, None, axis=dim), axis, forward
        )
        high = lax.ppermute(lax.slice_in_dim(block, 0, width, axis=dim), axis, backward)
        block = jnp.concatenate([low, block, high], axis=dim)
    return block


def looked_sum(field):
    shape = field.shape
    return jnp.sum(field.reshape(shape[:-2] + (shape[-2] // LOOK, LOOK, shape[-1])), axis=-2)


def window_sum(padded, axis):
    length = padded.shape[axis] - 2 * RADIUS
    total = lax.slice_in_dim(padded, 0, length, axis=axis)
    for shift_at in range(1, 2 * RADIUS + 1):
        total = total + lax.slice_in_dim(padded, shift_at, shift_at + length, axis=axis)
    return total


def ring_plan(slc, offsets, weights, estimate, direction, prev_mean):
    epochs_here = slc.shape[1]
    look_rows = slc.shape[2] // LOOK
    col_count = slc.shape[3]
    ahead = passed_along(slc, "epoch", -1)
    extended = jnp.concatenate([slc, ahead], axis=1)
    numbers = jnp.arange(epochs_here, dtype=jnp.int32)
    partner = numbers[:, None] + offsets
    own_real = slc[0].astype(jnp.float32)
    own_imag = slc[1].astype(jnp.float32)
    ext_real = extended[0].astype(jnp.float32)
    ext_imag = extended[1].astype(jnp.float32)
    powers = looked_sum(ext_real * ext_real + ext_imag * ext_imag)
    pieces = []
    for slot_index in range(SLOTS):
        mate_real = jnp.take(ext_real, partner[:, slot_index], axis=0)
        mate_imag = jnp.take(ext_imag, partner[:, slot_index], axis=0)
        pieces.append(looked_sum(own_real * mate_real + own_imag * mate_imag))
        pieces.append(looked_sum(own_imag * mate_real - own_real * mate_imag))
    pair_count = epochs_here * 2 * SLOTS
    stacked = jnp.concatenate(
        [jnp.stack(pieces, axis=1).reshape(pair_count, look_rows, col_count), powers], axis=0
    )
    padded = extended_2(stacked, (("space", 1), ("sub", 2)), RADIUS)
    boxed = window_sum(window_sum(padded, 1), 2)
    pair_boxed = boxed[:pair_count].reshape(epochs_here, 2 * SLOTS, look_rows, col_count)
    power_box = boxed[pair_count:]
    coh_real = pair_boxed[:, 0::2]
    coh_imag = pair_boxed[:, 1::2]
    denominator = power_box[:epochs_here, None] * jnp.take(power_box, partner, axis=0) + EPSILON
    coherence = (coh_real * coh_real + coh_imag * coh_imag) / denominator
    observed = coh_imag / jnp.sqrt(denominator)
    est_ahead = passed_along(estimate, "epoch", -1)
    est_extended = jnp.concatenate([estimate, est_ahead], axis=0)
    fitted = estimate[:, None] - jnp.take(est_extended, partner, axis=0)
    factor = weights[:, :, None, None] * coherence
    weighted = factor * (observed - fitted)
    flattened = weighted.reshape(epochs_here * SLOTS, look_rows * col_count)
    selector = (
        jnp.arange(epochs_here + OFFS, dtype=jnp.int32)[:, None] == partner.reshape(1, -1)
    ).astype(jnp.float32)
    gathered = jnp.dot(
        selector, flattened, precision=lax.Precision.HIGHEST, preferred_element_type=jnp.float32
    ).reshape(epochs_here + OFFS, look_rows, col_count)
    own_part = jnp.sum(weighted, axis=1) - gathered[:epochs_here]
    returned = passed_along(-gathered[epochs_here:], "epoch", 1)
    gradient = jnp.concatenate([own_part + returned, own_part[OFFS:]], axis=0)
    cell_count = float(
        epochs_here
        * lax.axis_size("epoch")
        * look_rows
        * lax.axis_size("space")
        * col_count
        * lax.axis_size("sub")
    )
    local_norm = jnp.sum(gradient * gradient)
    local_crossed = jnp.sum(gradient * direction)
    mean_before = prev_mean[0]
    fields_ahead = passed_along(
        jnp.stack([gradient, direction]).astype(jnp.bfloat16), "epoch", -1
    ).astype(jnp.float32)
    grad_extended = jnp.concatenate([gradient, fields_ahead[0]], axis=0)
    old_extended = jnp.concatenate([direction, fields_ahead[1]], axis=0)
    grad_spread = gradient[:, None] - jnp.take(grad_extended, partner, axis=0)
    old_spread = direction[:, None] - jnp.take(old_extended, partner, axis=0)
    totals = lax.psum(
        (
            local_norm,
            local_crossed,
            jnp.sum(factor * grad_spread * grad_spread),
            jnp.sum(factor * grad_spread * old_spread),
            jnp.sum(factor * old_spread * old_spread),
        ),
        ("epoch", "space", "sub"),
    )
    grad_norm, crossed, grad_term, mixed_term, old_term = totals
    momentum = grad_norm / cell_count / mean_before
    new_direction = gradient + momentum * direction
    curvature = grad_term + 2.0 * momentum * mixed_term + momentum * momentum * old_term
    along_sum = grad_norm + momentum * crossed
    step_size = along_sum / curvature
    return (estimate + step_size * new_direction, new_direction)


LANES = 128
SIDES = 2 * RADIUS
HALO = 16
PARAM_LANE = 96
VMEM = pl.BlockSpec(memory_space=pltpu.VMEM)
SMEM = pl.BlockSpec(memory_space=pltpu.SMEM)
VMEM_BYTES = 48 * 1024 * 1024


def split_two(value):
    high = value.astype(jnp.bfloat16)
    low = (value - high.astype(jnp.float32)).astype(jnp.bfloat16)
    return high, low


def edge_kernel(slc, estimate, direction, edge, fields):
    tiles = fields.shape[0]
    epochs = slc.shape[1]
    rows = slc.shape[2]
    look_rows = estimate.shape[1]
    lane = lax.broadcasted_iota(jnp.int32, (rows, LANES), 1)
    total = jnp.zeros((rows, LANES), jnp.float32)
    for part in range(2):
        for epoch in range(epochs):
            at = (part * epochs + epoch) * SIDES
            total = placed(lane, total, tile_of(slc, part, epoch, tiles - 1), LANES - RADIUS, at)
            total = placed(lane, total, tile_of(slc, part, epoch, 0), 0, at + RADIUS)
    edge[...] = total.astype(jnp.bfloat16)
    for tile in range(tiles):
        columns = slice(tile * LANES, (tile + 1) * LANES)
        for epoch in range(epochs):
            here = slice(epoch * look_rows, (epoch + 1) * look_rows)
            first, second = split_two(estimate[epoch, :, columns])
            fields[tile, 0, here, :] = first
            fields[tile, 1, here, :] = second
            fields[tile, 2, here, :] = direction[epoch, :, columns].astype(jnp.bfloat16)


def tile_of(slc, part, epoch, tile):
    return slc[part, epoch, :, tile * LANES : (tile + 1) * LANES].astype(jnp.float32)


def placed(lane, total, source, start, target):
    moved = pltpu.roll(source, (target - start) % LANES, axis=1)
    return jnp.where((lane >= target) & (lane < target + RADIUS), moved, total)


def pack_kernel(slc, params, left, right, strips):
    tiles = strips.shape[0]
    epochs = slc.shape[1]
    rows = slc.shape[2]
    lane = lax.broadcasted_iota(jnp.int32, (rows, LANES), 1)
    value = params[...]
    high = value.astype(jnp.bfloat16).astype(jnp.float32)
    middle = (value - high).astype(jnp.bfloat16).astype(jnp.float32)
    low = value - high - middle
    third = PARAM_LANE + 2 * SLOTS
    split = jnp.where(lane < third, high, jnp.where(lane < third + SLOTS, middle, low))
    split = jnp.where(lane >= PARAM_LANE, split, 0.0)
    for tile in range(tiles):
        total = split
        if tile == 0:
            total = total + left[...].astype(jnp.float32)
        if tile == tiles - 1:
            total = total + right[...].astype(jnp.float32)
        for part in range(2):
            for epoch in range(epochs):
                at = (part * epochs + epoch) * SIDES
                if tile > 0:
                    total = placed(lane, total, tile_of(slc, part, epoch, tile - 1), LANES - RADIUS, at)
                if tile < tiles - 1:
                    total = placed(lane, total, tile_of(slc, part, epoch, tile + 1), 0, at + RADIUS)
        strips[tile] = total.astype(jnp.bfloat16)


def pair_kernel(sizes, places, partner, weight, present, *refs):
    epochs, rows, operands = sizes
    inputs = refs[:operands]
    factors, pulls = refs[operands : operands + 2]
    full, rim_full, main, rim, looked, rim_looked, wide, outer, boxed, power_box = refs[operands + 2 :]
    count = len(places)
    look_rows = rows // LOOK
    tall = (rows + 2 * HALO) // LOOK
    first_look = HALO // LOOK - RADIUS
    total = count * epochs
    own_total = total - epochs
    group = 2 * SLOTS
    group_rows = group * tall
    share = LANES // SLOTS
    has_top = present[0]
    has_bottom = present[1]
    f32 = jnp.float32

    def band_of(shape, from_of, to_of):
        at = lax.broadcasted_iota(jnp.int32, shape, 0)
        to = lax.broadcasted_iota(jnp.int32, shape, 1)
        return (jnp.abs(from_of(at, to) - to_of(to)) <= RADIUS).astype(f32).astype(jnp.bfloat16)

    def rim_column(at, to):
        at = at % LANES
        side = at % share % SIDES
        column = jnp.where(side < RADIUS, side - RADIUS, LANES + side - RADIUS)
        inside = (at // share == to // LANES) & (at % share < LOOK * SIDES)
        return jnp.where(inside, column, -4 * LANES)

    band = band_of((2 * LANES, LANES), lambda at, to: at % LANES, lambda to: to)
    rim_band = band_of((2 * LANES, SLOTS * LANES), rim_column, lambda to: to % LANES)

    lane = lax.broadcasted_iota(jnp.int32, (tall, LANES), 1)
    for block, (tile_at, strip_at, strip_row, top_at, bottom_at, halo_slot) in enumerate(places):
        tile, strip, top, bottom = inputs[tile_at], inputs[strip_at], inputs[top_at], inputs[bottom_at]

        @pl.loop(0, 2 * epochs, unroll=4)
        def _(at):
            row = pl.multiple_of(at * HALO, HALO)
            own = pl.multiple_of(at * rows, rows)
            at = at + block * 2 * epochs
            full[at, :HALO] = top[halo_slot, pl.ds(row, HALO), :].astype(f32) * has_top
            full[at, HALO : HALO + rows] = tile[pl.ds(own, rows), :].astype(f32)
            full[at, HALO + rows :] = bottom[halo_slot, pl.ds(row, HALO), :].astype(f32) * has_bottom

        last = slice(2 * epochs * HALO, 2 * epochs * HALO + HALO)
        rim_full[block, :HALO] = top[halo_slot, last, :].astype(f32) * has_top
        rim_full[block, HALO : HALO + rows] = strip[strip_row : strip_row + rows, :].astype(f32)
        rim_full[block, HALO + rows :] = bottom[halo_slot, last, :].astype(f32) * has_bottom

    def places_of(epoch):
        at = epoch // epochs * (2 * epochs) + epoch % epochs
        return at, at + epochs

    @pl.loop(0, 2 * total, unroll=4)
    def _(at):
        for look in range(LOOK):
            main[at, look] = full[at, pl.ds(look, tall, stride=LOOK), :]

    for block in range(count):
        by_look = [rim_full[block, pl.ds(look, tall, stride=LOOK), :] for look in range(LOOK)]
        for at in range(2 * epochs):
            value = jnp.zeros((tall, LANES), f32)
            for look in range(LOOK):
                target = look * SIDES
                moved = pltpu.roll(by_look[look], (target - at * SIDES) % LANES, axis=1)
                value = jnp.where((lane >= target) & (lane < target + SIDES), moved, value)
            spread = share
            while spread < LANES:
                value = value + pltpu.roll(value, spread, axis=1)
                spread = 2 * spread
            rim[block * 2 * epochs + at] = value

    piece_lane = lax.broadcasted_iota(jnp.int32, (8, LANES), 1)
    slot_lane = [piece_lane // share == slot for slot in range(SLOTS)]

    def mixed(values):
        result = values[-1]
        for slot in range(SLOTS - 1):
            result = jnp.where(slot_lane[slot], values[slot], result)
        return result

    def channel_rows(batch, piece, channel):
        return pl.ds(batch * group_rows + piece * group + channel, 8, stride=group)

    for block in range(count):
        for piece in range(0, tall, 8):
            rows_at = slice(piece, piece + 8)
            for half in range(2):
                squares = []
                for slot in range(SLOTS):
                    channel = half * SLOTS + slot
                    re_at, im_at = places_of(block * epochs + channel)
                    value = None
                    for look in range(LOOK):
                        real = main[re_at, look, rows_at]
                        imag = main[im_at, look, rows_at]
                        one = real * real + imag * imag
                        value = one if value is None else value + one
                    looked[channel_rows(block, piece, channel), :] = value
                    real = rim[re_at, rows_at]
                    imag = rim[im_at, rows_at]
                    squares.append(real * real + imag * imag)
                at = block * 2 * tall + half * tall + piece
                rim_looked[at : at + 8, :] = mixed(squares)

    @pl.loop(0, own_total)
    def _(epoch):
        batch = count + epoch
        re_at, im_at = places_of(epoch)
        mates = [places_of(partner[epoch * SLOTS + slot]) for slot in range(SLOTS)]
        for piece in range(0, tall, 8):
            rows_at = slice(piece, piece + 8)
            own_re = [main[re_at, look, rows_at] for look in range(LOOK)]
            own_im = [main[im_at, look, rows_at] for look in range(LOOK)]
            for slot, (mate_re_at, mate_im_at) in enumerate(mates):
                real = None
                for look in range(LOOK):
                    mate_re = main[mate_re_at, look, rows_at]
                    mate_im = main[mate_im_at, look, rows_at]
                    one = own_re[look] * mate_re + own_im[look] * mate_im
                    two = own_im[look] * mate_re - own_re[look] * mate_im
                    real = one if real is None else real + one
                    imag = two if look == 0 else imag + two
                looked[channel_rows(batch, piece, slot), :] = real
                looked[channel_rows(batch, piece, SLOTS + slot), :] = imag
            rim_re = rim[re_at, rows_at]
            rim_im = rim[im_at, rows_at]
            mate_re = mixed([rim[at, rows_at] for at, _ in mates])
            mate_im = mixed([rim[at, rows_at] for _, at in mates])
            at = pl.multiple_of(batch * (2 * tall) + piece, 8)
            rim_looked[pl.ds(at, 8), :] = rim_re * mate_re + rim_im * mate_im
            at = pl.multiple_of(batch * (2 * tall) + tall + piece, 8)
            rim_looked[pl.ds(at, 8), :] = rim_im * mate_re - rim_re * mate_im

    def columns_summed(batch, batches):
        at = pl.ds(pl.multiple_of(batch * group_rows, group_rows), batches * group_rows)
        halves = jnp.concatenate(split_two(looked[at, :]), axis=1)
        wide[at, :] = jnp.dot(halves, band, preferred_element_type=f32)
        rim_at = pl.ds(pl.multiple_of(batch * (2 * tall), 2 * tall), batches * 2 * tall)
        halves = jnp.concatenate(split_two(rim_looked[rim_at, :]), axis=1)
        value = jnp.dot(halves, rim_band, preferred_element_type=f32)
        for one in range(batches):
            for half in range(2):
                for piece in range(0, tall, 8):
                    row = (2 * one + half) * tall + piece
                    for slot in range(SLOTS):
                        to = channel_rows(batch + one, piece, half * SLOTS + slot)
                        outer[to, :] = value[row : row + 8, slot * LANES : (slot + 1) * LANES]

    columns_summed(0, count)

    @pl.loop(0, own_total // 4)
    def _(quad):
        columns_summed(count + quad * 4, 4)

    def rows_summed(batch):
        values = []
        for look in range(tall):
            at = pl.ds(pl.multiple_of(batch * group_rows + look * group, group), group)
            values.append(wide[at, :] + outer[at, :])
        twos = {look: values[look] + values[look + 1] for look in range(first_look, tall - 2)}
        fours = {look: twos[look] + twos[look + 2] for look in range(first_look, tall - 4)}
        for out in range(look_rows):
            at = out + first_look
            seven = fours[at] + twos[at + 4] + values[at + 6]
            to = pl.ds(pl.multiple_of((batch * look_rows + out) * group, group), group)
            boxed[to, :] = seven

    def box_of(batch, channel):
        return boxed[pl.ds(batch * (look_rows * group) + channel, look_rows, stride=group), :]

    for block in range(count):
        rows_summed(block)
        for channel in range(epochs):
            power_box[block * epochs + channel] = box_of(block, channel)

    @pl.loop(0, own_total, unroll=2)
    def _(epoch):
        rows_summed(count + epoch)

    @pl.loop(0, own_total, unroll=2)
    def _(epoch):
        own_power = power_box[epoch]
        for slot in range(SLOTS):
            pair = epoch * SLOTS + slot
            inverse = lax.rsqrt(own_power * power_box[partner[pair]] + EPSILON)
            unit_re = box_of(count + epoch, slot) * inverse
            unit_im = box_of(count + epoch, SLOTS + slot) * inverse
            factor = weight[pair] * (unit_re * unit_re + unit_im * unit_im)
            factors[pair] = factor
            pulls[pair] = factor * unit_im


def gradient_kernel(sizes, partner, *refs):
    tiles, epochs, stages = sizes
    fields = refs[:tiles]
    factors = refs[tiles : tiles + len(stages)]
    pulls = refs[tiles + len(stages) : tiles + 2 * len(stages)]
    gradient, sums, est, old = refs[tiles + 2 * len(stages) :]
    look_rows = est.shape[1]
    total = tiles * epochs
    f32 = jnp.float32
    for block in range(tiles):

        @pl.loop(0, epochs)
        def _(epoch):
            here = pl.ds(pl.multiple_of(epoch * look_rows, look_rows), look_rows)
            est[block * epochs + epoch] = fields[block][0, here, :].astype(f32) + fields[block][1, here, :].astype(f32)
            old[block * epochs + epoch] = fields[block][2, here, :].astype(f32)

    @pl.loop(0, total)
    def _(epoch):
        gradient[epoch] = jnp.zeros((look_rows, LANES), f32)

    for stage, own_blocks in enumerate(stages):
        for number, block in enumerate(own_blocks):

            @pl.loop(0, epochs)
            def _(here):
                epoch = block * epochs + here
                own_est = est[epoch]
                own = jnp.zeros((look_rows, LANES), f32)
                for slot in range(SLOTS):
                    mate = partner[epoch * SLOTS + slot]
                    pair = (number * epochs + here) * SLOTS + slot
                    weighted = pulls[stage][pair] - factors[stage][pair] * (own_est - est[mate])
                    own = own + weighted
                    gradient[mate] = gradient[mate] - weighted
                gradient[epoch] = gradient[epoch] + own

    zero = jnp.zeros((look_rows, LANES), f32)
    results = (zero,) * 5
    for stage, own_blocks in enumerate(stages):
        for number, block in enumerate(own_blocks):

            def totals(here, carry):
                norm, crossed, grad_term, mixed, old_term = carry
                epoch = block * epochs + here
                own_grad = gradient[epoch]
                own_old = old[epoch]
                norm = norm + own_grad * own_grad
                crossed = crossed + own_grad * own_old
                for slot in range(SLOTS):
                    mate = partner[epoch * SLOTS + slot]
                    factor = factors[stage][(number * epochs + here) * SLOTS + slot]
                    grad_spread = own_grad - gradient[mate]
                    old_spread = own_old - old[mate]
                    pulled = factor * grad_spread
                    grad_term = grad_term + pulled * grad_spread
                    mixed = mixed + pulled * old_spread
                    old_term = old_term + factor * old_spread * old_spread
                return norm, crossed, grad_term, mixed, old_term

            results = lax.fori_loop(0, epochs, totals, results)
    sums[...] = jnp.zeros(sums.shape, f32)
    for at, value in enumerate(results):
        sums[at : at + 1, :] = jnp.sum(value, axis=0, keepdims=True)


def update_kernel(cell_count, me, prev_mean, estimate, direction, *refs):
    new_estimate, new_direction = refs[-2:]
    tiles = estimate.shape[2] // LANES
    pieces = refs[:tiles]
    scalars = refs[tiles:-2]
    epochs = estimate.shape[0]
    look_rows = estimate.shape[1]
    total = scalars[0][...]
    for other in scalars[1:]:
        total = total + other[...]
    total = jnp.sum(total, axis=1, keepdims=True)
    grad_norm, crossed, grad_term, mixed, old_term = (total[at : at + 1, :] for at in range(5))
    momentum = grad_norm / cell_count / prev_mean[0]
    curvature = grad_term + 2.0 * momentum * mixed + momentum * momentum * old_term
    step = (grad_norm + momentum * crossed) / curvature
    momentum = jnp.broadcast_to(momentum, (look_rows, LANES))
    step = jnp.broadcast_to(step, (look_rows, LANES))
    for shift, piece in enumerate(pieces):
        tile = lax.rem(me[0] - shift + tiles, tiles)
        columns = pl.ds(pl.multiple_of(tile * LANES, LANES), LANES)
        for epoch in range(epochs):
            gradient = piece[epoch]
            moved = gradient + momentum * direction[epoch, :, columns]
            new_direction[epoch, :, columns] = moved
            new_estimate[epoch, :, columns] = estimate[epoch, :, columns] + step * moved


def swapped(up, down, axis):
    size = lax.axis_size(axis)
    if size == 1:
        return jnp.zeros_like(up), jnp.zeros_like(down)
    if size == 2:
        first = lax.axis_index(axis) == 0
        got = lax.ppermute(jnp.where(first, up, down), axis, [(0, 1), (1, 0)])
        return got, got
    forward = [(i, i + 1) for i in range(size - 1)]
    backward = [(target, source) for source, target in forward]
    return lax.ppermute(up, axis, forward), lax.ppermute(down, axis, backward)


def to_ahead(x, axis, by):
    size = lax.axis_size(axis)
    return lax.ppermute(x, axis, [(i, (i + by) % size) for i in range(size)])


def transposed_plan(slc, offsets, weights, estimate, direction, prev_mean):
    f32 = jnp.float32
    bf16 = jnp.bfloat16
    tiles = lax.axis_size("epoch")
    me = lax.axis_index("epoch")
    epochs, rows, columns = slc.shape[1:]
    look_rows = rows // LOOK
    total = tiles * epochs
    tall = (rows + 2 * HALO) // LOOK
    tile_rows = 2 * epochs * rows
    params_of = pltpu.CompilerParams(vmem_limit_bytes=VMEM_BYTES)

    def for_device(shift):
        return lax.rem(me + shift, tiles)

    def tile_for(shift):
        return lax.dynamic_slice_in_dim(slc, for_device(shift) * LANES, LANES, axis=3).reshape(tile_rows, LANES)

    def fetched(send, shift):
        return to_ahead(send(tiles - shift), "epoch", tiles - shift)

    beside = [tiles - 1, 0, 1]
    far = list(range(2, tiles - 1))
    tile = {0: tile_for(0), 1: fetched(tile_for, 1), tiles - 1: fetched(tile_for, tiles - 1)}

    params = jnp.zeros((rows, LANES), f32)
    listed = jnp.concatenate([offsets.astype(f32), weights, weights, weights], axis=1)
    params = lax.dynamic_update_slice(params, listed, (0, PARAM_LANE))
    edge, fields = pl.pallas_call(
        edge_kernel,
        out_shape=(
            jax.ShapeDtypeStruct((rows, LANES), bf16),
            jax.ShapeDtypeStruct((tiles, 3, epochs * look_rows, LANES), bf16),
        ),
        in_specs=[VMEM] * 3,
        out_specs=(VMEM,) * 2,
        compiler_params=params_of,
        cost_estimate=pl.CostEstimate(flops=1_000_000, bytes_accessed=2_000_000, transcendentals=0),
    )(slc, estimate, direction)
    before, after = swapped(edge, edge, "sub")
    sub = lax.axis_index("sub")
    lane = lax.broadcasted_iota(jnp.int32, (rows, LANES), 1)
    inside = lane < 2 * epochs * SIDES
    left = jnp.where(inside & (lane % SIDES < RADIUS) & (sub > 0), before, jnp.zeros_like(edge))
    right = inside & (lane % SIDES >= RADIUS) & (sub < lax.axis_size("sub") - 1)
    right = jnp.where(right, after, jnp.zeros_like(edge))
    strips = pl.pallas_call(
        pack_kernel,
        out_shape=jax.ShapeDtypeStruct((tiles, rows, LANES), bf16),
        in_specs=[VMEM] * 4,
        out_specs=VMEM,
        compiler_params=params_of,
        cost_estimate=pl.CostEstimate(flops=3_000_000, bytes_accessed=2_000_000, transcendentals=0),
    )(slc, params, left, right)

    def strip_for(shift):
        return lax.dynamic_index_in_dim(strips, for_device(shift), axis=0, keepdims=False)

    def field_for(shift):
        return lax.dynamic_index_in_dim(fields, for_device(shift), axis=0, keepdims=False)

    def both_for(shift):
        return jnp.concatenate([tile_for(shift), strip_for(shift)], axis=0)

    strip = {0: strip_for(0), 1: fetched(strip_for, 1), tiles - 1: fetched(strip_for, tiles - 1)}
    both = {block: fetched(both_for, block) for block in far}
    field = {0: field_for(0)}
    fields = lax.optimization_barrier((fields, tile[1], tile[tiles - 1]))[0]
    for block in [1, tiles - 1] + far:
        field[block] = fetched(field_for, block)

    space = lax.axis_index("space")
    spaces = lax.axis_size("space")
    present = jnp.stack([space > 0, space < spaces - 1]).astype(f32)

    def halo(blocks):
        def border(from_row):
            parts = []
            for block in blocks:
                if block in tile:
                    own = tile[block].reshape(2 * epochs, rows, LANES)
                    rim = strip[block].reshape(1, rows, LANES)
                    pieces = [own, rim]
                else:
                    pieces = [both[block].reshape(2 * epochs + 1, rows, LANES)]
                for piece in pieces:
                    cut = lax.dynamic_slice_in_dim(piece, from_row, HALO, axis=1)
                    parts.append(cut.reshape(-1, LANES))
            return jnp.concatenate(parts, axis=0).reshape(len(blocks), (2 * epochs + 1) * HALO, LANES)

        if spaces == 2:
            mine = border(jnp.where(space == 0, rows - HALO, 0))
            got = lax.ppermute(mine, "space", [(0, 1), (1, 0)])
            return got, got
        return swapped(border(rows - HALO), border(0), "space")

    def params_in(block):
        source = strip[block] if block in strip else both[block][tile_rows:]
        return source[:epochs, PARAM_LANE : PARAM_LANE + 4 * SLOTS].astype(f32)

    def pairs_of(blocks, loaded):
        listed = jnp.concatenate([params_in(block) for block in blocks], axis=0)
        mate = jnp.arange(len(blocks) * epochs, dtype=jnp.int32)[:, None] + listed[:, :SLOTS].astype(jnp.int32)
        weight = listed[:, SLOTS : 2 * SLOTS] + listed[:, 2 * SLOTS : 3 * SLOTS] + listed[:, 3 * SLOTS :]
        return mate.reshape(-1), weight.reshape(-1)

    near_halo = halo(beside)
    def pair_stage(loaded):
        own = loaded[:-1]
        mate, weight = pairs_of(own, loaded)
        operands = []

        def index_of(array):
            for at, other in enumerate(operands):
                if other is array:
                    return at
            operands.append(array)
            return len(operands) - 1

        places = []
        for block in loaded:
            if block in tile:
                at = index_of(tile[block]), index_of(strip[block]), 0
            else:
                at = index_of(both[block]), index_of(both[block]), tile_rows
            source, slots = (near_halo, beside) if block in beside else (far_halo, far)
            places.append(at + (index_of(source[0]), index_of(source[1]), slots.index(block)))
        here = len(loaded) * epochs
        owned = len(own) * epochs
        group = 2 * SLOTS
        batches = len(loaded) + owned
        shape = jax.ShapeDtypeStruct((owned * SLOTS, look_rows, LANES), f32)
        return pl.pallas_call(
            functools.partial(pair_kernel, (epochs, rows, len(operands)), tuple(places)),
            out_shape=(shape, shape),
            in_specs=[SMEM] * 3 + [VMEM] * len(operands),
            out_specs=(VMEM, VMEM),
            scratch_shapes=[
                pltpu.VMEM((2 * here, rows + 2 * HALO, LANES), f32),
                pltpu.VMEM((len(loaded), rows + 2 * HALO, LANES), f32),
                pltpu.VMEM((2 * here, LOOK, tall, LANES), f32),
                pltpu.VMEM((2 * here, tall, LANES), f32),
                pltpu.VMEM((batches * group * tall, LANES), f32),
                pltpu.VMEM((batches * 2 * tall, LANES), f32),
                pltpu.VMEM((batches * group * tall, LANES), f32),
                pltpu.VMEM((batches * group * tall, LANES), f32),
                pltpu.VMEM((batches * group * look_rows, LANES), f32),
                pltpu.VMEM((here, look_rows, LANES), f32),
            ],
            compiler_params=params_of,
            cost_estimate=pl.CostEstimate(flops=20_000_000, bytes_accessed=30_000_000, transcendentals=0),
        )(mate, weight, present, *operands)

    near_stage = beside
    far_stage = list(range(1, tiles))
    near_pairs = pair_stage(near_stage)
    both, near_pairs = lax.optimization_barrier((both, near_pairs))
    far_halo = halo(far)
    far_pairs = pair_stage(far_stage)

    listed = jnp.concatenate([params_in(block) for block in range(tiles)], axis=0)
    partner = jnp.arange(total, dtype=jnp.int32)[:, None] + listed[:, :SLOTS].astype(jnp.int32)
    partner = lax.rem(partner, total).reshape(-1)
    stages = (tuple(near_stage[:-1]), tuple(far_stage[:-1]))
    gradient, sums = pl.pallas_call(
        functools.partial(gradient_kernel, (tiles, epochs, stages)),
        out_shape=(
            jax.ShapeDtypeStruct((total, look_rows, LANES), f32),
            jax.ShapeDtypeStruct((8, LANES), f32),
        ),
        in_specs=[SMEM] + [VMEM] * (tiles + 4),
        out_specs=(VMEM, VMEM),
        scratch_shapes=[pltpu.VMEM((total, look_rows, LANES), f32)] * 2,
        compiler_params=params_of,
        cost_estimate=pl.CostEstimate(flops=10_000_000, bytes_accessed=8_000_000, transcendentals=0),
    )(partner, *[field[block] for block in range(tiles)], near_pairs[0], far_pairs[0], near_pairs[1], far_pairs[1])

    place = ("space", "sub")
    count = spaces * lax.axis_size("sub")
    shared = [sums] + [lax.ppermute(sums, place, [(i, (i + by) % count) for i in range(count)]) for by in range(1, count)]
    here = sum(shared[1:], shared[0])
    scalars = [here] + [to_ahead(here, "epoch", by) for by in range(1, tiles)]
    returned = [gradient[:epochs]]
    returned += [to_ahead(gradient[by * epochs : (by + 1) * epochs], "epoch", by) for by in range(1, tiles)]
    cell_count = float(total * look_rows * spaces * columns * lax.axis_size("sub"))
    return pl.pallas_call(
        functools.partial(update_kernel, cell_count),
        out_shape=(jax.ShapeDtypeStruct(estimate.shape, f32),) * 2,
        in_specs=[SMEM] * 2 + [VMEM] * (2 + 2 * tiles),
        out_specs=(VMEM, VMEM),
        compiler_params=params_of,
        cost_estimate=pl.CostEstimate(flops=1_000_000, bytes_accessed=2_000_000, transcendentals=0),
    )(me.reshape(1), prev_mean, estimate, direction, *returned, *scalars)


def on_device(slc, offsets, weights, estimate, direction, prev_mean):
    epochs, rows, columns = slc.shape[1:]
    fits = columns == LANES * lax.axis_size("epoch") and lax.axis_size("epoch") > 3
    fits = fits and 2 * epochs * SIDES <= PARAM_LANE and rows % HALO == 0 and epochs == 2 * SLOTS
    plan = transposed_plan if fits else ring_plan
    return plan(slc, offsets, weights, estimate, direction, prev_mean)


def solution(mesh):
    return jax.shard_map(
        on_device,
        mesh=mesh,
        in_specs=(
            P(None, ("groups", "epoch"), "space", "sub"),
            P(("groups", "epoch"), None),
            P(("groups", "epoch"), None),
            P(("groups", "epoch"), "space", "sub"),
            P(("groups", "epoch"), "space", "sub"),
            P(),
        ),
        out_specs=(P(("groups", "epoch"), "space", "sub"), P(("groups", "epoch"), "space", "sub")),
        check_vma=False,
    )
```

```python
import functools

import jax
import jax.numpy as jnp
from jax import lax
from jax.experimental import pallas as pl
from jax.experimental.pallas import tpu as pltpu
from jax.sharding import PartitionSpec as P

SLOTS = 4
OFFS = 8
LOOK = 4
RADIUS = 3


EPSILON = 1e-06


def passed_along(x, axis, by):
    size = lax.axis_size(axis)
    return lax.ppermute(x, axis, [(i, (i + by) % size) for i in range(size)])


def extended_2(block, sides, width):
    for axis, dim in sides:
        count = lax.axis_size(axis)
        forward = [(i, i + 1) for i in range(count - 1)]
        backward = [(target, source) for source, target in forward]
        low = lax.ppermute(
            lax.slice_in_dim(block, block.shape[dim] - width, None, axis=dim), axis, forward
        )
        high = lax.ppermute(lax.slice_in_dim(block, 0, width, axis=dim), axis, backward)
        block = jnp.concatenate([low, block, high], axis=dim)
    return block


def looked_sum(field):
    shape = field.shape
    return jnp.sum(field.reshape(shape[:-2] + (shape[-2] // LOOK, LOOK, shape[-1])), axis=-2)


def window_sum(padded, axis):
    length = padded.shape[axis] - 2 * RADIUS
    total = lax.slice_in_dim(padded, 0, length, axis=axis)
    for shift_at in range(1, 2 * RADIUS + 1):
        total = total + lax.slice_in_dim(padded, shift_at, shift_at + length, axis=axis)
    return total


def ring_plan(slc, offsets, weights, estimate, direction, prev_mean):
    epochs_here = slc.shape[1]
    look_rows = slc.shape[2] // LOOK
    col_count = slc.shape[3]
    ahead = passed_along(slc, "epoch", -1)
    extended = jnp.concatenate([slc, ahead], axis=1)
    numbers = jnp.arange(epochs_here, dtype=jnp.int32)
    partner = numbers[:, None] + offsets
    own_real = slc[0].astype(jnp.float32)
    own_imag = slc[1].astype(jnp.float32)
    ext_real = extended[0].astype(jnp.float32)
    ext_imag = extended[1].astype(jnp.float32)
    powers = looked_sum(ext_real * ext_real + ext_imag * ext_imag)
    pieces = []
    for slot_index in range(SLOTS):
        mate_real = jnp.take(ext_real, partner[:, slot_index], axis=0)
        mate_imag = jnp.take(ext_imag, partner[:, slot_index], axis=0)
        pieces.append(looked_sum(own_real * mate_real + own_imag * mate_imag))
        pieces.append(looked_sum(own_imag * mate_real - own_real * mate_imag))
    pair_count = epochs_here * 2 * SLOTS
    stacked = jnp.concatenate(
        [jnp.stack(pieces, axis=1).reshape(pair_count, look_rows, col_count), powers], axis=0
    )
    padded = extended_2(stacked, (("space", 1), ("sub", 2)), RADIUS)
    boxed = window_sum(window_sum(padded, 1), 2)
    pair_boxed = boxed[:pair_count].reshape(epochs_here, 2 * SLOTS, look_rows, col_count)
    power_box = boxed[pair_count:]
    coh_real = pair_boxed[:, 0::2]
    coh_imag = pair_boxed[:, 1::2]
    denominator = power_box[:epochs_here, None] * jnp.take(power_box, partner, axis=0) + EPSILON
    coherence = (coh_real * coh_real + coh_imag * coh_imag) / denominator
    observed = coh_imag / jnp.sqrt(denominator)
    est_ahead = passed_along(estimate, "epoch", -1)
    est_extended = jnp.concatenate([estimate, est_ahead], axis=0)
    fitted = estimate[:, None] - jnp.take(est_extended, partner, axis=0)
    factor = weights[:, :, None, None] * coherence
    weighted = factor * (observed - fitted)
    flattened = weighted.reshape(epochs_here * SLOTS, look_rows * col_count)
    selector = (
        jnp.arange(epochs_here + OFFS, dtype=jnp.int32)[:, None] == partner.reshape(1, -1)
    ).astype(jnp.float32)
    gathered = jnp.dot(
        selector, flattened, precision=lax.Precision.HIGHEST, preferred_element_type=jnp.float32
    ).reshape(epochs_here + OFFS, look_rows, col_count)
    own_part = jnp.sum(weighted, axis=1) - gathered[:epochs_here]
    returned = passed_along(-gathered[epochs_here:], "epoch", 1)
    gradient = jnp.concatenate([own_part + returned, own_part[OFFS:]], axis=0)
    cell_count = float(
        epochs_here
        * lax.axis_size("epoch")
        * look_rows
        * lax.axis_size("space")
        * col_count
        * lax.axis_size("sub")
    )
    local_norm = jnp.sum(gradient * gradient)
    local_crossed = jnp.sum(gradient * direction)
    mean_before = prev_mean[0]
    fields_ahead = passed_along(
        jnp.stack([gradient, direction]).astype(jnp.bfloat16), "epoch", -1
    ).astype(jnp.float32)
    grad_extended = jnp.concatenate([gradient, fields_ahead[0]], axis=0)
    old_extended = jnp.concatenate([direction, fields_ahead[1]], axis=0)
    grad_spread = gradient[:, None] - jnp.take(grad_extended, partner, axis=0)
    old_spread = direction[:, None] - jnp.take(old_extended, partner, axis=0)
    totals = lax.psum(
        (
            local_norm,
            local_crossed,
            jnp.sum(factor * grad_spread * grad_spread),
            jnp.sum(factor * grad_spread * old_spread),
            jnp.sum(factor * old_spread * old_spread),
        ),
        ("epoch", "space", "sub"),
    )
    grad_norm, crossed, grad_term, mixed_term, old_term = totals
    momentum = grad_norm / cell_count / mean_before
    new_direction = gradient + momentum * direction
    curvature = grad_term + 2.0 * momentum * mixed_term + momentum * momentum * old_term
    along_sum = grad_norm + momentum * crossed
    step_size = along_sum / curvature
    return (estimate + step_size * new_direction, new_direction)


LANES = 128
SIDES = 2 * RADIUS
HALO = 16
PARAM_LANE = 96
VMEM = pl.BlockSpec(memory_space=pltpu.VMEM)
SMEM = pl.BlockSpec(memory_space=pltpu.SMEM)
VMEM_BYTES = 48 * 1024 * 1024


def split_two(value):
    high = value.astype(jnp.bfloat16)
    low = (value - high.astype(jnp.float32)).astype(jnp.bfloat16)
    return high, low


def edge_kernel(slc, estimate, direction, edge, fields):
    tiles = fields.shape[0]
    epochs = slc.shape[1]
    rows = slc.shape[2]
    look_rows = estimate.shape[1]
    lane = lax.broadcasted_iota(jnp.int32, (rows, LANES), 1)
    total = jnp.zeros((rows, LANES), jnp.float32)
    for part in range(2):
        for epoch in range(epochs):
            at = (part * epochs + epoch) * SIDES
            total = placed(lane, total, tile_of(slc, part, epoch, tiles - 1), LANES - RADIUS, at)
            total = placed(lane, total, tile_of(slc, part, epoch, 0), 0, at + RADIUS)
    edge[...] = total.astype(jnp.bfloat16)
    for tile in range(tiles):
        columns = slice(tile * LANES, (tile + 1) * LANES)
        for epoch in range(epochs):
            here = slice(epoch * look_rows, (epoch + 1) * look_rows)
            first, second = split_two(estimate[epoch, :, columns])
            fields[tile, 0, here, :] = first
            fields[tile, 1, here, :] = second
            fields[tile, 2, here, :] = direction[epoch, :, columns].astype(jnp.bfloat16)


def tile_of(slc, part, epoch, tile):
    return slc[part, epoch, :, tile * LANES : (tile + 1) * LANES].astype(jnp.float32)


def placed(lane, total, source, start, target):
    moved = pltpu.roll(source, (target - start) % LANES, axis=1)
    return jnp.where((lane >= target) & (lane < target + RADIUS), moved, total)


def pack_kernel(slc, params, left, right, strips):
    tiles = strips.shape[0]
    epochs = slc.shape[1]
    rows = slc.shape[2]
    lane = lax.broadcasted_iota(jnp.int32, (rows, LANES), 1)
    value = params[...]
    high = value.astype(jnp.bfloat16).astype(jnp.float32)
    middle = (value - high).astype(jnp.bfloat16).astype(jnp.float32)
    low = value - high - middle
    third = PARAM_LANE + 2 * SLOTS
    split = jnp.where(lane < third, high, jnp.where(lane < third + SLOTS, middle, low))
    split = jnp.where(lane >= PARAM_LANE, split, 0.0)
    for tile in range(tiles):
        total = split
        if tile == 0:
            total = total + left[...].astype(jnp.float32)
        if tile == tiles - 1:
            total = total + right[...].astype(jnp.float32)
        for part in range(2):
            for epoch in range(epochs):
                at = (part * epochs + epoch) * SIDES
                if tile > 0:
                    total = placed(lane, total, tile_of(slc, part, epoch, tile - 1), LANES - RADIUS, at)
                if tile < tiles - 1:
                    total = placed(lane, total, tile_of(slc, part, epoch, tile + 1), 0, at + RADIUS)
        strips[tile] = total.astype(jnp.bfloat16)


def pair_kernel(sizes, places, partner, weight, present, *refs):
    epochs, rows, operands = sizes
    inputs = refs[:operands]
    factors, pulls = refs[operands : operands + 2]
    main, rim, looked, rim_looked, wide, outer, boxed, power_box = refs[operands + 2 :]
    count = len(places)
    look_rows = rows // LOOK
    tall = (rows + 2 * HALO) // LOOK
    halo_looks = HALO // LOOK
    full_rows = rows + 2 * HALO
    total = count * epochs
    own_total = total - epochs
    group = 2 * SLOTS
    group_rows = group * tall
    share = LANES // SLOTS
    has_top = present[0]
    has_bottom = present[1]
    f32 = jnp.float32

    def band_of(shape, from_of, to_of):
        at = lax.broadcasted_iota(jnp.int32, shape, 0)
        to = lax.broadcasted_iota(jnp.int32, shape, 1)
        return (jnp.abs(from_of(at, to) - to_of(to)) <= RADIUS).astype(f32).astype(jnp.bfloat16)

    def rim_column(at, to):
        at = at % LANES
        side = at % share % SIDES
        column = jnp.where(side < RADIUS, side - RADIUS, LANES + side - RADIUS)
        inside = (at // share == to // LANES) & (at % share < LOOK * SIDES)
        return jnp.where(inside, column, -4 * LANES)

    band = band_of((2 * LANES, LANES), lambda at, to: at % LANES, lambda to: to)
    rim_band = band_of((2 * LANES, SLOTS * LANES), rim_column, lambda to: to % LANES)

    out_at = lax.broadcasted_iota(jnp.int32, (group * look_rows, group * tall), 0)
    in_at = lax.broadcasted_iota(jnp.int32, (group * look_rows, group * tall), 1)
    near = jnp.abs(in_at % tall - halo_looks - out_at % look_rows) <= RADIUS
    near = near & (in_at // tall == out_at // look_rows)
    sum_rows = near.astype(f32).astype(jnp.bfloat16)

    out_at = lax.broadcasted_iota(jnp.int32, (full_rows, full_rows), 0)
    in_at = lax.broadcasted_iota(jnp.int32, (full_rows, full_rows), 1)
    order = (in_at == out_at % tall * LOOK + out_at // tall).astype(f32)
    order = jnp.where(in_at < HALO, order * has_top, order)
    order = jnp.where(in_at >= HALO + rows, order * has_bottom, order).astype(jnp.bfloat16)

    lane = lax.broadcasted_iota(jnp.int32, (tall, LANES), 1)
    for block, (tile_at, strip_at, strip_row, top_at, bottom_at, halo_slot) in enumerate(places):
        tile, strip, top, bottom = inputs[tile_at], inputs[strip_at], inputs[top_at], inputs[bottom_at]

        @pl.loop(0, epochs // 2)
        def _(quad):
            for couple in range(2):
                columns = []
                for one in range(2):
                    at = quad * 4 + couple * 2 + one
                    row = pl.multiple_of(at * HALO, HALO)
                    own = pl.multiple_of(at * rows, rows)
                    parts = [top[halo_slot, pl.ds(row, HALO), :], tile[pl.ds(own, rows), :], bottom[halo_slot, pl.ds(row, HALO), :]]
                    columns.append(jnp.concatenate(parts, axis=0))
                value = jnp.dot(order, jnp.concatenate(columns, axis=1), preferred_element_type=f32)
                for one in range(2):
                    at = block * 2 * epochs + quad * 4 + couple * 2 + one
                    for look in range(LOOK):
                        main[at, look] = value[look * tall : (look + 1) * tall, one * LANES : (one + 1) * LANES]

        last = slice(2 * epochs * HALO, 2 * epochs * HALO + HALO)
        parts = [top[halo_slot, last, :], strip[strip_row : strip_row + rows, :], bottom[halo_slot, last, :]]
        by_look = jnp.dot(order, jnp.concatenate(parts, axis=0), preferred_element_type=f32)
        for at in range(2 * epochs):
            value = jnp.zeros((tall, LANES), f32)
            for look in range(LOOK):
                target = look * SIDES
                moved = by_look[look * tall : (look + 1) * tall]
                moved = pltpu.roll(moved, (target - at * SIDES) % LANES, axis=1)
                value = jnp.where((lane >= target) & (lane < target + SIDES), moved, value)
            spread = share
            while spread < LANES:
                value = value + pltpu.roll(value, spread, axis=1)
                spread = 2 * spread
            rim[block * 2 * epochs + at] = value

    def places_of(epoch):
        at = epoch // epochs * (2 * epochs) + epoch % epochs
        return at, at + epochs

    piece_lane = lax.broadcasted_iota(jnp.int32, (8, LANES), 1)
    slot_lane = [piece_lane // share == slot for slot in range(SLOTS)]

    def mixed(values):
        result = values[-1]
        for slot in range(SLOTS - 1):
            result = jnp.where(slot_lane[slot], values[slot], result)
        return result

    def channel_rows(batch, piece, channel):
        return pl.ds(pl.multiple_of(batch * group_rows + channel * tall + piece, 8), 8)

    for block in range(count):
        for piece in range(0, tall, 8):
            rows_at = slice(piece, piece + 8)
            for half in range(2):
                squares = []
                for slot in range(SLOTS):
                    channel = half * SLOTS + slot
                    re_at, im_at = places_of(block * epochs + channel)
                    value = None
                    for look in range(LOOK):
                        real = main[re_at, look, rows_at]
                        imag = main[im_at, look, rows_at]
                        one = real * real + imag * imag
                        value = one if value is None else value + one
                    looked[channel_rows(block, piece, channel), :] = value
                    real = rim[re_at, rows_at]
                    imag = rim[im_at, rows_at]
                    squares.append(real * real + imag * imag)
                at = block * 2 * tall + half * tall + piece
                rim_looked[at : at + 8, :] = mixed(squares)

    @pl.loop(0, own_total)
    def _(epoch):
        batch = count + epoch
        re_at, im_at = places_of(epoch)
        mates = [places_of(partner[epoch * SLOTS + slot]) for slot in range(SLOTS)]
        for piece in range(0, tall, 8):
            rows_at = slice(piece, piece + 8)
            own_re = [main[re_at, look, rows_at] for look in range(LOOK)]
            own_im = [main[im_at, look, rows_at] for look in range(LOOK)]
            for slot, (mate_re_at, mate_im_at) in enumerate(mates):
                real = None
                for look in range(LOOK):
                    mate_re = main[mate_re_at, look, rows_at]
                    mate_im = main[mate_im_at, look, rows_at]
                    one = own_re[look] * mate_re + own_im[look] * mate_im
                    two = own_im[look] * mate_re - own_re[look] * mate_im
                    real = one if real is None else real + one
                    imag = two if look == 0 else imag + two
                looked[channel_rows(batch, piece, slot), :] = real
                looked[channel_rows(batch, piece, SLOTS + slot), :] = imag
            rim_re = rim[re_at, rows_at]
            rim_im = rim[im_at, rows_at]
            mate_re = mixed([rim[at, rows_at] for at, _ in mates])
            mate_im = mixed([rim[at, rows_at] for _, at in mates])
            at = pl.multiple_of(batch * (2 * tall) + piece, 8)
            rim_looked[pl.ds(at, 8), :] = rim_re * mate_re + rim_im * mate_im
            at = pl.multiple_of(batch * (2 * tall) + tall + piece, 8)
            rim_looked[pl.ds(at, 8), :] = rim_im * mate_re - rim_re * mate_im

    def columns_summed(batch, batches):
        at = pl.ds(pl.multiple_of(batch * group_rows, group_rows), batches * group_rows)
        halves = jnp.concatenate(split_two(looked[at, :]), axis=1)
        wide[at, :] = jnp.dot(halves, band, preferred_element_type=f32)
        rim_at = pl.ds(pl.multiple_of(batch * (2 * tall), 2 * tall), batches * 2 * tall)
        halves = jnp.concatenate(split_two(rim_looked[rim_at, :]), axis=1)
        value = jnp.dot(halves, rim_band, preferred_element_type=f32)
        for one in range(batches):
            for half in range(2):
                for piece in range(0, tall, 8):
                    row = (2 * one + half) * tall + piece
                    for slot in range(SLOTS):
                        to = channel_rows(batch + one, piece, half * SLOTS + slot)
                        outer[to, :] = value[row : row + 8, slot * LANES : (slot + 1) * LANES]

    columns_summed(0, count)

    @pl.loop(0, own_total // 4)
    def _(quad):
        columns_summed(count + quad * 4, 4)

    def rows_summed(batch):
        at = pl.ds(pl.multiple_of(batch * group_rows, group_rows), group_rows)
        halves = jnp.concatenate(split_two(wide[at, :] + outer[at, :]), axis=1)
        value = jnp.dot(sum_rows, halves, preferred_element_type=f32)
        return value[:, :LANES] + value[:, LANES:]

    for block in range(count):
        value = rows_summed(block)
        for channel in range(epochs):
            power_box[block * epochs + channel] = value[channel * look_rows : (channel + 1) * look_rows]

    @pl.loop(0, own_total // 4)
    def _(quad):
        for one in range(4):
            boxed[quad * 4 + one] = rows_summed(count + quad * 4 + one)

    @pl.loop(0, own_total // 2)
    def _(couple):
        for one in range(2):
            epoch = couple * 2 + one
            own_power = power_box[epoch]
            for slot in range(SLOTS):
                pair = epoch * SLOTS + slot
                inverse = lax.rsqrt(own_power * power_box[partner[pair]] + EPSILON)
                unit_re = boxed[epoch, slot * look_rows : (slot + 1) * look_rows, :] * inverse
                unit_im = boxed[epoch, (SLOTS + slot) * look_rows : (SLOTS + slot + 1) * look_rows, :] * inverse
                factor = weight[pair] * (unit_re * unit_re + unit_im * unit_im)
                factors[pair] = factor
                pulls[pair] = factor * unit_im


def gradient_kernel(sizes, partner, *refs):
    tiles, epochs, stages = sizes
    fields = refs[:tiles]
    factors = refs[tiles : tiles + len(stages)]
    pulls = refs[tiles + len(stages) : tiles + 2 * len(stages)]
    gradient, sums, est, old = refs[tiles + 2 * len(stages) :]
    look_rows = est.shape[1]
    total = tiles * epochs
    f32 = jnp.float32
    for block in range(tiles):

        @pl.loop(0, epochs)
        def _(epoch):
            here = pl.ds(pl.multiple_of(epoch * look_rows, look_rows), look_rows)
            est[block * epochs + epoch] = fields[block][0, here, :].astype(f32) + fields[block][1, here, :].astype(f32)
            old[block * epochs + epoch] = fields[block][2, here, :].astype(f32)

    @pl.loop(0, total)
    def _(epoch):
        gradient[epoch] = jnp.zeros((look_rows, LANES), f32)

    for stage, own_blocks in enumerate(stages):
        for number, block in enumerate(own_blocks):

            @pl.loop(0, epochs)
            def _(here):
                epoch = block * epochs + here
                own_est = est[epoch]
                own = jnp.zeros((look_rows, LANES), f32)
                for slot in range(SLOTS):
                    mate = partner[epoch * SLOTS + slot]
                    pair = (number * epochs + here) * SLOTS + slot
                    weighted = pulls[stage][pair] - factors[stage][pair] * (own_est - est[mate])
                    own = own + weighted
                    gradient[mate] = gradient[mate] - weighted
                gradient[epoch] = gradient[epoch] + own

    zero = jnp.zeros((look_rows, LANES), f32)
    results = (zero,) * 5
    for stage, own_blocks in enumerate(stages):
        for number, block in enumerate(own_blocks):

            def totals(here, carry):
                norm, crossed, grad_term, mixed, old_term = carry
                epoch = block * epochs + here
                own_grad = gradient[epoch]
                own_old = old[epoch]
                norm = norm + own_grad * own_grad
                crossed = crossed + own_grad * own_old
                for slot in range(SLOTS):
                    mate = partner[epoch * SLOTS + slot]
                    factor = factors[stage][(number * epochs + here) * SLOTS + slot]
                    grad_spread = own_grad - gradient[mate]
                    old_spread = own_old - old[mate]
                    pulled = factor * grad_spread
                    grad_term = grad_term + pulled * grad_spread
                    mixed = mixed + pulled * old_spread
                    old_term = old_term + factor * old_spread * old_spread
                return norm, crossed, grad_term, mixed, old_term

            results = lax.fori_loop(0, epochs, totals, results)
    sums[...] = jnp.zeros(sums.shape, f32)
    for at, value in enumerate(results):
        sums[at : at + 1, :] = jnp.sum(value, axis=0, keepdims=True)


def update_kernel(cell_count, me, prev_mean, estimate, direction, *refs):
    new_estimate, new_direction = refs[-2:]
    tiles = estimate.shape[2] // LANES
    pieces = refs[:tiles]
    scalars = refs[tiles:-2]
    epochs = estimate.shape[0]
    look_rows = estimate.shape[1]
    total = scalars[0][...]
    for other in scalars[1:]:
        total = total + other[...]
    total = jnp.sum(total, axis=1, keepdims=True)
    grad_norm, crossed, grad_term, mixed, old_term = (total[at : at + 1, :] for at in range(5))
    momentum = grad_norm / cell_count / prev_mean[0]
    curvature = grad_term + 2.0 * momentum * mixed + momentum * momentum * old_term
    step = (grad_norm + momentum * crossed) / curvature
    momentum = jnp.broadcast_to(momentum, (look_rows, LANES))
    step = jnp.broadcast_to(step, (look_rows, LANES))
    for shift, piece in enumerate(pieces):
        tile = lax.rem(me[0] - shift + tiles, tiles)
        columns = pl.ds(pl.multiple_of(tile * LANES, LANES), LANES)
        for epoch in range(epochs):
            gradient = piece[epoch]
            moved = gradient + momentum * direction[epoch, :, columns]
            new_direction[epoch, :, columns] = moved
            new_estimate[epoch, :, columns] = estimate[epoch, :, columns] + step * moved


def swapped(up, down, axis):
    size = lax.axis_size(axis)
    if size == 1:
        return jnp.zeros_like(up), jnp.zeros_like(down)
    if size == 2:
        first = lax.axis_index(axis) == 0
        got = lax.ppermute(jnp.where(first, up, down), axis, [(0, 1), (1, 0)])
        return got, got
    forward = [(i, i + 1) for i in range(size - 1)]
    backward = [(target, source) for source, target in forward]
    return lax.ppermute(up, axis, forward), lax.ppermute(down, axis, backward)


def to_ahead(x, axis, by):
    size = lax.axis_size(axis)
    return lax.ppermute(x, axis, [(i, (i + by) % size) for i in range(size)])


def transposed_plan(slc, offsets, weights, estimate, direction, prev_mean):
    f32 = jnp.float32
    bf16 = jnp.bfloat16
    tiles = lax.axis_size("epoch")
    me = lax.axis_index("epoch")
    epochs, rows, columns = slc.shape[1:]
    look_rows = rows // LOOK
    total = tiles * epochs
    tall = (rows + 2 * HALO) // LOOK
    tile_rows = 2 * epochs * rows
    params_of = pltpu.CompilerParams(vmem_limit_bytes=VMEM_BYTES)

    def for_device(shift):
        return lax.rem(me + shift, tiles)

    def tile_for(shift):
        return lax.dynamic_slice_in_dim(slc, for_device(shift) * LANES, LANES, axis=3).reshape(tile_rows, LANES)

    def fetched(send, shift):
        return to_ahead(send(tiles - shift), "epoch", tiles - shift)

    beside = [tiles - 1, 0, 1]
    far = list(range(2, tiles - 1))
    tile = {0: tile_for(0), 1: fetched(tile_for, 1), tiles - 1: fetched(tile_for, tiles - 1)}

    params = jnp.zeros((rows, LANES), f32)
    listed = jnp.concatenate([offsets.astype(f32), weights, weights, weights], axis=1)
    params = lax.dynamic_update_slice(params, listed, (0, PARAM_LANE))
    edge, fields = pl.pallas_call(
        edge_kernel,
        out_shape=(
            jax.ShapeDtypeStruct((rows, LANES), bf16),
            jax.ShapeDtypeStruct((tiles, 3, epochs * look_rows, LANES), bf16),
        ),
        in_specs=[VMEM] * 3,
        out_specs=(VMEM,) * 2,
        compiler_params=params_of,
        cost_estimate=pl.CostEstimate(flops=1_000_000, bytes_accessed=2_000_000, transcendentals=0),
    )(slc, estimate, direction)
    before, after = swapped(edge, edge, "sub")
    sub = lax.axis_index("sub")
    lane = lax.broadcasted_iota(jnp.int32, (rows, LANES), 1)
    inside = lane < 2 * epochs * SIDES
    left = jnp.where(inside & (lane % SIDES < RADIUS) & (sub > 0), before, jnp.zeros_like(edge))
    right = inside & (lane % SIDES >= RADIUS) & (sub < lax.axis_size("sub") - 1)
    right = jnp.where(right, after, jnp.zeros_like(edge))
    strips = pl.pallas_call(
        pack_kernel,
        out_shape=jax.ShapeDtypeStruct((tiles, rows, LANES), bf16),
        in_specs=[VMEM] * 4,
        out_specs=VMEM,
        compiler_params=params_of,
        cost_estimate=pl.CostEstimate(flops=3_000_000, bytes_accessed=2_000_000, transcendentals=0),
    )(slc, params, left, right)

    def strip_for(shift):
        return lax.dynamic_index_in_dim(strips, for_device(shift), axis=0, keepdims=False)

    def field_for(shift):
        return lax.dynamic_index_in_dim(fields, for_device(shift), axis=0, keepdims=False)

    def both_for(shift):
        return jnp.concatenate([tile_for(shift), strip_for(shift)], axis=0)

    strip = {0: strip_for(0), 1: fetched(strip_for, 1), tiles - 1: fetched(strip_for, tiles - 1)}
    both = {block: fetched(both_for, block) for block in far}
    field = {0: field_for(0)}
    fields = lax.optimization_barrier((fields, tile[1], tile[tiles - 1]))[0]
    for block in [1, tiles - 1] + far:
        field[block] = fetched(field_for, block)

    space = lax.axis_index("space")
    spaces = lax.axis_size("space")
    present = jnp.stack([space > 0, space < spaces - 1]).astype(f32)

    def halo(blocks):
        def border(from_row):
            parts = []
            for block in blocks:
                if block in tile:
                    own = tile[block].reshape(2 * epochs, rows, LANES)
                    rim = strip[block].reshape(1, rows, LANES)
                    pieces = [own, rim]
                else:
                    pieces = [both[block].reshape(2 * epochs + 1, rows, LANES)]
                for piece in pieces:
                    cut = lax.dynamic_slice_in_dim(piece, from_row, HALO, axis=1)
                    parts.append(cut.reshape(-1, LANES))
            return jnp.concatenate(parts, axis=0).reshape(len(blocks), (2 * epochs + 1) * HALO, LANES)

        if spaces == 2:
            mine = border(jnp.where(space == 0, rows - HALO, 0))
            got = lax.ppermute(mine, "space", [(0, 1), (1, 0)])
            return got, got
        return swapped(border(rows - HALO), border(0), "space")

    def params_in(block):
        source = strip[block] if block in strip else both[block][tile_rows:]
        return source[:epochs, PARAM_LANE : PARAM_LANE + 4 * SLOTS].astype(f32)

    def pairs_of(blocks, loaded):
        listed = jnp.concatenate([params_in(block) for block in blocks], axis=0)
        mate = jnp.arange(len(blocks) * epochs, dtype=jnp.int32)[:, None] + listed[:, :SLOTS].astype(jnp.int32)
        weight = listed[:, SLOTS : 2 * SLOTS] + listed[:, 2 * SLOTS : 3 * SLOTS] + listed[:, 3 * SLOTS :]
        return mate.reshape(-1), weight.reshape(-1)

    near_halo = halo(beside)
    def pair_stage(loaded):
        own = loaded[:-1]
        mate, weight = pairs_of(own, loaded)
        operands = []

        def index_of(array):
            for at, other in enumerate(operands):
                if other is array:
                    return at
            operands.append(array)
            return len(operands) - 1

        places = []
        for block in loaded:
            if block in tile:
                at = index_of(tile[block]), index_of(strip[block]), 0
            else:
                at = index_of(both[block]), index_of(both[block]), tile_rows
            source, slots = (near_halo, beside) if block in beside else (far_halo, far)
            places.append(at + (index_of(source[0]), index_of(source[1]), slots.index(block)))
        here = len(loaded) * epochs
        owned = len(own) * epochs
        group = 2 * SLOTS
        batches = len(loaded) + owned
        shape = jax.ShapeDtypeStruct((owned * SLOTS, look_rows, LANES), f32)
        return pl.pallas_call(
            functools.partial(pair_kernel, (epochs, rows, len(operands)), tuple(places)),
            out_shape=(shape, shape),
            in_specs=[SMEM] * 3 + [VMEM] * len(operands),
            out_specs=(VMEM, VMEM),
            scratch_shapes=[
                pltpu.VMEM((2 * here, LOOK, tall, LANES), f32),
                pltpu.VMEM((2 * here, tall, LANES), f32),
                pltpu.VMEM((batches * group * tall, LANES), f32),
                pltpu.VMEM((batches * 2 * tall, LANES), f32),
                pltpu.VMEM((batches * group * tall, LANES), f32),
                pltpu.VMEM((batches * group * tall, LANES), f32),
                pltpu.VMEM((owned, group * look_rows, LANES), f32),
                pltpu.VMEM((here, look_rows, LANES), f32),
            ],
            compiler_params=params_of,
            cost_estimate=pl.CostEstimate(flops=20_000_000, bytes_accessed=30_000_000, transcendentals=0),
        )(mate, weight, present, *operands)

    near_stage = beside
    far_stage = list(range(1, tiles))
    near_pairs = pair_stage(near_stage)
    both, near_pairs = lax.optimization_barrier((both, near_pairs))
    far_halo = halo(far)
    far_pairs = pair_stage(far_stage)

    listed = jnp.concatenate([params_in(block) for block in range(tiles)], axis=0)
    partner = jnp.arange(total, dtype=jnp.int32)[:, None] + listed[:, :SLOTS].astype(jnp.int32)
    partner = lax.rem(partner, total).reshape(-1)
    stages = (tuple(near_stage[:-1]), tuple(far_stage[:-1]))
    gradient, sums = pl.pallas_call(
        functools.partial(gradient_kernel, (tiles, epochs, stages)),
        out_shape=(
            jax.ShapeDtypeStruct((total, look_rows, LANES), f32),
            jax.ShapeDtypeStruct((8, LANES), f32),
        ),
        in_specs=[SMEM] + [VMEM] * (tiles + 4),
        out_specs=(VMEM, VMEM),
        scratch_shapes=[pltpu.VMEM((total, look_rows, LANES), f32)] * 2,
        compiler_params=params_of,
        cost_estimate=pl.CostEstimate(flops=10_000_000, bytes_accessed=8_000_000, transcendentals=0),
    )(partner, *[field[block] for block in range(tiles)], near_pairs[0], far_pairs[0], near_pairs[1], far_pairs[1])

    place = ("space", "sub")
    count = spaces * lax.axis_size("sub")
    shared = [sums] + [lax.ppermute(sums, place, [(i, (i + by) % count) for i in range(count)]) for by in range(1, count)]
    here = sum(shared[1:], shared[0])
    scalars = [here] + [to_ahead(here, "epoch", by) for by in range(1, tiles)]
    returned = [gradient[:epochs]]
    returned += [to_ahead(gradient[by * epochs : (by + 1) * epochs], "epoch", by) for by in range(1, tiles)]
    cell_count = float(total * look_rows * spaces * columns * lax.axis_size("sub"))
    return pl.pallas_call(
        functools.partial(update_kernel, cell_count),
        out_shape=(jax.ShapeDtypeStruct(estimate.shape, f32),) * 2,
        in_specs=[SMEM] * 2 + [VMEM] * (2 + 2 * tiles),
        out_specs=(VMEM, VMEM),
        compiler_params=params_of,
        cost_estimate=pl.CostEstimate(flops=1_000_000, bytes_accessed=2_000_000, transcendentals=0),
    )(me.reshape(1), prev_mean, estimate, direction, *returned, *scalars)


def on_device(slc, offsets, weights, estimate, direction, prev_mean):
    epochs, rows, columns = slc.shape[1:]
    fits = columns == LANES * lax.axis_size("epoch") and lax.axis_size("epoch") > 3
    fits = fits and 2 * epochs * SIDES <= PARAM_LANE and rows % HALO == 0 and epochs == 2 * SLOTS
    plan = transposed_plan if fits else ring_plan
    return plan(slc, offsets, weights, estimate, direction, prev_mean)


def solution(mesh):
    return jax.shard_map(
        on_device,
        mesh=mesh,
        in_specs=(
            P(None, ("groups", "epoch"), "space", "sub"),
            P(("groups", "epoch"), None),
            P(("groups", "epoch"), None),
            P(("groups", "epoch"), "space", "sub"),
            P(("groups", "epoch"), "space", "sub"),
            P(),
        ),
        out_specs=(P(("groups", "epoch"), "space", "sub"), P(("groups", "epoch"), "space", "sub")),
        check_vma=False,
    )
```

```python
import functools

import jax
import jax.numpy as jnp
from jax import lax
from jax.experimental import pallas as pl
from jax.experimental.pallas import tpu as pltpu
from jax.sharding import PartitionSpec as P

SLOTS = 4
OFFS = 8
LOOK = 4
RADIUS = 3


EPSILON = 1e-06


def passed_along(x, axis, by):
    size = lax.axis_size(axis)
    return lax.ppermute(x, axis, [(i, (i + by) % size) for i in range(size)])


def extended_2(block, sides, width):
    for axis, dim in sides:
        count = lax.axis_size(axis)
        forward = [(i, i + 1) for i in range(count - 1)]
        backward = [(target, source) for source, target in forward]
        low = lax.ppermute(
            lax.slice_in_dim(block, block.shape[dim] - width, None, axis=dim), axis, forward
        )
        high = lax.ppermute(lax.slice_in_dim(block, 0, width, axis=dim), axis, backward)
        block = jnp.concatenate([low, block, high], axis=dim)
    return block


def looked_sum(field):
    shape = field.shape
    return jnp.sum(field.reshape(shape[:-2] + (shape[-2] // LOOK, LOOK, shape[-1])), axis=-2)


def window_sum(padded, axis):
    length = padded.shape[axis] - 2 * RADIUS
    total = lax.slice_in_dim(padded, 0, length, axis=axis)
    for shift_at in range(1, 2 * RADIUS + 1):
        total = total + lax.slice_in_dim(padded, shift_at, shift_at + length, axis=axis)
    return total


def ring_plan(slc, offsets, weights, estimate, direction, prev_mean):
    epochs_here = slc.shape[1]
    look_rows = slc.shape[2] // LOOK
    col_count = slc.shape[3]
    ahead = passed_along(slc, "epoch", -1)
    extended = jnp.concatenate([slc, ahead], axis=1)
    numbers = jnp.arange(epochs_here, dtype=jnp.int32)
    partner = numbers[:, None] + offsets
    own_real = slc[0].astype(jnp.float32)
    own_imag = slc[1].astype(jnp.float32)
    ext_real = extended[0].astype(jnp.float32)
    ext_imag = extended[1].astype(jnp.float32)
    powers = looked_sum(ext_real * ext_real + ext_imag * ext_imag)
    pieces = []
    for slot_index in range(SLOTS):
        mate_real = jnp.take(ext_real, partner[:, slot_index], axis=0)
        mate_imag = jnp.take(ext_imag, partner[:, slot_index], axis=0)
        pieces.append(looked_sum(own_real * mate_real + own_imag * mate_imag))
        pieces.append(looked_sum(own_imag * mate_real - own_real * mate_imag))
    pair_count = epochs_here * 2 * SLOTS
    stacked = jnp.concatenate(
        [jnp.stack(pieces, axis=1).reshape(pair_count, look_rows, col_count), powers], axis=0
    )
    padded = extended_2(stacked, (("space", 1), ("sub", 2)), RADIUS)
    boxed = window_sum(window_sum(padded, 1), 2)
    pair_boxed = boxed[:pair_count].reshape(epochs_here, 2 * SLOTS, look_rows, col_count)
    power_box = boxed[pair_count:]
    coh_real = pair_boxed[:, 0::2]
    coh_imag = pair_boxed[:, 1::2]
    denominator = power_box[:epochs_here, None] * jnp.take(power_box, partner, axis=0) + EPSILON
    coherence = (coh_real * coh_real + coh_imag * coh_imag) / denominator
    observed = coh_imag / jnp.sqrt(denominator)
    est_ahead = passed_along(estimate, "epoch", -1)
    est_extended = jnp.concatenate([estimate, est_ahead], axis=0)
    fitted = estimate[:, None] - jnp.take(est_extended, partner, axis=0)
    factor = weights[:, :, None, None] * coherence
    weighted = factor * (observed - fitted)
    flattened = weighted.reshape(epochs_here * SLOTS, look_rows * col_count)
    selector = (
        jnp.arange(epochs_here + OFFS, dtype=jnp.int32)[:, None] == partner.reshape(1, -1)
    ).astype(jnp.float32)
    gathered = jnp.dot(
        selector, flattened, precision=lax.Precision.HIGHEST, preferred_element_type=jnp.float32
    ).reshape(epochs_here + OFFS, look_rows, col_count)
    own_part = jnp.sum(weighted, axis=1) - gathered[:epochs_here]
    returned = passed_along(-gathered[epochs_here:], "epoch", 1)
    gradient = jnp.concatenate([own_part + returned, own_part[OFFS:]], axis=0)
    cell_count = float(
        epochs_here
        * lax.axis_size("epoch")
        * look_rows
        * lax.axis_size("space")
        * col_count
        * lax.axis_size("sub")
    )
    local_norm = jnp.sum(gradient * gradient)
    local_crossed = jnp.sum(gradient * direction)
    mean_before = prev_mean[0]
    fields_ahead = passed_along(
        jnp.stack([gradient, direction]).astype(jnp.bfloat16), "epoch", -1
    ).astype(jnp.float32)
    grad_extended = jnp.concatenate([gradient, fields_ahead[0]], axis=0)
    old_extended = jnp.concatenate([direction, fields_ahead[1]], axis=0)
    grad_spread = gradient[:, None] - jnp.take(grad_extended, partner, axis=0)
    old_spread = direction[:, None] - jnp.take(old_extended, partner, axis=0)
    totals = lax.psum(
        (
            local_norm,
            local_crossed,
            jnp.sum(factor * grad_spread * grad_spread),
            jnp.sum(factor * grad_spread * old_spread),
            jnp.sum(factor * old_spread * old_spread),
        ),
        ("epoch", "space", "sub"),
    )
    grad_norm, crossed, grad_term, mixed_term, old_term = totals
    momentum = grad_norm / cell_count / mean_before
    new_direction = gradient + momentum * direction
    curvature = grad_term + 2.0 * momentum * mixed_term + momentum * momentum * old_term
    along_sum = grad_norm + momentum * crossed
    step_size = along_sum / curvature
    return (estimate + step_size * new_direction, new_direction)


LANES = 128
SIDES = 2 * RADIUS
HALO = 16
PARAM_LANE = 96
VMEM = pl.BlockSpec(memory_space=pltpu.VMEM)
SMEM = pl.BlockSpec(memory_space=pltpu.SMEM)
VMEM_BYTES = 48 * 1024 * 1024


def split_two(value):
    high = value.astype(jnp.bfloat16)
    low = (value - high.astype(jnp.float32)).astype(jnp.bfloat16)
    return high, low


def edge_kernel(first, last, edge):
    epochs = first.shape[1]
    lane = lax.broadcasted_iota(jnp.int32, edge.shape, 1)
    total = jnp.zeros(edge.shape, jnp.float32)
    for part in range(2):
        for epoch in range(epochs):
            at = (part * epochs + epoch) * SIDES
            total = placed(lane, total, tile_of(last, part, epoch, 0), LANES - RADIUS, at)
            total = placed(lane, total, tile_of(first, part, epoch, 0), 0, at + RADIUS)
    edge[...] = total.astype(jnp.bfloat16)


def fields_kernel(estimate, direction, fields):
    look_rows = estimate.shape[1]
    for tile in range(fields.shape[0]):
        columns = slice(tile * LANES, (tile + 1) * LANES)
        for epoch in range(estimate.shape[0]):
            here = slice(epoch * look_rows, (epoch + 1) * look_rows)
            first, second = split_two(estimate[epoch, :, columns])
            fields[tile, 0, here, :] = first
            fields[tile, 1, here, :] = second
            fields[tile, 2, here, :] = direction[epoch, :, columns].astype(jnp.bfloat16)


def tile_of(slc, part, epoch, tile):
    return slc[part, epoch, :, tile * LANES : (tile + 1) * LANES].astype(jnp.float32)


def placed(lane, total, source, start, target):
    moved = pltpu.roll(source, (target - start) % LANES, axis=1)
    return jnp.where((lane >= target) & (lane < target + RADIUS), moved, total)


def pack_kernel(slc, params, left, right, strips):
    tiles = strips.shape[0]
    epochs = slc.shape[1]
    rows = slc.shape[2]
    lane = lax.broadcasted_iota(jnp.int32, (rows, LANES), 1)
    value = params[...]
    high = value.astype(jnp.bfloat16).astype(jnp.float32)
    middle = (value - high).astype(jnp.bfloat16).astype(jnp.float32)
    low = value - high - middle
    third = PARAM_LANE + 2 * SLOTS
    split = jnp.where(lane < third, high, jnp.where(lane < third + SLOTS, middle, low))
    split = jnp.where(lane >= PARAM_LANE, split, 0.0)
    for tile in range(tiles):
        total = split
        if tile == 0:
            total = total + left[...].astype(jnp.float32)
        if tile == tiles - 1:
            total = total + right[...].astype(jnp.float32)
        for part in range(2):
            for epoch in range(epochs):
                at = (part * epochs + epoch) * SIDES
                if tile > 0:
                    total = placed(lane, total, tile_of(slc, part, epoch, tile - 1), LANES - RADIUS, at)
                if tile < tiles - 1:
                    total = placed(lane, total, tile_of(slc, part, epoch, tile + 1), 0, at + RADIUS)
        strips[tile] = total.astype(jnp.bfloat16)


def pair_kernel(sizes, places, partner, weight, present, *refs):
    epochs, rows, operands = sizes
    inputs = refs[:operands]
    factors, pulls = refs[operands : operands + 2]
    main, rim, looked, rim_looked, wide, outer, boxed, power_box = refs[operands + 2 :]
    count = len(places)
    look_rows = rows // LOOK
    tall = (rows + 2 * HALO) // LOOK
    halo_looks = HALO // LOOK
    full_rows = rows + 2 * HALO
    total = count * epochs
    own_total = total - epochs
    group = 2 * SLOTS
    group_rows = group * tall
    share = LANES // SLOTS
    has_top = present[0]
    has_bottom = present[1]
    f32 = jnp.float32

    def band_of(shape, from_of, to_of):
        at = lax.broadcasted_iota(jnp.int32, shape, 0)
        to = lax.broadcasted_iota(jnp.int32, shape, 1)
        return (jnp.abs(from_of(at, to) - to_of(to)) <= RADIUS).astype(f32).astype(jnp.bfloat16)

    def rim_column(at, to):
        at = at % LANES
        side = at % share % SIDES
        column = jnp.where(side < RADIUS, side - RADIUS, LANES + side - RADIUS)
        inside = (at // share == to // LANES) & (at % share < LOOK * SIDES)
        return jnp.where(inside, column, -4 * LANES)

    band = band_of((2 * LANES, LANES), lambda at, to: at % LANES, lambda to: to)
    rim_band = band_of((2 * LANES, SLOTS * LANES), rim_column, lambda to: to % LANES)

    out_at = lax.broadcasted_iota(jnp.int32, (group * look_rows, group * tall), 0)
    in_at = lax.broadcasted_iota(jnp.int32, (group * look_rows, group * tall), 1)
    near = jnp.abs(in_at % tall - halo_looks - out_at % look_rows) <= RADIUS
    near = near & (in_at // tall == out_at // look_rows)
    sum_rows = near.astype(f32).astype(jnp.bfloat16)

    out_at = lax.broadcasted_iota(jnp.int32, (full_rows, full_rows), 0)
    in_at = lax.broadcasted_iota(jnp.int32, (full_rows, full_rows), 1)
    order = (in_at == out_at % tall * LOOK + out_at // tall).astype(f32)
    order = jnp.where(in_at < HALO, order * has_top, order)
    order = jnp.where(in_at >= HALO + rows, order * has_bottom, order).astype(jnp.bfloat16)

    lane = lax.broadcasted_iota(jnp.int32, (tall, LANES), 1)
    for block, (tile_at, strip_at, strip_row, top_at, bottom_at, halo_row) in enumerate(places):
        tile, strip, top, bottom = inputs[tile_at], inputs[strip_at], inputs[top_at], inputs[bottom_at]

        @pl.loop(0, epochs // 2)
        def _(quad):
            for couple in range(2):
                columns = []
                for one in range(2):
                    at = quad * 4 + couple * 2 + one
                    row = pl.multiple_of(halo_row + at * HALO, HALO)
                    own = pl.multiple_of(at * rows, rows)
                    parts = [top[pl.ds(row, HALO), :], tile[pl.ds(own, rows), :], bottom[pl.ds(row, HALO), :]]
                    columns.append(jnp.concatenate(parts, axis=0))
                value = jnp.dot(order, jnp.concatenate(columns, axis=1), preferred_element_type=f32)
                for one in range(2):
                    at = block * 2 * epochs + quad * 4 + couple * 2 + one
                    for look in range(LOOK):
                        main[at, look] = value[look * tall : (look + 1) * tall, one * LANES : (one + 1) * LANES]

        last = slice(halo_row + 2 * epochs * HALO, halo_row + 2 * epochs * HALO + HALO)
        parts = [top[last, :], strip[strip_row : strip_row + rows, :], bottom[last, :]]
        by_look = jnp.dot(order, jnp.concatenate(parts, axis=0), preferred_element_type=f32)
        for at in range(2 * epochs):
            value = jnp.zeros((tall, LANES), f32)
            for look in range(LOOK):
                target = look * SIDES
                moved = by_look[look * tall : (look + 1) * tall]
                moved = pltpu.roll(moved, (target - at * SIDES) % LANES, axis=1)
                value = jnp.where((lane >= target) & (lane < target + SIDES), moved, value)
            spread = share
            while spread < LANES:
                value = value + pltpu.roll(value, spread, axis=1)
                spread = 2 * spread
            rim[block * 2 * epochs + at] = value

    def places_of(epoch):
        at = epoch // epochs * (2 * epochs) + epoch % epochs
        return at, at + epochs

    piece_lane = lax.broadcasted_iota(jnp.int32, (8, LANES), 1)
    slot_lane = [piece_lane // share == slot for slot in range(SLOTS)]

    def mixed(values):
        result = values[-1]
        for slot in range(SLOTS - 1):
            result = jnp.where(slot_lane[slot], values[slot], result)
        return result

    def channel_rows(batch, piece, channel):
        return pl.ds(pl.multiple_of(batch * group_rows + channel * tall + piece, 8), 8)

    for block in range(count):
        for piece in range(0, tall, 8):
            rows_at = slice(piece, piece + 8)
            for half in range(2):
                squares = []
                for slot in range(SLOTS):
                    channel = half * SLOTS + slot
                    re_at, im_at = places_of(block * epochs + channel)
                    value = None
                    for look in range(LOOK):
                        real = main[re_at, look, rows_at]
                        imag = main[im_at, look, rows_at]
                        one = real * real + imag * imag
                        value = one if value is None else value + one
                    looked[channel_rows(block, piece, channel), :] = value
                    real = rim[re_at, rows_at]
                    imag = rim[im_at, rows_at]
                    squares.append(real * real + imag * imag)
                at = block * 2 * tall + half * tall + piece
                rim_looked[at : at + 8, :] = mixed(squares)

    @pl.loop(0, own_total)
    def _(epoch):
        batch = count + epoch
        re_at, im_at = places_of(epoch)
        mates = [places_of(partner[epoch * SLOTS + slot]) for slot in range(SLOTS)]
        for piece in range(0, tall, 8):
            rows_at = slice(piece, piece + 8)
            own_re = [main[re_at, look, rows_at] for look in range(LOOK)]
            own_im = [main[im_at, look, rows_at] for look in range(LOOK)]
            for slot, (mate_re_at, mate_im_at) in enumerate(mates):
                real = None
                for look in range(LOOK):
                    mate_re = main[mate_re_at, look, rows_at]
                    mate_im = main[mate_im_at, look, rows_at]
                    one = own_re[look] * mate_re + own_im[look] * mate_im
                    two = own_im[look] * mate_re - own_re[look] * mate_im
                    real = one if real is None else real + one
                    imag = two if look == 0 else imag + two
                looked[channel_rows(batch, piece, slot), :] = real
                looked[channel_rows(batch, piece, SLOTS + slot), :] = imag
            rim_re = rim[re_at, rows_at]
            rim_im = rim[im_at, rows_at]
            mate_re = mixed([rim[at, rows_at] for at, _ in mates])
            mate_im = mixed([rim[at, rows_at] for _, at in mates])
            at = pl.multiple_of(batch * (2 * tall) + piece, 8)
            rim_looked[pl.ds(at, 8), :] = rim_re * mate_re + rim_im * mate_im
            at = pl.multiple_of(batch * (2 * tall) + tall + piece, 8)
            rim_looked[pl.ds(at, 8), :] = rim_im * mate_re - rim_re * mate_im

    def columns_summed(batch, batches):
        at = pl.ds(pl.multiple_of(batch * group_rows, group_rows), batches * group_rows)
        halves = jnp.concatenate(split_two(looked[at, :]), axis=1)
        wide[at, :] = jnp.dot(halves, band, preferred_element_type=f32)
        rim_at = pl.ds(pl.multiple_of(batch * (2 * tall), 2 * tall), batches * 2 * tall)
        halves = jnp.concatenate(split_two(rim_looked[rim_at, :]), axis=1)
        value = jnp.dot(halves, rim_band, preferred_element_type=f32)
        for one in range(batches):
            for half in range(2):
                for piece in range(0, tall, 8):
                    row = (2 * one + half) * tall + piece
                    for slot in range(SLOTS):
                        to = channel_rows(batch + one, piece, half * SLOTS + slot)
                        outer[to, :] = value[row : row + 8, slot * LANES : (slot + 1) * LANES]

    columns_summed(0, count)

    @pl.loop(0, own_total // 4)
    def _(quad):
        columns_summed(count + quad * 4, 4)

    def rows_summed(batch):
        at = pl.ds(pl.multiple_of(batch * group_rows, group_rows), group_rows)
        halves = jnp.concatenate(split_two(wide[at, :] + outer[at, :]), axis=1)
        value = jnp.dot(sum_rows, halves, preferred_element_type=f32)
        return value[:, :LANES] + value[:, LANES:]

    for block in range(count):
        value = rows_summed(block)
        for channel in range(epochs):
            power_box[block * epochs + channel] = value[channel * look_rows : (channel + 1) * look_rows]

    @pl.loop(0, own_total // 4)
    def _(quad):
        for one in range(4):
            boxed[quad * 4 + one] = rows_summed(count + quad * 4 + one)

    @pl.loop(0, own_total // 2)
    def _(couple):
        for one in range(2):
            epoch = couple * 2 + one
            own_power = power_box[epoch]
            for slot in range(SLOTS):
                pair = epoch * SLOTS + slot
                inverse = lax.rsqrt(own_power * power_box[partner[pair]] + EPSILON)
                unit_re = boxed[epoch, slot * look_rows : (slot + 1) * look_rows, :] * inverse
                unit_im = boxed[epoch, (SLOTS + slot) * look_rows : (SLOTS + slot + 1) * look_rows, :] * inverse
                factor = weight[pair] * (unit_re * unit_re + unit_im * unit_im)
                factors[pair] = factor
                pulls[pair] = factor * unit_im


def gradient_kernel(sizes, partner, *refs):
    tiles, epochs, stages = sizes
    fields = refs[:tiles]
    factors = refs[tiles : tiles + len(stages)]
    pulls = refs[tiles + len(stages) : tiles + 2 * len(stages)]
    gradient, sums, est, old = refs[tiles + 2 * len(stages) :]
    look_rows = est.shape[1]
    total = tiles * epochs
    f32 = jnp.float32
    for block in range(tiles):

        @pl.loop(0, epochs)
        def _(epoch):
            here = pl.ds(pl.multiple_of(epoch * look_rows, look_rows), look_rows)
            est[block * epochs + epoch] = fields[block][0, here, :].astype(f32) + fields[block][1, here, :].astype(f32)
            old[block * epochs + epoch] = fields[block][2, here, :].astype(f32)

    @pl.loop(0, total)
    def _(epoch):
        gradient[epoch] = jnp.zeros((look_rows, LANES), f32)

    for stage, own_blocks in enumerate(stages):
        for number, block in enumerate(own_blocks):

            @pl.loop(0, epochs)
            def _(here):
                epoch = block * epochs + here
                own_est = est[epoch]
                own = jnp.zeros((look_rows, LANES), f32)
                for slot in range(SLOTS):
                    mate = partner[epoch * SLOTS + slot]
                    pair = (number * epochs + here) * SLOTS + slot
                    weighted = pulls[stage][pair] - factors[stage][pair] * (own_est - est[mate])
                    own = own + weighted
                    gradient[mate] = gradient[mate] - weighted
                gradient[epoch] = gradient[epoch] + own

    zero = jnp.zeros((look_rows, LANES), f32)
    results = (zero,) * 5
    for stage, own_blocks in enumerate(stages):
        for number, block in enumerate(own_blocks):

            def totals(here, carry):
                norm, crossed, grad_term, mixed, old_term = carry
                epoch = block * epochs + here
                own_grad = gradient[epoch]
                own_old = old[epoch]
                norm = norm + own_grad * own_grad
                crossed = crossed + own_grad * own_old
                for slot in range(SLOTS):
                    mate = partner[epoch * SLOTS + slot]
                    factor = factors[stage][(number * epochs + here) * SLOTS + slot]
                    grad_spread = own_grad - gradient[mate]
                    old_spread = own_old - old[mate]
                    pulled = factor * grad_spread
                    grad_term = grad_term + pulled * grad_spread
                    mixed = mixed + pulled * old_spread
                    old_term = old_term + factor * old_spread * old_spread
                return norm, crossed, grad_term, mixed, old_term

            results = lax.fori_loop(0, epochs, totals, results)
    sums[...] = jnp.zeros(sums.shape, f32)
    for at, value in enumerate(results):
        sums[at : at + 1, :] = jnp.sum(value, axis=0, keepdims=True)


def update_kernel(cell_count, me, prev_mean, estimate, direction, *refs):
    new_estimate, new_direction = refs[-2:]
    tiles = estimate.shape[2] // LANES
    pieces = refs[:tiles]
    scalars = refs[tiles:-2]
    epochs = estimate.shape[0]
    look_rows = estimate.shape[1]
    total = scalars[0][...]
    for other in scalars[1:]:
        total = total + other[...]
    total = jnp.sum(total, axis=1, keepdims=True)
    grad_norm, crossed, grad_term, mixed, old_term = (total[at : at + 1, :] for at in range(5))
    momentum = grad_norm / cell_count / prev_mean[0]
    curvature = grad_term + 2.0 * momentum * mixed + momentum * momentum * old_term
    step = (grad_norm + momentum * crossed) / curvature
    momentum = jnp.broadcast_to(momentum, (look_rows, LANES))
    step = jnp.broadcast_to(step, (look_rows, LANES))
    for shift, piece in enumerate(pieces):
        tile = lax.rem(me[0] - shift + tiles, tiles)
        columns = pl.ds(pl.multiple_of(tile * LANES, LANES), LANES)
        for epoch in range(epochs):
            gradient = piece[epoch]
            moved = gradient + momentum * direction[epoch, :, columns]
            new_direction[epoch, :, columns] = moved
            new_estimate[epoch, :, columns] = estimate[epoch, :, columns] + step * moved


def swapped(up, down, axis):
    size = lax.axis_size(axis)
    if size == 1:
        return jnp.zeros_like(up), jnp.zeros_like(down)
    if size == 2:
        first = lax.axis_index(axis) == 0
        got = lax.ppermute(jnp.where(first, up, down), axis, [(0, 1), (1, 0)])
        return got, got
    forward = [(i, i + 1) for i in range(size - 1)]
    backward = [(target, source) for source, target in forward]
    return lax.ppermute(up, axis, forward), lax.ppermute(down, axis, backward)


def to_ahead(x, axis, by):
    size = lax.axis_size(axis)
    return lax.ppermute(x, axis, [(i, (i + by) % size) for i in range(size)])


def transposed_plan(slc, offsets, weights, estimate, direction, prev_mean):
    f32 = jnp.float32
    bf16 = jnp.bfloat16
    tiles = lax.axis_size("epoch")
    me = lax.axis_index("epoch")
    epochs, rows, columns = slc.shape[1:]
    look_rows = rows // LOOK
    total = tiles * epochs
    tall = (rows + 2 * HALO) // LOOK
    tile_rows = 2 * epochs * rows
    params_of = pltpu.CompilerParams(vmem_limit_bytes=VMEM_BYTES)

    def for_device(shift):
        return lax.rem(me + shift, tiles)

    def tile_for(shift):
        return lax.dynamic_slice_in_dim(slc, for_device(shift) * LANES, LANES, axis=3).reshape(tile_rows, LANES)

    def fetched(send, shift):
        return to_ahead(send(tiles - shift), "epoch", tiles - shift)

    beside = [tiles - 1, 0, 1]
    far = list(range(2, tiles - 1))
    cut = {shift: tile_for(shift) for shift in beside}
    tile = {0: cut[0], 1: fetched(cut.get, 1), tiles - 1: fetched(cut.get, tiles - 1)}
    slc, estimate, direction, cut = lax.optimization_barrier((slc, estimate, direction, cut))

    params = jnp.zeros((rows, LANES), f32)
    listed = jnp.concatenate([offsets.astype(f32), weights, weights, weights], axis=1)
    params = lax.dynamic_update_slice(params, listed, (0, PARAM_LANE))
    outer_tile = (2, epochs, rows, LANES)
    edge = pl.pallas_call(
        edge_kernel,
        out_shape=jax.ShapeDtypeStruct((rows, LANES), bf16),
        grid=(1,),
        in_specs=[
            pl.BlockSpec(outer_tile, lambda _: (0, 0, 0, 0)),
            pl.BlockSpec(outer_tile, lambda _: (0, 0, 0, tiles - 1)),
        ],
        out_specs=pl.BlockSpec((rows, LANES), lambda _: (0, 0)),
        compiler_params=params_of,
        cost_estimate=pl.CostEstimate(flops=1_000_000, bytes_accessed=1_000_000, transcendentals=0),
    )(slc, slc)
    fields = pl.pallas_call(
        fields_kernel,
        out_shape=jax.ShapeDtypeStruct((tiles, 3, epochs * look_rows, LANES), bf16),
        in_specs=[VMEM] * 2,
        out_specs=VMEM,
        compiler_params=params_of,
        cost_estimate=pl.CostEstimate(flops=1_000_000, bytes_accessed=2_000_000, transcendentals=0),
    )(estimate, direction)
    before, after = swapped(edge, edge, "sub")
    sub = lax.axis_index("sub")
    lane = lax.broadcasted_iota(jnp.int32, (rows, LANES), 1)
    inside = lane < 2 * epochs * SIDES
    left = jnp.where(inside & (lane % SIDES < RADIUS) & (sub > 0), before, jnp.zeros_like(edge))
    right = inside & (lane % SIDES >= RADIUS) & (sub < lax.axis_size("sub") - 1)
    right = jnp.where(right, after, jnp.zeros_like(edge))
    strips = pl.pallas_call(
        pack_kernel,
        out_shape=jax.ShapeDtypeStruct((tiles, rows, LANES), bf16),
        in_specs=[VMEM] * 4,
        out_specs=VMEM,
        compiler_params=params_of,
        cost_estimate=pl.CostEstimate(flops=3_000_000, bytes_accessed=2_000_000, transcendentals=0),
    )(slc, params, left, right)

    def strip_for(shift):
        return lax.dynamic_index_in_dim(strips, for_device(shift), axis=0, keepdims=False)

    def field_for(shift):
        return lax.dynamic_index_in_dim(fields, for_device(shift), axis=0, keepdims=False)

    def both_for(shift):
        return jnp.concatenate([tile_for(shift), strip_for(shift)], axis=0)

    strip = {0: strip_for(0), 1: fetched(strip_for, 1), tiles - 1: fetched(strip_for, tiles - 1)}
    both = {block: fetched(both_for, block) for block in far}
    field = {0: field_for(0)}
    fields = lax.optimization_barrier((fields, tile[1], tile[tiles - 1]))[0]
    for block in [1, tiles - 1] + far:
        field[block] = fetched(field_for, block)

    space = lax.axis_index("space")
    spaces = lax.axis_size("space")
    present = jnp.stack([space > 0, space < spaces - 1]).astype(f32)

    def halo(pieces):
        def border(from_row):
            cuts = [lax.dynamic_slice_in_dim(piece, from_row, HALO, axis=1).reshape(-1, LANES) for piece in pieces]
            return jnp.concatenate(cuts, axis=0)

        if spaces == 2:
            got = lax.ppermute(border(jnp.where(space == 0, rows - HALO, 0)), "space", [(0, 1), (1, 0)])
            return got, got
        return swapped(border(rows - HALO), border(0), "space")

    def by_rows(array):
        return array.reshape(-1, rows, LANES)

    def params_in(block):
        source = strip[block] if block in strip else both[block][tile_rows:]
        return source[:epochs, PARAM_LANE : PARAM_LANE + 4 * SLOTS].astype(f32)

    def pairs_of(blocks, loaded):
        listed = jnp.concatenate([params_in(block) for block in blocks], axis=0)
        mate = jnp.arange(len(blocks) * epochs, dtype=jnp.int32)[:, None] + listed[:, :SLOTS].astype(jnp.int32)
        weight = listed[:, SLOTS : 2 * SLOTS] + listed[:, 2 * SLOTS : 3 * SLOTS] + listed[:, 3 * SLOTS :]
        return mate.reshape(-1), weight.reshape(-1)

    mine = lax.optimization_barrier((tile[0], strip[0], strip[1], strip[tiles - 1]))
    own_halo = halo([by_rows(mine[0]), by_rows(mine[1])])
    near_halo = halo([by_rows(array[block]) for block in (1, tiles - 1) for array in (tile, strip)])
    def pair_stage(loaded):
        own = loaded[:-1]
        mate, weight = pairs_of(own, loaded)
        operands = []

        def index_of(array):
            for at, other in enumerate(operands):
                if other is array:
                    return at
            operands.append(array)
            return len(operands) - 1

        places = []
        for block in loaded:
            if block in tile:
                at = index_of(tile[block]), index_of(strip[block]), 0
            else:
                at = index_of(both[block]), index_of(both[block]), tile_rows
            source, slots = (near_halo, [1, tiles - 1]) if block in beside else (far_halo, far)
            if block == 0:
                source, slots = own_halo, [0]
            halo_row = slots.index(block) * (2 * epochs + 1) * HALO
            places.append(at + (index_of(source[0]), index_of(source[1]), halo_row))
        here = len(loaded) * epochs
        owned = len(own) * epochs
        group = 2 * SLOTS
        batches = len(loaded) + owned
        shape = jax.ShapeDtypeStruct((owned * SLOTS, look_rows, LANES), f32)
        return pl.pallas_call(
            functools.partial(pair_kernel, (epochs, rows, len(operands)), tuple(places)),
            out_shape=(shape, shape),
            in_specs=[SMEM] * 3 + [VMEM] * len(operands),
            out_specs=(VMEM, VMEM),
            scratch_shapes=[
                pltpu.VMEM((2 * here, LOOK, tall, LANES), f32),
                pltpu.VMEM((2 * here, tall, LANES), f32),
                pltpu.VMEM((batches * group * tall, LANES), f32),
                pltpu.VMEM((batches * 2 * tall, LANES), f32),
                pltpu.VMEM((batches * group * tall, LANES), f32),
                pltpu.VMEM((batches * group * tall, LANES), f32),
                pltpu.VMEM((owned, group * look_rows, LANES), f32),
                pltpu.VMEM((here, look_rows, LANES), f32),
            ],
            compiler_params=params_of,
            cost_estimate=pl.CostEstimate(flops=20_000_000, bytes_accessed=30_000_000, transcendentals=0),
        )(mate, weight, present, *operands)

    near_stage = beside
    far_stage = list(range(1, tiles))
    near_pairs = pair_stage(near_stage)
    both, near_pairs = lax.optimization_barrier((both, near_pairs))
    far_halo = halo([by_rows(both[block]) for block in far])
    far_pairs = pair_stage(far_stage)

    listed = jnp.concatenate([params_in(block) for block in range(tiles)], axis=0)
    partner = jnp.arange(total, dtype=jnp.int32)[:, None] + listed[:, :SLOTS].astype(jnp.int32)
    partner = lax.rem(partner, total).reshape(-1)
    stages = (tuple(near_stage[:-1]), tuple(far_stage[:-1]))
    gradient, sums = pl.pallas_call(
        functools.partial(gradient_kernel, (tiles, epochs, stages)),
        out_shape=(
            jax.ShapeDtypeStruct((total, look_rows, LANES), f32),
            jax.ShapeDtypeStruct((8, LANES), f32),
        ),
        in_specs=[SMEM] + [VMEM] * (tiles + 4),
        out_specs=(VMEM, VMEM),
        scratch_shapes=[pltpu.VMEM((total, look_rows, LANES), f32)] * 2,
        compiler_params=params_of,
        cost_estimate=pl.CostEstimate(flops=10_000_000, bytes_accessed=8_000_000, transcendentals=0),
    )(partner, *[field[block] for block in range(tiles)], near_pairs[0], far_pairs[0], near_pairs[1], far_pairs[1])

    along = [sums] + [to_ahead(sums, "epoch", by) for by in range(1, tiles)]
    here = sum(along[1:], along[0])
    place = ("space", "sub")
    count = spaces * lax.axis_size("sub")
    scalars = [here] + [lax.ppermute(here, place, [(i, (i + by) % count) for i in range(count)]) for by in range(1, count)]
    returned = [gradient[:epochs]]
    returned += [to_ahead(gradient[by * epochs : (by + 1) * epochs], "epoch", by) for by in range(1, tiles)]
    cell_count = float(total * look_rows * spaces * columns * lax.axis_size("sub"))
    return pl.pallas_call(
        functools.partial(update_kernel, cell_count),
        out_shape=(jax.ShapeDtypeStruct(estimate.shape, f32),) * 2,
        in_specs=[SMEM] * 2 + [VMEM] * (2 + tiles + count),
        out_specs=(VMEM, VMEM),
        compiler_params=params_of,
        cost_estimate=pl.CostEstimate(flops=1_000_000, bytes_accessed=2_000_000, transcendentals=0),
    )(me.reshape(1), prev_mean, estimate, direction, *returned, *scalars)


def on_device(slc, offsets, weights, estimate, direction, prev_mean):
    epochs, rows, columns = slc.shape[1:]
    fits = columns == LANES * lax.axis_size("epoch") and lax.axis_size("epoch") > 3
    fits = fits and 2 * epochs * SIDES <= PARAM_LANE and rows % HALO == 0 and epochs == 2 * SLOTS
    plan = transposed_plan if fits else ring_plan
    return plan(slc, offsets, weights, estimate, direction, prev_mean)


def solution(mesh):
    return jax.shard_map(
        on_device,
        mesh=mesh,
        in_specs=(
            P(None, ("groups", "epoch"), "space", "sub"),
            P(("groups", "epoch"), None),
            P(("groups", "epoch"), None),
            P(("groups", "epoch"), "space", "sub"),
            P(("groups", "epoch"), "space", "sub"),
            P(),
        ),
        out_specs=(P(("groups", "epoch"), "space", "sub"), P(("groups", "epoch"), "space", "sub")),
        check_vma=False,
    )
```

```python
import functools

import jax
import jax.numpy as jnp
from jax import lax
from jax.experimental import pallas as pl
from jax.experimental.pallas import tpu as pltpu
from jax.sharding import PartitionSpec as P

SLOTS = 4
OFFS = 8
LOOK = 4
RADIUS = 3


EPSILON = 1e-06


def passed_along(x, axis, by):
    size = lax.axis_size(axis)
    return lax.ppermute(x, axis, [(i, (i + by) % size) for i in range(size)])


def extended_2(block, sides, width):
    for axis, dim in sides:
        count = lax.axis_size(axis)
        forward = [(i, i + 1) for i in range(count - 1)]
        backward = [(target, source) for source, target in forward]
        low = lax.ppermute(
            lax.slice_in_dim(block, block.shape[dim] - width, None, axis=dim), axis, forward
        )
        high = lax.ppermute(lax.slice_in_dim(block, 0, width, axis=dim), axis, backward)
        block = jnp.concatenate([low, block, high], axis=dim)
    return block


def looked_sum(field):
    shape = field.shape
    return jnp.sum(field.reshape(shape[:-2] + (shape[-2] // LOOK, LOOK, shape[-1])), axis=-2)


def window_sum(padded, axis):
    length = padded.shape[axis] - 2 * RADIUS
    total = lax.slice_in_dim(padded, 0, length, axis=axis)
    for shift_at in range(1, 2 * RADIUS + 1):
        total = total + lax.slice_in_dim(padded, shift_at, shift_at + length, axis=axis)
    return total


def ring_plan(slc, offsets, weights, estimate, direction, prev_mean):
    epochs_here = slc.shape[1]
    look_rows = slc.shape[2] // LOOK
    col_count = slc.shape[3]
    ahead = passed_along(slc, "epoch", -1)
    extended = jnp.concatenate([slc, ahead], axis=1)
    numbers = jnp.arange(epochs_here, dtype=jnp.int32)
    partner = numbers[:, None] + offsets
    own_real = slc[0].astype(jnp.float32)
    own_imag = slc[1].astype(jnp.float32)
    ext_real = extended[0].astype(jnp.float32)
    ext_imag = extended[1].astype(jnp.float32)
    powers = looked_sum(ext_real * ext_real + ext_imag * ext_imag)
    pieces = []
    for slot_index in range(SLOTS):
        mate_real = jnp.take(ext_real, partner[:, slot_index], axis=0)
        mate_imag = jnp.take(ext_imag, partner[:, slot_index], axis=0)
        pieces.append(looked_sum(own_real * mate_real + own_imag * mate_imag))
        pieces.append(looked_sum(own_imag * mate_real - own_real * mate_imag))
    pair_count = epochs_here * 2 * SLOTS
    stacked = jnp.concatenate(
        [jnp.stack(pieces, axis=1).reshape(pair_count, look_rows, col_count), powers], axis=0
    )
    padded = extended_2(stacked, (("space", 1), ("sub", 2)), RADIUS)
    boxed = window_sum(window_sum(padded, 1), 2)
    pair_boxed = boxed[:pair_count].reshape(epochs_here, 2 * SLOTS, look_rows, col_count)
    power_box = boxed[pair_count:]
    coh_real = pair_boxed[:, 0::2]
    coh_imag = pair_boxed[:, 1::2]
    denominator = power_box[:epochs_here, None] * jnp.take(power_box, partner, axis=0) + EPSILON
    coherence = (coh_real * coh_real + coh_imag * coh_imag) / denominator
    observed = coh_imag / jnp.sqrt(denominator)
    est_ahead = passed_along(estimate, "epoch", -1)
    est_extended = jnp.concatenate([estimate, est_ahead], axis=0)
    fitted = estimate[:, None] - jnp.take(est_extended, partner, axis=0)
    factor = weights[:, :, None, None] * coherence
    weighted = factor * (observed - fitted)
    flattened = weighted.reshape(epochs_here * SLOTS, look_rows * col_count)
    selector = (
        jnp.arange(epochs_here + OFFS, dtype=jnp.int32)[:, None] == partner.reshape(1, -1)
    ).astype(jnp.float32)
    gathered = jnp.dot(
        selector, flattened, precision=lax.Precision.HIGHEST, preferred_element_type=jnp.float32
    ).reshape(epochs_here + OFFS, look_rows, col_count)
    own_part = jnp.sum(weighted, axis=1) - gathered[:epochs_here]
    returned = passed_along(-gathered[epochs_here:], "epoch", 1)
    gradient = jnp.concatenate([own_part + returned, own_part[OFFS:]], axis=0)
    cell_count = float(
        epochs_here
        * lax.axis_size("epoch")
        * look_rows
        * lax.axis_size("space")
        * col_count
        * lax.axis_size("sub")
    )
    local_norm = jnp.sum(gradient * gradient)
    local_crossed = jnp.sum(gradient * direction)
    mean_before = prev_mean[0]
    fields_ahead = passed_along(
        jnp.stack([gradient, direction]).astype(jnp.bfloat16), "epoch", -1
    ).astype(jnp.float32)
    grad_extended = jnp.concatenate([gradient, fields_ahead[0]], axis=0)
    old_extended = jnp.concatenate([direction, fields_ahead[1]], axis=0)
    grad_spread = gradient[:, None] - jnp.take(grad_extended, partner, axis=0)
    old_spread = direction[:, None] - jnp.take(old_extended, partner, axis=0)
    totals = lax.psum(
        (
            local_norm,
            local_crossed,
            jnp.sum(factor * grad_spread * grad_spread),
            jnp.sum(factor * grad_spread * old_spread),
            jnp.sum(factor * old_spread * old_spread),
        ),
        ("epoch", "space", "sub"),
    )
    grad_norm, crossed, grad_term, mixed_term, old_term = totals
    momentum = grad_norm / cell_count / mean_before
    new_direction = gradient + momentum * direction
    curvature = grad_term + 2.0 * momentum * mixed_term + momentum * momentum * old_term
    along_sum = grad_norm + momentum * crossed
    step_size = along_sum / curvature
    return (estimate + step_size * new_direction, new_direction)


LANES = 128
SIDES = 2 * RADIUS
HALO = 16
PARAM_LANE = 96
VMEM = pl.BlockSpec(memory_space=pltpu.VMEM)
SMEM = pl.BlockSpec(memory_space=pltpu.SMEM)
VMEM_BYTES = 48 * 1024 * 1024


def split_two(value):
    high = value.astype(jnp.bfloat16)
    low = (value - high.astype(jnp.float32)).astype(jnp.bfloat16)
    return high, low


def edge_kernel(first, last, edge):
    epochs = first.shape[1]
    lane = lax.broadcasted_iota(jnp.int32, edge.shape, 1)
    total = jnp.zeros(edge.shape, jnp.float32)
    for part in range(2):
        for epoch in range(epochs):
            at = (part * epochs + epoch) * SIDES
            total = placed(lane, total, tile_of(last, part, epoch, 0), LANES - RADIUS, at)
            total = placed(lane, total, tile_of(first, part, epoch, 0), 0, at + RADIUS)
    edge[...] = total.astype(jnp.bfloat16)


def fields_kernel(me, estimate, direction, *fields):
    look_rows = estimate.shape[1]
    tiles = len(fields)
    for shift, out in enumerate(fields):
        tile = lax.rem(me[0] + shift, tiles)
        columns = pl.ds(pl.multiple_of(tile * LANES, LANES), LANES)
        for epoch in range(estimate.shape[0]):
            here = slice(epoch * look_rows, (epoch + 1) * look_rows)
            first, second = split_two(estimate[epoch, :, columns])
            out[0, here, :] = first
            out[1, here, :] = second
            out[2, here, :] = direction[epoch, :, columns].astype(jnp.bfloat16)


def tile_of(slc, part, epoch, tile):
    return slc[part, epoch, :, tile * LANES : (tile + 1) * LANES].astype(jnp.float32)


def placed(lane, total, source, start, target):
    moved = pltpu.roll(source, (target - start) % LANES, axis=1)
    return jnp.where((lane >= target) & (lane < target + RADIUS), moved, total)


def pack_kernel(me, present, slc, params, before, after, *refs):
    messages, strips = refs[:-1], refs[-1]
    tiles = len(messages)
    epochs = slc.shape[1]
    rows = slc.shape[2]
    lane = lax.broadcasted_iota(jnp.int32, (rows, LANES), 1)
    value = params[...]
    high = value.astype(jnp.bfloat16).astype(jnp.float32)
    middle = (value - high).astype(jnp.bfloat16).astype(jnp.float32)
    low = value - high - middle
    third = PARAM_LANE + 2 * SLOTS
    split = jnp.where(lane < third, high, jnp.where(lane < third + SLOTS, middle, low))
    split = jnp.where(lane >= PARAM_LANE, split, 0.0)
    inside = lane < 2 * epochs * SIDES
    for tile in range(tiles):
        total = split
        if tile == 0:
            edge = before[...].astype(jnp.float32) * present[0]
            total = jnp.where(inside & (lane % SIDES < RADIUS), edge, total)
        if tile == tiles - 1:
            edge = after[...].astype(jnp.float32) * present[1]
            total = jnp.where(inside & (lane % SIDES >= RADIUS), edge, total)
        for part in range(2):
            for epoch in range(epochs):
                at = (part * epochs + epoch) * SIDES
                if tile > 0:
                    total = placed(lane, total, tile_of(slc, part, epoch, tile - 1), LANES - RADIUS, at)
                if tile < tiles - 1:
                    total = placed(lane, total, tile_of(slc, part, epoch, tile + 1), 0, at + RADIUS)
        strips[tile] = total.astype(jnp.bfloat16)
    for shift, message in enumerate(messages):
        tile = lax.rem(me[0] + shift, tiles)
        columns = pl.ds(pl.multiple_of(tile * LANES, LANES), LANES)
        for part in range(2):
            for epoch in range(epochs):
                at = (part * epochs + epoch) * rows
                message[at : at + rows, :] = slc[part, epoch, :, columns]
        message[2 * epochs * rows :, :] = strips[tile]


def pair_kernel(sizes, places, partner, weight, present, *refs):
    epochs, rows, operands = sizes
    inputs = refs[:operands]
    factors, pulls = refs[operands : operands + 2]
    main, rim, looked, rim_looked, wide, outer, boxed, power_box = refs[operands + 2 :]
    count = len(places)
    look_rows = rows // LOOK
    tall = (rows + 2 * HALO) // LOOK
    halo_looks = HALO // LOOK
    full_rows = rows + 2 * HALO
    total = count * epochs
    own_total = total - epochs
    group = 2 * SLOTS
    group_rows = group * tall
    share = LANES // SLOTS
    has_top = present[0]
    has_bottom = present[1]
    f32 = jnp.float32

    def band_of(shape, from_of, to_of):
        at = lax.broadcasted_iota(jnp.int32, shape, 0)
        to = lax.broadcasted_iota(jnp.int32, shape, 1)
        return (jnp.abs(from_of(at, to) - to_of(to)) <= RADIUS).astype(f32).astype(jnp.bfloat16)

    def rim_column(at, to):
        at = at % LANES
        side = at % share % SIDES
        column = jnp.where(side < RADIUS, side - RADIUS, LANES + side - RADIUS)
        inside = (at // share == to // LANES) & (at % share < LOOK * SIDES)
        return jnp.where(inside, column, -4 * LANES)

    band = band_of((2 * LANES, LANES), lambda at, to: at % LANES, lambda to: to)
    rim_band = band_of((2 * LANES, SLOTS * LANES), rim_column, lambda to: to % LANES)

    out_at = lax.broadcasted_iota(jnp.int32, (group * look_rows, group * tall), 0)
    in_at = lax.broadcasted_iota(jnp.int32, (group * look_rows, group * tall), 1)
    near = jnp.abs(in_at % tall - halo_looks - out_at % look_rows) <= RADIUS
    near = near & (in_at // tall == out_at // look_rows)
    sum_rows = near.astype(f32).astype(jnp.bfloat16)

    out_at = lax.broadcasted_iota(jnp.int32, (full_rows, full_rows), 0)
    in_at = lax.broadcasted_iota(jnp.int32, (full_rows, full_rows), 1)
    order = (in_at == out_at % tall * LOOK + out_at // tall).astype(f32)
    order = jnp.where(in_at < HALO, order * has_top, order)
    order = jnp.where(in_at >= HALO + rows, order * has_bottom, order).astype(jnp.bfloat16)

    lane = lax.broadcasted_iota(jnp.int32, (tall, LANES), 1)
    for block, (tile_at, top_at, bottom_at, halo_row) in enumerate(places):
        tile, top, bottom = inputs[tile_at], inputs[top_at], inputs[bottom_at]

        @pl.loop(0, epochs // 2)
        def _(quad):
            for couple in range(2):
                columns = []
                for one in range(2):
                    at = quad * 4 + couple * 2 + one
                    row = pl.multiple_of(halo_row + at * HALO, HALO)
                    own = pl.multiple_of(at * rows, rows)
                    parts = [top[pl.ds(row, HALO), :], tile[pl.ds(own, rows), :], bottom[pl.ds(row, HALO), :]]
                    columns.append(jnp.concatenate(parts, axis=0))
                value = jnp.dot(order, jnp.concatenate(columns, axis=1), preferred_element_type=f32)
                for one in range(2):
                    at = block * 2 * epochs + quad * 4 + couple * 2 + one
                    for look in range(LOOK):
                        main[at, look] = value[look * tall : (look + 1) * tall, one * LANES : (one + 1) * LANES]

        last = slice(halo_row + 2 * epochs * HALO, halo_row + 2 * epochs * HALO + HALO)
        parts = [top[last, :], tile[2 * epochs * rows :, :], bottom[last, :]]
        by_look = jnp.dot(order, jnp.concatenate(parts, axis=0), preferred_element_type=f32)
        for at in range(2 * epochs):
            value = jnp.zeros((tall, LANES), f32)
            for look in range(LOOK):
                target = look * SIDES
                moved = by_look[look * tall : (look + 1) * tall]
                moved = pltpu.roll(moved, (target - at * SIDES) % LANES, axis=1)
                value = jnp.where((lane >= target) & (lane < target + SIDES), moved, value)
            spread = share
            while spread < LANES:
                value = value + pltpu.roll(value, spread, axis=1)
                spread = 2 * spread
            rim[block * 2 * epochs + at] = value

    def places_of(epoch):
        at = epoch // epochs * (2 * epochs) + epoch % epochs
        return at, at + epochs

    piece_lane = lax.broadcasted_iota(jnp.int32, (8, LANES), 1)
    slot_lane = [piece_lane // share == slot for slot in range(SLOTS)]

    def mixed(values):
        result = values[-1]
        for slot in range(SLOTS - 1):
            result = jnp.where(slot_lane[slot], values[slot], result)
        return result

    def channel_rows(batch, piece, channel):
        return pl.ds(pl.multiple_of(batch * group_rows + channel * tall + piece, 8), 8)

    for block in range(count):
        for piece in range(0, tall, 8):
            rows_at = slice(piece, piece + 8)
            for half in range(2):
                squares = []
                for slot in range(SLOTS):
                    channel = half * SLOTS + slot
                    re_at, im_at = places_of(block * epochs + channel)
                    value = None
                    for look in range(LOOK):
                        real = main[re_at, look, rows_at]
                        imag = main[im_at, look, rows_at]
                        one = real * real + imag * imag
                        value = one if value is None else value + one
                    looked[channel_rows(block, piece, channel), :] = value
                    real = rim[re_at, rows_at]
                    imag = rim[im_at, rows_at]
                    squares.append(real * real + imag * imag)
                at = block * 2 * tall + half * tall + piece
                rim_looked[at : at + 8, :] = mixed(squares)

    @pl.loop(0, own_total)
    def _(epoch):
        batch = count + epoch
        re_at, im_at = places_of(epoch)
        mates = [places_of(partner[epoch * SLOTS + slot]) for slot in range(SLOTS)]
        for piece in range(0, tall, 8):
            rows_at = slice(piece, piece + 8)
            own_re = [main[re_at, look, rows_at] for look in range(LOOK)]
            own_im = [main[im_at, look, rows_at] for look in range(LOOK)]
            for slot, (mate_re_at, mate_im_at) in enumerate(mates):
                real = None
                for look in range(LOOK):
                    mate_re = main[mate_re_at, look, rows_at]
                    mate_im = main[mate_im_at, look, rows_at]
                    one = own_re[look] * mate_re + own_im[look] * mate_im
                    two = own_im[look] * mate_re - own_re[look] * mate_im
                    real = one if real is None else real + one
                    imag = two if look == 0 else imag + two
                looked[channel_rows(batch, piece, slot), :] = real
                looked[channel_rows(batch, piece, SLOTS + slot), :] = imag
            rim_re = rim[re_at, rows_at]
            rim_im = rim[im_at, rows_at]
            mate_re = mixed([rim[at, rows_at] for at, _ in mates])
            mate_im = mixed([rim[at, rows_at] for _, at in mates])
            at = pl.multiple_of(batch * (2 * tall) + piece, 8)
            rim_looked[pl.ds(at, 8), :] = rim_re * mate_re + rim_im * mate_im
            at = pl.multiple_of(batch * (2 * tall) + tall + piece, 8)
            rim_looked[pl.ds(at, 8), :] = rim_im * mate_re - rim_re * mate_im

    def columns_summed(batch, batches):
        at = pl.ds(pl.multiple_of(batch * group_rows, group_rows), batches * group_rows)
        halves = jnp.concatenate(split_two(looked[at, :]), axis=1)
        wide[at, :] = jnp.dot(halves, band, preferred_element_type=f32)
        rim_at = pl.ds(pl.multiple_of(batch * (2 * tall), 2 * tall), batches * 2 * tall)
        halves = jnp.concatenate(split_two(rim_looked[rim_at, :]), axis=1)
        value = jnp.dot(halves, rim_band, preferred_element_type=f32)
        for one in range(batches):
            for half in range(2):
                for piece in range(0, tall, 8):
                    row = (2 * one + half) * tall + piece
                    for slot in range(SLOTS):
                        to = channel_rows(batch + one, piece, half * SLOTS + slot)
                        outer[to, :] = value[row : row + 8, slot * LANES : (slot + 1) * LANES]

    columns_summed(0, count)

    @pl.loop(0, own_total // 4)
    def _(quad):
        columns_summed(count + quad * 4, 4)

    def rows_summed(batch):
        at = pl.ds(pl.multiple_of(batch * group_rows, group_rows), group_rows)
        halves = jnp.concatenate(split_two(wide[at, :] + outer[at, :]), axis=1)
        value = jnp.dot(sum_rows, halves, preferred_element_type=f32)
        return value[:, :LANES] + value[:, LANES:]

    for block in range(count):
        value = rows_summed(block)
        for channel in range(epochs):
            power_box[block * epochs + channel] = value[channel * look_rows : (channel + 1) * look_rows]

    @pl.loop(0, own_total // 4)
    def _(quad):
        for one in range(4):
            boxed[quad * 4 + one] = rows_summed(count + quad * 4 + one)

    @pl.loop(0, own_total // 2)
    def _(couple):
        for one in range(2):
            epoch = couple * 2 + one
            own_power = power_box[epoch]
            for slot in range(SLOTS):
                pair = epoch * SLOTS + slot
                inverse = lax.rsqrt(own_power * power_box[partner[pair]] + EPSILON)
                unit_re = boxed[epoch, slot * look_rows : (slot + 1) * look_rows, :] * inverse
                unit_im = boxed[epoch, (SLOTS + slot) * look_rows : (SLOTS + slot + 1) * look_rows, :] * inverse
                factor = weight[pair] * (unit_re * unit_re + unit_im * unit_im)
                factors[pair] = factor
                pulls[pair] = factor * unit_im


def gradient_kernel(sizes, partner, *refs):
    tiles, epochs, stages = sizes
    fields = refs[:tiles]
    factors = refs[tiles : tiles + len(stages)]
    pulls = refs[tiles + len(stages) : tiles + 2 * len(stages)]
    gradient, est = refs[tiles + 2 * len(stages) :]
    look_rows = est.shape[1]
    f32 = jnp.float32
    for block in range(tiles):

        @pl.loop(0, epochs, unroll=4)
        def _(epoch):
            here = pl.ds(pl.multiple_of(epoch * look_rows, look_rows), look_rows)
            est[block * epochs + epoch] = fields[block][0, here, :].astype(f32) + fields[block][1, here, :].astype(f32)
            gradient[block * epochs + epoch] = jnp.zeros((look_rows, LANES), f32)

    for stage, own_blocks in enumerate(stages):
        for number, block in enumerate(own_blocks):

            @pl.loop(0, epochs, unroll=2)
            def _(here):
                epoch = block * epochs + here
                own_est = est[epoch]
                own = jnp.zeros((look_rows, LANES), f32)
                mates = [partner[epoch * SLOTS + slot] for slot in range(SLOTS)]
                values = []
                for slot, mate in enumerate(mates):
                    pair = (number * epochs + here) * SLOTS + slot
                    weighted = pulls[stage][pair] - factors[stage][pair] * (own_est - est[mate])
                    own = own + weighted
                    values.append(weighted)
                for mate, weighted in zip(mates, values):
                    gradient[mate] = gradient[mate] - weighted
                gradient[epoch] = gradient[epoch] + own


def sums_kernel(sizes, partner, gradient, *refs):
    tiles, epochs, stages = sizes
    fields = refs[:tiles]
    factors = refs[tiles : tiles + len(stages)]
    sums, old = refs[tiles + len(stages) :]
    look_rows = old.shape[1]
    f32 = jnp.float32
    for block in range(tiles):

        @pl.loop(0, epochs, unroll=4)
        def _(epoch):
            here = pl.ds(pl.multiple_of(epoch * look_rows, look_rows), look_rows)
            old[block * epochs + epoch] = fields[block][2, here, :].astype(f32)

    zero = jnp.zeros((look_rows, LANES), f32)
    results = (zero,) * 5
    for stage, own_blocks in enumerate(stages):
        for number, block in enumerate(own_blocks):

            def totals(here, carry):
                norm, crossed, grad_term, mixed, old_term = carry
                epoch = block * epochs + here
                own_grad = gradient[epoch]
                own_old = old[epoch]
                norm = norm + own_grad * own_grad
                crossed = crossed + own_grad * own_old
                for slot in range(SLOTS):
                    mate = partner[epoch * SLOTS + slot]
                    factor = factors[stage][(number * epochs + here) * SLOTS + slot]
                    grad_spread = own_grad - gradient[mate]
                    old_spread = own_old - old[mate]
                    pulled = factor * grad_spread
                    grad_term = grad_term + pulled * grad_spread
                    mixed = mixed + pulled * old_spread
                    old_term = old_term + factor * old_spread * old_spread
                return norm, crossed, grad_term, mixed, old_term

            results = lax.fori_loop(0, epochs, totals, results, unroll=2)
    sums[...] = jnp.zeros(sums.shape, f32)
    for at, value in enumerate(results):
        sums[at : at + 1, :] = jnp.sum(value, axis=0, keepdims=True)


def update_kernel(cell_count, me, prev_mean, estimate, direction, *refs):
    new_estimate, new_direction = refs[-2:]
    tiles = estimate.shape[2] // LANES
    pieces = refs[:tiles]
    scalars = refs[tiles:-2]
    epochs = estimate.shape[0]
    look_rows = estimate.shape[1]
    total = scalars[0][...]
    for other in scalars[1:]:
        total = total + other[...]
    total = jnp.sum(total, axis=1, keepdims=True)
    grad_norm, crossed, grad_term, mixed, old_term = (total[at : at + 1, :] for at in range(5))
    momentum = grad_norm / cell_count / prev_mean[0]
    curvature = grad_term + 2.0 * momentum * mixed + momentum * momentum * old_term
    step = (grad_norm + momentum * crossed) / curvature
    momentum = jnp.broadcast_to(momentum, (look_rows, LANES))
    step = jnp.broadcast_to(step, (look_rows, LANES))
    for shift, piece in enumerate(pieces):
        tile = lax.rem(me[0] - shift + tiles, tiles)
        columns = pl.ds(pl.multiple_of(tile * LANES, LANES), LANES)
        for epoch in range(epochs):
            gradient = piece[epoch]
            moved = gradient + momentum * direction[epoch, :, columns]
            new_direction[epoch, :, columns] = moved
            new_estimate[epoch, :, columns] = estimate[epoch, :, columns] + step * moved


def swapped(up, down, axis):
    size = lax.axis_size(axis)
    if size == 1:
        return jnp.zeros_like(up), jnp.zeros_like(down)
    if size == 2:
        first = lax.axis_index(axis) == 0
        got = lax.ppermute(jnp.where(first, up, down), axis, [(0, 1), (1, 0)])
        return got, got
    forward = [(i, i + 1) for i in range(size - 1)]
    backward = [(target, source) for source, target in forward]
    return lax.ppermute(up, axis, forward), lax.ppermute(down, axis, backward)


def to_ahead(x, axis, by):
    size = lax.axis_size(axis)
    return lax.ppermute(x, axis, [(i, (i + by) % size) for i in range(size)])


def transposed_plan(slc, offsets, weights, estimate, direction, prev_mean):
    f32 = jnp.float32
    bf16 = jnp.bfloat16
    tiles = lax.axis_size("epoch")
    me = lax.axis_index("epoch")
    epochs, rows, columns = slc.shape[1:]
    look_rows = rows // LOOK
    total = tiles * epochs
    tall = (rows + 2 * HALO) // LOOK
    tile_rows = 2 * epochs * rows
    params_of = pltpu.CompilerParams(vmem_limit_bytes=VMEM_BYTES)

    def fetched(messages, shift):
        return to_ahead(messages[tiles - shift], "epoch", tiles - shift)

    beside = [tiles - 1, 0, 1]
    far = list(range(2, tiles - 1))
    sub = lax.axis_index("sub")
    outer_tile = (2, epochs, rows, LANES)
    edge = pl.pallas_call(
        edge_kernel,
        out_shape=jax.ShapeDtypeStruct((rows, LANES), bf16),
        grid=(1,),
        in_specs=[
            pl.BlockSpec(outer_tile, lambda _: (0, 0, 0, 0)),
            pl.BlockSpec(outer_tile, lambda _: (0, 0, 0, tiles - 1)),
        ],
        out_specs=pl.BlockSpec((rows, LANES), lambda _: (0, 0)),
        compiler_params=params_of,
        cost_estimate=pl.CostEstimate(flops=1_000_000, bytes_accessed=1_000_000, transcendentals=0),
    )(slc, slc)
    before, after = swapped(edge, edge, "sub")
    params = jnp.zeros((rows, LANES), f32)
    listed = jnp.concatenate([offsets.astype(f32), weights, weights, weights], axis=1)
    params = lax.dynamic_update_slice(params, listed, (0, PARAM_LANE))
    sub_present = jnp.stack([sub > 0, sub < lax.axis_size("sub") - 1]).astype(f32)
    messages = pl.pallas_call(
        pack_kernel,
        out_shape=(jax.ShapeDtypeStruct((tile_rows + rows, LANES), bf16),) * tiles,
        in_specs=[SMEM] * 2 + [VMEM] * 4,
        out_specs=(VMEM,) * tiles,
        scratch_shapes=[pltpu.VMEM((tiles, rows, LANES), bf16)],
        compiler_params=params_of,
        cost_estimate=pl.CostEstimate(flops=3_000_000, bytes_accessed=4_000_000, transcendentals=0),
    )(me.reshape(1), sub_present, slc, params, before, after)
    block = {0: messages[0], 1: fetched(messages, 1), tiles - 1: fetched(messages, tiles - 1)}

    estimate, direction, _ = lax.optimization_barrier((estimate, direction, messages))
    fields = pl.pallas_call(
        fields_kernel,
        out_shape=(jax.ShapeDtypeStruct((3, epochs * look_rows, LANES), bf16),) * tiles,
        in_specs=[SMEM] + [VMEM] * 2,
        out_specs=(VMEM,) * tiles,
        compiler_params=params_of,
        cost_estimate=pl.CostEstimate(flops=1_000_000, bytes_accessed=2_000_000, transcendentals=0),
    )(me.reshape(1), estimate, direction)
    late = lax.optimization_barrier((fields, block[1], block[tiles - 1]))[0]
    field = {0: fields[0]}
    for shift in [1, tiles - 1] + far:
        field[shift] = fetched(late, shift)

    space = lax.axis_index("space")
    spaces = lax.axis_size("space")
    present = jnp.stack([space > 0, space < spaces - 1]).astype(f32)

    def halo(pieces):
        def border(from_row):
            cuts = [lax.dynamic_slice_in_dim(piece, from_row, HALO, axis=1).reshape(-1, LANES) for piece in pieces]
            return jnp.concatenate(cuts, axis=0)

        if spaces == 2:
            got = lax.ppermute(border(jnp.where(space == 0, rows - HALO, 0)), "space", [(0, 1), (1, 0)])
            return got, got
        return swapped(border(rows - HALO), border(0), "space")

    def by_rows(shift):
        return block[shift].reshape(-1, rows, LANES)

    def params_in(shift):
        return block[shift][tile_rows : tile_rows + epochs, PARAM_LANE : PARAM_LANE + 4 * SLOTS].astype(f32)

    def pairs_of(blocks, loaded):
        listed = jnp.concatenate([params_in(block) for block in blocks], axis=0)
        mate = jnp.arange(len(blocks) * epochs, dtype=jnp.int32)[:, None] + listed[:, :SLOTS].astype(jnp.int32)
        weight = listed[:, SLOTS : 2 * SLOTS] + listed[:, 2 * SLOTS : 3 * SLOTS] + listed[:, 3 * SLOTS :]
        return mate.reshape(-1), weight.reshape(-1)

    own_halo = halo([by_rows(0)])
    after_halo = lax.optimization_barrier((messages, own_halo))[0]
    block.update({shift: fetched(after_halo, shift) for shift in far})
    near_halo = halo([by_rows(1), by_rows(tiles - 1)])

    def pair_stage(loaded):
        own = loaded[:-1]
        mate, weight = pairs_of(own, loaded)
        operands = []

        def index_of(array):
            for at, other in enumerate(operands):
                if other is array:
                    return at
            operands.append(array)
            return len(operands) - 1

        places = []
        for shift in loaded:
            source, slots = (near_halo, [1, tiles - 1]) if shift in beside else (far_halo, far)
            if shift == 0:
                source, slots = own_halo, [0]
            halo_row = slots.index(shift) * (2 * epochs + 1) * HALO
            places.append((index_of(block[shift]), index_of(source[0]), index_of(source[1]), halo_row))
        here = len(loaded) * epochs
        owned = len(own) * epochs
        group = 2 * SLOTS
        batches = len(loaded) + owned
        shape = jax.ShapeDtypeStruct((owned * SLOTS, look_rows, LANES), f32)
        return pl.pallas_call(
            functools.partial(pair_kernel, (epochs, rows, len(operands)), tuple(places)),
            out_shape=(shape, shape),
            in_specs=[SMEM] * 3 + [VMEM] * len(operands),
            out_specs=(VMEM, VMEM),
            scratch_shapes=[
                pltpu.VMEM((2 * here, LOOK, tall, LANES), f32),
                pltpu.VMEM((2 * here, tall, LANES), f32),
                pltpu.VMEM((batches * group * tall, LANES), f32),
                pltpu.VMEM((batches * 2 * tall, LANES), f32),
                pltpu.VMEM((batches * group * tall, LANES), f32),
                pltpu.VMEM((batches * group * tall, LANES), f32),
                pltpu.VMEM((owned, group * look_rows, LANES), f32),
                pltpu.VMEM((here, look_rows, LANES), f32),
            ],
            compiler_params=params_of,
            cost_estimate=pl.CostEstimate(flops=20_000_000, bytes_accessed=30_000_000, transcendentals=0),
        )(mate, weight, present, *operands)

    near_stage = beside
    far_stage = list(range(1, tiles))
    near_pairs = pair_stage(near_stage)
    held, near_pairs = lax.optimization_barrier(([block[shift] for shift in far], near_pairs))
    block.update(zip(far, held))
    far_halo = halo([by_rows(shift) for shift in far])
    far_pairs = pair_stage(far_stage)

    listed = jnp.concatenate([params_in(shift) for shift in range(tiles)], axis=0)
    partner = jnp.arange(total, dtype=jnp.int32)[:, None] + listed[:, :SLOTS].astype(jnp.int32)
    partner = lax.rem(partner, total).reshape(-1)
    stages = (tuple(near_stage[:-1]), tuple(far_stage[:-1]))
    block_fields = [field[shift] for shift in range(tiles)]
    sizes = (tiles, epochs, stages)
    gradient = pl.pallas_call(
        functools.partial(gradient_kernel, sizes),
        out_shape=jax.ShapeDtypeStruct((total, look_rows, LANES), f32),
        in_specs=[SMEM] + [VMEM] * (tiles + 4),
        out_specs=VMEM,
        scratch_shapes=[pltpu.VMEM((total, look_rows, LANES), f32)],
        compiler_params=params_of,
        cost_estimate=pl.CostEstimate(flops=10_000_000, bytes_accessed=4_000_000, transcendentals=0),
    )(partner, *block_fields, near_pairs[0], far_pairs[0], near_pairs[1], far_pairs[1])
    returned = [gradient[:epochs]]
    returned += [to_ahead(gradient[by * epochs : (by + 1) * epochs], "epoch", by) for by in range(1, tiles)]
    gradient = lax.optimization_barrier((gradient, returned[1]))[0]
    sums = pl.pallas_call(
        functools.partial(sums_kernel, sizes),
        out_shape=jax.ShapeDtypeStruct((8, LANES), f32),
        in_specs=[SMEM] + [VMEM] * (tiles + 3),
        out_specs=VMEM,
        scratch_shapes=[pltpu.VMEM((total, look_rows, LANES), f32)],
        compiler_params=params_of,
        cost_estimate=pl.CostEstimate(flops=10_000_000, bytes_accessed=8_000_000, transcendentals=0),
    )(partner, gradient, *block_fields, near_pairs[0], far_pairs[0])
    place = ("space", "sub")
    count = spaces * lax.axis_size("sub")
    along = [sums] + [lax.ppermute(sums, place, [(i, (i + by) % count) for i in range(count)]) for by in range(1, count)]
    here = sum(along[1:], along[0])
    scalars = [here] + [to_ahead(here, "epoch", by) for by in range(1, tiles)]
    cell_count = float(total * look_rows * spaces * columns * lax.axis_size("sub"))
    return pl.pallas_call(
        functools.partial(update_kernel, cell_count),
        out_shape=(jax.ShapeDtypeStruct(estimate.shape, f32),) * 2,
        in_specs=[SMEM] * 2 + [VMEM] * (2 + 2 * tiles),
        out_specs=(VMEM, VMEM),
        compiler_params=params_of,
        cost_estimate=pl.CostEstimate(flops=1_000_000, bytes_accessed=2_000_000, transcendentals=0),
    )(me.reshape(1), prev_mean, estimate, direction, *returned, *scalars)


def on_device(slc, offsets, weights, estimate, direction, prev_mean):
    epochs, rows, columns = slc.shape[1:]
    fits = columns == LANES * lax.axis_size("epoch") and lax.axis_size("epoch") > 3
    fits = fits and 2 * epochs * SIDES <= PARAM_LANE and rows % HALO == 0 and epochs == 2 * SLOTS
    plan = transposed_plan if fits else ring_plan
    return plan(slc, offsets, weights, estimate, direction, prev_mean)


def solution(mesh):
    return jax.shard_map(
        on_device,
        mesh=mesh,
        in_specs=(
            P(None, ("groups", "epoch"), "space", "sub"),
            P(("groups", "epoch"), None),
            P(("groups", "epoch"), None),
            P(("groups", "epoch"), "space", "sub"),
            P(("groups", "epoch"), "space", "sub"),
            P(),
        ),
        out_specs=(P(("groups", "epoch"), "space", "sub"), P(("groups", "epoch"), "space", "sub")),
        check_vma=False,
    )
```

```python
import functools

import jax
import jax.numpy as jnp
from jax import lax
from jax.experimental import pallas as pl
from jax.experimental.pallas import tpu as pltpu
from jax.sharding import PartitionSpec as P

SLOTS = 4
OFFS = 8
LOOK = 4
RADIUS = 3


EPSILON = 1e-06


def passed_along(x, axis, by):
    size = lax.axis_size(axis)
    return lax.ppermute(x, axis, [(i, (i + by) % size) for i in range(size)])


def extended_2(block, sides, width):
    for axis, dim in sides:
        count = lax.axis_size(axis)
        forward = [(i, i + 1) for i in range(count - 1)]
        backward = [(target, source) for source, target in forward]
        low = lax.ppermute(
            lax.slice_in_dim(block, block.shape[dim] - width, None, axis=dim), axis, forward
        )
        high = lax.ppermute(lax.slice_in_dim(block, 0, width, axis=dim), axis, backward)
        block = jnp.concatenate([low, block, high], axis=dim)
    return block


def looked_sum(field):
    shape = field.shape
    return jnp.sum(field.reshape(shape[:-2] + (shape[-2] // LOOK, LOOK, shape[-1])), axis=-2)


def window_sum(padded, axis):
    length = padded.shape[axis] - 2 * RADIUS
    total = lax.slice_in_dim(padded, 0, length, axis=axis)
    for shift_at in range(1, 2 * RADIUS + 1):
        total = total + lax.slice_in_dim(padded, shift_at, shift_at + length, axis=axis)
    return total


def ring_plan(slc, offsets, weights, estimate, direction, prev_mean):
    epochs_here = slc.shape[1]
    look_rows = slc.shape[2] // LOOK
    col_count = slc.shape[3]
    ahead = passed_along(slc, "epoch", -1)
    extended = jnp.concatenate([slc, ahead], axis=1)
    numbers = jnp.arange(epochs_here, dtype=jnp.int32)
    partner = numbers[:, None] + offsets
    own_real = slc[0].astype(jnp.float32)
    own_imag = slc[1].astype(jnp.float32)
    ext_real = extended[0].astype(jnp.float32)
    ext_imag = extended[1].astype(jnp.float32)
    powers = looked_sum(ext_real * ext_real + ext_imag * ext_imag)
    pieces = []
    for slot_index in range(SLOTS):
        mate_real = jnp.take(ext_real, partner[:, slot_index], axis=0)
        mate_imag = jnp.take(ext_imag, partner[:, slot_index], axis=0)
        pieces.append(looked_sum(own_real * mate_real + own_imag * mate_imag))
        pieces.append(looked_sum(own_imag * mate_real - own_real * mate_imag))
    pair_count = epochs_here * 2 * SLOTS
    stacked = jnp.concatenate(
        [jnp.stack(pieces, axis=1).reshape(pair_count, look_rows, col_count), powers], axis=0
    )
    padded = extended_2(stacked, (("space", 1), ("sub", 2)), RADIUS)
    boxed = window_sum(window_sum(padded, 1), 2)
    pair_boxed = boxed[:pair_count].reshape(epochs_here, 2 * SLOTS, look_rows, col_count)
    power_box = boxed[pair_count:]
    coh_real = pair_boxed[:, 0::2]
    coh_imag = pair_boxed[:, 1::2]
    denominator = power_box[:epochs_here, None] * jnp.take(power_box, partner, axis=0) + EPSILON
    coherence = (coh_real * coh_real + coh_imag * coh_imag) / denominator
    observed = coh_imag / jnp.sqrt(denominator)
    est_ahead = passed_along(estimate, "epoch", -1)
    est_extended = jnp.concatenate([estimate, est_ahead], axis=0)
    fitted = estimate[:, None] - jnp.take(est_extended, partner, axis=0)
    factor = weights[:, :, None, None] * coherence
    weighted = factor * (observed - fitted)
    flattened = weighted.reshape(epochs_here * SLOTS, look_rows * col_count)
    selector = (
        jnp.arange(epochs_here + OFFS, dtype=jnp.int32)[:, None] == partner.reshape(1, -1)
    ).astype(jnp.float32)
    gathered = jnp.dot(
        selector, flattened, precision=lax.Precision.HIGHEST, preferred_element_type=jnp.float32
    ).reshape(epochs_here + OFFS, look_rows, col_count)
    own_part = jnp.sum(weighted, axis=1) - gathered[:epochs_here]
    returned = passed_along(-gathered[epochs_here:], "epoch", 1)
    gradient = jnp.concatenate([own_part + returned, own_part[OFFS:]], axis=0)
    cell_count = float(
        epochs_here
        * lax.axis_size("epoch")
        * look_rows
        * lax.axis_size("space")
        * col_count
        * lax.axis_size("sub")
    )
    local_norm = jnp.sum(gradient * gradient)
    local_crossed = jnp.sum(gradient * direction)
    mean_before = prev_mean[0]
    fields_ahead = passed_along(
        jnp.stack([gradient, direction]).astype(jnp.bfloat16), "epoch", -1
    ).astype(jnp.float32)
    grad_extended = jnp.concatenate([gradient, fields_ahead[0]], axis=0)
    old_extended = jnp.concatenate([direction, fields_ahead[1]], axis=0)
    grad_spread = gradient[:, None] - jnp.take(grad_extended, partner, axis=0)
    old_spread = direction[:, None] - jnp.take(old_extended, partner, axis=0)
    totals = lax.psum(
        (
            local_norm,
            local_crossed,
            jnp.sum(factor * grad_spread * grad_spread),
            jnp.sum(factor * grad_spread * old_spread),
            jnp.sum(factor * old_spread * old_spread),
        ),
        ("epoch", "space", "sub"),
    )
    grad_norm, crossed, grad_term, mixed_term, old_term = totals
    momentum = grad_norm / cell_count / mean_before
    new_direction = gradient + momentum * direction
    curvature = grad_term + 2.0 * momentum * mixed_term + momentum * momentum * old_term
    along_sum = grad_norm + momentum * crossed
    step_size = along_sum / curvature
    return (estimate + step_size * new_direction, new_direction)


LANES = 128
SIDES = 2 * RADIUS
HALO = 16
PARAM_LANE = 96
VMEM = pl.BlockSpec(memory_space=pltpu.VMEM)
SMEM = pl.BlockSpec(memory_space=pltpu.SMEM)
VMEM_BYTES = 48 * 1024 * 1024


def split_two(value):
    high = value.astype(jnp.bfloat16)
    low = (value - high.astype(jnp.float32)).astype(jnp.bfloat16)
    return high, low


def edge_kernel(first, last, edge):
    epochs = first.shape[1]
    lane = lax.broadcasted_iota(jnp.int32, edge.shape, 1)
    total = jnp.zeros(edge.shape, jnp.float32)
    for part in range(2):
        for epoch in range(epochs):
            at = (part * epochs + epoch) * SIDES
            total = placed(lane, total, tile_of(last, part, epoch, 0), LANES - RADIUS, at)
            total = placed(lane, total, tile_of(first, part, epoch, 0), 0, at + RADIUS)
    edge[...] = total.astype(jnp.bfloat16)


def fields_kernel(me, estimate, direction, *fields):
    look_rows = estimate.shape[1]
    tiles = len(fields)
    for shift, out in enumerate(fields):
        tile = lax.rem(me[0] + shift, tiles)
        columns = pl.ds(pl.multiple_of(tile * LANES, LANES), LANES)
        for epoch in range(estimate.shape[0]):
            here = slice(epoch * look_rows, (epoch + 1) * look_rows)
            first, second = split_two(estimate[epoch, :, columns])
            out[0, here, :] = first
            out[1, here, :] = second
            out[2, here, :] = direction[epoch, :, columns].astype(jnp.bfloat16)


def tile_of(slc, part, epoch, tile):
    return slc[part, epoch, :, tile * LANES : (tile + 1) * LANES].astype(jnp.float32)


def placed(lane, total, source, start, target):
    moved = pltpu.roll(source, (target - start) % LANES, axis=1)
    return jnp.where((lane >= target) & (lane < target + RADIUS), moved, total)


def pack_kernel(me, present, slc, params, before, after, *refs):
    messages, strips = refs[:-1], refs[-1]
    tiles = len(messages)
    epochs = slc.shape[1]
    rows = slc.shape[2]
    lane = lax.broadcasted_iota(jnp.int32, (rows, LANES), 1)
    value = params[...]
    high = value.astype(jnp.bfloat16).astype(jnp.float32)
    middle = (value - high).astype(jnp.bfloat16).astype(jnp.float32)
    low = value - high - middle
    third = PARAM_LANE + 2 * SLOTS
    split = jnp.where(lane < third, high, jnp.where(lane < third + SLOTS, middle, low))
    split = jnp.where(lane >= PARAM_LANE, split, 0.0)
    inside = lane < 2 * epochs * SIDES
    for tile in range(tiles):
        total = split
        if tile == 0:
            edge = before[...].astype(jnp.float32) * present[0]
            total = jnp.where(inside & (lane % SIDES < RADIUS), edge, total)
        if tile == tiles - 1:
            edge = after[...].astype(jnp.float32) * present[1]
            total = jnp.where(inside & (lane % SIDES >= RADIUS), edge, total)
        for part in range(2):
            for epoch in range(epochs):
                at = (part * epochs + epoch) * SIDES
                if tile > 0:
                    total = placed(lane, total, tile_of(slc, part, epoch, tile - 1), LANES - RADIUS, at)
                if tile < tiles - 1:
                    total = placed(lane, total, tile_of(slc, part, epoch, tile + 1), 0, at + RADIUS)
        strips[tile] = total.astype(jnp.bfloat16)
    for tile in range(tiles):
        shift = lax.rem(tile - me[0] + tiles, tiles)
        for number, message in enumerate(messages):

            @pl.when(shift == number)
            def _():
                for part in range(2):
                    for epoch in range(epochs):
                        at = (part * epochs + epoch) * rows
                        message[at : at + rows, :] = slc[part, epoch, :, tile * LANES : (tile + 1) * LANES]
                message[2 * epochs * rows :, :] = strips[tile]


def look_order(from_rows, keep):
    looks = from_rows // LOOK
    to = lax.broadcasted_iota(jnp.int32, (from_rows, from_rows), 0)
    at = lax.broadcasted_iota(jnp.int32, (from_rows, from_rows), 1)
    order = (at == to % looks * LOOK + to // looks).astype(jnp.float32)
    return (order * keep(at)).astype(jnp.bfloat16)


def unpack_tiles(order, sources, main, first, columns_of):
    looks = order.shape[0] // LOOK
    for start in range(0, len(sources), 4):
        parts = jnp.concatenate([columns_of(source) for source in sources[start : start + 4]], axis=1)
        value = jnp.dot(order, parts, preferred_element_type=jnp.float32)
        for one in range(4):
            for look in range(LOOK):
                main[first[start + one], look] = value[look * looks : (look + 1) * looks, one * LANES : (one + 1) * LANES]


def unpack_rims(by_look, looks, rim, first):
    share = LANES // SLOTS
    lane = lax.broadcasted_iota(jnp.int32, (looks, LANES), 1)
    for at, place in enumerate(first):
        value = jnp.zeros((looks, LANES), jnp.float32)
        for look in range(LOOK):
            target = look * SIDES
            moved = pltpu.roll(by_look[look * looks : (look + 1) * looks], (target - at * SIDES) % LANES, axis=1)
            value = jnp.where((lane >= target) & (lane < target + SIDES), moved, value)
        spread = share
        while spread < LANES:
            value = value + pltpu.roll(value, spread, axis=1)
            spread = 2 * spread
        rim[place] = value


def band_of(shape, from_of, to_of):
    at = lax.broadcasted_iota(jnp.int32, shape, 0)
    to = lax.broadcasted_iota(jnp.int32, shape, 1)
    return (jnp.abs(from_of(at, to) - to_of(at, to)) <= RADIUS).astype(jnp.float32).astype(jnp.bfloat16)


def column_bands():
    share = LANES // SLOTS

    def rim_from(at, to):
        side = at % share % SIDES
        return jnp.where(side < RADIUS, side - RADIUS, LANES + side - RADIUS)

    def rim_to(at, to):
        column = (to - at % LANES // share * share + LANES) % LANES
        inside = (column < RADIUS) | (column >= LANES - RADIUS)
        inside = inside & (at % share < LOOK * SIDES)
        return jnp.where(inside, column, 4 * LANES)

    band = band_of((2 * LANES, LANES), lambda at, to: at % LANES, lambda at, to: to)
    return band, band_of((2 * LANES, LANES), rim_from, rim_to)


def row_sums(look_rows, looks, look_of):
    group = 2 * SLOTS
    out_at = lax.broadcasted_iota(jnp.int32, (group * look_rows, group * looks), 0)
    in_at = lax.broadcasted_iota(jnp.int32, (group * look_rows, group * looks), 1)
    near = jnp.abs(look_of(in_at % looks) - out_at % look_rows) <= RADIUS
    near = near & (in_at // looks == out_at // look_rows)
    return near.astype(jnp.float32).astype(jnp.bfloat16)


def mixed(values):
    lane = lax.broadcasted_iota(jnp.int32, values[0].shape, 1)
    result = values[-1]
    for slot in range(SLOTS - 1):
        result = jnp.where(lane // (LANES // SLOTS) == slot, values[slot], result)
    return result


def power_batches(blocks, epochs, looks, main, rim, looked, rim_looked):
    total = blocks * epochs
    group = 2 * SLOTS
    for block in range(blocks):
        for piece in range(0, looks, 8):
            rows_at = slice(piece, piece + 8)
            for half in range(2):
                squares = []
                for slot in range(SLOTS):
                    channel = half * SLOTS + slot
                    epoch = block * epochs + channel
                    value = None
                    for look in range(LOOK):
                        real = main[epoch, look, rows_at]
                        imag = main[total + epoch, look, rows_at]
                        one = real * real + imag * imag
                        value = one if value is None else value + one
                    at = (block * group + channel) * looks + piece
                    looked[at : at + 8, :] = value
                    real = rim[epoch, rows_at]
                    imag = rim[total + epoch, rows_at]
                    squares.append(real * real + imag * imag)
                at = (block * 2 + half) * looks + piece
                rim_looked[at : at + 8, :] = mixed(squares)


def pair_batch(batch, epoch, mates, total, looks, main, rim, looked, rim_looked):
    group = 2 * SLOTS
    for piece in range(0, looks, 8):
        rows_at = slice(piece, piece + 8)
        own_re = [main[epoch, look, rows_at] for look in range(LOOK)]
        own_im = [main[total + epoch, look, rows_at] for look in range(LOOK)]
        for slot, mate in enumerate(mates):
            real = None
            for look in range(LOOK):
                mate_re = main[mate, look, rows_at]
                mate_im = main[total + mate, look, rows_at]
                one = own_re[look] * mate_re + own_im[look] * mate_im
                two = own_im[look] * mate_re - own_re[look] * mate_im
                real = one if real is None else real + one
                imag = two if look == 0 else imag + two
            at = pl.multiple_of((batch * group + slot) * looks + piece, 8)
            looked[pl.ds(at, 8), :] = real
            at = pl.multiple_of((batch * group + SLOTS + slot) * looks + piece, 8)
            looked[pl.ds(at, 8), :] = imag
        rim_re = rim[epoch, rows_at]
        rim_im = rim[total + epoch, rows_at]
        mate_re = mixed([rim[mate, rows_at] for mate in mates])
        mate_im = mixed([rim[total + mate, rows_at] for mate in mates])
        at = pl.multiple_of(batch * 2 * looks + piece, 8)
        rim_looked[pl.ds(at, 8), :] = rim_re * mate_re + rim_im * mate_im
        at = pl.multiple_of((batch * 2 + 1) * looks + piece, 8)
        rim_looked[pl.ds(at, 8), :] = rim_im * mate_re - rim_re * mate_im


def columns_summed(couple, looks, bands, looked, rim_looked, wide):
    group = 2 * SLOTS
    f32 = jnp.float32
    at = pl.ds(pl.multiple_of(couple * (2 * group * looks), 2 * group * looks), 2 * group * looks)
    halves = jnp.concatenate(split_two(looked[at, :]), axis=1)
    value = jnp.dot(halves, bands[0], preferred_element_type=f32)
    at = pl.ds(pl.multiple_of(couple * (4 * looks), 4 * looks), 4 * looks)
    halves = jnp.concatenate(split_two(rim_looked[at, :]), axis=1)
    outer = jnp.dot(halves, bands[1], preferred_element_type=f32)
    lane = lax.broadcasted_iota(jnp.int32, (looks, LANES), 1)
    outside = (lane < RADIUS) | (lane >= LANES - RADIUS)
    for channel in range(2 * group):
        batch, half, slot = channel // group, channel % group // SLOTS, channel % SLOTS
        row = (batch * 2 + half) * looks
        part = outer[row : row + looks]
        if slot > 0:
            part = pltpu.roll(part, LANES - slot * (LANES // SLOTS), axis=1)
        row = channel * looks
        to = pl.ds(pl.multiple_of(couple * (2 * group * looks) + row, 8), looks)
        wide[to, :] = value[row : row + looks] + jnp.where(outside, part, 0.0)


def rows_summed(batch, looks, sum_rows, wide):
    rows = 2 * SLOTS * looks
    at = pl.ds(pl.multiple_of(batch * rows, rows), rows)
    halves = jnp.concatenate(split_two(wide[at, :]), axis=1)
    value = jnp.dot(sum_rows, halves, preferred_element_type=jnp.float32)
    return value[:, :LANES] + value[:, LANES:]


def clipped(value, last):
    return jnp.minimum(jnp.maximum(value, 0), last)


def inner_kernel(sizes, partner, *refs):
    tiles, epochs, rows = sizes
    messages = refs[:tiles]
    boxed, main, rim, looked, rim_looked, wide = refs[tiles:]
    total = tiles * epochs
    look_rows = rows // LOOK
    order = look_order(rows, lambda at: 1.0)
    bands = column_bands()
    sum_rows = row_sums(look_rows, look_rows, lambda look: look)
    for block, message in enumerate(messages):
        first = [part * total + block * epochs + epoch for part in range(2) for epoch in range(epochs)]
        unpack_tiles(order, range(2 * epochs), main, first, lambda at: message[at * rows : (at + 1) * rows, :])
        by_look = jnp.dot(order, message[2 * epochs * rows :, :], preferred_element_type=jnp.float32)
        unpack_rims(by_look, look_rows, rim, first)
    power_batches(tiles, epochs, look_rows, main, rim, looked, rim_looked)
    last = (tiles + total) // 2 - 1

    @pl.loop(0, last + 2)
    def _(turn):
        here = clipped(turn, total // 2 - 1)
        for one in range(2):
            epoch = here * 2 + one
            mates = [partner[epoch * SLOTS + slot] for slot in range(SLOTS)]
            pair_batch(tiles + epoch, epoch, mates, total, look_rows, main, rim, looked, rim_looked)
        columns_summed(clipped(turn, last), look_rows, bands, looked, rim_looked, wide)
        here = clipped(turn - 1, last)
        for one in range(2):
            boxed[here * 2 + one] = rows_summed(here * 2 + one, look_rows, sum_rows, wide)


def border_kernel(sizes, partner, weight, present, *refs):
    tiles, epochs, look_rows = sizes
    top, bottom, inner, factors, pulls, boxed, main, rim, looked, rim_looked, wide = refs
    total = tiles * epochs
    looks = 2 * HALO // LOOK
    halo_looks = HALO // LOOK
    tile_rows = (2 * epochs + 1) * HALO
    order = look_order(2 * HALO, lambda at: jnp.where(at < HALO, present[0], present[1]))
    bands = column_bands()
    sum_rows = row_sums(look_rows, looks, lambda at: jnp.where(at < halo_looks, at - halo_looks, at - halo_looks + look_rows))
    for block in range(tiles):

        def border_of(at):
            here = slice(block * tile_rows + at * HALO, block * tile_rows + (at + 1) * HALO)
            return jnp.concatenate([top[here, :], bottom[here, :]], axis=0)

        first = [part * total + block * epochs + epoch for part in range(2) for epoch in range(epochs)]
        unpack_tiles(order, range(2 * epochs), main, first, border_of)
        by_look = jnp.dot(order, border_of(2 * epochs), preferred_element_type=jnp.float32)
        unpack_rims(by_look, looks, rim, first)
    power_batches(tiles, epochs, looks, main, rim, looked, rim_looked)
    last = (tiles + total) // 2 - 1

    def power_of(epoch):
        at = pl.ds(pl.multiple_of(epoch % epochs * look_rows, look_rows), look_rows)
        return boxed[epoch // epochs, at, :]

    @pl.loop(0, last + 3)
    def _(turn):
        here = clipped(turn, total // 2 - 1)
        for one in range(2):
            epoch = here * 2 + one
            mates = [partner[epoch * SLOTS + slot] for slot in range(SLOTS)]
            pair_batch(tiles + epoch, epoch, mates, total, looks, main, rim, looked, rim_looked)
        columns_summed(clipped(turn, last), looks, bands, looked, rim_looked, wide)
        here = clipped(turn - 2 - tiles // 2, total // 2 - 1)
        for one in range(2):
            epoch = here * 2 + one
            batch = tiles + epoch
            own_power = power_of(epoch)
            for slot in range(SLOTS):
                pair = epoch * SLOTS + slot
                inverse = lax.rsqrt(own_power * power_of(partner[pair]) + EPSILON)
                unit_re = boxed[batch, slot * look_rows : (slot + 1) * look_rows, :] * inverse
                unit_im = boxed[batch, (SLOTS + slot) * look_rows : (SLOTS + slot + 1) * look_rows, :] * inverse
                factor = weight[pair] * (unit_re * unit_re + unit_im * unit_im)
                factors[pair] = factor
                pulls[pair] = factor * unit_im
        here = clipped(turn - 1, last)
        for one in range(2):
            batch = here * 2 + one
            boxed[batch] = inner[batch] + rows_summed(batch, looks, sum_rows, wide)


def gradient_kernel(sizes, partner, *refs):
    tiles, epochs = sizes
    fields = refs[:tiles]
    factors, pulls, gradient, sums, est, old = refs[tiles:]
    look_rows = est.shape[1]
    total = tiles * epochs
    f32 = jnp.float32
    for block in range(tiles):

        @pl.loop(0, epochs, unroll=4)
        def _(epoch):
            here = pl.ds(pl.multiple_of(epoch * look_rows, look_rows), look_rows)
            est[block * epochs + epoch] = fields[block][0, here, :].astype(f32) + fields[block][1, here, :].astype(f32)
            old[block * epochs + epoch] = fields[block][2, here, :].astype(f32)
            gradient[block * epochs + epoch] = jnp.zeros((look_rows, LANES), f32)

    @pl.loop(0, total, unroll=2)
    def _(epoch):
        own_est = est[epoch]
        own = jnp.zeros((look_rows, LANES), f32)
        mates = [partner[epoch * SLOTS + slot] for slot in range(SLOTS)]
        values = []
        for slot, mate in enumerate(mates):
            pair = epoch * SLOTS + slot
            weighted = pulls[pair] - factors[pair] * (own_est - est[mate])
            own = own + weighted
            values.append(weighted)
        for mate, weighted in zip(mates, values):
            gradient[mate] = gradient[mate] - weighted
        gradient[epoch] = gradient[epoch] + own

    def totals(epoch, carry):
        norm, crossed, grad_term, mixed_term, old_term = carry
        own_grad = gradient[epoch]
        own_old = old[epoch]
        norm = norm + own_grad * own_grad
        crossed = crossed + own_grad * own_old
        for slot in range(SLOTS):
            mate = partner[epoch * SLOTS + slot]
            factor = factors[epoch * SLOTS + slot]
            grad_spread = own_grad - gradient[mate]
            old_spread = own_old - old[mate]
            pulled = factor * grad_spread
            grad_term = grad_term + pulled * grad_spread
            mixed_term = mixed_term + pulled * old_spread
            old_term = old_term + factor * old_spread * old_spread
        return norm, crossed, grad_term, mixed_term, old_term

    zero = jnp.zeros((look_rows, LANES), f32)
    results = lax.fori_loop(0, total, totals, (zero,) * 5, unroll=2)
    sums[...] = jnp.zeros(sums.shape, f32)
    for at, value in enumerate(results):
        sums[at : at + 1, :] = jnp.sum(value, axis=0, keepdims=True)


def return_kernel(tiles, gradient, *refs):
    pieces = refs[-tiles:]
    shared = refs[:-tiles]
    total = shared[0][...]
    for other in shared[1:]:
        total = total + other[...]
    epochs = gradient.shape[0] // len(pieces)
    look_rows = gradient.shape[1]
    for number, piece in enumerate(pieces):
        for epoch in range(epochs):
            piece[epoch * look_rows : (epoch + 1) * look_rows, :] = gradient[number * epochs + epoch]
        piece[epochs * look_rows :, :] = total


def update_kernel(cell_count, me, prev_mean, estimate, direction, *refs):
    new_estimate, new_direction = refs[-2:]
    pieces = refs[:-2]
    tiles = len(pieces)
    epochs = estimate.shape[0]
    look_rows = estimate.shape[1]
    total = pieces[0][epochs * look_rows :, :]
    for piece in pieces[1:]:
        total = total + piece[epochs * look_rows :, :]
    total = jnp.sum(total, axis=1, keepdims=True)
    grad_norm, crossed, grad_term, mixed, old_term = (total[at : at + 1, :] for at in range(5))
    momentum = grad_norm / cell_count / prev_mean[0]
    curvature = grad_term + 2.0 * momentum * mixed + momentum * momentum * old_term
    step = (grad_norm + momentum * crossed) / curvature
    momentum = jnp.broadcast_to(momentum, (look_rows, LANES))
    step = jnp.broadcast_to(step, (look_rows, LANES))
    for shift, piece in enumerate(pieces):
        tile = lax.rem(me[0] - shift + tiles, tiles)
        columns = pl.ds(pl.multiple_of(tile * LANES, LANES), LANES)
        for epoch in range(epochs):
            gradient = piece[epoch * look_rows : (epoch + 1) * look_rows, :]
            moved = gradient + momentum * direction[epoch, :, columns]
            new_direction[epoch, :, columns] = moved
            new_estimate[epoch, :, columns] = estimate[epoch, :, columns] + step * moved


def swapped(up, down, axis):
    size = lax.axis_size(axis)
    if size == 1:
        return jnp.zeros_like(up), jnp.zeros_like(down)
    if size == 2:
        first = lax.axis_index(axis) == 0
        got = lax.ppermute(jnp.where(first, up, down), axis, [(0, 1), (1, 0)])
        return got, got
    forward = [(i, i + 1) for i in range(size - 1)]
    backward = [(target, source) for source, target in forward]
    return lax.ppermute(up, axis, forward), lax.ppermute(down, axis, backward)


def to_ahead(x, axis, by):
    size = lax.axis_size(axis)
    return lax.ppermute(x, axis, [(i, (i + by) % size) for i in range(size)])


def transposed_plan(slc, offsets, weights, estimate, direction, prev_mean):
    f32 = jnp.float32
    bf16 = jnp.bfloat16
    tiles = lax.axis_size("epoch")
    me = lax.axis_index("epoch")
    epochs, rows, columns = slc.shape[1:]
    look_rows = rows // LOOK
    total = tiles * epochs
    tile_rows = 2 * epochs * rows
    params_of = pltpu.CompilerParams(vmem_limit_bytes=VMEM_BYTES)

    def fetched(messages, shift):
        return to_ahead(messages[tiles - shift], "epoch", tiles - shift)

    sub = lax.axis_index("sub")
    outer_tile = (2, epochs, rows, LANES)
    edge = pl.pallas_call(
        edge_kernel,
        out_shape=jax.ShapeDtypeStruct((rows, LANES), bf16),
        grid=(1,),
        in_specs=[
            pl.BlockSpec(outer_tile, lambda _: (0, 0, 0, 0)),
            pl.BlockSpec(outer_tile, lambda _: (0, 0, 0, tiles - 1)),
        ],
        out_specs=pl.BlockSpec((rows, LANES), lambda _: (0, 0)),
        compiler_params=params_of,
        cost_estimate=pl.CostEstimate(flops=1_000_000, bytes_accessed=1_000_000, transcendentals=0),
    )(slc, slc)
    before, after = swapped(edge, edge, "sub")
    params = jnp.zeros((rows, LANES), f32)
    listed = jnp.concatenate([offsets.astype(f32), weights, weights, weights], axis=1)
    params = lax.dynamic_update_slice(params, listed, (0, PARAM_LANE))
    sub_present = jnp.stack([sub > 0, sub < lax.axis_size("sub") - 1]).astype(f32)
    messages = pl.pallas_call(
        pack_kernel,
        out_shape=(jax.ShapeDtypeStruct((tile_rows + rows, LANES), bf16),) * tiles,
        in_specs=[SMEM] * 2 + [VMEM] * 4,
        out_specs=(VMEM,) * tiles,
        scratch_shapes=[pltpu.VMEM((tiles, rows, LANES), bf16)],
        compiler_params=params_of,
        cost_estimate=pl.CostEstimate(flops=3_000_000, bytes_accessed=4_000_000, transcendentals=0),
    )(me.reshape(1), sub_present, slc, params, before, after)
    block = [messages[0]] + [fetched(messages, shift) for shift in range(1, tiles)]

    estimate, direction, _ = lax.optimization_barrier((estimate, direction, messages))
    fields = pl.pallas_call(
        fields_kernel,
        out_shape=(jax.ShapeDtypeStruct((3, epochs * look_rows, LANES), bf16),) * tiles,
        in_specs=[SMEM] + [VMEM] * 2,
        out_specs=(VMEM,) * tiles,
        compiler_params=params_of,
        cost_estimate=pl.CostEstimate(flops=1_000_000, bytes_accessed=2_000_000, transcendentals=0),
    )(me.reshape(1), estimate, direction)
    late = lax.optimization_barrier((fields, block))[0]
    field = [fields[0]] + [fetched(late, shift) for shift in range(1, tiles)]

    space = lax.axis_index("space")
    spaces = lax.axis_size("space")
    present = jnp.stack([space > 0, space < spaces - 1]).astype(f32)

    def halo(pieces):
        def border(from_row):
            cuts = [lax.dynamic_slice_in_dim(piece, from_row, HALO, axis=1).reshape(-1, LANES) for piece in pieces]
            return jnp.concatenate(cuts, axis=0)

        if spaces == 2:
            got = lax.ppermute(border(jnp.where(space == 0, rows - HALO, 0)), "space", [(0, 1), (1, 0)])
            return got, got
        return swapped(border(rows - HALO), border(0), "space")

    def by_rows(shift):
        return block[shift].reshape(-1, rows, LANES)

    def params_in(shift):
        return block[shift][tile_rows : tile_rows + epochs, PARAM_LANE : PARAM_LANE + 4 * SLOTS].astype(f32)

    def pairs_of(blocks, loaded):
        listed = jnp.concatenate([params_in(block) for block in blocks], axis=0)
        mate = jnp.arange(len(blocks) * epochs, dtype=jnp.int32)[:, None] + listed[:, :SLOTS].astype(jnp.int32)
        weight = listed[:, SLOTS : 2 * SLOTS] + listed[:, 2 * SLOTS : 3 * SLOTS] + listed[:, 3 * SLOTS :]
        return mate.reshape(-1), weight.reshape(-1)

    top, bottom = halo([by_rows(shift) for shift in range(tiles)])
    listed = jnp.concatenate([params_in(shift) for shift in range(tiles)], axis=0)
    partner = jnp.arange(total, dtype=jnp.int32)[:, None] + listed[:, :SLOTS].astype(jnp.int32)
    partner = lax.rem(partner, total).reshape(-1)
    weight = listed[:, SLOTS : 2 * SLOTS] + listed[:, 2 * SLOTS : 3 * SLOTS] + listed[:, 3 * SLOTS :]
    weight = weight.reshape(-1)

    group = 2 * SLOTS
    batches = tiles + total

    def scratch(looks):
        return [
            pltpu.VMEM((2 * total, LOOK, looks, LANES), f32),
            pltpu.VMEM((2 * total, looks, LANES), f32),
            pltpu.VMEM((batches * group * looks, LANES), f32),
            pltpu.VMEM((batches * 2 * looks, LANES), f32),
            pltpu.VMEM((batches * group * looks, LANES), f32),
        ]

    boxed_shape = (batches, group * look_rows, LANES)
    inner = pl.pallas_call(
        functools.partial(inner_kernel, (tiles, epochs, rows)),
        out_shape=jax.ShapeDtypeStruct(boxed_shape, f32),
        in_specs=[SMEM] + [VMEM] * tiles,
        out_specs=VMEM,
        scratch_shapes=scratch(look_rows),
        compiler_params=params_of,
        cost_estimate=pl.CostEstimate(flops=20_000_000, bytes_accessed=20_000_000, transcendentals=0),
    )(partner, *block)
    pair_shape = jax.ShapeDtypeStruct((total * SLOTS, look_rows, LANES), f32)
    factors, pulls = pl.pallas_call(
        functools.partial(border_kernel, (tiles, epochs, look_rows)),
        out_shape=(pair_shape, pair_shape),
        in_specs=[SMEM] * 3 + [VMEM] * 3,
        out_specs=(VMEM, VMEM),
        scratch_shapes=[pltpu.VMEM(boxed_shape, f32)] + scratch(2 * HALO // LOOK),
        compiler_params=params_of,
        cost_estimate=pl.CostEstimate(flops=20_000_000, bytes_accessed=15_000_000, transcendentals=0),
    )(partner, weight, present, top, bottom, inner)
    gradient, sums = pl.pallas_call(
        functools.partial(gradient_kernel, (tiles, epochs)),
        out_shape=(
            jax.ShapeDtypeStruct((total, look_rows, LANES), f32),
            jax.ShapeDtypeStruct((8, LANES), f32),
        ),
        in_specs=[SMEM] + [VMEM] * (tiles + 2),
        out_specs=(VMEM, VMEM),
        scratch_shapes=[pltpu.VMEM((total, look_rows, LANES), f32)] * 2,
        compiler_params=params_of,
        cost_estimate=pl.CostEstimate(flops=10_000_000, bytes_accessed=8_000_000, transcendentals=0),
    )(partner, *field, factors, pulls)

    place = ("space", "sub")
    count = spaces * lax.axis_size("sub")
    shared = [sums] + [lax.ppermute(sums, place, [(i, (i + by) % count) for i in range(count)]) for by in range(1, count)]
    pieces = pl.pallas_call(
        functools.partial(return_kernel, tiles),
        out_shape=(jax.ShapeDtypeStruct((epochs * look_rows + 8, LANES), f32),) * tiles,
        in_specs=[VMEM] * (1 + count),
        out_specs=(VMEM,) * tiles,
        compiler_params=params_of,
        cost_estimate=pl.CostEstimate(flops=10_000, bytes_accessed=1_000_000, transcendentals=0),
    )(gradient, *shared)
    returned = [pieces[0]] + [to_ahead(pieces[by], "epoch", by) for by in range(1, tiles)]
    cell_count = float(total * look_rows * spaces * columns * lax.axis_size("sub"))
    return pl.pallas_call(
        functools.partial(update_kernel, cell_count),
        out_shape=(jax.ShapeDtypeStruct(estimate.shape, f32),) * 2,
        in_specs=[SMEM] * 2 + [VMEM] * (2 + tiles),
        out_specs=(VMEM, VMEM),
        compiler_params=params_of,
        cost_estimate=pl.CostEstimate(flops=1_000_000, bytes_accessed=2_000_000, transcendentals=0),
    )(me.reshape(1), prev_mean, estimate, direction, *returned)


def on_device(slc, offsets, weights, estimate, direction, prev_mean):
    epochs, rows, columns = slc.shape[1:]
    fits = columns == LANES * lax.axis_size("epoch") and lax.axis_size("epoch") % 2 == 0
    fits = fits and 2 * epochs * SIDES <= PARAM_LANE and rows % HALO == 0 and epochs == 2 * SLOTS
    plan = transposed_plan if fits else ring_plan
    return plan(slc, offsets, weights, estimate, direction, prev_mean)


def solution(mesh):
    return jax.shard_map(
        on_device,
        mesh=mesh,
        in_specs=(
            P(None, ("groups", "epoch"), "space", "sub"),
            P(("groups", "epoch"), None),
            P(("groups", "epoch"), None),
            P(("groups", "epoch"), "space", "sub"),
            P(("groups", "epoch"), "space", "sub"),
            P(),
        ),
        out_specs=(P(("groups", "epoch"), "space", "sub"), P(("groups", "epoch"), "space", "sub")),
        check_vma=False,
    )
```

```python
import functools

import jax
import jax.numpy as jnp
from jax import lax
from jax.experimental import pallas as pl
from jax.experimental.pallas import tpu as pltpu
from jax.sharding import PartitionSpec as P

SLOTS = 4
OFFS = 8
LOOK = 4
RADIUS = 3


EPSILON = 1e-06


def passed_along(x, axis, by):
    size = lax.axis_size(axis)
    return lax.ppermute(x, axis, [(i, (i + by) % size) for i in range(size)])


def extended_2(block, sides, width):
    for axis, dim in sides:
        count = lax.axis_size(axis)
        forward = [(i, i + 1) for i in range(count - 1)]
        backward = [(target, source) for source, target in forward]
        low = lax.ppermute(
            lax.slice_in_dim(block, block.shape[dim] - width, None, axis=dim), axis, forward
        )
        high = lax.ppermute(lax.slice_in_dim(block, 0, width, axis=dim), axis, backward)
        block = jnp.concatenate([low, block, high], axis=dim)
    return block


def looked_sum(field):
    shape = field.shape
    return jnp.sum(field.reshape(shape[:-2] + (shape[-2] // LOOK, LOOK, shape[-1])), axis=-2)


def window_sum(padded, axis):
    length = padded.shape[axis] - 2 * RADIUS
    total = lax.slice_in_dim(padded, 0, length, axis=axis)
    for shift_at in range(1, 2 * RADIUS + 1):
        total = total + lax.slice_in_dim(padded, shift_at, shift_at + length, axis=axis)
    return total


def ring_plan(slc, offsets, weights, estimate, direction, prev_mean):
    epochs_here = slc.shape[1]
    look_rows = slc.shape[2] // LOOK
    col_count = slc.shape[3]
    ahead = passed_along(slc, "epoch", -1)
    extended = jnp.concatenate([slc, ahead], axis=1)
    numbers = jnp.arange(epochs_here, dtype=jnp.int32)
    partner = numbers[:, None] + offsets
    own_real = slc[0].astype(jnp.float32)
    own_imag = slc[1].astype(jnp.float32)
    ext_real = extended[0].astype(jnp.float32)
    ext_imag = extended[1].astype(jnp.float32)
    powers = looked_sum(ext_real * ext_real + ext_imag * ext_imag)
    pieces = []
    for slot_index in range(SLOTS):
        mate_real = jnp.take(ext_real, partner[:, slot_index], axis=0)
        mate_imag = jnp.take(ext_imag, partner[:, slot_index], axis=0)
        pieces.append(looked_sum(own_real * mate_real + own_imag * mate_imag))
        pieces.append(looked_sum(own_imag * mate_real - own_real * mate_imag))
    pair_count = epochs_here * 2 * SLOTS
    stacked = jnp.concatenate(
        [jnp.stack(pieces, axis=1).reshape(pair_count, look_rows, col_count), powers], axis=0
    )
    padded = extended_2(stacked, (("space", 1), ("sub", 2)), RADIUS)
    boxed = window_sum(window_sum(padded, 1), 2)
    pair_boxed = boxed[:pair_count].reshape(epochs_here, 2 * SLOTS, look_rows, col_count)
    power_box = boxed[pair_count:]
    coh_real = pair_boxed[:, 0::2]
    coh_imag = pair_boxed[:, 1::2]
    denominator = power_box[:epochs_here, None] * jnp.take(power_box, partner, axis=0) + EPSILON
    coherence = (coh_real * coh_real + coh_imag * coh_imag) / denominator
    observed = coh_imag / jnp.sqrt(denominator)
    est_ahead = passed_along(estimate, "epoch", -1)
    est_extended = jnp.concatenate([estimate, est_ahead], axis=0)
    fitted = estimate[:, None] - jnp.take(est_extended, partner, axis=0)
    factor = weights[:, :, None, None] * coherence
    weighted = factor * (observed - fitted)
    flattened = weighted.reshape(epochs_here * SLOTS, look_rows * col_count)
    selector = (
        jnp.arange(epochs_here + OFFS, dtype=jnp.int32)[:, None] == partner.reshape(1, -1)
    ).astype(jnp.float32)
    gathered = jnp.dot(
        selector, flattened, precision=lax.Precision.HIGHEST, preferred_element_type=jnp.float32
    ).reshape(epochs_here + OFFS, look_rows, col_count)
    own_part = jnp.sum(weighted, axis=1) - gathered[:epochs_here]
    returned = passed_along(-gathered[epochs_here:], "epoch", 1)
    gradient = jnp.concatenate([own_part + returned, own_part[OFFS:]], axis=0)
    cell_count = float(
        epochs_here
        * lax.axis_size("epoch")
        * look_rows
        * lax.axis_size("space")
        * col_count
        * lax.axis_size("sub")
    )
    local_norm = jnp.sum(gradient * gradient)
    local_crossed = jnp.sum(gradient * direction)
    mean_before = prev_mean[0]
    fields_ahead = passed_along(
        jnp.stack([gradient, direction]).astype(jnp.bfloat16), "epoch", -1
    ).astype(jnp.float32)
    grad_extended = jnp.concatenate([gradient, fields_ahead[0]], axis=0)
    old_extended = jnp.concatenate([direction, fields_ahead[1]], axis=0)
    grad_spread = gradient[:, None] - jnp.take(grad_extended, partner, axis=0)
    old_spread = direction[:, None] - jnp.take(old_extended, partner, axis=0)
    totals = lax.psum(
        (
            local_norm,
            local_crossed,
            jnp.sum(factor * grad_spread * grad_spread),
            jnp.sum(factor * grad_spread * old_spread),
            jnp.sum(factor * old_spread * old_spread),
        ),
        ("epoch", "space", "sub"),
    )
    grad_norm, crossed, grad_term, mixed_term, old_term = totals
    momentum = grad_norm / cell_count / mean_before
    new_direction = gradient + momentum * direction
    curvature = grad_term + 2.0 * momentum * mixed_term + momentum * momentum * old_term
    along_sum = grad_norm + momentum * crossed
    step_size = along_sum / curvature
    return (estimate + step_size * new_direction, new_direction)


LANES = 128
SIDES = 2 * RADIUS
HALO = 16
PARAM_LANE = 96
VMEM = pl.BlockSpec(memory_space=pltpu.VMEM)
SMEM = pl.BlockSpec(memory_space=pltpu.SMEM)
VMEM_BYTES = 48 * 1024 * 1024


def split_two(value):
    high = value.astype(jnp.bfloat16)
    low = (value - high.astype(jnp.float32)).astype(jnp.bfloat16)
    return high, low


def edge_kernel(first, last, edge):
    epochs = first.shape[1]
    lane = lax.broadcasted_iota(jnp.int32, edge.shape, 1)
    total = jnp.zeros(edge.shape, jnp.float32)
    for part in range(2):
        for epoch in range(epochs):
            at = (part * epochs + epoch) * SIDES
            total = placed(lane, total, tile_of(last, part, epoch, 0), LANES - RADIUS, at)
            total = placed(lane, total, tile_of(first, part, epoch, 0), 0, at + RADIUS)
    edge[...] = total.astype(jnp.bfloat16)


def fields_kernel(me, estimate, direction, *fields):
    look_rows = estimate.shape[1]
    tiles = len(fields)
    for shift, out in enumerate(fields):
        tile = lax.rem(me[0] + shift, tiles)
        columns = pl.ds(pl.multiple_of(tile * LANES, LANES), LANES)
        for epoch in range(estimate.shape[0]):
            here = slice(epoch * look_rows, (epoch + 1) * look_rows)
            first, second = split_two(estimate[epoch, :, columns])
            out[0, here, :] = first
            out[1, here, :] = second
            out[2, here, :] = direction[epoch, :, columns].astype(jnp.bfloat16)


def tile_of(slc, part, epoch, tile):
    return slc[part, epoch, :, tile * LANES : (tile + 1) * LANES].astype(jnp.float32)


def placed(lane, total, source, start, target):
    moved = pltpu.roll(source, (target - start) % LANES, axis=1)
    return jnp.where((lane >= target) & (lane < target + RADIUS), moved, total)


def pack_kernel(me, present, slc, params, before, after, *refs):
    messages, strips = refs[:-1], refs[-1]
    tiles = len(messages)
    epochs = slc.shape[1]
    rows = slc.shape[2]
    lane = lax.broadcasted_iota(jnp.int32, (rows, LANES), 1)
    value = params[...]
    high = value.astype(jnp.bfloat16).astype(jnp.float32)
    middle = (value - high).astype(jnp.bfloat16).astype(jnp.float32)
    low = value - high - middle
    third = PARAM_LANE + 2 * SLOTS
    split = jnp.where(lane < third, high, jnp.where(lane < third + SLOTS, middle, low))
    split = jnp.where(lane >= PARAM_LANE, split, 0.0)
    inside = lane < 2 * epochs * SIDES
    for tile in range(tiles):
        total = split
        if tile == 0:
            edge = before[...].astype(jnp.float32) * present[0]
            total = jnp.where(inside & (lane % SIDES < RADIUS), edge, total)
        if tile == tiles - 1:
            edge = after[...].astype(jnp.float32) * present[1]
            total = jnp.where(inside & (lane % SIDES >= RADIUS), edge, total)
        for part in range(2):
            for epoch in range(epochs):
                at = (part * epochs + epoch) * SIDES
                if tile > 0:
                    total = placed(lane, total, tile_of(slc, part, epoch, tile - 1), LANES - RADIUS, at)
                if tile < tiles - 1:
                    total = placed(lane, total, tile_of(slc, part, epoch, tile + 1), 0, at + RADIUS)
        strips[tile] = total.astype(jnp.bfloat16)
    for tile in range(tiles):
        shift = lax.rem(tile - me[0] + tiles, tiles)
        for number, message in enumerate(messages):

            @pl.when(shift == number)
            def _():
                for part in range(2):
                    for epoch in range(epochs):
                        at = (part * epochs + epoch) * rows
                        message[at : at + rows, :] = slc[part, epoch, :, tile * LANES : (tile + 1) * LANES]
                message[2 * epochs * rows :, :] = strips[tile]


def look_order(from_rows, keep):
    looks = from_rows // LOOK
    to = lax.broadcasted_iota(jnp.int32, (from_rows, from_rows), 0)
    at = lax.broadcasted_iota(jnp.int32, (from_rows, from_rows), 1)
    order = (at == to % looks * LOOK + to // looks).astype(jnp.float32)
    return (order * keep(at)).astype(jnp.bfloat16)


def unpack_tiles(order, sources, main, first, columns_of):
    looks = order.shape[0] // LOOK
    for start in range(0, len(sources), 4):
        parts = jnp.concatenate([columns_of(source) for source in sources[start : start + 4]], axis=1)
        value = jnp.dot(order, parts, preferred_element_type=jnp.float32)
        for one in range(4):
            for look in range(LOOK):
                main[first[start + one], look] = value[look * looks : (look + 1) * looks, one * LANES : (one + 1) * LANES]


def unpack_rims(by_look, looks, rim, first):
    share = LANES // SLOTS
    lane = lax.broadcasted_iota(jnp.int32, (looks, LANES), 1)
    for at, place in enumerate(first):
        value = jnp.zeros((looks, LANES), jnp.float32)
        for look in range(LOOK):
            target = look * SIDES
            moved = pltpu.roll(by_look[look * looks : (look + 1) * looks], (target - at * SIDES) % LANES, axis=1)
            value = jnp.where((lane >= target) & (lane < target + SIDES), moved, value)
        spread = share
        while spread < LANES:
            value = value + pltpu.roll(value, spread, axis=1)
            spread = 2 * spread
        rim[place] = value


def band_of(shape, from_of, to_of):
    at = lax.broadcasted_iota(jnp.int32, shape, 0)
    to = lax.broadcasted_iota(jnp.int32, shape, 1)
    return (jnp.abs(from_of(at, to) - to_of(at, to)) <= RADIUS).astype(jnp.float32).astype(jnp.bfloat16)


def column_bands():
    share = LANES // SLOTS

    def rim_from(at, to):
        side = at % share % SIDES
        return jnp.where(side < RADIUS, side - RADIUS, LANES + side - RADIUS)

    def rim_to(at, to):
        column = (to - at % LANES // share * share + LANES) % LANES
        inside = (column < RADIUS) | (column >= LANES - RADIUS)
        inside = inside & (at % share < LOOK * SIDES)
        return jnp.where(inside, column, 4 * LANES)

    band = band_of((2 * LANES, LANES), lambda at, to: at % LANES, lambda at, to: to)
    return band, band_of((2 * LANES, LANES), rim_from, rim_to)


def row_sums(look_rows, looks, look_of):
    group = 2 * SLOTS
    out_at = lax.broadcasted_iota(jnp.int32, (group * look_rows, group * looks), 0)
    in_at = lax.broadcasted_iota(jnp.int32, (group * look_rows, group * looks), 1)
    near = jnp.abs(look_of(in_at % looks) - out_at % look_rows) <= RADIUS
    near = near & (in_at // looks == out_at // look_rows)
    return near.astype(jnp.float32).astype(jnp.bfloat16)


def mixed(values):
    lane = lax.broadcasted_iota(jnp.int32, values[0].shape, 1)
    result = values[-1]
    for slot in range(SLOTS - 1):
        result = jnp.where(lane // (LANES // SLOTS) == slot, values[slot], result)
    return result


def power_batches(blocks, epochs, looks, main, rim, looked, rim_looked):
    total = blocks * epochs
    group = 2 * SLOTS
    for block in range(blocks):
        for piece in range(0, looks, 8):
            rows_at = slice(piece, piece + 8)
            for half in range(2):
                squares = []
                for slot in range(SLOTS):
                    channel = half * SLOTS + slot
                    epoch = block * epochs + channel
                    value = None
                    for look in range(LOOK):
                        real = main[epoch, look, rows_at]
                        imag = main[total + epoch, look, rows_at]
                        one = real * real + imag * imag
                        value = one if value is None else value + one
                    at = (block * group + channel) * looks + piece
                    looked[at : at + 8, :] = value
                    real = rim[epoch, rows_at]
                    imag = rim[total + epoch, rows_at]
                    squares.append(real * real + imag * imag)
                at = (block * 2 + half) * looks + piece
                rim_looked[at : at + 8, :] = mixed(squares)


def pair_batch(batch, epoch, mates, total, looks, main, rim, looked, rim_looked):
    group = 2 * SLOTS
    for piece in range(0, looks, 8):
        rows_at = slice(piece, piece + 8)
        own_re = [main[epoch, look, rows_at] for look in range(LOOK)]
        own_im = [main[total + epoch, look, rows_at] for look in range(LOOK)]
        for slot, mate in enumerate(mates):
            real = None
            for look in range(LOOK):
                mate_re = main[mate, look, rows_at]
                mate_im = main[total + mate, look, rows_at]
                one = own_re[look] * mate_re + own_im[look] * mate_im
                two = own_im[look] * mate_re - own_re[look] * mate_im
                real = one if real is None else real + one
                imag = two if look == 0 else imag + two
            at = pl.multiple_of((batch * group + slot) * looks + piece, 8)
            looked[pl.ds(at, 8), :] = real
            at = pl.multiple_of((batch * group + SLOTS + slot) * looks + piece, 8)
            looked[pl.ds(at, 8), :] = imag
        rim_re = rim[epoch, rows_at]
        rim_im = rim[total + epoch, rows_at]
        mate_re = mixed([rim[mate, rows_at] for mate in mates])
        mate_im = mixed([rim[total + mate, rows_at] for mate in mates])
        at = pl.multiple_of(batch * 2 * looks + piece, 8)
        rim_looked[pl.ds(at, 8), :] = rim_re * mate_re + rim_im * mate_im
        at = pl.multiple_of((batch * 2 + 1) * looks + piece, 8)
        rim_looked[pl.ds(at, 8), :] = rim_im * mate_re - rim_re * mate_im


def columns_summed(couple, looks, bands, looked, rim_looked, wide):
    group = 2 * SLOTS
    f32 = jnp.float32
    at = pl.ds(pl.multiple_of(couple * (2 * group * looks), 2 * group * looks), 2 * group * looks)
    halves = jnp.concatenate(split_two(looked[at, :]), axis=1)
    value = jnp.dot(halves, bands[0], preferred_element_type=f32)
    at = pl.ds(pl.multiple_of(couple * (4 * looks), 4 * looks), 4 * looks)
    halves = jnp.concatenate(split_two(rim_looked[at, :]), axis=1)
    outer = jnp.dot(halves, bands[1], preferred_element_type=f32)
    lane = lax.broadcasted_iota(jnp.int32, (looks, LANES), 1)
    outside = (lane < RADIUS) | (lane >= LANES - RADIUS)
    for channel in range(2 * group):
        batch, half, slot = channel // group, channel % group // SLOTS, channel % SLOTS
        row = (batch * 2 + half) * looks
        part = outer[row : row + looks]
        if slot > 0:
            part = pltpu.roll(part, LANES - slot * (LANES // SLOTS), axis=1)
        row = channel * looks
        to = pl.ds(pl.multiple_of(couple * (2 * group * looks) + row, 8), looks)
        wide[to, :] = value[row : row + looks] + jnp.where(outside, part, 0.0)


def rows_summed(batch, looks, sum_rows, wide):
    rows = 2 * SLOTS * looks
    at = pl.ds(pl.multiple_of(batch * rows, rows), rows)
    halves = jnp.concatenate(split_two(wide[at, :]), axis=1)
    value = jnp.dot(sum_rows, halves, preferred_element_type=jnp.float32)
    return value[:, :LANES] + value[:, LANES:]


def clipped(value, last):
    return jnp.minimum(jnp.maximum(value, 0), last)


def inner_kernel(sizes, partner, *refs):
    tiles, epochs, rows = sizes
    messages = refs[:tiles]
    boxed, main, rim, looked, rim_looked, wide = refs[tiles:]
    total = tiles * epochs
    look_rows = rows // LOOK
    order = look_order(rows, lambda at: 1.0)
    bands = column_bands()
    sum_rows = row_sums(look_rows, look_rows, lambda look: look)
    for block, message in enumerate(messages):
        first = [part * total + block * epochs + epoch for part in range(2) for epoch in range(epochs)]
        unpack_tiles(order, range(2 * epochs), main, first, lambda at: message[at * rows : (at + 1) * rows, :])
        by_look = jnp.dot(order, message[2 * epochs * rows :, :], preferred_element_type=jnp.float32)
        unpack_rims(by_look, look_rows, rim, first)
    power_batches(tiles, epochs, look_rows, main, rim, looked, rim_looked)
    last = (tiles + total) // 2 - 1

    @pl.loop(0, last + 2)
    def _(turn):
        here = clipped(turn - 1, last)
        for one in range(2):
            boxed[here * 2 + one] = rows_summed(here * 2 + one, look_rows, sum_rows, wide)
        columns_summed(clipped(turn, last), look_rows, bands, looked, rim_looked, wide)
        here = clipped(turn, total // 2 - 1)
        for one in range(2):
            epoch = here * 2 + one
            mates = [partner[epoch * SLOTS + slot] for slot in range(SLOTS)]
            pair_batch(tiles + epoch, epoch, mates, total, look_rows, main, rim, looked, rim_looked)


def border_kernel(sizes, partner, weight, present, *refs):
    tiles, epochs, look_rows = sizes
    top, bottom, inner, factors, pulls, boxed, main, rim, looked, rim_looked, wide = refs
    total = tiles * epochs
    looks = 2 * HALO // LOOK
    halo_looks = HALO // LOOK
    tile_rows = (2 * epochs + 1) * HALO
    order = look_order(2 * HALO, lambda at: jnp.where(at < HALO, present[0], present[1]))
    bands = column_bands()
    sum_rows = row_sums(look_rows, looks, lambda at: jnp.where(at < halo_looks, at - halo_looks, at - halo_looks + look_rows))
    for block in range(tiles):

        def border_of(at):
            here = slice(block * tile_rows + at * HALO, block * tile_rows + (at + 1) * HALO)
            return jnp.concatenate([top[here, :], bottom[here, :]], axis=0)

        first = [part * total + block * epochs + epoch for part in range(2) for epoch in range(epochs)]
        unpack_tiles(order, range(2 * epochs), main, first, border_of)
        by_look = jnp.dot(order, border_of(2 * epochs), preferred_element_type=jnp.float32)
        unpack_rims(by_look, looks, rim, first)
    power_batches(tiles, epochs, looks, main, rim, looked, rim_looked)
    last = (tiles + total) // 2 - 1

    def power_of(epoch):
        at = pl.ds(pl.multiple_of(epoch % epochs * look_rows, look_rows), look_rows)
        return boxed[epoch // epochs, at, :]

    @pl.loop(0, last + 3)
    def _(turn):
        here = clipped(turn - 2 - tiles // 2, total // 2 - 1)
        for one in range(2):
            epoch = here * 2 + one
            batch = tiles + epoch
            own_power = power_of(epoch)
            for slot in range(SLOTS):
                pair = epoch * SLOTS + slot
                inverse = lax.rsqrt(own_power * power_of(partner[pair]) + EPSILON)
                unit_re = boxed[batch, slot * look_rows : (slot + 1) * look_rows, :] * inverse
                unit_im = boxed[batch, (SLOTS + slot) * look_rows : (SLOTS + slot + 1) * look_rows, :] * inverse
                factor = weight[pair] * (unit_re * unit_re + unit_im * unit_im)
                factors[pair] = factor
                pulls[pair] = factor * unit_im
        here = clipped(turn - 1, last)
        values = [inner[here * 2 + one] + rows_summed(here * 2 + one, looks, sum_rows, wide) for one in range(2)]
        for one in range(2):
            boxed[here * 2 + one] = values[one]
        columns_summed(clipped(turn, last), looks, bands, looked, rim_looked, wide)
        here = clipped(turn, total // 2 - 1)
        for one in range(2):
            epoch = here * 2 + one
            mates = [partner[epoch * SLOTS + slot] for slot in range(SLOTS)]
            pair_batch(tiles + epoch, epoch, mates, total, looks, main, rim, looked, rim_looked)


def gradient_kernel(sizes, partner, *refs):
    tiles, epochs = sizes
    fields = refs[:tiles]
    factors, pulls, gradient, sums, est, old = refs[tiles:]
    look_rows = est.shape[1]
    total = tiles * epochs
    f32 = jnp.float32
    for block in range(tiles):

        @pl.loop(0, epochs, unroll=4)
        def _(epoch):
            here = pl.ds(pl.multiple_of(epoch * look_rows, look_rows), look_rows)
            est[block * epochs + epoch] = fields[block][0, here, :].astype(f32) + fields[block][1, here, :].astype(f32)
            old[block * epochs + epoch] = fields[block][2, here, :].astype(f32)
            gradient[block * epochs + epoch] = jnp.zeros((look_rows, LANES), f32)

    @pl.loop(0, total, unroll=2)
    def _(epoch):
        own_est = est[epoch]
        own = jnp.zeros((look_rows, LANES), f32)
        mates = [partner[epoch * SLOTS + slot] for slot in range(SLOTS)]
        values = []
        for slot, mate in enumerate(mates):
            pair = epoch * SLOTS + slot
            weighted = pulls[pair] - factors[pair] * (own_est - est[mate])
            own = own + weighted
            values.append(weighted)
        for mate, weighted in zip(mates, values):
            gradient[mate] = gradient[mate] - weighted
        gradient[epoch] = gradient[epoch] + own

    def totals(epoch, carry):
        norm, crossed, grad_term, mixed_term, old_term = carry
        own_grad = gradient[epoch]
        own_old = old[epoch]
        norm = norm + own_grad * own_grad
        crossed = crossed + own_grad * own_old
        for slot in range(SLOTS):
            mate = partner[epoch * SLOTS + slot]
            factor = factors[epoch * SLOTS + slot]
            grad_spread = own_grad - gradient[mate]
            old_spread = own_old - old[mate]
            pulled = factor * grad_spread
            grad_term = grad_term + pulled * grad_spread
            mixed_term = mixed_term + pulled * old_spread
            old_term = old_term + factor * old_spread * old_spread
        return norm, crossed, grad_term, mixed_term, old_term

    zero = jnp.zeros((look_rows, LANES), f32)
    results = lax.fori_loop(0, total, totals, (zero,) * 5, unroll=2)
    sums[...] = jnp.zeros(sums.shape, f32)
    for at, value in enumerate(results):
        sums[at : at + 1, :] = jnp.sum(value, axis=0, keepdims=True)


def return_kernel(tiles, gradient, *refs):
    pieces = refs[-tiles:]
    shared = refs[:-tiles]
    total = shared[0][...]
    for other in shared[1:]:
        total = total + other[...]
    epochs = gradient.shape[0] // len(pieces)
    look_rows = gradient.shape[1]
    for number, piece in enumerate(pieces):
        for epoch in range(epochs):
            piece[epoch * look_rows : (epoch + 1) * look_rows, :] = gradient[number * epochs + epoch]
        piece[epochs * look_rows :, :] = total


def update_kernel(cell_count, me, prev_mean, estimate, direction, *refs):
    new_estimate, new_direction = refs[-2:]
    pieces = refs[:-2]
    tiles = len(pieces)
    epochs = estimate.shape[0]
    look_rows = estimate.shape[1]
    total = pieces[0][epochs * look_rows :, :]
    for piece in pieces[1:]:
        total = total + piece[epochs * look_rows :, :]
    total = jnp.sum(total, axis=1, keepdims=True)
    grad_norm, crossed, grad_term, mixed, old_term = (total[at : at + 1, :] for at in range(5))
    momentum = grad_norm / cell_count / prev_mean[0]
    curvature = grad_term + 2.0 * momentum * mixed + momentum * momentum * old_term
    step = (grad_norm + momentum * crossed) / curvature
    momentum = jnp.broadcast_to(momentum, (look_rows, LANES))
    step = jnp.broadcast_to(step, (look_rows, LANES))
    for shift, piece in enumerate(pieces):
        tile = lax.rem(me[0] - shift + tiles, tiles)
        columns = pl.ds(pl.multiple_of(tile * LANES, LANES), LANES)
        for epoch in range(epochs):
            gradient = piece[epoch * look_rows : (epoch + 1) * look_rows, :]
            moved = gradient + momentum * direction[epoch, :, columns]
            new_direction[epoch, :, columns] = moved
            new_estimate[epoch, :, columns] = estimate[epoch, :, columns] + step * moved


def swapped(up, down, axis):
    size = lax.axis_size(axis)
    if size == 1:
        return jnp.zeros_like(up), jnp.zeros_like(down)
    if size == 2:
        first = lax.axis_index(axis) == 0
        got = lax.ppermute(jnp.where(first, up, down), axis, [(0, 1), (1, 0)])
        return got, got
    forward = [(i, i + 1) for i in range(size - 1)]
    backward = [(target, source) for source, target in forward]
    return lax.ppermute(up, axis, forward), lax.ppermute(down, axis, backward)


def to_ahead(x, axis, by):
    size = lax.axis_size(axis)
    return lax.ppermute(x, axis, [(i, (i + by) % size) for i in range(size)])


def transposed_plan(slc, offsets, weights, estimate, direction, prev_mean):
    f32 = jnp.float32
    bf16 = jnp.bfloat16
    tiles = lax.axis_size("epoch")
    me = lax.axis_index("epoch")
    epochs, rows, columns = slc.shape[1:]
    look_rows = rows // LOOK
    total = tiles * epochs
    tile_rows = 2 * epochs * rows
    params_of = pltpu.CompilerParams(vmem_limit_bytes=VMEM_BYTES)

    def fetched(messages, shift):
        return to_ahead(messages[tiles - shift], "epoch", tiles - shift)

    sub = lax.axis_index("sub")
    outer_tile = (2, epochs, rows, LANES)
    edge = pl.pallas_call(
        edge_kernel,
        out_shape=jax.ShapeDtypeStruct((rows, LANES), bf16),
        grid=(1,),
        in_specs=[
            pl.BlockSpec(outer_tile, lambda _: (0, 0, 0, 0)),
            pl.BlockSpec(outer_tile, lambda _: (0, 0, 0, tiles - 1)),
        ],
        out_specs=pl.BlockSpec((rows, LANES), lambda _: (0, 0)),
        compiler_params=params_of,
        cost_estimate=pl.CostEstimate(flops=1_000_000, bytes_accessed=1_000_000, transcendentals=0),
    )(slc, slc)
    before, after = swapped(edge, edge, "sub")
    params = jnp.zeros((rows, LANES), f32)
    listed = jnp.concatenate([offsets.astype(f32), weights, weights, weights], axis=1)
    params = lax.dynamic_update_slice(params, listed, (0, PARAM_LANE))
    sub_present = jnp.stack([sub > 0, sub < lax.axis_size("sub") - 1]).astype(f32)
    messages = pl.pallas_call(
        pack_kernel,
        out_shape=(jax.ShapeDtypeStruct((tile_rows + rows, LANES), bf16),) * tiles,
        in_specs=[SMEM] * 2 + [VMEM] * 4,
        out_specs=(VMEM,) * tiles,
        scratch_shapes=[pltpu.VMEM((tiles, rows, LANES), bf16)],
        compiler_params=params_of,
        cost_estimate=pl.CostEstimate(flops=3_000_000, bytes_accessed=4_000_000, transcendentals=0),
    )(me.reshape(1), sub_present, slc, params, before, after)
    block = [messages[0]] + [fetched(messages, shift) for shift in range(1, tiles)]

    estimate, direction, _ = lax.optimization_barrier((estimate, direction, messages))
    fields = pl.pallas_call(
        fields_kernel,
        out_shape=(jax.ShapeDtypeStruct((3, epochs * look_rows, LANES), bf16),) * tiles,
        in_specs=[SMEM] + [VMEM] * 2,
        out_specs=(VMEM,) * tiles,
        compiler_params=params_of,
        cost_estimate=pl.CostEstimate(flops=1_000_000, bytes_accessed=2_000_000, transcendentals=0),
    )(me.reshape(1), estimate, direction)
    late = lax.optimization_barrier((fields, block))[0]
    field = [fields[0]] + [fetched(late, shift) for shift in range(1, tiles)]

    space = lax.axis_index("space")
    spaces = lax.axis_size("space")
    present = jnp.stack([space > 0, space < spaces - 1]).astype(f32)

    def halo(pieces):
        def border(from_row):
            cuts = [lax.dynamic_slice_in_dim(piece, from_row, HALO, axis=1).reshape(-1, LANES) for piece in pieces]
            return jnp.concatenate(cuts, axis=0)

        if spaces == 2:
            got = lax.ppermute(border(jnp.where(space == 0, rows - HALO, 0)), "space", [(0, 1), (1, 0)])
            return got, got
        return swapped(border(rows - HALO), border(0), "space")

    def by_rows(shift):
        return block[shift].reshape(-1, rows, LANES)

    def params_in(shift):
        return block[shift][tile_rows : tile_rows + epochs, PARAM_LANE : PARAM_LANE + 4 * SLOTS].astype(f32)

    def pairs_of(blocks, loaded):
        listed = jnp.concatenate([params_in(block) for block in blocks], axis=0)
        mate = jnp.arange(len(blocks) * epochs, dtype=jnp.int32)[:, None] + listed[:, :SLOTS].astype(jnp.int32)
        weight = listed[:, SLOTS : 2 * SLOTS] + listed[:, 2 * SLOTS : 3 * SLOTS] + listed[:, 3 * SLOTS :]
        return mate.reshape(-1), weight.reshape(-1)

    top, bottom = halo([by_rows(shift) for shift in range(tiles)])
    listed = jnp.concatenate([params_in(shift) for shift in range(tiles)], axis=0)
    partner = jnp.arange(total, dtype=jnp.int32)[:, None] + listed[:, :SLOTS].astype(jnp.int32)
    partner = lax.rem(partner, total).reshape(-1)
    weight = listed[:, SLOTS : 2 * SLOTS] + listed[:, 2 * SLOTS : 3 * SLOTS] + listed[:, 3 * SLOTS :]
    weight = weight.reshape(-1)

    group = 2 * SLOTS
    batches = tiles + total

    def scratch(looks):
        return [
            pltpu.VMEM((2 * total, LOOK, looks, LANES), f32),
            pltpu.VMEM((2 * total, looks, LANES), f32),
            pltpu.VMEM((batches * group * looks, LANES), f32),
            pltpu.VMEM((batches * 2 * looks, LANES), f32),
            pltpu.VMEM((batches * group * looks, LANES), f32),
        ]

    boxed_shape = (batches, group * look_rows, LANES)
    inner = pl.pallas_call(
        functools.partial(inner_kernel, (tiles, epochs, rows)),
        out_shape=jax.ShapeDtypeStruct(boxed_shape, f32),
        in_specs=[SMEM] + [VMEM] * tiles,
        out_specs=VMEM,
        scratch_shapes=scratch(look_rows),
        compiler_params=params_of,
        cost_estimate=pl.CostEstimate(flops=20_000_000, bytes_accessed=20_000_000, transcendentals=0),
    )(partner, *block)
    pair_shape = jax.ShapeDtypeStruct((total * SLOTS, look_rows, LANES), f32)
    factors, pulls = pl.pallas_call(
        functools.partial(border_kernel, (tiles, epochs, look_rows)),
        out_shape=(pair_shape, pair_shape),
        in_specs=[SMEM] * 3 + [VMEM] * 3,
        out_specs=(VMEM, VMEM),
        scratch_shapes=[pltpu.VMEM(boxed_shape, f32)] + scratch(2 * HALO // LOOK),
        compiler_params=params_of,
        cost_estimate=pl.CostEstimate(flops=20_000_000, bytes_accessed=15_000_000, transcendentals=0),
    )(partner, weight, present, top, bottom, inner)
    gradient, sums = pl.pallas_call(
        functools.partial(gradient_kernel, (tiles, epochs)),
        out_shape=(
            jax.ShapeDtypeStruct((total, look_rows, LANES), f32),
            jax.ShapeDtypeStruct((8, LANES), f32),
        ),
        in_specs=[SMEM] + [VMEM] * (tiles + 2),
        out_specs=(VMEM, VMEM),
        scratch_shapes=[pltpu.VMEM((total, look_rows, LANES), f32)] * 2,
        compiler_params=params_of,
        cost_estimate=pl.CostEstimate(flops=10_000_000, bytes_accessed=8_000_000, transcendentals=0),
    )(partner, *field, factors, pulls)

    place = ("space", "sub")
    count = spaces * lax.axis_size("sub")
    shared = [sums] + [lax.ppermute(sums, place, [(i, (i + by) % count) for i in range(count)]) for by in range(1, count)]
    pieces = pl.pallas_call(
        functools.partial(return_kernel, tiles),
        out_shape=(jax.ShapeDtypeStruct((epochs * look_rows + 8, LANES), f32),) * tiles,
        in_specs=[VMEM] * (1 + count),
        out_specs=(VMEM,) * tiles,
        compiler_params=params_of,
        cost_estimate=pl.CostEstimate(flops=10_000, bytes_accessed=1_000_000, transcendentals=0),
    )(gradient, *shared)
    returned = [pieces[0]] + [to_ahead(pieces[by], "epoch", by) for by in range(1, tiles)]
    cell_count = float(total * look_rows * spaces * columns * lax.axis_size("sub"))
    return pl.pallas_call(
        functools.partial(update_kernel, cell_count),
        out_shape=(jax.ShapeDtypeStruct(estimate.shape, f32),) * 2,
        in_specs=[SMEM] * 2 + [VMEM] * (2 + tiles),
        out_specs=(VMEM, VMEM),
        compiler_params=params_of,
        cost_estimate=pl.CostEstimate(flops=1_000_000, bytes_accessed=2_000_000, transcendentals=0),
    )(me.reshape(1), prev_mean, estimate, direction, *returned)


def on_device(slc, offsets, weights, estimate, direction, prev_mean):
    epochs, rows, columns = slc.shape[1:]
    fits = columns == LANES * lax.axis_size("epoch") and lax.axis_size("epoch") % 2 == 0
    fits = fits and 2 * epochs * SIDES <= PARAM_LANE and rows % HALO == 0 and epochs == 2 * SLOTS
    plan = transposed_plan if fits else ring_plan
    return plan(slc, offsets, weights, estimate, direction, prev_mean)


def solution(mesh):
    return jax.shard_map(
        on_device,
        mesh=mesh,
        in_specs=(
            P(None, ("groups", "epoch"), "space", "sub"),
            P(("groups", "epoch"), None),
            P(("groups", "epoch"), None),
            P(("groups", "epoch"), "space", "sub"),
            P(("groups", "epoch"), "space", "sub"),
            P(),
        ),
        out_specs=(P(("groups", "epoch"), "space", "sub"), P(("groups", "epoch"), "space", "sub")),
        check_vma=False,
    )
```

```python
import functools

import jax
import jax.numpy as jnp
from jax import lax
from jax.experimental import pallas as pl
from jax.experimental.pallas import tpu as pltpu
from jax.sharding import PartitionSpec as P

SLOTS = 4
OFFS = 8
LOOK = 4
RADIUS = 3


EPSILON = 1e-06


def passed_along(x, axis, by):
    size = lax.axis_size(axis)
    return lax.ppermute(x, axis, [(i, (i + by) % size) for i in range(size)])


def extended_2(block, sides, width):
    for axis, dim in sides:
        count = lax.axis_size(axis)
        forward = [(i, i + 1) for i in range(count - 1)]
        backward = [(target, source) for source, target in forward]
        low = lax.ppermute(
            lax.slice_in_dim(block, block.shape[dim] - width, None, axis=dim), axis, forward
        )
        high = lax.ppermute(lax.slice_in_dim(block, 0, width, axis=dim), axis, backward)
        block = jnp.concatenate([low, block, high], axis=dim)
    return block


def looked_sum(field):
    shape = field.shape
    return jnp.sum(field.reshape(shape[:-2] + (shape[-2] // LOOK, LOOK, shape[-1])), axis=-2)


def window_sum(padded, axis):
    length = padded.shape[axis] - 2 * RADIUS
    total = lax.slice_in_dim(padded, 0, length, axis=axis)
    for shift_at in range(1, 2 * RADIUS + 1):
        total = total + lax.slice_in_dim(padded, shift_at, shift_at + length, axis=axis)
    return total


def ring_plan(slc, offsets, weights, estimate, direction, prev_mean):
    epochs_here = slc.shape[1]
    look_rows = slc.shape[2] // LOOK
    col_count = slc.shape[3]
    ahead = passed_along(slc, "epoch", -1)
    extended = jnp.concatenate([slc, ahead], axis=1)
    numbers = jnp.arange(epochs_here, dtype=jnp.int32)
    partner = numbers[:, None] + offsets
    own_real = slc[0].astype(jnp.float32)
    own_imag = slc[1].astype(jnp.float32)
    ext_real = extended[0].astype(jnp.float32)
    ext_imag = extended[1].astype(jnp.float32)
    powers = looked_sum(ext_real * ext_real + ext_imag * ext_imag)
    pieces = []
    for slot_index in range(SLOTS):
        mate_real = jnp.take(ext_real, partner[:, slot_index], axis=0)
        mate_imag = jnp.take(ext_imag, partner[:, slot_index], axis=0)
        pieces.append(looked_sum(own_real * mate_real + own_imag * mate_imag))
        pieces.append(looked_sum(own_imag * mate_real - own_real * mate_imag))
    pair_count = epochs_here * 2 * SLOTS
    stacked = jnp.concatenate(
        [jnp.stack(pieces, axis=1).reshape(pair_count, look_rows, col_count), powers], axis=0
    )
    padded = extended_2(stacked, (("space", 1), ("sub", 2)), RADIUS)
    boxed = window_sum(window_sum(padded, 1), 2)
    pair_boxed = boxed[:pair_count].reshape(epochs_here, 2 * SLOTS, look_rows, col_count)
    power_box = boxed[pair_count:]
    coh_real = pair_boxed[:, 0::2]
    coh_imag = pair_boxed[:, 1::2]
    denominator = power_box[:epochs_here, None] * jnp.take(power_box, partner, axis=0) + EPSILON
    coherence = (coh_real * coh_real + coh_imag * coh_imag) / denominator
    observed = coh_imag / jnp.sqrt(denominator)
    est_ahead = passed_along(estimate, "epoch", -1)
    est_extended = jnp.concatenate([estimate, est_ahead], axis=0)
    fitted = estimate[:, None] - jnp.take(est_extended, partner, axis=0)
    factor = weights[:, :, None, None] * coherence
    weighted = factor * (observed - fitted)
    flattened = weighted.reshape(epochs_here * SLOTS, look_rows * col_count)
    selector = (
        jnp.arange(epochs_here + OFFS, dtype=jnp.int32)[:, None] == partner.reshape(1, -1)
    ).astype(jnp.float32)
    gathered = jnp.dot(
        selector, flattened, precision=lax.Precision.HIGHEST, preferred_element_type=jnp.float32
    ).reshape(epochs_here + OFFS, look_rows, col_count)
    own_part = jnp.sum(weighted, axis=1) - gathered[:epochs_here]
    returned = passed_along(-gathered[epochs_here:], "epoch", 1)
    gradient = jnp.concatenate([own_part + returned, own_part[OFFS:]], axis=0)
    cell_count = float(
        epochs_here
        * lax.axis_size("epoch")
        * look_rows
        * lax.axis_size("space")
        * col_count
        * lax.axis_size("sub")
    )
    local_norm = jnp.sum(gradient * gradient)
    local_crossed = jnp.sum(gradient * direction)
    mean_before = prev_mean[0]
    fields_ahead = passed_along(
        jnp.stack([gradient, direction]).astype(jnp.bfloat16), "epoch", -1
    ).astype(jnp.float32)
    grad_extended = jnp.concatenate([gradient, fields_ahead[0]], axis=0)
    old_extended = jnp.concatenate([direction, fields_ahead[1]], axis=0)
    grad_spread = gradient[:, None] - jnp.take(grad_extended, partner, axis=0)
    old_spread = direction[:, None] - jnp.take(old_extended, partner, axis=0)
    totals = lax.psum(
        (
            local_norm,
            local_crossed,
            jnp.sum(factor * grad_spread * grad_spread),
            jnp.sum(factor * grad_spread * old_spread),
            jnp.sum(factor * old_spread * old_spread),
        ),
        ("epoch", "space", "sub"),
    )
    grad_norm, crossed, grad_term, mixed_term, old_term = totals
    momentum = grad_norm / cell_count / mean_before
    new_direction = gradient + momentum * direction
    curvature = grad_term + 2.0 * momentum * mixed_term + momentum * momentum * old_term
    along_sum = grad_norm + momentum * crossed
    step_size = along_sum / curvature
    return (estimate + step_size * new_direction, new_direction)


LANES = 128
SIDES = 2 * RADIUS
HALO = 16
PARAM_LANE = 96
VMEM = pl.BlockSpec(memory_space=pltpu.VMEM)
SMEM = pl.BlockSpec(memory_space=pltpu.SMEM)
VMEM_BYTES = 48 * 1024 * 1024


def split_two(value):
    high = value.astype(jnp.bfloat16)
    low = (value - high.astype(jnp.float32)).astype(jnp.bfloat16)
    return high, low


def edge_kernel(first, last, edge):
    epochs = first.shape[1]
    lane = lax.broadcasted_iota(jnp.int32, edge.shape, 1)
    total = jnp.zeros(edge.shape, jnp.float32)
    for part in range(2):
        for epoch in range(epochs):
            at = (part * epochs + epoch) * SIDES
            total = placed(lane, total, tile_of(last, part, epoch, 0), LANES - RADIUS, at)
            total = placed(lane, total, tile_of(first, part, epoch, 0), 0, at + RADIUS)
    edge[...] = total.astype(jnp.bfloat16)


def fields_kernel(me, estimate, direction, *fields):
    look_rows = estimate.shape[1]
    tiles = len(fields)
    for shift, out in enumerate(fields):
        tile = lax.rem(me[0] + shift, tiles)
        columns = pl.ds(pl.multiple_of(tile * LANES, LANES), LANES)
        for epoch in range(estimate.shape[0]):
            here = slice(epoch * look_rows, (epoch + 1) * look_rows)
            first, second = split_two(estimate[epoch, :, columns])
            out[0, here, :] = first
            out[1, here, :] = second
            out[2, here, :] = direction[epoch, :, columns].astype(jnp.bfloat16)


def tile_of(slc, part, epoch, tile):
    return slc[part, epoch, :, tile * LANES : (tile + 1) * LANES].astype(jnp.float32)


def placed(lane, total, source, start, target):
    moved = pltpu.roll(source, (target - start) % LANES, axis=1)
    return jnp.where((lane >= target) & (lane < target + RADIUS), moved, total)


def pack_kernel(me, present, slc, params, before, after, *refs):
    messages, strips = refs[:-1], refs[-1]
    tiles = len(messages)
    epochs = slc.shape[1]
    rows = slc.shape[2]
    lane = lax.broadcasted_iota(jnp.int32, (rows, LANES), 1)
    value = params[...]
    high = value.astype(jnp.bfloat16).astype(jnp.float32)
    middle = (value - high).astype(jnp.bfloat16).astype(jnp.float32)
    low = value - high - middle
    third = PARAM_LANE + 2 * SLOTS
    split = jnp.where(lane < third, high, jnp.where(lane < third + SLOTS, middle, low))
    split = jnp.where(lane >= PARAM_LANE, split, 0.0)
    inside = lane < 2 * epochs * SIDES
    for tile in range(tiles):
        total = split
        if tile == 0:
            edge = before[...].astype(jnp.float32) * present[0]
            total = jnp.where(inside & (lane % SIDES < RADIUS), edge, total)
        if tile == tiles - 1:
            edge = after[...].astype(jnp.float32) * present[1]
            total = jnp.where(inside & (lane % SIDES >= RADIUS), edge, total)
        for part in range(2):
            for epoch in range(epochs):
                at = (part * epochs + epoch) * SIDES
                if tile > 0:
                    total = placed(lane, total, tile_of(slc, part, epoch, tile - 1), LANES - RADIUS, at)
                if tile < tiles - 1:
                    total = placed(lane, total, tile_of(slc, part, epoch, tile + 1), 0, at + RADIUS)
        strips[tile] = total.astype(jnp.bfloat16)
    for tile in range(tiles):
        shift = lax.rem(tile - me[0] + tiles, tiles)
        for number, message in enumerate(messages):

            @pl.when(shift == number)
            def _():
                for part in range(2):
                    for epoch in range(epochs):
                        at = (part * epochs + epoch) * rows
                        message[at : at + rows, :] = slc[part, epoch, :, tile * LANES : (tile + 1) * LANES]
                message[2 * epochs * rows :, :] = strips[tile]


def look_order(from_rows, keep):
    looks = from_rows // LOOK
    to = lax.broadcasted_iota(jnp.int32, (from_rows, from_rows), 0)
    at = lax.broadcasted_iota(jnp.int32, (from_rows, from_rows), 1)
    order = (at == to % looks * LOOK + to // looks).astype(jnp.float32)
    return (order * keep(at)).astype(jnp.bfloat16)


def unpack_tiles(order, sources, main, first, columns_of):
    looks = order.shape[0] // LOOK
    for start in range(0, len(sources), 4):
        parts = jnp.concatenate([columns_of(source) for source in sources[start : start + 4]], axis=1)
        value = jnp.dot(order, parts, preferred_element_type=jnp.float32)
        for one in range(4):
            for look in range(LOOK):
                main[first[start + one], look] = value[look * looks : (look + 1) * looks, one * LANES : (one + 1) * LANES]


def unpack_rims(by_look, looks, rim, first):
    share = LANES // SLOTS
    lane = lax.broadcasted_iota(jnp.int32, (looks, LANES), 1)
    for at, place in enumerate(first):
        value = jnp.zeros((looks, LANES), jnp.float32)
        for look in range(LOOK):
            target = look * SIDES
            moved = pltpu.roll(by_look[look * looks : (look + 1) * looks], (target - at * SIDES) % LANES, axis=1)
            value = jnp.where((lane >= target) & (lane < target + SIDES), moved, value)
        spread = share
        while spread < LANES:
            value = value + pltpu.roll(value, spread, axis=1)
            spread = 2 * spread
        rim[place] = value


def band_of(shape, from_of, to_of):
    at = lax.broadcasted_iota(jnp.int32, shape, 0)
    to = lax.broadcasted_iota(jnp.int32, shape, 1)
    return (jnp.abs(from_of(at, to) - to_of(at, to)) <= RADIUS).astype(jnp.float32).astype(jnp.bfloat16)


def column_bands():
    share = LANES // SLOTS

    def rim_from(at, to):
        side = at % share % SIDES
        return jnp.where(side < RADIUS, side - RADIUS, LANES + side - RADIUS)

    def rim_to(at, to):
        column = (to - at % LANES // share * share + LANES) % LANES
        inside = (column < RADIUS) | (column >= LANES - RADIUS)
        inside = inside & (at % share < LOOK * SIDES)
        return jnp.where(inside, column, 4 * LANES)

    band = band_of((2 * LANES, LANES), lambda at, to: at % LANES, lambda at, to: to)
    return band, band_of((2 * LANES, LANES), rim_from, rim_to)


def row_sums(look_rows, looks, look_of):
    group = 2 * SLOTS
    out_at = lax.broadcasted_iota(jnp.int32, (group * look_rows, group * looks), 0)
    in_at = lax.broadcasted_iota(jnp.int32, (group * look_rows, group * looks), 1)
    near = jnp.abs(look_of(in_at % looks) - out_at % look_rows) <= RADIUS
    near = near & (in_at // looks == out_at // look_rows)
    return near.astype(jnp.float32).astype(jnp.bfloat16)


def mixed(values):
    lane = lax.broadcasted_iota(jnp.int32, values[0].shape, 1)
    result = values[-1]
    for slot in range(SLOTS - 1):
        result = jnp.where(lane // (LANES // SLOTS) == slot, values[slot], result)
    return result


def power_batches(blocks, epochs, looks, main, rim, looked, rim_looked):
    total = blocks * epochs
    group = 2 * SLOTS
    for block in range(blocks):
        for piece in range(0, looks, 8):
            rows_at = slice(piece, piece + 8)
            for half in range(2):
                squares = []
                for slot in range(SLOTS):
                    channel = half * SLOTS + slot
                    epoch = block * epochs + channel
                    value = None
                    for look in range(LOOK):
                        real = main[epoch, look, rows_at]
                        imag = main[total + epoch, look, rows_at]
                        one = real * real + imag * imag
                        value = one if value is None else value + one
                    at = (block * group + channel) * looks + piece
                    looked[at : at + 8, :] = value
                    real = rim[epoch, rows_at]
                    imag = rim[total + epoch, rows_at]
                    squares.append(real * real + imag * imag)
                at = (block * 2 + half) * looks + piece
                rim_looked[at : at + 8, :] = mixed(squares)


def pair_batch(batch, epoch, mates, total, looks, main, rim):
    group = 2 * SLOTS
    products, rims = [], []
    for piece in range(0, looks, 8):
        rows_at = slice(piece, piece + 8)
        own_re = [main[epoch, look, rows_at] for look in range(LOOK)]
        own_im = [main[total + epoch, look, rows_at] for look in range(LOOK)]
        for slot, mate in enumerate(mates):
            real = None
            for look in range(LOOK):
                mate_re = main[mate, look, rows_at]
                mate_im = main[total + mate, look, rows_at]
                one = own_re[look] * mate_re + own_im[look] * mate_im
                two = own_im[look] * mate_re - own_re[look] * mate_im
                real = one if real is None else real + one
                imag = two if look == 0 else imag + two
            products.append(((batch * group + slot) * looks + piece, real))
            products.append(((batch * group + SLOTS + slot) * looks + piece, imag))
        rim_re = rim[epoch, rows_at]
        rim_im = rim[total + epoch, rows_at]
        mate_re = mixed([rim[mate, rows_at] for mate in mates])
        mate_im = mixed([rim[total + mate, rows_at] for mate in mates])
        rims.append((batch * 2 * looks + piece, rim_re * mate_re + rim_im * mate_im))
        rims.append(((batch * 2 + 1) * looks + piece, rim_im * mate_re - rim_re * mate_im))
    return products, rims


def put(ref, parts):
    for at, value in parts:
        ref[pl.ds(pl.multiple_of(at, 8), value.shape[0]), :] = value


def columns_summed(couple, looks, bands, looked, rim_looked):
    group = 2 * SLOTS
    f32 = jnp.float32
    at = pl.ds(pl.multiple_of(couple * (2 * group * looks), 2 * group * looks), 2 * group * looks)
    halves = jnp.concatenate(split_two(looked[at, :]), axis=1)
    value = jnp.dot(halves, bands[0], preferred_element_type=f32)
    at = pl.ds(pl.multiple_of(couple * (4 * looks), 4 * looks), 4 * looks)
    halves = jnp.concatenate(split_two(rim_looked[at, :]), axis=1)
    outer = jnp.dot(halves, bands[1], preferred_element_type=f32)
    lane = lax.broadcasted_iota(jnp.int32, (looks, LANES), 1)
    outside = (lane < RADIUS) | (lane >= LANES - RADIUS)
    results = []
    for channel in range(2 * group):
        batch, half, slot = channel // group, channel % group // SLOTS, channel % SLOTS
        row = (batch * 2 + half) * looks
        part = outer[row : row + looks]
        if slot > 0:
            part = pltpu.roll(part, LANES - slot * (LANES // SLOTS), axis=1)
        row = channel * looks
        results.append((couple * (2 * group * looks) + row, value[row : row + looks] + jnp.where(outside, part, 0.0)))
    return results


def rows_summed(batch, looks, sum_rows, wide):
    rows = 2 * SLOTS * looks
    at = pl.ds(pl.multiple_of(batch * rows, rows), rows)
    halves = jnp.concatenate(split_two(wide[at, :]), axis=1)
    value = jnp.dot(sum_rows, halves, preferred_element_type=jnp.float32)
    return value[:, :LANES] + value[:, LANES:]


def pair_couple(turn, tiles, total, partner, looks, main, rim):
    here = clipped(turn, total // 2 - 1)
    products, rims = [], []
    for one in range(2):
        epoch = here * 2 + one
        mates = [partner[epoch * SLOTS + slot] for slot in range(SLOTS)]
        more, more_rims = pair_batch(tiles + epoch, epoch, mates, total, looks, main, rim)
        products += more
        rims += more_rims
    return products, rims


def clipped(value, last):
    return jnp.minimum(jnp.maximum(value, 0), last)


def inner_kernel(sizes, partner, *refs):
    tiles, epochs, rows = sizes
    messages = refs[:tiles]
    boxed, main, rim, looked, rim_looked, wide = refs[tiles:]
    total = tiles * epochs
    look_rows = rows // LOOK
    order = look_order(rows, lambda at: 1.0)
    bands = column_bands()
    sum_rows = row_sums(look_rows, look_rows, lambda look: look)
    for block, message in enumerate(messages):
        first = [part * total + block * epochs + epoch for part in range(2) for epoch in range(epochs)]
        unpack_tiles(order, range(2 * epochs), main, first, lambda at: message[at * rows : (at + 1) * rows, :])
        by_look = jnp.dot(order, message[2 * epochs * rows :, :], preferred_element_type=jnp.float32)
        unpack_rims(by_look, look_rows, rim, first)
    power_batches(tiles, epochs, look_rows, main, rim, looked, rim_looked)
    last = (tiles + total) // 2 - 1

    @pl.loop(0, last + 2)
    def _(turn):
        here = clipped(turn - 1, last)
        sums = [rows_summed(here * 2 + one, look_rows, sum_rows, wide) for one in range(2)]
        columns = columns_summed(clipped(turn, last), look_rows, bands, looked, rim_looked)
        products, rims = pair_couple(turn, tiles, total, partner, look_rows, main, rim)
        for one in range(2):
            boxed[here * 2 + one] = sums[one]
        put(wide, columns)
        put(looked, products)
        put(rim_looked, rims)


def border_kernel(sizes, partner, weight, present, *refs):
    tiles, epochs, look_rows = sizes
    top, bottom, inner, factors, pulls, boxed, main, rim, looked, rim_looked, wide = refs
    total = tiles * epochs
    looks = 2 * HALO // LOOK
    halo_looks = HALO // LOOK
    tile_rows = (2 * epochs + 1) * HALO
    order = look_order(2 * HALO, lambda at: jnp.where(at < HALO, present[0], present[1]))
    bands = column_bands()
    sum_rows = row_sums(look_rows, looks, lambda at: jnp.where(at < halo_looks, at - halo_looks, at - halo_looks + look_rows))
    for block in range(tiles):

        def border_of(at):
            here = slice(block * tile_rows + at * HALO, block * tile_rows + (at + 1) * HALO)
            return jnp.concatenate([top[here, :], bottom[here, :]], axis=0)

        first = [part * total + block * epochs + epoch for part in range(2) for epoch in range(epochs)]
        unpack_tiles(order, range(2 * epochs), main, first, border_of)
        by_look = jnp.dot(order, border_of(2 * epochs), preferred_element_type=jnp.float32)
        unpack_rims(by_look, looks, rim, first)
    power_batches(tiles, epochs, looks, main, rim, looked, rim_looked)
    last = (tiles + total) // 2 - 1

    def power_of(epoch):
        at = pl.ds(pl.multiple_of(epoch % epochs * look_rows, look_rows), look_rows)
        return boxed[epoch // epochs, at, :]

    @pl.loop(0, last + 3)
    def _(turn):
        done = clipped(turn - 2 - tiles // 2, total // 2 - 1)
        results = []
        for one in range(2):
            epoch = done * 2 + one
            batch = tiles + epoch
            own_power = power_of(epoch)
            for slot in range(SLOTS):
                pair = epoch * SLOTS + slot
                inverse = lax.rsqrt(own_power * power_of(partner[pair]) + EPSILON)
                unit_re = boxed[batch, slot * look_rows : (slot + 1) * look_rows, :] * inverse
                unit_im = boxed[batch, (SLOTS + slot) * look_rows : (SLOTS + slot + 1) * look_rows, :] * inverse
                factor = weight[pair] * (unit_re * unit_re + unit_im * unit_im)
                results.append((pair, factor, factor * unit_im))
        here = clipped(turn - 1, last)
        sums = [inner[here * 2 + one] + rows_summed(here * 2 + one, looks, sum_rows, wide) for one in range(2)]
        columns = columns_summed(clipped(turn, last), looks, bands, looked, rim_looked)
        products, rims = pair_couple(turn, tiles, total, partner, looks, main, rim)
        for pair, factor, pull in results:
            factors[pair] = factor
            pulls[pair] = pull
        for one in range(2):
            boxed[here * 2 + one] = sums[one]
        put(wide, columns)
        put(looked, products)
        put(rim_looked, rims)


def gradient_kernel(sizes, partner, *refs):
    tiles, epochs = sizes
    fields = refs[:tiles]
    factors, pulls, gradient, sums, est, old = refs[tiles:]
    look_rows = est.shape[1]
    total = tiles * epochs
    f32 = jnp.float32
    for block in range(tiles):

        @pl.loop(0, epochs, unroll=4)
        def _(epoch):
            here = pl.ds(pl.multiple_of(epoch * look_rows, look_rows), look_rows)
            est[block * epochs + epoch] = fields[block][0, here, :].astype(f32) + fields[block][1, here, :].astype(f32)
            old[block * epochs + epoch] = fields[block][2, here, :].astype(f32)
            gradient[block * epochs + epoch] = jnp.zeros((look_rows, LANES), f32)

    @pl.loop(0, total, unroll=2)
    def _(epoch):
        own_est = est[epoch]
        own = jnp.zeros((look_rows, LANES), f32)
        mates = [partner[epoch * SLOTS + slot] for slot in range(SLOTS)]
        values = []
        for slot, mate in enumerate(mates):
            pair = epoch * SLOTS + slot
            weighted = pulls[pair] - factors[pair] * (own_est - est[mate])
            own = own + weighted
            values.append(weighted)
        for mate, weighted in zip(mates, values):
            gradient[mate] = gradient[mate] - weighted
        gradient[epoch] = gradient[epoch] + own

    def totals(epoch, carry):
        norm, crossed, grad_term, mixed_term, old_term = carry
        own_grad = gradient[epoch]
        own_old = old[epoch]
        norm = norm + own_grad * own_grad
        crossed = crossed + own_grad * own_old
        for slot in range(SLOTS):
            mate = partner[epoch * SLOTS + slot]
            factor = factors[epoch * SLOTS + slot]
            grad_spread = own_grad - gradient[mate]
            old_spread = own_old - old[mate]
            pulled = factor * grad_spread
            grad_term = grad_term + pulled * grad_spread
            mixed_term = mixed_term + pulled * old_spread
            old_term = old_term + factor * old_spread * old_spread
        return norm, crossed, grad_term, mixed_term, old_term

    zero = jnp.zeros((look_rows, LANES), f32)
    results = lax.fori_loop(0, total, totals, (zero,) * 5, unroll=2)
    sums[...] = jnp.zeros(sums.shape, f32)
    for at, value in enumerate(results):
        sums[at : at + 1, :] = jnp.sum(value, axis=0, keepdims=True)


def return_kernel(tiles, gradient, *refs):
    pieces = refs[-tiles:]
    shared = refs[:-tiles]
    total = shared[0][...]
    for other in shared[1:]:
        total = total + other[...]
    epochs = gradient.shape[0] // len(pieces)
    look_rows = gradient.shape[1]
    for number, piece in enumerate(pieces):
        for epoch in range(epochs):
            piece[epoch * look_rows : (epoch + 1) * look_rows, :] = gradient[number * epochs + epoch]
        piece[epochs * look_rows :, :] = total


def update_kernel(cell_count, me, prev_mean, estimate, direction, *refs):
    new_estimate, new_direction = refs[-2:]
    pieces = refs[:-2]
    tiles = len(pieces)
    epochs = estimate.shape[0]
    look_rows = estimate.shape[1]
    total = pieces[0][epochs * look_rows :, :]
    for piece in pieces[1:]:
        total = total + piece[epochs * look_rows :, :]
    total = jnp.sum(total, axis=1, keepdims=True)
    grad_norm, crossed, grad_term, mixed, old_term = (total[at : at + 1, :] for at in range(5))
    momentum = grad_norm / cell_count / prev_mean[0]
    curvature = grad_term + 2.0 * momentum * mixed + momentum * momentum * old_term
    step = (grad_norm + momentum * crossed) / curvature
    momentum = jnp.broadcast_to(momentum, (look_rows, LANES))
    step = jnp.broadcast_to(step, (look_rows, LANES))
    for shift, piece in enumerate(pieces):
        tile = lax.rem(me[0] - shift + tiles, tiles)
        columns = pl.ds(pl.multiple_of(tile * LANES, LANES), LANES)
        for epoch in range(epochs):
            gradient = piece[epoch * look_rows : (epoch + 1) * look_rows, :]
            moved = gradient + momentum * direction[epoch, :, columns]
            new_direction[epoch, :, columns] = moved
            new_estimate[epoch, :, columns] = estimate[epoch, :, columns] + step * moved


def swapped(up, down, axis):
    size = lax.axis_size(axis)
    if size == 1:
        return jnp.zeros_like(up), jnp.zeros_like(down)
    if size == 2:
        first = lax.axis_index(axis) == 0
        got = lax.ppermute(jnp.where(first, up, down), axis, [(0, 1), (1, 0)])
        return got, got
    forward = [(i, i + 1) for i in range(size - 1)]
    backward = [(target, source) for source, target in forward]
    return lax.ppermute(up, axis, forward), lax.ppermute(down, axis, backward)


def to_ahead(x, axis, by):
    size = lax.axis_size(axis)
    return lax.ppermute(x, axis, [(i, (i + by) % size) for i in range(size)])


def transposed_plan(slc, offsets, weights, estimate, direction, prev_mean):
    f32 = jnp.float32
    bf16 = jnp.bfloat16
    tiles = lax.axis_size("epoch")
    me = lax.axis_index("epoch")
    epochs, rows, columns = slc.shape[1:]
    look_rows = rows // LOOK
    total = tiles * epochs
    tile_rows = 2 * epochs * rows
    params_of = pltpu.CompilerParams(vmem_limit_bytes=VMEM_BYTES)

    def fetched(messages, shift):
        return to_ahead(messages[tiles - shift], "epoch", tiles - shift)

    sub = lax.axis_index("sub")
    outer_tile = (2, epochs, rows, LANES)
    edge = pl.pallas_call(
        edge_kernel,
        out_shape=jax.ShapeDtypeStruct((rows, LANES), bf16),
        grid=(1,),
        in_specs=[
            pl.BlockSpec(outer_tile, lambda _: (0, 0, 0, 0)),
            pl.BlockSpec(outer_tile, lambda _: (0, 0, 0, tiles - 1)),
        ],
        out_specs=pl.BlockSpec((rows, LANES), lambda _: (0, 0)),
        compiler_params=params_of,
        cost_estimate=pl.CostEstimate(flops=1_000_000, bytes_accessed=1_000_000, transcendentals=0),
    )(slc, slc)
    before, after = swapped(edge, edge, "sub")
    params = jnp.zeros((rows, LANES), f32)
    listed = jnp.concatenate([offsets.astype(f32), weights, weights, weights], axis=1)
    params = lax.dynamic_update_slice(params, listed, (0, PARAM_LANE))
    sub_present = jnp.stack([sub > 0, sub < lax.axis_size("sub") - 1]).astype(f32)
    messages = pl.pallas_call(
        pack_kernel,
        out_shape=(jax.ShapeDtypeStruct((tile_rows + rows, LANES), bf16),) * tiles,
        in_specs=[SMEM] * 2 + [VMEM] * 4,
        out_specs=(VMEM,) * tiles,
        scratch_shapes=[pltpu.VMEM((tiles, rows, LANES), bf16)],
        compiler_params=params_of,
        cost_estimate=pl.CostEstimate(flops=3_000_000, bytes_accessed=4_000_000, transcendentals=0),
    )(me.reshape(1), sub_present, slc, params, before, after)
    block = [messages[0]] + [fetched(messages, shift) for shift in range(1, tiles)]

    estimate, direction, _ = lax.optimization_barrier((estimate, direction, messages))
    fields = pl.pallas_call(
        fields_kernel,
        out_shape=(jax.ShapeDtypeStruct((3, epochs * look_rows, LANES), bf16),) * tiles,
        in_specs=[SMEM] + [VMEM] * 2,
        out_specs=(VMEM,) * tiles,
        compiler_params=params_of,
        cost_estimate=pl.CostEstimate(flops=1_000_000, bytes_accessed=2_000_000, transcendentals=0),
    )(me.reshape(1), estimate, direction)
    late = lax.optimization_barrier((fields, block))[0]
    field = [fields[0]] + [fetched(late, shift) for shift in range(1, tiles)]

    space = lax.axis_index("space")
    spaces = lax.axis_size("space")
    present = jnp.stack([space > 0, space < spaces - 1]).astype(f32)

    def halo(pieces):
        def border(from_row):
            cuts = [lax.dynamic_slice_in_dim(piece, from_row, HALO, axis=1).reshape(-1, LANES) for piece in pieces]
            return jnp.concatenate(cuts, axis=0)

        if spaces == 2:
            got = lax.ppermute(border(jnp.where(space == 0, rows - HALO, 0)), "space", [(0, 1), (1, 0)])
            return got, got
        return swapped(border(rows - HALO), border(0), "space")

    def by_rows(shift):
        return block[shift].reshape(-1, rows, LANES)

    def params_in(shift):
        return block[shift][tile_rows : tile_rows + epochs, PARAM_LANE : PARAM_LANE + 4 * SLOTS].astype(f32)

    def pairs_of(blocks, loaded):
        listed = jnp.concatenate([params_in(block) for block in blocks], axis=0)
        mate = jnp.arange(len(blocks) * epochs, dtype=jnp.int32)[:, None] + listed[:, :SLOTS].astype(jnp.int32)
        weight = listed[:, SLOTS : 2 * SLOTS] + listed[:, 2 * SLOTS : 3 * SLOTS] + listed[:, 3 * SLOTS :]
        return mate.reshape(-1), weight.reshape(-1)

    top, bottom = halo([by_rows(shift) for shift in range(tiles)])
    listed = jnp.concatenate([params_in(shift) for shift in range(tiles)], axis=0)
    partner = jnp.arange(total, dtype=jnp.int32)[:, None] + listed[:, :SLOTS].astype(jnp.int32)
    partner = lax.rem(partner, total).reshape(-1)
    weight = listed[:, SLOTS : 2 * SLOTS] + listed[:, 2 * SLOTS : 3 * SLOTS] + listed[:, 3 * SLOTS :]
    weight = weight.reshape(-1)

    group = 2 * SLOTS
    batches = tiles + total

    def scratch(looks):
        return [
            pltpu.VMEM((2 * total, LOOK, looks, LANES), f32),
            pltpu.VMEM((2 * total, looks, LANES), f32),
            pltpu.VMEM((batches * group * looks, LANES), f32),
            pltpu.VMEM((batches * 2 * looks, LANES), f32),
            pltpu.VMEM((batches * group * looks, LANES), f32),
        ]

    boxed_shape = (batches, group * look_rows, LANES)
    inner = pl.pallas_call(
        functools.partial(inner_kernel, (tiles, epochs, rows)),
        out_shape=jax.ShapeDtypeStruct(boxed_shape, f32),
        in_specs=[SMEM] + [VMEM] * tiles,
        out_specs=VMEM,
        scratch_shapes=scratch(look_rows),
        compiler_params=params_of,
        cost_estimate=pl.CostEstimate(flops=20_000_000, bytes_accessed=20_000_000, transcendentals=0),
    )(partner, *block)
    pair_shape = jax.ShapeDtypeStruct((total * SLOTS, look_rows, LANES), f32)
    factors, pulls = pl.pallas_call(
        functools.partial(border_kernel, (tiles, epochs, look_rows)),
        out_shape=(pair_shape, pair_shape),
        in_specs=[SMEM] * 3 + [VMEM] * 3,
        out_specs=(VMEM, VMEM),
        scratch_shapes=[pltpu.VMEM(boxed_shape, f32)] + scratch(2 * HALO // LOOK),
        compiler_params=params_of,
        cost_estimate=pl.CostEstimate(flops=20_000_000, bytes_accessed=15_000_000, transcendentals=0),
    )(partner, weight, present, top, bottom, inner)
    gradient, sums = pl.pallas_call(
        functools.partial(gradient_kernel, (tiles, epochs)),
        out_shape=(
            jax.ShapeDtypeStruct((total, look_rows, LANES), f32),
            jax.ShapeDtypeStruct((8, LANES), f32),
        ),
        in_specs=[SMEM] + [VMEM] * (tiles + 2),
        out_specs=(VMEM, VMEM),
        scratch_shapes=[pltpu.VMEM((total, look_rows, LANES), f32)] * 2,
        compiler_params=params_of,
        cost_estimate=pl.CostEstimate(flops=10_000_000, bytes_accessed=8_000_000, transcendentals=0),
    )(partner, *field, factors, pulls)

    place = ("space", "sub")
    count = spaces * lax.axis_size("sub")
    shared = [sums] + [lax.ppermute(sums, place, [(i, (i + by) % count) for i in range(count)]) for by in range(1, count)]
    pieces = pl.pallas_call(
        functools.partial(return_kernel, tiles),
        out_shape=(jax.ShapeDtypeStruct((epochs * look_rows + 8, LANES), f32),) * tiles,
        in_specs=[VMEM] * (1 + count),
        out_specs=(VMEM,) * tiles,
        compiler_params=params_of,
        cost_estimate=pl.CostEstimate(flops=10_000, bytes_accessed=1_000_000, transcendentals=0),
    )(gradient, *shared)
    returned = [pieces[0]] + [to_ahead(pieces[by], "epoch", by) for by in range(1, tiles)]
    cell_count = float(total * look_rows * spaces * columns * lax.axis_size("sub"))
    return pl.pallas_call(
        functools.partial(update_kernel, cell_count),
        out_shape=(jax.ShapeDtypeStruct(estimate.shape, f32),) * 2,
        in_specs=[SMEM] * 2 + [VMEM] * (2 + tiles),
        out_specs=(VMEM, VMEM),
        compiler_params=params_of,
        cost_estimate=pl.CostEstimate(flops=1_000_000, bytes_accessed=2_000_000, transcendentals=0),
    )(me.reshape(1), prev_mean, estimate, direction, *returned)


def on_device(slc, offsets, weights, estimate, direction, prev_mean):
    epochs, rows, columns = slc.shape[1:]
    fits = columns == LANES * lax.axis_size("epoch") and lax.axis_size("epoch") % 2 == 0
    fits = fits and 2 * epochs * SIDES <= PARAM_LANE and rows % HALO == 0 and epochs == 2 * SLOTS
    plan = transposed_plan if fits else ring_plan
    return plan(slc, offsets, weights, estimate, direction, prev_mean)


def solution(mesh):
    return jax.shard_map(
        on_device,
        mesh=mesh,
        in_specs=(
            P(None, ("groups", "epoch"), "space", "sub"),
            P(("groups", "epoch"), None),
            P(("groups", "epoch"), None),
            P(("groups", "epoch"), "space", "sub"),
            P(("groups", "epoch"), "space", "sub"),
            P(),
        ),
        out_specs=(P(("groups", "epoch"), "space", "sub"), P(("groups", "epoch"), "space", "sub")),
        check_vma=False,
    )
```

```python
import functools

import jax
import jax.numpy as jnp
from jax import lax
from jax.experimental import pallas as pl
from jax.experimental.pallas import tpu as pltpu
from jax.sharding import PartitionSpec as P

SLOTS = 4
OFFS = 8
LOOK = 4
RADIUS = 3


EPSILON = 1e-06


def passed_along(x, axis, by):
    size = lax.axis_size(axis)
    return lax.ppermute(x, axis, [(i, (i + by) % size) for i in range(size)])


def extended_2(block, sides, width):
    for axis, dim in sides:
        count = lax.axis_size(axis)
        forward = [(i, i + 1) for i in range(count - 1)]
        backward = [(target, source) for source, target in forward]
        low = lax.ppermute(
            lax.slice_in_dim(block, block.shape[dim] - width, None, axis=dim), axis, forward
        )
        high = lax.ppermute(lax.slice_in_dim(block, 0, width, axis=dim), axis, backward)
        block = jnp.concatenate([low, block, high], axis=dim)
    return block


def looked_sum(field):
    shape = field.shape
    return jnp.sum(field.reshape(shape[:-2] + (shape[-2] // LOOK, LOOK, shape[-1])), axis=-2)


def window_sum(padded, axis):
    length = padded.shape[axis] - 2 * RADIUS
    total = lax.slice_in_dim(padded, 0, length, axis=axis)
    for shift_at in range(1, 2 * RADIUS + 1):
        total = total + lax.slice_in_dim(padded, shift_at, shift_at + length, axis=axis)
    return total


def ring_plan(slc, offsets, weights, estimate, direction, prev_mean):
    epochs_here = slc.shape[1]
    look_rows = slc.shape[2] // LOOK
    col_count = slc.shape[3]
    ahead = passed_along(slc, "epoch", -1)
    extended = jnp.concatenate([slc, ahead], axis=1)
    numbers = jnp.arange(epochs_here, dtype=jnp.int32)
    partner = numbers[:, None] + offsets
    own_real = slc[0].astype(jnp.float32)
    own_imag = slc[1].astype(jnp.float32)
    ext_real = extended[0].astype(jnp.float32)
    ext_imag = extended[1].astype(jnp.float32)
    powers = looked_sum(ext_real * ext_real + ext_imag * ext_imag)
    pieces = []
    for slot_index in range(SLOTS):
        mate_real = jnp.take(ext_real, partner[:, slot_index], axis=0)
        mate_imag = jnp.take(ext_imag, partner[:, slot_index], axis=0)
        pieces.append(looked_sum(own_real * mate_real + own_imag * mate_imag))
        pieces.append(looked_sum(own_imag * mate_real - own_real * mate_imag))
    pair_count = epochs_here * 2 * SLOTS
    stacked = jnp.concatenate(
        [jnp.stack(pieces, axis=1).reshape(pair_count, look_rows, col_count), powers], axis=0
    )
    padded = extended_2(stacked, (("space", 1), ("sub", 2)), RADIUS)
    boxed = window_sum(window_sum(padded, 1), 2)
    pair_boxed = boxed[:pair_count].reshape(epochs_here, 2 * SLOTS, look_rows, col_count)
    power_box = boxed[pair_count:]
    coh_real = pair_boxed[:, 0::2]
    coh_imag = pair_boxed[:, 1::2]
    denominator = power_box[:epochs_here, None] * jnp.take(power_box, partner, axis=0) + EPSILON
    coherence = (coh_real * coh_real + coh_imag * coh_imag) / denominator
    observed = coh_imag / jnp.sqrt(denominator)
    est_ahead = passed_along(estimate, "epoch", -1)
    est_extended = jnp.concatenate([estimate, est_ahead], axis=0)
    fitted = estimate[:, None] - jnp.take(est_extended, partner, axis=0)
    factor = weights[:, :, None, None] * coherence
    weighted = factor * (observed - fitted)
    flattened = weighted.reshape(epochs_here * SLOTS, look_rows * col_count)
    selector = (
        jnp.arange(epochs_here + OFFS, dtype=jnp.int32)[:, None] == partner.reshape(1, -1)
    ).astype(jnp.float32)
    gathered = jnp.dot(
        selector, flattened, precision=lax.Precision.HIGHEST, preferred_element_type=jnp.float32
    ).reshape(epochs_here + OFFS, look_rows, col_count)
    own_part = jnp.sum(weighted, axis=1) - gathered[:epochs_here]
    returned = passed_along(-gathered[epochs_here:], "epoch", 1)
    gradient = jnp.concatenate([own_part + returned, own_part[OFFS:]], axis=0)
    cell_count = float(
        epochs_here
        * lax.axis_size("epoch")
        * look_rows
        * lax.axis_size("space")
        * col_count
        * lax.axis_size("sub")
    )
    local_norm = jnp.sum(gradient * gradient)
    local_crossed = jnp.sum(gradient * direction)
    mean_before = prev_mean[0]
    fields_ahead = passed_along(
        jnp.stack([gradient, direction]).astype(jnp.bfloat16), "epoch", -1
    ).astype(jnp.float32)
    grad_extended = jnp.concatenate([gradient, fields_ahead[0]], axis=0)
    old_extended = jnp.concatenate([direction, fields_ahead[1]], axis=0)
    grad_spread = gradient[:, None] - jnp.take(grad_extended, partner, axis=0)
    old_spread = direction[:, None] - jnp.take(old_extended, partner, axis=0)
    totals = lax.psum(
        (
            local_norm,
            local_crossed,
            jnp.sum(factor * grad_spread * grad_spread),
            jnp.sum(factor * grad_spread * old_spread),
            jnp.sum(factor * old_spread * old_spread),
        ),
        ("epoch", "space", "sub"),
    )
    grad_norm, crossed, grad_term, mixed_term, old_term = totals
    momentum = grad_norm / cell_count / mean_before
    new_direction = gradient + momentum * direction
    curvature = grad_term + 2.0 * momentum * mixed_term + momentum * momentum * old_term
    along_sum = grad_norm + momentum * crossed
    step_size = along_sum / curvature
    return (estimate + step_size * new_direction, new_direction)


LANES = 128
SIDES = 2 * RADIUS
HALO = 16
PARAM_LANE = 96
VMEM = pl.BlockSpec(memory_space=pltpu.VMEM)
SMEM = pl.BlockSpec(memory_space=pltpu.SMEM)
VMEM_BYTES = 48 * 1024 * 1024


def split_two(value):
    high = value.astype(jnp.bfloat16)
    low = (value - high.astype(jnp.float32)).astype(jnp.bfloat16)
    return high, low


def edge_kernel(first, last, edge):
    epochs = first.shape[1]
    lane = lax.broadcasted_iota(jnp.int32, edge.shape, 1)
    total = jnp.zeros(edge.shape, jnp.float32)
    for part in range(2):
        for epoch in range(epochs):
            at = (part * epochs + epoch) * SIDES
            total = placed(lane, total, tile_of(last, part, epoch, 0), LANES - RADIUS, at)
            total = placed(lane, total, tile_of(first, part, epoch, 0), 0, at + RADIUS)
    edge[...] = total.astype(jnp.bfloat16)


def fields_kernel(me, estimate, direction, *fields):
    look_rows = estimate.shape[1]
    tiles = len(fields)
    for shift, out in enumerate(fields):
        tile = lax.rem(me[0] + shift, tiles)
        columns = pl.ds(pl.multiple_of(tile * LANES, LANES), LANES)
        for epoch in range(estimate.shape[0]):
            here = slice(epoch * look_rows, (epoch + 1) * look_rows)
            first, second = split_two(estimate[epoch, :, columns])
            out[0, here, :] = first
            out[1, here, :] = second
            out[2, here, :] = direction[epoch, :, columns].astype(jnp.bfloat16)


def tile_of(slc, part, epoch, tile):
    return slc[part, epoch, :, tile * LANES : (tile + 1) * LANES].astype(jnp.float32)


def placed(lane, total, source, start, target):
    moved = pltpu.roll(source, (target - start) % LANES, axis=1)
    return jnp.where((lane >= target) & (lane < target + RADIUS), moved, total)


def pack_kernel(me, present, slc, params, before, after, *refs):
    messages, strips = refs[:-1], refs[-1]
    tiles = len(messages)
    epochs = slc.shape[1]
    rows = slc.shape[2]
    lane = lax.broadcasted_iota(jnp.int32, (rows, LANES), 1)
    value = params[...]
    high = value.astype(jnp.bfloat16).astype(jnp.float32)
    middle = (value - high).astype(jnp.bfloat16).astype(jnp.float32)
    low = value - high - middle
    third = PARAM_LANE + 2 * SLOTS
    split = jnp.where(lane < third, high, jnp.where(lane < third + SLOTS, middle, low))
    split = jnp.where(lane >= PARAM_LANE, split, 0.0)
    inside = lane < 2 * epochs * SIDES
    for tile in range(tiles):
        total = split
        if tile == 0:
            edge = before[...].astype(jnp.float32) * present[0]
            total = jnp.where(inside & (lane % SIDES < RADIUS), edge, total)
        if tile == tiles - 1:
            edge = after[...].astype(jnp.float32) * present[1]
            total = jnp.where(inside & (lane % SIDES >= RADIUS), edge, total)
        for part in range(2):
            for epoch in range(epochs):
                at = (part * epochs + epoch) * SIDES
                if tile > 0:
                    total = placed(lane, total, tile_of(slc, part, epoch, tile - 1), LANES - RADIUS, at)
                if tile < tiles - 1:
                    total = placed(lane, total, tile_of(slc, part, epoch, tile + 1), 0, at + RADIUS)
        strips[tile] = total.astype(jnp.bfloat16)
    for tile in range(tiles):
        shift = lax.rem(tile - me[0] + tiles, tiles)
        for number, message in enumerate(messages):

            @pl.when(shift == number)
            def _():
                for part in range(2):
                    for epoch in range(epochs):
                        at = (part * epochs + epoch) * rows
                        message[at : at + rows, :] = slc[part, epoch, :, tile * LANES : (tile + 1) * LANES]
                message[2 * epochs * rows :, :] = strips[tile]


def look_order(from_rows, keep):
    looks = from_rows // LOOK
    to = lax.broadcasted_iota(jnp.int32, (from_rows, from_rows), 0)
    at = lax.broadcasted_iota(jnp.int32, (from_rows, from_rows), 1)
    order = (at == to % looks * LOOK + to // looks).astype(jnp.float32)
    return (order * keep(at)).astype(jnp.bfloat16)


def unpack_tiles(order, sources, main, first, columns_of):
    looks = order.shape[0] // LOOK
    for start in range(0, len(sources), 4):
        parts = jnp.concatenate([columns_of(source) for source in sources[start : start + 4]], axis=1)
        value = jnp.dot(order, parts, preferred_element_type=jnp.float32)
        for one in range(4):
            for look in range(LOOK):
                main[first[start + one], look] = value[look * looks : (look + 1) * looks, one * LANES : (one + 1) * LANES]


def unpack_rims(by_look, looks, rim, first):
    share = LANES // SLOTS
    lane = lax.broadcasted_iota(jnp.int32, (looks, LANES), 1)
    for at, place in enumerate(first):
        value = jnp.zeros((looks, LANES), jnp.float32)
        for look in range(LOOK):
            target = look * SIDES
            moved = pltpu.roll(by_look[look * looks : (look + 1) * looks], (target - at * SIDES) % LANES, axis=1)
            value = jnp.where((lane >= target) & (lane < target + SIDES), moved, value)
        spread = share
        while spread < LANES:
            value = value + pltpu.roll(value, spread, axis=1)
            spread = 2 * spread
        rim[place] = value


def band_of(shape, from_of, to_of):
    at = lax.broadcasted_iota(jnp.int32, shape, 0)
    to = lax.broadcasted_iota(jnp.int32, shape, 1)
    return (jnp.abs(from_of(at, to) - to_of(at, to)) <= RADIUS).astype(jnp.float32).astype(jnp.bfloat16)


def column_bands():
    share = LANES // SLOTS

    def rim_from(at, to):
        side = at % share % SIDES
        return jnp.where(side < RADIUS, side - RADIUS, LANES + side - RADIUS)

    def rim_to(at, to):
        column = (to - at % LANES // share * share + LANES) % LANES
        inside = (column < RADIUS) | (column >= LANES - RADIUS)
        inside = inside & (at % share < LOOK * SIDES)
        return jnp.where(inside, column, 4 * LANES)

    band = band_of((2 * LANES, LANES), lambda at, to: at % LANES, lambda at, to: to)
    return band, band_of((2 * LANES, LANES), rim_from, rim_to)


def row_sums(look_rows, looks, look_of):
    group = 2 * SLOTS
    out_at = lax.broadcasted_iota(jnp.int32, (group * look_rows, group * looks), 0)
    in_at = lax.broadcasted_iota(jnp.int32, (group * look_rows, group * looks), 1)
    near = jnp.abs(look_of(in_at % looks) - out_at % look_rows) <= RADIUS
    near = near & (in_at // looks == out_at // look_rows)
    return near.astype(jnp.float32).astype(jnp.bfloat16)


def mixed(values):
    lane = lax.broadcasted_iota(jnp.int32, values[0].shape, 1)
    result = values[-1]
    for slot in range(SLOTS - 1):
        result = jnp.where(lane // (LANES // SLOTS) == slot, values[slot], result)
    return result


def power_batches(blocks, epochs, looks, main, rim, looked, rim_looked):
    total = blocks * epochs
    group = 2 * SLOTS
    for block in range(blocks):
        for piece in range(0, looks, 8):
            rows_at = slice(piece, piece + 8)
            for half in range(2):
                squares = []
                for slot in range(SLOTS):
                    channel = half * SLOTS + slot
                    epoch = block * epochs + channel
                    value = None
                    for look in range(LOOK):
                        real = main[epoch, look, rows_at]
                        imag = main[total + epoch, look, rows_at]
                        one = real * real + imag * imag
                        value = one if value is None else value + one
                    at = (block * group + channel) * looks + piece
                    looked[at : at + 8, :] = value
                    real = rim[epoch, rows_at]
                    imag = rim[total + epoch, rows_at]
                    squares.append(real * real + imag * imag)
                at = (block * 2 + half) * looks + piece
                rim_looked[at : at + 8, :] = mixed(squares)


def pair_batch(epoch, mates, total, main, rim):
    own_re, own_im = main[epoch], main[total + epoch]
    reals, imags = [], []
    for mate in mates:
        mate_re, mate_im = main[mate], main[total + mate]
        real = own_re[0] * mate_re[0] + own_im[0] * mate_im[0]
        imag = own_im[0] * mate_re[0] - own_re[0] * mate_im[0]
        for look in range(1, LOOK):
            real = real + (own_re[look] * mate_re[look] + own_im[look] * mate_im[look])
            imag = imag + (own_im[look] * mate_re[look] - own_re[look] * mate_im[look])
        reals.append(real)
        imags.append(imag)
    own_re, own_im = rim[epoch], rim[total + epoch]
    mate_re = mixed([rim[mate] for mate in mates])
    mate_im = mixed([rim[total + mate] for mate in mates])
    rims = [own_re * mate_re + own_im * mate_im, own_im * mate_re - own_re * mate_im]
    return reals + imags, rims


def put(ref, block, values):
    rows = sum(value.shape[0] for value in values)
    ref[pl.ds(pl.multiple_of(block * rows, rows), rows), :] = jnp.concatenate(values, axis=0)


def columns_summed(couple, looks, bands, looked, rim_looked):
    group = 2 * SLOTS
    f32 = jnp.float32
    at = pl.ds(pl.multiple_of(couple * (2 * group * looks), 2 * group * looks), 2 * group * looks)
    halves = jnp.concatenate(split_two(looked[at, :]), axis=1)
    value = jnp.dot(halves, bands[0], preferred_element_type=f32)
    at = pl.ds(pl.multiple_of(couple * (4 * looks), 4 * looks), 4 * looks)
    halves = jnp.concatenate(split_two(rim_looked[at, :]), axis=1)
    outer = jnp.dot(halves, bands[1], preferred_element_type=f32)
    lane = lax.broadcasted_iota(jnp.int32, (looks, LANES), 1)
    outside = (lane < RADIUS) | (lane >= LANES - RADIUS)
    results = []
    for channel in range(2 * group):
        batch, half, slot = channel // group, channel % group // SLOTS, channel % SLOTS
        row = (batch * 2 + half) * looks
        part = outer[row : row + looks]
        if slot > 0:
            part = pltpu.roll(part, LANES - slot * (LANES // SLOTS), axis=1)
        row = channel * looks
        results.append(value[row : row + looks] + jnp.where(outside, part, 0.0))
    return results


def rows_summed(batch, looks, sum_rows, wide):
    rows = 2 * SLOTS * looks
    at = pl.ds(pl.multiple_of(batch * rows, rows), rows)
    halves = jnp.concatenate(split_two(wide[at, :]), axis=1)
    value = jnp.dot(sum_rows, halves, preferred_element_type=jnp.float32)
    return value[:, :LANES] + value[:, LANES:]


def pair_couple(couple, total, partner, main, rim):
    products, rims = [], []
    for one in range(2):
        epoch = couple * 2 + one
        mates = [partner[epoch * SLOTS + slot] for slot in range(SLOTS)]
        more, more_rims = pair_batch(epoch, mates, total, main, rim)
        products += more
        rims += more_rims
    return products, rims


def clipped(value, last):
    return jnp.minimum(jnp.maximum(value, 0), last)


def inner_kernel(sizes, partner, *refs):
    tiles, epochs, rows = sizes
    messages = refs[:tiles]
    boxed, main, rim, looked, rim_looked, wide = refs[tiles:]
    total = tiles * epochs
    look_rows = rows // LOOK
    order = look_order(rows, lambda at: 1.0)
    bands = column_bands()
    sum_rows = row_sums(look_rows, look_rows, lambda look: look)
    for block, message in enumerate(messages):
        first = [part * total + block * epochs + epoch for part in range(2) for epoch in range(epochs)]
        unpack_tiles(order, range(2 * epochs), main, first, lambda at: message[at * rows : (at + 1) * rows, :])
        by_look = jnp.dot(order, message[2 * epochs * rows :, :], preferred_element_type=jnp.float32)
        unpack_rims(by_look, look_rows, rim, first)
    power_batches(tiles, epochs, look_rows, main, rim, looked, rim_looked)
    last = (tiles + total) // 2 - 1

    @pl.loop(0, last + 2)
    def _(turn):
        summed = clipped(turn - 1, last)
        sums = [rows_summed(summed * 2 + one, look_rows, sum_rows, wide) for one in range(2)]
        couple = clipped(turn, last)
        columns = columns_summed(couple, look_rows, bands, looked, rim_looked)
        here = clipped(turn, total // 2 - 1)
        products, rims = pair_couple(here, total, partner, main, rim)
        put(boxed, summed, sums)
        put(wide, couple, columns)
        put(looked, tiles // 2 + here, products)
        put(rim_looked, tiles // 2 + here, rims)


def border_kernel(sizes, partner, weight, present, *refs):
    tiles, epochs, look_rows = sizes
    top, bottom, inner, factors, pulls, boxed, main, rim, looked, rim_looked, wide = refs
    total = tiles * epochs
    looks = 2 * HALO // LOOK
    halo_looks = HALO // LOOK
    tile_rows = (2 * epochs + 1) * HALO
    order = look_order(2 * HALO, lambda at: jnp.where(at < HALO, present[0], present[1]))
    bands = column_bands()
    sum_rows = row_sums(look_rows, looks, lambda at: jnp.where(at < halo_looks, at - halo_looks, at - halo_looks + look_rows))
    for block in range(tiles):

        def border_of(at):
            here = slice(block * tile_rows + at * HALO, block * tile_rows + (at + 1) * HALO)
            return jnp.concatenate([top[here, :], bottom[here, :]], axis=0)

        first = [part * total + block * epochs + epoch for part in range(2) for epoch in range(epochs)]
        unpack_tiles(order, range(2 * epochs), main, first, border_of)
        by_look = jnp.dot(order, border_of(2 * epochs), preferred_element_type=jnp.float32)
        unpack_rims(by_look, looks, rim, first)
    power_batches(tiles, epochs, looks, main, rim, looked, rim_looked)
    last = (tiles + total) // 2 - 1

    def boxed_of(channel):
        return boxed[pl.ds(pl.multiple_of(channel * look_rows, look_rows), look_rows), :]

    @pl.loop(0, last + 3)
    def _(turn):
        done = clipped(turn - 2 - tiles // 2, total // 2 - 1)
        results = []
        for one in range(2):
            epoch = done * 2 + one
            own_power = boxed_of(epoch)
            first = (tiles + epoch) * (2 * SLOTS * look_rows)
            parts = boxed[pl.ds(pl.multiple_of(first, 2 * SLOTS * look_rows), 2 * SLOTS * look_rows), :]
            parts = parts.reshape(2 * SLOTS, look_rows, LANES)
            for slot in range(SLOTS):
                pair = epoch * SLOTS + slot
                inverse = lax.rsqrt(own_power * boxed_of(partner[pair]) + EPSILON)
                unit_re = parts[slot] * inverse
                unit_im = parts[SLOTS + slot] * inverse
                factor = weight[pair] * (unit_re * unit_re + unit_im * unit_im)
                results.append((factor, factor * unit_im))
        summed = clipped(turn - 1, last)
        half = 2 * SLOTS * look_rows
        share = inner[pl.ds(pl.multiple_of(summed * 2 * half, 2 * half), 2 * half), :]
        sums = [share[one * half : (one + 1) * half] + rows_summed(summed * 2 + one, looks, sum_rows, wide) for one in range(2)]
        couple = clipped(turn, last)
        columns = columns_summed(couple, looks, bands, looked, rim_looked)
        here = clipped(turn, total // 2 - 1)
        products, rims = pair_couple(here, total, partner, main, rim)
        for ref, values in zip((factors, pulls), zip(*results)):
            ref[pl.ds(done * 2 * SLOTS, 2 * SLOTS)] = jnp.stack(values)
        put(boxed, summed, sums)
        put(wide, couple, columns)
        put(looked, tiles // 2 + here, products)
        put(rim_looked, tiles // 2 + here, rims)


def gradient_kernel(sizes, partner, *refs):
    tiles, epochs = sizes
    fields = refs[:tiles]
    factors, pulls, gradient, sums, est, old = refs[tiles:]
    look_rows = est.shape[1]
    total = tiles * epochs
    f32 = jnp.float32
    for block in range(tiles):

        @pl.loop(0, epochs, unroll=4)
        def _(epoch):
            here = pl.ds(pl.multiple_of(epoch * look_rows, look_rows), look_rows)
            est[block * epochs + epoch] = fields[block][0, here, :].astype(f32) + fields[block][1, here, :].astype(f32)
            old[block * epochs + epoch] = fields[block][2, here, :].astype(f32)
            gradient[block * epochs + epoch] = jnp.zeros((look_rows, LANES), f32)

    @pl.loop(0, total, unroll=2)
    def _(epoch):
        own_est = est[epoch]
        own = jnp.zeros((look_rows, LANES), f32)
        mates = [partner[epoch * SLOTS + slot] for slot in range(SLOTS)]
        values = []
        for slot, mate in enumerate(mates):
            pair = epoch * SLOTS + slot
            weighted = pulls[pair] - factors[pair] * (own_est - est[mate])
            own = own + weighted
            values.append(weighted)
        for mate, weighted in zip(mates, values):
            gradient[mate] = gradient[mate] - weighted
        gradient[epoch] = gradient[epoch] + own

    def totals(epoch, carry):
        norm, crossed, grad_term, mixed_term, old_term = carry
        own_grad = gradient[epoch]
        own_old = old[epoch]
        norm = norm + own_grad * own_grad
        crossed = crossed + own_grad * own_old
        for slot in range(SLOTS):
            mate = partner[epoch * SLOTS + slot]
            factor = factors[epoch * SLOTS + slot]
            grad_spread = own_grad - gradient[mate]
            old_spread = own_old - old[mate]
            pulled = factor * grad_spread
            grad_term = grad_term + pulled * grad_spread
            mixed_term = mixed_term + pulled * old_spread
            old_term = old_term + factor * old_spread * old_spread
        return norm, crossed, grad_term, mixed_term, old_term

    zero = jnp.zeros((look_rows, LANES), f32)
    results = lax.fori_loop(0, total, totals, (zero,) * 5, unroll=2)
    sums[...] = jnp.zeros(sums.shape, f32)
    for at, value in enumerate(results):
        sums[at : at + 1, :] = jnp.sum(value, axis=0, keepdims=True)


def return_kernel(tiles, gradient, *refs):
    pieces = refs[-tiles:]
    shared = refs[:-tiles]
    total = shared[0][...]
    for other in shared[1:]:
        total = total + other[...]
    epochs = gradient.shape[0] // len(pieces)
    look_rows = gradient.shape[1]
    for number, piece in enumerate(pieces):
        for epoch in range(epochs):
            piece[epoch * look_rows : (epoch + 1) * look_rows, :] = gradient[number * epochs + epoch]
        piece[epochs * look_rows :, :] = total


def update_kernel(cell_count, me, prev_mean, estimate, direction, *refs):
    new_estimate, new_direction = refs[-2:]
    pieces = refs[:-2]
    tiles = len(pieces)
    epochs = estimate.shape[0]
    look_rows = estimate.shape[1]
    total = pieces[0][epochs * look_rows :, :]
    for piece in pieces[1:]:
        total = total + piece[epochs * look_rows :, :]
    total = jnp.sum(total, axis=1, keepdims=True)
    grad_norm, crossed, grad_term, mixed, old_term = (total[at : at + 1, :] for at in range(5))
    momentum = grad_norm / cell_count / prev_mean[0]
    curvature = grad_term + 2.0 * momentum * mixed + momentum * momentum * old_term
    step = (grad_norm + momentum * crossed) / curvature
    momentum = jnp.broadcast_to(momentum, (look_rows, LANES))
    step = jnp.broadcast_to(step, (look_rows, LANES))
    for shift, piece in enumerate(pieces):
        tile = lax.rem(me[0] - shift + tiles, tiles)
        columns = pl.ds(pl.multiple_of(tile * LANES, LANES), LANES)
        for epoch in range(epochs):
            gradient = piece[epoch * look_rows : (epoch + 1) * look_rows, :]
            moved = gradient + momentum * direction[epoch, :, columns]
            new_direction[epoch, :, columns] = moved
            new_estimate[epoch, :, columns] = estimate[epoch, :, columns] + step * moved


def swapped(up, down, axis):
    size = lax.axis_size(axis)
    if size == 1:
        return jnp.zeros_like(up), jnp.zeros_like(down)
    if size == 2:
        first = lax.axis_index(axis) == 0
        got = lax.ppermute(jnp.where(first, up, down), axis, [(0, 1), (1, 0)])
        return got, got
    forward = [(i, i + 1) for i in range(size - 1)]
    backward = [(target, source) for source, target in forward]
    return lax.ppermute(up, axis, forward), lax.ppermute(down, axis, backward)


def to_ahead(x, axis, by):
    size = lax.axis_size(axis)
    return lax.ppermute(x, axis, [(i, (i + by) % size) for i in range(size)])


def transposed_plan(slc, offsets, weights, estimate, direction, prev_mean):
    f32 = jnp.float32
    bf16 = jnp.bfloat16
    tiles = lax.axis_size("epoch")
    me = lax.axis_index("epoch")
    epochs, rows, columns = slc.shape[1:]
    look_rows = rows // LOOK
    total = tiles * epochs
    tile_rows = 2 * epochs * rows
    params_of = pltpu.CompilerParams(vmem_limit_bytes=VMEM_BYTES)

    def fetched(messages, shift):
        return to_ahead(messages[tiles - shift], "epoch", tiles - shift)

    sub = lax.axis_index("sub")
    outer_tile = (2, epochs, rows, LANES)
    edge = pl.pallas_call(
        edge_kernel,
        out_shape=jax.ShapeDtypeStruct((rows, LANES), bf16),
        grid=(1,),
        in_specs=[
            pl.BlockSpec(outer_tile, lambda _: (0, 0, 0, 0)),
            pl.BlockSpec(outer_tile, lambda _: (0, 0, 0, tiles - 1)),
        ],
        out_specs=pl.BlockSpec((rows, LANES), lambda _: (0, 0)),
        compiler_params=params_of,
        cost_estimate=pl.CostEstimate(flops=1_000_000, bytes_accessed=1_000_000, transcendentals=0),
    )(slc, slc)
    before, after = swapped(edge, edge, "sub")
    params = jnp.zeros((rows, LANES), f32)
    listed = jnp.concatenate([offsets.astype(f32), weights, weights, weights], axis=1)
    params = lax.dynamic_update_slice(params, listed, (0, PARAM_LANE))
    sub_present = jnp.stack([sub > 0, sub < lax.axis_size("sub") - 1]).astype(f32)
    messages = pl.pallas_call(
        pack_kernel,
        out_shape=(jax.ShapeDtypeStruct((tile_rows + rows, LANES), bf16),) * tiles,
        in_specs=[SMEM] * 2 + [VMEM] * 4,
        out_specs=(VMEM,) * tiles,
        scratch_shapes=[pltpu.VMEM((tiles, rows, LANES), bf16)],
        compiler_params=params_of,
        cost_estimate=pl.CostEstimate(flops=3_000_000, bytes_accessed=4_000_000, transcendentals=0),
    )(me.reshape(1), sub_present, slc, params, before, after)
    block = [messages[0]] + [fetched(messages, shift) for shift in range(1, tiles)]

    estimate, direction, _ = lax.optimization_barrier((estimate, direction, messages))
    fields = pl.pallas_call(
        fields_kernel,
        out_shape=(jax.ShapeDtypeStruct((3, epochs * look_rows, LANES), bf16),) * tiles,
        in_specs=[SMEM] + [VMEM] * 2,
        out_specs=(VMEM,) * tiles,
        compiler_params=params_of,
        cost_estimate=pl.CostEstimate(flops=1_000_000, bytes_accessed=2_000_000, transcendentals=0),
    )(me.reshape(1), estimate, direction)
    late = lax.optimization_barrier((fields, block))[0]
    field = [fields[0]] + [fetched(late, shift) for shift in range(1, tiles)]

    space = lax.axis_index("space")
    spaces = lax.axis_size("space")
    present = jnp.stack([space > 0, space < spaces - 1]).astype(f32)

    def halo(pieces):
        def border(from_row):
            cuts = [lax.dynamic_slice_in_dim(piece, from_row, HALO, axis=1).reshape(-1, LANES) for piece in pieces]
            return jnp.concatenate(cuts, axis=0)

        if spaces == 2:
            got = lax.ppermute(border(jnp.where(space == 0, rows - HALO, 0)), "space", [(0, 1), (1, 0)])
            return got, got
        return swapped(border(rows - HALO), border(0), "space")

    def by_rows(shift):
        return block[shift].reshape(-1, rows, LANES)

    def params_in(shift):
        return block[shift][tile_rows : tile_rows + epochs, PARAM_LANE : PARAM_LANE + 4 * SLOTS].astype(f32)

    def pairs_of(blocks, loaded):
        listed = jnp.concatenate([params_in(block) for block in blocks], axis=0)
        mate = jnp.arange(len(blocks) * epochs, dtype=jnp.int32)[:, None] + listed[:, :SLOTS].astype(jnp.int32)
        weight = listed[:, SLOTS : 2 * SLOTS] + listed[:, 2 * SLOTS : 3 * SLOTS] + listed[:, 3 * SLOTS :]
        return mate.reshape(-1), weight.reshape(-1)

    top, bottom = halo([by_rows(shift) for shift in range(tiles)])
    listed = jnp.concatenate([params_in(shift) for shift in range(tiles)], axis=0)
    partner = jnp.arange(total, dtype=jnp.int32)[:, None] + listed[:, :SLOTS].astype(jnp.int32)
    partner = lax.rem(partner, total).reshape(-1)
    weight = listed[:, SLOTS : 2 * SLOTS] + listed[:, 2 * SLOTS : 3 * SLOTS] + listed[:, 3 * SLOTS :]
    weight = weight.reshape(-1)

    group = 2 * SLOTS
    batches = tiles + total

    def scratch(looks):
        return [
            pltpu.VMEM((2 * total, LOOK, looks, LANES), f32),
            pltpu.VMEM((2 * total, looks, LANES), f32),
            pltpu.VMEM((batches * group * looks, LANES), f32),
            pltpu.VMEM((batches * 2 * looks, LANES), f32),
            pltpu.VMEM((batches * group * looks, LANES), f32),
        ]

    boxed_shape = (batches * group * look_rows, LANES)
    inner = pl.pallas_call(
        functools.partial(inner_kernel, (tiles, epochs, rows)),
        out_shape=jax.ShapeDtypeStruct(boxed_shape, f32),
        in_specs=[SMEM] + [VMEM] * tiles,
        out_specs=VMEM,
        scratch_shapes=scratch(look_rows),
        compiler_params=params_of,
        cost_estimate=pl.CostEstimate(flops=20_000_000, bytes_accessed=20_000_000, transcendentals=0),
    )(partner, *block)
    pair_shape = jax.ShapeDtypeStruct((total * SLOTS, look_rows, LANES), f32)
    factors, pulls = pl.pallas_call(
        functools.partial(border_kernel, (tiles, epochs, look_rows)),
        out_shape=(pair_shape, pair_shape),
        in_specs=[SMEM] * 3 + [VMEM] * 3,
        out_specs=(VMEM, VMEM),
        scratch_shapes=[pltpu.VMEM(boxed_shape, f32)] + scratch(2 * HALO // LOOK),
        compiler_params=params_of,
        cost_estimate=pl.CostEstimate(flops=20_000_000, bytes_accessed=15_000_000, transcendentals=0),
    )(partner, weight, present, top, bottom, inner)
    gradient, sums = pl.pallas_call(
        functools.partial(gradient_kernel, (tiles, epochs)),
        out_shape=(
            jax.ShapeDtypeStruct((total, look_rows, LANES), f32),
            jax.ShapeDtypeStruct((8, LANES), f32),
        ),
        in_specs=[SMEM] + [VMEM] * (tiles + 2),
        out_specs=(VMEM, VMEM),
        scratch_shapes=[pltpu.VMEM((total, look_rows, LANES), f32)] * 2,
        compiler_params=params_of,
        cost_estimate=pl.CostEstimate(flops=10_000_000, bytes_accessed=8_000_000, transcendentals=0),
    )(partner, *field, factors, pulls)

    place = ("space", "sub")
    count = spaces * lax.axis_size("sub")
    shared = [sums] + [lax.ppermute(sums, place, [(i, (i + by) % count) for i in range(count)]) for by in range(1, count)]
    pieces = pl.pallas_call(
        functools.partial(return_kernel, tiles),
        out_shape=(jax.ShapeDtypeStruct((epochs * look_rows + 8, LANES), f32),) * tiles,
        in_specs=[VMEM] * (1 + count),
        out_specs=(VMEM,) * tiles,
        compiler_params=params_of,
        cost_estimate=pl.CostEstimate(flops=10_000, bytes_accessed=1_000_000, transcendentals=0),
    )(gradient, *shared)
    returned = [pieces[0]] + [to_ahead(pieces[by], "epoch", by) for by in range(1, tiles)]
    cell_count = float(total * look_rows * spaces * columns * lax.axis_size("sub"))
    return pl.pallas_call(
        functools.partial(update_kernel, cell_count),
        out_shape=(jax.ShapeDtypeStruct(estimate.shape, f32),) * 2,
        in_specs=[SMEM] * 2 + [VMEM] * (2 + tiles),
        out_specs=(VMEM, VMEM),
        compiler_params=params_of,
        cost_estimate=pl.CostEstimate(flops=1_000_000, bytes_accessed=2_000_000, transcendentals=0),
    )(me.reshape(1), prev_mean, estimate, direction, *returned)


def on_device(slc, offsets, weights, estimate, direction, prev_mean):
    epochs, rows, columns = slc.shape[1:]
    fits = columns == LANES * lax.axis_size("epoch") and lax.axis_size("epoch") % 2 == 0
    fits = fits and 2 * epochs * SIDES <= PARAM_LANE and rows % HALO == 0 and epochs == 2 * SLOTS
    plan = transposed_plan if fits else ring_plan
    return plan(slc, offsets, weights, estimate, direction, prev_mean)


def solution(mesh):
    return jax.shard_map(
        on_device,
        mesh=mesh,
        in_specs=(
            P(None, ("groups", "epoch"), "space", "sub"),
            P(("groups", "epoch"), None),
            P(("groups", "epoch"), None),
            P(("groups", "epoch"), "space", "sub"),
            P(("groups", "epoch"), "space", "sub"),
            P(),
        ),
        out_specs=(P(("groups", "epoch"), "space", "sub"), P(("groups", "epoch"), "space", "sub")),
        check_vma=False,
    )
```

```python
import functools

import jax
import jax.numpy as jnp
from jax import lax
from jax.experimental import pallas as pl
from jax.experimental.pallas import tpu as pltpu
from jax.sharding import PartitionSpec as P

SLOTS = 4
OFFS = 8
LOOK = 4
RADIUS = 3


EPSILON = 1e-06


def passed_along(x, axis, by):
    size = lax.axis_size(axis)
    return lax.ppermute(x, axis, [(i, (i + by) % size) for i in range(size)])


def extended_2(block, sides, width):
    for axis, dim in sides:
        count = lax.axis_size(axis)
        forward = [(i, i + 1) for i in range(count - 1)]
        backward = [(target, source) for source, target in forward]
        low = lax.ppermute(
            lax.slice_in_dim(block, block.shape[dim] - width, None, axis=dim), axis, forward
        )
        high = lax.ppermute(lax.slice_in_dim(block, 0, width, axis=dim), axis, backward)
        block = jnp.concatenate([low, block, high], axis=dim)
    return block


def looked_sum(field):
    shape = field.shape
    return jnp.sum(field.reshape(shape[:-2] + (shape[-2] // LOOK, LOOK, shape[-1])), axis=-2)


def window_sum(padded, axis):
    length = padded.shape[axis] - 2 * RADIUS
    total = lax.slice_in_dim(padded, 0, length, axis=axis)
    for shift_at in range(1, 2 * RADIUS + 1):
        total = total + lax.slice_in_dim(padded, shift_at, shift_at + length, axis=axis)
    return total


def ring_plan(slc, offsets, weights, estimate, direction, prev_mean):
    epochs_here = slc.shape[1]
    look_rows = slc.shape[2] // LOOK
    col_count = slc.shape[3]
    ahead = passed_along(slc, "epoch", -1)
    extended = jnp.concatenate([slc, ahead], axis=1)
    numbers = jnp.arange(epochs_here, dtype=jnp.int32)
    partner = numbers[:, None] + offsets
    own_real = slc[0].astype(jnp.float32)
    own_imag = slc[1].astype(jnp.float32)
    ext_real = extended[0].astype(jnp.float32)
    ext_imag = extended[1].astype(jnp.float32)
    powers = looked_sum(ext_real * ext_real + ext_imag * ext_imag)
    pieces = []
    for slot_index in range(SLOTS):
        mate_real = jnp.take(ext_real, partner[:, slot_index], axis=0)
        mate_imag = jnp.take(ext_imag, partner[:, slot_index], axis=0)
        pieces.append(looked_sum(own_real * mate_real + own_imag * mate_imag))
        pieces.append(looked_sum(own_imag * mate_real - own_real * mate_imag))
    pair_count = epochs_here * 2 * SLOTS
    stacked = jnp.concatenate(
        [jnp.stack(pieces, axis=1).reshape(pair_count, look_rows, col_count), powers], axis=0
    )
    padded = extended_2(stacked, (("space", 1), ("sub", 2)), RADIUS)
    boxed = window_sum(window_sum(padded, 1), 2)
    pair_boxed = boxed[:pair_count].reshape(epochs_here, 2 * SLOTS, look_rows, col_count)
    power_box = boxed[pair_count:]
    coh_real = pair_boxed[:, 0::2]
    coh_imag = pair_boxed[:, 1::2]
    denominator = power_box[:epochs_here, None] * jnp.take(power_box, partner, axis=0) + EPSILON
    coherence = (coh_real * coh_real + coh_imag * coh_imag) / denominator
    observed = coh_imag / jnp.sqrt(denominator)
    est_ahead = passed_along(estimate, "epoch", -1)
    est_extended = jnp.concatenate([estimate, est_ahead], axis=0)
    fitted = estimate[:, None] - jnp.take(est_extended, partner, axis=0)
    factor = weights[:, :, None, None] * coherence
    weighted = factor * (observed - fitted)
    flattened = weighted.reshape(epochs_here * SLOTS, look_rows * col_count)
    selector = (
        jnp.arange(epochs_here + OFFS, dtype=jnp.int32)[:, None] == partner.reshape(1, -1)
    ).astype(jnp.float32)
    gathered = jnp.dot(
        selector, flattened, precision=lax.Precision.HIGHEST, preferred_element_type=jnp.float32
    ).reshape(epochs_here + OFFS, look_rows, col_count)
    own_part = jnp.sum(weighted, axis=1) - gathered[:epochs_here]
    returned = passed_along(-gathered[epochs_here:], "epoch", 1)
    gradient = jnp.concatenate([own_part + returned, own_part[OFFS:]], axis=0)
    cell_count = float(
        epochs_here
        * lax.axis_size("epoch")
        * look_rows
        * lax.axis_size("space")
        * col_count
        * lax.axis_size("sub")
    )
    local_norm = jnp.sum(gradient * gradient)
    local_crossed = jnp.sum(gradient * direction)
    mean_before = prev_mean[0]
    fields_ahead = passed_along(
        jnp.stack([gradient, direction]).astype(jnp.bfloat16), "epoch", -1
    ).astype(jnp.float32)
    grad_extended = jnp.concatenate([gradient, fields_ahead[0]], axis=0)
    old_extended = jnp.concatenate([direction, fields_ahead[1]], axis=0)
    grad_spread = gradient[:, None] - jnp.take(grad_extended, partner, axis=0)
    old_spread = direction[:, None] - jnp.take(old_extended, partner, axis=0)
    totals = lax.psum(
        (
            local_norm,
            local_crossed,
            jnp.sum(factor * grad_spread * grad_spread),
            jnp.sum(factor * grad_spread * old_spread),
            jnp.sum(factor * old_spread * old_spread),
        ),
        ("epoch", "space", "sub"),
    )
    grad_norm, crossed, grad_term, mixed_term, old_term = totals
    momentum = grad_norm / cell_count / mean_before
    new_direction = gradient + momentum * direction
    curvature = grad_term + 2.0 * momentum * mixed_term + momentum * momentum * old_term
    along_sum = grad_norm + momentum * crossed
    step_size = along_sum / curvature
    return (estimate + step_size * new_direction, new_direction)


LANES = 128
SIDES = 2 * RADIUS
HALO = 16
PARAM_LANE = 96
VMEM = pl.BlockSpec(memory_space=pltpu.VMEM)
SMEM = pl.BlockSpec(memory_space=pltpu.SMEM)
VMEM_BYTES = 48 * 1024 * 1024


def split_two(value):
    high = value.astype(jnp.bfloat16)
    low = (value - high.astype(jnp.float32)).astype(jnp.bfloat16)
    return high, low


def edge_kernel(first, last, edge):
    epochs = first.shape[1]
    lane = lax.broadcasted_iota(jnp.int32, edge.shape, 1)
    total = jnp.zeros(edge.shape, jnp.float32)
    for part in range(2):
        for epoch in range(epochs):
            at = (part * epochs + epoch) * SIDES
            total = placed(lane, total, tile_of(last, part, epoch, 0), LANES - RADIUS, at)
            total = placed(lane, total, tile_of(first, part, epoch, 0), 0, at + RADIUS)
    edge[...] = total.astype(jnp.bfloat16)


def fields_kernel(me, estimate, direction, *fields):
    look_rows = estimate.shape[1]
    tiles = len(fields)
    for shift, out in enumerate(fields):
        tile = lax.rem(me[0] + shift, tiles)
        columns = pl.ds(pl.multiple_of(tile * LANES, LANES), LANES)
        for epoch in range(estimate.shape[0]):
            here = slice(epoch * look_rows, (epoch + 1) * look_rows)
            first, second = split_two(estimate[epoch, :, columns])
            out[0, here, :] = first
            out[1, here, :] = second
            out[2, here, :] = direction[epoch, :, columns].astype(jnp.bfloat16)


def tile_of(slc, part, epoch, tile):
    return slc[part, epoch, :, tile * LANES : (tile + 1) * LANES].astype(jnp.float32)


def placed(lane, total, source, start, target):
    moved = pltpu.roll(source, (target - start) % LANES, axis=1)
    return jnp.where((lane >= target) & (lane < target + RADIUS), moved, total)


def pack_kernel(me, present, slc, params, before, after, *refs):
    messages, strips = refs[:-1], refs[-1]
    tiles = len(messages)
    epochs = slc.shape[1]
    rows = slc.shape[2]
    lane = lax.broadcasted_iota(jnp.int32, (rows, LANES), 1)
    value = params[...]
    high = value.astype(jnp.bfloat16).astype(jnp.float32)
    middle = (value - high).astype(jnp.bfloat16).astype(jnp.float32)
    low = value - high - middle
    third = PARAM_LANE + 2 * SLOTS
    split = jnp.where(lane < third, high, jnp.where(lane < third + SLOTS, middle, low))
    split = jnp.where(lane >= PARAM_LANE, split, 0.0)
    inside = lane < 2 * epochs * SIDES
    for tile in range(tiles):
        total = split
        if tile == 0:
            edge = before[...].astype(jnp.float32) * present[0]
            total = jnp.where(inside & (lane % SIDES < RADIUS), edge, total)
        if tile == tiles - 1:
            edge = after[...].astype(jnp.float32) * present[1]
            total = jnp.where(inside & (lane % SIDES >= RADIUS), edge, total)
        for part in range(2):
            for epoch in range(epochs):
                at = (part * epochs + epoch) * SIDES
                if tile > 0:
                    total = placed(lane, total, tile_of(slc, part, epoch, tile - 1), LANES - RADIUS, at)
                if tile < tiles - 1:
                    total = placed(lane, total, tile_of(slc, part, epoch, tile + 1), 0, at + RADIUS)
        strips[tile] = total.astype(jnp.bfloat16)
    for tile in range(tiles):
        shift = lax.rem(tile - me[0] + tiles, tiles)
        for number, message in enumerate(messages):

            @pl.when(shift == number)
            def _():
                for part in range(2):
                    for epoch in range(epochs):
                        at = (part * epochs + epoch) * rows
                        message[at : at + rows, :] = slc[part, epoch, :, tile * LANES : (tile + 1) * LANES]
                message[2 * epochs * rows :, :] = strips[tile]


def look_order(from_rows, keep):
    looks = from_rows // LOOK
    to = lax.broadcasted_iota(jnp.int32, (from_rows, from_rows), 0)
    at = lax.broadcasted_iota(jnp.int32, (from_rows, from_rows), 1)
    order = (at == to % looks * LOOK + to // looks).astype(jnp.float32)
    return (order * keep(at)).astype(jnp.bfloat16)


def unpack_tiles(order, sources, main, first, columns_of):
    looks = order.shape[0] // LOOK
    for start in range(0, len(sources), 4):
        parts = jnp.concatenate([columns_of(source) for source in sources[start : start + 4]], axis=1)
        value = jnp.dot(order, parts, preferred_element_type=jnp.float32)
        for one in range(4):
            for look in range(LOOK):
                main[first[start + one], look] = value[look * looks : (look + 1) * looks, one * LANES : (one + 1) * LANES]


def unpack_rims(by_look, looks, rim, first):
    share = LANES // SLOTS
    lane = lax.broadcasted_iota(jnp.int32, (looks, LANES), 1)
    for at, place in enumerate(first):
        value = jnp.zeros((looks, LANES), jnp.float32)
        for look in range(LOOK):
            target = look * SIDES
            moved = pltpu.roll(by_look[look * looks : (look + 1) * looks], (target - at * SIDES) % LANES, axis=1)
            value = jnp.where((lane >= target) & (lane < target + SIDES), moved, value)
        spread = share
        while spread < LANES:
            value = value + pltpu.roll(value, spread, axis=1)
            spread = 2 * spread
        rim[place] = value


def band_of(shape, from_of, to_of):
    at = lax.broadcasted_iota(jnp.int32, shape, 0)
    to = lax.broadcasted_iota(jnp.int32, shape, 1)
    return (jnp.abs(from_of(at, to) - to_of(at, to)) <= RADIUS).astype(jnp.float32).astype(jnp.bfloat16)


def column_bands():
    share = LANES // SLOTS

    def rim_from(at, to):
        side = at % share % SIDES
        return jnp.where(side < RADIUS, side - RADIUS, LANES + side - RADIUS)

    def rim_to(at, to):
        column = (to - at % LANES // share * share + LANES) % LANES
        inside = (column < RADIUS) | (column >= LANES - RADIUS)
        inside = inside & (at % share < LOOK * SIDES)
        return jnp.where(inside, column, 4 * LANES)

    band = band_of((2 * LANES, LANES), lambda at, to: at % LANES, lambda at, to: to)
    return band, band_of((2 * LANES, LANES), rim_from, rim_to)


def row_sums(look_rows, looks, look_of):
    group = 2 * SLOTS
    out_at = lax.broadcasted_iota(jnp.int32, (group * look_rows, group * looks), 0)
    in_at = lax.broadcasted_iota(jnp.int32, (group * look_rows, group * looks), 1)
    near = jnp.abs(look_of(in_at % looks) - out_at % look_rows) <= RADIUS
    near = near & (in_at // looks == out_at // look_rows)
    return near.astype(jnp.float32).astype(jnp.bfloat16)


def mixed(values):
    lane = lax.broadcasted_iota(jnp.int32, values[0].shape, 1)
    result = values[-1]
    for slot in range(SLOTS - 1):
        result = jnp.where(lane // (LANES // SLOTS) == slot, values[slot], result)
    return result


def power_batches(blocks, epochs, looks, main, rim, looked, rim_looked):
    total = blocks * epochs
    group = 2 * SLOTS
    for block in range(blocks):
        for piece in range(0, looks, 8):
            rows_at = slice(piece, piece + 8)
            for half in range(2):
                squares = []
                for slot in range(SLOTS):
                    channel = half * SLOTS + slot
                    epoch = block * epochs + channel
                    value = None
                    for look in range(LOOK):
                        real = main[epoch, look, rows_at]
                        imag = main[total + epoch, look, rows_at]
                        one = real * real + imag * imag
                        value = one if value is None else value + one
                    at = (block * group + channel) * looks + piece
                    looked[at : at + 8, :] = value
                    real = rim[epoch, rows_at]
                    imag = rim[total + epoch, rows_at]
                    squares.append(real * real + imag * imag)
                at = (block * 2 + half) * looks + piece
                rim_looked[at : at + 8, :] = mixed(squares)


def pair_batch(epoch, mates, total, main, rim):
    own_re, own_im = main[epoch], main[total + epoch]
    reals, imags = [], []
    for mate in mates:
        mate_re, mate_im = main[mate], main[total + mate]
        real = own_re[0] * mate_re[0] + own_im[0] * mate_im[0]
        imag = own_im[0] * mate_re[0] - own_re[0] * mate_im[0]
        for look in range(1, LOOK):
            real = real + (own_re[look] * mate_re[look] + own_im[look] * mate_im[look])
            imag = imag + (own_im[look] * mate_re[look] - own_re[look] * mate_im[look])
        reals.append(real)
        imags.append(imag)
    own_re, own_im = rim[epoch], rim[total + epoch]
    mate_re = mixed([rim[mate] for mate in mates])
    mate_im = mixed([rim[total + mate] for mate in mates])
    rims = [own_re * mate_re + own_im * mate_im, own_im * mate_re - own_re * mate_im]
    return reals + imags, rims


def put(ref, block, values):
    rows = sum(value.shape[0] for value in values)
    ref[pl.ds(pl.multiple_of(block * rows, rows), rows), :] = jnp.concatenate(values, axis=0)


def columns_summed(couple, looks, bands, looked, rim_looked):
    group = 2 * SLOTS
    f32 = jnp.float32
    at = pl.ds(pl.multiple_of(couple * (2 * group * looks), 2 * group * looks), 2 * group * looks)
    halves = jnp.concatenate(split_two(looked[at, :]), axis=1)
    value = jnp.dot(halves, bands[0], preferred_element_type=f32)
    at = pl.ds(pl.multiple_of(couple * (4 * looks), 4 * looks), 4 * looks)
    halves = jnp.concatenate(split_two(rim_looked[at, :]), axis=1)
    outer = jnp.dot(halves, bands[1], preferred_element_type=f32)
    lane = lax.broadcasted_iota(jnp.int32, (looks, LANES), 1)
    outside = (lane < RADIUS) | (lane >= LANES - RADIUS)
    results = []
    for channel in range(2 * group):
        batch, half, slot = channel // group, channel % group // SLOTS, channel % SLOTS
        row = (batch * 2 + half) * looks
        part = outer[row : row + looks]
        if slot > 0:
            part = pltpu.roll(part, LANES - slot * (LANES // SLOTS), axis=1)
        row = channel * looks
        results.append(value[row : row + looks] + jnp.where(outside, part, 0.0))
    return results


def rows_summed(batch, looks, sum_rows, wide):
    rows = 2 * SLOTS * looks
    at = pl.ds(pl.multiple_of(batch * rows, rows), rows)
    halves = jnp.concatenate(split_two(wide[at, :]), axis=1)
    value = jnp.dot(sum_rows, halves, preferred_element_type=jnp.float32)
    return value[:, :LANES] + value[:, LANES:]


def pair_couple(couple, total, partner, main, rim):
    products, rims = [], []
    for one in range(2):
        epoch = couple * 2 + one
        mates = [partner[epoch * SLOTS + slot] for slot in range(SLOTS)]
        more, more_rims = pair_batch(epoch, mates, total, main, rim)
        products += more
        rims += more_rims
    return products, rims


def clipped(value, last):
    return jnp.minimum(jnp.maximum(value, 0), last)


def pair_kernel(sizes, places, partner, weight, present, *refs):
    epochs, rows, operands = sizes
    inputs = refs[:operands]
    factors, pulls, boxed, main, rim, looked, rim_looked, wide = refs[operands:]
    count = len(places)
    total = count * epochs
    own_total = total - epochs
    look_rows = rows // LOOK
    halo_looks = HALO // LOOK
    looks = look_rows + 2 * halo_looks
    full_rows = rows + 2 * HALO
    group = 2 * SLOTS

    def keep(at):
        return jnp.where(at < HALO, present[0], jnp.where(at >= HALO + rows, present[1], 1.0))

    order = look_order(full_rows, keep)
    bands = column_bands()
    sum_rows = row_sums(look_rows, looks, lambda at: at - halo_looks)
    for block, (tile_at, top_at, bottom_at, halo_row) in enumerate(places):
        tile, top, bottom = inputs[tile_at], inputs[top_at], inputs[bottom_at]

        def rows_of(at):
            border = slice(halo_row + at * HALO, halo_row + (at + 1) * HALO)
            return jnp.concatenate([top[border, :], tile[at * rows : (at + 1) * rows, :], bottom[border, :]], axis=0)

        first = [part * total + block * epochs + epoch for part in range(2) for epoch in range(epochs)]
        unpack_tiles(order, range(2 * epochs), main, first, rows_of)
        by_look = jnp.dot(order, rows_of(2 * epochs), preferred_element_type=jnp.float32)
        unpack_rims(by_look, looks, rim, first)
    power_batches(count, epochs, looks, main, rim, looked, rim_looked)
    powers = (count + 1) // 2
    last = powers + own_total // 2 - 1

    def boxed_of(channel):
        return boxed[pl.ds(pl.multiple_of(channel * look_rows, look_rows), look_rows), :]

    @pl.loop(0, last + 3)
    def _(turn):
        done = clipped(turn - 2 - powers, own_total // 2 - 1)
        results = []
        for one in range(2):
            epoch = done * 2 + one
            own_power = boxed_of(epoch)
            first = (2 * powers + epoch) * (group * look_rows)
            parts = boxed[pl.ds(pl.multiple_of(first, group * look_rows), group * look_rows), :]
            parts = parts.reshape(group, look_rows, LANES)
            for slot in range(SLOTS):
                pair = epoch * SLOTS + slot
                inverse = lax.rsqrt(own_power * boxed_of(partner[pair]) + EPSILON)
                unit_re = parts[slot] * inverse
                unit_im = parts[SLOTS + slot] * inverse
                factor = weight[pair] * (unit_re * unit_re + unit_im * unit_im)
                results.append((factor, factor * unit_im))
        summed = clipped(turn - 1, last)
        sums = [rows_summed(summed * 2 + one, looks, sum_rows, wide) for one in range(2)]
        couple = clipped(turn, last)
        columns = columns_summed(couple, looks, bands, looked, rim_looked)
        here = clipped(turn, own_total // 2 - 1)
        products, rims = pair_couple(here, total, partner, main, rim)
        for ref, values in zip((factors, pulls), zip(*results)):
            ref[pl.ds(done * 2 * SLOTS, 2 * SLOTS)] = jnp.stack(values)
        put(boxed, summed, sums)
        put(wide, couple, columns)
        put(looked, powers + here, products)
        put(rim_looked, powers + here, rims)


def gradient_kernel(sizes, partner, *refs):
    tiles, epochs, stages = sizes
    fields = refs[:tiles]
    factors = refs[tiles : tiles + len(stages)]
    pulls = refs[tiles + len(stages) : tiles + 2 * len(stages)]
    gradient, sums, est, old = refs[tiles + 2 * len(stages) :]
    look_rows = est.shape[1]
    total = tiles * epochs
    f32 = jnp.float32
    for block in range(tiles):

        @pl.loop(0, epochs, unroll=4)
        def _(epoch):
            here = pl.ds(pl.multiple_of(epoch * look_rows, look_rows), look_rows)
            est[block * epochs + epoch] = fields[block][0, here, :].astype(f32) + fields[block][1, here, :].astype(f32)
            old[block * epochs + epoch] = fields[block][2, here, :].astype(f32)
            gradient[block * epochs + epoch] = jnp.zeros((look_rows, LANES), f32)

    for stage, (first, own_total) in enumerate(stages):

        @pl.loop(0, own_total, unroll=2)
        def _(here):
            epoch = lax.rem(first + here, total)
            own_est = est[epoch]
            own = jnp.zeros((look_rows, LANES), f32)
            mates = [partner[epoch * SLOTS + slot] for slot in range(SLOTS)]
            values = []
            for slot, mate in enumerate(mates):
                pair = here * SLOTS + slot
                weighted = pulls[stage][pair] - factors[stage][pair] * (own_est - est[mate])
                own = own + weighted
                values.append(weighted)
            for mate, weighted in zip(mates, values):
                gradient[mate] = gradient[mate] - weighted
            gradient[epoch] = gradient[epoch] + own

    zero = jnp.zeros((look_rows, LANES), f32)
    results = (zero,) * 5
    for stage, (first, own_total) in enumerate(stages):

        def totals(here, carry):
            norm, crossed, grad_term, mixed_term, old_term = carry
            epoch = lax.rem(first + here, total)
            own_grad = gradient[epoch]
            own_old = old[epoch]
            norm = norm + own_grad * own_grad
            crossed = crossed + own_grad * own_old
            for slot in range(SLOTS):
                mate = partner[epoch * SLOTS + slot]
                factor = factors[stage][here * SLOTS + slot]
                grad_spread = own_grad - gradient[mate]
                old_spread = own_old - old[mate]
                pulled = factor * grad_spread
                grad_term = grad_term + pulled * grad_spread
                mixed_term = mixed_term + pulled * old_spread
                old_term = old_term + factor * old_spread * old_spread
            return norm, crossed, grad_term, mixed_term, old_term

        results = lax.fori_loop(0, own_total, totals, results, unroll=2)
    sums[...] = jnp.zeros(sums.shape, f32)
    for at, value in enumerate(results):
        sums[at : at + 1, :] = jnp.sum(value, axis=0, keepdims=True)


def return_kernel(tiles, gradient, *refs):
    pieces = refs[-tiles:]
    shared = refs[:-tiles]
    total = shared[0][...]
    for other in shared[1:]:
        total = total + other[...]
    epochs = gradient.shape[0] // len(pieces)
    look_rows = gradient.shape[1]
    for number, piece in enumerate(pieces):
        for epoch in range(epochs):
            piece[epoch * look_rows : (epoch + 1) * look_rows, :] = gradient[number * epochs + epoch]
        piece[epochs * look_rows :, :] = total


def update_kernel(cell_count, me, prev_mean, estimate, direction, *refs):
    new_estimate, new_direction = refs[-2:]
    pieces = refs[:-2]
    tiles = len(pieces)
    epochs = estimate.shape[0]
    look_rows = estimate.shape[1]
    total = pieces[0][epochs * look_rows :, :]
    for piece in pieces[1:]:
        total = total + piece[epochs * look_rows :, :]
    total = jnp.sum(total, axis=1, keepdims=True)
    grad_norm, crossed, grad_term, mixed, old_term = (total[at : at + 1, :] for at in range(5))
    momentum = grad_norm / cell_count / prev_mean[0]
    curvature = grad_term + 2.0 * momentum * mixed + momentum * momentum * old_term
    step = (grad_norm + momentum * crossed) / curvature
    momentum = jnp.broadcast_to(momentum, (look_rows, LANES))
    step = jnp.broadcast_to(step, (look_rows, LANES))
    for shift, piece in enumerate(pieces):
        tile = lax.rem(me[0] - shift + tiles, tiles)
        columns = pl.ds(pl.multiple_of(tile * LANES, LANES), LANES)
        for epoch in range(epochs):
            gradient = piece[epoch * look_rows : (epoch + 1) * look_rows, :]
            moved = gradient + momentum * direction[epoch, :, columns]
            new_direction[epoch, :, columns] = moved
            new_estimate[epoch, :, columns] = estimate[epoch, :, columns] + step * moved


def swapped(up, down, axis):
    size = lax.axis_size(axis)
    if size == 1:
        return jnp.zeros_like(up), jnp.zeros_like(down)
    if size == 2:
        first = lax.axis_index(axis) == 0
        got = lax.ppermute(jnp.where(first, up, down), axis, [(0, 1), (1, 0)])
        return got, got
    forward = [(i, i + 1) for i in range(size - 1)]
    backward = [(target, source) for source, target in forward]
    return lax.ppermute(up, axis, forward), lax.ppermute(down, axis, backward)


def to_ahead(x, axis, by):
    size = lax.axis_size(axis)
    return lax.ppermute(x, axis, [(i, (i + by) % size) for i in range(size)])


def transposed_plan(slc, offsets, weights, estimate, direction, prev_mean):
    f32 = jnp.float32
    bf16 = jnp.bfloat16
    tiles = lax.axis_size("epoch")
    me = lax.axis_index("epoch")
    epochs, rows, columns = slc.shape[1:]
    look_rows = rows // LOOK
    total = tiles * epochs
    tile_rows = 2 * epochs * rows
    params_of = pltpu.CompilerParams(vmem_limit_bytes=VMEM_BYTES)

    def fetched(messages, shift):
        return to_ahead(messages[tiles - shift], "epoch", tiles - shift)

    sub = lax.axis_index("sub")
    outer_tile = (2, epochs, rows, LANES)
    edge = pl.pallas_call(
        edge_kernel,
        out_shape=jax.ShapeDtypeStruct((rows, LANES), bf16),
        grid=(1,),
        in_specs=[
            pl.BlockSpec(outer_tile, lambda _: (0, 0, 0, 0)),
            pl.BlockSpec(outer_tile, lambda _: (0, 0, 0, tiles - 1)),
        ],
        out_specs=pl.BlockSpec((rows, LANES), lambda _: (0, 0)),
        compiler_params=params_of,
        cost_estimate=pl.CostEstimate(flops=1_000_000, bytes_accessed=1_000_000, transcendentals=0),
    )(slc, slc)
    before, after = swapped(edge, edge, "sub")
    params = jnp.zeros((rows, LANES), f32)
    listed = jnp.concatenate([offsets.astype(f32), weights, weights, weights], axis=1)
    params = lax.dynamic_update_slice(params, listed, (0, PARAM_LANE))
    sub_present = jnp.stack([sub > 0, sub < lax.axis_size("sub") - 1]).astype(f32)
    messages = pl.pallas_call(
        pack_kernel,
        out_shape=(jax.ShapeDtypeStruct((tile_rows + rows, LANES), bf16),) * tiles,
        in_specs=[SMEM] * 2 + [VMEM] * 4,
        out_specs=(VMEM,) * tiles,
        scratch_shapes=[pltpu.VMEM((tiles, rows, LANES), bf16)],
        compiler_params=params_of,
        cost_estimate=pl.CostEstimate(flops=3_000_000, bytes_accessed=4_000_000, transcendentals=0),
    )(me.reshape(1), sub_present, slc, params, before, after)
    beside = [tiles - 1, 0, 1]
    far = list(range(2, tiles - 1))
    block = {0: messages[0], 1: fetched(messages, 1), tiles - 1: fetched(messages, tiles - 1)}
    held = lax.optimization_barrier((messages, block[1], block[tiles - 1]))[0]
    block.update({shift: fetched(held, shift) for shift in far})

    estimate, direction, _ = lax.optimization_barrier((estimate, direction, messages))
    fields = pl.pallas_call(
        fields_kernel,
        out_shape=(jax.ShapeDtypeStruct((3, epochs * look_rows, LANES), bf16),) * tiles,
        in_specs=[SMEM] + [VMEM] * 2,
        out_specs=(VMEM,) * tiles,
        compiler_params=params_of,
        cost_estimate=pl.CostEstimate(flops=1_000_000, bytes_accessed=2_000_000, transcendentals=0),
    )(me.reshape(1), estimate, direction)
    space = lax.axis_index("space")
    spaces = lax.axis_size("space")
    present = jnp.stack([space > 0, space < spaces - 1]).astype(f32)

    def halo(pieces):
        def border(from_row):
            cuts = [lax.dynamic_slice_in_dim(piece, from_row, HALO, axis=1).reshape(-1, LANES) for piece in pieces]
            return jnp.concatenate(cuts, axis=0)

        if spaces == 2:
            got = lax.ppermute(border(jnp.where(space == 0, rows - HALO, 0)), "space", [(0, 1), (1, 0)])
            return got, got
        return swapped(border(rows - HALO), border(0), "space")

    def by_rows(shift):
        return block[shift].reshape(-1, rows, LANES)

    def params_in(shift):
        return block[shift][tile_rows : tile_rows + epochs, PARAM_LANE : PARAM_LANE + 4 * SLOTS].astype(f32)

    def pairs_of(blocks, loaded):
        listed = jnp.concatenate([params_in(block) for block in blocks], axis=0)
        mate = jnp.arange(len(blocks) * epochs, dtype=jnp.int32)[:, None] + listed[:, :SLOTS].astype(jnp.int32)
        weight = listed[:, SLOTS : 2 * SLOTS] + listed[:, 2 * SLOTS : 3 * SLOTS] + listed[:, 3 * SLOTS :]
        return mate.reshape(-1), weight.reshape(-1)

    own_halo = halo([by_rows(0)])
    near_halo = halo([by_rows(1), by_rows(tiles - 1)])
    halos = {0: (own_halo, 0), 1: (near_halo, 0), tiles - 1: (near_halo, 1)}

    def pair_stage(loaded):
        own = loaded[:-1]
        listed = jnp.concatenate([params_in(shift) for shift in own], axis=0)
        mate = jnp.arange(len(own) * epochs, dtype=jnp.int32)[:, None] + listed[:, :SLOTS].astype(jnp.int32)
        weight = listed[:, SLOTS : 2 * SLOTS] + listed[:, 2 * SLOTS : 3 * SLOTS] + listed[:, 3 * SLOTS :]
        operands = []

        def index_of(array):
            for at, other in enumerate(operands):
                if other is array:
                    return at
            operands.append(array)
            return len(operands) - 1

        places = []
        for shift in loaded:
            (top, bottom), slot = halos[shift]
            place = index_of(block[shift]), index_of(top), index_of(bottom), slot * (2 * epochs + 1) * HALO
            places.append(place)
        here = len(loaded) * epochs
        owned = len(own) * epochs
        looks = (rows + 2 * HALO) // LOOK
        group = 2 * SLOTS
        batches = (len(loaded) + 1) // 2 * 2 + owned
        shape = jax.ShapeDtypeStruct((owned * SLOTS, look_rows, LANES), f32)
        return pl.pallas_call(
            functools.partial(pair_kernel, (epochs, rows, len(operands)), tuple(places)),
            out_shape=(shape, shape),
            in_specs=[SMEM] * 3 + [VMEM] * len(operands),
            out_specs=(VMEM, VMEM),
            scratch_shapes=[
                pltpu.VMEM((batches * group * look_rows, LANES), f32),
                pltpu.VMEM((2 * here, LOOK, looks, LANES), f32),
                pltpu.VMEM((2 * here, looks, LANES), f32),
                pltpu.VMEM((batches * group * looks, LANES), f32),
                pltpu.VMEM((batches * 2 * looks, LANES), f32),
                pltpu.VMEM((batches * group * looks, LANES), f32),
            ],
            compiler_params=params_of,
            cost_estimate=pl.CostEstimate(flops=20_000_000, bytes_accessed=30_000_000, transcendentals=0),
        )(mate.reshape(-1), weight.reshape(-1), present, *operands)

    near_stage = beside
    far_stage = list(range(1, tiles))
    near_pairs = pair_stage(near_stage)
    held, fields, near_pairs = lax.optimization_barrier(([block[shift] for shift in far], fields, near_pairs))
    block.update(zip(far, held))
    far_halo = halo([by_rows(shift) for shift in far])
    halos.update({shift: (far_halo, at) for at, shift in enumerate(far)})
    field = [fields[0]] + [fetched(fields, shift) for shift in range(1, tiles)]
    far_pairs = pair_stage(far_stage)

    listed = jnp.concatenate([params_in(shift) for shift in range(tiles)], axis=0)
    partner = jnp.arange(total, dtype=jnp.int32)[:, None] + listed[:, :SLOTS].astype(jnp.int32)
    partner = lax.rem(partner, total).reshape(-1)
    stages = tuple((stage[0] * epochs, (len(stage) - 1) * epochs) for stage in (near_stage, far_stage))
    gradient, sums = pl.pallas_call(
        functools.partial(gradient_kernel, (tiles, epochs, stages)),
        out_shape=(
            jax.ShapeDtypeStruct((total, look_rows, LANES), f32),
            jax.ShapeDtypeStruct((8, LANES), f32),
        ),
        in_specs=[SMEM] + [VMEM] * (tiles + 4),
        out_specs=(VMEM, VMEM),
        scratch_shapes=[pltpu.VMEM((total, look_rows, LANES), f32)] * 2,
        compiler_params=params_of,
        cost_estimate=pl.CostEstimate(flops=10_000_000, bytes_accessed=8_000_000, transcendentals=0),
    )(partner, *field, near_pairs[0], far_pairs[0], near_pairs[1], far_pairs[1])

    place = ("space", "sub")
    count = spaces * lax.axis_size("sub")
    shared = [sums] + [lax.ppermute(sums, place, [(i, (i + by) % count) for i in range(count)]) for by in range(1, count)]
    pieces = pl.pallas_call(
        functools.partial(return_kernel, tiles),
        out_shape=(jax.ShapeDtypeStruct((epochs * look_rows + 8, LANES), f32),) * tiles,
        in_specs=[VMEM] * (1 + count),
        out_specs=(VMEM,) * tiles,
        compiler_params=params_of,
        cost_estimate=pl.CostEstimate(flops=10_000, bytes_accessed=1_000_000, transcendentals=0),
    )(gradient, *shared)
    returned = [pieces[0]] + [to_ahead(pieces[by], "epoch", by) for by in range(1, tiles)]
    cell_count = float(total * look_rows * spaces * columns * lax.axis_size("sub"))
    return pl.pallas_call(
        functools.partial(update_kernel, cell_count),
        out_shape=(jax.ShapeDtypeStruct(estimate.shape, f32),) * 2,
        in_specs=[SMEM] * 2 + [VMEM] * (2 + tiles),
        out_specs=(VMEM, VMEM),
        compiler_params=params_of,
        cost_estimate=pl.CostEstimate(flops=1_000_000, bytes_accessed=2_000_000, transcendentals=0),
    )(me.reshape(1), prev_mean, estimate, direction, *returned)


def on_device(slc, offsets, weights, estimate, direction, prev_mean):
    epochs, rows, columns = slc.shape[1:]
    fits = columns == LANES * lax.axis_size("epoch") and lax.axis_size("epoch") > 3
    fits = fits and 2 * epochs * SIDES <= PARAM_LANE and rows % HALO == 0 and epochs == 2 * SLOTS
    plan = transposed_plan if fits else ring_plan
    return plan(slc, offsets, weights, estimate, direction, prev_mean)


def solution(mesh):
    return jax.shard_map(
        on_device,
        mesh=mesh,
        in_specs=(
            P(None, ("groups", "epoch"), "space", "sub"),
            P(("groups", "epoch"), None),
            P(("groups", "epoch"), None),
            P(("groups", "epoch"), "space", "sub"),
            P(("groups", "epoch"), "space", "sub"),
            P(),
        ),
        out_specs=(P(("groups", "epoch"), "space", "sub"), P(("groups", "epoch"), "space", "sub")),
        check_vma=False,
    )
```

```python
import functools

import jax
import jax.numpy as jnp
from jax import lax
from jax.experimental import pallas as pl
from jax.experimental.pallas import tpu as pltpu
from jax.sharding import PartitionSpec as P

SLOTS = 4
OFFS = 8
LOOK = 4
RADIUS = 3


EPSILON = 1e-06


def passed_along(x, axis, by):
    size = lax.axis_size(axis)
    return lax.ppermute(x, axis, [(i, (i + by) % size) for i in range(size)])


def extended_2(block, sides, width):
    for axis, dim in sides:
        count = lax.axis_size(axis)
        forward = [(i, i + 1) for i in range(count - 1)]
        backward = [(target, source) for source, target in forward]
        low = lax.ppermute(
            lax.slice_in_dim(block, block.shape[dim] - width, None, axis=dim), axis, forward
        )
        high = lax.ppermute(lax.slice_in_dim(block, 0, width, axis=dim), axis, backward)
        block = jnp.concatenate([low, block, high], axis=dim)
    return block


def looked_sum(field):
    shape = field.shape
    return jnp.sum(field.reshape(shape[:-2] + (shape[-2] // LOOK, LOOK, shape[-1])), axis=-2)


def window_sum(padded, axis):
    length = padded.shape[axis] - 2 * RADIUS
    total = lax.slice_in_dim(padded, 0, length, axis=axis)
    for shift_at in range(1, 2 * RADIUS + 1):
        total = total + lax.slice_in_dim(padded, shift_at, shift_at + length, axis=axis)
    return total


def ring_plan(slc, offsets, weights, estimate, direction, prev_mean):
    epochs_here = slc.shape[1]
    look_rows = slc.shape[2] // LOOK
    col_count = slc.shape[3]
    ahead = passed_along(slc, "epoch", -1)
    extended = jnp.concatenate([slc, ahead], axis=1)
    numbers = jnp.arange(epochs_here, dtype=jnp.int32)
    partner = numbers[:, None] + offsets
    own_real = slc[0].astype(jnp.float32)
    own_imag = slc[1].astype(jnp.float32)
    ext_real = extended[0].astype(jnp.float32)
    ext_imag = extended[1].astype(jnp.float32)
    powers = looked_sum(ext_real * ext_real + ext_imag * ext_imag)
    pieces = []
    for slot_index in range(SLOTS):
        mate_real = jnp.take(ext_real, partner[:, slot_index], axis=0)
        mate_imag = jnp.take(ext_imag, partner[:, slot_index], axis=0)
        pieces.append(looked_sum(own_real * mate_real + own_imag * mate_imag))
        pieces.append(looked_sum(own_imag * mate_real - own_real * mate_imag))
    pair_count = epochs_here * 2 * SLOTS
    stacked = jnp.concatenate(
        [jnp.stack(pieces, axis=1).reshape(pair_count, look_rows, col_count), powers], axis=0
    )
    padded = extended_2(stacked, (("space", 1), ("sub", 2)), RADIUS)
    boxed = window_sum(window_sum(padded, 1), 2)
    pair_boxed = boxed[:pair_count].reshape(epochs_here, 2 * SLOTS, look_rows, col_count)
    power_box = boxed[pair_count:]
    coh_real = pair_boxed[:, 0::2]
    coh_imag = pair_boxed[:, 1::2]
    denominator = power_box[:epochs_here, None] * jnp.take(power_box, partner, axis=0) + EPSILON
    coherence = (coh_real * coh_real + coh_imag * coh_imag) / denominator
    observed = coh_imag / jnp.sqrt(denominator)
    est_ahead = passed_along(estimate, "epoch", -1)
    est_extended = jnp.concatenate([estimate, est_ahead], axis=0)
    fitted = estimate[:, None] - jnp.take(est_extended, partner, axis=0)
    factor = weights[:, :, None, None] * coherence
    weighted = factor * (observed - fitted)
    flattened = weighted.reshape(epochs_here * SLOTS, look_rows * col_count)
    selector = (
        jnp.arange(epochs_here + OFFS, dtype=jnp.int32)[:, None] == partner.reshape(1, -1)
    ).astype(jnp.float32)
    gathered = jnp.dot(
        selector, flattened, precision=lax.Precision.HIGHEST, preferred_element_type=jnp.float32
    ).reshape(epochs_here + OFFS, look_rows, col_count)
    own_part = jnp.sum(weighted, axis=1) - gathered[:epochs_here]
    returned = passed_along(-gathered[epochs_here:], "epoch", 1)
    gradient = jnp.concatenate([own_part + returned, own_part[OFFS:]], axis=0)
    cell_count = float(
        epochs_here
        * lax.axis_size("epoch")
        * look_rows
        * lax.axis_size("space")
        * col_count
        * lax.axis_size("sub")
    )
    local_norm = jnp.sum(gradient * gradient)
    local_crossed = jnp.sum(gradient * direction)
    mean_before = prev_mean[0]
    fields_ahead = passed_along(
        jnp.stack([gradient, direction]).astype(jnp.bfloat16), "epoch", -1
    ).astype(jnp.float32)
    grad_extended = jnp.concatenate([gradient, fields_ahead[0]], axis=0)
    old_extended = jnp.concatenate([direction, fields_ahead[1]], axis=0)
    grad_spread = gradient[:, None] - jnp.take(grad_extended, partner, axis=0)
    old_spread = direction[:, None] - jnp.take(old_extended, partner, axis=0)
    totals = lax.psum(
        (
            local_norm,
            local_crossed,
            jnp.sum(factor * grad_spread * grad_spread),
            jnp.sum(factor * grad_spread * old_spread),
            jnp.sum(factor * old_spread * old_spread),
        ),
        ("epoch", "space", "sub"),
    )
    grad_norm, crossed, grad_term, mixed_term, old_term = totals
    momentum = grad_norm / cell_count / mean_before
    new_direction = gradient + momentum * direction
    curvature = grad_term + 2.0 * momentum * mixed_term + momentum * momentum * old_term
    along_sum = grad_norm + momentum * crossed
    step_size = along_sum / curvature
    return (estimate + step_size * new_direction, new_direction)


LANES = 128
SIDES = 2 * RADIUS
HALO = 16
PARAM_LANE = 96
VMEM = pl.BlockSpec(memory_space=pltpu.VMEM)
SMEM = pl.BlockSpec(memory_space=pltpu.SMEM)
VMEM_BYTES = 48 * 1024 * 1024


def split_two(value):
    high = value.astype(jnp.bfloat16)
    low = (value - high.astype(jnp.float32)).astype(jnp.bfloat16)
    return high, low


def edge_kernel(first, last, edge):
    epochs = first.shape[1]
    lane = lax.broadcasted_iota(jnp.int32, edge.shape, 1)
    total = jnp.zeros(edge.shape, jnp.float32)
    for part in range(2):
        for epoch in range(epochs):
            at = (part * epochs + epoch) * SIDES
            total = placed(lane, total, tile_of(last, part, epoch, 0), LANES - RADIUS, at)
            total = placed(lane, total, tile_of(first, part, epoch, 0), 0, at + RADIUS)
    edge[...] = total.astype(jnp.bfloat16)


def fields_kernel(me, estimate, direction, *fields):
    look_rows = estimate.shape[1]
    tiles = len(fields)
    for shift, out in enumerate(fields):
        tile = lax.rem(me[0] + shift, tiles)
        columns = pl.ds(pl.multiple_of(tile * LANES, LANES), LANES)
        for epoch in range(estimate.shape[0]):
            here = slice(epoch * look_rows, (epoch + 1) * look_rows)
            first, second = split_two(estimate[epoch, :, columns])
            out[0, here, :] = first
            out[1, here, :] = second
            out[2, here, :] = direction[epoch, :, columns].astype(jnp.bfloat16)


def tile_of(slc, part, epoch, tile):
    return slc[part, epoch, :, tile * LANES : (tile + 1) * LANES].astype(jnp.float32)


def placed(lane, total, source, start, target):
    moved = pltpu.roll(source, (target - start) % LANES, axis=1)
    return jnp.where((lane >= target) & (lane < target + RADIUS), moved, total)


def pack_kernel(me, present, slc, params, before, after, *refs):
    messages, strips = refs[:-1], refs[-1]
    tiles = len(messages)
    epochs = slc.shape[1]
    rows = slc.shape[2]
    lane = lax.broadcasted_iota(jnp.int32, (rows, LANES), 1)
    value = params[...]
    high = value.astype(jnp.bfloat16).astype(jnp.float32)
    middle = (value - high).astype(jnp.bfloat16).astype(jnp.float32)
    low = value - high - middle
    third = PARAM_LANE + 2 * SLOTS
    split = jnp.where(lane < third, high, jnp.where(lane < third + SLOTS, middle, low))
    split = jnp.where(lane >= PARAM_LANE, split, 0.0)
    inside = lane < 2 * epochs * SIDES
    for tile in range(tiles):
        total = split
        if tile == 0:
            edge = before[...].astype(jnp.float32) * present[0]
            total = jnp.where(inside & (lane % SIDES < RADIUS), edge, total)
        if tile == tiles - 1:
            edge = after[...].astype(jnp.float32) * present[1]
            total = jnp.where(inside & (lane % SIDES >= RADIUS), edge, total)
        for part in range(2):
            for epoch in range(epochs):
                at = (part * epochs + epoch) * SIDES
                if tile > 0:
                    total = placed(lane, total, tile_of(slc, part, epoch, tile - 1), LANES - RADIUS, at)
                if tile < tiles - 1:
                    total = placed(lane, total, tile_of(slc, part, epoch, tile + 1), 0, at + RADIUS)
        strips[tile] = total.astype(jnp.bfloat16)
    for tile in range(tiles):
        shift = lax.rem(tile - me[0] + tiles, tiles)
        for number, message in enumerate(messages):

            @pl.when(shift == number)
            def _():
                for part in range(2):
                    for epoch in range(epochs):
                        at = (part * epochs + epoch) * rows
                        message[at : at + rows, :] = slc[part, epoch, :, tile * LANES : (tile + 1) * LANES]
                message[2 * epochs * rows :, :] = strips[tile]


def look_order(from_rows, first, keep):
    looks = from_rows // LOOK
    to = lax.broadcasted_iota(jnp.int32, (from_rows, from_rows), 0)
    at = lax.broadcasted_iota(jnp.int32, (from_rows, from_rows), 1)
    order = (at == (to + first) % looks * LOOK + to // looks).astype(jnp.float32)
    return (order * keep(at)).astype(jnp.bfloat16)


def unpack_tiles(order, sources, main, first, columns_of):
    looks = order.shape[0] // LOOK
    for start in range(0, len(sources), 4):
        parts = jnp.concatenate([columns_of(source) for source in sources[start : start + 4]], axis=1)
        value = jnp.dot(order, parts, preferred_element_type=jnp.float32)
        for one in range(4):
            for look in range(LOOK):
                main[first[start + one], look] = value[look * looks : (look + 1) * looks, one * LANES : (one + 1) * LANES]


def unpack_rims(by_look, looks, rim, first):
    share = LANES // SLOTS
    lane = lax.broadcasted_iota(jnp.int32, (looks, LANES), 1)
    for at, place in enumerate(first):
        value = jnp.zeros((looks, LANES), jnp.float32)
        for look in range(LOOK):
            target = look * SIDES
            moved = pltpu.roll(by_look[look * looks : (look + 1) * looks], (target - at * SIDES) % LANES, axis=1)
            value = jnp.where((lane >= target) & (lane < target + SIDES), moved, value)
        spread = share
        while spread < LANES:
            value = value + pltpu.roll(value, spread, axis=1)
            spread = 2 * spread
        rim[place] = value


def band_of(shape, from_of, to_of):
    at = lax.broadcasted_iota(jnp.int32, shape, 0)
    to = lax.broadcasted_iota(jnp.int32, shape, 1)
    return (jnp.abs(from_of(at, to) - to_of(at, to)) <= RADIUS).astype(jnp.float32).astype(jnp.bfloat16)


def column_bands():
    share = LANES // SLOTS

    def rim_from(at, to):
        side = at % share % SIDES
        return jnp.where(side < RADIUS, side - RADIUS, LANES + side - RADIUS)

    def rim_to(at, to):
        column = (to - at % LANES // share * share + LANES) % LANES
        inside = (column < RADIUS) | (column >= LANES - RADIUS)
        inside = inside & (at % share < LOOK * SIDES)
        return jnp.where(inside, column, 4 * LANES)

    band = band_of((2 * LANES, LANES), lambda at, to: at % LANES, lambda at, to: to)
    return band, band_of((2 * LANES, LANES), rim_from, rim_to)


def mixed(values):
    lane = lax.broadcasted_iota(jnp.int32, values[0].shape, 1)
    result = values[-1]
    for slot in range(SLOTS - 1):
        result = jnp.where(lane // (LANES // SLOTS) == slot, values[slot], result)
    return result


def power_batches(blocks, epochs, looks, main, rim, looked, rim_looked):
    total = blocks * epochs
    group = 2 * SLOTS
    for block in range(blocks):
        for piece in range(0, looks, 8):
            rows_at = slice(piece, piece + 8)
            for half in range(2):
                squares = []
                for slot in range(SLOTS):
                    channel = half * SLOTS + slot
                    epoch = block * epochs + channel
                    value = None
                    for look in range(LOOK):
                        real = main[epoch, look, rows_at]
                        imag = main[total + epoch, look, rows_at]
                        one = real * real + imag * imag
                        value = one if value is None else value + one
                    at = (block * group + channel) * looks + piece
                    looked[at : at + 8, :] = value
                    real = rim[epoch, rows_at]
                    imag = rim[total + epoch, rows_at]
                    squares.append(real * real + imag * imag)
                at = (block * 2 + half) * looks + piece
                rim_looked[at : at + 8, :] = mixed(squares)


def pair_batch(epoch, mates, total, main, rim):
    own_re, own_im = main[epoch], main[total + epoch]
    reals, imags = [], []
    for mate in mates:
        mate_re, mate_im = main[mate], main[total + mate]
        real = own_re[0] * mate_re[0] + own_im[0] * mate_im[0]
        imag = own_im[0] * mate_re[0] - own_re[0] * mate_im[0]
        for look in range(1, LOOK):
            real = real + (own_re[look] * mate_re[look] + own_im[look] * mate_im[look])
            imag = imag + (own_im[look] * mate_re[look] - own_re[look] * mate_im[look])
        reals.append(real)
        imags.append(imag)
    own_re, own_im = rim[epoch], rim[total + epoch]
    mate_re = mixed([rim[mate] for mate in mates])
    mate_im = mixed([rim[total + mate] for mate in mates])
    rims = [own_re * mate_re + own_im * mate_im, own_im * mate_re - own_re * mate_im]
    return reals + imags, rims


def put(ref, block, values):
    rows = sum(value.shape[0] for value in values)
    ref[pl.ds(pl.multiple_of(block * rows, rows), rows), :] = jnp.concatenate(values, axis=0)


def columns_summed(couple, looks, bands, looked, rim_looked):
    group = 2 * SLOTS
    f32 = jnp.float32
    at = pl.ds(pl.multiple_of(couple * (2 * group * looks), 2 * group * looks), 2 * group * looks)
    halves = jnp.concatenate(split_two(looked[at, :]), axis=1)
    value = jnp.dot(halves, bands[0], preferred_element_type=f32)
    at = pl.ds(pl.multiple_of(couple * (4 * looks), 4 * looks), 4 * looks)
    halves = jnp.concatenate(split_two(rim_looked[at, :]), axis=1)
    outer = jnp.dot(halves, bands[1], preferred_element_type=f32)
    lane = lax.broadcasted_iota(jnp.int32, (looks, LANES), 1)
    outside = (lane < RADIUS) | (lane >= LANES - RADIUS)
    results = []
    for channel in range(2 * group):
        batch, half, slot = channel // group, channel % group // SLOTS, channel % SLOTS
        row = (batch * 2 + half) * looks
        part = outer[row : row + looks]
        if slot > 0:
            part = pltpu.roll(part, LANES - slot * (LANES // SLOTS), axis=1)
        row = channel * looks
        results.append(value[row : row + looks] + jnp.where(outside, part, 0.0))
    return results


def rows_summed(channel, looks, look_rows, wide):
    first = channel * looks
    total = wide[pl.ds(first, look_rows), :]
    for shift in range(1, 2 * RADIUS + 1):
        total = total + wide[pl.ds(first + shift, look_rows), :]
    return total


def pair_couple(couple, total, partner, main, rim):
    products, rims = [], []
    for one in range(2):
        epoch = couple * 2 + one
        mates = [partner[epoch * SLOTS + slot] for slot in range(SLOTS)]
        more, more_rims = pair_batch(epoch, mates, total, main, rim)
        products += more
        rims += more_rims
    return products, rims


def clipped(value, last):
    return jnp.minimum(jnp.maximum(value, 0), last)


def pair_kernel(sizes, places, partner, weight, present, *refs):
    epochs, rows, operands = sizes
    inputs = refs[:operands]
    factors, pulls, boxed, main, rim, looked, rim_looked, wide = refs[operands:]
    count = len(places)
    total = count * epochs
    own_total = total - epochs
    look_rows = rows // LOOK
    halo_looks = HALO // LOOK
    looks = look_rows + 2 * halo_looks
    full_rows = rows + 2 * HALO
    group = 2 * SLOTS

    def keep(at):
        return jnp.where(at < HALO, present[0], jnp.where(at >= HALO + rows, present[1], 1.0))

    order = look_order(full_rows, halo_looks - RADIUS, keep)
    bands = column_bands()
    for block, (tile_at, top_at, bottom_at, halo_row) in enumerate(places):
        tile, top, bottom = inputs[tile_at], inputs[top_at], inputs[bottom_at]

        def rows_of(at):
            border = slice(halo_row + at * HALO, halo_row + (at + 1) * HALO)
            return jnp.concatenate([top[border, :], tile[at * rows : (at + 1) * rows, :], bottom[border, :]], axis=0)

        first = [part * total + block * epochs + epoch for part in range(2) for epoch in range(epochs)]
        unpack_tiles(order, range(2 * epochs), main, first, rows_of)
        by_look = jnp.dot(order, rows_of(2 * epochs), preferred_element_type=jnp.float32)
        unpack_rims(by_look, looks, rim, first)
    power_batches(count, epochs, looks, main, rim, looked, rim_looked)
    powers = (count + 1) // 2
    last = powers + own_total // 2 - 1

    def boxed_of(channel):
        return boxed[pl.ds(pl.multiple_of(channel * look_rows, look_rows), look_rows), :]

    @pl.loop(0, last + 3)
    def _(turn):
        done = clipped(turn - 2 - powers, own_total // 2 - 1)
        results = []
        for one in range(2):
            epoch = done * 2 + one
            own_power = boxed_of(epoch)
            first = (2 * powers + epoch) * (group * look_rows)
            parts = boxed[pl.ds(pl.multiple_of(first, group * look_rows), group * look_rows), :]
            parts = parts.reshape(group, look_rows, LANES)
            for slot in range(SLOTS):
                pair = epoch * SLOTS + slot
                inverse = lax.rsqrt(own_power * boxed_of(partner[pair]) + EPSILON)
                unit_re = parts[slot] * inverse
                unit_im = parts[SLOTS + slot] * inverse
                factor = weight[pair] * (unit_re * unit_re + unit_im * unit_im)
                results.append((factor, factor * unit_im))
        summed = clipped(turn - 1, last)
        sums = [rows_summed(summed * 2 * group + one, looks, look_rows, wide) for one in range(2 * group)]
        couple = clipped(turn, last)
        columns = columns_summed(couple, looks, bands, looked, rim_looked)
        here = clipped(turn, own_total // 2 - 1)
        products, rims = pair_couple(here, total, partner, main, rim)
        for ref, values in zip((factors, pulls), zip(*results)):
            ref[pl.ds(done * 2 * SLOTS, 2 * SLOTS)] = jnp.stack(values)
        put(boxed, summed, sums)
        put(wide, couple, columns)
        put(looked, powers + here, products)
        put(rim_looked, powers + here, rims)


def gradient_kernel(sizes, partner, *refs):
    tiles, epochs, stages = sizes
    fields = refs[:tiles]
    factors = refs[tiles : tiles + len(stages)]
    pulls = refs[tiles + len(stages) : tiles + 2 * len(stages)]
    gradient, sums, est, old = refs[tiles + 2 * len(stages) :]
    look_rows = est.shape[1]
    total = tiles * epochs
    f32 = jnp.float32
    for block in range(tiles):

        @pl.loop(0, epochs, unroll=4)
        def _(epoch):
            here = pl.ds(pl.multiple_of(epoch * look_rows, look_rows), look_rows)
            est[block * epochs + epoch] = fields[block][0, here, :].astype(f32) + fields[block][1, here, :].astype(f32)
            old[block * epochs + epoch] = fields[block][2, here, :].astype(f32)
            gradient[block * epochs + epoch] = jnp.zeros((look_rows, LANES), f32)

    for stage, (first, own_total) in enumerate(stages):

        @pl.loop(0, own_total, unroll=2)
        def _(here):
            epoch = lax.rem(first + here, total)
            own_est = est[epoch]
            own = jnp.zeros((look_rows, LANES), f32)
            mates = [partner[epoch * SLOTS + slot] for slot in range(SLOTS)]
            values = []
            for slot, mate in enumerate(mates):
                pair = here * SLOTS + slot
                weighted = pulls[stage][pair] - factors[stage][pair] * (own_est - est[mate])
                own = own + weighted
                values.append(weighted)
            for mate, weighted in zip(mates, values):
                gradient[mate] = gradient[mate] - weighted
            gradient[epoch] = gradient[epoch] + own

    zero = jnp.zeros((look_rows, LANES), f32)
    results = (zero,) * 5
    for stage, (first, own_total) in enumerate(stages):

        def totals(here, carry):
            norm, crossed, grad_term, mixed_term, old_term = carry
            epoch = lax.rem(first + here, total)
            own_grad = gradient[epoch]
            own_old = old[epoch]
            norm = norm + own_grad * own_grad
            crossed = crossed + own_grad * own_old
            for slot in range(SLOTS):
                mate = partner[epoch * SLOTS + slot]
                factor = factors[stage][here * SLOTS + slot]
                grad_spread = own_grad - gradient[mate]
                old_spread = own_old - old[mate]
                pulled = factor * grad_spread
                grad_term = grad_term + pulled * grad_spread
                mixed_term = mixed_term + pulled * old_spread
                old_term = old_term + factor * old_spread * old_spread
            return norm, crossed, grad_term, mixed_term, old_term

        results = lax.fori_loop(0, own_total, totals, results, unroll=2)
    sums[...] = jnp.zeros(sums.shape, f32)
    for at, value in enumerate(results):
        sums[at : at + 1, :] = jnp.sum(value, axis=0, keepdims=True)


def return_kernel(tiles, gradient, *refs):
    pieces = refs[-tiles:]
    shared = refs[:-tiles]
    total = shared[0][...]
    for other in shared[1:]:
        total = total + other[...]
    epochs = gradient.shape[0] // len(pieces)
    look_rows = gradient.shape[1]
    for number, piece in enumerate(pieces):
        for epoch in range(epochs):
            piece[epoch * look_rows : (epoch + 1) * look_rows, :] = gradient[number * epochs + epoch]
        piece[epochs * look_rows :, :] = total


def update_kernel(cell_count, me, prev_mean, estimate, direction, *refs):
    new_estimate, new_direction = refs[-2:]
    pieces = refs[:-2]
    tiles = len(pieces)
    epochs = estimate.shape[0]
    look_rows = estimate.shape[1]
    total = pieces[0][epochs * look_rows :, :]
    for piece in pieces[1:]:
        total = total + piece[epochs * look_rows :, :]
    total = jnp.sum(total, axis=1, keepdims=True)
    grad_norm, crossed, grad_term, mixed, old_term = (total[at : at + 1, :] for at in range(5))
    momentum = grad_norm / cell_count / prev_mean[0]
    curvature = grad_term + 2.0 * momentum * mixed + momentum * momentum * old_term
    step = (grad_norm + momentum * crossed) / curvature
    momentum = jnp.broadcast_to(momentum, (look_rows, LANES))
    step = jnp.broadcast_to(step, (look_rows, LANES))
    for shift, piece in enumerate(pieces):
        tile = lax.rem(me[0] - shift + tiles, tiles)
        columns = pl.ds(pl.multiple_of(tile * LANES, LANES), LANES)
        for epoch in range(epochs):
            gradient = piece[epoch * look_rows : (epoch + 1) * look_rows, :]
            moved = gradient + momentum * direction[epoch, :, columns]
            new_direction[epoch, :, columns] = moved
            new_estimate[epoch, :, columns] = estimate[epoch, :, columns] + step * moved


def swapped(up, down, axis):
    size = lax.axis_size(axis)
    if size == 1:
        return jnp.zeros_like(up), jnp.zeros_like(down)
    if size == 2:
        first = lax.axis_index(axis) == 0
        got = lax.ppermute(jnp.where(first, up, down), axis, [(0, 1), (1, 0)])
        return got, got
    forward = [(i, i + 1) for i in range(size - 1)]
    backward = [(target, source) for source, target in forward]
    return lax.ppermute(up, axis, forward), lax.ppermute(down, axis, backward)


def to_ahead(x, axis, by):
    size = lax.axis_size(axis)
    return lax.ppermute(x, axis, [(i, (i + by) % size) for i in range(size)])


def transposed_plan(slc, offsets, weights, estimate, direction, prev_mean):
    f32 = jnp.float32
    bf16 = jnp.bfloat16
    tiles = lax.axis_size("epoch")
    me = lax.axis_index("epoch")
    epochs, rows, columns = slc.shape[1:]
    look_rows = rows // LOOK
    total = tiles * epochs
    tile_rows = 2 * epochs * rows
    params_of = pltpu.CompilerParams(vmem_limit_bytes=VMEM_BYTES)

    def fetched(messages, shift):
        return to_ahead(messages[tiles - shift], "epoch", tiles - shift)

    sub = lax.axis_index("sub")
    outer_tile = (2, epochs, rows, LANES)
    edge = pl.pallas_call(
        edge_kernel,
        out_shape=jax.ShapeDtypeStruct((rows, LANES), bf16),
        grid=(1,),
        in_specs=[
            pl.BlockSpec(outer_tile, lambda _: (0, 0, 0, 0)),
            pl.BlockSpec(outer_tile, lambda _: (0, 0, 0, tiles - 1)),
        ],
        out_specs=pl.BlockSpec((rows, LANES), lambda _: (0, 0)),
        compiler_params=params_of,
        cost_estimate=pl.CostEstimate(flops=1_000_000, bytes_accessed=1_000_000, transcendentals=0),
    )(slc, slc)
    before, after = swapped(edge, edge, "sub")
    params = jnp.zeros((rows, LANES), f32)
    listed = jnp.concatenate([offsets.astype(f32), weights, weights, weights], axis=1)
    params = lax.dynamic_update_slice(params, listed, (0, PARAM_LANE))
    sub_present = jnp.stack([sub > 0, sub < lax.axis_size("sub") - 1]).astype(f32)
    messages = pl.pallas_call(
        pack_kernel,
        out_shape=(jax.ShapeDtypeStruct((tile_rows + rows, LANES), bf16),) * tiles,
        in_specs=[SMEM] * 2 + [VMEM] * 4,
        out_specs=(VMEM,) * tiles,
        scratch_shapes=[pltpu.VMEM((tiles, rows, LANES), bf16)],
        compiler_params=params_of,
        cost_estimate=pl.CostEstimate(flops=3_000_000, bytes_accessed=4_000_000, transcendentals=0),
    )(me.reshape(1), sub_present, slc, params, before, after)
    beside = [tiles - 1, 0, 1]
    far = list(range(2, tiles - 1))
    block = {0: messages[0], 1: fetched(messages, 1), tiles - 1: fetched(messages, tiles - 1)}
    held = lax.optimization_barrier((messages, block[1], block[tiles - 1]))[0]
    block.update({shift: fetched(held, shift) for shift in far})

    estimate, direction, _ = lax.optimization_barrier((estimate, direction, messages))
    fields = pl.pallas_call(
        fields_kernel,
        out_shape=(jax.ShapeDtypeStruct((3, epochs * look_rows, LANES), bf16),) * tiles,
        in_specs=[SMEM] + [VMEM] * 2,
        out_specs=(VMEM,) * tiles,
        compiler_params=params_of,
        cost_estimate=pl.CostEstimate(flops=1_000_000, bytes_accessed=2_000_000, transcendentals=0),
    )(me.reshape(1), estimate, direction)
    space = lax.axis_index("space")
    spaces = lax.axis_size("space")
    present = jnp.stack([space > 0, space < spaces - 1]).astype(f32)

    def halo(pieces):
        def border(from_row):
            cuts = [lax.dynamic_slice_in_dim(piece, from_row, HALO, axis=1).reshape(-1, LANES) for piece in pieces]
            return jnp.concatenate(cuts, axis=0)

        if spaces == 2:
            got = lax.ppermute(border(jnp.where(space == 0, rows - HALO, 0)), "space", [(0, 1), (1, 0)])
            return got, got
        return swapped(border(rows - HALO), border(0), "space")

    def by_rows(shift):
        return block[shift].reshape(-1, rows, LANES)

    def params_in(shift):
        return block[shift][tile_rows : tile_rows + epochs, PARAM_LANE : PARAM_LANE + 4 * SLOTS].astype(f32)

    def pairs_of(blocks, loaded):
        listed = jnp.concatenate([params_in(block) for block in blocks], axis=0)
        mate = jnp.arange(len(blocks) * epochs, dtype=jnp.int32)[:, None] + listed[:, :SLOTS].astype(jnp.int32)
        weight = listed[:, SLOTS : 2 * SLOTS] + listed[:, 2 * SLOTS : 3 * SLOTS] + listed[:, 3 * SLOTS :]
        return mate.reshape(-1), weight.reshape(-1)

    own_halo = halo([by_rows(0)])
    near_halo = halo([by_rows(1), by_rows(tiles - 1)])
    halos = {0: (own_halo, 0), 1: (near_halo, 0), tiles - 1: (near_halo, 1)}

    def pair_stage(loaded):
        own = loaded[:-1]
        listed = jnp.concatenate([params_in(shift) for shift in own], axis=0)
        mate = jnp.arange(len(own) * epochs, dtype=jnp.int32)[:, None] + listed[:, :SLOTS].astype(jnp.int32)
        weight = listed[:, SLOTS : 2 * SLOTS] + listed[:, 2 * SLOTS : 3 * SLOTS] + listed[:, 3 * SLOTS :]
        operands = []

        def index_of(array):
            for at, other in enumerate(operands):
                if other is array:
                    return at
            operands.append(array)
            return len(operands) - 1

        places = []
        for shift in loaded:
            (top, bottom), slot = halos[shift]
            place = index_of(block[shift]), index_of(top), index_of(bottom), slot * (2 * epochs + 1) * HALO
            places.append(place)
        here = len(loaded) * epochs
        owned = len(own) * epochs
        looks = (rows + 2 * HALO) // LOOK
        group = 2 * SLOTS
        batches = (len(loaded) + 1) // 2 * 2 + owned
        shape = jax.ShapeDtypeStruct((owned * SLOTS, look_rows, LANES), f32)
        return pl.pallas_call(
            functools.partial(pair_kernel, (epochs, rows, len(operands)), tuple(places)),
            out_shape=(shape, shape),
            in_specs=[SMEM] * 3 + [VMEM] * len(operands),
            out_specs=(VMEM, VMEM),
            scratch_shapes=[
                pltpu.VMEM((batches * group * look_rows, LANES), f32),
                pltpu.VMEM((2 * here, LOOK, looks, LANES), f32),
                pltpu.VMEM((2 * here, looks, LANES), f32),
                pltpu.VMEM((batches * group * looks, LANES), f32),
                pltpu.VMEM((batches * 2 * looks, LANES), f32),
                pltpu.VMEM((batches * group * looks, LANES), f32),
            ],
            compiler_params=params_of,
            cost_estimate=pl.CostEstimate(flops=20_000_000, bytes_accessed=30_000_000, transcendentals=0),
        )(mate.reshape(-1), weight.reshape(-1), present, *operands)

    near_stage = beside
    far_stage = list(range(1, tiles))
    near_pairs = pair_stage(near_stage)
    held, fields, near_pairs = lax.optimization_barrier(([block[shift] for shift in far], fields, near_pairs))
    block.update(zip(far, held))
    far_halo = halo([by_rows(shift) for shift in far])
    halos.update({shift: (far_halo, at) for at, shift in enumerate(far)})
    field = [fields[0]] + [fetched(fields, shift) for shift in range(1, tiles)]
    far_pairs = pair_stage(far_stage)

    listed = jnp.concatenate([params_in(shift) for shift in range(tiles)], axis=0)
    partner = jnp.arange(total, dtype=jnp.int32)[:, None] + listed[:, :SLOTS].astype(jnp.int32)
    partner = lax.rem(partner, total).reshape(-1)
    stages = tuple((stage[0] * epochs, (len(stage) - 1) * epochs) for stage in (near_stage, far_stage))
    gradient, sums = pl.pallas_call(
        functools.partial(gradient_kernel, (tiles, epochs, stages)),
        out_shape=(
            jax.ShapeDtypeStruct((total, look_rows, LANES), f32),
            jax.ShapeDtypeStruct((8, LANES), f32),
        ),
        in_specs=[SMEM] + [VMEM] * (tiles + 4),
        out_specs=(VMEM, VMEM),
        scratch_shapes=[pltpu.VMEM((total, look_rows, LANES), f32)] * 2,
        compiler_params=params_of,
        cost_estimate=pl.CostEstimate(flops=10_000_000, bytes_accessed=8_000_000, transcendentals=0),
    )(partner, *field, near_pairs[0], far_pairs[0], near_pairs[1], far_pairs[1])

    place = ("space", "sub")
    count = spaces * lax.axis_size("sub")
    shared = [sums] + [lax.ppermute(sums, place, [(i, (i + by) % count) for i in range(count)]) for by in range(1, count)]
    pieces = pl.pallas_call(
        functools.partial(return_kernel, tiles),
        out_shape=(jax.ShapeDtypeStruct((epochs * look_rows + 8, LANES), f32),) * tiles,
        in_specs=[VMEM] * (1 + count),
        out_specs=(VMEM,) * tiles,
        compiler_params=params_of,
        cost_estimate=pl.CostEstimate(flops=10_000, bytes_accessed=1_000_000, transcendentals=0),
    )(gradient, *shared)
    returned = [pieces[0]] + [to_ahead(pieces[by], "epoch", by) for by in range(1, tiles)]
    cell_count = float(total * look_rows * spaces * columns * lax.axis_size("sub"))
    return pl.pallas_call(
        functools.partial(update_kernel, cell_count),
        out_shape=(jax.ShapeDtypeStruct(estimate.shape, f32),) * 2,
        in_specs=[SMEM] * 2 + [VMEM] * (2 + tiles),
        out_specs=(VMEM, VMEM),
        compiler_params=params_of,
        cost_estimate=pl.CostEstimate(flops=1_000_000, bytes_accessed=2_000_000, transcendentals=0),
    )(me.reshape(1), prev_mean, estimate, direction, *returned)


def on_device(slc, offsets, weights, estimate, direction, prev_mean):
    epochs, rows, columns = slc.shape[1:]
    fits = columns == LANES * lax.axis_size("epoch") and lax.axis_size("epoch") > 3
    fits = fits and 2 * epochs * SIDES <= PARAM_LANE and rows % HALO == 0 and epochs == 2 * SLOTS
    plan = transposed_plan if fits else ring_plan
    return plan(slc, offsets, weights, estimate, direction, prev_mean)


def solution(mesh):
    return jax.shard_map(
        on_device,
        mesh=mesh,
        in_specs=(
            P(None, ("groups", "epoch"), "space", "sub"),
            P(("groups", "epoch"), None),
            P(("groups", "epoch"), None),
            P(("groups", "epoch"), "space", "sub"),
            P(("groups", "epoch"), "space", "sub"),
            P(),
        ),
        out_specs=(P(("groups", "epoch"), "space", "sub"), P(("groups", "epoch"), "space", "sub")),
        check_vma=False,
    )
```

```python
import functools

import jax
import jax.numpy as jnp
import numpy as np
from jax import lax
from jax.experimental import pallas as pl
from jax.experimental.pallas import tpu as pltpu
from jax.sharding import PartitionSpec as P

SLOTS = 4
OFFS = 8
LOOK = 4
RADIUS = 3


EPSILON = 1e-06


def passed_along(x, axis, by):
    size = lax.axis_size(axis)
    return lax.ppermute(x, axis, [(i, (i + by) % size) for i in range(size)])


def extended_2(block, sides, width):
    for axis, dim in sides:
        count = lax.axis_size(axis)
        forward = [(i, i + 1) for i in range(count - 1)]
        backward = [(target, source) for source, target in forward]
        low = lax.ppermute(
            lax.slice_in_dim(block, block.shape[dim] - width, None, axis=dim), axis, forward
        )
        high = lax.ppermute(lax.slice_in_dim(block, 0, width, axis=dim), axis, backward)
        block = jnp.concatenate([low, block, high], axis=dim)
    return block


def looked_sum(field):
    shape = field.shape
    return jnp.sum(field.reshape(shape[:-2] + (shape[-2] // LOOK, LOOK, shape[-1])), axis=-2)


def window_sum(padded, axis):
    length = padded.shape[axis] - 2 * RADIUS
    total = lax.slice_in_dim(padded, 0, length, axis=axis)
    for shift_at in range(1, 2 * RADIUS + 1):
        total = total + lax.slice_in_dim(padded, shift_at, shift_at + length, axis=axis)
    return total


def ring_plan(slc, offsets, weights, estimate, direction, prev_mean):
    epochs_here = slc.shape[1]
    look_rows = slc.shape[2] // LOOK
    col_count = slc.shape[3]
    ahead = passed_along(slc, "epoch", -1)
    extended = jnp.concatenate([slc, ahead], axis=1)
    numbers = jnp.arange(epochs_here, dtype=jnp.int32)
    partner = numbers[:, None] + offsets
    own_real = slc[0].astype(jnp.float32)
    own_imag = slc[1].astype(jnp.float32)
    ext_real = extended[0].astype(jnp.float32)
    ext_imag = extended[1].astype(jnp.float32)
    powers = looked_sum(ext_real * ext_real + ext_imag * ext_imag)
    pieces = []
    for slot_index in range(SLOTS):
        mate_real = jnp.take(ext_real, partner[:, slot_index], axis=0)
        mate_imag = jnp.take(ext_imag, partner[:, slot_index], axis=0)
        pieces.append(looked_sum(own_real * mate_real + own_imag * mate_imag))
        pieces.append(looked_sum(own_imag * mate_real - own_real * mate_imag))
    pair_count = epochs_here * 2 * SLOTS
    stacked = jnp.concatenate(
        [jnp.stack(pieces, axis=1).reshape(pair_count, look_rows, col_count), powers], axis=0
    )
    padded = extended_2(stacked, (("space", 1), ("sub", 2)), RADIUS)
    boxed = window_sum(window_sum(padded, 1), 2)
    pair_boxed = boxed[:pair_count].reshape(epochs_here, 2 * SLOTS, look_rows, col_count)
    power_box = boxed[pair_count:]
    coh_real = pair_boxed[:, 0::2]
    coh_imag = pair_boxed[:, 1::2]
    denominator = power_box[:epochs_here, None] * jnp.take(power_box, partner, axis=0) + EPSILON
    coherence = (coh_real * coh_real + coh_imag * coh_imag) / denominator
    observed = coh_imag / jnp.sqrt(denominator)
    est_ahead = passed_along(estimate, "epoch", -1)
    est_extended = jnp.concatenate([estimate, est_ahead], axis=0)
    fitted = estimate[:, None] - jnp.take(est_extended, partner, axis=0)
    factor = weights[:, :, None, None] * coherence
    weighted = factor * (observed - fitted)
    flattened = weighted.reshape(epochs_here * SLOTS, look_rows * col_count)
    selector = (
        jnp.arange(epochs_here + OFFS, dtype=jnp.int32)[:, None] == partner.reshape(1, -1)
    ).astype(jnp.float32)
    gathered = jnp.dot(
        selector, flattened, precision=lax.Precision.HIGHEST, preferred_element_type=jnp.float32
    ).reshape(epochs_here + OFFS, look_rows, col_count)
    own_part = jnp.sum(weighted, axis=1) - gathered[:epochs_here]
    returned = passed_along(-gathered[epochs_here:], "epoch", 1)
    gradient = jnp.concatenate([own_part + returned, own_part[OFFS:]], axis=0)
    cell_count = float(
        epochs_here
        * lax.axis_size("epoch")
        * look_rows
        * lax.axis_size("space")
        * col_count
        * lax.axis_size("sub")
    )
    local_norm = jnp.sum(gradient * gradient)
    local_crossed = jnp.sum(gradient * direction)
    mean_before = prev_mean[0]
    fields_ahead = passed_along(
        jnp.stack([gradient, direction]).astype(jnp.bfloat16), "epoch", -1
    ).astype(jnp.float32)
    grad_extended = jnp.concatenate([gradient, fields_ahead[0]], axis=0)
    old_extended = jnp.concatenate([direction, fields_ahead[1]], axis=0)
    grad_spread = gradient[:, None] - jnp.take(grad_extended, partner, axis=0)
    old_spread = direction[:, None] - jnp.take(old_extended, partner, axis=0)
    totals = lax.psum(
        (
            local_norm,
            local_crossed,
            jnp.sum(factor * grad_spread * grad_spread),
            jnp.sum(factor * grad_spread * old_spread),
            jnp.sum(factor * old_spread * old_spread),
        ),
        ("epoch", "space", "sub"),
    )
    grad_norm, crossed, grad_term, mixed_term, old_term = totals
    momentum = grad_norm / cell_count / mean_before
    new_direction = gradient + momentum * direction
    curvature = grad_term + 2.0 * momentum * mixed_term + momentum * momentum * old_term
    along_sum = grad_norm + momentum * crossed
    step_size = along_sum / curvature
    return (estimate + step_size * new_direction, new_direction)


LANES = 128
SIDES = 2 * RADIUS
HALO = 16
PARAM_LANE = 96
VMEM = pl.BlockSpec(memory_space=pltpu.VMEM)
SMEM = pl.BlockSpec(memory_space=pltpu.SMEM)
VMEM_BYTES = 48 * 1024 * 1024


def split_two(value):
    high = value.astype(jnp.bfloat16)
    low = (value - high.astype(jnp.float32)).astype(jnp.bfloat16)
    return high, low


def edge_kernel(first, last, edge):
    epochs = first.shape[1]
    lane = lax.broadcasted_iota(jnp.int32, edge.shape, 1)
    total = jnp.zeros(edge.shape, jnp.float32)
    for part in range(2):
        for epoch in range(epochs):
            at = (part * epochs + epoch) * SIDES
            total = placed(lane, total, tile_of(last, part, epoch, 0), LANES - RADIUS, at)
            total = placed(lane, total, tile_of(first, part, epoch, 0), 0, at + RADIUS)
    edge[...] = total.astype(jnp.bfloat16)


def fields_kernel(me, estimate, direction, *fields):
    look_rows = estimate.shape[1]
    tiles = len(fields)
    for shift, out in enumerate(fields):
        tile = lax.rem(me[0] + shift, tiles)
        columns = pl.ds(pl.multiple_of(tile * LANES, LANES), LANES)
        for epoch in range(estimate.shape[0]):
            here = slice(epoch * look_rows, (epoch + 1) * look_rows)
            first, second = split_two(estimate[epoch, :, columns])
            out[0, here, :] = first
            out[1, here, :] = second
            out[2, here, :] = direction[epoch, :, columns].astype(jnp.bfloat16)


def tile_of(slc, part, epoch, tile):
    return slc[part, epoch, :, tile * LANES : (tile + 1) * LANES].astype(jnp.float32)


def placed(lane, total, source, start, target):
    moved = pltpu.roll(source, (target - start) % LANES, axis=1)
    return jnp.where((lane >= target) & (lane < target + RADIUS), moved, total)


def pack_kernel(me, present, slc, params, outer, before, after, *refs):
    messages, strips = refs[:-1], refs[-1]
    tiles = len(messages)
    epochs = slc.shape[1]
    rows = slc.shape[2]
    lane = lax.broadcasted_iota(jnp.int32, (rows, LANES), 1)
    value = params[...]
    high = value.astype(jnp.bfloat16).astype(jnp.float32)
    middle = (value - high).astype(jnp.bfloat16).astype(jnp.float32)
    low = value - high - middle
    third = PARAM_LANE + 2 * SLOTS
    split = jnp.where(lane < third, high, jnp.where(lane < third + SLOTS, middle, low))
    split = jnp.where(lane >= PARAM_LANE, split, 0.0)
    sides = outer[...]
    for tile in range(tiles):
        total = split
        if tile == 0:
            edge = before[...].astype(jnp.float32) * present[0]
            total = jnp.where(sides == 1.0, edge, total)
        if tile == tiles - 1:
            edge = after[...].astype(jnp.float32) * present[1]
            total = jnp.where(sides == 2.0, edge, total)
        for part in range(2):
            for epoch in range(epochs):
                at = (part * epochs + epoch) * SIDES
                if tile > 0:
                    total = placed(lane, total, tile_of(slc, part, epoch, tile - 1), LANES - RADIUS, at)
                if tile < tiles - 1:
                    total = placed(lane, total, tile_of(slc, part, epoch, tile + 1), 0, at + RADIUS)
        strips[tile] = total.astype(jnp.bfloat16)
    for tile in range(tiles):
        shift = lax.rem(tile - me[0] + tiles, tiles)
        for number, message in enumerate(messages):

            @pl.when(shift == number)
            def _():
                for part in range(2):
                    for epoch in range(epochs):
                        at = (part * epochs + epoch) * rows
                        message[at : at + rows, :] = slc[part, epoch, :, tile * LANES : (tile + 1) * LANES]
                message[2 * epochs * rows :, :] = strips[tile]


def look_order(from_rows, first):
    looks = from_rows // LOOK
    to = np.arange(from_rows)[:, None]
    at = np.arange(from_rows)[None, :]
    return jnp.asarray(at == (to + first) % looks * LOOK + to // looks, jnp.bfloat16)


def unpack_tiles(order, sources, main, first, columns_of):
    looks = order.shape[0] // LOOK
    for start in range(0, len(sources), 4):
        parts = jnp.concatenate([columns_of(source) for source in sources[start : start + 4]], axis=1)
        value = jnp.dot(order, parts, preferred_element_type=jnp.float32)
        for one in range(4):
            for look in range(LOOK):
                main[first[start + one], look] = value[look * looks : (look + 1) * looks, one * LANES : (one + 1) * LANES]


def unpack_rims(by_look, looks, rim, first):
    share = LANES // SLOTS
    lane = lax.broadcasted_iota(jnp.int32, (looks, LANES), 1)
    for at, place in enumerate(first):
        value = jnp.zeros((looks, LANES), jnp.float32)
        for look in range(LOOK):
            target = look * SIDES
            moved = pltpu.roll(by_look[look * looks : (look + 1) * looks], (target - at * SIDES) % LANES, axis=1)
            value = jnp.where((lane >= target) & (lane < target + SIDES), moved, value)
        spread = share
        while spread < LANES:
            value = value + pltpu.roll(value, spread, axis=1)
            spread = 2 * spread
        rim[place] = value


def column_bands():
    share = LANES // SLOTS
    at = np.arange(2 * LANES)[:, None] % LANES
    to = np.arange(LANES)[None, :]
    side = at % share % SIDES
    source = np.where(side < RADIUS, side - RADIUS, LANES + side - RADIUS)
    column = (to - at // share * share) % LANES
    inside = (column < RADIUS) | (column >= LANES - RADIUS)
    inside = inside & (at % share < LOOK * SIDES)
    band = np.abs(at - to) <= RADIUS
    rim_band = inside & (np.abs(source - column) <= RADIUS)
    return jnp.asarray(band, jnp.bfloat16), jnp.asarray(rim_band, jnp.bfloat16)


def mixed(values):
    lane = lax.broadcasted_iota(jnp.int32, values[0].shape, 1)
    result = values[-1]
    for slot in range(SLOTS - 1):
        result = jnp.where(lane < (SLOTS - 1 - slot) * (LANES // SLOTS), values[SLOTS - 2 - slot], result)
    return result


def power_batches(blocks, epochs, looks, main, rim, looked, rim_looked):
    total = blocks * epochs
    group = 2 * SLOTS
    for block in range(blocks):
        for piece in range(0, looks, 8):
            rows_at = slice(piece, piece + 8)
            for half in range(2):
                squares = []
                for slot in range(SLOTS):
                    channel = half * SLOTS + slot
                    epoch = block * epochs + channel
                    value = None
                    for look in range(LOOK):
                        real = main[epoch, look, rows_at]
                        imag = main[total + epoch, look, rows_at]
                        one = real * real + imag * imag
                        value = one if value is None else value + one
                    at = (block * group + channel) * looks + piece
                    looked[at : at + 8, :] = value
                    real = rim[epoch, rows_at]
                    imag = rim[total + epoch, rows_at]
                    squares.append(real * real + imag * imag)
                at = (block * 2 + half) * looks + piece
                rim_looked[at : at + 8, :] = mixed(squares)


def pair_batch(epoch, mates, total, main, rim):
    own_re, own_im = main[epoch], main[total + epoch]
    reals, imags = [], []
    for mate in mates:
        mate_re, mate_im = main[mate], main[total + mate]
        real = own_re[0] * mate_re[0] + own_im[0] * mate_im[0]
        imag = own_im[0] * mate_re[0] - own_re[0] * mate_im[0]
        for look in range(1, LOOK):
            real = real + (own_re[look] * mate_re[look] + own_im[look] * mate_im[look])
            imag = imag + (own_im[look] * mate_re[look] - own_re[look] * mate_im[look])
        reals.append(real)
        imags.append(imag)
    own_re, own_im = rim[epoch], rim[total + epoch]
    mate_re = mixed([rim[mate] for mate in mates])
    mate_im = mixed([rim[total + mate] for mate in mates])
    rims = [own_re * mate_re + own_im * mate_im, own_im * mate_re - own_re * mate_im]
    return reals + imags, rims


def put(ref, block, values):
    rows = sum(value.shape[0] for value in values)
    ref[pl.ds(pl.multiple_of(block * rows, rows), rows), :] = jnp.concatenate(values, axis=0)


def columns_summed(couple, looks, bands, looked, rim_looked):
    group = 2 * SLOTS
    f32 = jnp.float32
    at = pl.ds(pl.multiple_of(couple * (2 * group * looks), 2 * group * looks), 2 * group * looks)
    halves = jnp.concatenate(split_two(looked[at, :]), axis=1)
    value = jnp.dot(halves, bands[0], preferred_element_type=f32)
    at = pl.ds(pl.multiple_of(couple * (4 * looks), 4 * looks), 4 * looks)
    halves = jnp.concatenate(split_two(rim_looked[at, :]), axis=1)
    outer = jnp.dot(halves, bands[1], preferred_element_type=f32)
    lane = lax.broadcasted_iota(jnp.int32, (looks, LANES), 1)
    outside = (lane < RADIUS) | (lane >= LANES - RADIUS)
    results = []
    for channel in range(2 * group):
        batch, half, slot = channel // group, channel % group // SLOTS, channel % SLOTS
        row = (batch * 2 + half) * looks
        part = outer[row : row + looks]
        if slot > 0:
            part = pltpu.roll(part, LANES - slot * (LANES // SLOTS), axis=1)
        row = channel * looks
        results.append(value[row : row + looks] + jnp.where(outside, part, 0.0))
    return results


def rows_summed(channel, looks, look_rows, wide):
    first = channel * looks
    total = wide[pl.ds(first, look_rows), :]
    for shift in range(1, 2 * RADIUS + 1):
        total = total + wide[pl.ds(first + shift, look_rows), :]
    return total


def pair_couple(couple, total, partner, main, rim):
    products, rims = [], []
    for one in range(2):
        epoch = couple * 2 + one
        mates = [partner[epoch * SLOTS + slot] for slot in range(SLOTS)]
        more, more_rims = pair_batch(epoch, mates, total, main, rim)
        products += more
        rims += more_rims
    return products, rims


def clipped(value, last):
    return jnp.minimum(jnp.maximum(value, 0), last)


def pair_kernel(sizes, places, partner, weight, present, order, band, rim_band, *refs):
    epochs, rows, operands = sizes
    inputs = refs[:operands]
    factors, pulls, boxed, main, rim, looked, rim_looked, wide = refs[operands:]
    count = len(places)
    total = count * epochs
    own_total = total - epochs
    look_rows = rows // LOOK
    halo_looks = HALO // LOOK
    looks = look_rows + 2 * halo_looks
    full_rows = rows + 2 * HALO
    group = 2 * SLOTS

    at = lax.broadcasted_iota(jnp.int32, (full_rows, full_rows), 1)
    keep = jnp.where(at < HALO, present[0], jnp.where(at >= HALO + rows, present[1], 1.0))
    order = (order[...].astype(jnp.float32) * keep).astype(jnp.bfloat16)
    bands = band[...], rim_band[...]
    for block, (tile_at, top_at, bottom_at, halo_row) in enumerate(places):
        tile, top, bottom = inputs[tile_at], inputs[top_at], inputs[bottom_at]

        def rows_of(at):
            border = slice(halo_row + at * HALO, halo_row + (at + 1) * HALO)
            return jnp.concatenate([top[border, :], tile[at * rows : (at + 1) * rows, :], bottom[border, :]], axis=0)

        first = [part * total + block * epochs + epoch for part in range(2) for epoch in range(epochs)]
        unpack_tiles(order, range(2 * epochs), main, first, rows_of)
        by_look = jnp.dot(order, rows_of(2 * epochs), preferred_element_type=jnp.float32)
        unpack_rims(by_look, looks, rim, first)
    power_batches(count, epochs, looks, main, rim, looked, rim_looked)
    powers = (count + 1) // 2
    last = powers + own_total // 2 - 1

    def boxed_of(channel):
        return boxed[pl.ds(pl.multiple_of(channel * look_rows, look_rows), look_rows), :]

    @pl.loop(0, last + 3)
    def _(turn):
        done = clipped(turn - 2 - powers, own_total // 2 - 1)
        results = []
        for one in range(2):
            epoch = done * 2 + one
            own_power = boxed_of(epoch)
            first = (2 * powers + epoch) * (group * look_rows)
            parts = boxed[pl.ds(pl.multiple_of(first, group * look_rows), group * look_rows), :]
            parts = parts.reshape(group, look_rows, LANES)
            for slot in range(SLOTS):
                pair = epoch * SLOTS + slot
                inverse = lax.rsqrt(own_power * boxed_of(partner[pair]) + EPSILON)
                unit_re = parts[slot] * inverse
                unit_im = parts[SLOTS + slot] * inverse
                factor = weight[pair] * (unit_re * unit_re + unit_im * unit_im)
                results.append((factor, factor * unit_im))
        summed = clipped(turn - 1, last)
        sums = [rows_summed(summed * 2 * group + one, looks, look_rows, wide) for one in range(2 * group)]
        couple = clipped(turn, last)
        columns = columns_summed(couple, looks, bands, looked, rim_looked)
        here = clipped(turn, own_total // 2 - 1)
        products, rims = pair_couple(here, total, partner, main, rim)
        for ref, values in zip((factors, pulls), zip(*results)):
            ref[pl.ds(done * 2 * SLOTS, 2 * SLOTS)] = jnp.stack(values)
        put(boxed, summed, sums)
        put(wide, couple, columns)
        put(looked, powers + here, products)
        put(rim_looked, powers + here, rims)


def gradient_kernel(sizes, partner, *refs):
    tiles, epochs, stages = sizes
    fields = refs[:tiles]
    factors = refs[tiles : tiles + len(stages)]
    pulls = refs[tiles + len(stages) : tiles + 2 * len(stages)]
    gradient, sums, est, old = refs[tiles + 2 * len(stages) :]
    look_rows = est.shape[1]
    total = tiles * epochs
    f32 = jnp.float32
    for block in range(tiles):

        @pl.loop(0, epochs, unroll=4)
        def _(epoch):
            here = pl.ds(pl.multiple_of(epoch * look_rows, look_rows), look_rows)
            est[block * epochs + epoch] = fields[block][0, here, :].astype(f32) + fields[block][1, here, :].astype(f32)
            old[block * epochs + epoch] = fields[block][2, here, :].astype(f32)
            gradient[block * epochs + epoch] = jnp.zeros((look_rows, LANES), f32)

    for stage, (first, own_total) in enumerate(stages):

        @pl.loop(0, own_total, unroll=2)
        def _(here):
            epoch = first + here
            epoch = jnp.where(epoch < total, epoch, epoch - total)
            own_est = est[epoch]
            own = jnp.zeros((look_rows, LANES), f32)
            mates = [partner[epoch * SLOTS + slot] for slot in range(SLOTS)]
            values = []
            for slot, mate in enumerate(mates):
                pair = here * SLOTS + slot
                weighted = pulls[stage][pair] - factors[stage][pair] * (own_est - est[mate])
                own = own + weighted
                values.append(weighted)
            for mate, weighted in zip(mates, values):
                gradient[mate] = gradient[mate] - weighted
            gradient[epoch] = gradient[epoch] + own

    zero = jnp.zeros((look_rows, LANES), f32)
    results = (zero,) * 5
    for stage, (first, own_total) in enumerate(stages):

        def totals(here, carry):
            norm, crossed, grad_term, mixed_term, old_term = carry
            epoch = first + here
            epoch = jnp.where(epoch < total, epoch, epoch - total)
            own_grad = gradient[epoch]
            own_old = old[epoch]
            norm = norm + own_grad * own_grad
            crossed = crossed + own_grad * own_old
            for slot in range(SLOTS):
                mate = partner[epoch * SLOTS + slot]
                factor = factors[stage][here * SLOTS + slot]
                grad_spread = own_grad - gradient[mate]
                old_spread = own_old - old[mate]
                pulled = factor * grad_spread
                grad_term = grad_term + pulled * grad_spread
                mixed_term = mixed_term + pulled * old_spread
                old_term = old_term + factor * old_spread * old_spread
            return norm, crossed, grad_term, mixed_term, old_term

        results = lax.fori_loop(0, own_total, totals, results, unroll=2)
    sums[...] = jnp.zeros(sums.shape, f32)
    for at, value in enumerate(results):
        sums[at : at + 1, :] = jnp.sum(value, axis=0, keepdims=True)


def return_kernel(tiles, gradient, *refs):
    pieces = refs[-tiles:]
    shared = refs[:-tiles]
    total = shared[0][...]
    for other in shared[1:]:
        total = total + other[...]
    epochs = gradient.shape[0] // len(pieces)
    look_rows = gradient.shape[1]
    for number, piece in enumerate(pieces):
        for epoch in range(epochs):
            piece[epoch * look_rows : (epoch + 1) * look_rows, :] = gradient[number * epochs + epoch]
        piece[epochs * look_rows :, :] = total


def update_kernel(cell_count, me, prev_mean, estimate, direction, *refs):
    new_estimate, new_direction = refs[-2:]
    pieces = refs[:-2]
    tiles = len(pieces)
    epochs = estimate.shape[0]
    look_rows = estimate.shape[1]
    total = pieces[0][epochs * look_rows :, :]
    for piece in pieces[1:]:
        total = total + piece[epochs * look_rows :, :]
    total = jnp.sum(total, axis=1, keepdims=True)
    grad_norm, crossed, grad_term, mixed, old_term = (total[at : at + 1, :] for at in range(5))
    momentum = grad_norm / cell_count / prev_mean[0]
    curvature = grad_term + 2.0 * momentum * mixed + momentum * momentum * old_term
    step = (grad_norm + momentum * crossed) / curvature
    momentum = jnp.broadcast_to(momentum, (look_rows, LANES))
    step = jnp.broadcast_to(step, (look_rows, LANES))
    for shift, piece in enumerate(pieces):
        tile = lax.rem(me[0] - shift + tiles, tiles)
        columns = pl.ds(pl.multiple_of(tile * LANES, LANES), LANES)
        for epoch in range(epochs):
            gradient = piece[epoch * look_rows : (epoch + 1) * look_rows, :]
            moved = gradient + momentum * direction[epoch, :, columns]
            new_direction[epoch, :, columns] = moved
            new_estimate[epoch, :, columns] = estimate[epoch, :, columns] + step * moved


def swapped(up, down, axis):
    size = lax.axis_size(axis)
    if size == 1:
        return jnp.zeros_like(up), jnp.zeros_like(down)
    if size == 2:
        first = lax.axis_index(axis) == 0
        got = lax.ppermute(jnp.where(first, up, down), axis, [(0, 1), (1, 0)])
        return got, got
    forward = [(i, i + 1) for i in range(size - 1)]
    backward = [(target, source) for source, target in forward]
    return lax.ppermute(up, axis, forward), lax.ppermute(down, axis, backward)


def to_ahead(x, axis, by):
    size = lax.axis_size(axis)
    return lax.ppermute(x, axis, [(i, (i + by) % size) for i in range(size)])


def transposed_plan(slc, offsets, weights, estimate, direction, prev_mean):
    f32 = jnp.float32
    bf16 = jnp.bfloat16
    tiles = lax.axis_size("epoch")
    me = lax.axis_index("epoch")
    epochs, rows, columns = slc.shape[1:]
    look_rows = rows // LOOK
    total = tiles * epochs
    tile_rows = 2 * epochs * rows
    params_of = pltpu.CompilerParams(vmem_limit_bytes=VMEM_BYTES)

    def fetched(messages, shift):
        return to_ahead(messages[tiles - shift], "epoch", tiles - shift)

    sub = lax.axis_index("sub")
    outer_tile = (2, epochs, rows, LANES)
    edge = pl.pallas_call(
        edge_kernel,
        out_shape=jax.ShapeDtypeStruct((rows, LANES), bf16),
        grid=(1,),
        in_specs=[
            pl.BlockSpec(outer_tile, lambda _: (0, 0, 0, 0)),
            pl.BlockSpec(outer_tile, lambda _: (0, 0, 0, tiles - 1)),
        ],
        out_specs=pl.BlockSpec((rows, LANES), lambda _: (0, 0)),
        compiler_params=params_of,
        cost_estimate=pl.CostEstimate(flops=1_000_000, bytes_accessed=1_000_000, transcendentals=0),
    )(slc, slc)
    before, after = swapped(edge, edge, "sub")
    params = jnp.zeros((rows, LANES), f32)
    listed = jnp.concatenate([offsets.astype(f32), weights, weights, weights], axis=1)
    params = lax.dynamic_update_slice(params, listed, (0, PARAM_LANE))
    lane = np.arange(LANES)
    sides = np.where(lane < 2 * epochs * SIDES, np.where(lane % SIDES < RADIUS, 1.0, 2.0), 0.0)
    sides = jnp.asarray(np.broadcast_to(sides, (rows, LANES)), f32)
    sub_present = jnp.stack([sub > 0, sub < lax.axis_size("sub") - 1]).astype(f32)
    messages = pl.pallas_call(
        pack_kernel,
        out_shape=(jax.ShapeDtypeStruct((tile_rows + rows, LANES), bf16),) * tiles,
        in_specs=[SMEM] * 2 + [VMEM] * 5,
        out_specs=(VMEM,) * tiles,
        scratch_shapes=[pltpu.VMEM((tiles, rows, LANES), bf16)],
        compiler_params=params_of,
        cost_estimate=pl.CostEstimate(flops=3_000_000, bytes_accessed=4_000_000, transcendentals=0),
    )(me.reshape(1), sub_present, slc, params, sides, before, after)
    beside = [tiles - 1, 0, 1]
    far = list(range(2, tiles - 1))
    block = {0: messages[0], 1: fetched(messages, 1), tiles - 1: fetched(messages, tiles - 1)}
    held = lax.optimization_barrier((messages, block[1], block[tiles - 1]))[0]
    block.update({shift: fetched(held, shift) for shift in far})

    estimate, direction, _ = lax.optimization_barrier((estimate, direction, messages))
    fields = pl.pallas_call(
        fields_kernel,
        out_shape=(jax.ShapeDtypeStruct((3, epochs * look_rows, LANES), bf16),) * tiles,
        in_specs=[SMEM] + [VMEM] * 2,
        out_specs=(VMEM,) * tiles,
        compiler_params=params_of,
        cost_estimate=pl.CostEstimate(flops=1_000_000, bytes_accessed=2_000_000, transcendentals=0),
    )(me.reshape(1), estimate, direction)
    space = lax.axis_index("space")
    spaces = lax.axis_size("space")
    present = jnp.stack([space > 0, space < spaces - 1]).astype(f32)

    def halo(pieces):
        def border(from_row):
            cuts = [lax.dynamic_slice_in_dim(piece, from_row, HALO, axis=1).reshape(-1, LANES) for piece in pieces]
            return jnp.concatenate(cuts, axis=0)

        if spaces == 2:
            got = lax.ppermute(border(jnp.where(space == 0, rows - HALO, 0)), "space", [(0, 1), (1, 0)])
            return got, got
        return swapped(border(rows - HALO), border(0), "space")

    def by_rows(shift):
        return block[shift].reshape(-1, rows, LANES)

    def params_in(shift):
        return block[shift][tile_rows : tile_rows + epochs, PARAM_LANE : PARAM_LANE + 4 * SLOTS].astype(f32)

    def pairs_of(blocks, loaded):
        listed = jnp.concatenate([params_in(block) for block in blocks], axis=0)
        mate = jnp.arange(len(blocks) * epochs, dtype=jnp.int32)[:, None] + listed[:, :SLOTS].astype(jnp.int32)
        weight = listed[:, SLOTS : 2 * SLOTS] + listed[:, 2 * SLOTS : 3 * SLOTS] + listed[:, 3 * SLOTS :]
        return mate.reshape(-1), weight.reshape(-1)

    own_halo = halo([by_rows(0)])
    near_halo = halo([by_rows(1), by_rows(tiles - 1)])
    halos = {0: (own_halo, 0), 1: (near_halo, 0), tiles - 1: (near_halo, 1)}

    order = look_order(rows + 2 * HALO, HALO // LOOK - RADIUS)
    bands = column_bands()

    def pair_stage(loaded):
        own = loaded[:-1]
        listed = jnp.concatenate([params_in(shift) for shift in own], axis=0)
        mate = jnp.arange(len(own) * epochs, dtype=jnp.int32)[:, None] + listed[:, :SLOTS].astype(jnp.int32)
        weight = listed[:, SLOTS : 2 * SLOTS] + listed[:, 2 * SLOTS : 3 * SLOTS] + listed[:, 3 * SLOTS :]
        operands = []

        def index_of(array):
            for at, other in enumerate(operands):
                if other is array:
                    return at
            operands.append(array)
            return len(operands) - 1

        places = []
        for shift in loaded:
            (top, bottom), slot = halos[shift]
            place = index_of(block[shift]), index_of(top), index_of(bottom), slot * (2 * epochs + 1) * HALO
            places.append(place)
        here = len(loaded) * epochs
        owned = len(own) * epochs
        looks = (rows + 2 * HALO) // LOOK
        group = 2 * SLOTS
        batches = (len(loaded) + 1) // 2 * 2 + owned
        shape = jax.ShapeDtypeStruct((owned * SLOTS, look_rows, LANES), f32)
        return pl.pallas_call(
            functools.partial(pair_kernel, (epochs, rows, len(operands)), tuple(places)),
            out_shape=(shape, shape),
            in_specs=[SMEM] * 3 + [VMEM] * (3 + len(operands)),
            out_specs=(VMEM, VMEM),
            scratch_shapes=[
                pltpu.VMEM((batches * group * look_rows, LANES), f32),
                pltpu.VMEM((2 * here, LOOK, looks, LANES), f32),
                pltpu.VMEM((2 * here, looks, LANES), f32),
                pltpu.VMEM((batches * group * looks, LANES), f32),
                pltpu.VMEM((batches * 2 * looks, LANES), f32),
                pltpu.VMEM((batches * group * looks, LANES), f32),
            ],
            compiler_params=params_of,
            cost_estimate=pl.CostEstimate(flops=20_000_000, bytes_accessed=30_000_000, transcendentals=0),
        )(mate.reshape(-1), weight.reshape(-1), present, order, *bands, *operands)

    near_stage = beside
    far_stage = list(range(1, tiles))
    near_pairs = pair_stage(near_stage)
    held, fields, near_pairs = lax.optimization_barrier(([block[shift] for shift in far], fields, near_pairs))
    block.update(zip(far, held))
    far_halo = halo([by_rows(shift) for shift in far])
    halos.update({shift: (far_halo, at) for at, shift in enumerate(far)})
    field = [fields[0]] + [fetched(fields, shift) for shift in range(1, tiles)]
    far_pairs = pair_stage(far_stage)

    listed = jnp.concatenate([params_in(shift) for shift in range(tiles)], axis=0)
    partner = jnp.arange(total, dtype=jnp.int32)[:, None] + listed[:, :SLOTS].astype(jnp.int32)
    partner = lax.rem(partner, total).reshape(-1)
    stages = tuple((stage[0] * epochs, (len(stage) - 1) * epochs) for stage in (near_stage, far_stage))
    gradient, sums = pl.pallas_call(
        functools.partial(gradient_kernel, (tiles, epochs, stages)),
        out_shape=(
            jax.ShapeDtypeStruct((total, look_rows, LANES), f32),
            jax.ShapeDtypeStruct((8, LANES), f32),
        ),
        in_specs=[SMEM] + [VMEM] * (tiles + 4),
        out_specs=(VMEM, VMEM),
        scratch_shapes=[pltpu.VMEM((total, look_rows, LANES), f32)] * 2,
        compiler_params=params_of,
        cost_estimate=pl.CostEstimate(flops=10_000_000, bytes_accessed=8_000_000, transcendentals=0),
    )(partner, *field, near_pairs[0], far_pairs[0], near_pairs[1], far_pairs[1])

    place = ("space", "sub")
    count = spaces * lax.axis_size("sub")
    shared = [sums] + [lax.ppermute(sums, place, [(i, (i + by) % count) for i in range(count)]) for by in range(1, count)]
    pieces = pl.pallas_call(
        functools.partial(return_kernel, tiles),
        out_shape=(jax.ShapeDtypeStruct((epochs * look_rows + 8, LANES), f32),) * tiles,
        in_specs=[VMEM] * (1 + count),
        out_specs=(VMEM,) * tiles,
        compiler_params=params_of,
        cost_estimate=pl.CostEstimate(flops=10_000, bytes_accessed=1_000_000, transcendentals=0),
    )(gradient, *shared)
    returned = [pieces[0]] + [to_ahead(pieces[by], "epoch", by) for by in range(1, tiles)]
    cell_count = float(total * look_rows * spaces * columns * lax.axis_size("sub"))
    return pl.pallas_call(
        functools.partial(update_kernel, cell_count),
        out_shape=(jax.ShapeDtypeStruct(estimate.shape, f32),) * 2,
        in_specs=[SMEM] * 2 + [VMEM] * (2 + tiles),
        out_specs=(VMEM, VMEM),
        compiler_params=params_of,
        cost_estimate=pl.CostEstimate(flops=1_000_000, bytes_accessed=2_000_000, transcendentals=0),
    )(me.reshape(1), prev_mean, estimate, direction, *returned)


def on_device(slc, offsets, weights, estimate, direction, prev_mean):
    epochs, rows, columns = slc.shape[1:]
    fits = columns == LANES * lax.axis_size("epoch") and lax.axis_size("epoch") > 3
    fits = fits and 2 * epochs * SIDES <= PARAM_LANE and rows % HALO == 0 and epochs == 2 * SLOTS
    plan = transposed_plan if fits else ring_plan
    return plan(slc, offsets, weights, estimate, direction, prev_mean)


def solution(mesh):
    return jax.shard_map(
        on_device,
        mesh=mesh,
        in_specs=(
            P(None, ("groups", "epoch"), "space", "sub"),
            P(("groups", "epoch"), None),
            P(("groups", "epoch"), None),
            P(("groups", "epoch"), "space", "sub"),
            P(("groups", "epoch"), "space", "sub"),
            P(),
        ),
        out_specs=(P(("groups", "epoch"), "space", "sub"), P(("groups", "epoch"), "space", "sub")),
        check_vma=False,
    )
```

```python
import functools

import jax
import jax.numpy as jnp
import numpy as np
from jax import lax
from jax.experimental import pallas as pl
from jax.experimental.pallas import tpu as pltpu
from jax.sharding import PartitionSpec as P

SLOTS = 4
OFFS = 8
LOOK = 4
RADIUS = 3


EPSILON = 1e-06


def passed_along(x, axis, by):
    size = lax.axis_size(axis)
    return lax.ppermute(x, axis, [(i, (i + by) % size) for i in range(size)])


def extended_2(block, sides, width):
    for axis, dim in sides:
        count = lax.axis_size(axis)
        forward = [(i, i + 1) for i in range(count - 1)]
        backward = [(target, source) for source, target in forward]
        low = lax.ppermute(
            lax.slice_in_dim(block, block.shape[dim] - width, None, axis=dim), axis, forward
        )
        high = lax.ppermute(lax.slice_in_dim(block, 0, width, axis=dim), axis, backward)
        block = jnp.concatenate([low, block, high], axis=dim)
    return block


def looked_sum(field):
    shape = field.shape
    return jnp.sum(field.reshape(shape[:-2] + (shape[-2] // LOOK, LOOK, shape[-1])), axis=-2)


def window_sum(padded, axis):
    length = padded.shape[axis] - 2 * RADIUS
    total = lax.slice_in_dim(padded, 0, length, axis=axis)
    for shift_at in range(1, 2 * RADIUS + 1):
        total = total + lax.slice_in_dim(padded, shift_at, shift_at + length, axis=axis)
    return total


def ring_plan(slc, offsets, weights, estimate, direction, prev_mean):
    epochs_here = slc.shape[1]
    look_rows = slc.shape[2] // LOOK
    col_count = slc.shape[3]
    ahead = passed_along(slc, "epoch", -1)
    extended = jnp.concatenate([slc, ahead], axis=1)
    numbers = jnp.arange(epochs_here, dtype=jnp.int32)
    partner = numbers[:, None] + offsets
    own_real = slc[0].astype(jnp.float32)
    own_imag = slc[1].astype(jnp.float32)
    ext_real = extended[0].astype(jnp.float32)
    ext_imag = extended[1].astype(jnp.float32)
    powers = looked_sum(ext_real * ext_real + ext_imag * ext_imag)
    pieces = []
    for slot_index in range(SLOTS):
        mate_real = jnp.take(ext_real, partner[:, slot_index], axis=0)
        mate_imag = jnp.take(ext_imag, partner[:, slot_index], axis=0)
        pieces.append(looked_sum(own_real * mate_real + own_imag * mate_imag))
        pieces.append(looked_sum(own_imag * mate_real - own_real * mate_imag))
    pair_count = epochs_here * 2 * SLOTS
    stacked = jnp.concatenate(
        [jnp.stack(pieces, axis=1).reshape(pair_count, look_rows, col_count), powers], axis=0
    )
    padded = extended_2(stacked, (("space", 1), ("sub", 2)), RADIUS)
    boxed = window_sum(window_sum(padded, 1), 2)
    pair_boxed = boxed[:pair_count].reshape(epochs_here, 2 * SLOTS, look_rows, col_count)
    power_box = boxed[pair_count:]
    coh_real = pair_boxed[:, 0::2]
    coh_imag = pair_boxed[:, 1::2]
    denominator = power_box[:epochs_here, None] * jnp.take(power_box, partner, axis=0) + EPSILON
    coherence = (coh_real * coh_real + coh_imag * coh_imag) / denominator
    observed = coh_imag / jnp.sqrt(denominator)
    est_ahead = passed_along(estimate, "epoch", -1)
    est_extended = jnp.concatenate([estimate, est_ahead], axis=0)
    fitted = estimate[:, None] - jnp.take(est_extended, partner, axis=0)
    factor = weights[:, :, None, None] * coherence
    weighted = factor * (observed - fitted)
    flattened = weighted.reshape(epochs_here * SLOTS, look_rows * col_count)
    selector = (
        jnp.arange(epochs_here + OFFS, dtype=jnp.int32)[:, None] == partner.reshape(1, -1)
    ).astype(jnp.float32)
    gathered = jnp.dot(
        selector, flattened, precision=lax.Precision.HIGHEST, preferred_element_type=jnp.float32
    ).reshape(epochs_here + OFFS, look_rows, col_count)
    own_part = jnp.sum(weighted, axis=1) - gathered[:epochs_here]
    returned = passed_along(-gathered[epochs_here:], "epoch", 1)
    gradient = jnp.concatenate([own_part + returned, own_part[OFFS:]], axis=0)
    cell_count = float(
        epochs_here
        * lax.axis_size("epoch")
        * look_rows
        * lax.axis_size("space")
        * col_count
        * lax.axis_size("sub")
    )
    local_norm = jnp.sum(gradient * gradient)
    local_crossed = jnp.sum(gradient * direction)
    mean_before = prev_mean[0]
    fields_ahead = passed_along(
        jnp.stack([gradient, direction]).astype(jnp.bfloat16), "epoch", -1
    ).astype(jnp.float32)
    grad_extended = jnp.concatenate([gradient, fields_ahead[0]], axis=0)
    old_extended = jnp.concatenate([direction, fields_ahead[1]], axis=0)
    grad_spread = gradient[:, None] - jnp.take(grad_extended, partner, axis=0)
    old_spread = direction[:, None] - jnp.take(old_extended, partner, axis=0)
    totals = lax.psum(
        (
            local_norm,
            local_crossed,
            jnp.sum(factor * grad_spread * grad_spread),
            jnp.sum(factor * grad_spread * old_spread),
            jnp.sum(factor * old_spread * old_spread),
        ),
        ("epoch", "space", "sub"),
    )
    grad_norm, crossed, grad_term, mixed_term, old_term = totals
    momentum = grad_norm / cell_count / mean_before
    new_direction = gradient + momentum * direction
    curvature = grad_term + 2.0 * momentum * mixed_term + momentum * momentum * old_term
    along_sum = grad_norm + momentum * crossed
    step_size = along_sum / curvature
    return (estimate + step_size * new_direction, new_direction)


LANES = 128
SIDES = 2 * RADIUS
HALO = 16
PARAM_LANE = 96
VMEM = pl.BlockSpec(memory_space=pltpu.VMEM)
SMEM = pl.BlockSpec(memory_space=pltpu.SMEM)
VMEM_BYTES = 48 * 1024 * 1024


def split_two(value):
    high = value.astype(jnp.bfloat16)
    low = (value - high.astype(jnp.float32)).astype(jnp.bfloat16)
    return high, low


def edge_kernel(first, last, edge):
    epochs = first.shape[1]
    lane = lax.broadcasted_iota(jnp.int32, edge.shape, 1)
    total = jnp.zeros(edge.shape, jnp.float32)
    for part in range(2):
        for epoch in range(epochs):
            at = (part * epochs + epoch) * SIDES
            total = placed(lane, total, tile_of(last, part, epoch, 0), LANES - RADIUS, at)
            total = placed(lane, total, tile_of(first, part, epoch, 0), 0, at + RADIUS)
    edge[...] = total.astype(jnp.bfloat16)


def fields_kernel(me, estimate, direction, *fields):
    look_rows = estimate.shape[1]
    tiles = len(fields)
    for shift, out in enumerate(fields):
        tile = lax.rem(me[0] + shift, tiles)
        columns = pl.ds(pl.multiple_of(tile * LANES, LANES), LANES)
        for epoch in range(estimate.shape[0]):
            here = slice(epoch * look_rows, (epoch + 1) * look_rows)
            first, second = split_two(estimate[epoch, :, columns])
            out[0, here, :] = first
            out[1, here, :] = second
            out[2, here, :] = direction[epoch, :, columns].astype(jnp.bfloat16)


def tile_of(slc, part, epoch, tile):
    return slc[part, epoch, :, tile * LANES : (tile + 1) * LANES].astype(jnp.float32)


def placed(lane, total, source, start, target):
    moved = pltpu.roll(source, (target - start) % LANES, axis=1)
    return jnp.where((lane >= target) & (lane < target + RADIUS), moved, total)


def pack_kernel(me, present, slc, params, before, after, *refs):
    messages, strips = refs[:-1], refs[-1]
    tiles = len(messages)
    epochs = slc.shape[1]
    rows = slc.shape[2]
    lane = lax.broadcasted_iota(jnp.int32, (rows, LANES), 1)
    value = params[...]
    high = value.astype(jnp.bfloat16).astype(jnp.float32)
    middle = (value - high).astype(jnp.bfloat16).astype(jnp.float32)
    low = value - high - middle
    third = PARAM_LANE + 2 * SLOTS
    split = jnp.where(lane < third, high, jnp.where(lane < third + SLOTS, middle, low))
    split = jnp.where(lane >= PARAM_LANE, split, 0.0)
    inside = lane < 2 * epochs * SIDES
    for tile in range(tiles):
        total = split
        if tile == 0:
            edge = before[...].astype(jnp.float32) * present[0]
            total = jnp.where(inside & (lane % SIDES < RADIUS), edge, total)
        if tile == tiles - 1:
            edge = after[...].astype(jnp.float32) * present[1]
            total = jnp.where(inside & (lane % SIDES >= RADIUS), edge, total)
        for part in range(2):
            for epoch in range(epochs):
                at = (part * epochs + epoch) * SIDES
                if tile > 0:
                    total = placed(lane, total, tile_of(slc, part, epoch, tile - 1), LANES - RADIUS, at)
                if tile < tiles - 1:
                    total = placed(lane, total, tile_of(slc, part, epoch, tile + 1), 0, at + RADIUS)
        strips[tile] = total.astype(jnp.bfloat16)
    for tile in range(tiles):
        shift = lax.rem(tile - me[0] + tiles, tiles)
        for number, message in enumerate(messages):

            @pl.when(shift == number)
            def _():
                for part in range(2):
                    for epoch in range(epochs):
                        at = (part * epochs + epoch) * rows
                        message[at : at + rows, :] = slc[part, epoch, :, tile * LANES : (tile + 1) * LANES]
                message[2 * epochs * rows :, :] = strips[tile]


def look_order(from_rows, first):
    looks = from_rows // LOOK
    to = np.arange(from_rows)[:, None]
    at = np.arange(from_rows)[None, :]
    return jnp.asarray(at == (to + first) % looks * LOOK + to // looks, jnp.bfloat16)


def unpack_tiles(order, sources, main, first, columns_of):
    looks = order.shape[0] // LOOK
    for start in range(0, len(sources), 4):
        parts = jnp.concatenate([columns_of(source) for source in sources[start : start + 4]], axis=1)
        value = jnp.dot(order, parts, preferred_element_type=jnp.float32)
        for one in range(4):
            for look in range(LOOK):
                main[first[start + one], look] = value[look * looks : (look + 1) * looks, one * LANES : (one + 1) * LANES]


def unpack_rims(by_look, looks, rim, first):
    share = LANES // SLOTS
    lane = lax.broadcasted_iota(jnp.int32, (looks, LANES), 1)
    for at, place in enumerate(first):
        value = jnp.zeros((looks, LANES), jnp.float32)
        for look in range(LOOK):
            target = look * SIDES
            moved = pltpu.roll(by_look[look * looks : (look + 1) * looks], (target - at * SIDES) % LANES, axis=1)
            value = jnp.where((lane >= target) & (lane < target + SIDES), moved, value)
        spread = share
        while spread < LANES:
            value = value + pltpu.roll(value, spread, axis=1)
            spread = 2 * spread
        rim[place] = value


def column_bands():
    share = LANES // SLOTS
    at = np.arange(2 * LANES)[:, None] % LANES
    to = np.arange(LANES)[None, :]
    side = at % share % SIDES
    source = np.where(side < RADIUS, side - RADIUS, LANES + side - RADIUS)
    column = (to - at // share * share) % LANES
    inside = (column < RADIUS) | (column >= LANES - RADIUS)
    inside = inside & (at % share < LOOK * SIDES)
    band = np.abs(at - to) <= RADIUS
    rim_band = inside & (np.abs(source - column) <= RADIUS)
    return jnp.asarray(band, jnp.bfloat16), jnp.asarray(rim_band, jnp.bfloat16)


def mixed(values):
    lane = lax.broadcasted_iota(jnp.int32, values[0].shape, 1)
    result = values[-1]
    for slot in range(SLOTS - 1):
        result = jnp.where(lane < (SLOTS - 1 - slot) * (LANES // SLOTS), values[SLOTS - 2 - slot], result)
    return result


def power_batches(blocks, epochs, looks, main, rim, looked, rim_looked):
    total = blocks * epochs
    group = 2 * SLOTS
    for block in range(blocks):
        for piece in range(0, looks, 8):
            rows_at = slice(piece, piece + 8)
            for half in range(2):
                squares = []
                for slot in range(SLOTS):
                    channel = half * SLOTS + slot
                    epoch = block * epochs + channel
                    value = None
                    for look in range(LOOK):
                        real = main[epoch, look, rows_at]
                        imag = main[total + epoch, look, rows_at]
                        one = real * real + imag * imag
                        value = one if value is None else value + one
                    at = (block * group + channel) * looks + piece
                    looked[at : at + 8, :] = value
                    real = rim[epoch, rows_at]
                    imag = rim[total + epoch, rows_at]
                    squares.append(real * real + imag * imag)
                at = (block * 2 + half) * looks + piece
                rim_looked[at : at + 8, :] = mixed(squares)


def pair_batch(epoch, mates, total, main, rim):
    own_re, own_im = main[epoch], main[total + epoch]
    reals, imags = [], []
    for mate in mates:
        mate_re, mate_im = main[mate], main[total + mate]
        real = own_re[0] * mate_re[0] + own_im[0] * mate_im[0]
        imag = own_im[0] * mate_re[0] - own_re[0] * mate_im[0]
        for look in range(1, LOOK):
            real = real + (own_re[look] * mate_re[look] + own_im[look] * mate_im[look])
            imag = imag + (own_im[look] * mate_re[look] - own_re[look] * mate_im[look])
        reals.append(real)
        imags.append(imag)
    own_re, own_im = rim[epoch], rim[total + epoch]
    mate_re = mixed([rim[mate] for mate in mates])
    mate_im = mixed([rim[total + mate] for mate in mates])
    rims = [own_re * mate_re + own_im * mate_im, own_im * mate_re - own_re * mate_im]
    return reals + imags, rims


def put(ref, block, values):
    rows = sum(value.shape[0] for value in values)
    ref[pl.ds(pl.multiple_of(block * rows, rows), rows), :] = jnp.concatenate(values, axis=0)


def columns_summed(couple, looks, bands, looked, rim_looked):
    group = 2 * SLOTS
    f32 = jnp.float32
    at = pl.ds(pl.multiple_of(couple * (2 * group * looks), 2 * group * looks), 2 * group * looks)
    halves = jnp.concatenate(split_two(looked[at, :]), axis=1)
    value = jnp.dot(halves, bands[0], preferred_element_type=f32)
    at = pl.ds(pl.multiple_of(couple * (4 * looks), 4 * looks), 4 * looks)
    halves = jnp.concatenate(split_two(rim_looked[at, :]), axis=1)
    outer = jnp.dot(halves, bands[1], preferred_element_type=f32)
    lane = lax.broadcasted_iota(jnp.int32, (looks, LANES), 1)
    outside = (lane < RADIUS) | (lane >= LANES - RADIUS)
    results = []
    for channel in range(2 * group):
        batch, half, slot = channel // group, channel % group // SLOTS, channel % SLOTS
        row = (batch * 2 + half) * looks
        part = outer[row : row + looks]
        if slot > 0:
            part = pltpu.roll(part, LANES - slot * (LANES // SLOTS), axis=1)
        row = channel * looks
        results.append(value[row : row + looks] + jnp.where(outside, part, 0.0))
    return results


def rows_summed(channel, looks, look_rows, wide):
    first = channel * looks
    total = wide[pl.ds(first, look_rows), :]
    for shift in range(1, 2 * RADIUS + 1):
        total = total + wide[pl.ds(first + shift, look_rows), :]
    return total


def pair_couple(couple, total, partner, main, rim):
    products, rims = [], []
    for one in range(2):
        epoch = couple * 2 + one
        mates = [partner[epoch * SLOTS + slot] for slot in range(SLOTS)]
        more, more_rims = pair_batch(epoch, mates, total, main, rim)
        products += more
        rims += more_rims
    return products, rims


def clipped(value, last):
    return jnp.minimum(jnp.maximum(value, 0), last)


def pair_kernel(sizes, places, partner, weight, present, order, band, rim_band, *refs):
    epochs, rows, operands = sizes
    inputs = refs[:operands]
    factors, pulls, boxed, main, rim, looked, rim_looked, wide = refs[operands:]
    count = len(places)
    total = count * epochs
    own_total = total - epochs
    look_rows = rows // LOOK
    halo_looks = HALO // LOOK
    looks = look_rows + 2 * halo_looks
    full_rows = rows + 2 * HALO
    group = 2 * SLOTS

    at = lax.broadcasted_iota(jnp.int32, (full_rows, full_rows), 1)
    keep = jnp.where(at < HALO, present[0], jnp.where(at >= HALO + rows, present[1], 1.0))
    order = (order[...].astype(jnp.float32) * keep).astype(jnp.bfloat16)
    bands = band[...], rim_band[...]
    for block, (tile_at, top_at, bottom_at, top_row, bottom_row) in enumerate(places):
        tile, top, bottom = inputs[tile_at], inputs[top_at], inputs[bottom_at]

        def rows_of(at):
            above = top[top_row + at * HALO : top_row + (at + 1) * HALO, :]
            below = bottom[bottom_row + at * HALO : bottom_row + (at + 1) * HALO, :]
            return jnp.concatenate([above, tile[at * rows : (at + 1) * rows, :], below], axis=0)

        first = [part * total + block * epochs + epoch for part in range(2) for epoch in range(epochs)]
        unpack_tiles(order, range(2 * epochs), main, first, rows_of)
        by_look = jnp.dot(order, rows_of(2 * epochs), preferred_element_type=jnp.float32)
        unpack_rims(by_look, looks, rim, first)
    power_batches(count, epochs, looks, main, rim, looked, rim_looked)
    powers = (count + 1) // 2
    couples = own_total // 2

    def boxed_of(channel):
        return boxed[pl.ds(pl.multiple_of(channel * look_rows, look_rows), look_rows), :]

    def finished(couple):
        results = []
        for one in range(2):
            epoch = couple * 2 + one
            own_power = boxed_of(epoch)
            first = (2 * powers + epoch) * (group * look_rows)
            parts = boxed[pl.ds(pl.multiple_of(first, group * look_rows), group * look_rows), :]
            parts = parts.reshape(group, look_rows, LANES)
            for slot in range(SLOTS):
                pair = epoch * SLOTS + slot
                inverse = lax.rsqrt(own_power * boxed_of(partner[pair]) + EPSILON)
                unit_re = parts[slot] * inverse
                unit_im = parts[SLOTS + slot] * inverse
                factor = weight[pair] * (unit_re * unit_re + unit_im * unit_im)
                results.append((factor, factor * unit_im))
        return results

    def boxes(couple):
        return [rows_summed(couple * 2 * group + one, looks, look_rows, wide) for one in range(2 * group)]

    def turn(number, steps):
        if 3 in steps:
            results = finished(number - 3)
        if 2 in steps:
            sums = boxes(powers + number - 2)
        if 1 in steps:
            columns = columns_summed(powers + number - 1, looks, bands, looked, rim_looked)
        if 0 in steps:
            products, rims = pair_couple(number, total, partner, main, rim)
        if 3 in steps:
            for ref, values in zip((factors, pulls), zip(*results)):
                ref[pl.ds((number - 3) * 2 * SLOTS, 2 * SLOTS)] = jnp.stack(values)
        if 2 in steps:
            put(boxed, powers + number - 2, sums)
        if 1 in steps:
            put(wide, powers + number - 1, columns)
        if 0 in steps:
            put(looked, powers + number, products)
            put(rim_looked, powers + number, rims)

    for couple in range(powers):
        put(wide, couple, columns_summed(couple, looks, bands, looked, rim_looked))
    turn(0, (0,))
    for couple in range(powers):
        put(boxed, couple, boxes(couple))
    turn(1, (0, 1))
    turn(2, (0, 1, 2))
    pl.loop(3, couples)(lambda number: turn(number, (0, 1, 2, 3)))
    turn(couples, (1, 2, 3))
    turn(couples + 1, (2, 3))
    turn(couples + 2, (3,))


def gradient_kernel(sizes, partner, *refs):
    tiles, epochs, stages = sizes
    fields = refs[:tiles]
    factors = refs[tiles : tiles + len(stages)]
    pulls = refs[tiles + len(stages) : tiles + 2 * len(stages)]
    gradient, sums, est, old = refs[tiles + 2 * len(stages) :]
    look_rows = est.shape[1]
    total = tiles * epochs
    f32 = jnp.float32
    for block in range(tiles):

        @pl.loop(0, epochs, unroll=4)
        def _(epoch):
            here = pl.ds(pl.multiple_of(epoch * look_rows, look_rows), look_rows)
            est[block * epochs + epoch] = fields[block][0, here, :].astype(f32) + fields[block][1, here, :].astype(f32)
            old[block * epochs + epoch] = fields[block][2, here, :].astype(f32)
            gradient[block * epochs + epoch] = jnp.zeros((look_rows, LANES), f32)

    for stage, (first, own_total) in enumerate(stages):

        @pl.loop(0, own_total, unroll=2)
        def _(here):
            epoch = first + here
            epoch = jnp.where(epoch < total, epoch, epoch - total)
            own_est = est[epoch]
            own = jnp.zeros((look_rows, LANES), f32)
            mates = [partner[epoch * SLOTS + slot] for slot in range(SLOTS)]
            values = []
            for slot, mate in enumerate(mates):
                pair = here * SLOTS + slot
                weighted = pulls[stage][pair] - factors[stage][pair] * (own_est - est[mate])
                own = own + weighted
                values.append(weighted)
            for mate, weighted in zip(mates, values):
                gradient[mate] = gradient[mate] - weighted
            gradient[epoch] = gradient[epoch] + own

    zero = jnp.zeros((look_rows, LANES), f32)
    results = (zero,) * 5
    for stage, (first, own_total) in enumerate(stages):

        def totals(here, carry):
            norm, crossed, grad_term, mixed_term, old_term = carry
            epoch = first + here
            epoch = jnp.where(epoch < total, epoch, epoch - total)
            own_grad = gradient[epoch]
            own_old = old[epoch]
            norm = norm + own_grad * own_grad
            crossed = crossed + own_grad * own_old
            for slot in range(SLOTS):
                mate = partner[epoch * SLOTS + slot]
                factor = factors[stage][here * SLOTS + slot]
                grad_spread = own_grad - gradient[mate]
                old_spread = own_old - old[mate]
                pulled = factor * grad_spread
                grad_term = grad_term + pulled * grad_spread
                mixed_term = mixed_term + pulled * old_spread
                old_term = old_term + factor * old_spread * old_spread
            return norm, crossed, grad_term, mixed_term, old_term

        results = lax.fori_loop(0, own_total, totals, results, unroll=2)
    sums[...] = jnp.zeros(sums.shape, f32)
    for at, value in enumerate(results):
        sums[at : at + 1, :] = jnp.sum(value, axis=0, keepdims=True)


def return_kernel(tiles, gradient, *refs):
    pieces = refs[-tiles:]
    shared = refs[:-tiles]
    total = shared[0][...]
    for other in shared[1:]:
        total = total + other[...]
    epochs = gradient.shape[0] // len(pieces)
    look_rows = gradient.shape[1]
    for number, piece in enumerate(pieces):
        for epoch in range(epochs):
            piece[epoch * look_rows : (epoch + 1) * look_rows, :] = gradient[number * epochs + epoch]
        piece[epochs * look_rows :, :] = total


def update_kernel(cell_count, me, prev_mean, estimate, direction, *refs):
    new_estimate, new_direction = refs[-2:]
    pieces = refs[:-2]
    tiles = len(pieces)
    epochs = estimate.shape[0]
    look_rows = estimate.shape[1]
    total = pieces[0][epochs * look_rows :, :]
    for piece in pieces[1:]:
        total = total + piece[epochs * look_rows :, :]
    total = jnp.sum(total, axis=1, keepdims=True)
    grad_norm, crossed, grad_term, mixed, old_term = (total[at : at + 1, :] for at in range(5))
    momentum = grad_norm / cell_count / prev_mean[0]
    curvature = grad_term + 2.0 * momentum * mixed + momentum * momentum * old_term
    step = (grad_norm + momentum * crossed) / curvature
    momentum = jnp.broadcast_to(momentum, (look_rows, LANES))
    step = jnp.broadcast_to(step, (look_rows, LANES))
    for shift, piece in enumerate(pieces):
        tile = lax.rem(me[0] - shift + tiles, tiles)
        columns = pl.ds(pl.multiple_of(tile * LANES, LANES), LANES)
        for epoch in range(epochs):
            gradient = piece[epoch * look_rows : (epoch + 1) * look_rows, :]
            moved = gradient + momentum * direction[epoch, :, columns]
            new_direction[epoch, :, columns] = moved
            new_estimate[epoch, :, columns] = estimate[epoch, :, columns] + step * moved


def swapped(up, down, axis):
    size = lax.axis_size(axis)
    if size == 1:
        return jnp.zeros_like(up), jnp.zeros_like(down)
    if size == 2:
        first = lax.axis_index(axis) == 0
        got = lax.ppermute(jnp.where(first, up, down), axis, [(0, 1), (1, 0)])
        return got, got
    forward = [(i, i + 1) for i in range(size - 1)]
    backward = [(target, source) for source, target in forward]
    return lax.ppermute(up, axis, forward), lax.ppermute(down, axis, backward)


def to_ahead(x, axis, by):
    size = lax.axis_size(axis)
    return lax.ppermute(x, axis, [(i, (i + by) % size) for i in range(size)])


def transposed_plan(slc, offsets, weights, estimate, direction, prev_mean):
    f32 = jnp.float32
    bf16 = jnp.bfloat16
    tiles = lax.axis_size("epoch")
    me = lax.axis_index("epoch")
    epochs, rows, columns = slc.shape[1:]
    look_rows = rows // LOOK
    total = tiles * epochs
    tile_rows = 2 * epochs * rows
    params_of = pltpu.CompilerParams(vmem_limit_bytes=VMEM_BYTES)

    def fetched(messages, shift):
        return to_ahead(messages[tiles - shift], "epoch", tiles - shift)

    sub = lax.axis_index("sub")
    outer_tile = (2, epochs, rows, LANES)
    edge = pl.pallas_call(
        edge_kernel,
        out_shape=jax.ShapeDtypeStruct((rows, LANES), bf16),
        grid=(1,),
        in_specs=[
            pl.BlockSpec(outer_tile, lambda _: (0, 0, 0, 0)),
            pl.BlockSpec(outer_tile, lambda _: (0, 0, 0, tiles - 1)),
        ],
        out_specs=pl.BlockSpec((rows, LANES), lambda _: (0, 0)),
        compiler_params=params_of,
        cost_estimate=pl.CostEstimate(flops=1_000_000, bytes_accessed=1_000_000, transcendentals=0),
    )(slc, slc)
    before, after = swapped(edge, edge, "sub")
    params = jnp.zeros((rows, LANES), f32)
    listed = jnp.concatenate([offsets.astype(f32), weights, weights, weights], axis=1)
    params = lax.dynamic_update_slice(params, listed, (0, PARAM_LANE))
    sub_present = jnp.stack([sub > 0, sub < lax.axis_size("sub") - 1]).astype(f32)
    messages = pl.pallas_call(
        pack_kernel,
        out_shape=(jax.ShapeDtypeStruct((tile_rows + rows, LANES), bf16),) * tiles,
        in_specs=[SMEM] * 2 + [VMEM] * 4,
        out_specs=(VMEM,) * tiles,
        scratch_shapes=[pltpu.VMEM((tiles, rows, LANES), bf16)],
        compiler_params=params_of,
        cost_estimate=pl.CostEstimate(flops=3_000_000, bytes_accessed=4_000_000, transcendentals=0),
    )(me.reshape(1), sub_present, slc, params, before, after)
    space = lax.axis_index("space")
    spaces = lax.axis_size("space")
    present = jnp.stack([space > 0, space < spaces - 1]).astype(f32)

    def halo(pieces):
        def border(from_row):
            cuts = [lax.dynamic_slice_in_dim(piece, from_row, HALO, axis=1).reshape(-1, LANES) for piece in pieces]
            return jnp.concatenate(cuts, axis=0)

        if spaces == 2:
            got = lax.ppermute(border(jnp.where(space == 0, rows - HALO, 0)), "space", [(0, 1), (1, 0)])
            return got, got
        return swapped(border(rows - HALO), border(0), "space")

    beside = [tiles - 1, 0, 1]
    far = list(range(2, tiles - 1))
    block = {0: messages[0], 1: fetched(messages, 1), tiles - 1: fetched(messages, tiles - 1)}
    early = {0: halo([messages[0].reshape(-1, rows, LANES)])}
    ready = lax.optimization_barrier((messages, block[1]))[0]
    early.update({shift: halo([ready[shift].reshape(-1, rows, LANES)]) for shift in far})
    sent = {shift: messages[shift] for shift in far}
    for shift in far:
        borders = early[shift][:1] if spaces == 2 else early[shift]
        sent[shift] = jnp.concatenate((messages[shift],) + borders, axis=0)
    sent = lax.optimization_barrier((sent, block[1], block[tiles - 1]))[0]
    block.update({shift: fetched(sent, shift) for shift in far})

    estimate, direction, _ = lax.optimization_barrier((estimate, direction, messages))
    fields = pl.pallas_call(
        fields_kernel,
        out_shape=(jax.ShapeDtypeStruct((3, epochs * look_rows, LANES), bf16),) * tiles,
        in_specs=[SMEM] + [VMEM] * 2,
        out_specs=(VMEM,) * tiles,
        compiler_params=params_of,
        cost_estimate=pl.CostEstimate(flops=1_000_000, bytes_accessed=2_000_000, transcendentals=0),
    )(me.reshape(1), estimate, direction)
    def by_rows(shift):
        return block[shift].reshape(-1, rows, LANES)

    def params_in(shift):
        return block[shift][tile_rows : tile_rows + epochs, PARAM_LANE : PARAM_LANE + 4 * SLOTS].astype(f32)

    def pairs_of(blocks, loaded):
        listed = jnp.concatenate([params_in(block) for block in blocks], axis=0)
        mate = jnp.arange(len(blocks) * epochs, dtype=jnp.int32)[:, None] + listed[:, :SLOTS].astype(jnp.int32)
        weight = listed[:, SLOTS : 2 * SLOTS] + listed[:, 2 * SLOTS : 3 * SLOTS] + listed[:, 3 * SLOTS :]
        return mate.reshape(-1), weight.reshape(-1)

    border_rows = (2 * epochs + 1) * HALO
    near_halo = halo([by_rows(1), by_rows(tiles - 1)])
    halos = {0: early[0] + (0, 0), 1: near_halo + (0, 0), tiles - 1: near_halo + (border_rows, border_rows)}
    for shift in far:
        bottom_at = tile_rows + rows if spaces == 2 else tile_rows + rows + border_rows
        halos[shift] = block[shift], block[shift], tile_rows + rows, bottom_at

    order = look_order(rows + 2 * HALO, HALO // LOOK - RADIUS)
    bands = column_bands()

    def pair_stage(loaded):
        own = loaded[:-1]
        listed = jnp.concatenate([params_in(shift) for shift in own], axis=0)
        mate = jnp.arange(len(own) * epochs, dtype=jnp.int32)[:, None] + listed[:, :SLOTS].astype(jnp.int32)
        weight = listed[:, SLOTS : 2 * SLOTS] + listed[:, 2 * SLOTS : 3 * SLOTS] + listed[:, 3 * SLOTS :]
        operands = []

        def index_of(array):
            for at, other in enumerate(operands):
                if other is array:
                    return at
            operands.append(array)
            return len(operands) - 1

        places = []
        for shift in loaded:
            top, bottom, top_row, bottom_row = halos[shift]
            places.append((index_of(block[shift]), index_of(top), index_of(bottom), top_row, bottom_row))
        here = len(loaded) * epochs
        owned = len(own) * epochs
        looks = (rows + 2 * HALO) // LOOK
        group = 2 * SLOTS
        batches = (len(loaded) + 1) // 2 * 2 + owned
        shape = jax.ShapeDtypeStruct((owned * SLOTS, look_rows, LANES), f32)
        return pl.pallas_call(
            functools.partial(pair_kernel, (epochs, rows, len(operands)), tuple(places)),
            out_shape=(shape, shape),
            in_specs=[SMEM] * 3 + [VMEM] * (3 + len(operands)),
            out_specs=(VMEM, VMEM),
            scratch_shapes=[
                pltpu.VMEM((batches * group * look_rows, LANES), f32),
                pltpu.VMEM((2 * here, LOOK, looks, LANES), f32),
                pltpu.VMEM((2 * here, looks, LANES), f32),
                pltpu.VMEM((batches * group * looks, LANES), f32),
                pltpu.VMEM((batches * 2 * looks, LANES), f32),
                pltpu.VMEM((batches * group * looks, LANES), f32),
            ],
            compiler_params=params_of,
            cost_estimate=pl.CostEstimate(flops=20_000_000, bytes_accessed=30_000_000, transcendentals=0),
        )(mate.reshape(-1), weight.reshape(-1), present, order, *bands, *operands)

    near_stage = beside
    far_stage = list(range(1, tiles))
    near_pairs = pair_stage(near_stage)
    fields, near_pairs = lax.optimization_barrier((fields, near_pairs))
    field = [fields[0]] + [fetched(fields, shift) for shift in range(1, tiles)]
    far_pairs = pair_stage(far_stage)

    listed = jnp.concatenate([params_in(shift) for shift in range(tiles)], axis=0)
    partner = jnp.arange(total, dtype=jnp.int32)[:, None] + listed[:, :SLOTS].astype(jnp.int32)
    partner = lax.rem(partner, total).reshape(-1)
    stages = tuple((stage[0] * epochs, (len(stage) - 1) * epochs) for stage in (near_stage, far_stage))
    gradient, sums = pl.pallas_call(
        functools.partial(gradient_kernel, (tiles, epochs, stages)),
        out_shape=(
            jax.ShapeDtypeStruct((total, look_rows, LANES), f32),
            jax.ShapeDtypeStruct((8, LANES), f32),
        ),
        in_specs=[SMEM] + [VMEM] * (tiles + 4),
        out_specs=(VMEM, VMEM),
        scratch_shapes=[pltpu.VMEM((total, look_rows, LANES), f32)] * 2,
        compiler_params=params_of,
        cost_estimate=pl.CostEstimate(flops=10_000_000, bytes_accessed=8_000_000, transcendentals=0),
    )(partner, *field, near_pairs[0], far_pairs[0], near_pairs[1], far_pairs[1])

    place = ("space", "sub")
    count = spaces * lax.axis_size("sub")
    shared = [sums] + [lax.ppermute(sums, place, [(i, (i + by) % count) for i in range(count)]) for by in range(1, count)]
    pieces = pl.pallas_call(
        functools.partial(return_kernel, tiles),
        out_shape=(jax.ShapeDtypeStruct((epochs * look_rows + 8, LANES), f32),) * tiles,
        in_specs=[VMEM] * (1 + count),
        out_specs=(VMEM,) * tiles,
        compiler_params=params_of,
        cost_estimate=pl.CostEstimate(flops=10_000, bytes_accessed=1_000_000, transcendentals=0),
    )(gradient, *shared)
    returned = [pieces[0]] + [to_ahead(pieces[by], "epoch", by) for by in range(1, tiles)]
    cell_count = float(total * look_rows * spaces * columns * lax.axis_size("sub"))
    return pl.pallas_call(
        functools.partial(update_kernel, cell_count),
        out_shape=(jax.ShapeDtypeStruct(estimate.shape, f32),) * 2,
        in_specs=[SMEM] * 2 + [VMEM] * (2 + tiles),
        out_specs=(VMEM, VMEM),
        compiler_params=params_of,
        cost_estimate=pl.CostEstimate(flops=1_000_000, bytes_accessed=2_000_000, transcendentals=0),
    )(me.reshape(1), prev_mean, estimate, direction, *returned)


def on_device(slc, offsets, weights, estimate, direction, prev_mean):
    epochs, rows, columns = slc.shape[1:]
    fits = columns == LANES * lax.axis_size("epoch") and lax.axis_size("epoch") > 3
    fits = fits and 2 * epochs * SIDES <= PARAM_LANE and rows % HALO == 0 and epochs == 2 * SLOTS
    plan = transposed_plan if fits else ring_plan
    return plan(slc, offsets, weights, estimate, direction, prev_mean)


def solution(mesh):
    return jax.shard_map(
        on_device,
        mesh=mesh,
        in_specs=(
            P(None, ("groups", "epoch"), "space", "sub"),
            P(("groups", "epoch"), None),
            P(("groups", "epoch"), None),
            P(("groups", "epoch"), "space", "sub"),
            P(("groups", "epoch"), "space", "sub"),
            P(),
        ),
        out_specs=(P(("groups", "epoch"), "space", "sub"), P(("groups", "epoch"), "space", "sub")),
        check_vma=False,
    )
```

```python
import functools

import jax
import jax.numpy as jnp
import numpy as np
from jax import lax
from jax.experimental import pallas as pl
from jax.experimental.pallas import tpu as pltpu
from jax.sharding import PartitionSpec as P

SLOTS = 4
OFFS = 8
LOOK = 4
RADIUS = 3


EPSILON = 1e-06


def passed_along(x, axis, by):
    size = lax.axis_size(axis)
    return lax.ppermute(x, axis, [(i, (i + by) % size) for i in range(size)])


def extended_2(block, sides, width):
    for axis, dim in sides:
        count = lax.axis_size(axis)
        forward = [(i, i + 1) for i in range(count - 1)]
        backward = [(target, source) for source, target in forward]
        low = lax.ppermute(
            lax.slice_in_dim(block, block.shape[dim] - width, None, axis=dim), axis, forward
        )
        high = lax.ppermute(lax.slice_in_dim(block, 0, width, axis=dim), axis, backward)
        block = jnp.concatenate([low, block, high], axis=dim)
    return block


def looked_sum(field):
    shape = field.shape
    return jnp.sum(field.reshape(shape[:-2] + (shape[-2] // LOOK, LOOK, shape[-1])), axis=-2)


def window_sum(padded, axis):
    length = padded.shape[axis] - 2 * RADIUS
    total = lax.slice_in_dim(padded, 0, length, axis=axis)
    for shift_at in range(1, 2 * RADIUS + 1):
        total = total + lax.slice_in_dim(padded, shift_at, shift_at + length, axis=axis)
    return total


def ring_plan(slc, offsets, weights, estimate, direction, prev_mean):
    epochs_here = slc.shape[1]
    look_rows = slc.shape[2] // LOOK
    col_count = slc.shape[3]
    ahead = passed_along(slc, "epoch", -1)
    extended = jnp.concatenate([slc, ahead], axis=1)
    numbers = jnp.arange(epochs_here, dtype=jnp.int32)
    partner = numbers[:, None] + offsets
    own_real = slc[0].astype(jnp.float32)
    own_imag = slc[1].astype(jnp.float32)
    ext_real = extended[0].astype(jnp.float32)
    ext_imag = extended[1].astype(jnp.float32)
    powers = looked_sum(ext_real * ext_real + ext_imag * ext_imag)
    pieces = []
    for slot_index in range(SLOTS):
        mate_real = jnp.take(ext_real, partner[:, slot_index], axis=0)
        mate_imag = jnp.take(ext_imag, partner[:, slot_index], axis=0)
        pieces.append(looked_sum(own_real * mate_real + own_imag * mate_imag))
        pieces.append(looked_sum(own_imag * mate_real - own_real * mate_imag))
    pair_count = epochs_here * 2 * SLOTS
    stacked = jnp.concatenate(
        [jnp.stack(pieces, axis=1).reshape(pair_count, look_rows, col_count), powers], axis=0
    )
    padded = extended_2(stacked, (("space", 1), ("sub", 2)), RADIUS)
    boxed = window_sum(window_sum(padded, 1), 2)
    pair_boxed = boxed[:pair_count].reshape(epochs_here, 2 * SLOTS, look_rows, col_count)
    power_box = boxed[pair_count:]
    coh_real = pair_boxed[:, 0::2]
    coh_imag = pair_boxed[:, 1::2]
    denominator = power_box[:epochs_here, None] * jnp.take(power_box, partner, axis=0) + EPSILON
    coherence = (coh_real * coh_real + coh_imag * coh_imag) / denominator
    observed = coh_imag / jnp.sqrt(denominator)
    est_ahead = passed_along(estimate, "epoch", -1)
    est_extended = jnp.concatenate([estimate, est_ahead], axis=0)
    fitted = estimate[:, None] - jnp.take(est_extended, partner, axis=0)
    factor = weights[:, :, None, None] * coherence
    weighted = factor * (observed - fitted)
    flattened = weighted.reshape(epochs_here * SLOTS, look_rows * col_count)
    selector = (
        jnp.arange(epochs_here + OFFS, dtype=jnp.int32)[:, None] == partner.reshape(1, -1)
    ).astype(jnp.float32)
    gathered = jnp.dot(
        selector, flattened, precision=lax.Precision.HIGHEST, preferred_element_type=jnp.float32
    ).reshape(epochs_here + OFFS, look_rows, col_count)
    own_part = jnp.sum(weighted, axis=1) - gathered[:epochs_here]
    returned = passed_along(-gathered[epochs_here:], "epoch", 1)
    gradient = jnp.concatenate([own_part + returned, own_part[OFFS:]], axis=0)
    cell_count = float(
        epochs_here
        * lax.axis_size("epoch")
        * look_rows
        * lax.axis_size("space")
        * col_count
        * lax.axis_size("sub")
    )
    local_norm = jnp.sum(gradient * gradient)
    local_crossed = jnp.sum(gradient * direction)
    mean_before = prev_mean[0]
    fields_ahead = passed_along(
        jnp.stack([gradient, direction]).astype(jnp.bfloat16), "epoch", -1
    ).astype(jnp.float32)
    grad_extended = jnp.concatenate([gradient, fields_ahead[0]], axis=0)
    old_extended = jnp.concatenate([direction, fields_ahead[1]], axis=0)
    grad_spread = gradient[:, None] - jnp.take(grad_extended, partner, axis=0)
    old_spread = direction[:, None] - jnp.take(old_extended, partner, axis=0)
    totals = lax.psum(
        (
            local_norm,
            local_crossed,
            jnp.sum(factor * grad_spread * grad_spread),
            jnp.sum(factor * grad_spread * old_spread),
            jnp.sum(factor * old_spread * old_spread),
        ),
        ("epoch", "space", "sub"),
    )
    grad_norm, crossed, grad_term, mixed_term, old_term = totals
    momentum = grad_norm / cell_count / mean_before
    new_direction = gradient + momentum * direction
    curvature = grad_term + 2.0 * momentum * mixed_term + momentum * momentum * old_term
    along_sum = grad_norm + momentum * crossed
    step_size = along_sum / curvature
    return (estimate + step_size * new_direction, new_direction)


LANES = 128
SIDES = 2 * RADIUS
HALO = 16
PARAM_LANE = 96
VMEM = pl.BlockSpec(memory_space=pltpu.VMEM)
SMEM = pl.BlockSpec(memory_space=pltpu.SMEM)
VMEM_BYTES = 48 * 1024 * 1024


def split_two(value):
    high = value.astype(jnp.bfloat16)
    low = (value - high.astype(jnp.float32)).astype(jnp.bfloat16)
    return high, low


def edge_kernel(first, last, edge):
    epochs = first.shape[1]
    lane = lax.broadcasted_iota(jnp.int32, edge.shape, 1)
    total = jnp.zeros(edge.shape, jnp.float32)
    for part in range(2):
        for epoch in range(epochs):
            at = (part * epochs + epoch) * SIDES
            total = placed(lane, total, tile_of(last, part, epoch, 0), LANES - RADIUS, at)
            total = placed(lane, total, tile_of(first, part, epoch, 0), 0, at + RADIUS)
    edge[...] = total.astype(jnp.bfloat16)


def fields_kernel(me, estimate, direction, *fields):
    look_rows = estimate.shape[1]
    tiles = len(fields)
    for shift, out in enumerate(fields):
        tile = lax.rem(me[0] + shift, tiles)
        columns = pl.ds(pl.multiple_of(tile * LANES, LANES), LANES)
        for epoch in range(estimate.shape[0]):
            here = slice(epoch * look_rows, (epoch + 1) * look_rows)
            first, second = split_two(estimate[epoch, :, columns])
            out[0, here, :] = first
            out[1, here, :] = second
            out[2, here, :] = direction[epoch, :, columns].astype(jnp.bfloat16)


def tile_of(slc, part, epoch, tile):
    return slc[part, epoch, :, tile * LANES : (tile + 1) * LANES].astype(jnp.float32)


def placed(lane, total, source, start, target):
    moved = pltpu.roll(source, (target - start) % LANES, axis=1)
    return jnp.where((lane >= target) & (lane < target + RADIUS), moved, total)


def pack_kernel(me, present, slc, params, before, after, *refs):
    messages, strips = refs[:-1], refs[-1]
    tiles = len(messages)
    epochs = slc.shape[1]
    rows = slc.shape[2]
    lane = lax.broadcasted_iota(jnp.int32, (rows, LANES), 1)
    value = params[...]
    high = value.astype(jnp.bfloat16).astype(jnp.float32)
    middle = (value - high).astype(jnp.bfloat16).astype(jnp.float32)
    low = value - high - middle
    third = PARAM_LANE + 2 * SLOTS
    split = jnp.where(lane < third, high, jnp.where(lane < third + SLOTS, middle, low))
    split = jnp.where(lane >= PARAM_LANE, split, 0.0)
    inside = lane < 2 * epochs * SIDES
    for tile in range(tiles):
        total = split
        if tile == 0:
            edge = before[...].astype(jnp.float32) * present[0]
            total = jnp.where(inside & (lane % SIDES < RADIUS), edge, total)
        if tile == tiles - 1:
            edge = after[...].astype(jnp.float32) * present[1]
            total = jnp.where(inside & (lane % SIDES >= RADIUS), edge, total)
        for part in range(2):
            for epoch in range(epochs):
                at = (part * epochs + epoch) * SIDES
                if tile > 0:
                    total = placed(lane, total, tile_of(slc, part, epoch, tile - 1), LANES - RADIUS, at)
                if tile < tiles - 1:
                    total = placed(lane, total, tile_of(slc, part, epoch, tile + 1), 0, at + RADIUS)
        strips[tile] = total.astype(jnp.bfloat16)
    for tile in range(tiles):
        shift = lax.rem(tile - me[0] + tiles, tiles)
        for number, message in enumerate(messages):

            @pl.when(shift == number)
            def _():
                for part in range(2):
                    for epoch in range(epochs):
                        at = (part * epochs + epoch) * rows
                        message[at : at + rows, :] = slc[part, epoch, :, tile * LANES : (tile + 1) * LANES]
                message[2 * epochs * rows :, :] = strips[tile]


def look_order(from_rows, first):
    looks = from_rows // LOOK
    to = np.arange(from_rows)[:, None]
    at = np.arange(from_rows)[None, :]
    return jnp.asarray(at == (to + first) % looks * LOOK + to // looks, jnp.bfloat16)


def unpack_tiles(order, sources, main, first, columns_of):
    looks = order.shape[0] // LOOK
    for start in range(0, len(sources), 4):
        parts = jnp.concatenate([columns_of(source) for source in sources[start : start + 4]], axis=1)
        value = jnp.dot(order, parts, preferred_element_type=jnp.float32)
        for one in range(4):
            for look in range(LOOK):
                main[first[start + one], look] = value[look * looks : (look + 1) * looks, one * LANES : (one + 1) * LANES]


def unpack_rims(by_look, looks, rim, first):
    share = LANES // SLOTS
    lane = lax.broadcasted_iota(jnp.int32, (looks, LANES), 1)
    for at, place in enumerate(first):
        value = jnp.zeros((looks, LANES), jnp.float32)
        for look in range(LOOK):
            target = look * SIDES
            moved = pltpu.roll(by_look[look * looks : (look + 1) * looks], (target - at * SIDES) % LANES, axis=1)
            value = jnp.where((lane >= target) & (lane < target + SIDES), moved, value)
        spread = share
        while spread < LANES:
            value = value + pltpu.roll(value, spread, axis=1)
            spread = 2 * spread
        rim[place] = value


def column_bands():
    share = LANES // SLOTS
    at = np.arange(2 * LANES)[:, None] % LANES
    to = np.arange(LANES)[None, :]
    side = at % share % SIDES
    source = np.where(side < RADIUS, side - RADIUS, LANES + side - RADIUS)
    column = (to - at // share * share) % LANES
    inside = (column < RADIUS) | (column >= LANES - RADIUS)
    inside = inside & (at % share < LOOK * SIDES)
    band = np.abs(at - to) <= RADIUS
    rim_band = inside & (np.abs(source - column) <= RADIUS)
    return jnp.asarray(band, jnp.bfloat16), jnp.asarray(rim_band, jnp.bfloat16)


def mixed(values):
    lane = lax.broadcasted_iota(jnp.int32, values[0].shape, 1)
    result = values[-1]
    for slot in range(SLOTS - 1):
        result = jnp.where(lane < (SLOTS - 1 - slot) * (LANES // SLOTS), values[SLOTS - 2 - slot], result)
    return result


def power_batches(blocks, epochs, looks, main, rim, looked, rim_looked):
    total = blocks * epochs
    group = 2 * SLOTS
    for block in range(blocks):
        for piece in range(0, looks, 8):
            rows_at = slice(piece, piece + 8)
            for half in range(2):
                squares = []
                for slot in range(SLOTS):
                    channel = half * SLOTS + slot
                    epoch = block * epochs + channel
                    value = None
                    for look in range(LOOK):
                        real = main[epoch, look, rows_at]
                        imag = main[total + epoch, look, rows_at]
                        one = real * real + imag * imag
                        value = one if value is None else value + one
                    at = (block * group + channel) * looks + piece
                    looked[at : at + 8, :] = value
                    real = rim[epoch, rows_at]
                    imag = rim[total + epoch, rows_at]
                    squares.append(real * real + imag * imag)
                at = (block * 2 + half) * looks + piece
                rim_looked[at : at + 8, :] = mixed(squares)


def pair_batch(epoch, mates, total, main, rim):
    own_re, own_im = main[epoch], main[total + epoch]
    reals, imags = [], []
    for mate in mates:
        mate_re, mate_im = main[mate], main[total + mate]
        real = own_re[0] * mate_re[0] + own_im[0] * mate_im[0]
        imag = own_im[0] * mate_re[0] - own_re[0] * mate_im[0]
        for look in range(1, LOOK):
            real = real + (own_re[look] * mate_re[look] + own_im[look] * mate_im[look])
            imag = imag + (own_im[look] * mate_re[look] - own_re[look] * mate_im[look])
        reals.append(real)
        imags.append(imag)
    own_re, own_im = rim[epoch], rim[total + epoch]
    mate_re = mixed([rim[mate] for mate in mates])
    mate_im = mixed([rim[total + mate] for mate in mates])
    rims = [own_re * mate_re + own_im * mate_im, own_im * mate_re - own_re * mate_im]
    return reals + imags, rims


def put(ref, block, values):
    rows = sum(value.shape[0] for value in values)
    ref[pl.ds(pl.multiple_of(block * rows, rows), rows), :] = jnp.concatenate(values, axis=0)


def columns_summed(couple, looks, bands, looked, rim_looked):
    group = 2 * SLOTS
    f32 = jnp.float32
    at = pl.ds(pl.multiple_of(couple * (2 * group * looks), 2 * group * looks), 2 * group * looks)
    halves = jnp.concatenate(split_two(looked[at, :]), axis=1)
    value = jnp.dot(halves, bands[0], preferred_element_type=f32)
    at = pl.ds(pl.multiple_of(couple * (4 * looks), 4 * looks), 4 * looks)
    halves = jnp.concatenate(split_two(rim_looked[at, :]), axis=1)
    outer = jnp.dot(halves, bands[1], preferred_element_type=f32)
    lane = lax.broadcasted_iota(jnp.int32, (looks, LANES), 1)
    outside = (lane < RADIUS) | (lane >= LANES - RADIUS)
    results = []
    for channel in range(2 * group):
        batch, half, slot = channel // group, channel % group // SLOTS, channel % SLOTS
        row = (batch * 2 + half) * looks
        part = outer[row : row + looks]
        if slot > 0:
            part = pltpu.roll(part, LANES - slot * (LANES // SLOTS), axis=1)
        row = channel * looks
        results.append(value[row : row + looks] + jnp.where(outside, part, 0.0))
    return results


def rows_summed(channel, looks, look_rows, wide):
    first = channel * looks
    total = wide[pl.ds(first, look_rows), :]
    for shift in range(1, 2 * RADIUS + 1):
        total = total + wide[pl.ds(first + shift, look_rows), :]
    return total


def pair_couple(couple, total, partner, main, rim):
    products, rims = [], []
    for one in range(2):
        epoch = couple * 2 + one
        mates = [partner[epoch * SLOTS + slot] for slot in range(SLOTS)]
        more, more_rims = pair_batch(epoch, mates, total, main, rim)
        products += more
        rims += more_rims
    return products, rims


def clipped(value, last):
    return jnp.minimum(jnp.maximum(value, 0), last)


def pair_kernel(sizes, places, partner, weight, present, order, band, rim_band, *refs):
    epochs, rows, operands = sizes
    inputs = refs[:operands]
    factors, pulls, boxed, main, rim, looked, rim_looked, wide = refs[operands:]
    count = len(places)
    total = count * epochs
    look_rows = rows // LOOK
    halo_looks = HALO // LOOK
    looks = look_rows + 2 * halo_looks
    full_rows = rows + 2 * HALO
    group = 2 * SLOTS

    at = lax.broadcasted_iota(jnp.int32, (full_rows, full_rows), 1)
    keep = jnp.where(at < HALO, present[0], jnp.where(at >= HALO + rows, present[1], 1.0))
    order = (order[...].astype(jnp.float32) * keep).astype(jnp.bfloat16)
    bands = band[...], rim_band[...]
    for block, (tile_at, top_at, bottom_at, top_row, bottom_row) in enumerate(places):
        tile, top, bottom = inputs[tile_at], inputs[top_at], inputs[bottom_at]

        def rows_of(at):
            above = top[top_row + at * HALO : top_row + (at + 1) * HALO, :]
            below = bottom[bottom_row + at * HALO : bottom_row + (at + 1) * HALO, :]
            return jnp.concatenate([above, tile[at * rows : (at + 1) * rows, :], below], axis=0)

        first = [part * total + block * epochs + epoch for part in range(2) for epoch in range(epochs)]
        unpack_tiles(order, range(2 * epochs), main, first, rows_of)
        by_look = jnp.dot(order, rows_of(2 * epochs), preferred_element_type=jnp.float32)
        unpack_rims(by_look, looks, rim, first)
    power_batches(count, epochs, looks, main, rim, looked, rim_looked)
    powers = count // 2
    couples = total // 2

    def boxed_of(channel):
        return boxed[pl.ds(pl.multiple_of(channel * look_rows, look_rows), look_rows), :]

    def finished(couple):
        results = []
        for one in range(2):
            epoch = couple * 2 + one
            own_power = boxed_of(epoch)
            first = (2 * powers + epoch) * (group * look_rows)
            parts = boxed[pl.ds(pl.multiple_of(first, group * look_rows), group * look_rows), :]
            parts = parts.reshape(group, look_rows, LANES)
            for slot in range(SLOTS):
                pair = epoch * SLOTS + slot
                inverse = lax.rsqrt(own_power * boxed_of(partner[pair]) + EPSILON)
                unit_re = parts[slot] * inverse
                unit_im = parts[SLOTS + slot] * inverse
                factor = weight[pair] * (unit_re * unit_re + unit_im * unit_im)
                results.append((factor, factor * unit_im))
        return results

    def boxes(couple):
        return [rows_summed(couple * 2 * group + one, looks, look_rows, wide) for one in range(2 * group)]

    def turn(number, steps):
        if 3 in steps:
            results = finished(number - 3)
        if 2 in steps:
            sums = boxes(powers + number - 2)
        if 1 in steps:
            columns = columns_summed(powers + number - 1, looks, bands, looked, rim_looked)
        if 0 in steps:
            products, rims = pair_couple(number, total, partner, main, rim)
        if 3 in steps:
            for ref, values in zip((factors, pulls), zip(*results)):
                ref[pl.ds((number - 3) * 2 * SLOTS, 2 * SLOTS)] = jnp.stack(values)
        if 2 in steps:
            put(boxed, powers + number - 2, sums)
        if 1 in steps:
            put(wide, powers + number - 1, columns)
        if 0 in steps:
            put(looked, powers + number, products)
            put(rim_looked, powers + number, rims)

    for couple in range(powers):
        put(wide, couple, columns_summed(couple, looks, bands, looked, rim_looked))
    turn(0, (0,))
    for couple in range(powers):
        put(boxed, couple, boxes(couple))
    turn(1, (0, 1))
    turn(2, (0, 1, 2))
    pl.loop(3, couples)(lambda number: turn(number, (0, 1, 2, 3)))
    turn(couples, (1, 2, 3))
    turn(couples + 1, (2, 3))
    turn(couples + 2, (3,))


def gradient_kernel(sizes, partner, *refs):
    tiles, epochs = sizes
    fields = refs[:tiles]
    factors, pulls, gradient, sums, est, old = refs[tiles:]
    look_rows = est.shape[1]
    total = tiles * epochs
    f32 = jnp.float32
    for block in range(tiles):

        @pl.loop(0, epochs, unroll=4)
        def _(epoch):
            here = pl.ds(pl.multiple_of(epoch * look_rows, look_rows), look_rows)
            est[block * epochs + epoch] = fields[block][0, here, :].astype(f32) + fields[block][1, here, :].astype(f32)
            old[block * epochs + epoch] = fields[block][2, here, :].astype(f32)
            gradient[block * epochs + epoch] = jnp.zeros((look_rows, LANES), f32)

    @pl.loop(0, total, unroll=2)
    def _(epoch):
        own_est = est[epoch]
        own = jnp.zeros((look_rows, LANES), f32)
        mates = [partner[epoch * SLOTS + slot] for slot in range(SLOTS)]
        values = []
        for slot, mate in enumerate(mates):
            pair = epoch * SLOTS + slot
            weighted = pulls[pair] - factors[pair] * (own_est - est[mate])
            own = own + weighted
            values.append(weighted)
        for mate, weighted in zip(mates, values):
            gradient[mate] = gradient[mate] - weighted
        gradient[epoch] = gradient[epoch] + own

    def totals(epoch, carry):
        norm, crossed, grad_term, mixed_term, old_term = carry
        own_grad = gradient[epoch]
        own_old = old[epoch]
        norm = norm + own_grad * own_grad
        crossed = crossed + own_grad * own_old
        for slot in range(SLOTS):
            mate = partner[epoch * SLOTS + slot]
            factor = factors[epoch * SLOTS + slot]
            grad_spread = own_grad - gradient[mate]
            old_spread = own_old - old[mate]
            pulled = factor * grad_spread
            grad_term = grad_term + pulled * grad_spread
            mixed_term = mixed_term + pulled * old_spread
            old_term = old_term + factor * old_spread * old_spread
        return norm, crossed, grad_term, mixed_term, old_term

    zero = jnp.zeros((look_rows, LANES), f32)
    results = lax.fori_loop(0, total, totals, (zero,) * 5, unroll=2)
    sums[...] = jnp.zeros(sums.shape, f32)
    for at, value in enumerate(results):
        sums[at : at + 1, :] = jnp.sum(value, axis=0, keepdims=True)


def return_kernel(tiles, gradient, *refs):
    pieces = refs[-tiles:]
    shared = refs[:-tiles]
    total = shared[0][...]
    for other in shared[1:]:
        total = total + other[...]
    epochs = gradient.shape[0] // len(pieces)
    look_rows = gradient.shape[1]
    for number, piece in enumerate(pieces):
        for epoch in range(epochs):
            piece[epoch * look_rows : (epoch + 1) * look_rows, :] = gradient[number * epochs + epoch]
        piece[epochs * look_rows :, :] = total


def update_kernel(cell_count, me, prev_mean, estimate, direction, *refs):
    new_estimate, new_direction = refs[-2:]
    pieces = refs[:-2]
    tiles = len(pieces)
    epochs = estimate.shape[0]
    look_rows = estimate.shape[1]
    total = pieces[0][epochs * look_rows :, :]
    for piece in pieces[1:]:
        total = total + piece[epochs * look_rows :, :]
    total = jnp.sum(total, axis=1, keepdims=True)
    grad_norm, crossed, grad_term, mixed, old_term = (total[at : at + 1, :] for at in range(5))
    momentum = grad_norm / cell_count / prev_mean[0]
    curvature = grad_term + 2.0 * momentum * mixed + momentum * momentum * old_term
    step = (grad_norm + momentum * crossed) / curvature
    momentum = jnp.broadcast_to(momentum, (look_rows, LANES))
    step = jnp.broadcast_to(step, (look_rows, LANES))
    for shift, piece in enumerate(pieces):
        tile = lax.rem(me[0] - shift + tiles, tiles)
        columns = pl.ds(pl.multiple_of(tile * LANES, LANES), LANES)
        for epoch in range(epochs):
            gradient = piece[epoch * look_rows : (epoch + 1) * look_rows, :]
            moved = gradient + momentum * direction[epoch, :, columns]
            new_direction[epoch, :, columns] = moved
            new_estimate[epoch, :, columns] = estimate[epoch, :, columns] + step * moved


def swapped(up, down, axis):
    size = lax.axis_size(axis)
    if size == 1:
        return jnp.zeros_like(up), jnp.zeros_like(down)
    if size == 2:
        first = lax.axis_index(axis) == 0
        got = lax.ppermute(jnp.where(first, up, down), axis, [(0, 1), (1, 0)])
        return got, got
    forward = [(i, i + 1) for i in range(size - 1)]
    backward = [(target, source) for source, target in forward]
    return lax.ppermute(up, axis, forward), lax.ppermute(down, axis, backward)


def to_ahead(x, axis, by):
    size = lax.axis_size(axis)
    return lax.ppermute(x, axis, [(i, (i + by) % size) for i in range(size)])


def transposed_plan(slc, offsets, weights, estimate, direction, prev_mean):
    f32 = jnp.float32
    bf16 = jnp.bfloat16
    tiles = lax.axis_size("epoch")
    me = lax.axis_index("epoch")
    epochs, rows, columns = slc.shape[1:]
    look_rows = rows // LOOK
    total = tiles * epochs
    tile_rows = 2 * epochs * rows
    params_of = pltpu.CompilerParams(vmem_limit_bytes=VMEM_BYTES)

    def fetched(messages, shift):
        return to_ahead(messages[tiles - shift], "epoch", tiles - shift)

    sub = lax.axis_index("sub")
    outer_tile = (2, epochs, rows, LANES)
    edge = pl.pallas_call(
        edge_kernel,
        out_shape=jax.ShapeDtypeStruct((rows, LANES), bf16),
        grid=(1,),
        in_specs=[
            pl.BlockSpec(outer_tile, lambda _: (0, 0, 0, 0)),
            pl.BlockSpec(outer_tile, lambda _: (0, 0, 0, tiles - 1)),
        ],
        out_specs=pl.BlockSpec((rows, LANES), lambda _: (0, 0)),
        compiler_params=params_of,
        cost_estimate=pl.CostEstimate(flops=1_000_000, bytes_accessed=1_000_000, transcendentals=0),
    )(slc, slc)
    before, after = swapped(edge, edge, "sub")
    params = jnp.zeros((rows, LANES), f32)
    listed = jnp.concatenate([offsets.astype(f32), weights, weights, weights], axis=1)
    params = lax.dynamic_update_slice(params, listed, (0, PARAM_LANE))
    sub_present = jnp.stack([sub > 0, sub < lax.axis_size("sub") - 1]).astype(f32)
    messages = pl.pallas_call(
        pack_kernel,
        out_shape=(jax.ShapeDtypeStruct((tile_rows + rows, LANES), bf16),) * tiles,
        in_specs=[SMEM] * 2 + [VMEM] * 4,
        out_specs=(VMEM,) * tiles,
        scratch_shapes=[pltpu.VMEM((tiles, rows, LANES), bf16)],
        compiler_params=params_of,
        cost_estimate=pl.CostEstimate(flops=3_000_000, bytes_accessed=4_000_000, transcendentals=0),
    )(me.reshape(1), sub_present, slc, params, before, after)
    space = lax.axis_index("space")
    spaces = lax.axis_size("space")
    present = jnp.stack([space > 0, space < spaces - 1]).astype(f32)

    def halo(pieces):
        def border(from_row):
            cuts = [lax.dynamic_slice_in_dim(piece, from_row, HALO, axis=1).reshape(-1, LANES) for piece in pieces]
            return jnp.concatenate(cuts, axis=0)

        if spaces == 2:
            got = lax.ppermute(border(jnp.where(space == 0, rows - HALO, 0)), "space", [(0, 1), (1, 0)])
            return got, got
        return swapped(border(rows - HALO), border(0), "space")

    block = [messages[0]] + [fetched(messages, shift) for shift in range(1, tiles)]
    estimate, direction, _ = lax.optimization_barrier((estimate, direction, messages))
    fields = pl.pallas_call(
        fields_kernel,
        out_shape=(jax.ShapeDtypeStruct((3, epochs * look_rows, LANES), bf16),) * tiles,
        in_specs=[SMEM] + [VMEM] * 2,
        out_specs=(VMEM,) * tiles,
        compiler_params=params_of,
        cost_estimate=pl.CostEstimate(flops=1_000_000, bytes_accessed=2_000_000, transcendentals=0),
    )(me.reshape(1), estimate, direction)
    def params_in(shift):
        return block[shift][tile_rows : tile_rows + epochs, PARAM_LANE : PARAM_LANE + 4 * SLOTS].astype(f32)

    def pairs_of(blocks, loaded):
        listed = jnp.concatenate([params_in(block) for block in blocks], axis=0)
        mate = jnp.arange(len(blocks) * epochs, dtype=jnp.int32)[:, None] + listed[:, :SLOTS].astype(jnp.int32)
        weight = listed[:, SLOTS : 2 * SLOTS] + listed[:, 2 * SLOTS : 3 * SLOTS] + listed[:, 3 * SLOTS :]
        return mate.reshape(-1), weight.reshape(-1)

    halos = [halo([array.reshape(-1, rows, LANES)]) for array in block]
    late = lax.optimization_barrier((fields, block))[0]
    field = [fields[0]] + [fetched(late, shift) for shift in range(1, tiles)]

    listed = jnp.concatenate([params_in(shift) for shift in range(tiles)], axis=0)
    partner = jnp.arange(total, dtype=jnp.int32)[:, None] + listed[:, :SLOTS].astype(jnp.int32)
    partner = lax.rem(partner, total).reshape(-1)
    weight = listed[:, SLOTS : 2 * SLOTS] + listed[:, 2 * SLOTS : 3 * SLOTS] + listed[:, 3 * SLOTS :]
    order = look_order(rows + 2 * HALO, HALO // LOOK - RADIUS)
    bands = column_bands()
    operands = list(block)
    places = []
    for shift in range(tiles):
        top, bottom = halos[shift]
        operands.append(top)
        top_at = bottom_at = len(operands) - 1
        if bottom is not top:
            operands.append(bottom)
            bottom_at = len(operands) - 1
        places.append((shift, top_at, bottom_at, 0, 0))
    looks = (rows + 2 * HALO) // LOOK
    group = 2 * SLOTS
    batches = tiles + total
    shape = jax.ShapeDtypeStruct((total * SLOTS, look_rows, LANES), f32)
    factors, pulls = pl.pallas_call(
        functools.partial(pair_kernel, (epochs, rows, len(operands)), tuple(places)),
        out_shape=(shape, shape),
        in_specs=[SMEM] * 3 + [VMEM] * (3 + len(operands)),
        out_specs=(VMEM, VMEM),
        scratch_shapes=[
            pltpu.VMEM((batches * group * look_rows, LANES), f32),
            pltpu.VMEM((2 * total, LOOK, looks, LANES), f32),
            pltpu.VMEM((2 * total, looks, LANES), f32),
            pltpu.VMEM((batches * group * looks, LANES), f32),
            pltpu.VMEM((batches * 2 * looks, LANES), f32),
            pltpu.VMEM((batches * group * looks, LANES), f32),
        ],
        compiler_params=params_of,
        cost_estimate=pl.CostEstimate(flops=20_000_000, bytes_accessed=30_000_000, transcendentals=0),
    )(partner, weight.reshape(-1), present, order, *bands, *operands)
    gradient, sums = pl.pallas_call(
        functools.partial(gradient_kernel, (tiles, epochs)),
        out_shape=(
            jax.ShapeDtypeStruct((total, look_rows, LANES), f32),
            jax.ShapeDtypeStruct((8, LANES), f32),
        ),
        in_specs=[SMEM] + [VMEM] * (tiles + 2),
        out_specs=(VMEM, VMEM),
        scratch_shapes=[pltpu.VMEM((total, look_rows, LANES), f32)] * 2,
        compiler_params=params_of,
        cost_estimate=pl.CostEstimate(flops=10_000_000, bytes_accessed=8_000_000, transcendentals=0),
    )(partner, *field, factors, pulls)

    place = ("space", "sub")
    count = spaces * lax.axis_size("sub")
    shared = [sums] + [lax.ppermute(sums, place, [(i, (i + by) % count) for i in range(count)]) for by in range(1, count)]
    pieces = pl.pallas_call(
        functools.partial(return_kernel, tiles),
        out_shape=(jax.ShapeDtypeStruct((epochs * look_rows + 8, LANES), f32),) * tiles,
        in_specs=[VMEM] * (1 + count),
        out_specs=(VMEM,) * tiles,
        compiler_params=params_of,
        cost_estimate=pl.CostEstimate(flops=10_000, bytes_accessed=1_000_000, transcendentals=0),
    )(gradient, *shared)
    returned = [pieces[0]] + [to_ahead(pieces[by], "epoch", by) for by in range(1, tiles)]
    cell_count = float(total * look_rows * spaces * columns * lax.axis_size("sub"))
    return pl.pallas_call(
        functools.partial(update_kernel, cell_count),
        out_shape=(jax.ShapeDtypeStruct(estimate.shape, f32),) * 2,
        in_specs=[SMEM] * 2 + [VMEM] * (2 + tiles),
        out_specs=(VMEM, VMEM),
        compiler_params=params_of,
        cost_estimate=pl.CostEstimate(flops=1_000_000, bytes_accessed=2_000_000, transcendentals=0),
    )(me.reshape(1), prev_mean, estimate, direction, *returned)


def on_device(slc, offsets, weights, estimate, direction, prev_mean):
    epochs, rows, columns = slc.shape[1:]
    fits = columns == LANES * lax.axis_size("epoch") and lax.axis_size("epoch") % 2 == 0
    fits = fits and 2 * epochs * SIDES <= PARAM_LANE and rows % HALO == 0 and epochs == 2 * SLOTS
    plan = transposed_plan if fits else ring_plan
    return plan(slc, offsets, weights, estimate, direction, prev_mean)


def solution(mesh):
    return jax.shard_map(
        on_device,
        mesh=mesh,
        in_specs=(
            P(None, ("groups", "epoch"), "space", "sub"),
            P(("groups", "epoch"), None),
            P(("groups", "epoch"), None),
            P(("groups", "epoch"), "space", "sub"),
            P(("groups", "epoch"), "space", "sub"),
            P(),
        ),
        out_specs=(P(("groups", "epoch"), "space", "sub"), P(("groups", "epoch"), "space", "sub")),
        check_vma=False,
    )
```

```python
import functools

import jax
import jax.numpy as jnp
import numpy as np
from jax import lax
from jax.experimental import pallas as pl
from jax.experimental.pallas import tpu as pltpu
from jax.sharding import PartitionSpec as P

SLOTS = 4
OFFS = 8
LOOK = 4
RADIUS = 3


EPSILON = 1e-06


def passed_along(x, axis, by):
    size = lax.axis_size(axis)
    return lax.ppermute(x, axis, [(i, (i + by) % size) for i in range(size)])


def extended_2(block, sides, width):
    for axis, dim in sides:
        count = lax.axis_size(axis)
        forward = [(i, i + 1) for i in range(count - 1)]
        backward = [(target, source) for source, target in forward]
        low = lax.ppermute(
            lax.slice_in_dim(block, block.shape[dim] - width, None, axis=dim), axis, forward
        )
        high = lax.ppermute(lax.slice_in_dim(block, 0, width, axis=dim), axis, backward)
        block = jnp.concatenate([low, block, high], axis=dim)
    return block


def looked_sum(field):
    shape = field.shape
    return jnp.sum(field.reshape(shape[:-2] + (shape[-2] // LOOK, LOOK, shape[-1])), axis=-2)


def window_sum(padded, axis):
    length = padded.shape[axis] - 2 * RADIUS
    total = lax.slice_in_dim(padded, 0, length, axis=axis)
    for shift_at in range(1, 2 * RADIUS + 1):
        total = total + lax.slice_in_dim(padded, shift_at, shift_at + length, axis=axis)
    return total


def ring_plan(slc, offsets, weights, estimate, direction, prev_mean):
    epochs_here = slc.shape[1]
    look_rows = slc.shape[2] // LOOK
    col_count = slc.shape[3]
    ahead = passed_along(slc, "epoch", -1)
    extended = jnp.concatenate([slc, ahead], axis=1)
    numbers = jnp.arange(epochs_here, dtype=jnp.int32)
    partner = numbers[:, None] + offsets
    own_real = slc[0].astype(jnp.float32)
    own_imag = slc[1].astype(jnp.float32)
    ext_real = extended[0].astype(jnp.float32)
    ext_imag = extended[1].astype(jnp.float32)
    powers = looked_sum(ext_real * ext_real + ext_imag * ext_imag)
    pieces = []
    for slot_index in range(SLOTS):
        mate_real = jnp.take(ext_real, partner[:, slot_index], axis=0)
        mate_imag = jnp.take(ext_imag, partner[:, slot_index], axis=0)
        pieces.append(looked_sum(own_real * mate_real + own_imag * mate_imag))
        pieces.append(looked_sum(own_imag * mate_real - own_real * mate_imag))
    pair_count = epochs_here * 2 * SLOTS
    stacked = jnp.concatenate(
        [jnp.stack(pieces, axis=1).reshape(pair_count, look_rows, col_count), powers], axis=0
    )
    padded = extended_2(stacked, (("space", 1), ("sub", 2)), RADIUS)
    boxed = window_sum(window_sum(padded, 1), 2)
    pair_boxed = boxed[:pair_count].reshape(epochs_here, 2 * SLOTS, look_rows, col_count)
    power_box = boxed[pair_count:]
    coh_real = pair_boxed[:, 0::2]
    coh_imag = pair_boxed[:, 1::2]
    denominator = power_box[:epochs_here, None] * jnp.take(power_box, partner, axis=0) + EPSILON
    coherence = (coh_real * coh_real + coh_imag * coh_imag) / denominator
    observed = coh_imag / jnp.sqrt(denominator)
    est_ahead = passed_along(estimate, "epoch", -1)
    est_extended = jnp.concatenate([estimate, est_ahead], axis=0)
    fitted = estimate[:, None] - jnp.take(est_extended, partner, axis=0)
    factor = weights[:, :, None, None] * coherence
    weighted = factor * (observed - fitted)
    flattened = weighted.reshape(epochs_here * SLOTS, look_rows * col_count)
    selector = (
        jnp.arange(epochs_here + OFFS, dtype=jnp.int32)[:, None] == partner.reshape(1, -1)
    ).astype(jnp.float32)
    gathered = jnp.dot(
        selector, flattened, precision=lax.Precision.HIGHEST, preferred_element_type=jnp.float32
    ).reshape(epochs_here + OFFS, look_rows, col_count)
    own_part = jnp.sum(weighted, axis=1) - gathered[:epochs_here]
    returned = passed_along(-gathered[epochs_here:], "epoch", 1)
    gradient = jnp.concatenate([own_part + returned, own_part[OFFS:]], axis=0)
    cell_count = float(
        epochs_here
        * lax.axis_size("epoch")
        * look_rows
        * lax.axis_size("space")
        * col_count
        * lax.axis_size("sub")
    )
    local_norm = jnp.sum(gradient * gradient)
    local_crossed = jnp.sum(gradient * direction)
    mean_before = prev_mean[0]
    fields_ahead = passed_along(
        jnp.stack([gradient, direction]).astype(jnp.bfloat16), "epoch", -1
    ).astype(jnp.float32)
    grad_extended = jnp.concatenate([gradient, fields_ahead[0]], axis=0)
    old_extended = jnp.concatenate([direction, fields_ahead[1]], axis=0)
    grad_spread = gradient[:, None] - jnp.take(grad_extended, partner, axis=0)
    old_spread = direction[:, None] - jnp.take(old_extended, partner, axis=0)
    totals = lax.psum(
        (
            local_norm,
            local_crossed,
            jnp.sum(factor * grad_spread * grad_spread),
            jnp.sum(factor * grad_spread * old_spread),
            jnp.sum(factor * old_spread * old_spread),
        ),
        ("epoch", "space", "sub"),
    )
    grad_norm, crossed, grad_term, mixed_term, old_term = totals
    momentum = grad_norm / cell_count / mean_before
    new_direction = gradient + momentum * direction
    curvature = grad_term + 2.0 * momentum * mixed_term + momentum * momentum * old_term
    along_sum = grad_norm + momentum * crossed
    step_size = along_sum / curvature
    return (estimate + step_size * new_direction, new_direction)


LANES = 128
SIDES = 2 * RADIUS
HALO = 16
PARAM_LANE = 96
VMEM = pl.BlockSpec(memory_space=pltpu.VMEM)
SMEM = pl.BlockSpec(memory_space=pltpu.SMEM)
VMEM_BYTES = 48 * 1024 * 1024


def split_two(value):
    high = value.astype(jnp.bfloat16)
    low = (value - high.astype(jnp.float32)).astype(jnp.bfloat16)
    return high, low


def edge_kernel(first, last, edge):
    epochs = first.shape[1]
    lane = lax.broadcasted_iota(jnp.int32, edge.shape, 1)
    total = jnp.zeros(edge.shape, jnp.float32)
    for part in range(2):
        for epoch in range(epochs):
            at = (part * epochs + epoch) * SIDES
            total = placed(lane, total, tile_of(last, part, epoch, 0), LANES - RADIUS, at)
            total = placed(lane, total, tile_of(first, part, epoch, 0), 0, at + RADIUS)
    edge[...] = total.astype(jnp.bfloat16)


def fields_kernel(me, estimate, direction, *fields):
    look_rows = estimate.shape[1]
    tiles = len(fields)
    for shift, out in enumerate(fields):
        tile = lax.rem(me[0] + shift, tiles)
        columns = pl.ds(pl.multiple_of(tile * LANES, LANES), LANES)
        for epoch in range(estimate.shape[0]):
            here = slice(epoch * look_rows, (epoch + 1) * look_rows)
            first, second = split_two(estimate[epoch, :, columns])
            out[0, here, :] = first
            out[1, here, :] = second
            out[2, here, :] = direction[epoch, :, columns].astype(jnp.bfloat16)


def tile_of(slc, part, epoch, tile):
    return slc[part, epoch, :, tile * LANES : (tile + 1) * LANES].astype(jnp.float32)


def placed(lane, total, source, start, target):
    moved = pltpu.roll(source, (target - start) % LANES, axis=1)
    return jnp.where((lane >= target) & (lane < target + RADIUS), moved, total)


def pack_kernel(me, present, slc, params, before, after, *refs):
    messages, strips = refs[:-1], refs[-1]
    tiles = len(messages)
    epochs = slc.shape[1]
    rows = slc.shape[2]
    lane = lax.broadcasted_iota(jnp.int32, (rows, LANES), 1)
    value = params[...]
    high = value.astype(jnp.bfloat16).astype(jnp.float32)
    middle = (value - high).astype(jnp.bfloat16).astype(jnp.float32)
    low = value - high - middle
    third = PARAM_LANE + 2 * SLOTS
    split = jnp.where(lane < third, high, jnp.where(lane < third + SLOTS, middle, low))
    split = jnp.where(lane >= PARAM_LANE, split, 0.0)
    inside = lane < 2 * epochs * SIDES
    for tile in range(tiles):
        total = split
        if tile == 0:
            edge = before[...].astype(jnp.float32) * present[0]
            total = jnp.where(inside & (lane % SIDES < RADIUS), edge, total)
        if tile == tiles - 1:
            edge = after[...].astype(jnp.float32) * present[1]
            total = jnp.where(inside & (lane % SIDES >= RADIUS), edge, total)
        for part in range(2):
            for epoch in range(epochs):
                at = (part * epochs + epoch) * SIDES
                if tile > 0:
                    total = placed(lane, total, tile_of(slc, part, epoch, tile - 1), LANES - RADIUS, at)
                if tile < tiles - 1:
                    total = placed(lane, total, tile_of(slc, part, epoch, tile + 1), 0, at + RADIUS)
        strips[tile] = total.astype(jnp.bfloat16)
    for tile in range(tiles):
        shift = lax.rem(tile - me[0] + tiles, tiles)
        for number, message in enumerate(messages):

            @pl.when(shift == number)
            def _():
                for part in range(2):
                    for epoch in range(epochs):
                        at = (part * epochs + epoch) * rows
                        message[at : at + rows, :] = slc[part, epoch, :, tile * LANES : (tile + 1) * LANES]
                message[2 * epochs * rows :, :] = strips[tile]


def look_order(from_rows, first):
    looks = from_rows // LOOK
    to = np.arange(from_rows)[:, None]
    at = np.arange(from_rows)[None, :]
    return jnp.asarray(at == (to + first) % looks * LOOK + to // looks, jnp.bfloat16)


def unpack_tiles(order, sources, main, first, columns_of):
    looks = order.shape[0] // LOOK
    for start in range(0, len(sources), 4):
        parts = jnp.concatenate([columns_of(source) for source in sources[start : start + 4]], axis=1)
        value = jnp.dot(order, parts, preferred_element_type=jnp.float32)
        for one in range(4):
            for look in range(LOOK):
                main[first[start + one], look] = value[look * looks : (look + 1) * looks, one * LANES : (one + 1) * LANES]


def unpack_rims(by_look, looks, rim, first):
    share = LANES // SLOTS
    lane = lax.broadcasted_iota(jnp.int32, (looks, LANES), 1)
    for at, place in enumerate(first):
        value = jnp.zeros((looks, LANES), jnp.float32)
        for look in range(LOOK):
            target = look * SIDES
            moved = pltpu.roll(by_look[look * looks : (look + 1) * looks], (target - at * SIDES) % LANES, axis=1)
            value = jnp.where((lane >= target) & (lane < target + SIDES), moved, value)
        spread = share
        while spread < LANES:
            value = value + pltpu.roll(value, spread, axis=1)
            spread = 2 * spread
        rim[place] = value


def column_bands():
    share = LANES // SLOTS
    at = np.arange(2 * LANES)[:, None] % LANES
    to = np.arange(LANES)[None, :]
    side = at % share % SIDES
    source = np.where(side < RADIUS, side - RADIUS, LANES + side - RADIUS)
    column = (to - at // share * share) % LANES
    inside = (column < RADIUS) | (column >= LANES - RADIUS)
    inside = inside & (at % share < LOOK * SIDES)
    band = np.abs(at - to) <= RADIUS
    rim_band = inside & (np.abs(source - column) <= RADIUS)
    return jnp.asarray(band, jnp.bfloat16), jnp.asarray(rim_band, jnp.bfloat16)


def mixed(values):
    lane = lax.broadcasted_iota(jnp.int32, values[0].shape, 1)
    result = values[-1]
    for slot in range(SLOTS - 1):
        result = jnp.where(lane < (SLOTS - 1 - slot) * (LANES // SLOTS), values[SLOTS - 2 - slot], result)
    return result


def power_batches(blocks, epochs, looks, main, rim, looked, rim_looked):
    total = blocks * epochs
    group = 2 * SLOTS
    for block in range(blocks):
        for piece in range(0, looks, 8):
            rows_at = slice(piece, piece + 8)
            for half in range(2):
                squares = []
                for slot in range(SLOTS):
                    channel = half * SLOTS + slot
                    epoch = block * epochs + channel
                    value = None
                    for look in range(LOOK):
                        real = main[epoch, look, rows_at]
                        imag = main[total + epoch, look, rows_at]
                        one = real * real + imag * imag
                        value = one if value is None else value + one
                    at = (block * group + channel) * looks + piece
                    looked[at : at + 8, :] = value
                    real = rim[epoch, rows_at]
                    imag = rim[total + epoch, rows_at]
                    squares.append(real * real + imag * imag)
                at = (block * 2 + half) * looks + piece
                rim_looked[at : at + 8, :] = mixed(squares)


def pair_batch(epoch, mates, total, main, rim):
    own_re, own_im = main[epoch], main[total + epoch]
    reals, imags = [], []
    for mate in mates:
        mate_re, mate_im = main[mate], main[total + mate]
        real = own_re[0] * mate_re[0] + own_im[0] * mate_im[0]
        imag = own_im[0] * mate_re[0] - own_re[0] * mate_im[0]
        for look in range(1, LOOK):
            real = real + (own_re[look] * mate_re[look] + own_im[look] * mate_im[look])
            imag = imag + (own_im[look] * mate_re[look] - own_re[look] * mate_im[look])
        reals.append(real)
        imags.append(imag)
    own_re, own_im = rim[epoch], rim[total + epoch]
    mate_re = mixed([rim[mate] for mate in mates])
    mate_im = mixed([rim[total + mate] for mate in mates])
    rims = [own_re * mate_re + own_im * mate_im, own_im * mate_re - own_re * mate_im]
    return reals + imags, rims


def put(ref, block, values):
    rows = sum(value.shape[0] for value in values)
    ref[block * rows : (block + 1) * rows, :] = jnp.concatenate(values, axis=0)


def columns_summed(couple, looks, bands, looked, rim_looked):
    group = 2 * SLOTS
    f32 = jnp.float32
    at = slice(couple * 2 * group * looks, (couple + 1) * 2 * group * looks)
    halves = jnp.concatenate(split_two(looked[at, :]), axis=1)
    value = jnp.dot(halves, bands[0], preferred_element_type=f32)
    at = slice(couple * 4 * looks, (couple + 1) * 4 * looks)
    halves = jnp.concatenate(split_two(rim_looked[at, :]), axis=1)
    outer = jnp.dot(halves, bands[1], preferred_element_type=f32)
    lane = lax.broadcasted_iota(jnp.int32, (looks, LANES), 1)
    outside = (lane < RADIUS) | (lane >= LANES - RADIUS)
    results = []
    for channel in range(2 * group):
        batch, half, slot = channel // group, channel % group // SLOTS, channel % SLOTS
        row = (batch * 2 + half) * looks
        part = outer[row : row + looks]
        if slot > 0:
            part = pltpu.roll(part, LANES - slot * (LANES // SLOTS), axis=1)
        row = channel * looks
        results.append(value[row : row + looks] + jnp.where(outside, part, 0.0))
    return results


def rows_summed(channel, looks, look_rows, wide):
    first = channel * looks
    total = wide[pl.ds(first, look_rows), :]
    for shift in range(1, 2 * RADIUS + 1):
        total = total + wide[pl.ds(first + shift, look_rows), :]
    return total


def pair_couple(couple, total, partner, main, rim):
    products, rims = [], []
    for one in range(2):
        epoch = couple * 2 + one
        mates = [partner[epoch * SLOTS + slot] for slot in range(SLOTS)]
        more, more_rims = pair_batch(epoch, mates, total, main, rim)
        products += more
        rims += more_rims
    return products, rims


def clipped(value, last):
    return jnp.minimum(jnp.maximum(value, 0), last)


def pair_kernel(sizes, places, partner, weight, present, order, band, rim_band, *refs):
    epochs, rows, operands = sizes
    inputs = refs[:operands]
    factors, pulls, boxed, main, rim, looked, rim_looked, wide = refs[operands:]
    count = len(places)
    total = count * epochs
    look_rows = rows // LOOK
    halo_looks = HALO // LOOK
    looks = look_rows + 2 * halo_looks
    full_rows = rows + 2 * HALO
    group = 2 * SLOTS

    at = lax.broadcasted_iota(jnp.int32, (full_rows, full_rows), 1)
    keep = jnp.where(at < HALO, present[0], jnp.where(at >= HALO + rows, present[1], 1.0))
    order = (order[...].astype(jnp.float32) * keep).astype(jnp.bfloat16)
    bands = band[...], rim_band[...]
    for block, (tile_at, top_at, bottom_at, top_row, bottom_row) in enumerate(places):
        tile, top, bottom = inputs[tile_at], inputs[top_at], inputs[bottom_at]

        def rows_of(at):
            above = top[top_row + at * HALO : top_row + (at + 1) * HALO, :]
            below = bottom[bottom_row + at * HALO : bottom_row + (at + 1) * HALO, :]
            return jnp.concatenate([above, tile[at * rows : (at + 1) * rows, :], below], axis=0)

        first = [part * total + block * epochs + epoch for part in range(2) for epoch in range(epochs)]
        unpack_tiles(order, range(2 * epochs), main, first, rows_of)
        by_look = jnp.dot(order, rows_of(2 * epochs), preferred_element_type=jnp.float32)
        unpack_rims(by_look, looks, rim, first)
    power_batches(count, epochs, looks, main, rim, looked, rim_looked)
    powers = count // 2
    couples = total // 2

    def boxed_of(channel):
        return boxed[pl.ds(pl.multiple_of(channel * look_rows, look_rows), look_rows), :]

    def finished(couple):
        results = []
        for one in range(2):
            epoch = couple * 2 + one
            own_power = boxed_of(epoch)
            first = (2 * powers + epoch) * (group * look_rows)
            parts = boxed[first : first + group * look_rows, :]
            parts = parts.reshape(group, look_rows, LANES)
            for slot in range(SLOTS):
                pair = epoch * SLOTS + slot
                inverse = lax.rsqrt(own_power * boxed_of(partner[pair]) + EPSILON)
                unit_re = parts[slot] * inverse
                unit_im = parts[SLOTS + slot] * inverse
                factor = weight[pair] * (unit_re * unit_re + unit_im * unit_im)
                results.append((factor, factor * unit_im))
        return results

    def boxes(couple):
        return [rows_summed(couple * 2 * group + one, looks, look_rows, wide) for one in range(2 * group)]

    def turn(number, steps):
        if 3 in steps:
            results = finished(number - 3)
        if 2 in steps:
            sums = boxes(powers + number - 2)
        if 1 in steps:
            columns = columns_summed(powers + number - 1, looks, bands, looked, rim_looked)
        if 0 in steps:
            products, rims = pair_couple(number, total, partner, main, rim)
        if 3 in steps:
            for ref, values in zip((factors, pulls), zip(*results)):
                ref[pl.ds((number - 3) * 2 * SLOTS, 2 * SLOTS)] = jnp.stack(values)
        if 2 in steps:
            put(boxed, powers + number - 2, sums)
        if 1 in steps:
            put(wide, powers + number - 1, columns)
        if 0 in steps:
            put(looked, powers + number, products)
            put(rim_looked, powers + number, rims)

    for couple in range(powers):
        put(wide, couple, columns_summed(couple, looks, bands, looked, rim_looked))
    turn(0, (0,))
    for couple in range(powers):
        put(boxed, couple, boxes(couple))
    turn(1, (0, 1))
    turn(2, (0, 1, 2))
    for number in range(3, couples):
        turn(number, (0, 1, 2, 3))
    turn(couples, (1, 2, 3))
    turn(couples + 1, (2, 3))
    turn(couples + 2, (3,))


def gradient_kernel(sizes, partner, *refs):
    tiles, epochs = sizes
    fields = refs[:tiles]
    factors, pulls, gradient, sums, est, old = refs[tiles:]
    look_rows = est.shape[1]
    total = tiles * epochs
    f32 = jnp.float32
    for block in range(tiles):

        @pl.loop(0, epochs, unroll=4)
        def _(epoch):
            here = pl.ds(pl.multiple_of(epoch * look_rows, look_rows), look_rows)
            est[block * epochs + epoch] = fields[block][0, here, :].astype(f32) + fields[block][1, here, :].astype(f32)
            old[block * epochs + epoch] = fields[block][2, here, :].astype(f32)
            gradient[block * epochs + epoch] = jnp.zeros((look_rows, LANES), f32)

    @pl.loop(0, total, unroll=2)
    def _(epoch):
        own_est = est[epoch]
        own = jnp.zeros((look_rows, LANES), f32)
        mates = [partner[epoch * SLOTS + slot] for slot in range(SLOTS)]
        values = []
        for slot, mate in enumerate(mates):
            pair = epoch * SLOTS + slot
            weighted = pulls[pair] - factors[pair] * (own_est - est[mate])
            own = own + weighted
            values.append(weighted)
        for mate, weighted in zip(mates, values):
            gradient[mate] = gradient[mate] - weighted
        gradient[epoch] = gradient[epoch] + own

    def totals(epoch, carry):
        norm, crossed, grad_term, mixed_term, old_term = carry
        own_grad = gradient[epoch]
        own_old = old[epoch]
        norm = norm + own_grad * own_grad
        crossed = crossed + own_grad * own_old
        for slot in range(SLOTS):
            mate = partner[epoch * SLOTS + slot]
            factor = factors[epoch * SLOTS + slot]
            grad_spread = own_grad - gradient[mate]
            old_spread = own_old - old[mate]
            pulled = factor * grad_spread
            grad_term = grad_term + pulled * grad_spread
            mixed_term = mixed_term + pulled * old_spread
            old_term = old_term + factor * old_spread * old_spread
        return norm, crossed, grad_term, mixed_term, old_term

    zero = jnp.zeros((look_rows, LANES), f32)
    results = lax.fori_loop(0, total, totals, (zero,) * 5, unroll=2)
    sums[...] = jnp.zeros(sums.shape, f32)
    for at, value in enumerate(results):
        sums[at : at + 1, :] = jnp.sum(value, axis=0, keepdims=True)


def return_kernel(tiles, gradient, *refs):
    pieces = refs[-tiles:]
    shared = refs[:-tiles]
    total = shared[0][...]
    for other in shared[1:]:
        total = total + other[...]
    epochs = gradient.shape[0] // len(pieces)
    look_rows = gradient.shape[1]
    for number, piece in enumerate(pieces):
        for epoch in range(epochs):
            piece[epoch * look_rows : (epoch + 1) * look_rows, :] = gradient[number * epochs + epoch]
        piece[epochs * look_rows :, :] = total


def update_kernel(cell_count, me, prev_mean, estimate, direction, *refs):
    new_estimate, new_direction = refs[-2:]
    pieces = refs[:-2]
    tiles = len(pieces)
    epochs = estimate.shape[0]
    look_rows = estimate.shape[1]
    total = pieces[0][epochs * look_rows :, :]
    for piece in pieces[1:]:
        total = total + piece[epochs * look_rows :, :]
    total = jnp.sum(total, axis=1, keepdims=True)
    grad_norm, crossed, grad_term, mixed, old_term = (total[at : at + 1, :] for at in range(5))
    momentum = grad_norm / cell_count / prev_mean[0]
    curvature = grad_term + 2.0 * momentum * mixed + momentum * momentum * old_term
    step = (grad_norm + momentum * crossed) / curvature
    momentum = jnp.broadcast_to(momentum, (look_rows, LANES))
    step = jnp.broadcast_to(step, (look_rows, LANES))
    for shift, piece in enumerate(pieces):
        tile = lax.rem(me[0] - shift + tiles, tiles)
        columns = pl.ds(pl.multiple_of(tile * LANES, LANES), LANES)
        for epoch in range(epochs):
            gradient = piece[epoch * look_rows : (epoch + 1) * look_rows, :]
            moved = gradient + momentum * direction[epoch, :, columns]
            new_direction[epoch, :, columns] = moved
            new_estimate[epoch, :, columns] = estimate[epoch, :, columns] + step * moved


def swapped(up, down, axis):
    size = lax.axis_size(axis)
    if size == 1:
        return jnp.zeros_like(up), jnp.zeros_like(down)
    if size == 2:
        first = lax.axis_index(axis) == 0
        got = lax.ppermute(jnp.where(first, up, down), axis, [(0, 1), (1, 0)])
        return got, got
    forward = [(i, i + 1) for i in range(size - 1)]
    backward = [(target, source) for source, target in forward]
    return lax.ppermute(up, axis, forward), lax.ppermute(down, axis, backward)


def to_ahead(x, axis, by):
    size = lax.axis_size(axis)
    return lax.ppermute(x, axis, [(i, (i + by) % size) for i in range(size)])


def transposed_plan(slc, offsets, weights, estimate, direction, prev_mean):
    f32 = jnp.float32
    bf16 = jnp.bfloat16
    tiles = lax.axis_size("epoch")
    me = lax.axis_index("epoch")
    epochs, rows, columns = slc.shape[1:]
    look_rows = rows // LOOK
    total = tiles * epochs
    tile_rows = 2 * epochs * rows
    params_of = pltpu.CompilerParams(vmem_limit_bytes=VMEM_BYTES)

    def fetched(messages, shift):
        return to_ahead(messages[tiles - shift], "epoch", tiles - shift)

    sub = lax.axis_index("sub")
    outer_tile = (2, epochs, rows, LANES)
    edge = pl.pallas_call(
        edge_kernel,
        out_shape=jax.ShapeDtypeStruct((rows, LANES), bf16),
        grid=(1,),
        in_specs=[
            pl.BlockSpec(outer_tile, lambda _: (0, 0, 0, 0)),
            pl.BlockSpec(outer_tile, lambda _: (0, 0, 0, tiles - 1)),
        ],
        out_specs=pl.BlockSpec((rows, LANES), lambda _: (0, 0)),
        compiler_params=params_of,
        cost_estimate=pl.CostEstimate(flops=1_000_000, bytes_accessed=1_000_000, transcendentals=0),
    )(slc, slc)
    before, after = swapped(edge, edge, "sub")
    params = jnp.zeros((rows, LANES), f32)
    listed = jnp.concatenate([offsets.astype(f32), weights, weights, weights], axis=1)
    params = lax.dynamic_update_slice(params, listed, (0, PARAM_LANE))
    sub_present = jnp.stack([sub > 0, sub < lax.axis_size("sub") - 1]).astype(f32)
    messages = pl.pallas_call(
        pack_kernel,
        out_shape=(jax.ShapeDtypeStruct((tile_rows + rows, LANES), bf16),) * tiles,
        in_specs=[SMEM] * 2 + [VMEM] * 4,
        out_specs=(VMEM,) * tiles,
        scratch_shapes=[pltpu.VMEM((tiles, rows, LANES), bf16)],
        compiler_params=params_of,
        cost_estimate=pl.CostEstimate(flops=3_000_000, bytes_accessed=4_000_000, transcendentals=0),
    )(me.reshape(1), sub_present, slc, params, before, after)
    space = lax.axis_index("space")
    spaces = lax.axis_size("space")
    present = jnp.stack([space > 0, space < spaces - 1]).astype(f32)

    def halo(pieces):
        def border(from_row):
            cuts = [lax.dynamic_slice_in_dim(piece, from_row, HALO, axis=1).reshape(-1, LANES) for piece in pieces]
            return jnp.concatenate(cuts, axis=0)

        if spaces == 2:
            got = lax.ppermute(border(jnp.where(space == 0, rows - HALO, 0)), "space", [(0, 1), (1, 0)])
            return got, got
        return swapped(border(rows - HALO), border(0), "space")

    block = [messages[0]] + [fetched(messages, shift) for shift in range(1, tiles)]
    estimate, direction, _ = lax.optimization_barrier((estimate, direction, messages))
    fields = pl.pallas_call(
        fields_kernel,
        out_shape=(jax.ShapeDtypeStruct((3, epochs * look_rows, LANES), bf16),) * tiles,
        in_specs=[SMEM] + [VMEM] * 2,
        out_specs=(VMEM,) * tiles,
        compiler_params=params_of,
        cost_estimate=pl.CostEstimate(flops=1_000_000, bytes_accessed=2_000_000, transcendentals=0),
    )(me.reshape(1), estimate, direction)
    def params_in(shift):
        return block[shift][tile_rows : tile_rows + epochs, PARAM_LANE : PARAM_LANE + 4 * SLOTS].astype(f32)

    def pairs_of(blocks, loaded):
        listed = jnp.concatenate([params_in(block) for block in blocks], axis=0)
        mate = jnp.arange(len(blocks) * epochs, dtype=jnp.int32)[:, None] + listed[:, :SLOTS].astype(jnp.int32)
        weight = listed[:, SLOTS : 2 * SLOTS] + listed[:, 2 * SLOTS : 3 * SLOTS] + listed[:, 3 * SLOTS :]
        return mate.reshape(-1), weight.reshape(-1)

    halos = [halo([array.reshape(-1, rows, LANES)]) for array in block]
    late = lax.optimization_barrier((fields, block))[0]
    field = [fields[0]] + [fetched(late, shift) for shift in range(1, tiles)]

    listed = jnp.concatenate([params_in(shift) for shift in range(tiles)], axis=0)
    partner = jnp.arange(total, dtype=jnp.int32)[:, None] + listed[:, :SLOTS].astype(jnp.int32)
    partner = lax.rem(partner, total).reshape(-1)
    weight = listed[:, SLOTS : 2 * SLOTS] + listed[:, 2 * SLOTS : 3 * SLOTS] + listed[:, 3 * SLOTS :]
    order = look_order(rows + 2 * HALO, HALO // LOOK - RADIUS)
    bands = column_bands()
    operands = list(block)
    places = []
    for shift in range(tiles):
        top, bottom = halos[shift]
        operands.append(top)
        top_at = bottom_at = len(operands) - 1
        if bottom is not top:
            operands.append(bottom)
            bottom_at = len(operands) - 1
        places.append((shift, top_at, bottom_at, 0, 0))
    looks = (rows + 2 * HALO) // LOOK
    group = 2 * SLOTS
    batches = tiles + total
    shape = jax.ShapeDtypeStruct((total * SLOTS, look_rows, LANES), f32)
    factors, pulls = pl.pallas_call(
        functools.partial(pair_kernel, (epochs, rows, len(operands)), tuple(places)),
        out_shape=(shape, shape),
        in_specs=[SMEM] * 3 + [VMEM] * (3 + len(operands)),
        out_specs=(VMEM, VMEM),
        scratch_shapes=[
            pltpu.VMEM((batches * group * look_rows, LANES), f32),
            pltpu.VMEM((2 * total, LOOK, looks, LANES), f32),
            pltpu.VMEM((2 * total, looks, LANES), f32),
            pltpu.VMEM((batches * group * looks, LANES), f32),
            pltpu.VMEM((batches * 2 * looks, LANES), f32),
            pltpu.VMEM((batches * group * looks, LANES), f32),
        ],
        compiler_params=params_of,
        cost_estimate=pl.CostEstimate(flops=20_000_000, bytes_accessed=30_000_000, transcendentals=0),
    )(partner, weight.reshape(-1), present, order, *bands, *operands)
    gradient, sums = pl.pallas_call(
        functools.partial(gradient_kernel, (tiles, epochs)),
        out_shape=(
            jax.ShapeDtypeStruct((total, look_rows, LANES), f32),
            jax.ShapeDtypeStruct((8, LANES), f32),
        ),
        in_specs=[SMEM] + [VMEM] * (tiles + 2),
        out_specs=(VMEM, VMEM),
        scratch_shapes=[pltpu.VMEM((total, look_rows, LANES), f32)] * 2,
        compiler_params=params_of,
        cost_estimate=pl.CostEstimate(flops=10_000_000, bytes_accessed=8_000_000, transcendentals=0),
    )(partner, *field, factors, pulls)

    place = ("space", "sub")
    count = spaces * lax.axis_size("sub")
    shared = [sums] + [lax.ppermute(sums, place, [(i, (i + by) % count) for i in range(count)]) for by in range(1, count)]
    pieces = pl.pallas_call(
        functools.partial(return_kernel, tiles),
        out_shape=(jax.ShapeDtypeStruct((epochs * look_rows + 8, LANES), f32),) * tiles,
        in_specs=[VMEM] * (1 + count),
        out_specs=(VMEM,) * tiles,
        compiler_params=params_of,
        cost_estimate=pl.CostEstimate(flops=10_000, bytes_accessed=1_000_000, transcendentals=0),
    )(gradient, *shared)
    returned = [pieces[0]] + [to_ahead(pieces[by], "epoch", by) for by in range(1, tiles)]
    cell_count = float(total * look_rows * spaces * columns * lax.axis_size("sub"))
    return pl.pallas_call(
        functools.partial(update_kernel, cell_count),
        out_shape=(jax.ShapeDtypeStruct(estimate.shape, f32),) * 2,
        in_specs=[SMEM] * 2 + [VMEM] * (2 + tiles),
        out_specs=(VMEM, VMEM),
        compiler_params=params_of,
        cost_estimate=pl.CostEstimate(flops=1_000_000, bytes_accessed=2_000_000, transcendentals=0),
    )(me.reshape(1), prev_mean, estimate, direction, *returned)


def on_device(slc, offsets, weights, estimate, direction, prev_mean):
    epochs, rows, columns = slc.shape[1:]
    fits = columns == LANES * lax.axis_size("epoch") and lax.axis_size("epoch") % 2 == 0
    fits = fits and 2 * epochs * SIDES <= PARAM_LANE and rows % HALO == 0 and epochs == 2 * SLOTS
    plan = transposed_plan if fits else ring_plan
    return plan(slc, offsets, weights, estimate, direction, prev_mean)


def solution(mesh):
    return jax.shard_map(
        on_device,
        mesh=mesh,
        in_specs=(
            P(None, ("groups", "epoch"), "space", "sub"),
            P(("groups", "epoch"), None),
            P(("groups", "epoch"), None),
            P(("groups", "epoch"), "space", "sub"),
            P(("groups", "epoch"), "space", "sub"),
            P(),
        ),
        out_specs=(P(("groups", "epoch"), "space", "sub"), P(("groups", "epoch"), "space", "sub")),
        check_vma=False,
    )
```

```python
import functools

import jax
import jax.numpy as jnp
import numpy as np
from jax import lax
from jax.experimental import pallas as pl
from jax.experimental.pallas import tpu as pltpu
from jax.sharding import PartitionSpec as P

SLOTS = 4
OFFS = 8
LOOK = 4
RADIUS = 3


EPSILON = 1e-06


def passed_along(x, axis, by):
    size = lax.axis_size(axis)
    return lax.ppermute(x, axis, [(i, (i + by) % size) for i in range(size)])


def extended_2(block, sides, width):
    for axis, dim in sides:
        count = lax.axis_size(axis)
        forward = [(i, i + 1) for i in range(count - 1)]
        backward = [(target, source) for source, target in forward]
        low = lax.ppermute(
            lax.slice_in_dim(block, block.shape[dim] - width, None, axis=dim), axis, forward
        )
        high = lax.ppermute(lax.slice_in_dim(block, 0, width, axis=dim), axis, backward)
        block = jnp.concatenate([low, block, high], axis=dim)
    return block


def looked_sum(field):
    shape = field.shape
    return jnp.sum(field.reshape(shape[:-2] + (shape[-2] // LOOK, LOOK, shape[-1])), axis=-2)


def window_sum(padded, axis):
    length = padded.shape[axis] - 2 * RADIUS
    total = lax.slice_in_dim(padded, 0, length, axis=axis)
    for shift_at in range(1, 2 * RADIUS + 1):
        total = total + lax.slice_in_dim(padded, shift_at, shift_at + length, axis=axis)
    return total


def ring_plan(slc, offsets, weights, estimate, direction, prev_mean):
    epochs_here = slc.shape[1]
    look_rows = slc.shape[2] // LOOK
    col_count = slc.shape[3]
    ahead = passed_along(slc, "epoch", -1)
    extended = jnp.concatenate([slc, ahead], axis=1)
    numbers = jnp.arange(epochs_here, dtype=jnp.int32)
    partner = numbers[:, None] + offsets
    own_real = slc[0].astype(jnp.float32)
    own_imag = slc[1].astype(jnp.float32)
    ext_real = extended[0].astype(jnp.float32)
    ext_imag = extended[1].astype(jnp.float32)
    powers = looked_sum(ext_real * ext_real + ext_imag * ext_imag)
    pieces = []
    for slot_index in range(SLOTS):
        mate_real = jnp.take(ext_real, partner[:, slot_index], axis=0)
        mate_imag = jnp.take(ext_imag, partner[:, slot_index], axis=0)
        pieces.append(looked_sum(own_real * mate_real + own_imag * mate_imag))
        pieces.append(looked_sum(own_imag * mate_real - own_real * mate_imag))
    pair_count = epochs_here * 2 * SLOTS
    stacked = jnp.concatenate(
        [jnp.stack(pieces, axis=1).reshape(pair_count, look_rows, col_count), powers], axis=0
    )
    padded = extended_2(stacked, (("space", 1), ("sub", 2)), RADIUS)
    boxed = window_sum(window_sum(padded, 1), 2)
    pair_boxed = boxed[:pair_count].reshape(epochs_here, 2 * SLOTS, look_rows, col_count)
    power_box = boxed[pair_count:]
    coh_real = pair_boxed[:, 0::2]
    coh_imag = pair_boxed[:, 1::2]
    denominator = power_box[:epochs_here, None] * jnp.take(power_box, partner, axis=0) + EPSILON
    coherence = (coh_real * coh_real + coh_imag * coh_imag) / denominator
    observed = coh_imag / jnp.sqrt(denominator)
    est_ahead = passed_along(estimate, "epoch", -1)
    est_extended = jnp.concatenate([estimate, est_ahead], axis=0)
    fitted = estimate[:, None] - jnp.take(est_extended, partner, axis=0)
    factor = weights[:, :, None, None] * coherence
    weighted = factor * (observed - fitted)
    flattened = weighted.reshape(epochs_here * SLOTS, look_rows * col_count)
    selector = (
        jnp.arange(epochs_here + OFFS, dtype=jnp.int32)[:, None] == partner.reshape(1, -1)
    ).astype(jnp.float32)
    gathered = jnp.dot(
        selector, flattened, precision=lax.Precision.HIGHEST, preferred_element_type=jnp.float32
    ).reshape(epochs_here + OFFS, look_rows, col_count)
    own_part = jnp.sum(weighted, axis=1) - gathered[:epochs_here]
    returned = passed_along(-gathered[epochs_here:], "epoch", 1)
    gradient = jnp.concatenate([own_part + returned, own_part[OFFS:]], axis=0)
    cell_count = float(
        epochs_here
        * lax.axis_size("epoch")
        * look_rows
        * lax.axis_size("space")
        * col_count
        * lax.axis_size("sub")
    )
    local_norm = jnp.sum(gradient * gradient)
    local_crossed = jnp.sum(gradient * direction)
    mean_before = prev_mean[0]
    fields_ahead = passed_along(
        jnp.stack([gradient, direction]).astype(jnp.bfloat16), "epoch", -1
    ).astype(jnp.float32)
    grad_extended = jnp.concatenate([gradient, fields_ahead[0]], axis=0)
    old_extended = jnp.concatenate([direction, fields_ahead[1]], axis=0)
    grad_spread = gradient[:, None] - jnp.take(grad_extended, partner, axis=0)
    old_spread = direction[:, None] - jnp.take(old_extended, partner, axis=0)
    totals = lax.psum(
        (
            local_norm,
            local_crossed,
            jnp.sum(factor * grad_spread * grad_spread),
            jnp.sum(factor * grad_spread * old_spread),
            jnp.sum(factor * old_spread * old_spread),
        ),
        ("epoch", "space", "sub"),
    )
    grad_norm, crossed, grad_term, mixed_term, old_term = totals
    momentum = grad_norm / cell_count / mean_before
    new_direction = gradient + momentum * direction
    curvature = grad_term + 2.0 * momentum * mixed_term + momentum * momentum * old_term
    along_sum = grad_norm + momentum * crossed
    step_size = along_sum / curvature
    return (estimate + step_size * new_direction, new_direction)


LANES = 128
SIDES = 2 * RADIUS
HALO = 16
FIELD_STEPS = 16383.0
PARAM_LANE = 96
VMEM = pl.BlockSpec(memory_space=pltpu.VMEM)
SMEM = pl.BlockSpec(memory_space=pltpu.SMEM)
VMEM_BYTES = 48 * 1024 * 1024


def split_two(value):
    high = value.astype(jnp.bfloat16)
    low = (value - high.astype(jnp.float32)).astype(jnp.bfloat16)
    return high, low


def edge_kernel(first, last, edge):
    epochs = first.shape[1]
    lane = lax.broadcasted_iota(jnp.int32, edge.shape, 1)
    total = jnp.zeros(edge.shape, jnp.float32)
    for part in range(2):
        for epoch in range(epochs):
            at = (part * epochs + epoch) * SIDES
            total = placed(lane, total, tile_of(last, part, epoch, 0), LANES - RADIUS, at)
            total = placed(lane, total, tile_of(first, part, epoch, 0), 0, at + RADIUS)
    edge[...] = total.astype(jnp.bfloat16)


def fixed_point(value):
    return jnp.floor(value * FIELD_STEPS + 0.5).astype(jnp.int32).astype(jnp.int16)


def from_fixed_point(value):
    return value.astype(jnp.int32).astype(jnp.float32) * (1.0 / FIELD_STEPS)


def fields_kernel(me, estimate, direction, *fields):
    look_rows = estimate.shape[1]
    tiles = len(fields)
    for shift, out in enumerate(fields):
        tile = lax.rem(me[0] + shift, tiles)
        columns = pl.ds(pl.multiple_of(tile * LANES, LANES), LANES)
        for epoch in range(estimate.shape[0]):
            here = slice(epoch * look_rows, (epoch + 1) * look_rows)
            out[0, here, :] = fixed_point(estimate[epoch, :, columns])
            out[1, here, :] = fixed_point(direction[epoch, :, columns])


def tile_of(slc, part, epoch, tile):
    return slc[part, epoch, :, tile * LANES : (tile + 1) * LANES].astype(jnp.float32)


def placed(lane, total, source, start, target):
    moved = pltpu.roll(source, (target - start) % LANES, axis=1)
    return jnp.where((lane >= target) & (lane < target + RADIUS), moved, total)


def pack_kernel(me, present, slc, params, before, after, *refs):
    messages, strips = refs[:-1], refs[-1]
    tiles = len(messages)
    epochs = slc.shape[1]
    rows = slc.shape[2]
    lane = lax.broadcasted_iota(jnp.int32, (rows, LANES), 1)
    value = params[...]
    high = value.astype(jnp.bfloat16).astype(jnp.float32)
    middle = (value - high).astype(jnp.bfloat16).astype(jnp.float32)
    low = value - high - middle
    third = PARAM_LANE + 2 * SLOTS
    split = jnp.where(lane < third, high, jnp.where(lane < third + SLOTS, middle, low))
    split = jnp.where(lane >= PARAM_LANE, split, 0.0)
    inside = lane < 2 * epochs * SIDES
    for tile in range(tiles):
        total = split
        if tile == 0:
            edge = before[...].astype(jnp.float32) * present[0]
            total = jnp.where(inside & (lane % SIDES < RADIUS), edge, total)
        if tile == tiles - 1:
            edge = after[...].astype(jnp.float32) * present[1]
            total = jnp.where(inside & (lane % SIDES >= RADIUS), edge, total)
        for part in range(2):
            for epoch in range(epochs):
                at = (part * epochs + epoch) * SIDES
                if tile > 0:
                    total = placed(lane, total, tile_of(slc, part, epoch, tile - 1), LANES - RADIUS, at)
                if tile < tiles - 1:
                    total = placed(lane, total, tile_of(slc, part, epoch, tile + 1), 0, at + RADIUS)
        strips[tile] = total.astype(jnp.bfloat16)
    for tile in range(tiles):
        shift = lax.rem(tile - me[0] + tiles, tiles)
        for number, message in enumerate(messages):

            @pl.when(shift == number)
            def _():
                for part in range(2):
                    for epoch in range(epochs):
                        at = (part * epochs + epoch) * rows
                        message[at : at + rows, :] = slc[part, epoch, :, tile * LANES : (tile + 1) * LANES]
                message[2 * epochs * rows :, :] = strips[tile]


def look_order(from_rows, first):
    looks = from_rows // LOOK
    to = np.arange(from_rows)[:, None]
    at = np.arange(from_rows)[None, :]
    return jnp.asarray(at == (to + first) % looks * LOOK + to // looks, jnp.bfloat16)


def unpack_tiles(order, sources, main, first, columns_of):
    looks = order.shape[0] // LOOK
    for start in range(0, len(sources), 4):
        parts = jnp.concatenate([columns_of(source) for source in sources[start : start + 4]], axis=1)
        value = jnp.dot(order, parts, preferred_element_type=jnp.float32)
        for one in range(4):
            for look in range(LOOK):
                main[first[start + one], look] = value[look * looks : (look + 1) * looks, one * LANES : (one + 1) * LANES]


def unpack_rims(by_look, looks, rim, first):
    share = LANES // SLOTS
    lane = lax.broadcasted_iota(jnp.int32, (looks, LANES), 1)
    for at, place in enumerate(first):
        value = jnp.zeros((looks, LANES), jnp.float32)
        for look in range(LOOK):
            target = look * SIDES
            moved = pltpu.roll(by_look[look * looks : (look + 1) * looks], (target - at * SIDES) % LANES, axis=1)
            value = jnp.where((lane >= target) & (lane < target + SIDES), moved, value)
        spread = share
        while spread < LANES:
            value = value + pltpu.roll(value, spread, axis=1)
            spread = 2 * spread
        rim[place] = value


def column_bands():
    share = LANES // SLOTS
    at = np.arange(2 * LANES)[:, None] % LANES
    to = np.arange(LANES)[None, :]
    side = at % share % SIDES
    source = np.where(side < RADIUS, side - RADIUS, LANES + side - RADIUS)
    column = (to - at // share * share) % LANES
    inside = (column < RADIUS) | (column >= LANES - RADIUS)
    inside = inside & (at % share < LOOK * SIDES)
    band = np.abs(at - to) <= RADIUS
    rim_band = inside & (np.abs(source - column) <= RADIUS)
    return jnp.asarray(band, jnp.bfloat16), jnp.asarray(rim_band, jnp.bfloat16)


def mixed(values):
    lane = lax.broadcasted_iota(jnp.int32, values[0].shape, 1)
    result = values[-1]
    for slot in range(SLOTS - 1):
        result = jnp.where(lane < (SLOTS - 1 - slot) * (LANES // SLOTS), values[SLOTS - 2 - slot], result)
    return result


def power_batches(blocks, epochs, looks, main, rim, looked, rim_looked):
    total = blocks * epochs
    group = 2 * SLOTS
    for block in range(blocks):
        for piece in range(0, looks, 8):
            rows_at = slice(piece, piece + 8)
            for half in range(2):
                squares = []
                for slot in range(SLOTS):
                    channel = half * SLOTS + slot
                    epoch = block * epochs + channel
                    value = None
                    for look in range(LOOK):
                        real = main[epoch, look, rows_at]
                        imag = main[total + epoch, look, rows_at]
                        one = real * real + imag * imag
                        value = one if value is None else value + one
                    at = (block * group + channel) * looks + piece
                    looked[at : at + 8, :] = value
                    real = rim[epoch, rows_at]
                    imag = rim[total + epoch, rows_at]
                    squares.append(real * real + imag * imag)
                at = (block * 2 + half) * looks + piece
                rim_looked[at : at + 8, :] = mixed(squares)


def pair_batch(epoch, mates, total, main, rim):
    own_re, own_im = main[epoch], main[total + epoch]
    reals, imags = [], []
    for mate in mates:
        mate_re, mate_im = main[mate], main[total + mate]
        real = own_re[0] * mate_re[0] + own_im[0] * mate_im[0]
        imag = own_im[0] * mate_re[0] - own_re[0] * mate_im[0]
        for look in range(1, LOOK):
            real = real + (own_re[look] * mate_re[look] + own_im[look] * mate_im[look])
            imag = imag + (own_im[look] * mate_re[look] - own_re[look] * mate_im[look])
        reals.append(real)
        imags.append(imag)
    own_re, own_im = rim[epoch], rim[total + epoch]
    mate_re = mixed([rim[mate] for mate in mates])
    mate_im = mixed([rim[total + mate] for mate in mates])
    rims = [own_re * mate_re + own_im * mate_im, own_im * mate_re - own_re * mate_im]
    return reals + imags, rims


def put(ref, block, values):
    rows = sum(value.shape[0] for value in values)
    ref[block * rows : (block + 1) * rows, :] = jnp.concatenate(values, axis=0)


def columns_summed(couple, looks, bands, looked, rim_looked):
    group = 2 * SLOTS
    f32 = jnp.float32
    at = slice(couple * 2 * group * looks, (couple + 1) * 2 * group * looks)
    halves = jnp.concatenate(split_two(looked[at, :]), axis=1)
    value = jnp.dot(halves, bands[0], preferred_element_type=f32)
    at = slice(couple * 4 * looks, (couple + 1) * 4 * looks)
    halves = jnp.concatenate(split_two(rim_looked[at, :]), axis=1)
    outer = jnp.dot(halves, bands[1], preferred_element_type=f32)
    lane = lax.broadcasted_iota(jnp.int32, (looks, LANES), 1)
    outside = (lane < RADIUS) | (lane >= LANES - RADIUS)
    results = []
    for channel in range(2 * group):
        batch, half, slot = channel // group, channel % group // SLOTS, channel % SLOTS
        row = (batch * 2 + half) * looks
        part = outer[row : row + looks]
        if slot > 0:
            part = pltpu.roll(part, LANES - slot * (LANES // SLOTS), axis=1)
        row = channel * looks
        results.append(value[row : row + looks] + jnp.where(outside, part, 0.0))
    return results


def rows_summed(channel, looks, look_rows, wide):
    first = channel * looks
    total = wide[pl.ds(first, look_rows), :]
    for shift in range(1, 2 * RADIUS + 1):
        total = total + wide[pl.ds(first + shift, look_rows), :]
    return total


def pair_couple(couple, total, partner, main, rim):
    products, rims = [], []
    for one in range(2):
        epoch = couple * 2 + one
        mates = [partner[epoch * SLOTS + slot] for slot in range(SLOTS)]
        more, more_rims = pair_batch(epoch, mates, total, main, rim)
        products += more
        rims += more_rims
    return products, rims


def clipped(value, last):
    return jnp.minimum(jnp.maximum(value, 0), last)


def pair_kernel(sizes, places, partner, weight, present, order, band, rim_band, *refs):
    epochs, rows, operands = sizes
    inputs = refs[:operands]
    factors, pulls, boxed, main, rim, looked, rim_looked, wide = refs[operands:]
    count = len(places)
    total = count * epochs
    look_rows = rows // LOOK
    halo_looks = HALO // LOOK
    looks = look_rows + 2 * halo_looks
    full_rows = rows + 2 * HALO
    group = 2 * SLOTS

    at = lax.broadcasted_iota(jnp.int32, (full_rows, full_rows), 1)
    keep = jnp.where(at < HALO, present[0], jnp.where(at >= HALO + rows, present[1], 1.0))
    order = (order[...].astype(jnp.float32) * keep).astype(jnp.bfloat16)
    bands = band[...], rim_band[...]
    for block, (tile_at, top_at, bottom_at, top_row, bottom_row) in enumerate(places):
        tile, top, bottom = inputs[tile_at], inputs[top_at], inputs[bottom_at]

        def rows_of(at):
            above = top[top_row + at * HALO : top_row + (at + 1) * HALO, :]
            below = bottom[bottom_row + at * HALO : bottom_row + (at + 1) * HALO, :]
            return jnp.concatenate([above, tile[at * rows : (at + 1) * rows, :], below], axis=0)

        first = [part * total + block * epochs + epoch for part in range(2) for epoch in range(epochs)]
        unpack_tiles(order, range(2 * epochs), main, first, rows_of)
        by_look = jnp.dot(order, rows_of(2 * epochs), preferred_element_type=jnp.float32)
        unpack_rims(by_look, looks, rim, first)
    power_batches(count, epochs, looks, main, rim, looked, rim_looked)
    powers = count // 2
    couples = total // 2

    def boxed_of(channel):
        return boxed[pl.ds(pl.multiple_of(channel * look_rows, look_rows), look_rows), :]

    def finished(couple):
        results = []
        for one in range(2):
            epoch = couple * 2 + one
            own_power = boxed_of(epoch)
            first = (2 * powers + epoch) * (group * look_rows)
            parts = boxed[first : first + group * look_rows, :]
            parts = parts.reshape(group, look_rows, LANES)
            for slot in range(SLOTS):
                pair = epoch * SLOTS + slot
                inverse = lax.rsqrt(own_power * boxed_of(partner[pair]) + EPSILON)
                unit_re = parts[slot] * inverse
                unit_im = parts[SLOTS + slot] * inverse
                factor = weight[pair] * (unit_re * unit_re + unit_im * unit_im)
                results.append((factor, factor * unit_im))
        return results

    def boxes(couple):
        return [rows_summed(couple * 2 * group + one, looks, look_rows, wide) for one in range(2 * group)]

    def turn(number, steps):
        if 3 in steps:
            results = finished(number - 3)
        if 2 in steps:
            sums = boxes(powers + number - 2)
        if 1 in steps:
            columns = columns_summed(powers + number - 1, looks, bands, looked, rim_looked)
        if 0 in steps:
            products, rims = pair_couple(number, total, partner, main, rim)
        if 3 in steps:
            for ref, values in zip((factors, pulls), zip(*results)):
                ref[pl.ds((number - 3) * 2 * SLOTS, 2 * SLOTS)] = jnp.stack(values)
        if 2 in steps:
            put(boxed, powers + number - 2, sums)
        if 1 in steps:
            put(wide, powers + number - 1, columns)
        if 0 in steps:
            put(looked, powers + number, products)
            put(rim_looked, powers + number, rims)

    for couple in range(powers):
        put(wide, couple, columns_summed(couple, looks, bands, looked, rim_looked))
    turn(0, (0,))
    for couple in range(powers):
        put(boxed, couple, boxes(couple))
    turn(1, (0, 1))
    turn(2, (0, 1, 2))
    for number in range(3, couples):
        turn(number, (0, 1, 2, 3))
    turn(couples, (1, 2, 3))
    turn(couples + 1, (2, 3))
    turn(couples + 2, (3,))


def gradient_kernel(sizes, partner, *refs):
    tiles, epochs = sizes
    fields = refs[:tiles]
    factors, pulls, gradient, sums, est, old, shares = refs[tiles:]
    look_rows = est.shape[1]
    total = tiles * epochs
    f32 = jnp.float32
    for block in range(tiles):
        for epoch in range(epochs):
            here = slice(epoch * look_rows, (epoch + 1) * look_rows)
            est[block * epochs + epoch] = from_fixed_point(fields[block][0, here, :])
            old[block * epochs + epoch] = from_fixed_point(fields[block][1, here, :])
    mates = [[partner[epoch * SLOTS + slot] for slot in range(SLOTS)] for epoch in range(total)]
    for epoch in range(total):
        own_est = est[epoch]
        own = None
        for slot, mate in enumerate(mates[epoch]):
            pair = epoch * SLOTS + slot
            weighted = pulls[pair] - factors[pair] * (own_est - est[mate])
            own = weighted if own is None else own + weighted
            shares[pair] = weighted
        gradient[epoch] = own
    for epoch in range(total):
        values = [gradient[mate] - shares[epoch * SLOTS + slot] for slot, mate in enumerate(mates[epoch])]
        for mate, value in zip(mates[epoch], values):
            gradient[mate] = value

    zero = jnp.zeros((look_rows, LANES), f32)
    norm, crossed, grad_term, mixed_term, old_term = (zero,) * 5
    for epoch in range(total):
        own_grad = gradient[epoch]
        own_old = old[epoch]
        norm = norm + own_grad * own_grad
        crossed = crossed + own_grad * own_old
        for slot, mate in enumerate(mates[epoch]):
            factor = factors[epoch * SLOTS + slot]
            grad_spread = own_grad - gradient[mate]
            old_spread = own_old - old[mate]
            pulled = factor * grad_spread
            grad_term = grad_term + pulled * grad_spread
            mixed_term = mixed_term + pulled * old_spread
            old_term = old_term + factor * old_spread * old_spread
    sums[...] = jnp.zeros(sums.shape, f32)
    for at, value in enumerate((norm, crossed, grad_term, mixed_term, old_term)):
        sums[at : at + 1, :] = jnp.sum(value, axis=0, keepdims=True)


def return_kernel(tiles, gradient, *refs):
    pieces = refs[-tiles:]
    shared = refs[:-tiles]
    total = shared[0][...]
    for other in shared[1:]:
        total = total + other[...]
    epochs = gradient.shape[0] // len(pieces)
    look_rows = gradient.shape[1]
    for number, piece in enumerate(pieces):
        for epoch in range(epochs):
            piece[epoch * look_rows : (epoch + 1) * look_rows, :] = gradient[number * epochs + epoch]
        piece[epochs * look_rows :, :] = total


def update_kernel(cell_count, me, prev_mean, estimate, direction, *refs):
    new_estimate, new_direction = refs[-2:]
    pieces = refs[:-2]
    tiles = len(pieces)
    epochs = estimate.shape[0]
    look_rows = estimate.shape[1]
    total = pieces[0][epochs * look_rows :, :]
    for piece in pieces[1:]:
        total = total + piece[epochs * look_rows :, :]
    total = jnp.sum(total, axis=1, keepdims=True)
    grad_norm, crossed, grad_term, mixed, old_term = (total[at : at + 1, :] for at in range(5))
    momentum = grad_norm / cell_count / prev_mean[0]
    curvature = grad_term + 2.0 * momentum * mixed + momentum * momentum * old_term
    step = (grad_norm + momentum * crossed) / curvature
    momentum = jnp.broadcast_to(momentum, (look_rows, LANES))
    step = jnp.broadcast_to(step, (look_rows, LANES))
    for shift, piece in enumerate(pieces):
        tile = lax.rem(me[0] - shift + tiles, tiles)
        columns = pl.ds(pl.multiple_of(tile * LANES, LANES), LANES)
        for epoch in range(epochs):
            gradient = piece[epoch * look_rows : (epoch + 1) * look_rows, :]
            moved = gradient + momentum * direction[epoch, :, columns]
            new_direction[epoch, :, columns] = moved
            new_estimate[epoch, :, columns] = estimate[epoch, :, columns] + step * moved


def swapped(up, down, axis):
    size = lax.axis_size(axis)
    if size == 1:
        return jnp.zeros_like(up), jnp.zeros_like(down)
    if size == 2:
        first = lax.axis_index(axis) == 0
        got = lax.ppermute(jnp.where(first, up, down), axis, [(0, 1), (1, 0)])
        return got, got
    forward = [(i, i + 1) for i in range(size - 1)]
    backward = [(target, source) for source, target in forward]
    return lax.ppermute(up, axis, forward), lax.ppermute(down, axis, backward)


def to_ahead(x, axis, by):
    size = lax.axis_size(axis)
    return lax.ppermute(x, axis, [(i, (i + by) % size) for i in range(size)])


def transposed_plan(slc, offsets, weights, estimate, direction, prev_mean):
    f32 = jnp.float32
    bf16 = jnp.bfloat16
    tiles = lax.axis_size("epoch")
    me = lax.axis_index("epoch")
    epochs, rows, columns = slc.shape[1:]
    look_rows = rows // LOOK
    total = tiles * epochs
    tile_rows = 2 * epochs * rows
    params_of = pltpu.CompilerParams(vmem_limit_bytes=VMEM_BYTES)

    def fetched(messages, shift):
        return to_ahead(messages[tiles - shift], "epoch", tiles - shift)

    sub = lax.axis_index("sub")
    outer_tile = (2, epochs, rows, LANES)
    edge = pl.pallas_call(
        edge_kernel,
        out_shape=jax.ShapeDtypeStruct((rows, LANES), bf16),
        grid=(1,),
        in_specs=[
            pl.BlockSpec(outer_tile, lambda _: (0, 0, 0, 0)),
            pl.BlockSpec(outer_tile, lambda _: (0, 0, 0, tiles - 1)),
        ],
        out_specs=pl.BlockSpec((rows, LANES), lambda _: (0, 0)),
        compiler_params=params_of,
        cost_estimate=pl.CostEstimate(flops=1_000_000, bytes_accessed=1_000_000, transcendentals=0),
    )(slc, slc)
    before, after = swapped(edge, edge, "sub")
    params = jnp.zeros((rows, LANES), f32)
    listed = jnp.concatenate([offsets.astype(f32), weights, weights, weights], axis=1)
    params = lax.dynamic_update_slice(params, listed, (0, PARAM_LANE))
    sub_present = jnp.stack([sub > 0, sub < lax.axis_size("sub") - 1]).astype(f32)
    messages = pl.pallas_call(
        pack_kernel,
        out_shape=(jax.ShapeDtypeStruct((tile_rows + rows, LANES), bf16),) * tiles,
        in_specs=[SMEM] * 2 + [VMEM] * 4,
        out_specs=(VMEM,) * tiles,
        scratch_shapes=[pltpu.VMEM((tiles, rows, LANES), bf16)],
        compiler_params=params_of,
        cost_estimate=pl.CostEstimate(flops=3_000_000, bytes_accessed=4_000_000, transcendentals=0),
    )(me.reshape(1), sub_present, slc, params, before, after)
    space = lax.axis_index("space")
    spaces = lax.axis_size("space")
    present = jnp.stack([space > 0, space < spaces - 1]).astype(f32)

    def halo(pieces):
        def border(from_row):
            cuts = [lax.dynamic_slice_in_dim(piece, from_row, HALO, axis=1).reshape(-1, LANES) for piece in pieces]
            return jnp.concatenate(cuts, axis=0)

        if spaces == 2:
            got = lax.ppermute(border(jnp.where(space == 0, rows - HALO, 0)), "space", [(0, 1), (1, 0)])
            return got, got
        return swapped(border(rows - HALO), border(0), "space")

    block = [messages[0]] + [fetched(messages, shift) for shift in range(1, tiles)]
    estimate, direction, _ = lax.optimization_barrier((estimate, direction, messages))
    fields = pl.pallas_call(
        fields_kernel,
        out_shape=(jax.ShapeDtypeStruct((2, epochs * look_rows, LANES), jnp.int16),) * tiles,
        in_specs=[SMEM] + [VMEM] * 2,
        out_specs=(VMEM,) * tiles,
        compiler_params=params_of,
        cost_estimate=pl.CostEstimate(flops=1_000_000, bytes_accessed=2_000_000, transcendentals=0),
    )(me.reshape(1), estimate, direction)
    def params_in(shift):
        return block[shift][tile_rows : tile_rows + epochs, PARAM_LANE : PARAM_LANE + 4 * SLOTS].astype(f32)

    def pairs_of(blocks, loaded):
        listed = jnp.concatenate([params_in(block) for block in blocks], axis=0)
        mate = jnp.arange(len(blocks) * epochs, dtype=jnp.int32)[:, None] + listed[:, :SLOTS].astype(jnp.int32)
        weight = listed[:, SLOTS : 2 * SLOTS] + listed[:, 2 * SLOTS : 3 * SLOTS] + listed[:, 3 * SLOTS :]
        return mate.reshape(-1), weight.reshape(-1)

    halos = [halo([array.reshape(-1, rows, LANES)]) for array in block]
    late = lax.optimization_barrier((fields, block))[0]
    field = [fields[0]] + [fetched(late, shift) for shift in range(1, tiles)]

    listed = jnp.concatenate([params_in(shift) for shift in range(tiles)], axis=0)
    partner = jnp.arange(total, dtype=jnp.int32)[:, None] + listed[:, :SLOTS].astype(jnp.int32)
    partner = lax.rem(partner, total).reshape(-1)
    weight = listed[:, SLOTS : 2 * SLOTS] + listed[:, 2 * SLOTS : 3 * SLOTS] + listed[:, 3 * SLOTS :]
    order = look_order(rows + 2 * HALO, HALO // LOOK - RADIUS)
    bands = column_bands()
    operands = list(block)
    places = []
    for shift in range(tiles):
        top, bottom = halos[shift]
        operands.append(top)
        top_at = bottom_at = len(operands) - 1
        if bottom is not top:
            operands.append(bottom)
            bottom_at = len(operands) - 1
        places.append((shift, top_at, bottom_at, 0, 0))
    looks = (rows + 2 * HALO) // LOOK
    group = 2 * SLOTS
    batches = tiles + total
    shape = jax.ShapeDtypeStruct((total * SLOTS, look_rows, LANES), f32)
    factors, pulls = pl.pallas_call(
        functools.partial(pair_kernel, (epochs, rows, len(operands)), tuple(places)),
        out_shape=(shape, shape),
        in_specs=[SMEM] * 3 + [VMEM] * (3 + len(operands)),
        out_specs=(VMEM, VMEM),
        scratch_shapes=[
            pltpu.VMEM((batches * group * look_rows, LANES), f32),
            pltpu.VMEM((2 * total, LOOK, looks, LANES), f32),
            pltpu.VMEM((2 * total, looks, LANES), f32),
            pltpu.VMEM((batches * group * looks, LANES), f32),
            pltpu.VMEM((batches * 2 * looks, LANES), f32),
            pltpu.VMEM((batches * group * looks, LANES), f32),
        ],
        compiler_params=params_of,
        cost_estimate=pl.CostEstimate(flops=20_000_000, bytes_accessed=30_000_000, transcendentals=0),
    )(partner, weight.reshape(-1), present, order, *bands, *operands)
    gradient, sums = pl.pallas_call(
        functools.partial(gradient_kernel, (tiles, epochs)),
        out_shape=(
            jax.ShapeDtypeStruct((total, look_rows, LANES), f32),
            jax.ShapeDtypeStruct((8, LANES), f32),
        ),
        in_specs=[SMEM] + [VMEM] * (tiles + 2),
        out_specs=(VMEM, VMEM),
        scratch_shapes=[pltpu.VMEM((total, look_rows, LANES), f32)] * 2
        + [pltpu.VMEM((total * SLOTS, look_rows, LANES), f32)],
        compiler_params=params_of,
        cost_estimate=pl.CostEstimate(flops=10_000_000, bytes_accessed=8_000_000, transcendentals=0),
    )(partner, *field, factors, pulls)

    place = ("space", "sub")
    count = spaces * lax.axis_size("sub")
    shared = [sums] + [lax.ppermute(sums, place, [(i, (i + by) % count) for i in range(count)]) for by in range(1, count)]
    pieces = pl.pallas_call(
        functools.partial(return_kernel, tiles),
        out_shape=(jax.ShapeDtypeStruct((epochs * look_rows + 8, LANES), f32),) * tiles,
        in_specs=[VMEM] * (1 + count),
        out_specs=(VMEM,) * tiles,
        compiler_params=params_of,
        cost_estimate=pl.CostEstimate(flops=10_000, bytes_accessed=1_000_000, transcendentals=0),
    )(gradient, *shared)
    returned = [pieces[0]] + [to_ahead(pieces[by], "epoch", by) for by in range(1, tiles)]
    cell_count = float(total * look_rows * spaces * columns * lax.axis_size("sub"))
    return pl.pallas_call(
        functools.partial(update_kernel, cell_count),
        out_shape=(jax.ShapeDtypeStruct(estimate.shape, f32),) * 2,
        in_specs=[SMEM] * 2 + [VMEM] * (2 + tiles),
        out_specs=(VMEM, VMEM),
        compiler_params=params_of,
        cost_estimate=pl.CostEstimate(flops=1_000_000, bytes_accessed=2_000_000, transcendentals=0),
    )(me.reshape(1), prev_mean, estimate, direction, *returned)


def on_device(slc, offsets, weights, estimate, direction, prev_mean):
    epochs, rows, columns = slc.shape[1:]
    fits = columns == LANES * lax.axis_size("epoch") and lax.axis_size("epoch") % 2 == 0
    fits = fits and 2 * epochs * SIDES <= PARAM_LANE and rows % HALO == 0 and epochs == 2 * SLOTS
    plan = transposed_plan if fits else ring_plan
    return plan(slc, offsets, weights, estimate, direction, prev_mean)


def solution(mesh):
    return jax.shard_map(
        on_device,
        mesh=mesh,
        in_specs=(
            P(None, ("groups", "epoch"), "space", "sub"),
            P(("groups", "epoch"), None),
            P(("groups", "epoch"), None),
            P(("groups", "epoch"), "space", "sub"),
            P(("groups", "epoch"), "space", "sub"),
            P(),
        ),
        out_specs=(P(("groups", "epoch"), "space", "sub"), P(("groups", "epoch"), "space", "sub")),
        check_vma=False,
    )
```

```python
import functools
import math

import jax
import jax.numpy as jnp
import numpy as np
from jax import lax
from jax.experimental import pallas as pl
from jax.experimental.pallas import tpu as pltpu
from jax.sharding import PartitionSpec as P

SLOTS = 4
OFFS = 8
LOOK = 4
RADIUS = 3


EPSILON = 1e-06


def passed_along(x, axis, by):
    size = lax.axis_size(axis)
    return lax.ppermute(x, axis, [(i, (i + by) % size) for i in range(size)])


def extended_2(block, sides, width):
    for axis, dim in sides:
        count = lax.axis_size(axis)
        forward = [(i, i + 1) for i in range(count - 1)]
        backward = [(target, source) for source, target in forward]
        low = lax.ppermute(
            lax.slice_in_dim(block, block.shape[dim] - width, None, axis=dim), axis, forward
        )
        high = lax.ppermute(lax.slice_in_dim(block, 0, width, axis=dim), axis, backward)
        block = jnp.concatenate([low, block, high], axis=dim)
    return block


def looked_sum(field):
    shape = field.shape
    return jnp.sum(field.reshape(shape[:-2] + (shape[-2] // LOOK, LOOK, shape[-1])), axis=-2)


def window_sum(padded, axis):
    length = padded.shape[axis] - 2 * RADIUS
    total = lax.slice_in_dim(padded, 0, length, axis=axis)
    for shift_at in range(1, 2 * RADIUS + 1):
        total = total + lax.slice_in_dim(padded, shift_at, shift_at + length, axis=axis)
    return total


def ring_plan(slc, offsets, weights, estimate, direction, prev_mean):
    epochs_here = slc.shape[1]
    look_rows = slc.shape[2] // LOOK
    col_count = slc.shape[3]
    ahead = passed_along(slc, "epoch", -1)
    extended = jnp.concatenate([slc, ahead], axis=1)
    numbers = jnp.arange(epochs_here, dtype=jnp.int32)
    partner = numbers[:, None] + offsets
    own_real = slc[0].astype(jnp.float32)
    own_imag = slc[1].astype(jnp.float32)
    ext_real = extended[0].astype(jnp.float32)
    ext_imag = extended[1].astype(jnp.float32)
    powers = looked_sum(ext_real * ext_real + ext_imag * ext_imag)
    pieces = []
    for slot_index in range(SLOTS):
        mate_real = jnp.take(ext_real, partner[:, slot_index], axis=0)
        mate_imag = jnp.take(ext_imag, partner[:, slot_index], axis=0)
        pieces.append(looked_sum(own_real * mate_real + own_imag * mate_imag))
        pieces.append(looked_sum(own_imag * mate_real - own_real * mate_imag))
    pair_count = epochs_here * 2 * SLOTS
    stacked = jnp.concatenate(
        [jnp.stack(pieces, axis=1).reshape(pair_count, look_rows, col_count), powers], axis=0
    )
    padded = extended_2(stacked, (("space", 1), ("sub", 2)), RADIUS)
    boxed = window_sum(window_sum(padded, 1), 2)
    pair_boxed = boxed[:pair_count].reshape(epochs_here, 2 * SLOTS, look_rows, col_count)
    power_box = boxed[pair_count:]
    coh_real = pair_boxed[:, 0::2]
    coh_imag = pair_boxed[:, 1::2]
    denominator = power_box[:epochs_here, None] * jnp.take(power_box, partner, axis=0) + EPSILON
    coherence = (coh_real * coh_real + coh_imag * coh_imag) / denominator
    observed = coh_imag / jnp.sqrt(denominator)
    est_ahead = passed_along(estimate, "epoch", -1)
    est_extended = jnp.concatenate([estimate, est_ahead], axis=0)
    fitted = estimate[:, None] - jnp.take(est_extended, partner, axis=0)
    factor = weights[:, :, None, None] * coherence
    weighted = factor * (observed - fitted)
    flattened = weighted.reshape(epochs_here * SLOTS, look_rows * col_count)
    selector = (
        jnp.arange(epochs_here + OFFS, dtype=jnp.int32)[:, None] == partner.reshape(1, -1)
    ).astype(jnp.float32)
    gathered = jnp.dot(
        selector, flattened, precision=lax.Precision.HIGHEST, preferred_element_type=jnp.float32
    ).reshape(epochs_here + OFFS, look_rows, col_count)
    own_part = jnp.sum(weighted, axis=1) - gathered[:epochs_here]
    returned = passed_along(-gathered[epochs_here:], "epoch", 1)
    gradient = jnp.concatenate([own_part + returned, own_part[OFFS:]], axis=0)
    cell_count = float(
        epochs_here
        * lax.axis_size("epoch")
        * look_rows
        * lax.axis_size("space")
        * col_count
        * lax.axis_size("sub")
    )
    local_norm = jnp.sum(gradient * gradient)
    local_crossed = jnp.sum(gradient * direction)
    mean_before = prev_mean[0]
    fields_ahead = passed_along(
        jnp.stack([gradient, direction]).astype(jnp.bfloat16), "epoch", -1
    ).astype(jnp.float32)
    grad_extended = jnp.concatenate([gradient, fields_ahead[0]], axis=0)
    old_extended = jnp.concatenate([direction, fields_ahead[1]], axis=0)
    grad_spread = gradient[:, None] - jnp.take(grad_extended, partner, axis=0)
    old_spread = direction[:, None] - jnp.take(old_extended, partner, axis=0)
    totals = lax.psum(
        (
            local_norm,
            local_crossed,
            jnp.sum(factor * grad_spread * grad_spread),
            jnp.sum(factor * grad_spread * old_spread),
            jnp.sum(factor * old_spread * old_spread),
        ),
        ("epoch", "space", "sub"),
    )
    grad_norm, crossed, grad_term, mixed_term, old_term = totals
    momentum = grad_norm / cell_count / mean_before
    new_direction = gradient + momentum * direction
    curvature = grad_term + 2.0 * momentum * mixed_term + momentum * momentum * old_term
    along_sum = grad_norm + momentum * crossed
    step_size = along_sum / curvature
    return (estimate + step_size * new_direction, new_direction)


LANES = 128
SIDES = 2 * RADIUS
HALO = 16
FIELD_STEPS = 16383.0
GRADIENT_STEPS = 32000.0
PARAM_LANE = 96
VMEM = pl.BlockSpec(memory_space=pltpu.VMEM)
SMEM = pl.BlockSpec(memory_space=pltpu.SMEM)
VMEM_BYTES = 48 * 1024 * 1024


def split_two(value):
    high = value.astype(jnp.bfloat16)
    low = (value - high.astype(jnp.float32)).astype(jnp.bfloat16)
    return high, low


def edge_kernel(first, last, edge):
    epochs = first.shape[1]
    lane = lax.broadcasted_iota(jnp.int32, edge.shape, 1)
    total = jnp.zeros(edge.shape, jnp.float32)
    for part in range(2):
        for epoch in range(epochs):
            at = (part * epochs + epoch) * SIDES
            total = placed(lane, total, tile_of(last, part, epoch, 0), LANES - RADIUS, at)
            total = placed(lane, total, tile_of(first, part, epoch, 0), 0, at + RADIUS)
    edge[...] = total.astype(jnp.bfloat16)


def fixed_point(value):
    return jnp.floor(value * FIELD_STEPS + 0.5).astype(jnp.int32).astype(jnp.int16)


def from_fixed_point(value):
    return value.astype(jnp.int32).astype(jnp.float32) * (1.0 / FIELD_STEPS)


def fields_kernel(me, estimate, direction, *fields):
    look_rows = estimate.shape[1]
    tiles = len(fields)
    for shift, out in enumerate(fields):
        tile = lax.rem(me[0] + shift, tiles)
        columns = pl.ds(pl.multiple_of(tile * LANES, LANES), LANES)
        for epoch in range(estimate.shape[0]):
            here = slice(epoch * look_rows, (epoch + 1) * look_rows)
            out[0, here, :] = fixed_point(estimate[epoch, :, columns])
            out[1, here, :] = fixed_point(direction[epoch, :, columns])


def tile_of(slc, part, epoch, tile):
    return slc[part, epoch, :, tile * LANES : (tile + 1) * LANES].astype(jnp.float32)


def placed(lane, total, source, start, target):
    moved = pltpu.roll(source, (target - start) % LANES, axis=1)
    return jnp.where((lane >= target) & (lane < target + RADIUS), moved, total)


def pack_kernel(me, present, slc, params, before, after, *refs):
    messages, strips = refs[:-1], refs[-1]
    tiles = len(messages)
    epochs = slc.shape[1]
    rows = slc.shape[2]
    lane = lax.broadcasted_iota(jnp.int32, (rows, LANES), 1)
    value = params[...]
    high = value.astype(jnp.bfloat16).astype(jnp.float32)
    middle = (value - high).astype(jnp.bfloat16).astype(jnp.float32)
    low = value - high - middle
    third = PARAM_LANE + 2 * SLOTS
    split = jnp.where(lane < third, high, jnp.where(lane < third + SLOTS, middle, low))
    split = jnp.where(lane >= PARAM_LANE, split, 0.0)
    inside = lane < 2 * epochs * SIDES
    for tile in range(tiles):
        total = split
        if tile == 0:
            edge = before[...].astype(jnp.float32) * present[0]
            total = jnp.where(inside & (lane % SIDES < RADIUS), edge, total)
        if tile == tiles - 1:
            edge = after[...].astype(jnp.float32) * present[1]
            total = jnp.where(inside & (lane % SIDES >= RADIUS), edge, total)
        for part in range(2):
            for epoch in range(epochs):
                at = (part * epochs + epoch) * SIDES
                if tile > 0:
                    total = placed(lane, total, tile_of(slc, part, epoch, tile - 1), LANES - RADIUS, at)
                if tile < tiles - 1:
                    total = placed(lane, total, tile_of(slc, part, epoch, tile + 1), 0, at + RADIUS)
        strips[tile] = total.astype(jnp.bfloat16)
    for tile in range(tiles):
        shift = lax.rem(tile - me[0] + tiles, tiles)
        for number, message in enumerate(messages):

            @pl.when(shift == number)
            def _():
                for part in range(2):
                    for epoch in range(epochs):
                        at = (part * epochs + epoch) * rows
                        message[at : at + rows, :] = slc[part, epoch, :, tile * LANES : (tile + 1) * LANES]
                message[2 * epochs * rows :, :] = strips[tile]


def look_order(from_rows, first):
    looks = from_rows // LOOK
    to = np.arange(from_rows)[:, None]
    at = np.arange(from_rows)[None, :]
    return jnp.asarray(at == (to + first) % looks * LOOK + to // looks, jnp.bfloat16)


def unpack_tiles(order, sources, main, first, columns_of):
    looks = order.shape[0] // LOOK
    for start in range(0, len(sources), 4):
        parts = jnp.concatenate([columns_of(source) for source in sources[start : start + 4]], axis=1)
        value = jnp.dot(order, parts, preferred_element_type=jnp.float32)
        for one in range(4):
            for look in range(LOOK):
                main[first[start + one], look] = value[look * looks : (look + 1) * looks, one * LANES : (one + 1) * LANES]


def unpack_rims(by_look, looks, rim, first):
    share = LANES // SLOTS
    lane = lax.broadcasted_iota(jnp.int32, (looks, LANES), 1)
    for at, place in enumerate(first):
        value = jnp.zeros((looks, LANES), jnp.float32)
        for look in range(LOOK):
            target = look * SIDES
            moved = pltpu.roll(by_look[look * looks : (look + 1) * looks], (target - at * SIDES) % LANES, axis=1)
            value = jnp.where((lane >= target) & (lane < target + SIDES), moved, value)
        spread = share
        while spread < LANES:
            value = value + pltpu.roll(value, spread, axis=1)
            spread = 2 * spread
        rim[place] = value


def column_bands():
    share = LANES // SLOTS
    at = np.arange(2 * LANES)[:, None] % LANES
    to = np.arange(LANES)[None, :]
    side = at % share % SIDES
    source = np.where(side < RADIUS, side - RADIUS, LANES + side - RADIUS)
    column = (to - at // share * share) % LANES
    inside = (column < RADIUS) | (column >= LANES - RADIUS)
    inside = inside & (at % share < LOOK * SIDES)
    band = np.abs(at - to) <= RADIUS
    rim_band = inside & (np.abs(source - column) <= RADIUS)
    return jnp.asarray(band, jnp.bfloat16), jnp.asarray(rim_band, jnp.bfloat16)


def mixed(values):
    lane = lax.broadcasted_iota(jnp.int32, values[0].shape, 1)
    result = values[-1]
    for slot in range(SLOTS - 1):
        result = jnp.where(lane < (SLOTS - 1 - slot) * (LANES // SLOTS), values[SLOTS - 2 - slot], result)
    return result


def power_batches(blocks, epochs, looks, main, rim, looked, rim_looked):
    total = blocks * epochs
    group = 2 * SLOTS
    for block in range(blocks):
        for piece in range(0, looks, 8):
            rows_at = slice(piece, piece + 8)
            for half in range(2):
                squares = []
                for slot in range(SLOTS):
                    channel = half * SLOTS + slot
                    epoch = block * epochs + channel
                    value = None
                    for look in range(LOOK):
                        real = main[epoch, look, rows_at]
                        imag = main[total + epoch, look, rows_at]
                        one = real * real + imag * imag
                        value = one if value is None else value + one
                    at = (block * group + channel) * looks + piece
                    looked[at : at + 8, :] = value
                    real = rim[epoch, rows_at]
                    imag = rim[total + epoch, rows_at]
                    squares.append(real * real + imag * imag)
                at = (block * 2 + half) * looks + piece
                rim_looked[at : at + 8, :] = mixed(squares)


def pair_batch(epoch, mates, total, main, rim):
    own_re, own_im = main[epoch], main[total + epoch]
    reals, imags = [], []
    for mate in mates:
        mate_re, mate_im = main[mate], main[total + mate]
        real = own_re[0] * mate_re[0] + own_im[0] * mate_im[0]
        imag = own_im[0] * mate_re[0] - own_re[0] * mate_im[0]
        for look in range(1, LOOK):
            real = real + (own_re[look] * mate_re[look] + own_im[look] * mate_im[look])
            imag = imag + (own_im[look] * mate_re[look] - own_re[look] * mate_im[look])
        reals.append(real)
        imags.append(imag)
    own_re, own_im = rim[epoch], rim[total + epoch]
    mate_re = mixed([rim[mate] for mate in mates])
    mate_im = mixed([rim[total + mate] for mate in mates])
    rims = [own_re * mate_re + own_im * mate_im, own_im * mate_re - own_re * mate_im]
    return reals + imags, rims


def put(ref, block, values):
    rows = sum(value.shape[0] for value in values)
    ref[block * rows : (block + 1) * rows, :] = jnp.concatenate(values, axis=0)


def columns_summed(couple, looks, bands, looked, rim_looked):
    group = 2 * SLOTS
    f32 = jnp.float32
    at = slice(couple * 2 * group * looks, (couple + 1) * 2 * group * looks)
    halves = jnp.concatenate(split_two(looked[at, :]), axis=1)
    value = jnp.dot(halves, bands[0], preferred_element_type=f32)
    at = slice(couple * 4 * looks, (couple + 1) * 4 * looks)
    halves = jnp.concatenate(split_two(rim_looked[at, :]), axis=1)
    outer = jnp.dot(halves, bands[1], preferred_element_type=f32)
    lane = lax.broadcasted_iota(jnp.int32, (looks, LANES), 1)
    outside = (lane < RADIUS) | (lane >= LANES - RADIUS)
    results = []
    for channel in range(2 * group):
        batch, half, slot = channel // group, channel % group // SLOTS, channel % SLOTS
        row = (batch * 2 + half) * looks
        part = outer[row : row + looks]
        if slot > 0:
            part = pltpu.roll(part, LANES - slot * (LANES // SLOTS), axis=1)
        row = channel * looks
        results.append(value[row : row + looks] + jnp.where(outside, part, 0.0))
    return results


def rows_summed(channel, looks, look_rows, wide):
    first = channel * looks
    total = wide[pl.ds(first, look_rows), :]
    for shift in range(1, 2 * RADIUS + 1):
        total = total + wide[pl.ds(first + shift, look_rows), :]
    return total


def pair_couple(couple, total, partner, main, rim):
    products, rims = [], []
    for one in range(2):
        epoch = couple * 2 + one
        mates = [partner[epoch * SLOTS + slot] for slot in range(SLOTS)]
        more, more_rims = pair_batch(epoch, mates, total, main, rim)
        products += more
        rims += more_rims
    return products, rims


def clipped(value, last):
    return jnp.minimum(jnp.maximum(value, 0), last)


def pair_kernel(sizes, places, partner, weight, present, order, band, rim_band, *refs):
    epochs, rows, operands = sizes
    inputs = refs[:operands]
    factors, pulls, boxed, main, rim, looked, rim_looked, wide = refs[operands:]
    count = len(places)
    total = count * epochs
    look_rows = rows // LOOK
    halo_looks = HALO // LOOK
    looks = look_rows + 2 * halo_looks
    full_rows = rows + 2 * HALO
    group = 2 * SLOTS

    at = lax.broadcasted_iota(jnp.int32, (full_rows, full_rows), 1)
    keep = jnp.where(at < HALO, present[0], jnp.where(at >= HALO + rows, present[1], 1.0))
    order = (order[...].astype(jnp.float32) * keep).astype(jnp.bfloat16)
    bands = band[...], rim_band[...]
    for block, (tile_at, top_at, bottom_at, top_row, bottom_row) in enumerate(places):
        tile, top, bottom = inputs[tile_at], inputs[top_at], inputs[bottom_at]

        def rows_of(at):
            above = top[top_row + at * HALO : top_row + (at + 1) * HALO, :]
            below = bottom[bottom_row + at * HALO : bottom_row + (at + 1) * HALO, :]
            return jnp.concatenate([above, tile[at * rows : (at + 1) * rows, :], below], axis=0)

        first = [part * total + block * epochs + epoch for part in range(2) for epoch in range(epochs)]
        unpack_tiles(order, range(2 * epochs), main, first, rows_of)
        by_look = jnp.dot(order, rows_of(2 * epochs), preferred_element_type=jnp.float32)
        unpack_rims(by_look, looks, rim, first)
    power_batches(count, epochs, looks, main, rim, looked, rim_looked)
    powers = count // 2
    couples = total // 2

    def boxed_of(channel):
        return boxed[pl.ds(pl.multiple_of(channel * look_rows, look_rows), look_rows), :]

    def finished(couple):
        results = []
        for one in range(2):
            epoch = couple * 2 + one
            own_power = boxed_of(epoch)
            first = (2 * powers + epoch) * (group * look_rows)
            parts = boxed[first : first + group * look_rows, :]
            parts = parts.reshape(group, look_rows, LANES)
            for slot in range(SLOTS):
                pair = epoch * SLOTS + slot
                inverse = lax.rsqrt(own_power * boxed_of(partner[pair]) + EPSILON)
                unit_re = parts[slot] * inverse
                unit_im = parts[SLOTS + slot] * inverse
                factor = weight[pair] * (unit_re * unit_re + unit_im * unit_im)
                results.append((factor, factor * unit_im))
        return results

    def boxes(couple):
        return [rows_summed(couple * 2 * group + one, looks, look_rows, wide) for one in range(2 * group)]

    def turn(number, steps):
        if 3 in steps:
            results = finished(number - 3)
        if 2 in steps:
            sums = boxes(powers + number - 2)
        if 1 in steps:
            columns = columns_summed(powers + number - 1, looks, bands, looked, rim_looked)
        if 0 in steps:
            products, rims = pair_couple(number, total, partner, main, rim)
        if 3 in steps:
            for ref, values in zip((factors, pulls), zip(*results)):
                ref[pl.ds((number - 3) * 2 * SLOTS, 2 * SLOTS)] = jnp.stack(values)
        if 2 in steps:
            put(boxed, powers + number - 2, sums)
        if 1 in steps:
            put(wide, powers + number - 1, columns)
        if 0 in steps:
            put(looked, powers + number, products)
            put(rim_looked, powers + number, rims)

    for couple in range(powers):
        put(wide, couple, columns_summed(couple, looks, bands, looked, rim_looked))
    turn(0, (0,))
    for couple in range(powers):
        put(boxed, couple, boxes(couple))
    turn(1, (0, 1))
    turn(2, (0, 1, 2))
    for number in range(3, couples):
        turn(number, (0, 1, 2, 3))
    turn(couples, (1, 2, 3))
    turn(couples + 1, (2, 3))
    turn(couples + 2, (3,))


def gradient_kernel(sizes, partner, *refs):
    tiles, epochs = sizes
    fields = refs[:tiles]
    factors, pulls, gradient, sums, est, old, shares = refs[tiles:]
    look_rows = est.shape[1]
    total = tiles * epochs
    f32 = jnp.float32
    for block in range(tiles):
        for epoch in range(epochs):
            here = slice(epoch * look_rows, (epoch + 1) * look_rows)
            est[block * epochs + epoch] = from_fixed_point(fields[block][0, here, :])
            old[block * epochs + epoch] = from_fixed_point(fields[block][1, here, :])
    mates = [[partner[epoch * SLOTS + slot] for slot in range(SLOTS)] for epoch in range(total)]
    for epoch in range(total):
        own_est = est[epoch]
        own = None
        for slot, mate in enumerate(mates[epoch]):
            pair = epoch * SLOTS + slot
            weighted = pulls[pair] - factors[pair] * (own_est - est[mate])
            own = weighted if own is None else own + weighted
            shares[pair] = weighted
        gradient[epoch] = own
    for epoch in range(total):
        values = [gradient[mate] - shares[epoch * SLOTS + slot] for slot, mate in enumerate(mates[epoch])]
        for mate, value in zip(mates[epoch], values):
            gradient[mate] = value

    zero = jnp.zeros((look_rows, LANES), f32)
    norm, crossed, grad_term, mixed_term, old_term = (zero,) * 5
    for epoch in range(total):
        own_grad = gradient[epoch]
        own_old = old[epoch]
        norm = norm + own_grad * own_grad
        crossed = crossed + own_grad * own_old
        for slot, mate in enumerate(mates[epoch]):
            factor = factors[epoch * SLOTS + slot]
            grad_spread = own_grad - gradient[mate]
            old_spread = own_old - old[mate]
            pulled = factor * grad_spread
            grad_term = grad_term + pulled * grad_spread
            mixed_term = mixed_term + pulled * old_spread
            old_term = old_term + factor * old_spread * old_spread
    sums[...] = jnp.zeros(sums.shape, f32)
    for at, value in enumerate((norm, crossed, grad_term, mixed_term, old_term)):
        sums[at : at + 1, :] = jnp.sum(value, axis=0, keepdims=True)


def exponent_of(size):
    power = jnp.ceil(jnp.log(jnp.maximum(size, 1e-30)) * (1.0 / math.log(2.0)))
    return jnp.clip(power, -110.0, 110.0)


def whole(value):
    return jnp.floor(value + 0.5).astype(jnp.int32).astype(jnp.int16)


def number_of(value):
    return value.astype(jnp.int32).astype(jnp.float32)


def code_kernel(gradient, *coded):
    epochs = gradient.shape[0] // (len(coded) + 1)
    look_rows = gradient.shape[1]
    for number, out in enumerate(coded):
        powers = []
        for epoch in range(epochs):
            value = gradient[(number + 1) * epochs + epoch]
            power = exponent_of(jnp.max(jnp.abs(value), axis=0, keepdims=True))
            out[epoch * look_rows : (epoch + 1) * look_rows, :] = whole(value * (jnp.exp2(-power) * GRADIENT_STEPS))
            powers.append(power)
        powers.append(jnp.zeros((HALO - epochs, LANES), jnp.float32))
        out[epochs * look_rows :, :] = whole(jnp.concatenate(powers, axis=0))


def return_kernel(tiles, *refs):
    coded, shared = refs[: tiles - 1], refs[tiles - 1 : -tiles]
    own, pieces = refs[-tiles], refs[1 - tiles :]
    total = shared[0][...]
    for other in shared[1:]:
        total = total + other[...]
    own[...] = total
    power = exponent_of(jnp.abs(total))
    share = total * jnp.exp2(-power) * float(1 << 14)
    high = jnp.floor(share + 0.5)
    low = (share - high) * float(1 << 15)
    parts = whole(jnp.concatenate([power, high, low, jnp.zeros_like(power)], axis=0))
    for piece, source in zip(pieces, coded):
        piece[: source.shape[0], :] = source[...]
        piece[source.shape[0] :, :] = parts


def update_kernel(cell_count, me, prev_mean, estimate, direction, gradient, sums, *refs):
    pieces = refs[:-2]
    new_estimate, new_direction = refs[-2:]
    tiles = len(pieces) + 1
    epochs = estimate.shape[0]
    look_rows = estimate.shape[1]
    coded_rows = epochs * look_rows + HALO
    total = sums[...]
    for piece in pieces:
        parts = number_of(piece[coded_rows:, :])
        value = (parts[8:16] + parts[16:24] * (1.0 / (1 << 15))) * (1.0 / (1 << 14))
        total = total + value * jnp.exp2(parts[:8])
    total = jnp.sum(total, axis=1, keepdims=True)
    grad_norm, crossed, grad_term, mixed, old_term = (total[at : at + 1, :] for at in range(5))
    momentum = grad_norm / cell_count / prev_mean[0]
    curvature = grad_term + 2.0 * momentum * mixed + momentum * momentum * old_term
    step = (grad_norm + momentum * crossed) / curvature
    momentum = jnp.broadcast_to(momentum, (look_rows, LANES))
    step = jnp.broadcast_to(step, (look_rows, LANES))
    for shift in range(tiles):
        tile = lax.rem(me[0] - shift + tiles, tiles)
        columns = pl.ds(pl.multiple_of(tile * LANES, LANES), LANES)
        if shift > 0:
            piece = pieces[shift - 1]
            scale = jnp.exp2(number_of(piece[epochs * look_rows : coded_rows, :])) * (1.0 / GRADIENT_STEPS)
        for epoch in range(epochs):
            if shift == 0:
                value = gradient[epoch]
            else:
                value = number_of(piece[epoch * look_rows : (epoch + 1) * look_rows, :]) * scale[epoch : epoch + 1, :]
            moved = value + momentum * direction[epoch, :, columns]
            new_direction[epoch, :, columns] = moved
            new_estimate[epoch, :, columns] = estimate[epoch, :, columns] + step * moved


def swapped(up, down, axis):
    size = lax.axis_size(axis)
    if size == 1:
        return jnp.zeros_like(up), jnp.zeros_like(down)
    if size == 2:
        first = lax.axis_index(axis) == 0
        got = lax.ppermute(jnp.where(first, up, down), axis, [(0, 1), (1, 0)])
        return got, got
    forward = [(i, i + 1) for i in range(size - 1)]
    backward = [(target, source) for source, target in forward]
    return lax.ppermute(up, axis, forward), lax.ppermute(down, axis, backward)


def to_ahead(x, axis, by):
    size = lax.axis_size(axis)
    return lax.ppermute(x, axis, [(i, (i + by) % size) for i in range(size)])


def transposed_plan(slc, offsets, weights, estimate, direction, prev_mean):
    f32 = jnp.float32
    bf16 = jnp.bfloat16
    tiles = lax.axis_size("epoch")
    me = lax.axis_index("epoch")
    epochs, rows, columns = slc.shape[1:]
    look_rows = rows // LOOK
    total = tiles * epochs
    tile_rows = 2 * epochs * rows
    params_of = pltpu.CompilerParams(vmem_limit_bytes=VMEM_BYTES)

    def fetched(messages, shift):
        return to_ahead(messages[tiles - shift], "epoch", tiles - shift)

    sub = lax.axis_index("sub")
    outer_tile = (2, epochs, rows, LANES)
    edge = pl.pallas_call(
        edge_kernel,
        out_shape=jax.ShapeDtypeStruct((rows, LANES), bf16),
        grid=(1,),
        in_specs=[
            pl.BlockSpec(outer_tile, lambda _: (0, 0, 0, 0)),
            pl.BlockSpec(outer_tile, lambda _: (0, 0, 0, tiles - 1)),
        ],
        out_specs=pl.BlockSpec((rows, LANES), lambda _: (0, 0)),
        compiler_params=params_of,
        cost_estimate=pl.CostEstimate(flops=1_000_000, bytes_accessed=1_000_000, transcendentals=0),
    )(slc, slc)
    before, after = swapped(edge, edge, "sub")
    params = jnp.zeros((rows, LANES), f32)
    listed = jnp.concatenate([offsets.astype(f32), weights, weights, weights], axis=1)
    params = lax.dynamic_update_slice(params, listed, (0, PARAM_LANE))
    sub_present = jnp.stack([sub > 0, sub < lax.axis_size("sub") - 1]).astype(f32)
    messages = pl.pallas_call(
        pack_kernel,
        out_shape=(jax.ShapeDtypeStruct((tile_rows + rows, LANES), bf16),) * tiles,
        in_specs=[SMEM] * 2 + [VMEM] * 4,
        out_specs=(VMEM,) * tiles,
        scratch_shapes=[pltpu.VMEM((tiles, rows, LANES), bf16)],
        compiler_params=params_of,
        cost_estimate=pl.CostEstimate(flops=3_000_000, bytes_accessed=4_000_000, transcendentals=0),
    )(me.reshape(1), sub_present, slc, params, before, after)
    space = lax.axis_index("space")
    spaces = lax.axis_size("space")
    present = jnp.stack([space > 0, space < spaces - 1]).astype(f32)

    def halo(pieces):
        def border(from_row):
            cuts = [lax.dynamic_slice_in_dim(piece, from_row, HALO, axis=1).reshape(-1, LANES) for piece in pieces]
            return jnp.concatenate(cuts, axis=0)

        if spaces == 2:
            got = lax.ppermute(border(jnp.where(space == 0, rows - HALO, 0)), "space", [(0, 1), (1, 0)])
            return got, got
        return swapped(border(rows - HALO), border(0), "space")

    block = [messages[0]] + [fetched(messages, shift) for shift in range(1, tiles)]
    estimate, direction, _ = lax.optimization_barrier((estimate, direction, messages))
    fields = pl.pallas_call(
        fields_kernel,
        out_shape=(jax.ShapeDtypeStruct((2, epochs * look_rows, LANES), jnp.int16),) * tiles,
        in_specs=[SMEM] + [VMEM] * 2,
        out_specs=(VMEM,) * tiles,
        compiler_params=params_of,
        cost_estimate=pl.CostEstimate(flops=1_000_000, bytes_accessed=2_000_000, transcendentals=0),
    )(me.reshape(1), estimate, direction)
    def params_in(shift):
        return block[shift][tile_rows : tile_rows + epochs, PARAM_LANE : PARAM_LANE + 4 * SLOTS].astype(f32)

    def pairs_of(blocks, loaded):
        listed = jnp.concatenate([params_in(block) for block in blocks], axis=0)
        mate = jnp.arange(len(blocks) * epochs, dtype=jnp.int32)[:, None] + listed[:, :SLOTS].astype(jnp.int32)
        weight = listed[:, SLOTS : 2 * SLOTS] + listed[:, 2 * SLOTS : 3 * SLOTS] + listed[:, 3 * SLOTS :]
        return mate.reshape(-1), weight.reshape(-1)

    halos = [halo([array.reshape(-1, rows, LANES)]) for array in block]
    late = lax.optimization_barrier((fields, block, halos[2:]))[0]
    field = [fields[0]] + [fetched(late, shift) for shift in range(1, tiles)]

    listed = jnp.concatenate([params_in(shift) for shift in range(tiles)], axis=0)
    partner = jnp.arange(total, dtype=jnp.int32)[:, None] + listed[:, :SLOTS].astype(jnp.int32)
    partner = lax.rem(partner, total).reshape(-1)
    weight = listed[:, SLOTS : 2 * SLOTS] + listed[:, 2 * SLOTS : 3 * SLOTS] + listed[:, 3 * SLOTS :]
    order = look_order(rows + 2 * HALO, HALO // LOOK - RADIUS)
    bands = column_bands()
    operands = list(block)
    places = []
    for shift in range(tiles):
        top, bottom = halos[shift]
        operands.append(top)
        top_at = bottom_at = len(operands) - 1
        if bottom is not top:
            operands.append(bottom)
            bottom_at = len(operands) - 1
        places.append((shift, top_at, bottom_at, 0, 0))
    looks = (rows + 2 * HALO) // LOOK
    group = 2 * SLOTS
    batches = tiles + total
    shape = jax.ShapeDtypeStruct((total * SLOTS, look_rows, LANES), f32)
    factors, pulls = pl.pallas_call(
        functools.partial(pair_kernel, (epochs, rows, len(operands)), tuple(places)),
        out_shape=(shape, shape),
        in_specs=[SMEM] * 3 + [VMEM] * (3 + len(operands)),
        out_specs=(VMEM, VMEM),
        scratch_shapes=[
            pltpu.VMEM((batches * group * look_rows, LANES), f32),
            pltpu.VMEM((2 * total, LOOK, looks, LANES), f32),
            pltpu.VMEM((2 * total, looks, LANES), f32),
            pltpu.VMEM((batches * group * looks, LANES), f32),
            pltpu.VMEM((batches * 2 * looks, LANES), f32),
            pltpu.VMEM((batches * group * looks, LANES), f32),
        ],
        compiler_params=params_of,
        cost_estimate=pl.CostEstimate(flops=20_000_000, bytes_accessed=30_000_000, transcendentals=0),
    )(partner, weight.reshape(-1), present, order, *bands, *operands)
    gradient, sums = pl.pallas_call(
        functools.partial(gradient_kernel, (tiles, epochs)),
        out_shape=(
            jax.ShapeDtypeStruct((total, look_rows, LANES), f32),
            jax.ShapeDtypeStruct((8, LANES), f32),
        ),
        in_specs=[SMEM] + [VMEM] * (tiles + 2),
        out_specs=(VMEM, VMEM),
        scratch_shapes=[pltpu.VMEM((total, look_rows, LANES), f32)] * 2
        + [pltpu.VMEM((total * SLOTS, look_rows, LANES), f32)],
        compiler_params=params_of,
        cost_estimate=pl.CostEstimate(flops=10_000_000, bytes_accessed=8_000_000, transcendentals=0),
    )(partner, *field, factors, pulls)

    place = ("space", "sub")
    count = spaces * lax.axis_size("sub")
    shared = [sums] + [lax.ppermute(sums, place, [(i, (i + by) % count) for i in range(count)]) for by in range(1, count)]
    coded_shape = jax.ShapeDtypeStruct((epochs * look_rows + HALO, LANES), jnp.int16)
    coded = pl.pallas_call(
        code_kernel,
        out_shape=(coded_shape,) * (tiles - 1),
        in_specs=[VMEM],
        out_specs=(VMEM,) * (tiles - 1),
        compiler_params=params_of,
        cost_estimate=pl.CostEstimate(flops=1_000_000, bytes_accessed=1_000_000, transcendentals=0),
    )(gradient)
    piece_shape = jax.ShapeDtypeStruct((epochs * look_rows + HALO + 32, LANES), jnp.int16)
    own_sums, *pieces = pl.pallas_call(
        functools.partial(return_kernel, tiles),
        out_shape=(jax.ShapeDtypeStruct((8, LANES), f32),) + (piece_shape,) * (tiles - 1),
        in_specs=[VMEM] * (tiles - 1 + count),
        out_specs=(VMEM,) * tiles,
        compiler_params=params_of,
        cost_estimate=pl.CostEstimate(flops=10_000, bytes_accessed=1_000_000, transcendentals=0),
    )(*coded, *shared)
    returned = [to_ahead(piece, "epoch", by + 1) for by, piece in enumerate(pieces)]
    cell_count = float(total * look_rows * spaces * columns * lax.axis_size("sub"))
    return pl.pallas_call(
        functools.partial(update_kernel, cell_count),
        out_shape=(jax.ShapeDtypeStruct(estimate.shape, f32),) * 2,
        in_specs=[SMEM] * 2 + [VMEM] * (3 + tiles),
        out_specs=(VMEM, VMEM),
        compiler_params=params_of,
        cost_estimate=pl.CostEstimate(flops=1_000_000, bytes_accessed=2_000_000, transcendentals=0),
    )(me.reshape(1), prev_mean, estimate, direction, gradient[:epochs], own_sums, *returned)


def on_device(slc, offsets, weights, estimate, direction, prev_mean):
    epochs, rows, columns = slc.shape[1:]
    fits = columns == LANES * lax.axis_size("epoch") and lax.axis_size("epoch") % 2 == 0
    fits = fits and 2 * epochs * SIDES <= PARAM_LANE and rows % HALO == 0 and epochs == 2 * SLOTS
    plan = transposed_plan if fits else ring_plan
    return plan(slc, offsets, weights, estimate, direction, prev_mean)


def solution(mesh):
    return jax.shard_map(
        on_device,
        mesh=mesh,
        in_specs=(
            P(None, ("groups", "epoch"), "space", "sub"),
            P(("groups", "epoch"), None),
            P(("groups", "epoch"), None),
            P(("groups", "epoch"), "space", "sub"),
            P(("groups", "epoch"), "space", "sub"),
            P(),
        ),
        out_specs=(P(("groups", "epoch"), "space", "sub"), P(("groups", "epoch"), "space", "sub")),
        check_vma=False,
    )
```

```python
import functools
import math

import jax
import jax.numpy as jnp
import numpy as np
from jax import lax
from jax.experimental import pallas as pl
from jax.experimental.pallas import tpu as pltpu
from jax.sharding import PartitionSpec as P

SLOTS = 4
OFFS = 8
LOOK = 4
RADIUS = 3


EPSILON = 1e-06


def passed_along(x, axis, by):
    size = lax.axis_size(axis)
    return lax.ppermute(x, axis, [(i, (i + by) % size) for i in range(size)])


def extended_2(block, sides, width):
    for axis, dim in sides:
        count = lax.axis_size(axis)
        forward = [(i, i + 1) for i in range(count - 1)]
        backward = [(target, source) for source, target in forward]
        low = lax.ppermute(
            lax.slice_in_dim(block, block.shape[dim] - width, None, axis=dim), axis, forward
        )
        high = lax.ppermute(lax.slice_in_dim(block, 0, width, axis=dim), axis, backward)
        block = jnp.concatenate([low, block, high], axis=dim)
    return block


def looked_sum(field):
    shape = field.shape
    return jnp.sum(field.reshape(shape[:-2] + (shape[-2] // LOOK, LOOK, shape[-1])), axis=-2)


def window_sum(padded, axis):
    length = padded.shape[axis] - 2 * RADIUS
    total = lax.slice_in_dim(padded, 0, length, axis=axis)
    for shift_at in range(1, 2 * RADIUS + 1):
        total = total + lax.slice_in_dim(padded, shift_at, shift_at + length, axis=axis)
    return total


def ring_plan(slc, offsets, weights, estimate, direction, prev_mean):
    epochs_here = slc.shape[1]
    look_rows = slc.shape[2] // LOOK
    col_count = slc.shape[3]
    ahead = passed_along(slc, "epoch", -1)
    extended = jnp.concatenate([slc, ahead], axis=1)
    numbers = jnp.arange(epochs_here, dtype=jnp.int32)
    partner = numbers[:, None] + offsets
    own_real = slc[0].astype(jnp.float32)
    own_imag = slc[1].astype(jnp.float32)
    ext_real = extended[0].astype(jnp.float32)
    ext_imag = extended[1].astype(jnp.float32)
    powers = looked_sum(ext_real * ext_real + ext_imag * ext_imag)
    pieces = []
    for slot_index in range(SLOTS):
        mate_real = jnp.take(ext_real, partner[:, slot_index], axis=0)
        mate_imag = jnp.take(ext_imag, partner[:, slot_index], axis=0)
        pieces.append(looked_sum(own_real * mate_real + own_imag * mate_imag))
        pieces.append(looked_sum(own_imag * mate_real - own_real * mate_imag))
    pair_count = epochs_here * 2 * SLOTS
    stacked = jnp.concatenate(
        [jnp.stack(pieces, axis=1).reshape(pair_count, look_rows, col_count), powers], axis=0
    )
    padded = extended_2(stacked, (("space", 1), ("sub", 2)), RADIUS)
    boxed = window_sum(window_sum(padded, 1), 2)
    pair_boxed = boxed[:pair_count].reshape(epochs_here, 2 * SLOTS, look_rows, col_count)
    power_box = boxed[pair_count:]
    coh_real = pair_boxed[:, 0::2]
    coh_imag = pair_boxed[:, 1::2]
    denominator = power_box[:epochs_here, None] * jnp.take(power_box, partner, axis=0) + EPSILON
    coherence = (coh_real * coh_real + coh_imag * coh_imag) / denominator
    observed = coh_imag / jnp.sqrt(denominator)
    est_ahead = passed_along(estimate, "epoch", -1)
    est_extended = jnp.concatenate([estimate, est_ahead], axis=0)
    fitted = estimate[:, None] - jnp.take(est_extended, partner, axis=0)
    factor = weights[:, :, None, None] * coherence
    weighted = factor * (observed - fitted)
    flattened = weighted.reshape(epochs_here * SLOTS, look_rows * col_count)
    selector = (
        jnp.arange(epochs_here + OFFS, dtype=jnp.int32)[:, None] == partner.reshape(1, -1)
    ).astype(jnp.float32)
    gathered = jnp.dot(
        selector, flattened, precision=lax.Precision.HIGHEST, preferred_element_type=jnp.float32
    ).reshape(epochs_here + OFFS, look_rows, col_count)
    own_part = jnp.sum(weighted, axis=1) - gathered[:epochs_here]
    returned = passed_along(-gathered[epochs_here:], "epoch", 1)
    gradient = jnp.concatenate([own_part + returned, own_part[OFFS:]], axis=0)
    cell_count = float(
        epochs_here
        * lax.axis_size("epoch")
        * look_rows
        * lax.axis_size("space")
        * col_count
        * lax.axis_size("sub")
    )
    local_norm = jnp.sum(gradient * gradient)
    local_crossed = jnp.sum(gradient * direction)
    mean_before = prev_mean[0]
    fields_ahead = passed_along(
        jnp.stack([gradient, direction]).astype(jnp.bfloat16), "epoch", -1
    ).astype(jnp.float32)
    grad_extended = jnp.concatenate([gradient, fields_ahead[0]], axis=0)
    old_extended = jnp.concatenate([direction, fields_ahead[1]], axis=0)
    grad_spread = gradient[:, None] - jnp.take(grad_extended, partner, axis=0)
    old_spread = direction[:, None] - jnp.take(old_extended, partner, axis=0)
    totals = lax.psum(
        (
            local_norm,
            local_crossed,
            jnp.sum(factor * grad_spread * grad_spread),
            jnp.sum(factor * grad_spread * old_spread),
            jnp.sum(factor * old_spread * old_spread),
        ),
        ("epoch", "space", "sub"),
    )
    grad_norm, crossed, grad_term, mixed_term, old_term = totals
    momentum = grad_norm / cell_count / mean_before
    new_direction = gradient + momentum * direction
    curvature = grad_term + 2.0 * momentum * mixed_term + momentum * momentum * old_term
    along_sum = grad_norm + momentum * crossed
    step_size = along_sum / curvature
    return (estimate + step_size * new_direction, new_direction)


LANES = 128
SIDES = 2 * RADIUS
HALO = 16
FIELD_STEPS = 16383.0
GRADIENT_STEPS = 32000.0
PARAM_LANE = 96
VMEM = pl.BlockSpec(memory_space=pltpu.VMEM)
SMEM = pl.BlockSpec(memory_space=pltpu.SMEM)
VMEM_BYTES = 48 * 1024 * 1024


def split_two(value):
    high = value.astype(jnp.bfloat16)
    low = (value - high.astype(jnp.float32)).astype(jnp.bfloat16)
    return high, low


def edge_kernel(first, last, edge):
    epochs = first.shape[1]
    lane = lax.broadcasted_iota(jnp.int32, edge.shape, 1)
    total = jnp.zeros(edge.shape, jnp.float32)
    for part in range(2):
        for epoch in range(epochs):
            at = (part * epochs + epoch) * SIDES
            total = placed(lane, total, tile_of(last, part, epoch, 0), LANES - RADIUS, at)
            total = placed(lane, total, tile_of(first, part, epoch, 0), 0, at + RADIUS)
    edge[...] = total.astype(jnp.bfloat16)


def fixed_point(value):
    return jnp.floor(value * FIELD_STEPS + 0.5).astype(jnp.int32).astype(jnp.int16)


def from_fixed_point(value):
    return value.astype(jnp.int32).astype(jnp.float32) * (1.0 / FIELD_STEPS)


def fields_kernel(me, estimate, direction, *fields):
    look_rows = estimate.shape[1]
    tiles = len(fields)
    for shift, out in enumerate(fields):
        tile = lax.bitwise_xor(me[0], shift)
        columns = pl.ds(pl.multiple_of(tile * LANES, LANES), LANES)
        for epoch in range(estimate.shape[0]):
            here = slice(epoch * look_rows, (epoch + 1) * look_rows)
            out[0, here, :] = fixed_point(estimate[epoch, :, columns])
            out[1, here, :] = fixed_point(direction[epoch, :, columns])


def tile_of(slc, part, epoch, tile):
    return slc[part, epoch, :, tile * LANES : (tile + 1) * LANES].astype(jnp.float32)


def placed(lane, total, source, start, target):
    moved = pltpu.roll(source, (target - start) % LANES, axis=1)
    return jnp.where((lane >= target) & (lane < target + RADIUS), moved, total)


def pack_kernel(me, present, slc, params, before, after, *refs):
    messages, strips = refs[:-1], refs[-1]
    tiles = len(messages)
    epochs = slc.shape[1]
    rows = slc.shape[2]
    lane = lax.broadcasted_iota(jnp.int32, (rows, LANES), 1)
    value = params[...]
    high = value.astype(jnp.bfloat16).astype(jnp.float32)
    middle = (value - high).astype(jnp.bfloat16).astype(jnp.float32)
    low = value - high - middle
    third = PARAM_LANE + 2 * SLOTS
    split = jnp.where(lane < third, high, jnp.where(lane < third + SLOTS, middle, low))
    split = jnp.where(lane >= PARAM_LANE, split, 0.0)
    inside = lane < 2 * epochs * SIDES
    for tile in range(tiles):
        total = split
        if tile == 0:
            edge = before[...].astype(jnp.float32) * present[0]
            total = jnp.where(inside & (lane % SIDES < RADIUS), edge, total)
        if tile == tiles - 1:
            edge = after[...].astype(jnp.float32) * present[1]
            total = jnp.where(inside & (lane % SIDES >= RADIUS), edge, total)
        for part in range(2):
            for epoch in range(epochs):
                at = (part * epochs + epoch) * SIDES
                if tile > 0:
                    total = placed(lane, total, tile_of(slc, part, epoch, tile - 1), LANES - RADIUS, at)
                if tile < tiles - 1:
                    total = placed(lane, total, tile_of(slc, part, epoch, tile + 1), 0, at + RADIUS)
        strips[tile] = total.astype(jnp.bfloat16)
    for tile in range(tiles):
        shift = lax.bitwise_xor(me[0], tile)
        for number, message in enumerate(messages):

            @pl.when(shift == number)
            def _():
                for part in range(2):
                    for epoch in range(epochs):
                        at = (part * epochs + epoch) * rows
                        message[at : at + rows, :] = slc[part, epoch, :, tile * LANES : (tile + 1) * LANES]
                message[2 * epochs * rows :, :] = strips[tile]


def look_order(from_rows, first):
    looks = from_rows // LOOK
    to = np.arange(from_rows)[:, None]
    at = np.arange(from_rows)[None, :]
    return jnp.asarray(at == (to + first) % looks * LOOK + to // looks, jnp.bfloat16)


def unpack_tiles(order, sources, main, first, columns_of):
    looks = order.shape[0] // LOOK
    for start in range(0, len(sources), 4):
        parts = jnp.concatenate([columns_of(source) for source in sources[start : start + 4]], axis=1)
        value = jnp.dot(order, parts, preferred_element_type=jnp.float32)
        for one in range(4):
            for look in range(LOOK):
                main[first[start + one], look] = value[look * looks : (look + 1) * looks, one * LANES : (one + 1) * LANES]


def unpack_rims(by_look, looks, rim, first):
    share = LANES // SLOTS
    lane = lax.broadcasted_iota(jnp.int32, (looks, LANES), 1)
    for at, place in enumerate(first):
        value = jnp.zeros((looks, LANES), jnp.float32)
        for look in range(LOOK):
            target = look * SIDES
            moved = pltpu.roll(by_look[look * looks : (look + 1) * looks], (target - at * SIDES) % LANES, axis=1)
            value = jnp.where((lane >= target) & (lane < target + SIDES), moved, value)
        spread = share
        while spread < LANES:
            value = value + pltpu.roll(value, spread, axis=1)
            spread = 2 * spread
        rim[place] = value


def column_bands():
    share = LANES // SLOTS
    at = np.arange(2 * LANES)[:, None] % LANES
    to = np.arange(LANES)[None, :]
    side = at % share % SIDES
    source = np.where(side < RADIUS, side - RADIUS, LANES + side - RADIUS)
    column = (to - at // share * share) % LANES
    inside = (column < RADIUS) | (column >= LANES - RADIUS)
    inside = inside & (at % share < LOOK * SIDES)
    band = np.abs(at - to) <= RADIUS
    rim_band = inside & (np.abs(source - column) <= RADIUS)
    return jnp.asarray(band, jnp.bfloat16), jnp.asarray(rim_band, jnp.bfloat16)


def mixed(values):
    lane = lax.broadcasted_iota(jnp.int32, values[0].shape, 1)
    result = values[-1]
    for slot in range(SLOTS - 1):
        result = jnp.where(lane < (SLOTS - 1 - slot) * (LANES // SLOTS), values[SLOTS - 2 - slot], result)
    return result


def power_batches(blocks, epochs, looks, main, rim, looked, rim_looked):
    total = blocks * epochs
    group = 2 * SLOTS
    for block in range(blocks):
        for piece in range(0, looks, 8):
            rows_at = slice(piece, piece + 8)
            for half in range(2):
                squares = []
                for slot in range(SLOTS):
                    channel = half * SLOTS + slot
                    epoch = block * epochs + channel
                    value = None
                    for look in range(LOOK):
                        real = main[epoch, look, rows_at]
                        imag = main[total + epoch, look, rows_at]
                        one = real * real + imag * imag
                        value = one if value is None else value + one
                    at = (block * group + channel) * looks + piece
                    looked[at : at + 8, :] = value
                    real = rim[epoch, rows_at]
                    imag = rim[total + epoch, rows_at]
                    squares.append(real * real + imag * imag)
                at = (block * 2 + half) * looks + piece
                rim_looked[at : at + 8, :] = mixed(squares)


def pair_batch(epoch, mates, total, main, rim):
    own_re, own_im = main[epoch], main[total + epoch]
    reals, imags = [], []
    for mate in mates:
        mate_re, mate_im = main[mate], main[total + mate]
        real = own_re[0] * mate_re[0] + own_im[0] * mate_im[0]
        imag = own_im[0] * mate_re[0] - own_re[0] * mate_im[0]
        for look in range(1, LOOK):
            real = real + (own_re[look] * mate_re[look] + own_im[look] * mate_im[look])
            imag = imag + (own_im[look] * mate_re[look] - own_re[look] * mate_im[look])
        reals.append(real)
        imags.append(imag)
    own_re, own_im = rim[epoch], rim[total + epoch]
    mate_re = mixed([rim[mate] for mate in mates])
    mate_im = mixed([rim[total + mate] for mate in mates])
    rims = [own_re * mate_re + own_im * mate_im, own_im * mate_re - own_re * mate_im]
    return reals + imags, rims


def put(ref, block, values):
    rows = sum(value.shape[0] for value in values)
    ref[block * rows : (block + 1) * rows, :] = jnp.concatenate(values, axis=0)


def columns_summed(couple, looks, bands, looked, rim_looked):
    group = 2 * SLOTS
    f32 = jnp.float32
    at = slice(couple * 2 * group * looks, (couple + 1) * 2 * group * looks)
    halves = jnp.concatenate(split_two(looked[at, :]), axis=1)
    value = jnp.dot(halves, bands[0], preferred_element_type=f32)
    at = slice(couple * 4 * looks, (couple + 1) * 4 * looks)
    halves = jnp.concatenate(split_two(rim_looked[at, :]), axis=1)
    outer = jnp.dot(halves, bands[1], preferred_element_type=f32)
    lane = lax.broadcasted_iota(jnp.int32, (looks, LANES), 1)
    outside = (lane < RADIUS) | (lane >= LANES - RADIUS)
    results = []
    for channel in range(2 * group):
        batch, half, slot = channel // group, channel % group // SLOTS, channel % SLOTS
        row = (batch * 2 + half) * looks
        part = outer[row : row + looks]
        if slot > 0:
            part = pltpu.roll(part, LANES - slot * (LANES // SLOTS), axis=1)
        row = channel * looks
        results.append(value[row : row + looks] + jnp.where(outside, part, 0.0))
    return results


def rows_summed(channel, looks, look_rows, wide):
    first = channel * looks
    total = wide[pl.ds(first, look_rows), :]
    for shift in range(1, 2 * RADIUS + 1):
        total = total + wide[pl.ds(first + shift, look_rows), :]
    return total


def pair_couple(couple, total, partner, main, rim):
    products, rims = [], []
    for one in range(2):
        epoch = couple * 2 + one
        mates = [partner[epoch * SLOTS + slot] for slot in range(SLOTS)]
        more, more_rims = pair_batch(epoch, mates, total, main, rim)
        products += more
        rims += more_rims
    return products, rims


def clipped(value, last):
    return jnp.minimum(jnp.maximum(value, 0), last)


def pair_kernel(sizes, places, partner, weight, present, order, band, rim_band, *refs):
    epochs, rows, operands = sizes
    inputs = refs[:operands]
    factors, pulls, boxed, main, rim, looked, rim_looked, wide = refs[operands:]
    count = len(places)
    total = count * epochs
    look_rows = rows // LOOK
    halo_looks = HALO // LOOK
    looks = look_rows + 2 * halo_looks
    full_rows = rows + 2 * HALO
    group = 2 * SLOTS

    at = lax.broadcasted_iota(jnp.int32, (full_rows, full_rows), 1)
    keep = jnp.where(at < HALO, present[0], jnp.where(at >= HALO + rows, present[1], 1.0))
    order = (order[...].astype(jnp.float32) * keep).astype(jnp.bfloat16)
    bands = band[...], rim_band[...]
    for block, (tile_at, top_at, bottom_at, top_row, bottom_row) in enumerate(places):
        tile, top, bottom = inputs[tile_at], inputs[top_at], inputs[bottom_at]

        def rows_of(at):
            above = top[top_row + at * HALO : top_row + (at + 1) * HALO, :]
            below = bottom[bottom_row + at * HALO : bottom_row + (at + 1) * HALO, :]
            return jnp.concatenate([above, tile[at * rows : (at + 1) * rows, :], below], axis=0)

        first = [part * total + block * epochs + epoch for part in range(2) for epoch in range(epochs)]
        unpack_tiles(order, range(2 * epochs), main, first, rows_of)
        by_look = jnp.dot(order, rows_of(2 * epochs), preferred_element_type=jnp.float32)
        unpack_rims(by_look, looks, rim, first)
    power_batches(count, epochs, looks, main, rim, looked, rim_looked)
    powers = count // 2
    couples = total // 2

    def boxed_of(channel):
        return boxed[pl.ds(pl.multiple_of(channel * look_rows, look_rows), look_rows), :]

    def finished(couple):
        results = []
        for one in range(2):
            epoch = couple * 2 + one
            own_power = boxed_of(epoch)
            first = (2 * powers + epoch) * (group * look_rows)
            parts = boxed[first : first + group * look_rows, :]
            parts = parts.reshape(group, look_rows, LANES)
            for slot in range(SLOTS):
                pair = epoch * SLOTS + slot
                inverse = lax.rsqrt(own_power * boxed_of(partner[pair]) + EPSILON)
                unit_re = parts[slot] * inverse
                unit_im = parts[SLOTS + slot] * inverse
                factor = weight[pair] * (unit_re * unit_re + unit_im * unit_im)
                results.append((factor, factor * unit_im))
        return results

    def boxes(couple):
        return [rows_summed(couple * 2 * group + one, looks, look_rows, wide) for one in range(2 * group)]

    def turn(number, steps):
        if 3 in steps:
            results = finished(number - 3)
        if 2 in steps:
            sums = boxes(powers + number - 2)
        if 1 in steps:
            columns = columns_summed(powers + number - 1, looks, bands, looked, rim_looked)
        if 0 in steps:
            products, rims = pair_couple(number, total, partner, main, rim)
        if 3 in steps:
            for ref, values in zip((factors, pulls), zip(*results)):
                ref[pl.ds((number - 3) * 2 * SLOTS, 2 * SLOTS)] = jnp.stack(values)
        if 2 in steps:
            put(boxed, powers + number - 2, sums)
        if 1 in steps:
            put(wide, powers + number - 1, columns)
        if 0 in steps:
            put(looked, powers + number, products)
            put(rim_looked, powers + number, rims)

    for couple in range(powers):
        put(wide, couple, columns_summed(couple, looks, bands, looked, rim_looked))
    turn(0, (0,))
    for couple in range(powers):
        put(boxed, couple, boxes(couple))
    turn(1, (0, 1))
    turn(2, (0, 1, 2))
    for number in range(3, couples):
        turn(number, (0, 1, 2, 3))
    turn(couples, (1, 2, 3))
    turn(couples + 1, (2, 3))
    turn(couples + 2, (3,))


def gradient_kernel(sizes, partner, *refs):
    tiles, epochs = sizes
    fields = refs[:tiles]
    factors, pulls, gradient, sums, est, old, shares = refs[tiles:]
    look_rows = est.shape[1]
    total = tiles * epochs
    f32 = jnp.float32
    for block in range(tiles):
        for epoch in range(epochs):
            here = slice(epoch * look_rows, (epoch + 1) * look_rows)
            est[block * epochs + epoch] = from_fixed_point(fields[block][0, here, :])
            old[block * epochs + epoch] = from_fixed_point(fields[block][1, here, :])
    mates = [[partner[epoch * SLOTS + slot] for slot in range(SLOTS)] for epoch in range(total)]
    for epoch in range(total):
        own_est = est[epoch]
        own = None
        for slot, mate in enumerate(mates[epoch]):
            pair = epoch * SLOTS + slot
            weighted = pulls[pair] - factors[pair] * (own_est - est[mate])
            own = weighted if own is None else own + weighted
            shares[pair] = weighted
        gradient[epoch] = own
    for epoch in range(total):
        values = [gradient[mate] - shares[epoch * SLOTS + slot] for slot, mate in enumerate(mates[epoch])]
        for mate, value in zip(mates[epoch], values):
            gradient[mate] = value

    zero = jnp.zeros((look_rows, LANES), f32)
    norm, crossed, grad_term, mixed_term, old_term = (zero,) * 5
    for epoch in range(total):
        own_grad = gradient[epoch]
        own_old = old[epoch]
        norm = norm + own_grad * own_grad
        crossed = crossed + own_grad * own_old
        for slot, mate in enumerate(mates[epoch]):
            factor = factors[epoch * SLOTS + slot]
            grad_spread = own_grad - gradient[mate]
            old_spread = own_old - old[mate]
            pulled = factor * grad_spread
            grad_term = grad_term + pulled * grad_spread
            mixed_term = mixed_term + pulled * old_spread
            old_term = old_term + factor * old_spread * old_spread
    sums[...] = jnp.zeros(sums.shape, f32)
    for at, value in enumerate((norm, crossed, grad_term, mixed_term, old_term)):
        sums[at : at + 1, :] = jnp.sum(value, axis=0, keepdims=True)


def exponent_of(size):
    power = jnp.ceil(jnp.log(jnp.maximum(size, 1e-30)) * (1.0 / math.log(2.0)))
    return jnp.clip(power, -110.0, 110.0)


def whole(value):
    return jnp.floor(value + 0.5).astype(jnp.int32).astype(jnp.int16)


def number_of(value):
    return value.astype(jnp.int32).astype(jnp.float32)


def code_kernel(gradient, *coded):
    epochs = gradient.shape[0] // (len(coded) + 1)
    look_rows = gradient.shape[1]
    for number, out in enumerate(coded):
        powers = []
        for epoch in range(epochs):
            value = gradient[(number + 1) * epochs + epoch]
            power = exponent_of(jnp.max(jnp.abs(value), axis=0, keepdims=True))
            out[epoch * look_rows : (epoch + 1) * look_rows, :] = whole(value * (jnp.exp2(-power) * GRADIENT_STEPS))
            powers.append(power)
        powers.append(jnp.zeros((HALO - epochs, LANES), jnp.float32))
        out[epochs * look_rows :, :] = whole(jnp.concatenate(powers, axis=0))


def return_kernel(tiles, *refs):
    coded, shared = refs[: tiles - 1], refs[tiles - 1 : -tiles]
    own, pieces = refs[-tiles], refs[1 - tiles :]
    total = shared[0][...]
    for other in shared[1:]:
        total = total + other[...]
    own[...] = total
    power = exponent_of(jnp.abs(total))
    share = total * jnp.exp2(-power) * float(1 << 14)
    high = jnp.floor(share + 0.5)
    low = (share - high) * float(1 << 15)
    parts = whole(jnp.concatenate([power, high, low, jnp.zeros_like(power)], axis=0))
    for piece, source in zip(pieces, coded):
        piece[: source.shape[0], :] = source[...]
        piece[source.shape[0] :, :] = parts


def update_kernel(cell_count, me, prev_mean, estimate, direction, gradient, sums, *refs):
    pieces = refs[:-2]
    new_estimate, new_direction = refs[-2:]
    tiles = len(pieces) + 1
    epochs = estimate.shape[0]
    look_rows = estimate.shape[1]
    coded_rows = epochs * look_rows + HALO
    total = sums[...]
    for piece in pieces:
        parts = number_of(piece[coded_rows:, :])
        value = (parts[8:16] + parts[16:24] * (1.0 / (1 << 15))) * (1.0 / (1 << 14))
        total = total + value * jnp.exp2(parts[:8])
    total = jnp.sum(total, axis=1, keepdims=True)
    grad_norm, crossed, grad_term, mixed, old_term = (total[at : at + 1, :] for at in range(5))
    momentum = grad_norm / cell_count / prev_mean[0]
    curvature = grad_term + 2.0 * momentum * mixed + momentum * momentum * old_term
    step = (grad_norm + momentum * crossed) / curvature
    momentum = jnp.broadcast_to(momentum, (look_rows, LANES))
    step = jnp.broadcast_to(step, (look_rows, LANES))
    for shift in range(tiles):
        tile = lax.bitwise_xor(me[0], shift)
        columns = pl.ds(pl.multiple_of(tile * LANES, LANES), LANES)
        if shift > 0:
            piece = pieces[shift - 1]
            scale = jnp.exp2(number_of(piece[epochs * look_rows : coded_rows, :])) * (1.0 / GRADIENT_STEPS)
        for epoch in range(epochs):
            if shift == 0:
                value = gradient[epoch]
            else:
                value = number_of(piece[epoch * look_rows : (epoch + 1) * look_rows, :]) * scale[epoch : epoch + 1, :]
            moved = value + momentum * direction[epoch, :, columns]
            new_direction[epoch, :, columns] = moved
            new_estimate[epoch, :, columns] = estimate[epoch, :, columns] + step * moved


def swapped(up, down, axis):
    size = lax.axis_size(axis)
    if size == 1:
        return jnp.zeros_like(up), jnp.zeros_like(down)
    if size == 2:
        first = lax.axis_index(axis) == 0
        got = lax.ppermute(jnp.where(first, up, down), axis, [(0, 1), (1, 0)])
        return got, got
    forward = [(i, i + 1) for i in range(size - 1)]
    backward = [(target, source) for source, target in forward]
    return lax.ppermute(up, axis, forward), lax.ppermute(down, axis, backward)


def exchanged(x, axis, by):
    size = lax.axis_size(axis)
    return lax.ppermute(x, axis, [(i, i ^ by) for i in range(size)])


def transposed_plan(slc, offsets, weights, estimate, direction, prev_mean):
    f32 = jnp.float32
    bf16 = jnp.bfloat16
    tiles = lax.axis_size("epoch")
    me = lax.axis_index("epoch")
    epochs, rows, columns = slc.shape[1:]
    look_rows = rows // LOOK
    total = tiles * epochs
    tile_rows = 2 * epochs * rows
    params_of = pltpu.CompilerParams(vmem_limit_bytes=VMEM_BYTES)

    sub = lax.axis_index("sub")
    outer_tile = (2, epochs, rows, LANES)
    edge = pl.pallas_call(
        edge_kernel,
        out_shape=jax.ShapeDtypeStruct((rows, LANES), bf16),
        grid=(1,),
        in_specs=[
            pl.BlockSpec(outer_tile, lambda _: (0, 0, 0, 0)),
            pl.BlockSpec(outer_tile, lambda _: (0, 0, 0, tiles - 1)),
        ],
        out_specs=pl.BlockSpec((rows, LANES), lambda _: (0, 0)),
        compiler_params=params_of,
        cost_estimate=pl.CostEstimate(flops=1_000_000, bytes_accessed=1_000_000, transcendentals=0),
    )(slc, slc)
    before, after = swapped(edge, edge, "sub")
    params = jnp.zeros((rows, LANES), f32)
    listed = jnp.concatenate([offsets.astype(f32), weights, weights, weights], axis=1)
    params = lax.dynamic_update_slice(params, listed, (0, PARAM_LANE))
    sub_present = jnp.stack([sub > 0, sub < lax.axis_size("sub") - 1]).astype(f32)
    messages = pl.pallas_call(
        pack_kernel,
        out_shape=(jax.ShapeDtypeStruct((tile_rows + rows, LANES), bf16),) * tiles,
        in_specs=[SMEM] * 2 + [VMEM] * 4,
        out_specs=(VMEM,) * tiles,
        scratch_shapes=[pltpu.VMEM((tiles, rows, LANES), bf16)],
        compiler_params=params_of,
        cost_estimate=pl.CostEstimate(flops=3_000_000, bytes_accessed=4_000_000, transcendentals=0),
    )(me.reshape(1), sub_present, slc, params, before, after)
    space = lax.axis_index("space")
    spaces = lax.axis_size("space")
    present = jnp.stack([space > 0, space < spaces - 1]).astype(f32)

    def halo(pieces):
        def border(from_row):
            cuts = [lax.dynamic_slice_in_dim(piece, from_row, HALO, axis=1).reshape(-1, LANES) for piece in pieces]
            return jnp.concatenate(cuts, axis=0)

        if spaces == 2:
            got = lax.ppermute(border(jnp.where(space == 0, rows - HALO, 0)), "space", [(0, 1), (1, 0)])
            return got, got
        return swapped(border(rows - HALO), border(0), "space")

    block = [messages[0]] + [exchanged(messages[by], "epoch", by) for by in range(1, tiles)]
    estimate, direction, _ = lax.optimization_barrier((estimate, direction, messages))
    fields = pl.pallas_call(
        fields_kernel,
        out_shape=(jax.ShapeDtypeStruct((2, epochs * look_rows, LANES), jnp.int16),) * tiles,
        in_specs=[SMEM] + [VMEM] * 2,
        out_specs=(VMEM,) * tiles,
        compiler_params=params_of,
        cost_estimate=pl.CostEstimate(flops=1_000_000, bytes_accessed=2_000_000, transcendentals=0),
    )(me.reshape(1), estimate, direction)
    def params_in(shift):
        return block[shift][tile_rows : tile_rows + epochs, PARAM_LANE : PARAM_LANE + 4 * SLOTS].astype(f32)

    halos = [halo([array.reshape(-1, rows, LANES)]) for array in block]
    late = lax.optimization_barrier((fields, block, halos[1:-1]))[0]
    field = [fields[0]] + [exchanged(late[by], "epoch", by) for by in range(1, tiles)]

    listed = jnp.concatenate([params_in(shift) for shift in range(tiles)], axis=0)
    place = jnp.arange(total, dtype=jnp.int32)[:, None]
    first = lax.bitwise_xor(place // epochs, me) * epochs + place % epochs
    mate = lax.rem(first + listed[:, :SLOTS].astype(jnp.int32), total)
    partner = (lax.bitwise_xor(mate // epochs, me) * epochs + mate % epochs).reshape(-1)
    weight = listed[:, SLOTS : 2 * SLOTS] + listed[:, 2 * SLOTS : 3 * SLOTS] + listed[:, 3 * SLOTS :]
    order = look_order(rows + 2 * HALO, HALO // LOOK - RADIUS)
    bands = column_bands()
    operands = list(block)
    places = []
    for shift in range(tiles):
        top, bottom = halos[shift]
        operands.append(top)
        top_at = bottom_at = len(operands) - 1
        if bottom is not top:
            operands.append(bottom)
            bottom_at = len(operands) - 1
        places.append((shift, top_at, bottom_at, 0, 0))
    looks = (rows + 2 * HALO) // LOOK
    group = 2 * SLOTS
    batches = tiles + total
    shape = jax.ShapeDtypeStruct((total * SLOTS, look_rows, LANES), f32)
    factors, pulls = pl.pallas_call(
        functools.partial(pair_kernel, (epochs, rows, len(operands)), tuple(places)),
        out_shape=(shape, shape),
        in_specs=[SMEM] * 3 + [VMEM] * (3 + len(operands)),
        out_specs=(VMEM, VMEM),
        scratch_shapes=[
            pltpu.VMEM((batches * group * look_rows, LANES), f32),
            pltpu.VMEM((2 * total, LOOK, looks, LANES), f32),
            pltpu.VMEM((2 * total, looks, LANES), f32),
            pltpu.VMEM((batches * group * looks, LANES), f32),
            pltpu.VMEM((batches * 2 * looks, LANES), f32),
            pltpu.VMEM((batches * group * looks, LANES), f32),
        ],
        compiler_params=params_of,
        cost_estimate=pl.CostEstimate(flops=20_000_000, bytes_accessed=30_000_000, transcendentals=0),
    )(partner, weight.reshape(-1), present, order, *bands, *operands)
    gradient, sums = pl.pallas_call(
        functools.partial(gradient_kernel, (tiles, epochs)),
        out_shape=(
            jax.ShapeDtypeStruct((total, look_rows, LANES), f32),
            jax.ShapeDtypeStruct((8, LANES), f32),
        ),
        in_specs=[SMEM] + [VMEM] * (tiles + 2),
        out_specs=(VMEM, VMEM),
        scratch_shapes=[pltpu.VMEM((total, look_rows, LANES), f32)] * 2
        + [pltpu.VMEM((total * SLOTS, look_rows, LANES), f32)],
        compiler_params=params_of,
        cost_estimate=pl.CostEstimate(flops=10_000_000, bytes_accessed=8_000_000, transcendentals=0),
    )(partner, *field, factors, pulls)

    place = ("space", "sub")
    count = spaces * lax.axis_size("sub")
    shared = [sums] + [lax.ppermute(sums, place, [(i, (i + by) % count) for i in range(count)]) for by in range(1, count)]
    coded_shape = jax.ShapeDtypeStruct((epochs * look_rows + HALO, LANES), jnp.int16)
    coded = pl.pallas_call(
        code_kernel,
        out_shape=(coded_shape,) * (tiles - 1),
        in_specs=[VMEM],
        out_specs=(VMEM,) * (tiles - 1),
        compiler_params=params_of,
        cost_estimate=pl.CostEstimate(flops=1_000_000, bytes_accessed=1_000_000, transcendentals=0),
    )(gradient)
    piece_shape = jax.ShapeDtypeStruct((epochs * look_rows + HALO + 32, LANES), jnp.int16)
    own_sums, *pieces = pl.pallas_call(
        functools.partial(return_kernel, tiles),
        out_shape=(jax.ShapeDtypeStruct((8, LANES), f32),) + (piece_shape,) * (tiles - 1),
        in_specs=[VMEM] * (tiles - 1 + count),
        out_specs=(VMEM,) * tiles,
        compiler_params=params_of,
        cost_estimate=pl.CostEstimate(flops=10_000, bytes_accessed=1_000_000, transcendentals=0),
    )(*coded, *shared)
    returned = [exchanged(piece, "epoch", by + 1) for by, piece in enumerate(pieces)]
    cell_count = float(total * look_rows * spaces * columns * lax.axis_size("sub"))
    return pl.pallas_call(
        functools.partial(update_kernel, cell_count),
        out_shape=(jax.ShapeDtypeStruct(estimate.shape, f32),) * 2,
        in_specs=[SMEM] * 2 + [VMEM] * (3 + tiles),
        out_specs=(VMEM, VMEM),
        compiler_params=params_of,
        cost_estimate=pl.CostEstimate(flops=1_000_000, bytes_accessed=2_000_000, transcendentals=0),
    )(me.reshape(1), prev_mean, estimate, direction, gradient[:epochs], own_sums, *returned)


def on_device(slc, offsets, weights, estimate, direction, prev_mean):
    epochs, rows, columns = slc.shape[1:]
    fits = columns == LANES * lax.axis_size("epoch") and lax.axis_size("epoch") > 1
    size = lax.axis_size("epoch")
    fits = fits and size & (size - 1) == 0 and 2 * epochs * SIDES <= PARAM_LANE and rows % HALO == 0 and epochs == 2 * SLOTS
    plan = transposed_plan if fits else ring_plan
    return plan(slc, offsets, weights, estimate, direction, prev_mean)


def solution(mesh):
    return jax.shard_map(
        on_device,
        mesh=mesh,
        in_specs=(
            P(None, ("groups", "epoch"), "space", "sub"),
            P(("groups", "epoch"), None),
            P(("groups", "epoch"), None),
            P(("groups", "epoch"), "space", "sub"),
            P(("groups", "epoch"), "space", "sub"),
            P(),
        ),
        out_specs=(P(("groups", "epoch"), "space", "sub"), P(("groups", "epoch"), "space", "sub")),
        check_vma=False,
    )
```

```python
import functools
import math

import jax
import jax.numpy as jnp
import numpy as np
from jax import lax
from jax.experimental import pallas as pl
from jax.experimental.pallas import tpu as pltpu
from jax.sharding import PartitionSpec as P

SLOTS = 4
OFFS = 8
LOOK = 4
RADIUS = 3


EPSILON = 1e-06


def passed_along(x, axis, by):
    size = lax.axis_size(axis)
    return lax.ppermute(x, axis, [(i, (i + by) % size) for i in range(size)])


def extended_2(block, sides, width):
    for axis, dim in sides:
        count = lax.axis_size(axis)
        forward = [(i, i + 1) for i in range(count - 1)]
        backward = [(target, source) for source, target in forward]
        low = lax.ppermute(
            lax.slice_in_dim(block, block.shape[dim] - width, None, axis=dim), axis, forward
        )
        high = lax.ppermute(lax.slice_in_dim(block, 0, width, axis=dim), axis, backward)
        block = jnp.concatenate([low, block, high], axis=dim)
    return block


def looked_sum(field):
    shape = field.shape
    return jnp.sum(field.reshape(shape[:-2] + (shape[-2] // LOOK, LOOK, shape[-1])), axis=-2)


def window_sum(padded, axis):
    length = padded.shape[axis] - 2 * RADIUS
    total = lax.slice_in_dim(padded, 0, length, axis=axis)
    for shift_at in range(1, 2 * RADIUS + 1):
        total = total + lax.slice_in_dim(padded, shift_at, shift_at + length, axis=axis)
    return total


def ring_plan(slc, offsets, weights, estimate, direction, prev_mean):
    epochs_here = slc.shape[1]
    look_rows = slc.shape[2] // LOOK
    col_count = slc.shape[3]
    ahead = passed_along(slc, "epoch", -1)
    extended = jnp.concatenate([slc, ahead], axis=1)
    numbers = jnp.arange(epochs_here, dtype=jnp.int32)
    partner = numbers[:, None] + offsets
    own_real = slc[0].astype(jnp.float32)
    own_imag = slc[1].astype(jnp.float32)
    ext_real = extended[0].astype(jnp.float32)
    ext_imag = extended[1].astype(jnp.float32)
    powers = looked_sum(ext_real * ext_real + ext_imag * ext_imag)
    pieces = []
    for slot_index in range(SLOTS):
        mate_real = jnp.take(ext_real, partner[:, slot_index], axis=0)
        mate_imag = jnp.take(ext_imag, partner[:, slot_index], axis=0)
        pieces.append(looked_sum(own_real * mate_real + own_imag * mate_imag))
        pieces.append(looked_sum(own_imag * mate_real - own_real * mate_imag))
    pair_count = epochs_here * 2 * SLOTS
    stacked = jnp.concatenate(
        [jnp.stack(pieces, axis=1).reshape(pair_count, look_rows, col_count), powers], axis=0
    )
    padded = extended_2(stacked, (("space", 1), ("sub", 2)), RADIUS)
    boxed = window_sum(window_sum(padded, 1), 2)
    pair_boxed = boxed[:pair_count].reshape(epochs_here, 2 * SLOTS, look_rows, col_count)
    power_box = boxed[pair_count:]
    coh_real = pair_boxed[:, 0::2]
    coh_imag = pair_boxed[:, 1::2]
    denominator = power_box[:epochs_here, None] * jnp.take(power_box, partner, axis=0) + EPSILON
    coherence = (coh_real * coh_real + coh_imag * coh_imag) / denominator
    observed = coh_imag / jnp.sqrt(denominator)
    est_ahead = passed_along(estimate, "epoch", -1)
    est_extended = jnp.concatenate([estimate, est_ahead], axis=0)
    fitted = estimate[:, None] - jnp.take(est_extended, partner, axis=0)
    factor = weights[:, :, None, None] * coherence
    weighted = factor * (observed - fitted)
    flattened = weighted.reshape(epochs_here * SLOTS, look_rows * col_count)
    selector = (
        jnp.arange(epochs_here + OFFS, dtype=jnp.int32)[:, None] == partner.reshape(1, -1)
    ).astype(jnp.float32)
    gathered = jnp.dot(
        selector, flattened, precision=lax.Precision.HIGHEST, preferred_element_type=jnp.float32
    ).reshape(epochs_here + OFFS, look_rows, col_count)
    own_part = jnp.sum(weighted, axis=1) - gathered[:epochs_here]
    returned = passed_along(-gathered[epochs_here:], "epoch", 1)
    gradient = jnp.concatenate([own_part + returned, own_part[OFFS:]], axis=0)
    cell_count = float(
        epochs_here
        * lax.axis_size("epoch")
        * look_rows
        * lax.axis_size("space")
        * col_count
        * lax.axis_size("sub")
    )
    local_norm = jnp.sum(gradient * gradient)
    local_crossed = jnp.sum(gradient * direction)
    mean_before = prev_mean[0]
    fields_ahead = passed_along(
        jnp.stack([gradient, direction]).astype(jnp.bfloat16), "epoch", -1
    ).astype(jnp.float32)
    grad_extended = jnp.concatenate([gradient, fields_ahead[0]], axis=0)
    old_extended = jnp.concatenate([direction, fields_ahead[1]], axis=0)
    grad_spread = gradient[:, None] - jnp.take(grad_extended, partner, axis=0)
    old_spread = direction[:, None] - jnp.take(old_extended, partner, axis=0)
    totals = lax.psum(
        (
            local_norm,
            local_crossed,
            jnp.sum(factor * grad_spread * grad_spread),
            jnp.sum(factor * grad_spread * old_spread),
            jnp.sum(factor * old_spread * old_spread),
        ),
        ("epoch", "space", "sub"),
    )
    grad_norm, crossed, grad_term, mixed_term, old_term = totals
    momentum = grad_norm / cell_count / mean_before
    new_direction = gradient + momentum * direction
    curvature = grad_term + 2.0 * momentum * mixed_term + momentum * momentum * old_term
    along_sum = grad_norm + momentum * crossed
    step_size = along_sum / curvature
    return (estimate + step_size * new_direction, new_direction)


LANES = 128
SIDES = 2 * RADIUS
HALO = 16
FIELD_STEPS = 16383.0
GRADIENT_STEPS = 32000.0
PARAM_LANE = 96
VMEM = pl.BlockSpec(memory_space=pltpu.VMEM)
SMEM = pl.BlockSpec(memory_space=pltpu.SMEM)
VMEM_BYTES = 48 * 1024 * 1024


def split_two(value):
    high = value.astype(jnp.bfloat16)
    low = (value - high.astype(jnp.float32)).astype(jnp.bfloat16)
    return high, low


def edge_kernel(first, last, edge):
    epochs = first.shape[1]
    lane = lax.broadcasted_iota(jnp.int32, edge.shape, 1)
    total = jnp.zeros(edge.shape, jnp.float32)
    for part in range(2):
        for epoch in range(epochs):
            at = (part * epochs + epoch) * SIDES
            total = placed(lane, total, tile_of(last, part, epoch, 0), LANES - RADIUS, at)
            total = placed(lane, total, tile_of(first, part, epoch, 0), 0, at + RADIUS)
    edge[...] = total.astype(jnp.bfloat16)


def fixed_point(value):
    return jnp.floor(value * FIELD_STEPS + 0.5).astype(jnp.int32).astype(jnp.int16)


def from_fixed_point(value):
    return value.astype(jnp.int32).astype(jnp.float32) * (1.0 / FIELD_STEPS)


def fields_kernel(me, estimate, direction, *fields):
    look_rows = estimate.shape[1]
    tiles = len(fields)
    for shift, out in enumerate(fields):
        tile = lax.bitwise_xor(me[0], shift)
        columns = pl.ds(pl.multiple_of(tile * LANES, LANES), LANES)
        for epoch in range(estimate.shape[0]):
            here = slice(epoch * look_rows, (epoch + 1) * look_rows)
            out[0, here, :] = fixed_point(estimate[epoch, :, columns])
            out[1, here, :] = fixed_point(direction[epoch, :, columns])


def tile_of(slc, part, epoch, tile):
    return slc[part, epoch, :, tile * LANES : (tile + 1) * LANES].astype(jnp.float32)


def placed(lane, total, source, start, target):
    moved = pltpu.roll(source, (target - start) % LANES, axis=1)
    return jnp.where((lane >= target) & (lane < target + RADIUS), moved, total)


def pack_kernel(me, present, slc, params, before, after, *refs):
    messages, strips = refs[:-1], refs[-1]
    tiles = len(messages)
    epochs = slc.shape[1]
    rows = slc.shape[2]
    lane = lax.broadcasted_iota(jnp.int32, (rows, LANES), 1)
    value = params[...]
    high = value.astype(jnp.bfloat16).astype(jnp.float32)
    middle = (value - high).astype(jnp.bfloat16).astype(jnp.float32)
    low = value - high - middle
    third = PARAM_LANE + 2 * SLOTS
    split = jnp.where(lane < third, high, jnp.where(lane < third + SLOTS, middle, low))
    split = jnp.where(lane >= PARAM_LANE, split, 0.0)
    inside = lane < 2 * epochs * SIDES
    for tile in range(tiles):
        total = split
        if tile == 0:
            edge = before[...].astype(jnp.float32) * present[0]
            total = jnp.where(inside & (lane % SIDES < RADIUS), edge, total)
        if tile == tiles - 1:
            edge = after[...].astype(jnp.float32) * present[1]
            total = jnp.where(inside & (lane % SIDES >= RADIUS), edge, total)
        for part in range(2):
            for epoch in range(epochs):
                at = (part * epochs + epoch) * SIDES
                if tile > 0:
                    total = placed(lane, total, tile_of(slc, part, epoch, tile - 1), LANES - RADIUS, at)
                if tile < tiles - 1:
                    total = placed(lane, total, tile_of(slc, part, epoch, tile + 1), 0, at + RADIUS)
        strips[tile] = total.astype(jnp.bfloat16)
    for tile in range(tiles):
        shift = lax.bitwise_xor(me[0], tile)
        for number, message in enumerate(messages):

            @pl.when(shift == number)
            def _():
                for part in range(2):
                    for epoch in range(epochs):
                        at = (part * epochs + epoch) * rows
                        message[at : at + rows, :] = slc[part, epoch, :, tile * LANES : (tile + 1) * LANES]
                message[2 * epochs * rows :, :] = strips[tile]


def look_order(from_rows, first):
    looks = from_rows // LOOK
    to = np.arange(from_rows)[:, None]
    at = np.arange(from_rows)[None, :]
    return jnp.asarray(at == (to + first) % looks * LOOK + to // looks, jnp.bfloat16)


def unpack_tiles(order, sources, main, first, columns_of):
    looks = order.shape[0] // LOOK
    for start in range(0, len(sources), 4):
        parts = jnp.concatenate([columns_of(source) for source in sources[start : start + 4]], axis=1)
        value = jnp.dot(order, parts, preferred_element_type=jnp.float32)
        for one in range(4):
            for look in range(LOOK):
                main[first[start + one], look] = value[look * looks : (look + 1) * looks, one * LANES : (one + 1) * LANES]


def unpack_rims(by_look, looks, rim, first):
    share = LANES // SLOTS
    lane = lax.broadcasted_iota(jnp.int32, (looks, LANES), 1)
    for at, place in enumerate(first):
        value = jnp.zeros((looks, LANES), jnp.float32)
        for look in range(LOOK):
            target = look * SIDES
            moved = pltpu.roll(by_look[look * looks : (look + 1) * looks], (target - at * SIDES) % LANES, axis=1)
            value = jnp.where((lane >= target) & (lane < target + SIDES), moved, value)
        spread = share
        while spread < LANES:
            value = value + pltpu.roll(value, spread, axis=1)
            spread = 2 * spread
        rim[place] = value


def column_bands():
    share = LANES // SLOTS
    at = np.arange(2 * LANES)[:, None] % LANES
    to = np.arange(LANES)[None, :]
    side = at % share % SIDES
    source = np.where(side < RADIUS, side - RADIUS, LANES + side - RADIUS)
    column = (to - at // share * share) % LANES
    inside = (column < RADIUS) | (column >= LANES - RADIUS)
    inside = inside & (at % share < LOOK * SIDES)
    band = np.abs(at - to) <= RADIUS
    rim_band = inside & (np.abs(source - column) <= RADIUS)
    return jnp.asarray(band, jnp.bfloat16), jnp.asarray(rim_band, jnp.bfloat16)


def mixed(values):
    lane = lax.broadcasted_iota(jnp.int32, values[0].shape, 1)
    result = values[-1]
    for slot in range(SLOTS - 1):
        result = jnp.where(lane < (SLOTS - 1 - slot) * (LANES // SLOTS), values[SLOTS - 2 - slot], result)
    return result


def power_batches(blocks, epochs, looks, main, rim, looked, rim_looked):
    total = blocks * epochs
    group = 2 * SLOTS
    for block in range(blocks):
        for piece in range(0, looks, 8):
            rows_at = slice(piece, piece + 8)
            for half in range(2):
                squares = []
                for slot in range(SLOTS):
                    channel = half * SLOTS + slot
                    epoch = block * epochs + channel
                    value = None
                    for look in range(LOOK):
                        real = main[epoch, look, rows_at]
                        imag = main[total + epoch, look, rows_at]
                        one = real * real + imag * imag
                        value = one if value is None else value + one
                    at = (block * group + channel) * looks + piece
                    looked[at : at + 8, :] = value
                    real = rim[epoch, rows_at]
                    imag = rim[total + epoch, rows_at]
                    squares.append(real * real + imag * imag)
                at = (block * 2 + half) * looks + piece
                rim_looked[at : at + 8, :] = mixed(squares)


def pair_batch(epoch, mates, total, main, rim):
    own_re, own_im = main[epoch], main[total + epoch]
    reals, imags = [], []
    for mate in mates:
        mate_re, mate_im = main[mate], main[total + mate]
        real = own_re[0] * mate_re[0] + own_im[0] * mate_im[0]
        imag = own_im[0] * mate_re[0] - own_re[0] * mate_im[0]
        for look in range(1, LOOK):
            real = real + (own_re[look] * mate_re[look] + own_im[look] * mate_im[look])
            imag = imag + (own_im[look] * mate_re[look] - own_re[look] * mate_im[look])
        reals.append(real)
        imags.append(imag)
    own_re, own_im = rim[epoch], rim[total + epoch]
    mate_re = mixed([rim[mate] for mate in mates])
    mate_im = mixed([rim[total + mate] for mate in mates])
    rims = [own_re * mate_re + own_im * mate_im, own_im * mate_re - own_re * mate_im]
    return reals + imags, rims


def put(ref, block, values):
    rows = sum(value.shape[0] for value in values)
    ref[block * rows : (block + 1) * rows, :] = jnp.concatenate(values, axis=0)


def columns_summed(couple, looks, bands, looked, rim_looked):
    group = 2 * SLOTS
    f32 = jnp.float32
    at = slice(couple * 2 * group * looks, (couple + 1) * 2 * group * looks)
    halves = jnp.concatenate(split_two(looked[at, :]), axis=1)
    value = jnp.dot(halves, bands[0], preferred_element_type=f32)
    at = slice(couple * 4 * looks, (couple + 1) * 4 * looks)
    halves = jnp.concatenate(split_two(rim_looked[at, :]), axis=1)
    outer = jnp.dot(halves, bands[1], preferred_element_type=f32)
    lane = lax.broadcasted_iota(jnp.int32, (looks, LANES), 1)
    outside = (lane < RADIUS) | (lane >= LANES - RADIUS)
    results = []
    for channel in range(2 * group):
        batch, half, slot = channel // group, channel % group // SLOTS, channel % SLOTS
        row = (batch * 2 + half) * looks
        part = outer[row : row + looks]
        if slot > 0:
            part = pltpu.roll(part, LANES - slot * (LANES // SLOTS), axis=1)
        row = channel * looks
        results.append(value[row : row + looks] + jnp.where(outside, part, 0.0))
    return results


def rows_summed(channel, looks, look_rows, wide):
    first = channel * looks
    total = wide[pl.ds(first, look_rows), :]
    for shift in range(1, 2 * RADIUS + 1):
        total = total + wide[pl.ds(first + shift, look_rows), :]
    return total


def pair_couple(couple, total, partner, main, rim):
    products, rims = [], []
    for one in range(2):
        epoch = couple * 2 + one
        mates = [partner[epoch * SLOTS + slot] for slot in range(SLOTS)]
        more, more_rims = pair_batch(epoch, mates, total, main, rim)
        products += more
        rims += more_rims
    return products, rims


def clipped(value, last):
    return jnp.minimum(jnp.maximum(value, 0), last)


def pair_kernel(sizes, places, partner, weight, present, order, band, rim_band, *refs):
    epochs, rows, operands = sizes
    inputs = refs[:operands]
    factors, pulls, boxed, main, rim, looked, rim_looked, wide = refs[operands:]
    count = len(places)
    total = count * epochs
    look_rows = rows // LOOK
    halo_looks = HALO // LOOK
    looks = look_rows + 2 * halo_looks
    full_rows = rows + 2 * HALO
    group = 2 * SLOTS

    at = lax.broadcasted_iota(jnp.int32, (full_rows, full_rows), 1)
    keep = jnp.where(at < HALO, present[0], jnp.where(at >= HALO + rows, present[1], 1.0))
    order = (order[...].astype(jnp.float32) * keep).astype(jnp.bfloat16)
    bands = band[...], rim_band[...]
    for block, (tile_at, top_at, bottom_at, top_row, bottom_row) in enumerate(places):
        tile, top, bottom = inputs[tile_at], inputs[top_at], inputs[bottom_at]

        def rows_of(at):
            above = top[top_row + at * HALO : top_row + (at + 1) * HALO, :]
            below = bottom[bottom_row + at * HALO : bottom_row + (at + 1) * HALO, :]
            return jnp.concatenate([above, tile[at * rows : (at + 1) * rows, :], below], axis=0)

        first = [part * total + block * epochs + epoch for part in range(2) for epoch in range(epochs)]
        unpack_tiles(order, range(2 * epochs), main, first, rows_of)
        by_look = jnp.dot(order, rows_of(2 * epochs), preferred_element_type=jnp.float32)
        unpack_rims(by_look, looks, rim, first)
    power_batches(count, epochs, looks, main, rim, looked, rim_looked)
    powers = count // 2
    couples = total // 2

    def boxed_of(channel):
        return boxed[pl.ds(pl.multiple_of(channel * look_rows, look_rows), look_rows), :]

    def finished(couple):
        results = []
        for one in range(2):
            epoch = couple * 2 + one
            own_power = boxed_of(epoch)
            first = (2 * powers + epoch) * (group * look_rows)
            parts = boxed[first : first + group * look_rows, :]
            parts = parts.reshape(group, look_rows, LANES)
            for slot in range(SLOTS):
                pair = epoch * SLOTS + slot
                inverse = lax.rsqrt(own_power * boxed_of(partner[pair]) + EPSILON)
                unit_re = parts[slot] * inverse
                unit_im = parts[SLOTS + slot] * inverse
                factor = weight[pair] * (unit_re * unit_re + unit_im * unit_im)
                results.append((factor, factor * unit_im))
        return results

    def boxes(couple):
        return [rows_summed(couple * 2 * group + one, looks, look_rows, wide) for one in range(2 * group)]

    def turn(number, steps):
        if 3 in steps:
            results = finished(number - 3)
        if 2 in steps:
            sums = boxes(powers + number - 2)
        if 1 in steps:
            columns = columns_summed(powers + number - 1, looks, bands, looked, rim_looked)
        if 0 in steps:
            products, rims = pair_couple(number, total, partner, main, rim)
        if 3 in steps:
            for ref, values in zip((factors, pulls), zip(*results)):
                ref[pl.ds((number - 3) * 2 * SLOTS, 2 * SLOTS)] = jnp.stack(values)
        if 2 in steps:
            put(boxed, powers + number - 2, sums)
        if 1 in steps:
            put(wide, powers + number - 1, columns)
        if 0 in steps:
            put(looked, powers + number, products)
            put(rim_looked, powers + number, rims)

    for couple in range(powers):
        put(wide, couple, columns_summed(couple, looks, bands, looked, rim_looked))
    turn(0, (0,))
    for couple in range(powers):
        put(boxed, couple, boxes(couple))
    turn(1, (0, 1))
    turn(2, (0, 1, 2))
    for number in range(3, couples):
        turn(number, (0, 1, 2, 3))
    turn(couples, (1, 2, 3))
    turn(couples + 1, (2, 3))
    turn(couples + 2, (3,))


def gradient_kernel(sizes, partner, *refs):
    tiles, epochs = sizes
    fields = refs[:tiles]
    factors, pulls, gradient, sums, est, old, shares = refs[tiles:]
    look_rows = est.shape[1]
    total = tiles * epochs
    f32 = jnp.float32
    for block in range(tiles):
        for epoch in range(epochs):
            here = slice(epoch * look_rows, (epoch + 1) * look_rows)
            est[block * epochs + epoch] = from_fixed_point(fields[block][0, here, :])
            old[block * epochs + epoch] = from_fixed_point(fields[block][1, here, :])
    mates = [[partner[epoch * SLOTS + slot] for slot in range(SLOTS)] for epoch in range(total)]
    for epoch in range(total):
        own_est = est[epoch]
        own = None
        for slot, mate in enumerate(mates[epoch]):
            pair = epoch * SLOTS + slot
            weighted = pulls[pair] - factors[pair] * (own_est - est[mate])
            own = weighted if own is None else own + weighted
            shares[pair] = weighted
        gradient[epoch] = own
    for epoch in range(total):
        values = [gradient[mate] - shares[epoch * SLOTS + slot] for slot, mate in enumerate(mates[epoch])]
        for mate, value in zip(mates[epoch], values):
            gradient[mate] = value

    zero = jnp.zeros((look_rows, LANES), f32)
    norm, crossed, grad_term, mixed_term, old_term = (zero,) * 5
    for epoch in range(total):
        own_grad = gradient[epoch]
        own_old = old[epoch]
        norm = norm + own_grad * own_grad
        crossed = crossed + own_grad * own_old
        for slot, mate in enumerate(mates[epoch]):
            factor = factors[epoch * SLOTS + slot]
            grad_spread = own_grad - gradient[mate]
            old_spread = own_old - old[mate]
            pulled = factor * grad_spread
            grad_term = grad_term + pulled * grad_spread
            mixed_term = mixed_term + pulled * old_spread
            old_term = old_term + factor * old_spread * old_spread
    sums[...] = jnp.zeros(sums.shape, f32)
    for at, value in enumerate((norm, crossed, grad_term, mixed_term, old_term)):
        sums[at : at + 1, :] = jnp.sum(value, axis=0, keepdims=True)


def exponent_of(size):
    power = jnp.ceil(jnp.log(jnp.maximum(size, 1e-30)) * (1.0 / math.log(2.0)))
    return jnp.clip(power, -110.0, 110.0)


def whole(value):
    return jnp.floor(value + 0.5).astype(jnp.int32).astype(jnp.int16)


def number_of(value):
    return value.astype(jnp.int32).astype(jnp.float32)


def code_kernel(gradient, *coded):
    epochs = gradient.shape[0] // (len(coded) + 1)
    look_rows = gradient.shape[1]
    for number, out in enumerate(coded):
        powers = []
        for epoch in range(epochs):
            value = gradient[(number + 1) * epochs + epoch]
            power = exponent_of(jnp.max(jnp.abs(value), axis=0, keepdims=True))
            out[epoch * look_rows : (epoch + 1) * look_rows, :] = whole(value * (jnp.exp2(-power) * GRADIENT_STEPS))
            powers.append(power)
        powers.append(jnp.zeros((HALO - epochs, LANES), jnp.float32))
        out[epochs * look_rows :, :] = whole(jnp.concatenate(powers, axis=0))


def return_kernel(tiles, *refs):
    coded, shared = refs[: tiles - 1], refs[tiles - 1 : -tiles]
    own, pieces = refs[-tiles], refs[1 - tiles :]
    total = shared[0][...]
    for other in shared[1:]:
        total = total + other[...]
    own[...] = total
    power = exponent_of(jnp.abs(total))
    share = total * jnp.exp2(-power) * float(1 << 14)
    high = jnp.floor(share + 0.5)
    low = (share - high) * float(1 << 15)
    parts = whole(jnp.concatenate([power, high, low, jnp.zeros_like(power)], axis=0))
    for piece, source in zip(pieces, coded):
        piece[: source.shape[0], :] = source[...]
        piece[source.shape[0] :, :] = parts


def update_kernel(cell_count, me, prev_mean, estimate, direction, gradient, sums, *refs):
    pieces = refs[:-2]
    new_estimate, new_direction = refs[-2:]
    tiles = len(pieces) + 1
    epochs = estimate.shape[0]
    look_rows = estimate.shape[1]
    coded_rows = epochs * look_rows + HALO
    total = sums[...]
    for piece in pieces:
        parts = number_of(piece[coded_rows:, :])
        value = (parts[8:16] + parts[16:24] * (1.0 / (1 << 15))) * (1.0 / (1 << 14))
        total = total + value * jnp.exp2(parts[:8])
    total = jnp.sum(total, axis=1, keepdims=True)
    grad_norm, crossed, grad_term, mixed, old_term = (total[at : at + 1, :] for at in range(5))
    momentum = grad_norm / cell_count / prev_mean[0]
    curvature = grad_term + 2.0 * momentum * mixed + momentum * momentum * old_term
    step = (grad_norm + momentum * crossed) / curvature
    momentum = jnp.broadcast_to(momentum, (look_rows, LANES))
    step = jnp.broadcast_to(step, (look_rows, LANES))
    for shift in range(tiles):
        tile = lax.bitwise_xor(me[0], shift)
        columns = pl.ds(pl.multiple_of(tile * LANES, LANES), LANES)
        if shift > 0:
            piece = pieces[shift - 1]
            scale = jnp.exp2(number_of(piece[epochs * look_rows : coded_rows, :])) * (1.0 / GRADIENT_STEPS)
        for epoch in range(epochs):
            if shift == 0:
                value = gradient[epoch]
            else:
                value = number_of(piece[epoch * look_rows : (epoch + 1) * look_rows, :]) * scale[epoch : epoch + 1, :]
            moved = value + momentum * direction[epoch, :, columns]
            new_direction[epoch, :, columns] = moved
            new_estimate[epoch, :, columns] = estimate[epoch, :, columns] + step * moved


def swapped(up, down, axis):
    size = lax.axis_size(axis)
    if size == 1:
        return jnp.zeros_like(up), jnp.zeros_like(down)
    if size == 2:
        first = lax.axis_index(axis) == 0
        got = lax.ppermute(jnp.where(first, up, down), axis, [(0, 1), (1, 0)])
        return got, got
    forward = [(i, i + 1) for i in range(size - 1)]
    backward = [(target, source) for source, target in forward]
    return lax.ppermute(up, axis, forward), lax.ppermute(down, axis, backward)


def exchanged(x, axis, by):
    size = lax.axis_size(axis)
    return lax.ppermute(x, axis, [(i, i ^ by) for i in range(size)])


def transposed_plan(slc, offsets, weights, estimate, direction, prev_mean):
    f32 = jnp.float32
    bf16 = jnp.bfloat16
    tiles = lax.axis_size("epoch")
    me = lax.axis_index("epoch")
    epochs, rows, columns = slc.shape[1:]
    look_rows = rows // LOOK
    total = tiles * epochs
    tile_rows = 2 * epochs * rows
    params_of = pltpu.CompilerParams(vmem_limit_bytes=VMEM_BYTES)

    sub = lax.axis_index("sub")
    outer_tile = (2, epochs, rows, LANES)
    edge = pl.pallas_call(
        edge_kernel,
        out_shape=jax.ShapeDtypeStruct((rows, LANES), bf16),
        grid=(1,),
        in_specs=[
            pl.BlockSpec(outer_tile, lambda _: (0, 0, 0, 0)),
            pl.BlockSpec(outer_tile, lambda _: (0, 0, 0, tiles - 1)),
        ],
        out_specs=pl.BlockSpec((rows, LANES), lambda _: (0, 0)),
        compiler_params=params_of,
        cost_estimate=pl.CostEstimate(flops=1_000_000, bytes_accessed=1_000_000, transcendentals=0),
    )(slc, slc)
    before, after = swapped(edge, edge, "sub")
    params = jnp.zeros((rows, LANES), f32)
    listed = jnp.concatenate([offsets.astype(f32), weights, weights, weights], axis=1)
    params = lax.dynamic_update_slice(params, listed, (0, PARAM_LANE))
    sub_present = jnp.stack([sub > 0, sub < lax.axis_size("sub") - 1]).astype(f32)
    messages = pl.pallas_call(
        pack_kernel,
        out_shape=(jax.ShapeDtypeStruct((tile_rows + rows, LANES), bf16),) * tiles,
        in_specs=[SMEM] * 2 + [VMEM] * 4,
        out_specs=(VMEM,) * tiles,
        scratch_shapes=[pltpu.VMEM((tiles, rows, LANES), bf16)],
        compiler_params=params_of,
        cost_estimate=pl.CostEstimate(flops=3_000_000, bytes_accessed=4_000_000, transcendentals=0),
    )(me.reshape(1), sub_present, slc, params, before, after)
    space = lax.axis_index("space")
    spaces = lax.axis_size("space")
    present = jnp.stack([space > 0, space < spaces - 1]).astype(f32)

    def halo(pieces):
        def border(from_row):
            cuts = [lax.dynamic_slice_in_dim(piece, from_row, HALO, axis=1).reshape(-1, LANES) for piece in pieces]
            return jnp.concatenate(cuts, axis=0)

        if spaces == 2:
            got = lax.ppermute(border(jnp.where(space == 0, rows - HALO, 0)), "space", [(0, 1), (1, 0)])
            return got, got
        return swapped(border(rows - HALO), border(0), "space")

    turns = sorted(range(1, tiles), key=lambda by: (by == tiles - 1, by == 1))
    block = {by: exchanged(messages[by], "epoch", by) for by in turns}
    block[0] = messages[0]
    estimate, direction, _ = lax.optimization_barrier((estimate, direction, messages))
    fields = pl.pallas_call(
        fields_kernel,
        out_shape=(jax.ShapeDtypeStruct((2, epochs * look_rows, LANES), jnp.int16),) * tiles,
        in_specs=[SMEM] + [VMEM] * 2,
        out_specs=(VMEM,) * tiles,
        compiler_params=params_of,
        cost_estimate=pl.CostEstimate(flops=1_000_000, bytes_accessed=2_000_000, transcendentals=0),
    )(me.reshape(1), estimate, direction)
    def params_in(shift):
        return block[shift][tile_rows : tile_rows + epochs, PARAM_LANE : PARAM_LANE + 4 * SLOTS].astype(f32)

    halos = {by: halo([block[by].reshape(-1, rows, LANES)]) for by in [0] + turns}
    field = {0: fields[0]}
    for at, by in enumerate(turns):
        awaited = [halos[0]] + [block[other] for other in turns[: at + 1]]
        if by == turns[-1]:
            awaited += [halos[other] for other in turns[:-1]]
        field[by] = exchanged(lax.optimization_barrier((fields[by], awaited))[0], "epoch", by)
    block, field = ([array[by] for by in range(tiles)] for array in (block, field))

    listed = jnp.concatenate([params_in(shift) for shift in range(tiles)], axis=0)
    place = jnp.arange(total, dtype=jnp.int32)[:, None]
    first = lax.bitwise_xor(place // epochs, me) * epochs + place % epochs
    mate = lax.rem(first + listed[:, :SLOTS].astype(jnp.int32), total)
    partner = (lax.bitwise_xor(mate // epochs, me) * epochs + mate % epochs).reshape(-1)
    weight = listed[:, SLOTS : 2 * SLOTS] + listed[:, 2 * SLOTS : 3 * SLOTS] + listed[:, 3 * SLOTS :]
    order = look_order(rows + 2 * HALO, HALO // LOOK - RADIUS)
    bands = column_bands()
    operands = list(block)
    places = []
    for shift in range(tiles):
        top, bottom = halos[shift]
        operands.append(top)
        top_at = bottom_at = len(operands) - 1
        if bottom is not top:
            operands.append(bottom)
            bottom_at = len(operands) - 1
        places.append((shift, top_at, bottom_at, 0, 0))
    looks = (rows + 2 * HALO) // LOOK
    group = 2 * SLOTS
    batches = tiles + total
    shape = jax.ShapeDtypeStruct((total * SLOTS, look_rows, LANES), f32)
    factors, pulls = pl.pallas_call(
        functools.partial(pair_kernel, (epochs, rows, len(operands)), tuple(places)),
        out_shape=(shape, shape),
        in_specs=[SMEM] * 3 + [VMEM] * (3 + len(operands)),
        out_specs=(VMEM, VMEM),
        scratch_shapes=[
            pltpu.VMEM((batches * group * look_rows, LANES), f32),
            pltpu.VMEM((2 * total, LOOK, looks, LANES), f32),
            pltpu.VMEM((2 * total, looks, LANES), f32),
            pltpu.VMEM((batches * group * looks, LANES), f32),
            pltpu.VMEM((batches * 2 * looks, LANES), f32),
            pltpu.VMEM((batches * group * looks, LANES), f32),
        ],
        compiler_params=params_of,
        cost_estimate=pl.CostEstimate(flops=20_000_000, bytes_accessed=30_000_000, transcendentals=0),
    )(partner, weight.reshape(-1), present, order, *bands, *operands)
    gradient, sums = pl.pallas_call(
        functools.partial(gradient_kernel, (tiles, epochs)),
        out_shape=(
            jax.ShapeDtypeStruct((total, look_rows, LANES), f32),
            jax.ShapeDtypeStruct((8, LANES), f32),
        ),
        in_specs=[SMEM] + [VMEM] * (tiles + 2),
        out_specs=(VMEM, VMEM),
        scratch_shapes=[pltpu.VMEM((total, look_rows, LANES), f32)] * 2
        + [pltpu.VMEM((total * SLOTS, look_rows, LANES), f32)],
        compiler_params=params_of,
        cost_estimate=pl.CostEstimate(flops=10_000_000, bytes_accessed=8_000_000, transcendentals=0),
    )(partner, *field, factors, pulls)

    place = ("space", "sub")
    count = spaces * lax.axis_size("sub")
    shared = [sums] + [lax.ppermute(sums, place, [(i, (i + by) % count) for i in range(count)]) for by in range(1, count)]
    coded_shape = jax.ShapeDtypeStruct((epochs * look_rows + HALO, LANES), jnp.int16)
    coded = pl.pallas_call(
        code_kernel,
        out_shape=(coded_shape,) * (tiles - 1),
        in_specs=[VMEM],
        out_specs=(VMEM,) * (tiles - 1),
        compiler_params=params_of,
        cost_estimate=pl.CostEstimate(flops=1_000_000, bytes_accessed=1_000_000, transcendentals=0),
    )(gradient)
    piece_shape = jax.ShapeDtypeStruct((epochs * look_rows + HALO + 32, LANES), jnp.int16)
    own_sums, *pieces = pl.pallas_call(
        functools.partial(return_kernel, tiles),
        out_shape=(jax.ShapeDtypeStruct((8, LANES), f32),) + (piece_shape,) * (tiles - 1),
        in_specs=[VMEM] * (tiles - 1 + count),
        out_specs=(VMEM,) * tiles,
        compiler_params=params_of,
        cost_estimate=pl.CostEstimate(flops=10_000, bytes_accessed=1_000_000, transcendentals=0),
    )(*coded, *shared)
    returned = [exchanged(piece, "epoch", by + 1) for by, piece in enumerate(pieces)]
    cell_count = float(total * look_rows * spaces * columns * lax.axis_size("sub"))
    return pl.pallas_call(
        functools.partial(update_kernel, cell_count),
        out_shape=(jax.ShapeDtypeStruct(estimate.shape, f32),) * 2,
        in_specs=[SMEM] * 2 + [VMEM] * (3 + tiles),
        out_specs=(VMEM, VMEM),
        compiler_params=params_of,
        cost_estimate=pl.CostEstimate(flops=1_000_000, bytes_accessed=2_000_000, transcendentals=0),
    )(me.reshape(1), prev_mean, estimate, direction, gradient[:epochs], own_sums, *returned)


def on_device(slc, offsets, weights, estimate, direction, prev_mean):
    epochs, rows, columns = slc.shape[1:]
    fits = columns == LANES * lax.axis_size("epoch") and lax.axis_size("epoch") > 1
    size = lax.axis_size("epoch")
    fits = fits and size & (size - 1) == 0 and 2 * epochs * SIDES <= PARAM_LANE and rows % HALO == 0 and epochs == 2 * SLOTS
    plan = transposed_plan if fits else ring_plan
    return plan(slc, offsets, weights, estimate, direction, prev_mean)


def solution(mesh):
    return jax.shard_map(
        on_device,
        mesh=mesh,
        in_specs=(
            P(None, ("groups", "epoch"), "space", "sub"),
            P(("groups", "epoch"), None),
            P(("groups", "epoch"), None),
            P(("groups", "epoch"), "space", "sub"),
            P(("groups", "epoch"), "space", "sub"),
            P(),
        ),
        out_specs=(P(("groups", "epoch"), "space", "sub"), P(("groups", "epoch"), "space", "sub")),
        check_vma=False,
    )
```

```python
import functools
import math

import jax
import jax.numpy as jnp
import numpy as np
from jax import lax
from jax.experimental import pallas as pl
from jax.experimental.pallas import tpu as pltpu
from jax.sharding import PartitionSpec as P

SLOTS = 4
OFFS = 8
LOOK = 4
RADIUS = 3


EPSILON = 1e-06


def passed_along(x, axis, by):
    size = lax.axis_size(axis)
    return lax.ppermute(x, axis, [(i, (i + by) % size) for i in range(size)])


def extended_2(block, sides, width):
    for axis, dim in sides:
        count = lax.axis_size(axis)
        forward = [(i, i + 1) for i in range(count - 1)]
        backward = [(target, source) for source, target in forward]
        low = lax.ppermute(
            lax.slice_in_dim(block, block.shape[dim] - width, None, axis=dim), axis, forward
        )
        high = lax.ppermute(lax.slice_in_dim(block, 0, width, axis=dim), axis, backward)
        block = jnp.concatenate([low, block, high], axis=dim)
    return block


def looked_sum(field):
    shape = field.shape
    return jnp.sum(field.reshape(shape[:-2] + (shape[-2] // LOOK, LOOK, shape[-1])), axis=-2)


def window_sum(padded, axis):
    length = padded.shape[axis] - 2 * RADIUS
    total = lax.slice_in_dim(padded, 0, length, axis=axis)
    for shift_at in range(1, 2 * RADIUS + 1):
        total = total + lax.slice_in_dim(padded, shift_at, shift_at + length, axis=axis)
    return total


def ring_plan(slc, offsets, weights, estimate, direction, prev_mean):
    epochs_here = slc.shape[1]
    look_rows = slc.shape[2] // LOOK
    col_count = slc.shape[3]
    ahead = passed_along(slc, "epoch", -1)
    extended = jnp.concatenate([slc, ahead], axis=1)
    numbers = jnp.arange(epochs_here, dtype=jnp.int32)
    partner = numbers[:, None] + offsets
    own_real = slc[0].astype(jnp.float32)
    own_imag = slc[1].astype(jnp.float32)
    ext_real = extended[0].astype(jnp.float32)
    ext_imag = extended[1].astype(jnp.float32)
    powers = looked_sum(ext_real * ext_real + ext_imag * ext_imag)
    pieces = []
    for slot_index in range(SLOTS):
        mate_real = jnp.take(ext_real, partner[:, slot_index], axis=0)
        mate_imag = jnp.take(ext_imag, partner[:, slot_index], axis=0)
        pieces.append(looked_sum(own_real * mate_real + own_imag * mate_imag))
        pieces.append(looked_sum(own_imag * mate_real - own_real * mate_imag))
    pair_count = epochs_here * 2 * SLOTS
    stacked = jnp.concatenate(
        [jnp.stack(pieces, axis=1).reshape(pair_count, look_rows, col_count), powers], axis=0
    )
    padded = extended_2(stacked, (("space", 1), ("sub", 2)), RADIUS)
    boxed = window_sum(window_sum(padded, 1), 2)
    pair_boxed = boxed[:pair_count].reshape(epochs_here, 2 * SLOTS, look_rows, col_count)
    power_box = boxed[pair_count:]
    coh_real = pair_boxed[:, 0::2]
    coh_imag = pair_boxed[:, 1::2]
    denominator = power_box[:epochs_here, None] * jnp.take(power_box, partner, axis=0) + EPSILON
    coherence = (coh_real * coh_real + coh_imag * coh_imag) / denominator
    observed = coh_imag / jnp.sqrt(denominator)
    est_ahead = passed_along(estimate, "epoch", -1)
    est_extended = jnp.concatenate([estimate, est_ahead], axis=0)
    fitted = estimate[:, None] - jnp.take(est_extended, partner, axis=0)
    factor = weights[:, :, None, None] * coherence
    weighted = factor * (observed - fitted)
    flattened = weighted.reshape(epochs_here * SLOTS, look_rows * col_count)
    selector = (
        jnp.arange(epochs_here + OFFS, dtype=jnp.int32)[:, None] == partner.reshape(1, -1)
    ).astype(jnp.float32)
    gathered = jnp.dot(
        selector, flattened, precision=lax.Precision.HIGHEST, preferred_element_type=jnp.float32
    ).reshape(epochs_here + OFFS, look_rows, col_count)
    own_part = jnp.sum(weighted, axis=1) - gathered[:epochs_here]
    returned = passed_along(-gathered[epochs_here:], "epoch", 1)
    gradient = jnp.concatenate([own_part + returned, own_part[OFFS:]], axis=0)
    cell_count = float(
        epochs_here
        * lax.axis_size("epoch")
        * look_rows
        * lax.axis_size("space")
        * col_count
        * lax.axis_size("sub")
    )
    local_norm = jnp.sum(gradient * gradient)
    local_crossed = jnp.sum(gradient * direction)
    mean_before = prev_mean[0]
    fields_ahead = passed_along(
        jnp.stack([gradient, direction]).astype(jnp.bfloat16), "epoch", -1
    ).astype(jnp.float32)
    grad_extended = jnp.concatenate([gradient, fields_ahead[0]], axis=0)
    old_extended = jnp.concatenate([direction, fields_ahead[1]], axis=0)
    grad_spread = gradient[:, None] - jnp.take(grad_extended, partner, axis=0)
    old_spread = direction[:, None] - jnp.take(old_extended, partner, axis=0)
    totals = lax.psum(
        (
            local_norm,
            local_crossed,
            jnp.sum(factor * grad_spread * grad_spread),
            jnp.sum(factor * grad_spread * old_spread),
            jnp.sum(factor * old_spread * old_spread),
        ),
        ("epoch", "space", "sub"),
    )
    grad_norm, crossed, grad_term, mixed_term, old_term = totals
    momentum = grad_norm / cell_count / mean_before
    new_direction = gradient + momentum * direction
    curvature = grad_term + 2.0 * momentum * mixed_term + momentum * momentum * old_term
    along_sum = grad_norm + momentum * crossed
    step_size = along_sum / curvature
    return (estimate + step_size * new_direction, new_direction)


LANES = 128
SIDES = 2 * RADIUS
HALO = 16
FIELD_STEPS = 16383.0
GRADIENT_STEPS = 32000.0
PARAM_LANE = 96
VMEM = pl.BlockSpec(memory_space=pltpu.VMEM)
SMEM = pl.BlockSpec(memory_space=pltpu.SMEM)
VMEM_BYTES = 48 * 1024 * 1024


def split_two(value):
    high = value.astype(jnp.bfloat16)
    low = (value - high.astype(jnp.float32)).astype(jnp.bfloat16)
    return high, low


def edge_kernel(first, last, edge):
    epochs = first.shape[1]
    lane = lax.broadcasted_iota(jnp.int32, edge.shape, 1)
    total = jnp.zeros(edge.shape, jnp.float32)
    for part in range(2):
        for epoch in range(epochs):
            at = (part * epochs + epoch) * SIDES
            total = placed(lane, total, tile_of(last, part, epoch, 0), LANES - RADIUS, at)
            total = placed(lane, total, tile_of(first, part, epoch, 0), 0, at + RADIUS)
    edge[...] = total.astype(jnp.bfloat16)


def fixed_point(value):
    return jnp.floor(value * FIELD_STEPS + 0.5).astype(jnp.int32).astype(jnp.int16)


def from_fixed_point(value):
    return value.astype(jnp.int32).astype(jnp.float32) * (1.0 / FIELD_STEPS)


def fields_kernel(me, estimate, direction, *fields):
    look_rows = estimate.shape[1]
    tiles = len(fields)
    for shift, out in enumerate(fields):
        tile = lax.bitwise_xor(me[0], shift)
        columns = pl.ds(pl.multiple_of(tile * LANES, LANES), LANES)
        for epoch in range(estimate.shape[0]):
            here = slice(epoch * look_rows, (epoch + 1) * look_rows)
            out[0, here, :] = fixed_point(estimate[epoch, :, columns])
            out[1, here, :] = fixed_point(direction[epoch, :, columns])


def tile_of(slc, part, epoch, tile):
    return slc[part, epoch, :, tile * LANES : (tile + 1) * LANES].astype(jnp.float32)


def placed(lane, total, source, start, target):
    moved = pltpu.roll(source, (target - start) % LANES, axis=1)
    return jnp.where((lane >= target) & (lane < target + RADIUS), moved, total)


def pack_kernel(me, present, slc, params, before, after, *refs):
    messages, strips = refs[:-1], refs[-1]
    tiles = len(messages)
    epochs = slc.shape[1]
    rows = slc.shape[2]
    lane = lax.broadcasted_iota(jnp.int32, (rows, LANES), 1)
    value = params[...]
    high = value.astype(jnp.bfloat16).astype(jnp.float32)
    middle = (value - high).astype(jnp.bfloat16).astype(jnp.float32)
    low = value - high - middle
    third = PARAM_LANE + 2 * SLOTS
    split = jnp.where(lane < third, high, jnp.where(lane < third + SLOTS, middle, low))
    split = jnp.where(lane >= PARAM_LANE, split, 0.0)
    inside = lane < 2 * epochs * SIDES
    for tile in range(tiles):
        total = split
        if tile == 0:
            edge = before[...].astype(jnp.float32) * present[0]
            total = jnp.where(inside & (lane % SIDES < RADIUS), edge, total)
        if tile == tiles - 1:
            edge = after[...].astype(jnp.float32) * present[1]
            total = jnp.where(inside & (lane % SIDES >= RADIUS), edge, total)
        for part in range(2):
            for epoch in range(epochs):
                at = (part * epochs + epoch) * SIDES
                if tile > 0:
                    total = placed(lane, total, tile_of(slc, part, epoch, tile - 1), LANES - RADIUS, at)
                if tile < tiles - 1:
                    total = placed(lane, total, tile_of(slc, part, epoch, tile + 1), 0, at + RADIUS)
        strips[tile] = total.astype(jnp.bfloat16)
    for tile in range(tiles):
        shift = lax.bitwise_xor(me[0], tile)
        for number, message in enumerate(messages):

            @pl.when(shift == number)
            def _():
                for part in range(2):
                    for epoch in range(epochs):
                        at = (part * epochs + epoch) * rows
                        message[at : at + rows, :] = slc[part, epoch, :, tile * LANES : (tile + 1) * LANES]
                message[2 * epochs * rows :, :] = strips[tile]


def look_order(from_rows, first):
    looks = from_rows // LOOK
    to = np.arange(from_rows)[:, None]
    at = np.arange(from_rows)[None, :]
    return jnp.asarray(at == (to + first) % looks * LOOK + to // looks, jnp.bfloat16)


def unpack_tiles(order, sources, main, first, columns_of):
    looks = order.shape[0] // LOOK
    for start in range(0, len(sources), 4):
        parts = jnp.concatenate([columns_of(source) for source in sources[start : start + 4]], axis=1)
        value = jnp.dot(order, parts, preferred_element_type=jnp.float32)
        for one in range(4):
            for look in range(LOOK):
                main[first[start + one], look] = value[look * looks : (look + 1) * looks, one * LANES : (one + 1) * LANES]


def unpack_rims(by_look, looks, rim, first):
    share = LANES // SLOTS
    lane = lax.broadcasted_iota(jnp.int32, (looks, LANES), 1)
    for at, place in enumerate(first):
        value = jnp.zeros((looks, LANES), jnp.float32)
        for look in range(LOOK):
            target = look * SIDES
            moved = pltpu.roll(by_look[look * looks : (look + 1) * looks], (target - at * SIDES) % LANES, axis=1)
            value = jnp.where((lane >= target) & (lane < target + SIDES), moved, value)
        spread = share
        while spread < LANES:
            value = value + pltpu.roll(value, spread, axis=1)
            spread = 2 * spread
        rim[place] = value


def column_bands():
    share = LANES // SLOTS
    at = np.arange(2 * LANES)[:, None] % LANES
    to = np.arange(LANES)[None, :]
    side = at % share % SIDES
    source = np.where(side < RADIUS, side - RADIUS, LANES + side - RADIUS)
    column = (to - at // share * share) % LANES
    inside = (column < RADIUS) | (column >= LANES - RADIUS)
    inside = inside & (at % share < LOOK * SIDES)
    band = np.abs(at - to) <= RADIUS
    rim_band = inside & (np.abs(source - column) <= RADIUS)
    return jnp.asarray(band, jnp.bfloat16), jnp.asarray(rim_band, jnp.bfloat16)


def mixed(values):
    lane = lax.broadcasted_iota(jnp.int32, values[0].shape, 1)
    result = values[-1]
    for slot in range(SLOTS - 1):
        result = jnp.where(lane < (SLOTS - 1 - slot) * (LANES // SLOTS), values[SLOTS - 2 - slot], result)
    return result


def power_batches(blocks, epochs, looks, main, rim, looked, rim_looked):
    total = blocks * epochs
    group = 2 * SLOTS
    for block in range(blocks):
        for piece in range(0, looks, 8):
            rows_at = slice(piece, piece + 8)
            for half in range(2):
                squares = []
                for slot in range(SLOTS):
                    channel = half * SLOTS + slot
                    epoch = block * epochs + channel
                    value = None
                    for look in range(LOOK):
                        real = main[epoch, look, rows_at]
                        imag = main[total + epoch, look, rows_at]
                        one = real * real + imag * imag
                        value = one if value is None else value + one
                    at = (block * group + channel) * looks + piece
                    looked[at : at + 8, :] = value
                    real = rim[epoch, rows_at]
                    imag = rim[total + epoch, rows_at]
                    squares.append(real * real + imag * imag)
                at = (block * 2 + half) * looks + piece
                rim_looked[at : at + 8, :] = mixed(squares)


def pair_batch(epoch, mates, total, main, rim):
    own_re, own_im = main[epoch], main[total + epoch]
    reals, imags = [], []
    for mate in mates:
        mate_re, mate_im = main[mate], main[total + mate]
        real = own_re[0] * mate_re[0] + own_im[0] * mate_im[0]
        imag = own_im[0] * mate_re[0] - own_re[0] * mate_im[0]
        for look in range(1, LOOK):
            real = real + (own_re[look] * mate_re[look] + own_im[look] * mate_im[look])
            imag = imag + (own_im[look] * mate_re[look] - own_re[look] * mate_im[look])
        reals.append(real)
        imags.append(imag)
    own_re, own_im = rim[epoch], rim[total + epoch]
    mate_re = mixed([rim[mate] for mate in mates])
    mate_im = mixed([rim[total + mate] for mate in mates])
    rims = [own_re * mate_re + own_im * mate_im, own_im * mate_re - own_re * mate_im]
    return reals + imags, rims


def put(ref, block, values):
    rows = sum(value.shape[0] for value in values)
    ref[block * rows : (block + 1) * rows, :] = jnp.concatenate(values, axis=0)


def columns_summed(couple, looks, bands, looked, rim_looked):
    group = 2 * SLOTS
    f32 = jnp.float32
    at = slice(couple * 2 * group * looks, (couple + 1) * 2 * group * looks)
    halves = jnp.concatenate(split_two(looked[at, :]), axis=1)
    value = jnp.dot(halves, bands[0], preferred_element_type=f32)
    at = slice(couple * 4 * looks, (couple + 1) * 4 * looks)
    halves = jnp.concatenate(split_two(rim_looked[at, :]), axis=1)
    outer = jnp.dot(halves, bands[1], preferred_element_type=f32)
    lane = lax.broadcasted_iota(jnp.int32, (looks, LANES), 1)
    outside = (lane < RADIUS) | (lane >= LANES - RADIUS)
    results = []
    for channel in range(2 * group):
        batch, half, slot = channel // group, channel % group // SLOTS, channel % SLOTS
        row = (batch * 2 + half) * looks
        part = outer[row : row + looks]
        if slot > 0:
            part = pltpu.roll(part, LANES - slot * (LANES // SLOTS), axis=1)
        row = channel * looks
        results.append(value[row : row + looks] + jnp.where(outside, part, 0.0))
    return results


def rows_summed(channel, looks, look_rows, wide):
    first = channel * looks
    total = wide[pl.ds(first, look_rows), :]
    for shift in range(1, 2 * RADIUS + 1):
        total = total + wide[pl.ds(first + shift, look_rows), :]
    return total


def pair_couple(couple, total, partner, main, rim):
    products, rims = [], []
    for one in range(2):
        epoch = couple * 2 + one
        mates = [partner[epoch * SLOTS + slot] for slot in range(SLOTS)]
        more, more_rims = pair_batch(epoch, mates, total, main, rim)
        products += more
        rims += more_rims
    return products, rims


def clipped(value, last):
    return jnp.minimum(jnp.maximum(value, 0), last)


def pair_kernel(sizes, places, partner, weight, present, order, band, rim_band, *refs):
    epochs, rows, operands = sizes
    inputs = refs[:operands]
    factors, pulls, boxed, main, rim, looked, rim_looked, wide = refs[operands:]
    count = len(places)
    total = count * epochs
    look_rows = rows // LOOK
    halo_looks = HALO // LOOK
    looks = look_rows + 2 * halo_looks
    full_rows = rows + 2 * HALO
    group = 2 * SLOTS

    at = lax.broadcasted_iota(jnp.int32, (full_rows, full_rows), 1)
    keep = jnp.where(at < HALO, present[0], jnp.where(at >= HALO + rows, present[1], 1.0))
    order = (order[...].astype(jnp.float32) * keep).astype(jnp.bfloat16)
    bands = band[...], rim_band[...]
    for block, (tile_at, top_at, bottom_at, top_row, bottom_row) in enumerate(places):
        tile, top, bottom = inputs[tile_at], inputs[top_at], inputs[bottom_at]

        def rows_of(at):
            above = top[top_row + at * HALO : top_row + (at + 1) * HALO, :]
            below = bottom[bottom_row + at * HALO : bottom_row + (at + 1) * HALO, :]
            return jnp.concatenate([above, tile[at * rows : (at + 1) * rows, :], below], axis=0)

        first = [part * total + block * epochs + epoch for part in range(2) for epoch in range(epochs)]
        unpack_tiles(order, range(2 * epochs), main, first, rows_of)
        by_look = jnp.dot(order, rows_of(2 * epochs), preferred_element_type=jnp.float32)
        unpack_rims(by_look, looks, rim, first)
    power_batches(count, epochs, looks, main, rim, looked, rim_looked)
    powers = count // 2
    couples = total // 2

    def boxed_of(channel):
        return boxed[pl.ds(pl.multiple_of(channel * look_rows, look_rows), look_rows), :]

    def finished(couple):
        results = []
        for one in range(2):
            epoch = couple * 2 + one
            own_power = boxed_of(epoch)
            first = (2 * powers + epoch) * (group * look_rows)
            parts = boxed[first : first + group * look_rows, :]
            parts = parts.reshape(group, look_rows, LANES)
            for slot in range(SLOTS):
                pair = epoch * SLOTS + slot
                inverse = lax.rsqrt(own_power * boxed_of(partner[pair]) + EPSILON)
                unit_re = parts[slot] * inverse
                unit_im = parts[SLOTS + slot] * inverse
                factor = weight[pair] * (unit_re * unit_re + unit_im * unit_im)
                results.append((factor, factor * unit_im))
        return results

    def boxes(couple):
        return [rows_summed(couple * 2 * group + one, looks, look_rows, wide) for one in range(2 * group)]

    def turn(number, steps):
        if 3 in steps:
            results = finished(number - 3)
        if 2 in steps:
            sums = boxes(powers + number - 2)
        if 1 in steps:
            columns = columns_summed(powers + number - 1, looks, bands, looked, rim_looked)
        if 0 in steps:
            products, rims = pair_couple(number, total, partner, main, rim)
        if 3 in steps:
            for ref, values in zip((factors, pulls), zip(*results)):
                ref[pl.ds((number - 3) * 2 * SLOTS, 2 * SLOTS)] = jnp.stack(values)
        if 2 in steps:
            put(boxed, powers + number - 2, sums)
        if 1 in steps:
            put(wide, powers + number - 1, columns)
        if 0 in steps:
            put(looked, powers + number, products)
            put(rim_looked, powers + number, rims)

    for couple in range(powers):
        put(wide, couple, columns_summed(couple, looks, bands, looked, rim_looked))
    turn(0, (0,))
    for couple in range(powers):
        put(boxed, couple, boxes(couple))
    turn(1, (0, 1))
    turn(2, (0, 1, 2))
    for number in range(3, couples):
        turn(number, (0, 1, 2, 3))
    turn(couples, (1, 2, 3))
    turn(couples + 1, (2, 3))
    turn(couples + 2, (3,))


def gradient_kernel(sizes, partner, *refs):
    tiles, epochs = sizes
    fields = refs[:tiles]
    factors, pulls, gradient, sums, est, old, shares = refs[tiles:]
    look_rows = est.shape[1]
    total = tiles * epochs
    f32 = jnp.float32
    for block in range(tiles):
        for epoch in range(epochs):
            here = slice(epoch * look_rows, (epoch + 1) * look_rows)
            est[block * epochs + epoch] = from_fixed_point(fields[block][0, here, :])
            old[block * epochs + epoch] = from_fixed_point(fields[block][1, here, :])
    mates = [[partner[epoch * SLOTS + slot] for slot in range(SLOTS)] for epoch in range(total)]
    for epoch in range(total):
        own_est = est[epoch]
        own = None
        for slot, mate in enumerate(mates[epoch]):
            pair = epoch * SLOTS + slot
            weighted = pulls[pair] - factors[pair] * (own_est - est[mate])
            own = weighted if own is None else own + weighted
            shares[pair] = weighted
        gradient[epoch] = own
    for epoch in range(total):
        values = [gradient[mate] - shares[epoch * SLOTS + slot] for slot, mate in enumerate(mates[epoch])]
        for mate, value in zip(mates[epoch], values):
            gradient[mate] = value

    zero = jnp.zeros((look_rows, LANES), f32)
    norm, crossed, grad_term, mixed_term, old_term = (zero,) * 5
    for epoch in range(total):
        own_grad = gradient[epoch]
        own_old = old[epoch]
        norm = norm + own_grad * own_grad
        crossed = crossed + own_grad * own_old
        for slot, mate in enumerate(mates[epoch]):
            factor = factors[epoch * SLOTS + slot]
            grad_spread = own_grad - gradient[mate]
            old_spread = own_old - old[mate]
            pulled = factor * grad_spread
            grad_term = grad_term + pulled * grad_spread
            mixed_term = mixed_term + pulled * old_spread
            old_term = old_term + factor * old_spread * old_spread
    sums[...] = jnp.zeros(sums.shape, f32)
    for at, value in enumerate((norm, crossed, grad_term, mixed_term, old_term)):
        sums[at : at + 1, :] = jnp.sum(value, axis=0, keepdims=True)


def exponent_of(size):
    power = jnp.ceil(jnp.log(jnp.maximum(size, 1e-30)) * (1.0 / math.log(2.0)))
    return jnp.clip(power, -110.0, 110.0)


def whole(value):
    return jnp.floor(value + 0.5).astype(jnp.int32).astype(jnp.int16)


def number_of(value):
    return value.astype(jnp.int32).astype(jnp.float32)


def code_kernel(gradient, *coded):
    epochs = gradient.shape[0] // (len(coded) + 1)
    look_rows = gradient.shape[1]
    for number, out in enumerate(coded):
        powers = []
        for epoch in range(epochs):
            value = gradient[(number + 1) * epochs + epoch]
            power = exponent_of(jnp.max(jnp.abs(value), axis=0, keepdims=True))
            out[epoch * look_rows : (epoch + 1) * look_rows, :] = whole(value * (jnp.exp2(-power) * GRADIENT_STEPS))
            powers.append(power)
        powers.append(jnp.zeros((HALO - epochs, LANES), jnp.float32))
        out[epochs * look_rows :, :] = whole(jnp.concatenate(powers, axis=0))


def return_kernel(tiles, *refs):
    coded, shared = refs[: tiles - 1], refs[tiles - 1 : -tiles]
    own, pieces = refs[-tiles], refs[1 - tiles :]
    total = shared[0][...]
    for other in shared[1:]:
        total = total + other[...]
    own[...] = total
    power = exponent_of(jnp.abs(total))
    share = total * jnp.exp2(-power) * float(1 << 14)
    high = jnp.floor(share + 0.5)
    low = (share - high) * float(1 << 15)
    parts = whole(jnp.concatenate([power, high, low, jnp.zeros_like(power)], axis=0))
    for piece, source in zip(pieces, coded):
        piece[: source.shape[0], :] = source[...]
        piece[source.shape[0] :, :] = parts


def update_kernel(cell_count, me, prev_mean, estimate, direction, gradient, sums, *refs):
    pieces = refs[:-2]
    new_estimate, new_direction = refs[-2:]
    tiles = len(pieces) + 1
    epochs = estimate.shape[0]
    look_rows = estimate.shape[1]
    coded_rows = epochs * look_rows + HALO
    total = sums[...]
    for piece in pieces:
        parts = number_of(piece[coded_rows:, :])
        value = (parts[8:16] + parts[16:24] * (1.0 / (1 << 15))) * (1.0 / (1 << 14))
        total = total + value * jnp.exp2(parts[:8])
    total = jnp.sum(total, axis=1, keepdims=True)
    grad_norm, crossed, grad_term, mixed, old_term = (total[at : at + 1, :] for at in range(5))
    momentum = grad_norm / cell_count / prev_mean[0]
    curvature = grad_term + 2.0 * momentum * mixed + momentum * momentum * old_term
    step = (grad_norm + momentum * crossed) / curvature
    momentum = jnp.broadcast_to(momentum, (look_rows, LANES))
    step = jnp.broadcast_to(step, (look_rows, LANES))
    for shift in range(tiles):
        tile = lax.bitwise_xor(me[0], shift)
        columns = pl.ds(pl.multiple_of(tile * LANES, LANES), LANES)
        if shift > 0:
            piece = pieces[shift - 1]
            scale = jnp.exp2(number_of(piece[epochs * look_rows : coded_rows, :])) * (1.0 / GRADIENT_STEPS)
        for epoch in range(epochs):
            if shift == 0:
                value = gradient[epoch]
            else:
                value = number_of(piece[epoch * look_rows : (epoch + 1) * look_rows, :]) * scale[epoch : epoch + 1, :]
            moved = value + momentum * direction[epoch, :, columns]
            new_direction[epoch, :, columns] = moved
            new_estimate[epoch, :, columns] = estimate[epoch, :, columns] + step * moved


def swapped(up, down, axis):
    size = lax.axis_size(axis)
    if size == 1:
        return jnp.zeros_like(up), jnp.zeros_like(down)
    if size == 2:
        first = lax.axis_index(axis) == 0
        got = lax.ppermute(jnp.where(first, up, down), axis, [(0, 1), (1, 0)])
        return got, got
    forward = [(i, i + 1) for i in range(size - 1)]
    backward = [(target, source) for source, target in forward]
    return lax.ppermute(up, axis, forward), lax.ppermute(down, axis, backward)


def exchanged(x, axis, by):
    size = lax.axis_size(axis)
    return lax.ppermute(x, axis, [(i, i ^ by) for i in range(size)])


def transposed_plan(slc, offsets, weights, estimate, direction, prev_mean):
    f32 = jnp.float32
    bf16 = jnp.bfloat16
    tiles = lax.axis_size("epoch")
    me = lax.axis_index("epoch")
    epochs, rows, columns = slc.shape[1:]
    look_rows = rows // LOOK
    total = tiles * epochs
    tile_rows = 2 * epochs * rows
    params_of = pltpu.CompilerParams(vmem_limit_bytes=VMEM_BYTES)

    sub = lax.axis_index("sub")
    outer_tile = (2, epochs, rows, LANES)
    edge = pl.pallas_call(
        edge_kernel,
        out_shape=jax.ShapeDtypeStruct((rows, LANES), bf16),
        grid=(1,),
        in_specs=[
            pl.BlockSpec(outer_tile, lambda _: (0, 0, 0, 0)),
            pl.BlockSpec(outer_tile, lambda _: (0, 0, 0, tiles - 1)),
        ],
        out_specs=pl.BlockSpec((rows, LANES), lambda _: (0, 0)),
        compiler_params=params_of,
        cost_estimate=pl.CostEstimate(flops=1_000_000, bytes_accessed=1_000_000, transcendentals=0),
    )(slc, slc)
    before, after = swapped(edge, edge, "sub")
    params = jnp.zeros((rows, LANES), f32)
    listed = jnp.concatenate([offsets.astype(f32), weights, weights, weights], axis=1)
    params = lax.dynamic_update_slice(params, listed, (0, PARAM_LANE))
    sub_present = jnp.stack([sub > 0, sub < lax.axis_size("sub") - 1]).astype(f32)
    messages = pl.pallas_call(
        pack_kernel,
        out_shape=(jax.ShapeDtypeStruct((tile_rows + rows, LANES), bf16),) * tiles,
        in_specs=[SMEM] * 2 + [VMEM] * 4,
        out_specs=(VMEM,) * tiles,
        scratch_shapes=[pltpu.VMEM((tiles, rows, LANES), bf16)],
        compiler_params=params_of,
        cost_estimate=pl.CostEstimate(flops=3_000_000, bytes_accessed=4_000_000, transcendentals=0),
    )(me.reshape(1), sub_present, slc, params, before, after)
    space = lax.axis_index("space")
    spaces = lax.axis_size("space")
    present = jnp.stack([space > 0, space < spaces - 1]).astype(f32)

    def halo(pieces):
        def border(from_row):
            cuts = [lax.dynamic_slice_in_dim(piece, from_row, HALO, axis=1).reshape(-1, LANES) for piece in pieces]
            return jnp.concatenate(cuts, axis=0)

        if spaces == 2:
            got = lax.ppermute(border(jnp.where(space == 0, rows - HALO, 0)), "space", [(0, 1), (1, 0)])
            return got, got
        return swapped(border(rows - HALO), border(0), "space")

    turns = list(range(2, tiles)) + [1]
    halos = {0: halo([messages[0].reshape(-1, rows, LANES)])}
    near = lax.optimization_barrier((messages[1], halos[0]))[0]
    block = {by: exchanged(near if by == 1 else messages[by], "epoch", by) for by in turns}
    block[0] = messages[0]
    estimate, direction, _ = lax.optimization_barrier((estimate, direction, messages))
    fields = pl.pallas_call(
        fields_kernel,
        out_shape=(jax.ShapeDtypeStruct((2, epochs * look_rows, LANES), jnp.int16),) * tiles,
        in_specs=[SMEM] + [VMEM] * 2,
        out_specs=(VMEM,) * tiles,
        compiler_params=params_of,
        cost_estimate=pl.CostEstimate(flops=1_000_000, bytes_accessed=2_000_000, transcendentals=0),
    )(me.reshape(1), estimate, direction)
    def params_in(shift):
        return block[shift][tile_rows : tile_rows + epochs, PARAM_LANE : PARAM_LANE + 4 * SLOTS].astype(f32)

    halos.update({by: halo([block[by].reshape(-1, rows, LANES)]) for by in turns})
    late = lax.optimization_barrier((fields, block, [halos[by] for by in turns[:-2]]))[0]
    field = {by: exchanged(late[by], "epoch", by) for by in range(1, tiles)}
    field[0] = fields[0]
    block, field = ([array[by] for by in range(tiles)] for array in (block, field))

    listed = jnp.concatenate([params_in(shift) for shift in range(tiles)], axis=0)
    place = jnp.arange(total, dtype=jnp.int32)[:, None]
    first = lax.bitwise_xor(place // epochs, me) * epochs + place % epochs
    mate = lax.rem(first + listed[:, :SLOTS].astype(jnp.int32), total)
    partner = (lax.bitwise_xor(mate // epochs, me) * epochs + mate % epochs).reshape(-1)
    weight = listed[:, SLOTS : 2 * SLOTS] + listed[:, 2 * SLOTS : 3 * SLOTS] + listed[:, 3 * SLOTS :]
    order = look_order(rows + 2 * HALO, HALO // LOOK - RADIUS)
    bands = column_bands()
    operands = list(block)
    places = []
    for shift in range(tiles):
        top, bottom = halos[shift]
        operands.append(top)
        top_at = bottom_at = len(operands) - 1
        if bottom is not top:
            operands.append(bottom)
            bottom_at = len(operands) - 1
        places.append((shift, top_at, bottom_at, 0, 0))
    looks = (rows + 2 * HALO) // LOOK
    group = 2 * SLOTS
    batches = tiles + total
    shape = jax.ShapeDtypeStruct((total * SLOTS, look_rows, LANES), f32)
    factors, pulls = pl.pallas_call(
        functools.partial(pair_kernel, (epochs, rows, len(operands)), tuple(places)),
        out_shape=(shape, shape),
        in_specs=[SMEM] * 3 + [VMEM] * (3 + len(operands)),
        out_specs=(VMEM, VMEM),
        scratch_shapes=[
            pltpu.VMEM((batches * group * look_rows, LANES), f32),
            pltpu.VMEM((2 * total, LOOK, looks, LANES), f32),
            pltpu.VMEM((2 * total, looks, LANES), f32),
            pltpu.VMEM((batches * group * looks, LANES), f32),
            pltpu.VMEM((batches * 2 * looks, LANES), f32),
            pltpu.VMEM((batches * group * looks, LANES), f32),
        ],
        compiler_params=params_of,
        cost_estimate=pl.CostEstimate(flops=20_000_000, bytes_accessed=30_000_000, transcendentals=0),
    )(partner, weight.reshape(-1), present, order, *bands, *operands)
    gradient, sums = pl.pallas_call(
        functools.partial(gradient_kernel, (tiles, epochs)),
        out_shape=(
            jax.ShapeDtypeStruct((total, look_rows, LANES), f32),
            jax.ShapeDtypeStruct((8, LANES), f32),
        ),
        in_specs=[SMEM] + [VMEM] * (tiles + 2),
        out_specs=(VMEM, VMEM),
        scratch_shapes=[pltpu.VMEM((total, look_rows, LANES), f32)] * 2
        + [pltpu.VMEM((total * SLOTS, look_rows, LANES), f32)],
        compiler_params=params_of,
        cost_estimate=pl.CostEstimate(flops=10_000_000, bytes_accessed=8_000_000, transcendentals=0),
    )(partner, *field, factors, pulls)

    place = ("space", "sub")
    count = spaces * lax.axis_size("sub")
    shared = [sums] + [lax.ppermute(sums, place, [(i, (i + by) % count) for i in range(count)]) for by in range(1, count)]
    coded_shape = jax.ShapeDtypeStruct((epochs * look_rows + HALO, LANES), jnp.int16)
    coded = pl.pallas_call(
        code_kernel,
        out_shape=(coded_shape,) * (tiles - 1),
        in_specs=[VMEM],
        out_specs=(VMEM,) * (tiles - 1),
        compiler_params=params_of,
        cost_estimate=pl.CostEstimate(flops=1_000_000, bytes_accessed=1_000_000, transcendentals=0),
    )(gradient)
    piece_shape = jax.ShapeDtypeStruct((epochs * look_rows + HALO + 32, LANES), jnp.int16)
    own_sums, *pieces = pl.pallas_call(
        functools.partial(return_kernel, tiles),
        out_shape=(jax.ShapeDtypeStruct((8, LANES), f32),) + (piece_shape,) * (tiles - 1),
        in_specs=[VMEM] * (tiles - 1 + count),
        out_specs=(VMEM,) * tiles,
        compiler_params=params_of,
        cost_estimate=pl.CostEstimate(flops=10_000, bytes_accessed=1_000_000, transcendentals=0),
    )(*coded, *shared)
    returned = [exchanged(piece, "epoch", by + 1) for by, piece in enumerate(pieces)]
    cell_count = float(total * look_rows * spaces * columns * lax.axis_size("sub"))
    return pl.pallas_call(
        functools.partial(update_kernel, cell_count),
        out_shape=(jax.ShapeDtypeStruct(estimate.shape, f32),) * 2,
        in_specs=[SMEM] * 2 + [VMEM] * (3 + tiles),
        out_specs=(VMEM, VMEM),
        compiler_params=params_of,
        cost_estimate=pl.CostEstimate(flops=1_000_000, bytes_accessed=2_000_000, transcendentals=0),
    )(me.reshape(1), prev_mean, estimate, direction, gradient[:epochs], own_sums, *returned)


def on_device(slc, offsets, weights, estimate, direction, prev_mean):
    epochs, rows, columns = slc.shape[1:]
    fits = columns == LANES * lax.axis_size("epoch") and lax.axis_size("epoch") > 1
    size = lax.axis_size("epoch")
    fits = fits and size & (size - 1) == 0 and 2 * epochs * SIDES <= PARAM_LANE and rows % HALO == 0 and epochs == 2 * SLOTS
    plan = transposed_plan if fits else ring_plan
    return plan(slc, offsets, weights, estimate, direction, prev_mean)


def solution(mesh):
    return jax.shard_map(
        on_device,
        mesh=mesh,
        in_specs=(
            P(None, ("groups", "epoch"), "space", "sub"),
            P(("groups", "epoch"), None),
            P(("groups", "epoch"), None),
            P(("groups", "epoch"), "space", "sub"),
            P(("groups", "epoch"), "space", "sub"),
            P(),
        ),
        out_specs=(P(("groups", "epoch"), "space", "sub"), P(("groups", "epoch"), "space", "sub")),
        check_vma=False,
    )
```

```python
import functools
import math

import jax
import jax.numpy as jnp
import numpy as np
from jax import lax
from jax.experimental import pallas as pl
from jax.experimental.pallas import tpu as pltpu
from jax.sharding import PartitionSpec as P

SLOTS = 4
OFFS = 8
LOOK = 4
RADIUS = 3


EPSILON = 1e-06


def passed_along(x, axis, by):
    size = lax.axis_size(axis)
    return lax.ppermute(x, axis, [(i, (i + by) % size) for i in range(size)])


def extended_2(block, sides, width):
    for axis, dim in sides:
        count = lax.axis_size(axis)
        forward = [(i, i + 1) for i in range(count - 1)]
        backward = [(target, source) for source, target in forward]
        low = lax.ppermute(
            lax.slice_in_dim(block, block.shape[dim] - width, None, axis=dim), axis, forward
        )
        high = lax.ppermute(lax.slice_in_dim(block, 0, width, axis=dim), axis, backward)
        block = jnp.concatenate([low, block, high], axis=dim)
    return block


def looked_sum(field):
    shape = field.shape
    return jnp.sum(field.reshape(shape[:-2] + (shape[-2] // LOOK, LOOK, shape[-1])), axis=-2)


def window_sum(padded, axis):
    length = padded.shape[axis] - 2 * RADIUS
    total = lax.slice_in_dim(padded, 0, length, axis=axis)
    for shift_at in range(1, 2 * RADIUS + 1):
        total = total + lax.slice_in_dim(padded, shift_at, shift_at + length, axis=axis)
    return total


def ring_plan(slc, offsets, weights, estimate, direction, prev_mean):
    epochs_here = slc.shape[1]
    look_rows = slc.shape[2] // LOOK
    col_count = slc.shape[3]
    ahead = passed_along(slc, "epoch", -1)
    extended = jnp.concatenate([slc, ahead], axis=1)
    numbers = jnp.arange(epochs_here, dtype=jnp.int32)
    partner = numbers[:, None] + offsets
    own_real = slc[0].astype(jnp.float32)
    own_imag = slc[1].astype(jnp.float32)
    ext_real = extended[0].astype(jnp.float32)
    ext_imag = extended[1].astype(jnp.float32)
    powers = looked_sum(ext_real * ext_real + ext_imag * ext_imag)
    pieces = []
    for slot_index in range(SLOTS):
        mate_real = jnp.take(ext_real, partner[:, slot_index], axis=0)
        mate_imag = jnp.take(ext_imag, partner[:, slot_index], axis=0)
        pieces.append(looked_sum(own_real * mate_real + own_imag * mate_imag))
        pieces.append(looked_sum(own_imag * mate_real - own_real * mate_imag))
    pair_count = epochs_here * 2 * SLOTS
    stacked = jnp.concatenate(
        [jnp.stack(pieces, axis=1).reshape(pair_count, look_rows, col_count), powers], axis=0
    )
    padded = extended_2(stacked, (("space", 1), ("sub", 2)), RADIUS)
    boxed = window_sum(window_sum(padded, 1), 2)
    pair_boxed = boxed[:pair_count].reshape(epochs_here, 2 * SLOTS, look_rows, col_count)
    power_box = boxed[pair_count:]
    coh_real = pair_boxed[:, 0::2]
    coh_imag = pair_boxed[:, 1::2]
    denominator = power_box[:epochs_here, None] * jnp.take(power_box, partner, axis=0) + EPSILON
    coherence = (coh_real * coh_real + coh_imag * coh_imag) / denominator
    observed = coh_imag / jnp.sqrt(denominator)
    est_ahead = passed_along(estimate, "epoch", -1)
    est_extended = jnp.concatenate([estimate, est_ahead], axis=0)
    fitted = estimate[:, None] - jnp.take(est_extended, partner, axis=0)
    factor = weights[:, :, None, None] * coherence
    weighted = factor * (observed - fitted)
    flattened = weighted.reshape(epochs_here * SLOTS, look_rows * col_count)
    selector = (
        jnp.arange(epochs_here + OFFS, dtype=jnp.int32)[:, None] == partner.reshape(1, -1)
    ).astype(jnp.float32)
    gathered = jnp.dot(
        selector, flattened, precision=lax.Precision.HIGHEST, preferred_element_type=jnp.float32
    ).reshape(epochs_here + OFFS, look_rows, col_count)
    own_part = jnp.sum(weighted, axis=1) - gathered[:epochs_here]
    returned = passed_along(-gathered[epochs_here:], "epoch", 1)
    gradient = jnp.concatenate([own_part + returned, own_part[OFFS:]], axis=0)
    cell_count = float(
        epochs_here
        * lax.axis_size("epoch")
        * look_rows
        * lax.axis_size("space")
        * col_count
        * lax.axis_size("sub")
    )
    local_norm = jnp.sum(gradient * gradient)
    local_crossed = jnp.sum(gradient * direction)
    mean_before = prev_mean[0]
    fields_ahead = passed_along(
        jnp.stack([gradient, direction]).astype(jnp.bfloat16), "epoch", -1
    ).astype(jnp.float32)
    grad_extended = jnp.concatenate([gradient, fields_ahead[0]], axis=0)
    old_extended = jnp.concatenate([direction, fields_ahead[1]], axis=0)
    grad_spread = gradient[:, None] - jnp.take(grad_extended, partner, axis=0)
    old_spread = direction[:, None] - jnp.take(old_extended, partner, axis=0)
    totals = lax.psum(
        (
            local_norm,
            local_crossed,
            jnp.sum(factor * grad_spread * grad_spread),
            jnp.sum(factor * grad_spread * old_spread),
            jnp.sum(factor * old_spread * old_spread),
        ),
        ("epoch", "space", "sub"),
    )
    grad_norm, crossed, grad_term, mixed_term, old_term = totals
    momentum = grad_norm / cell_count / mean_before
    new_direction = gradient + momentum * direction
    curvature = grad_term + 2.0 * momentum * mixed_term + momentum * momentum * old_term
    along_sum = grad_norm + momentum * crossed
    step_size = along_sum / curvature
    return (estimate + step_size * new_direction, new_direction)


LANES = 128
SIDES = 2 * RADIUS
HALO = 16
FIELD_STEPS = 16383.0
GRADIENT_STEPS = 32000.0
PARAM_LANE = 96
VMEM = pl.BlockSpec(memory_space=pltpu.VMEM)
SMEM = pl.BlockSpec(memory_space=pltpu.SMEM)
VMEM_BYTES = 48 * 1024 * 1024


def split_two(value):
    high = value.astype(jnp.bfloat16)
    low = (value - high.astype(jnp.float32)).astype(jnp.bfloat16)
    return high, low


def edge_kernel(first, last, edge):
    epochs = first.shape[1]
    lane = lax.broadcasted_iota(jnp.int32, edge.shape, 1)
    total = jnp.zeros(edge.shape, jnp.float32)
    for part in range(2):
        for epoch in range(epochs):
            at = (part * epochs + epoch) * SIDES
            total = placed(lane, total, tile_of(last, part, epoch, 0), LANES - RADIUS, at)
            total = placed(lane, total, tile_of(first, part, epoch, 0), 0, at + RADIUS)
    edge[...] = total.astype(jnp.bfloat16)


def fixed_point(value):
    return jnp.floor(value * FIELD_STEPS + 0.5).astype(jnp.int32).astype(jnp.int16)


def from_fixed_point(value):
    return value.astype(jnp.int32).astype(jnp.float32) * (1.0 / FIELD_STEPS)


def fields_kernel(me, estimate, direction, *fields):
    look_rows = estimate.shape[1]
    tiles = len(fields)
    for shift, out in enumerate(fields):
        tile = lax.bitwise_xor(me[0], shift)
        columns = pl.ds(pl.multiple_of(tile * LANES, LANES), LANES)
        for epoch in range(estimate.shape[0]):
            here = slice(epoch * look_rows, (epoch + 1) * look_rows)
            out[0, here, :] = fixed_point(estimate[epoch, :, columns])
            out[1, here, :] = fixed_point(direction[epoch, :, columns])


def tile_of(slc, part, epoch, tile):
    return slc[part, epoch, :, tile * LANES : (tile + 1) * LANES].astype(jnp.float32)


def placed(lane, total, source, start, target):
    moved = pltpu.roll(source, (target - start) % LANES, axis=1)
    return jnp.where((lane >= target) & (lane < target + RADIUS), moved, total)


def pack_kernel(me, present, slc, params, before, after, *refs):
    messages, strips = refs[:-1], refs[-1]
    tiles = len(messages)
    epochs = slc.shape[1]
    rows = slc.shape[2]
    lane = lax.broadcasted_iota(jnp.int32, (rows, LANES), 1)
    value = params[...]
    high = value.astype(jnp.bfloat16).astype(jnp.float32)
    middle = (value - high).astype(jnp.bfloat16).astype(jnp.float32)
    low = value - high - middle
    third = PARAM_LANE + 2 * SLOTS
    split = jnp.where(lane < third, high, jnp.where(lane < third + SLOTS, middle, low))
    split = jnp.where(lane >= PARAM_LANE, split, 0.0)
    inside = lane < 2 * epochs * SIDES
    for tile in range(tiles):
        total = split
        if tile == 0:
            edge = before[...].astype(jnp.float32) * present[0]
            total = jnp.where(inside & (lane % SIDES < RADIUS), edge, total)
        if tile == tiles - 1:
            edge = after[...].astype(jnp.float32) * present[1]
            total = jnp.where(inside & (lane % SIDES >= RADIUS), edge, total)
        for part in range(2):
            for epoch in range(epochs):
                at = (part * epochs + epoch) * SIDES
                if tile > 0:
                    total = placed(lane, total, tile_of(slc, part, epoch, tile - 1), LANES - RADIUS, at)
                if tile < tiles - 1:
                    total = placed(lane, total, tile_of(slc, part, epoch, tile + 1), 0, at + RADIUS)
        strips[tile] = total.astype(jnp.bfloat16)
    for tile in range(tiles):
        shift = lax.bitwise_xor(me[0], tile)
        for number, message in enumerate(messages):

            @pl.when(shift == number)
            def _():
                for part in range(2):
                    for epoch in range(epochs):
                        at = (part * epochs + epoch) * rows
                        message[at : at + rows, :] = slc[part, epoch, :, tile * LANES : (tile + 1) * LANES]
                message[2 * epochs * rows :, :] = strips[tile]


def look_order(from_rows, first):
    looks = from_rows // LOOK
    to = np.arange(from_rows)[:, None]
    at = np.arange(from_rows)[None, :]
    return jnp.asarray(at == (to + first) % looks * LOOK + to // looks, jnp.bfloat16)


def unpack_tiles(order, sources, main, first, columns_of):
    looks = order.shape[0] // LOOK
    for start in range(0, len(sources), 4):
        parts = jnp.concatenate([columns_of(source) for source in sources[start : start + 4]], axis=1)
        value = jnp.dot(order, parts, preferred_element_type=jnp.float32)
        for one in range(4):
            for look in range(LOOK):
                main[first[start + one], look] = value[look * looks : (look + 1) * looks, one * LANES : (one + 1) * LANES]


def unpack_rims(by_look, looks, rim, first):
    share = LANES // SLOTS
    lane = lax.broadcasted_iota(jnp.int32, (looks, LANES), 1)
    for at, place in enumerate(first):
        value = jnp.zeros((looks, LANES), jnp.float32)
        for look in range(LOOK):
            target = look * SIDES
            moved = pltpu.roll(by_look[look * looks : (look + 1) * looks], (target - at * SIDES) % LANES, axis=1)
            value = jnp.where((lane >= target) & (lane < target + SIDES), moved, value)
        spread = share
        while spread < LANES:
            value = value + pltpu.roll(value, spread, axis=1)
            spread = 2 * spread
        rim[place] = value


def column_bands():
    share = LANES // SLOTS
    at = np.arange(2 * LANES)[:, None] % LANES
    to = np.arange(LANES)[None, :]
    side = at % share % SIDES
    source = np.where(side < RADIUS, side - RADIUS, LANES + side - RADIUS)
    column = (to - at // share * share) % LANES
    inside = (column < RADIUS) | (column >= LANES - RADIUS)
    inside = inside & (at % share < LOOK * SIDES)
    band = np.abs(at - to) <= RADIUS
    rim_band = inside & (np.abs(source - column) <= RADIUS)
    return jnp.asarray(band, jnp.bfloat16), jnp.asarray(rim_band, jnp.bfloat16)


def mixed(values):
    lane = lax.broadcasted_iota(jnp.int32, values[0].shape, 1)
    result = values[-1]
    for slot in range(SLOTS - 1):
        result = jnp.where(lane < (SLOTS - 1 - slot) * (LANES // SLOTS), values[SLOTS - 2 - slot], result)
    return result


def power_batches(blocks, epochs, looks, main, rim, looked, rim_looked):
    total = blocks * epochs
    group = 2 * SLOTS
    for block in range(blocks):
        for piece in range(0, looks, 8):
            rows_at = slice(piece, piece + 8)
            for half in range(2):
                squares = []
                for slot in range(SLOTS):
                    channel = half * SLOTS + slot
                    epoch = block * epochs + channel
                    value = None
                    for look in range(LOOK):
                        real = main[epoch, look, rows_at]
                        imag = main[total + epoch, look, rows_at]
                        one = real * real + imag * imag
                        value = one if value is None else value + one
                    at = (block * group + channel) * looks + piece
                    looked[at : at + 8, :] = value
                    real = rim[epoch, rows_at]
                    imag = rim[total + epoch, rows_at]
                    squares.append(real * real + imag * imag)
                at = (block * 2 + half) * looks + piece
                rim_looked[at : at + 8, :] = mixed(squares)


def pair_batch(epoch, mates, total, main, rim):
    own_re, own_im = main[epoch], main[total + epoch]
    reals, imags = [], []
    for mate in mates:
        mate_re, mate_im = main[mate], main[total + mate]
        real = own_re[0] * mate_re[0] + own_im[0] * mate_im[0]
        imag = own_im[0] * mate_re[0] - own_re[0] * mate_im[0]
        for look in range(1, LOOK):
            real = real + (own_re[look] * mate_re[look] + own_im[look] * mate_im[look])
            imag = imag + (own_im[look] * mate_re[look] - own_re[look] * mate_im[look])
        reals.append(real)
        imags.append(imag)
    own_re, own_im = rim[epoch], rim[total + epoch]
    mate_re = mixed([rim[mate] for mate in mates])
    mate_im = mixed([rim[total + mate] for mate in mates])
    rims = [own_re * mate_re + own_im * mate_im, own_im * mate_re - own_re * mate_im]
    return reals + imags, rims


def put(ref, block, values):
    rows = sum(value.shape[0] for value in values)
    ref[block * rows : (block + 1) * rows, :] = jnp.concatenate(values, axis=0)


def columns_summed(couple, looks, bands, looked, rim_looked):
    group = 2 * SLOTS
    f32 = jnp.float32
    at = slice(couple * 2 * group * looks, (couple + 1) * 2 * group * looks)
    halves = jnp.concatenate(split_two(looked[at, :]), axis=1)
    value = jnp.dot(halves, bands[0], preferred_element_type=f32)
    at = slice(couple * 4 * looks, (couple + 1) * 4 * looks)
    halves = jnp.concatenate(split_two(rim_looked[at, :]), axis=1)
    outer = jnp.dot(halves, bands[1], preferred_element_type=f32)
    lane = lax.broadcasted_iota(jnp.int32, (looks, LANES), 1)
    outside = (lane < RADIUS) | (lane >= LANES - RADIUS)
    results = []
    for channel in range(2 * group):
        batch, half, slot = channel // group, channel % group // SLOTS, channel % SLOTS
        row = (batch * 2 + half) * looks
        part = outer[row : row + looks]
        if slot > 0:
            part = pltpu.roll(part, LANES - slot * (LANES // SLOTS), axis=1)
        row = channel * looks
        results.append(value[row : row + looks] + jnp.where(outside, part, 0.0))
    return results


def rows_summed(channel, looks, look_rows, wide):
    first = channel * looks
    total = wide[pl.ds(first, look_rows), :]
    for shift in range(1, 2 * RADIUS + 1):
        total = total + wide[pl.ds(first + shift, look_rows), :]
    return total


def pair_couple(couple, total, partner, main, rim):
    products, rims = [], []
    for one in range(2):
        epoch = couple * 2 + one
        mates = [partner[epoch * SLOTS + slot] for slot in range(SLOTS)]
        more, more_rims = pair_batch(epoch, mates, total, main, rim)
        products += more
        rims += more_rims
    return products, rims


def clipped(value, last):
    return jnp.minimum(jnp.maximum(value, 0), last)


def pair_kernel(sizes, places, partner, weight, present, order, band, rim_band, *refs):
    epochs, rows, operands = sizes
    inputs = refs[:operands]
    factors, pulls, boxed, main, rim, looked, rim_looked, wide = refs[operands:]
    count = len(places)
    total = count * epochs
    look_rows = rows // LOOK
    halo_looks = HALO // LOOK
    looks = look_rows + 2 * halo_looks
    full_rows = rows + 2 * HALO
    group = 2 * SLOTS

    at = lax.broadcasted_iota(jnp.int32, (full_rows, full_rows), 1)
    keep = jnp.where(at < HALO, present[0], jnp.where(at >= HALO + rows, present[1], 1.0))
    order = (order[...].astype(jnp.float32) * keep).astype(jnp.bfloat16)
    bands = band[...], rim_band[...]
    for block, (tile_at, top_at, bottom_at, top_row, bottom_row) in enumerate(places):
        tile, top, bottom = inputs[tile_at], inputs[top_at], inputs[bottom_at]

        def rows_of(at):
            above = top[top_row + at * HALO : top_row + (at + 1) * HALO, :]
            below = bottom[bottom_row + at * HALO : bottom_row + (at + 1) * HALO, :]
            return jnp.concatenate([above, tile[at * rows : (at + 1) * rows, :], below], axis=0)

        first = [part * total + block * epochs + epoch for part in range(2) for epoch in range(epochs)]
        unpack_tiles(order, range(2 * epochs), main, first, rows_of)
        by_look = jnp.dot(order, rows_of(2 * epochs), preferred_element_type=jnp.float32)
        unpack_rims(by_look, looks, rim, first)
    power_batches(count, epochs, looks, main, rim, looked, rim_looked)
    powers = count // 2
    couples = total // 2

    def boxed_of(channel):
        return boxed[pl.ds(pl.multiple_of(channel * look_rows, look_rows), look_rows), :]

    def finished(couple):
        results = []
        for one in range(2):
            epoch = couple * 2 + one
            own_power = boxed_of(epoch)
            first = (2 * powers + epoch) * (group * look_rows)
            parts = boxed[first : first + group * look_rows, :]
            parts = parts.reshape(group, look_rows, LANES)
            for slot in range(SLOTS):
                pair = epoch * SLOTS + slot
                inverse = lax.rsqrt(own_power * boxed_of(partner[pair]) + EPSILON)
                unit_re = parts[slot] * inverse
                unit_im = parts[SLOTS + slot] * inverse
                factor = weight[pair] * (unit_re * unit_re + unit_im * unit_im)
                results.append((factor, factor * unit_im))
        return results

    def boxes(couple):
        return [rows_summed(couple * 2 * group + one, looks, look_rows, wide) for one in range(2 * group)]

    def turn(number, steps):
        if 3 in steps:
            results = finished(number - 3)
        if 2 in steps:
            sums = boxes(powers + number - 2)
        if 1 in steps:
            columns = columns_summed(powers + number - 1, looks, bands, looked, rim_looked)
        if 0 in steps:
            products, rims = pair_couple(number, total, partner, main, rim)
        if 3 in steps:
            for ref, values in zip((factors, pulls), zip(*results)):
                ref[pl.ds((number - 3) * 2 * SLOTS, 2 * SLOTS)] = jnp.stack(values)
        if 2 in steps:
            put(boxed, powers + number - 2, sums)
        if 1 in steps:
            put(wide, powers + number - 1, columns)
        if 0 in steps:
            put(looked, powers + number, products)
            put(rim_looked, powers + number, rims)

    for couple in range(powers):
        put(wide, couple, columns_summed(couple, looks, bands, looked, rim_looked))
    turn(0, (0,))
    for couple in range(powers):
        put(boxed, couple, boxes(couple))
    turn(1, (0, 1))
    turn(2, (0, 1, 2))
    for number in range(3, couples):
        turn(number, (0, 1, 2, 3))
    turn(couples, (1, 2, 3))
    turn(couples + 1, (2, 3))
    turn(couples + 2, (3,))


def gradient_kernel(sizes, partner, *refs):
    tiles, epochs = sizes
    fields = refs[:tiles]
    factors, pulls, gradient, sums, est, old, shares = refs[tiles:]
    look_rows = est.shape[1]
    total = tiles * epochs
    f32 = jnp.float32
    for block in range(tiles):
        for epoch in range(epochs):
            here = slice(epoch * look_rows, (epoch + 1) * look_rows)
            est[block * epochs + epoch] = from_fixed_point(fields[block][0, here, :])
            old[block * epochs + epoch] = from_fixed_point(fields[block][1, here, :])
    mates = [[partner[epoch * SLOTS + slot] for slot in range(SLOTS)] for epoch in range(total)]
    for epoch in range(total):
        own_est = est[epoch]
        own = None
        for slot, mate in enumerate(mates[epoch]):
            pair = epoch * SLOTS + slot
            weighted = pulls[pair] - factors[pair] * (own_est - est[mate])
            own = weighted if own is None else own + weighted
            shares[pair] = weighted
        gradient[epoch] = own
    for epoch in range(total):
        values = [gradient[mate] - shares[epoch * SLOTS + slot] for slot, mate in enumerate(mates[epoch])]
        for mate, value in zip(mates[epoch], values):
            gradient[mate] = value

    zero = jnp.zeros((look_rows, LANES), f32)
    norm, crossed, grad_term, mixed_term, old_term = (zero,) * 5
    for epoch in range(total):
        own_grad = gradient[epoch]
        own_old = old[epoch]
        norm = norm + own_grad * own_grad
        crossed = crossed + own_grad * own_old
        for slot, mate in enumerate(mates[epoch]):
            factor = factors[epoch * SLOTS + slot]
            grad_spread = own_grad - gradient[mate]
            old_spread = own_old - old[mate]
            pulled = factor * grad_spread
            grad_term = grad_term + pulled * grad_spread
            mixed_term = mixed_term + pulled * old_spread
            old_term = old_term + factor * old_spread * old_spread
    sums[...] = jnp.zeros(sums.shape, f32)
    for at, value in enumerate((norm, crossed, grad_term, mixed_term, old_term)):
        sums[at : at + 1, :] = jnp.sum(value, axis=0, keepdims=True)


def exponent_of(size):
    power = jnp.ceil(jnp.log(jnp.maximum(size, 1e-30)) * (1.0 / math.log(2.0)))
    return jnp.clip(power, -110.0, 110.0)


def whole(value):
    return jnp.floor(value + 0.5).astype(jnp.int32).astype(jnp.int16)


def number_of(value):
    return value.astype(jnp.int32).astype(jnp.float32)


def code_kernel(gradient, *coded):
    epochs = gradient.shape[0] // (len(coded) + 1)
    look_rows = gradient.shape[1]
    for number, out in enumerate(coded):
        powers = []
        for epoch in range(epochs):
            value = gradient[(number + 1) * epochs + epoch]
            power = exponent_of(jnp.max(jnp.abs(value), axis=0, keepdims=True))
            out[epoch * look_rows : (epoch + 1) * look_rows, :] = whole(value * (jnp.exp2(-power) * GRADIENT_STEPS))
            powers.append(power)
        powers.append(jnp.zeros((HALO - epochs, LANES), jnp.float32))
        out[epochs * look_rows :, :] = whole(jnp.concatenate(powers, axis=0))


def update_kernel(cell_count, me, prev_mean, estimate, direction, gradient, *refs):
    new_estimate, new_direction = refs[-2:]
    tiles = estimate.shape[2] // LANES
    pieces, scalars = refs[: tiles - 1], refs[tiles - 1 : -2]
    epochs = estimate.shape[0]
    look_rows = estimate.shape[1]
    coded_rows = epochs * look_rows + HALO
    total = scalars[0][...]
    for other in scalars[1:]:
        total = total + other[...]
    total = jnp.sum(total, axis=1, keepdims=True)
    grad_norm, crossed, grad_term, mixed, old_term = (total[at : at + 1, :] for at in range(5))
    momentum = grad_norm / cell_count / prev_mean[0]
    curvature = grad_term + 2.0 * momentum * mixed + momentum * momentum * old_term
    step = (grad_norm + momentum * crossed) / curvature
    momentum = jnp.broadcast_to(momentum, (look_rows, LANES))
    step = jnp.broadcast_to(step, (look_rows, LANES))
    for shift in range(tiles):
        tile = lax.bitwise_xor(me[0], shift)
        columns = pl.ds(pl.multiple_of(tile * LANES, LANES), LANES)
        if shift > 0:
            piece = pieces[shift - 1]
            scale = jnp.exp2(number_of(piece[epochs * look_rows : coded_rows, :])) * (1.0 / GRADIENT_STEPS)
        for epoch in range(epochs):
            if shift == 0:
                value = gradient[epoch]
            else:
                value = number_of(piece[epoch * look_rows : (epoch + 1) * look_rows, :]) * scale[epoch : epoch + 1, :]
            moved = value + momentum * direction[epoch, :, columns]
            new_direction[epoch, :, columns] = moved
            new_estimate[epoch, :, columns] = estimate[epoch, :, columns] + step * moved


def swapped(up, down, axis):
    size = lax.axis_size(axis)
    if size == 1:
        return jnp.zeros_like(up), jnp.zeros_like(down)
    if size == 2:
        first = lax.axis_index(axis) == 0
        got = lax.ppermute(jnp.where(first, up, down), axis, [(0, 1), (1, 0)])
        return got, got
    forward = [(i, i + 1) for i in range(size - 1)]
    backward = [(target, source) for source, target in forward]
    return lax.ppermute(up, axis, forward), lax.ppermute(down, axis, backward)


def exchanged(x, axis, by):
    size = lax.axis_size(axis)
    return lax.ppermute(x, axis, [(i, i ^ by) for i in range(size)])


def transposed_plan(slc, offsets, weights, estimate, direction, prev_mean):
    f32 = jnp.float32
    bf16 = jnp.bfloat16
    tiles = lax.axis_size("epoch")
    me = lax.axis_index("epoch")
    epochs, rows, columns = slc.shape[1:]
    look_rows = rows // LOOK
    total = tiles * epochs
    tile_rows = 2 * epochs * rows
    params_of = pltpu.CompilerParams(vmem_limit_bytes=VMEM_BYTES)

    sub = lax.axis_index("sub")
    outer_tile = (2, epochs, rows, LANES)
    edge = pl.pallas_call(
        edge_kernel,
        out_shape=jax.ShapeDtypeStruct((rows, LANES), bf16),
        grid=(1,),
        in_specs=[
            pl.BlockSpec(outer_tile, lambda _: (0, 0, 0, 0)),
            pl.BlockSpec(outer_tile, lambda _: (0, 0, 0, tiles - 1)),
        ],
        out_specs=pl.BlockSpec((rows, LANES), lambda _: (0, 0)),
        compiler_params=params_of,
        cost_estimate=pl.CostEstimate(flops=1_000_000, bytes_accessed=1_000_000, transcendentals=0),
    )(slc, slc)
    before, after = swapped(edge, edge, "sub")
    params = jnp.zeros((rows, LANES), f32)
    listed = jnp.concatenate([offsets.astype(f32), weights, weights, weights], axis=1)
    params = lax.dynamic_update_slice(params, listed, (0, PARAM_LANE))
    sub_present = jnp.stack([sub > 0, sub < lax.axis_size("sub") - 1]).astype(f32)
    messages = pl.pallas_call(
        pack_kernel,
        out_shape=(jax.ShapeDtypeStruct((tile_rows + rows, LANES), bf16),) * tiles,
        in_specs=[SMEM] * 2 + [VMEM] * 4,
        out_specs=(VMEM,) * tiles,
        scratch_shapes=[pltpu.VMEM((tiles, rows, LANES), bf16)],
        compiler_params=params_of,
        cost_estimate=pl.CostEstimate(flops=3_000_000, bytes_accessed=4_000_000, transcendentals=0),
    )(me.reshape(1), sub_present, slc, params, before, after)
    space = lax.axis_index("space")
    spaces = lax.axis_size("space")
    present = jnp.stack([space > 0, space < spaces - 1]).astype(f32)

    def halo(pieces):
        def border(from_row):
            cuts = [lax.dynamic_slice_in_dim(piece, from_row, HALO, axis=1).reshape(-1, LANES) for piece in pieces]
            return jnp.concatenate(cuts, axis=0)

        if spaces == 2:
            got = lax.ppermute(border(jnp.where(space == 0, rows - HALO, 0)), "space", [(0, 1), (1, 0)])
            return got, got
        return swapped(border(rows - HALO), border(0), "space")

    block = [messages[0]] + [exchanged(messages[by], "epoch", by) for by in range(1, tiles)]
    estimate, direction, _ = lax.optimization_barrier((estimate, direction, messages))
    fields = pl.pallas_call(
        fields_kernel,
        out_shape=(jax.ShapeDtypeStruct((2, epochs * look_rows, LANES), jnp.int16),) * tiles,
        in_specs=[SMEM] + [VMEM] * 2,
        out_specs=(VMEM,) * tiles,
        compiler_params=params_of,
        cost_estimate=pl.CostEstimate(flops=1_000_000, bytes_accessed=2_000_000, transcendentals=0),
    )(me.reshape(1), estimate, direction)
    def params_in(shift):
        return block[shift][tile_rows : tile_rows + epochs, PARAM_LANE : PARAM_LANE + 4 * SLOTS].astype(f32)

    halos = [halo([array.reshape(-1, rows, LANES)]) for array in block]
    late = lax.optimization_barrier((fields, block, halos[1:-1]))[0]
    field = [fields[0]] + [exchanged(late[by], "epoch", by) for by in range(1, tiles)]

    listed = jnp.concatenate([params_in(shift) for shift in range(tiles)], axis=0)
    place = jnp.arange(total, dtype=jnp.int32)[:, None]
    first = lax.bitwise_xor(place // epochs, me) * epochs + place % epochs
    mate = lax.rem(first + listed[:, :SLOTS].astype(jnp.int32), total)
    partner = (lax.bitwise_xor(mate // epochs, me) * epochs + mate % epochs).reshape(-1)
    weight = listed[:, SLOTS : 2 * SLOTS] + listed[:, 2 * SLOTS : 3 * SLOTS] + listed[:, 3 * SLOTS :]
    order = look_order(rows + 2 * HALO, HALO // LOOK - RADIUS)
    bands = column_bands()
    operands = list(block)
    places = []
    for shift in range(tiles):
        top, bottom = halos[shift]
        operands.append(top)
        top_at = bottom_at = len(operands) - 1
        if bottom is not top:
            operands.append(bottom)
            bottom_at = len(operands) - 1
        places.append((shift, top_at, bottom_at, 0, 0))
    looks = (rows + 2 * HALO) // LOOK
    group = 2 * SLOTS
    batches = tiles + total
    shape = jax.ShapeDtypeStruct((total * SLOTS, look_rows, LANES), f32)
    factors, pulls = pl.pallas_call(
        functools.partial(pair_kernel, (epochs, rows, len(operands)), tuple(places)),
        out_shape=(shape, shape),
        in_specs=[SMEM] * 3 + [VMEM] * (3 + len(operands)),
        out_specs=(VMEM, VMEM),
        scratch_shapes=[
            pltpu.VMEM((batches * group * look_rows, LANES), f32),
            pltpu.VMEM((2 * total, LOOK, looks, LANES), f32),
            pltpu.VMEM((2 * total, looks, LANES), f32),
            pltpu.VMEM((batches * group * looks, LANES), f32),
            pltpu.VMEM((batches * 2 * looks, LANES), f32),
            pltpu.VMEM((batches * group * looks, LANES), f32),
        ],
        compiler_params=params_of,
        cost_estimate=pl.CostEstimate(flops=20_000_000, bytes_accessed=30_000_000, transcendentals=0),
    )(partner, weight.reshape(-1), present, order, *bands, *operands)
    gradient, sums = pl.pallas_call(
        functools.partial(gradient_kernel, (tiles, epochs)),
        out_shape=(
            jax.ShapeDtypeStruct((total, look_rows, LANES), f32),
            jax.ShapeDtypeStruct((8, LANES), f32),
        ),
        in_specs=[SMEM] + [VMEM] * (tiles + 2),
        out_specs=(VMEM, VMEM),
        scratch_shapes=[pltpu.VMEM((total, look_rows, LANES), f32)] * 2
        + [pltpu.VMEM((total * SLOTS, look_rows, LANES), f32)],
        compiler_params=params_of,
        cost_estimate=pl.CostEstimate(flops=10_000_000, bytes_accessed=8_000_000, transcendentals=0),
    )(partner, *field, factors, pulls)

    place = ("space", "sub")
    count = spaces * lax.axis_size("sub")
    shared = [sums] + [lax.ppermute(sums, place, [(i, (i + by) % count) for i in range(count)]) for by in range(1, count)]
    coded_shape = jax.ShapeDtypeStruct((epochs * look_rows + HALO, LANES), jnp.int16)
    coded = pl.pallas_call(
        code_kernel,
        out_shape=(coded_shape,) * (tiles - 1),
        in_specs=[VMEM],
        out_specs=(VMEM,) * (tiles - 1),
        compiler_params=params_of,
        cost_estimate=pl.CostEstimate(flops=1_000_000, bytes_accessed=1_000_000, transcendentals=0),
    )(gradient)
    returned = [exchanged(piece, "epoch", by + 1) for by, piece in enumerate(coded)]
    here = lax.optimization_barrier((sum(shared[1:], shared[0]), returned[0]))[0]
    scalars = [here] + [exchanged(here, "epoch", by) for by in range(1, tiles)]
    cell_count = float(total * look_rows * spaces * columns * lax.axis_size("sub"))
    return pl.pallas_call(
        functools.partial(update_kernel, cell_count),
        out_shape=(jax.ShapeDtypeStruct(estimate.shape, f32),) * 2,
        in_specs=[SMEM] * 2 + [VMEM] * (2 + 2 * tiles),
        out_specs=(VMEM, VMEM),
        compiler_params=params_of,
        cost_estimate=pl.CostEstimate(flops=1_000_000, bytes_accessed=2_000_000, transcendentals=0),
    )(me.reshape(1), prev_mean, estimate, direction, gradient[:epochs], *returned, *scalars)


def on_device(slc, offsets, weights, estimate, direction, prev_mean):
    epochs, rows, columns = slc.shape[1:]
    fits = columns == LANES * lax.axis_size("epoch") and lax.axis_size("epoch") > 1
    size = lax.axis_size("epoch")
    fits = fits and size & (size - 1) == 0 and 2 * epochs * SIDES <= PARAM_LANE and rows % HALO == 0 and epochs == 2 * SLOTS
    plan = transposed_plan if fits else ring_plan
    return plan(slc, offsets, weights, estimate, direction, prev_mean)


def solution(mesh):
    return jax.shard_map(
        on_device,
        mesh=mesh,
        in_specs=(
            P(None, ("groups", "epoch"), "space", "sub"),
            P(("groups", "epoch"), None),
            P(("groups", "epoch"), None),
            P(("groups", "epoch"), "space", "sub"),
            P(("groups", "epoch"), "space", "sub"),
            P(),
        ),
        out_specs=(P(("groups", "epoch"), "space", "sub"), P(("groups", "epoch"), "space", "sub")),
        check_vma=False,
    )
```

```python
import functools
import math

import jax
import jax.numpy as jnp
import numpy as np
from jax import lax
from jax.experimental import pallas as pl
from jax.experimental.pallas import tpu as pltpu
from jax.sharding import PartitionSpec as P

SLOTS = 4
OFFS = 8
LOOK = 4
RADIUS = 3


EPSILON = 1e-06


def passed_along(x, axis, by):
    size = lax.axis_size(axis)
    return lax.ppermute(x, axis, [(i, (i + by) % size) for i in range(size)])


def extended_2(block, sides, width):
    for axis, dim in sides:
        count = lax.axis_size(axis)
        forward = [(i, i + 1) for i in range(count - 1)]
        backward = [(target, source) for source, target in forward]
        low = lax.ppermute(
            lax.slice_in_dim(block, block.shape[dim] - width, None, axis=dim), axis, forward
        )
        high = lax.ppermute(lax.slice_in_dim(block, 0, width, axis=dim), axis, backward)
        block = jnp.concatenate([low, block, high], axis=dim)
    return block


def looked_sum(field):
    shape = field.shape
    return jnp.sum(field.reshape(shape[:-2] + (shape[-2] // LOOK, LOOK, shape[-1])), axis=-2)


def window_sum(padded, axis):
    length = padded.shape[axis] - 2 * RADIUS
    total = lax.slice_in_dim(padded, 0, length, axis=axis)
    for shift_at in range(1, 2 * RADIUS + 1):
        total = total + lax.slice_in_dim(padded, shift_at, shift_at + length, axis=axis)
    return total


def ring_plan(slc, offsets, weights, estimate, direction, prev_mean):
    epochs_here = slc.shape[1]
    look_rows = slc.shape[2] // LOOK
    col_count = slc.shape[3]
    ahead = passed_along(slc, "epoch", -1)
    extended = jnp.concatenate([slc, ahead], axis=1)
    numbers = jnp.arange(epochs_here, dtype=jnp.int32)
    partner = numbers[:, None] + offsets
    own_real = slc[0].astype(jnp.float32)
    own_imag = slc[1].astype(jnp.float32)
    ext_real = extended[0].astype(jnp.float32)
    ext_imag = extended[1].astype(jnp.float32)
    powers = looked_sum(ext_real * ext_real + ext_imag * ext_imag)
    pieces = []
    for slot_index in range(SLOTS):
        mate_real = jnp.take(ext_real, partner[:, slot_index], axis=0)
        mate_imag = jnp.take(ext_imag, partner[:, slot_index], axis=0)
        pieces.append(looked_sum(own_real * mate_real + own_imag * mate_imag))
        pieces.append(looked_sum(own_imag * mate_real - own_real * mate_imag))
    pair_count = epochs_here * 2 * SLOTS
    stacked = jnp.concatenate(
        [jnp.stack(pieces, axis=1).reshape(pair_count, look_rows, col_count), powers], axis=0
    )
    padded = extended_2(stacked, (("space", 1), ("sub", 2)), RADIUS)
    boxed = window_sum(window_sum(padded, 1), 2)
    pair_boxed = boxed[:pair_count].reshape(epochs_here, 2 * SLOTS, look_rows, col_count)
    power_box = boxed[pair_count:]
    coh_real = pair_boxed[:, 0::2]
    coh_imag = pair_boxed[:, 1::2]
    denominator = power_box[:epochs_here, None] * jnp.take(power_box, partner, axis=0) + EPSILON
    coherence = (coh_real * coh_real + coh_imag * coh_imag) / denominator
    observed = coh_imag / jnp.sqrt(denominator)
    est_ahead = passed_along(estimate, "epoch", -1)
    est_extended = jnp.concatenate([estimate, est_ahead], axis=0)
    fitted = estimate[:, None] - jnp.take(est_extended, partner, axis=0)
    factor = weights[:, :, None, None] * coherence
    weighted = factor * (observed - fitted)
    flattened = weighted.reshape(epochs_here * SLOTS, look_rows * col_count)
    selector = (
        jnp.arange(epochs_here + OFFS, dtype=jnp.int32)[:, None] == partner.reshape(1, -1)
    ).astype(jnp.float32)
    gathered = jnp.dot(
        selector, flattened, precision=lax.Precision.HIGHEST, preferred_element_type=jnp.float32
    ).reshape(epochs_here + OFFS, look_rows, col_count)
    own_part = jnp.sum(weighted, axis=1) - gathered[:epochs_here]
    returned = passed_along(-gathered[epochs_here:], "epoch", 1)
    gradient = jnp.concatenate([own_part + returned, own_part[OFFS:]], axis=0)
    cell_count = float(
        epochs_here
        * lax.axis_size("epoch")
        * look_rows
        * lax.axis_size("space")
        * col_count
        * lax.axis_size("sub")
    )
    local_norm = jnp.sum(gradient * gradient)
    local_crossed = jnp.sum(gradient * direction)
    mean_before = prev_mean[0]
    fields_ahead = passed_along(
        jnp.stack([gradient, direction]).astype(jnp.bfloat16), "epoch", -1
    ).astype(jnp.float32)
    grad_extended = jnp.concatenate([gradient, fields_ahead[0]], axis=0)
    old_extended = jnp.concatenate([direction, fields_ahead[1]], axis=0)
    grad_spread = gradient[:, None] - jnp.take(grad_extended, partner, axis=0)
    old_spread = direction[:, None] - jnp.take(old_extended, partner, axis=0)
    totals = lax.psum(
        (
            local_norm,
            local_crossed,
            jnp.sum(factor * grad_spread * grad_spread),
            jnp.sum(factor * grad_spread * old_spread),
            jnp.sum(factor * old_spread * old_spread),
        ),
        ("epoch", "space", "sub"),
    )
    grad_norm, crossed, grad_term, mixed_term, old_term = totals
    momentum = grad_norm / cell_count / mean_before
    new_direction = gradient + momentum * direction
    curvature = grad_term + 2.0 * momentum * mixed_term + momentum * momentum * old_term
    along_sum = grad_norm + momentum * crossed
    step_size = along_sum / curvature
    return (estimate + step_size * new_direction, new_direction)


LANES = 128
SIDES = 2 * RADIUS
HALO = 16
FIELD_STEPS = 16383.0
GRADIENT_STEPS = 32000.0
PARAM_LANE = 96
VMEM = pl.BlockSpec(memory_space=pltpu.VMEM)
SMEM = pl.BlockSpec(memory_space=pltpu.SMEM)
VMEM_BYTES = 48 * 1024 * 1024


def split_two(value):
    high = value.astype(jnp.bfloat16)
    low = (value - high.astype(jnp.float32)).astype(jnp.bfloat16)
    return high, low


def edge_kernel(first, last, edge):
    epochs = first.shape[1]
    lane = lax.broadcasted_iota(jnp.int32, edge.shape, 1)
    total = jnp.zeros(edge.shape, jnp.float32)
    for part in range(2):
        for epoch in range(epochs):
            at = (part * epochs + epoch) * SIDES
            total = placed(lane, total, tile_of(last, part, epoch, 0), LANES - RADIUS, at)
            total = placed(lane, total, tile_of(first, part, epoch, 0), 0, at + RADIUS)
    edge[...] = total.astype(jnp.bfloat16)


def fixed_point(value):
    return jnp.floor(value * FIELD_STEPS + 0.5).astype(jnp.int32).astype(jnp.int16)


def from_fixed_point(value):
    return value.astype(jnp.int32).astype(jnp.float32) * (1.0 / FIELD_STEPS)


def fields_kernel(me, estimate, direction, *fields):
    look_rows = estimate.shape[1]
    tiles = len(fields)
    for shift, out in enumerate(fields):
        tile = lax.bitwise_xor(me[0], shift)
        columns = pl.ds(pl.multiple_of(tile * LANES, LANES), LANES)
        for epoch in range(estimate.shape[0]):
            here = slice(epoch * look_rows, (epoch + 1) * look_rows)
            out[0, here, :] = fixed_point(estimate[epoch, :, columns])
            out[1, here, :] = fixed_point(direction[epoch, :, columns])


def tile_of(slc, part, epoch, tile):
    return slc[part, epoch, :, tile * LANES : (tile + 1) * LANES].astype(jnp.float32)


def placed(lane, total, source, start, target):
    moved = pltpu.roll(source, (target - start) % LANES, axis=1)
    return jnp.where((lane >= target) & (lane < target + RADIUS), moved, total)


def pack_kernel(me, present, slc, params, before, after, *refs):
    messages, strips = refs[:-1], refs[-1]
    tiles = len(messages)
    epochs = slc.shape[1]
    rows = slc.shape[2]
    lane = lax.broadcasted_iota(jnp.int32, (rows, LANES), 1)
    value = params[...]
    high = value.astype(jnp.bfloat16).astype(jnp.float32)
    middle = (value - high).astype(jnp.bfloat16).astype(jnp.float32)
    low = value - high - middle
    third = PARAM_LANE + 2 * SLOTS
    split = jnp.where(lane < third, high, jnp.where(lane < third + SLOTS, middle, low))
    split = jnp.where(lane >= PARAM_LANE, split, 0.0)
    inside = lane < 2 * epochs * SIDES
    for tile in range(tiles):
        total = split
        if tile == 0:
            edge = before[...].astype(jnp.float32) * present[0]
            total = jnp.where(inside & (lane % SIDES < RADIUS), edge, total)
        if tile == tiles - 1:
            edge = after[...].astype(jnp.float32) * present[1]
            total = jnp.where(inside & (lane % SIDES >= RADIUS), edge, total)
        for part in range(2):
            for epoch in range(epochs):
                at = (part * epochs + epoch) * SIDES
                if tile > 0:
                    total = placed(lane, total, tile_of(slc, part, epoch, tile - 1), LANES - RADIUS, at)
                if tile < tiles - 1:
                    total = placed(lane, total, tile_of(slc, part, epoch, tile + 1), 0, at + RADIUS)
        strips[tile] = total.astype(jnp.bfloat16)
    for tile in range(tiles):
        shift = lax.bitwise_xor(me[0], tile)
        for number, message in enumerate(messages):

            @pl.when(shift == number)
            def _():
                for part in range(2):
                    for epoch in range(epochs):
                        at = (part * epochs + epoch) * rows
                        message[at : at + rows, :] = slc[part, epoch, :, tile * LANES : (tile + 1) * LANES]
                message[2 * epochs * rows :, :] = strips[tile]


def look_order(from_rows, first):
    looks = from_rows // LOOK
    to = np.arange(from_rows)[:, None]
    at = np.arange(from_rows)[None, :]
    return jnp.asarray(at == (to + first) % looks * LOOK + to // looks, jnp.bfloat16)


def unpack_tiles(order, sources, main, first, columns_of):
    looks = order.shape[0] // LOOK
    for start in range(0, len(sources), 4):
        parts = jnp.concatenate([columns_of(source) for source in sources[start : start + 4]], axis=1)
        value = jnp.dot(order, parts, preferred_element_type=jnp.float32)
        for one in range(4):
            for look in range(LOOK):
                main[first[start + one], look] = value[look * looks : (look + 1) * looks, one * LANES : (one + 1) * LANES]


def unpack_rims(by_look, looks, rim, first):
    share = LANES // SLOTS
    lane = lax.broadcasted_iota(jnp.int32, (looks, LANES), 1)
    for at, place in enumerate(first):
        value = jnp.zeros((looks, LANES), jnp.float32)
        for look in range(LOOK):
            target = look * SIDES
            moved = pltpu.roll(by_look[look * looks : (look + 1) * looks], (target - at * SIDES) % LANES, axis=1)
            value = jnp.where((lane >= target) & (lane < target + SIDES), moved, value)
        spread = share
        while spread < LANES:
            value = value + pltpu.roll(value, spread, axis=1)
            spread = 2 * spread
        rim[place] = value


def column_bands():
    share = LANES // SLOTS
    at = np.arange(2 * LANES)[:, None] % LANES
    to = np.arange(LANES)[None, :]
    side = at % share % SIDES
    source = np.where(side < RADIUS, side - RADIUS, LANES + side - RADIUS)
    column = (to - at // share * share) % LANES
    inside = (column < RADIUS) | (column >= LANES - RADIUS)
    inside = inside & (at % share < LOOK * SIDES)
    band = np.abs(at - to) <= RADIUS
    rim_band = inside & (np.abs(source - column) <= RADIUS)
    return jnp.asarray(band, jnp.bfloat16), jnp.asarray(rim_band, jnp.bfloat16)


def mixed(values):
    lane = lax.broadcasted_iota(jnp.int32, values[0].shape, 1)
    result = values[-1]
    for slot in range(SLOTS - 1):
        result = jnp.where(lane < (SLOTS - 1 - slot) * (LANES // SLOTS), values[SLOTS - 2 - slot], result)
    return result


def power_batches(blocks, epochs, looks, main, rim, looked, rim_looked):
    total = blocks * epochs
    group = 2 * SLOTS
    for block in range(blocks):
        for piece in range(0, looks, 8):
            rows_at = slice(piece, piece + 8)
            for half in range(2):
                squares = []
                for slot in range(SLOTS):
                    channel = half * SLOTS + slot
                    epoch = block * epochs + channel
                    value = None
                    for look in range(LOOK):
                        real = main[epoch, look, rows_at]
                        imag = main[total + epoch, look, rows_at]
                        one = real * real + imag * imag
                        value = one if value is None else value + one
                    at = (block * group + channel) * looks + piece
                    looked[at : at + 8, :] = value
                    real = rim[epoch, rows_at]
                    imag = rim[total + epoch, rows_at]
                    squares.append(real * real + imag * imag)
                at = (block * 2 + half) * looks + piece
                rim_looked[at : at + 8, :] = mixed(squares)


def pair_batch(epoch, mates, total, main, rim):
    own_re, own_im = main[epoch], main[total + epoch]
    reals, imags = [], []
    for mate in mates:
        mate_re, mate_im = main[mate], main[total + mate]
        real = own_re[0] * mate_re[0] + own_im[0] * mate_im[0]
        imag = own_im[0] * mate_re[0] - own_re[0] * mate_im[0]
        for look in range(1, LOOK):
            real = real + (own_re[look] * mate_re[look] + own_im[look] * mate_im[look])
            imag = imag + (own_im[look] * mate_re[look] - own_re[look] * mate_im[look])
        reals.append(real)
        imags.append(imag)
    own_re, own_im = rim[epoch], rim[total + epoch]
    mate_re = mixed([rim[mate] for mate in mates])
    mate_im = mixed([rim[total + mate] for mate in mates])
    rims = [own_re * mate_re + own_im * mate_im, own_im * mate_re - own_re * mate_im]
    return reals + imags, rims


def put(ref, block, values):
    rows = sum(value.shape[0] for value in values)
    ref[block * rows : (block + 1) * rows, :] = jnp.concatenate(values, axis=0)


def columns_summed(couple, looks, bands, looked, rim_looked):
    group = 2 * SLOTS
    f32 = jnp.float32
    at = slice(couple * 2 * group * looks, (couple + 1) * 2 * group * looks)
    halves = jnp.concatenate(split_two(looked[at, :]), axis=1)
    value = jnp.dot(halves, bands[0], preferred_element_type=f32)
    at = slice(couple * 4 * looks, (couple + 1) * 4 * looks)
    halves = jnp.concatenate(split_two(rim_looked[at, :]), axis=1)
    outer = jnp.dot(halves, bands[1], preferred_element_type=f32)
    lane = lax.broadcasted_iota(jnp.int32, (looks, LANES), 1)
    outside = (lane < RADIUS) | (lane >= LANES - RADIUS)
    results = []
    for channel in range(2 * group):
        batch, half, slot = channel // group, channel % group // SLOTS, channel % SLOTS
        row = (batch * 2 + half) * looks
        part = outer[row : row + looks]
        if slot > 0:
            part = pltpu.roll(part, LANES - slot * (LANES // SLOTS), axis=1)
        row = channel * looks
        results.append(value[row : row + looks] + jnp.where(outside, part, 0.0))
    return results


def rows_summed(channel, looks, look_rows, wide):
    first = channel * looks
    total = wide[pl.ds(first, look_rows), :]
    for shift in range(1, 2 * RADIUS + 1):
        total = total + wide[pl.ds(first + shift, look_rows), :]
    return total


def pair_couple(couple, total, partner, main, rim):
    products, rims = [], []
    for one in range(2):
        epoch = couple * 2 + one
        mates = [partner[epoch * SLOTS + slot] for slot in range(SLOTS)]
        more, more_rims = pair_batch(epoch, mates, total, main, rim)
        products += more
        rims += more_rims
    return products, rims


def clipped(value, last):
    return jnp.minimum(jnp.maximum(value, 0), last)


def pair_kernel(sizes, places, partner, weight, present, order, band, rim_band, *refs):
    epochs, rows, operands = sizes
    inputs = refs[:operands]
    factors, pulls, boxed, main, rim, looked, rim_looked, wide = refs[operands:]
    count = len(places)
    total = count * epochs
    look_rows = rows // LOOK
    halo_looks = HALO // LOOK
    looks = look_rows + 2 * halo_looks
    full_rows = rows + 2 * HALO
    group = 2 * SLOTS

    at = lax.broadcasted_iota(jnp.int32, (full_rows, full_rows), 1)
    keep = jnp.where(at < HALO, present[0], jnp.where(at >= HALO + rows, present[1], 1.0))
    order = (order[...].astype(jnp.float32) * keep).astype(jnp.bfloat16)
    bands = band[...], rim_band[...]
    for block, (tile_at, top_at, bottom_at, top_row, bottom_row) in enumerate(places):
        tile, top, bottom = inputs[tile_at], inputs[top_at], inputs[bottom_at]

        def rows_of(at):
            above = top[top_row + at * HALO : top_row + (at + 1) * HALO, :]
            below = bottom[bottom_row + at * HALO : bottom_row + (at + 1) * HALO, :]
            return jnp.concatenate([above, tile[at * rows : (at + 1) * rows, :], below], axis=0)

        first = [part * total + block * epochs + epoch for part in range(2) for epoch in range(epochs)]
        unpack_tiles(order, range(2 * epochs), main, first, rows_of)
        by_look = jnp.dot(order, rows_of(2 * epochs), preferred_element_type=jnp.float32)
        unpack_rims(by_look, looks, rim, first)
    power_batches(count, epochs, looks, main, rim, looked, rim_looked)
    powers = count // 2
    couples = total // 2

    def boxed_of(channel):
        return boxed[pl.ds(pl.multiple_of(channel * look_rows, look_rows), look_rows), :]

    def finished(couple):
        results = []
        for one in range(2):
            epoch = couple * 2 + one
            own_power = boxed_of(epoch)
            first = (2 * powers + epoch) * (group * look_rows)
            parts = boxed[first : first + group * look_rows, :]
            parts = parts.reshape(group, look_rows, LANES)
            for slot in range(SLOTS):
                pair = epoch * SLOTS + slot
                inverse = lax.rsqrt(own_power * boxed_of(partner[pair]) + EPSILON)
                unit_re = parts[slot] * inverse
                unit_im = parts[SLOTS + slot] * inverse
                factor = weight[pair] * (unit_re * unit_re + unit_im * unit_im)
                results.append((factor, factor * unit_im))
        return results

    def boxes(couple):
        return [rows_summed(couple * 2 * group + one, looks, look_rows, wide) for one in range(2 * group)]

    def turn(number, steps):
        if 3 in steps:
            results = finished(number - 3)
        if 2 in steps:
            sums = boxes(powers + number - 2)
        if 1 in steps:
            columns = columns_summed(powers + number - 1, looks, bands, looked, rim_looked)
        if 0 in steps:
            products, rims = pair_couple(number, total, partner, main, rim)
        if 3 in steps:
            for ref, values in zip((factors, pulls), zip(*results)):
                ref[pl.ds((number - 3) * 2 * SLOTS, 2 * SLOTS)] = jnp.stack(values)
        if 2 in steps:
            put(boxed, powers + number - 2, sums)
        if 1 in steps:
            put(wide, powers + number - 1, columns)
        if 0 in steps:
            put(looked, powers + number, products)
            put(rim_looked, powers + number, rims)

    for couple in range(powers):
        put(wide, couple, columns_summed(couple, looks, bands, looked, rim_looked))
    turn(0, (0,))
    for couple in range(powers):
        put(boxed, couple, boxes(couple))
    turn(1, (0, 1))
    turn(2, (0, 1, 2))
    for number in range(3, couples):
        turn(number, (0, 1, 2, 3))
    turn(couples, (1, 2, 3))
    turn(couples + 1, (2, 3))
    turn(couples + 2, (3,))


def gradient_kernel(sizes, partner, *refs):
    tiles, epochs = sizes
    fields = refs[:tiles]
    factors, pulls, gradient, sums, est, old, shares = refs[tiles:]
    look_rows = est.shape[1]
    total = tiles * epochs
    f32 = jnp.float32
    for block in range(tiles):
        for epoch in range(epochs):
            here = slice(epoch * look_rows, (epoch + 1) * look_rows)
            est[block * epochs + epoch] = from_fixed_point(fields[block][0, here, :])
            old[block * epochs + epoch] = from_fixed_point(fields[block][1, here, :])
    mates = [[partner[epoch * SLOTS + slot] for slot in range(SLOTS)] for epoch in range(total)]
    for epoch in range(total):
        own_est = est[epoch]
        own = None
        for slot, mate in enumerate(mates[epoch]):
            pair = epoch * SLOTS + slot
            weighted = pulls[pair] - factors[pair] * (own_est - est[mate])
            own = weighted if own is None else own + weighted
            shares[pair] = weighted
        gradient[epoch] = own
    for epoch in range(total):
        values = [gradient[mate] - shares[epoch * SLOTS + slot] for slot, mate in enumerate(mates[epoch])]
        for mate, value in zip(mates[epoch], values):
            gradient[mate] = value

    zero = jnp.zeros((look_rows, LANES), f32)
    norm, crossed, grad_term, mixed_term, old_term = (zero,) * 5
    for epoch in range(total):
        own_grad = gradient[epoch]
        own_old = old[epoch]
        norm = norm + own_grad * own_grad
        crossed = crossed + own_grad * own_old
        for slot, mate in enumerate(mates[epoch]):
            factor = factors[epoch * SLOTS + slot]
            grad_spread = own_grad - gradient[mate]
            old_spread = own_old - old[mate]
            pulled = factor * grad_spread
            grad_term = grad_term + pulled * grad_spread
            mixed_term = mixed_term + pulled * old_spread
            old_term = old_term + factor * old_spread * old_spread
    sums[...] = jnp.zeros(sums.shape, f32)
    for at, value in enumerate((norm, crossed, grad_term, mixed_term, old_term)):
        sums[at : at + 1, :] = jnp.sum(value, axis=0, keepdims=True)


def exponent_of(size):
    power = jnp.ceil(jnp.log(jnp.maximum(size, 1e-30)) * (1.0 / math.log(2.0)))
    return jnp.clip(power, -110.0, 110.0)


def whole(value):
    return jnp.floor(value + 0.5).astype(jnp.int32).astype(jnp.int16)


def number_of(value):
    return value.astype(jnp.int32).astype(jnp.float32)


def code_kernel(gradient, *coded):
    epochs = gradient.shape[0] // (len(coded) + 1)
    look_rows = gradient.shape[1]
    for number, out in enumerate(coded):
        powers = []
        for epoch in range(epochs):
            value = gradient[(number + 1) * epochs + epoch]
            power = exponent_of(jnp.max(jnp.abs(value), axis=0, keepdims=True))
            out[epoch * look_rows : (epoch + 1) * look_rows, :] = whole(value * (jnp.exp2(-power) * GRADIENT_STEPS))
            powers.append(power)
        powers.append(jnp.zeros((HALO - epochs, LANES), jnp.float32))
        out[epochs * look_rows :, :] = whole(jnp.concatenate(powers, axis=0))


def update_kernel(cell_count, me, prev_mean, estimate, direction, gradient, *refs):
    new_estimate, new_direction = refs[-2:]
    tiles = estimate.shape[2] // LANES
    pieces, scalars = refs[: tiles - 1], refs[tiles - 1 : -2]
    epochs = estimate.shape[0]
    look_rows = estimate.shape[1]
    coded_rows = epochs * look_rows + HALO
    total = scalars[0][...]
    for other in scalars[1:]:
        total = total + other[...]
    total = jnp.sum(total, axis=1, keepdims=True)
    grad_norm, crossed, grad_term, mixed, old_term = (total[at : at + 1, :] for at in range(5))
    momentum = grad_norm / cell_count / prev_mean[0]
    curvature = grad_term + 2.0 * momentum * mixed + momentum * momentum * old_term
    step = (grad_norm + momentum * crossed) / curvature
    momentum = jnp.broadcast_to(momentum, (look_rows, LANES))
    step = jnp.broadcast_to(step, (look_rows, LANES))
    for shift in range(tiles):
        tile = lax.bitwise_xor(me[0], shift)
        columns = pl.ds(pl.multiple_of(tile * LANES, LANES), LANES)
        if shift > 0:
            piece = pieces[shift - 1]
            scale = jnp.exp2(number_of(piece[epochs * look_rows : coded_rows, :])) * (1.0 / GRADIENT_STEPS)
        for epoch in range(epochs):
            if shift == 0:
                value = gradient[epoch]
            else:
                value = number_of(piece[epoch * look_rows : (epoch + 1) * look_rows, :]) * scale[epoch : epoch + 1, :]
            moved = value + momentum * direction[epoch, :, columns]
            new_direction[epoch, :, columns] = moved
            new_estimate[epoch, :, columns] = estimate[epoch, :, columns] + step * moved


def swapped(up, down, axis):
    size = lax.axis_size(axis)
    if size == 1:
        return jnp.zeros_like(up), jnp.zeros_like(down)
    if size == 2:
        first = lax.axis_index(axis) == 0
        got = lax.ppermute(jnp.where(first, up, down), axis, [(0, 1), (1, 0)])
        return got, got
    forward = [(i, i + 1) for i in range(size - 1)]
    backward = [(target, source) for source, target in forward]
    return lax.ppermute(up, axis, forward), lax.ppermute(down, axis, backward)


def exchanged(x, axis, by):
    size = lax.axis_size(axis)
    return lax.ppermute(x, axis, [(i, i ^ by) for i in range(size)])


def transposed_plan(slc, offsets, weights, estimate, direction, prev_mean):
    f32 = jnp.float32
    bf16 = jnp.bfloat16
    tiles = lax.axis_size("epoch")
    me = lax.axis_index("epoch")
    epochs, rows, columns = slc.shape[1:]
    look_rows = rows // LOOK
    total = tiles * epochs
    tile_rows = 2 * epochs * rows
    params_of = pltpu.CompilerParams(vmem_limit_bytes=VMEM_BYTES)

    sub = lax.axis_index("sub")
    outer_tile = (2, epochs, rows, LANES)
    edge = pl.pallas_call(
        edge_kernel,
        out_shape=jax.ShapeDtypeStruct((rows, LANES), bf16),
        grid=(1,),
        in_specs=[
            pl.BlockSpec(outer_tile, lambda _: (0, 0, 0, 0)),
            pl.BlockSpec(outer_tile, lambda _: (0, 0, 0, tiles - 1)),
        ],
        out_specs=pl.BlockSpec((rows, LANES), lambda _: (0, 0)),
        compiler_params=params_of,
        cost_estimate=pl.CostEstimate(flops=1_000_000, bytes_accessed=1_000_000, transcendentals=0),
    )(slc, slc)
    before, after = swapped(edge, edge, "sub")
    params = jnp.zeros((rows, LANES), f32)
    listed = jnp.concatenate([offsets.astype(f32), weights, weights, weights], axis=1)
    params = lax.dynamic_update_slice(params, listed, (0, PARAM_LANE))
    sub_present = jnp.stack([sub > 0, sub < lax.axis_size("sub") - 1]).astype(f32)
    messages = pl.pallas_call(
        pack_kernel,
        out_shape=(jax.ShapeDtypeStruct((tile_rows + rows, LANES), bf16),) * tiles,
        in_specs=[SMEM] * 2 + [VMEM] * 4,
        out_specs=(VMEM,) * tiles,
        scratch_shapes=[pltpu.VMEM((tiles, rows, LANES), bf16)],
        compiler_params=params_of,
        cost_estimate=pl.CostEstimate(flops=3_000_000, bytes_accessed=4_000_000, transcendentals=0),
    )(me.reshape(1), sub_present, slc, params, before, after)
    space = lax.axis_index("space")
    spaces = lax.axis_size("space")
    present = jnp.stack([space > 0, space < spaces - 1]).astype(f32)

    def halo(pieces):
        def border(from_row):
            cuts = [lax.dynamic_slice_in_dim(piece, from_row, HALO, axis=1).reshape(-1, LANES) for piece in pieces]
            return jnp.concatenate(cuts, axis=0)

        if spaces == 2:
            got = lax.ppermute(border(jnp.where(space == 0, rows - HALO, 0)), "space", [(0, 1), (1, 0)])
            return got, got
        return swapped(border(rows - HALO), border(0), "space")

    block = [messages[0]] + [exchanged(messages[by], "epoch", by) for by in range(1, tiles)]
    estimate, direction, _ = lax.optimization_barrier((estimate, direction, messages))
    fields = pl.pallas_call(
        fields_kernel,
        out_shape=(jax.ShapeDtypeStruct((2, epochs * look_rows, LANES), jnp.int16),) * tiles,
        in_specs=[SMEM] + [VMEM] * 2,
        out_specs=(VMEM,) * tiles,
        compiler_params=params_of,
        cost_estimate=pl.CostEstimate(flops=1_000_000, bytes_accessed=2_000_000, transcendentals=0),
    )(me.reshape(1), estimate, direction)
    def params_in(shift):
        return block[shift][tile_rows : tile_rows + epochs, PARAM_LANE : PARAM_LANE + 4 * SLOTS].astype(f32)

    halos = [halo([array.reshape(-1, rows, LANES)]) for array in block]
    late = lax.optimization_barrier((fields, block, halos[1:-1]))[0]
    near = lax.optimization_barrier((fields[1], block[1], halos[0]))[0]
    field = [fields[0], exchanged(near, "epoch", 1)] + [exchanged(late[by], "epoch", by) for by in range(2, tiles)]

    listed = jnp.concatenate([params_in(shift) for shift in range(tiles)], axis=0)
    place = jnp.arange(total, dtype=jnp.int32)[:, None]
    first = lax.bitwise_xor(place // epochs, me) * epochs + place % epochs
    mate = lax.rem(first + listed[:, :SLOTS].astype(jnp.int32), total)
    partner = (lax.bitwise_xor(mate // epochs, me) * epochs + mate % epochs).reshape(-1)
    weight = listed[:, SLOTS : 2 * SLOTS] + listed[:, 2 * SLOTS : 3 * SLOTS] + listed[:, 3 * SLOTS :]
    order = look_order(rows + 2 * HALO, HALO // LOOK - RADIUS)
    bands = column_bands()
    operands = list(block)
    places = []
    for shift in range(tiles):
        top, bottom = halos[shift]
        operands.append(top)
        top_at = bottom_at = len(operands) - 1
        if bottom is not top:
            operands.append(bottom)
            bottom_at = len(operands) - 1
        places.append((shift, top_at, bottom_at, 0, 0))
    looks = (rows + 2 * HALO) // LOOK
    group = 2 * SLOTS
    batches = tiles + total
    shape = jax.ShapeDtypeStruct((total * SLOTS, look_rows, LANES), f32)
    factors, pulls = pl.pallas_call(
        functools.partial(pair_kernel, (epochs, rows, len(operands)), tuple(places)),
        out_shape=(shape, shape),
        in_specs=[SMEM] * 3 + [VMEM] * (3 + len(operands)),
        out_specs=(VMEM, VMEM),
        scratch_shapes=[
            pltpu.VMEM((batches * group * look_rows, LANES), f32),
            pltpu.VMEM((2 * total, LOOK, looks, LANES), f32),
            pltpu.VMEM((2 * total, looks, LANES), f32),
            pltpu.VMEM((batches * group * looks, LANES), f32),
            pltpu.VMEM((batches * 2 * looks, LANES), f32),
            pltpu.VMEM((batches * group * looks, LANES), f32),
        ],
        compiler_params=params_of,
        cost_estimate=pl.CostEstimate(flops=20_000_000, bytes_accessed=30_000_000, transcendentals=0),
    )(partner, weight.reshape(-1), present, order, *bands, *operands)
    gradient, sums = pl.pallas_call(
        functools.partial(gradient_kernel, (tiles, epochs)),
        out_shape=(
            jax.ShapeDtypeStruct((total, look_rows, LANES), f32),
            jax.ShapeDtypeStruct((8, LANES), f32),
        ),
        in_specs=[SMEM] + [VMEM] * (tiles + 2),
        out_specs=(VMEM, VMEM),
        scratch_shapes=[pltpu.VMEM((total, look_rows, LANES), f32)] * 2
        + [pltpu.VMEM((total * SLOTS, look_rows, LANES), f32)],
        compiler_params=params_of,
        cost_estimate=pl.CostEstimate(flops=10_000_000, bytes_accessed=8_000_000, transcendentals=0),
    )(partner, *field, factors, pulls)

    place = ("space", "sub")
    count = spaces * lax.axis_size("sub")
    shared = [sums] + [lax.ppermute(sums, place, [(i, (i + by) % count) for i in range(count)]) for by in range(1, count)]
    coded_shape = jax.ShapeDtypeStruct((epochs * look_rows + HALO, LANES), jnp.int16)
    coded = pl.pallas_call(
        code_kernel,
        out_shape=(coded_shape,) * (tiles - 1),
        in_specs=[VMEM],
        out_specs=(VMEM,) * (tiles - 1),
        compiler_params=params_of,
        cost_estimate=pl.CostEstimate(flops=1_000_000, bytes_accessed=1_000_000, transcendentals=0),
    )(gradient)
    returned = [exchanged(piece, "epoch", by + 1) for by, piece in enumerate(coded)]
    here = lax.optimization_barrier((sum(shared[1:], shared[0]), returned[0]))[0]
    scalars = [here] + [exchanged(here, "epoch", by) for by in range(1, tiles)]
    cell_count = float(total * look_rows * spaces * columns * lax.axis_size("sub"))
    return pl.pallas_call(
        functools.partial(update_kernel, cell_count),
        out_shape=(jax.ShapeDtypeStruct(estimate.shape, f32),) * 2,
        in_specs=[SMEM] * 2 + [VMEM] * (2 + 2 * tiles),
        out_specs=(VMEM, VMEM),
        compiler_params=params_of,
        cost_estimate=pl.CostEstimate(flops=1_000_000, bytes_accessed=2_000_000, transcendentals=0),
    )(me.reshape(1), prev_mean, estimate, direction, gradient[:epochs], *returned, *scalars)


def on_device(slc, offsets, weights, estimate, direction, prev_mean):
    epochs, rows, columns = slc.shape[1:]
    fits = columns == LANES * lax.axis_size("epoch") and lax.axis_size("epoch") > 1
    size = lax.axis_size("epoch")
    fits = fits and size & (size - 1) == 0 and 2 * epochs * SIDES <= PARAM_LANE and rows % HALO == 0 and epochs == 2 * SLOTS
    plan = transposed_plan if fits else ring_plan
    return plan(slc, offsets, weights, estimate, direction, prev_mean)


def solution(mesh):
    return jax.shard_map(
        on_device,
        mesh=mesh,
        in_specs=(
            P(None, ("groups", "epoch"), "space", "sub"),
            P(("groups", "epoch"), None),
            P(("groups", "epoch"), None),
            P(("groups", "epoch"), "space", "sub"),
            P(("groups", "epoch"), "space", "sub"),
            P(),
        ),
        out_specs=(P(("groups", "epoch"), "space", "sub"), P(("groups", "epoch"), "space", "sub")),
        check_vma=False,
    )
```
